32 devices in a mesh: dp: 4 (over y, x), mp: 8 (over z, core).
Axes of the slice: x: 2, y: 2, z: 4, core: 2. Of those that a mesh axis runs over, the one named last changes fastest.
Arguments:
- tokens: bfloat16 [2, 1024, 2048], P(None, 'dp', 'mp'), may hold values from -6 to 6
- out_grad: bfloat16 [2, 1024, 2048], P(None, 'dp'), may hold values from -6 to 6
- domain: int32 [2, 1024], P(None, 'dp'), may hold values from 0 to 2, as said below
- group_weight: float32 [3], replicated, may hold values from 0.2 to 0.6
- w_qkv: bfloat16 [3, 2048, 2048], P(None, 'dp', 'mp'), may hold values from -0.125 to 0.125
- conv_weight: bfloat16 [3, 4, 16, 128], P(None, None, 'mp', 'dp'), may hold values from -3 to 3
- w_beta: bfloat16 [2048, 16], P('dp', 'mp'), may hold values from -0.125 to 0.125
- w_outgate: bfloat16 [2048, 2048], P('dp', 'mp'), may hold values from -0.125 to 0.125
- head_gain: bfloat16 [128], P('dp'), may hold values from 0.099609375 to 1.8984375
- w_out: bfloat16 [2048, 2048], P('mp', 'dp'), may hold values from -0.1875 to 0.1875
- mixer_gain: bfloat16 [2048], P('dp'), may hold values from 0.099609375 to 1.8984375
- mlp_gain: bfloat16 [2048], P('dp'), may hold values from 0.099609375 to 1.8984375
- w_gateup: bfloat16 [2, 2048, 5632], P(None, 'dp', 'mp'), may hold values from -0.125 to 0.125
- w_down: bfloat16 [5632, 2048], P('mp', 'dp'), may hold values from -0.15625 to 0.15625
Outputs:
- mixed_out: bfloat16 [2, 1024, 2048], P(None, 'dp', 'mp')
- tokens_grad: bfloat16 [2, 1024, 2048], P(None, 'dp', 'mp')
- grad_qkv: float32 [3, 2048, 2048], P(None, 'dp', 'mp')
- grad_conv: float32 [3, 4, 16, 128], P(None, None, 'mp', 'dp')
- grad_beta: float32 [2048, 16], P('dp', 'mp')
- grad_outgate: float32 [2048, 2048], P('dp', 'mp')
- grad_headgain: float32 [128], P('dp')
- grad_outproj: float32 [2048, 2048], P('mp', 'dp')
- grad_mixgain: float32 [2048], P('dp')
- grad_mlpgain: float32 [2048], P('dp')
- grad_gateup: float32 [2, 2048, 5632], P(None, 'dp', 'mp')
- grad_down: float32 [5632, 2048], P('mp', 'dp')
The draws below stay inside these ranges and needn't reach their ends.
Inputs may be any that keep to these rules, and one draw needn't show every extreme that they name: `domain`: the first three tokens of every sequence have domains 0, 1 and 2.
All inputs are finite; a program needn't handle non-finite values.
Results may differ from the reference program's by a relative error of at most 0.025.
Values may be sent and summed in bfloat16 or wider, within the bound.
No kernel may reach another device: no remote copies, remote signals or barrier semaphores. Data moves between devices by JAX's collectives and lax.ppermute only.
A program may use at most 128 MiB of HBM per device.

```python
import jax
import jax.numpy as jnp
from jax import lax

D = 2048
H = 16
DK = 128
FF = 5632
KW = 4
CH = 64
SEQS = 2
HD = 2048
LENGTH = 1024
TOKENS = 2048


def draw_domain(key, part):
    key = jax.random.fold_in(key, 17)
    position = jnp.arange(LENGTH, dtype=jnp.int32)[None, :]
    drawn_values = jax.random.randint(key, (SEQS, LENGTH), 0, 4 * LENGTH, dtype=jnp.int32)
    others = jnp.where(drawn_values % 3 == 0, 2, 1)
    domains = jnp.where(drawn_values < LENGTH + 2 * position, 0, others)
    return jnp.where(position < 3, position + 0 * drawn_values, domains).astype(jnp.int32)


def steps_of(rng, dims, cuts, least, largest):
    gain, own = 1.0, jax.random.fold_in(rng, 6)
    for dim, shards_of in cuts:
        draws = jnp.exp(jax.random.uniform(jax.random.fold_in(own, dim), (shards_of,), jnp.float32, least / len(cuts), largest / len(cuts)))
        gain = gain * jnp.repeat(draws, dims[dim] // shards_of).reshape([-1 if axis == dim else 1 for axis in range(len(dims))])
    return gain


def centred(stream_key, shape, scale, bound, cuts=(), kind=jnp.bfloat16):
    level = steps_of(stream_key, shape, cuts, -0.22, 0.18) if cuts else 1.0
    values = jax.random.normal(stream_key, shape, jnp.float32) * scale * level
    return jnp.minimum(jnp.maximum(values, -bound), bound).astype(kind)


def setup_inputs(seed: int = 0) -> dict:
    key_list = jax.random.split(jax.random.key(seed), 15)
    return {
        "tokens": centred(key_list[0], (SEQS, LENGTH, D), 1.0, 6.0, ((1, 4), (2, 8))),
        "out_grad": centred(key_list[1], (SEQS, LENGTH, D), 1.0, 6.0, ((1, 4),)),
        "domain": draw_domain(jax.random.fold_in(key_list[14], 71), 0),
        "group_weight": jnp.clip(jax.random.uniform(key_list[3], (3,), jnp.float32, 0.2, 0.6), 0.2, 0.6),
        "w_qkv": centred(key_list[4], (3, D, HD), D ** -0.5, 0.125, ((1, 4), (2, 8))),
        "conv_weight": centred(key_list[5], (3, KW, H, DK), KW ** -0.5, 3.0, ((2, 8), (3, 4))),
        "w_beta": centred(key_list[6], (D, H), D ** -0.5, 0.125, ((0, 4), (1, 8))),
        "w_outgate": centred(key_list[7], (D, HD), D ** -0.5, 0.125, ((0, 4), (1, 8))),
        "head_gain": jnp.clip(1.0 + 0.18 * jax.random.normal(key_list[8], (DK,), jnp.float32), 0.099609375, 1.8984375).astype(jnp.bfloat16),
        "w_out": centred(key_list[9], (HD, D), (HD // 2) ** -0.5, 0.1875, ((0, 8), (1, 4))),
        "mixer_gain": jnp.clip(1.0 + 0.18 * jax.random.normal(key_list[10], (D,), jnp.float32), 0.099609375, 1.8984375).astype(jnp.bfloat16),
        "mlp_gain": jnp.clip(1.0 + 0.18 * jax.random.normal(key_list[11], (D,), jnp.float32), 0.099609375, 1.8984375).astype(jnp.bfloat16),
        "w_gateup": centred(key_list[12], (2, D, FF), D ** -0.5, 0.125, ((1, 4), (2, 8))),
        "w_down": centred(key_list[13], (FF, D), (FF // 4) ** -0.5, 0.15625, ((0, 8), (1, 4))),
    }


eps_norm = 1e-06
eps_unit = 1e-06
exact_mode = lax.Precision.HIGHEST

@jax.custom_vjp
def low(v):
    return lax.optimization_barrier(v.astype(jnp.bfloat16)).astype(jnp.float32)

@jax.custom_vjp
def low_back(v):
    return v

def low_keep(v):
    return (low(v), None)

def low_pass(kept, grad):
    return (grad,)

def back_keep(v):
    return (v, None)

def back_low(kept, grad):
    return (low(grad),)
low.defvjp(low_keep, low_pass)
low_back.defvjp(back_keep, back_low)

def rms_scale(values):
    return lax.rsqrt(lax.optimization_barrier(jnp.mean(values * values, -1, keepdims=True)) + eps_norm)

def unit_rows(values):
    return values * lax.rsqrt(lax.optimization_barrier(jnp.sum(values * values, -1, keepdims=True)) + eps_unit)

def piece_step(state, pieces):
    query_rows, key_rows, value_rows, beta_rows = pieces
    width = key_rows.shape[-2]
    strict = jnp.tril(jnp.ones((width, width), jnp.float32), -1)
    filled = jnp.tril(jnp.ones((width, width), jnp.float32))
    gram = jnp.einsum('...ik,...jk->...ij', key_rows, key_rows, precision=exact_mode)
    matrix = jnp.eye(width, dtype=jnp.float32) + beta_rows[..., :, None] * gram * strict
    target = beta_rows[..., :, None] * (value_rows - jnp.einsum('...ik,...kv->...iv', key_rows, state, precision=exact_mode))
    deltas = lax.linalg.triangular_solve(matrix, target, left_side=True, lower=True, unit_diagonal=True)
    scores = jnp.einsum('...ik,...jk->...ij', query_rows, key_rows, precision=exact_mode) * filled
    output = jnp.einsum('...ik,...kv->...iv', query_rows, state, precision=exact_mode)
    output = output + jnp.einsum('...ij,...jv->...iv', scores, deltas, precision=exact_mode)
    state = state + jnp.einsum('...ik,...iv->...kv', key_rows, deltas, precision=exact_mode)
    return (state, output)

def delta_rule(queries, keys, values, betas):
    heads, length, head_dim = keys.shape
    count = length // CH

    def split(array):
        return jnp.moveaxis(array.reshape(heads, count, CH, head_dim), 1, 0)
    beta_pieces = jnp.moveaxis(betas.reshape(heads, count, CH), 1, 0)
    start = jnp.zeros((heads, head_dim, head_dim), jnp.float32)
    scaled = queries * head_dim ** (-0.5)
    final, outputs = lax.scan(jax.checkpoint(piece_step), start, (split(scaled), split(keys), split(values), beta_pieces))
    return jnp.moveaxis(outputs, 0, 1).reshape(heads, length, head_dim)

def forward(tokens, w_qkv, conv_weight, w_beta, w_outgate, head_gain, w_out, mixer_gain, mlp_gain, w_gateup, w_down):
    length = tokens.shape[0]
    heads = conv_weight.shape[2]
    head_dim = conv_weight.shape[3]
    inner = heads * head_dim
    hidden_one = low(tokens * rms_scale(tokens) * mixer_gain)
    projected = low_back(low(jnp.einsum('td,idc->itc', hidden_one, w_qkv, precision=exact_mode)))
    kernel = conv_weight.reshape(3, KW, inner)
    padded = jnp.concatenate([jnp.zeros((3, KW - 1, inner), jnp.float32), projected], 1)
    convolved = kernel[:, 0, None, :] * padded[:, 0:length, :]
    for tap_index in range(1, KW):
        convolved = convolved + kernel[:, tap_index, None, :] * padded[:, tap_index:tap_index + length, :]
    acts = jax.nn.silu(convolved).reshape(3, length, heads, head_dim).transpose(0, 2, 1, 3)
    queries = low(unit_rows(acts[0]))
    keys = low(unit_rows(acts[1]))
    values = low(acts[2])
    betas = jax.nn.sigmoid(low_back(jnp.dot(hidden_one, w_beta, precision=exact_mode))).T
    gates = low_back(jnp.dot(hidden_one, w_outgate, precision=exact_mode))
    rule_out = delta_rule(queries, keys, values, betas).transpose(1, 0, 2)
    gate_heads = gates.reshape(length, heads, head_dim)
    normed = rule_out * rms_scale(rule_out) * head_gain * jax.nn.silu(gate_heads)
    normed = low(normed.reshape(length, inner))
    middle = tokens + low_back(jnp.dot(normed, w_out, precision=exact_mode))
    hidden_two = low(middle * rms_scale(middle) * mlp_gain)
    gate_up = low_back(jnp.einsum('td,idf->itf', hidden_two, w_gateup, precision=exact_mode))
    hidden_mlp = low(jax.nn.silu(gate_up[0]) * gate_up[1])
    return middle + jnp.dot(hidden_mlp, w_down, precision=exact_mode)

def reference(tokens, out_grad, domain, group_weight, w_qkv, conv_weight, w_beta, w_outgate, head_gain, w_out, mixer_gain, mlp_gain, w_gateup, w_down):
    onehot = (domain[..., None] == jnp.arange(3, dtype=jnp.int32)).astype(jnp.float32)
    counts = lax.optimization_barrier(jnp.sum(onehot, axis=(0, 1)))
    table = group_weight * TOKENS / counts
    factor = lax.optimization_barrier(jnp.sum(onehot * table, -1))
    cotangent = (out_grad.astype(jnp.float32) * factor[..., None]).astype(jnp.bfloat16).astype(jnp.float32)
    weights = tuple((item.astype(jnp.float32) for item in (w_qkv, conv_weight, w_beta, w_outgate, head_gain, w_out, mixer_gain, mlp_gain, w_gateup, w_down)))

    def one_sequence(totals, pieces):
        sequence, seq_grad = pieces
        result, pull_back = jax.vjp(forward, sequence.astype(jnp.float32), *weights)
        grads = pull_back(seq_grad)
        totals = tuple((left + right for left, right in zip(totals, grads[1:])))
        return (totals, (result.astype(jnp.bfloat16), grads[0].astype(jnp.bfloat16)))
    zeros = tuple((jnp.zeros_like(item) for item in weights))
    totals, (mixed_out, tokens_grad) = lax.scan(one_sequence, zeros, (tokens, cotangent))
    return (mixed_out, tokens_grad, totals[0], totals[1], totals[2], totals[3], totals[4], totals[5], totals[6], totals[7], totals[8], totals[9])
```

```python
import jax
import jax.numpy as jnp
from jax import lax
from jax.experimental import pallas as pl
from jax.experimental.pallas import tpu as pltpu
from jax.sharding import PartitionSpec as P

DK = 128
KW = 4
PAD = 8

eps_norm = 1e-06
eps_unit = 1e-06

f32 = jnp.float32
bf16 = jnp.bfloat16


def split(v):
    if v.dtype == bf16:
        return v, None
    high = v.astype(bf16)
    return high, (v - high.astype(f32)).astype(bf16)


def mm(a, b, ca=1, cb=0, passes=3):
    def one(x, y):
        return lax.dot_general(x, y, (((ca,), (cb,)), ((), ())), preferred_element_type=f32)

    if passes == 1:
        return one(a.astype(bf16), b.astype(bf16))
    (ah, al), (bh, bl) = split(a), split(b)
    out = one(ah, bh)
    if bl is not None:
        out = out + one(ah, bl)
    if al is not None:
        out = out + one(al, bh)
    return out


def places(rows, cols):
    return (
        lax.broadcasted_iota(jnp.int32, (rows, cols), 0),
        lax.broadcasted_iota(jnp.int32, (rows, cols), 1),
    )


def unit_lower_inverses(blocks):
    size = blocks[0].shape[0]
    if size > 128:
        half = size // 2
        parts = unit_lower_inverses(
            [a[:half, :half] for a in blocks] + [a[half:, half:] for a in blocks]
        )
        firsts, seconds = parts[: len(blocks)], parts[len(blocks) :]
        inner = [mm(a[half:, :half], x) for a, x in zip(blocks, firsts)]
        lower = [-mm(x, y) for x, y in zip(seconds, inner)]
        zero = jnp.zeros((half, half), f32)
        return [
            jnp.concatenate(
                [jnp.concatenate([x, zero], 1), jnp.concatenate([y, z], 1)], 0
            )
            for x, y, z in zip(firsts, lower, seconds)
        ]
    rows, cols = places(size, size)
    eye = (rows == cols).astype(f32)
    level = 0
    inverses = None
    while (1 << level) < size:
        mask = (
            ((rows >> (level + 1)) == (cols >> (level + 1)))
            & (((rows >> level) & 1) == 1)
            & (((cols >> level) & 1) == 0)
        ).astype(f32)
        lows = [a * mask for a in blocks]
        if level == 0:
            inverses = [eye - low for low in lows]
        else:
            inner = [mm(low, x) for low, x in zip(lows, inverses)]
            inverses = [x - mm(x, y) for x, y in zip(inverses, inner)]
        level += 1
    return inverses


def head_slice(h):
    return slice(h * DK, (h + 1) * DK)


def convolve(rows, before, taps, i, h, inner):
    lanes = slice(i * inner + h * DK, i * inner + (h + 1) * DK)
    own = rows[:, lanes].astype(bf16).astype(f32)
    ext = jnp.concatenate([before[:, lanes], own], 0)
    length = own.shape[0]
    shifts = [ext[PAD - KW + 1 + j : PAD - KW + 1 + j + length] for j in range(KW)]
    out = None
    for j in range(KW):
        tap = taps[i * KW + j : i * KW + j + 1, head_slice(h)]
        out = tap * shifts[j] if out is None else out + tap * shifts[j]
    sig = jax.nn.sigmoid(out)
    return shifts, out, sig, out * sig


def unit(acts):
    inv = lax.rsqrt(jnp.sum(acts * acts, -1, keepdims=True) + eps_unit)
    return acts * inv, inv


def rule_inputs(rows, before, taps, h, inner):
    parts = [convolve(rows, before, taps, i, h, inner) for i in range(3)]
    q, q_inv = unit(parts[0][3])
    k, k_inv = unit(parts[1][3])
    return parts, (q, q_inv), (k, k_inv), parts[2][3]


def pre_kernel(cat_ref, before_ref, taps_ref, beta_ref, x_ref, wu_ref, qo_ref, to_ref):
    heads = to_ref.shape[1]
    inner = heads * DK
    rows, before, taps = cat_ref[0], before_ref[0], taps_ref[...]
    length = rows.shape[0]
    r, c = places(length, length)
    strict = (r > c).astype(f32)
    full = (r >= c).astype(f32)
    saved, blocks = [], []
    for h in range(heads):
        _, (q, _), (k, _), v = rule_inputs(rows, before, taps, h, inner)
        q, k, v = q.astype(bf16), k.astype(bf16), v.astype(bf16)
        beta = beta_ref[0, :, h : h + 1]
        gram = mm(k, k, 1, 1)
        blocks.append(beta * gram * strict)
        saved.append((q, k, v, beta))
    inverses = unit_lower_inverses(blocks)
    r, c = places(DK, DK)
    eye = (r == c).astype(f32)
    for h in range(heads):
        q, k, v, beta = saved[h]
        x = inverses[h]
        x_ref[0, h] = x
        kv = jnp.concatenate([k.astype(f32), v.astype(f32)], 1) * beta
        wu = mm(x, kv)
        wu_ref[0, h] = wu
        scores = mm(q, k, 1, 1) * full
        pwu = mm(scores, wu)
        qo_ref[0, h, :, :DK] = q.astype(f32) - pwu[:, :DK]
        qo_ref[0, h, :, DK:] = pwu[:, DK:]
        kwu = mm(k, wu, 0, 0)
        to_ref[0, h, :, :DK] = (eye - kwu[:, :DK]).astype(bf16)
        to_ref[0, h, :, DK:] = kwu[:, DK:].astype(bf16)


def mix_kernel(*refs):
    near, (qo_ref, cat_ref, gain_ref, normed_ref, rule_ref, state_ref) = refs[:-6], refs[-6:]
    heads = state_ref.shape[1]
    inner = heads * DK
    for h in range(heads):
        state = jnp.zeros((DK, DK), f32)
        for ref in reversed(near):
            state = mm(ref[0, h, :, :DK], state) + ref[0, h, :, DK:].astype(f32)
        state_ref[0, h] = state
        qo = qo_ref[0, h]
        out = (mm(qo[:, :DK], state) + qo[:, DK:]) * DK ** (-0.5)
        rule_ref[0, :, head_slice(h)] = out
        gate = cat_ref[0, :, 3 * inner + h * DK : 3 * inner + (h + 1) * DK]
        factor = lax.rsqrt(jnp.mean(out * out, -1, keepdims=True) + eps_norm)
        normed = out * factor * gain_ref[...] * (gate * jax.nn.sigmoid(gate))
        normed_ref[0, :, head_slice(h)] = normed.astype(bf16)


def gate_back_kernel(
    grad_ref, rule_ref, cat_ref, gain_ref, qo_ref, drule_ref, dgate_ref, dgain_ref, direct_ref
):
    heads = direct_ref.shape[1]
    inner = heads * DK
    total = jnp.zeros((1, DK), f32)
    for h in range(heads):
        grad = grad_ref[0, :, head_slice(h)]
        out = rule_ref[0, :, head_slice(h)]
        gate = cat_ref[0, :, 3 * inner + h * DK : 3 * inner + (h + 1) * DK]
        gain = gain_ref[...]
        factor = lax.rsqrt(jnp.mean(out * out, -1, keepdims=True) + eps_norm)
        n = out * factor
        sig = jax.nn.sigmoid(gate)
        silu = gate * sig
        gg = grad * gain
        dn = gg * silu
        drule = factor * (dn - n * jnp.mean(dn * n, -1, keepdims=True))
        drule_ref[0, :, head_slice(h)] = drule
        dgate = gg * n * sig * (1.0 + gate * (1.0 - sig))
        dgate_ref[0, :, head_slice(h)] = dgate.astype(bf16)
        total = total + jnp.sum(grad * n * silu, 0, keepdims=True)
        direct = mm(qo_ref[0, h, :, :DK], drule, 0, 0) * DK ** (-0.5)
        direct_ref[0, h] = direct.astype(bf16)
    dgain_ref[0] = total


def back_kernel(*refs):
    (
        cat_ref,
        before_ref,
        taps_ref,
        beta_ref,
        x_ref,
        wu_ref,
        state_ref,
        drule_ref,
        dgate_ref,
    ) = refs[:9]
    dcat_ref, last_ref, first_ref, dtaps_ref, dlogit_ref = refs[-5:]
    others = refs[9:-5]
    count = (len(others) + 1) // 2
    directs, nexts = others[:count], others[count:]
    heads = state_ref.shape[1]
    inner = heads * DK
    rows, before, taps = cat_ref[0], before_ref[0], taps_ref[...]
    length = rows.shape[0]
    r, c = places(length, length)
    strict = (r > c).astype(f32)
    full = (r >= c).astype(f32)
    zeros = jnp.zeros((PAD, DK), f32)
    for h in range(heads):
        parts, (qu, q_inv), (ku, k_inv), vu = rule_inputs(rows, before, taps, h, inner)
        q, k, v = qu.astype(bf16), ku.astype(bf16), vu.astype(bf16)
        beta = beta_ref[0, :, h : h + 1]
        leave = jnp.zeros((DK, DK), f32)
        for j in reversed(range(count)):
            here = directs[j][0, h].astype(f32)
            leave = here if j == count - 1 else mm(nexts[j][0, h, :, :DK], leave, 0, 0) + here
        state = state_ref[0, h]
        wu = wu_ref[0, h]
        u = wu[:, DK:] - mm(wu[:, :DK], state)
        resid = v.astype(f32) - mm(k, state)
        dout = drule_ref[0, :, head_slice(h)] * DK ** (-0.5)
        gram = mm(k, k, 1, 1)
        scores = mm(q, k, 1, 1) * full
        du = mm(scores, dout, 0, 0) + mm(k, leave)
        y = mm(x_ref[0, h], du, 0, 0)
        by = beta * y
        da = -(mm(y, u, 1, 1) * strict)
        dbeta = jnp.sum(y * resid, -1, keepdims=True) + jnp.sum(da * gram, -1, keepdims=True)
        dgram = beta * da
        dscores = mm(dout, u, 1, 1) * full
        dq = mm(dout, state, 1, 1) + mm(dscores, k)
        dk = (
            mm(dgram, k)
            + mm(dgram, k, 0, 0)
            + mm(dscores, q, 0, 0)
            + mm(u, leave, 1, 1)
            - mm(by, state, 1, 1)
        )
        dlogit_ref[0, :, h : h + 1] = (dbeta * beta * (1.0 - beta)).astype(bf16)
        dq = (dq - qu * jnp.sum(qu * dq, -1, keepdims=True)) * q_inv
        dk = (dk - ku * jnp.sum(ku * dk, -1, keepdims=True)) * k_inv
        for i, dact in enumerate((dq, dk, by)):
            shifts, out, sig, _ = parts[i]
            dconv = dact * sig * (1.0 + out * (1.0 - sig))
            ext = jnp.concatenate([zeros, dconv, zeros], 0)
            total = None
            for j in range(KW):
                at = i * KW + j
                dtaps_ref[0, at : at + 1, head_slice(h)] = jnp.sum(
                    dconv * shifts[j], 0, keepdims=True
                )
                tap = taps[at : at + 1, head_slice(h)]
                term = tap * ext[KW - 1 - j : KW - 1 - j + PAD + length]
                total = term if total is None else total + term
            lanes = slice(i * inner + h * DK, i * inner + (h + 1) * DK)
            first_ref[0, :, lanes] = total[:PAD]
            last_ref[0, :, lanes] = total[length:]
            dcat_ref[0, :, lanes] = total[PAD:].astype(bf16)
    dcat_ref[0, :, 3 * inner :] = dgate_ref[0]


def per_sequence(kernel, ins, outs, shared=()):
    seqs = outs[0].shape[0]

    def spec(shape, whole):
        if whole:
            return pl.BlockSpec(shape, lambda s: (0,) * len(shape))
        return pl.BlockSpec((1,) + tuple(shape[1:]), lambda s: (s,) + (0,) * (len(shape) - 1))

    return pl.pallas_call(
        kernel,
        grid=(seqs,),
        in_specs=[spec(a.shape, n in shared) for n, a in enumerate(ins)],
        out_specs=[spec(o.shape, False) for o in outs],
        out_shape=outs,
        compiler_params=pltpu.CompilerParams(vmem_limit_bytes=48 * 2**20),
    )(*ins)


def shape_of(shape, dtype):
    return jax.ShapeDtypeStruct(shape, dtype)


def shifted(array, axis, by):
    devices = lax.axis_size(axis)
    pairs = [(i, i + by) for i in range(devices) if 0 <= i + by < devices]
    return lax.ppermute(array, axis, pairs)


def pack(parts):
    return jnp.concatenate([p.reshape(-1) for p in parts])


def unpack(flat, shapes):
    out, at = [], 0
    for shape in shapes:
        size = 1
        for n in shape:
            size *= n
        out.append(flat[..., at : at + size].reshape(flat.shape[:-1] + tuple(shape)))
        at += size
    return out


def padded(flat, multiple=1024):
    return jnp.pad(flat, (0, -flat.shape[0] % multiple))


def rms_factor(values):
    return lax.rsqrt(jnp.mean(values * values, -1, keepdims=True) + eps_norm)


def body(
    tokens,
    out_grad,
    domain,
    group_weight,
    w_qkv,
    conv_weight,
    w_beta,
    w_outgate,
    head_gain,
    w_out,
    mixer_gain,
    mlp_gain,
    w_gateup,
    w_down,
):
    dp = lax.axis_size("dp")
    place = lax.axis_index("dp")
    seqs, block, local_width = tokens.shape
    count_rows = seqs * block
    heads = conv_weight.shape[2]
    inner = heads * DK
    column = lax.axis_index("mp") * local_width

    onehot = (domain[..., None] == jnp.arange(3, dtype=jnp.int32)).astype(f32)
    own_counts = jnp.sum(onehot, axis=(0, 1))
    high = jnp.floor(own_counts / 128.0)
    digits = jnp.concatenate([high, own_counts - 128.0 * high]).astype(bf16)
    small = [w_beta, conv_weight, head_gain, mixer_gain, mlp_gain, digits]
    gathered = lax.all_gather(padded(pack(small)), "dp")
    g_beta, g_conv, g_head, g_mix, g_mlp, g_digits = unpack(gathered, [a.shape for a in small])
    full_beta = g_beta.reshape(-1, heads)
    full_conv = jnp.moveaxis(g_conv, 0, 3).reshape(3 * KW, inner).astype(f32)
    gain_head = g_head.reshape(1, DK).astype(f32)
    gain_one = g_mix.reshape(-1).astype(f32)
    gain_two = g_mlp.reshape(-1).astype(f32)
    sums = jnp.sum(g_digits.astype(f32), 0)
    counts = 128.0 * sums[:3] + sums[3:]

    rows = lax.all_gather(tokens, "mp", axis=2, tiled=True)
    cat_own = jnp.concatenate([w_qkv[0], w_qkv[1], w_qkv[2], w_outgate], 1)
    full_cat = lax.all_gather(cat_own, "dp", axis=0, tiled=True)
    full_out = lax.all_gather(w_out, "dp", axis=1, tiled=True)
    full_gateup = lax.all_gather(w_gateup, "dp", axis=1, tiled=True)
    full_down = lax.all_gather(w_down, "dp", axis=1, tiled=True)

    width = rows.shape[2]
    rows_f = rows.astype(f32).reshape(count_rows, width)
    scale_one = rms_factor(rows_f)
    hidden_one = (rows_f * scale_one * gain_one).astype(bf16)
    cat = jnp.dot(hidden_one, full_cat, preferred_element_type=f32)
    cat = cat.reshape(seqs, block, 4 * inner)
    tail = cat[:, block - PAD :, : 3 * inner].astype(bf16)
    before = shifted(tail, "dp", 1).astype(f32)
    logits = jnp.dot(hidden_one, full_beta, preferred_element_type=f32)
    betas = jax.nn.sigmoid(logits).reshape(seqs, block, heads)

    pair = (seqs, heads)
    inverse, wu, qo, to = per_sequence(
        pre_kernel,
        [cat, before, full_conv, betas],
        [
            shape_of(pair + (block, block), f32),
            shape_of(pair + (block, 2 * DK), f32),
            shape_of(pair + (block, 2 * DK), f32),
            shape_of(pair + (DK, 2 * DK), bf16),
        ],
        shared=(2,),
    )
    near = [shifted(to, "dp", c) for c in range(1, dp)]
    normed, rule, state = per_sequence(
        mix_kernel,
        near + [qo, cat, gain_head],
        [
            shape_of((seqs, block, inner), bf16),
            shape_of((seqs, block, inner), f32),
            shape_of(pair + (DK, DK), f32),
        ],
        shared=(len(near) + 2,),
    )
    normed = normed.reshape(count_rows, inner)
    mixer_part = jnp.dot(normed, full_out, preferred_element_type=f32)
    mixer_total = lax.psum(mixer_part.astype(bf16), "mp").astype(f32)
    middle = rows_f + mixer_total
    scale_two = rms_factor(middle)
    normal_two = middle * scale_two
    hidden_two = (normal_two * gain_two).astype(bf16)
    gate_up = jnp.einsum("td,idf->itf", hidden_two, full_gateup, preferred_element_type=f32)
    gate_act, up_act = (gate_up[0], gate_up[1])
    sigmoid_gate = jax.nn.sigmoid(gate_act)
    silu_gate = gate_act * sigmoid_gate
    hidden_mlp = (silu_gate * up_act).astype(bf16)

    table = group_weight * (domain.shape[0] * domain.shape[1] * dp) / counts
    factor = jnp.sum(onehot * table, -1)
    cotangent = (out_grad.astype(f32) * factor[..., None]).astype(bf16).reshape(count_rows, width)
    grad_hidden = jnp.einsum("td,fd->tf", cotangent, full_down, preferred_element_type=f32)
    grad_gate = grad_hidden * up_act * sigmoid_gate * (1.0 + gate_act * (1.0 - sigmoid_gate))
    grad_pair = jnp.stack([grad_gate, grad_hidden * silu_gate]).astype(bf16)
    grad_two_part = jnp.einsum("itf,idf->td", grad_pair, full_gateup, preferred_element_type=f32)
    grad_two = lax.psum(grad_two_part.astype(bf16), "mp").astype(f32)

    down_part = jnp.dot(hidden_mlp, full_down, preferred_element_type=f32)
    grad_down = jnp.einsum("tf,td->fd", hidden_mlp, cotangent, preferred_element_type=f32)
    grad_gateup = jnp.einsum("td,itf->idf", hidden_two, grad_pair, preferred_element_type=f32)
    sum_gateup = lax.psum_scatter(grad_gateup.astype(bf16), "dp", scatter_dimension=1, tiled=True)
    sum_down = lax.psum_scatter(grad_down.astype(bf16), "dp", scatter_dimension=1, tiled=True)
    mlp_share = lax.psum_scatter(
        down_part.astype(bf16).reshape(seqs, block, width), "mp", scatter_dimension=2, tiled=True
    ).astype(f32)
    middle_share = lax.dynamic_slice_in_dim(
        middle.reshape(seqs, block, width), column, local_width, 2
    )
    mixed_out = (middle_share + mlp_share).astype(bf16)

    scaled = grad_two * gain_two
    grad_middle = cotangent.astype(f32) + scale_two * (
        scaled - normal_two * jnp.mean(scaled * normal_two, -1, keepdims=True)
    )
    grad_mlpgain = jnp.sum(grad_two * normal_two, 0)
    grad_mix = grad_middle.astype(bf16)
    grad_normed = jnp.einsum("td,cd->tc", grad_mix, full_out, preferred_element_type=f32)
    grad_outproj = jnp.einsum("tc,td->cd", normed, grad_mix, preferred_element_type=f32)
    drule, dgate, dgain, direct = per_sequence(
        gate_back_kernel,
        [grad_normed.reshape(seqs, block, inner), rule, cat, gain_head, qo],
        [
            shape_of((seqs, block, inner), f32),
            shape_of((seqs, block, inner), bf16),
            shape_of((seqs, 1, DK), f32),
            shape_of(pair + (DK, DK), bf16),
        ],
        shared=(3,),
    )
    directs = [shifted(direct, "dp", -c) for c in range(1, dp)]
    nexts = [shifted(to, "dp", -c) for c in range(1, dp - 1)]
    dcat, last, first, dtaps, dlogits = per_sequence(
        back_kernel,
        [cat, before, full_conv, betas, inverse, wu, state, drule, dgate] + directs + nexts,
        [
            shape_of((seqs, block, 4 * inner), bf16),
            shape_of((seqs, PAD, 3 * inner), f32),
            shape_of((seqs, PAD, 3 * inner), f32),
            shape_of((seqs, 3 * KW, inner), f32),
            shape_of((seqs, block, heads), bf16),
        ],
        shared=(2,),
    )
    later = shifted(first, "dp", -1)
    dcat = lax.dynamic_update_slice(dcat, (last + later).astype(bf16), (0, block - PAD, 0))
    dcat = dcat.reshape(count_rows, 4 * inner)
    dlogits = dlogits.reshape(count_rows, heads)
    grad_one_part = jnp.einsum("tc,dc->td", dcat, full_cat, preferred_element_type=f32)
    grad_one_part = grad_one_part + jnp.einsum(
        "th,dh->td", dlogits, full_beta, preferred_element_type=f32
    )
    normal_one = rows_f * scale_one
    row_part = jnp.sum(grad_one_part * gain_one * normal_one, -1)
    gain_part = jnp.sum(grad_one_part * normal_one, 0)
    one_share = lax.psum_scatter(
        grad_one_part.astype(bf16).reshape(seqs, block, width), "mp", scatter_dimension=2, tiled=True
    ).astype(f32)
    stats = [row_part, gain_part, jnp.sum(dgain, (0, 1))]
    stat_sum = jnp.sum(lax.all_gather(pack(stats), "mp"), 0)
    row_sum, mixgain_sum, headgain_sum = unpack(stat_sum, [a.shape for a in stats])

    grad_cat = jnp.einsum("td,tc->dc", hidden_one, dcat, preferred_element_type=f32)
    grad_beta = jnp.einsum("td,th->dh", hidden_one, dlogits, preferred_element_type=f32)
    sum_cat = lax.psum_scatter(grad_cat.astype(bf16), "dp", scatter_dimension=0, tiled=True)
    sum_out = lax.psum_scatter(grad_outproj.astype(bf16), "dp", scatter_dimension=1, tiled=True)

    def own(array):
        return lax.dynamic_slice_in_dim(
            array.reshape(seqs, block, width), column, local_width, 2
        )

    row_mean = (row_sum / width).reshape(seqs, block, 1)
    gain_own = lax.dynamic_slice_in_dim(gain_one, column, local_width, 0)
    normal_own = tokens.astype(f32) * scale_one.reshape(seqs, block, 1)
    tokens_grad = own(grad_middle) + scale_one.reshape(seqs, block, 1) * (
        one_share * gain_own - normal_own * row_mean
    )

    def pieces(array, axis):
        shape = array.shape
        cut = array.reshape(shape[:axis] + (dp, shape[axis] // dp) + shape[axis + 1 :])
        return jnp.moveaxis(cut, axis, 0).reshape(dp, -1)

    smalls = [
        pieces(jnp.sum(dtaps, 0).reshape(3, KW, heads, DK), 3),
        pieces(grad_beta, 0),
        pieces(headgain_sum, 0),
        pieces(mixgain_sum, 0),
        pieces(grad_mlpgain, 0),
    ]
    everyone = lax.all_gather(jnp.concatenate(smalls, 1).astype(bf16), "dp")
    mine = jnp.sum(
        lax.dynamic_index_in_dim(everyone, place, 1, keepdims=False).astype(f32), 0
    )
    sum_conv, sum_beta, sum_head, sum_mix, sum_mlp = unpack(
        mine,
        [conv_weight.shape, w_beta.shape, head_gain.shape, mixer_gain.shape, mlp_gain.shape],
    )
    sum_cat = sum_cat.astype(f32)
    grad_qkv = jnp.stack([sum_cat[:, i * inner : (i + 1) * inner] for i in range(3)])
    return (
        mixed_out,
        tokens_grad.astype(bf16),
        grad_qkv,
        sum_conv,
        sum_beta,
        sum_cat[:, 3 * inner :],
        sum_head,
        sum_out.astype(f32),
        sum_mix,
        sum_mlp,
        sum_gateup.astype(f32),
        sum_down.astype(f32),
    )


def solution(mesh):
    return jax.shard_map(
        body,
        mesh=mesh,
        in_specs=(
            P(None, "dp", "mp"),
            P(None, "dp", None),
            P(None, "dp"),
            P(),
            P(None, "dp", "mp"),
            P(None, None, "mp", "dp"),
            P("dp", "mp"),
            P("dp", "mp"),
            P("dp"),
            P("mp", "dp"),
            P("dp"),
            P("dp"),
            P(None, "dp", "mp"),
            P("mp", "dp"),
        ),
        out_specs=(
            P(None, "dp", "mp"),
            P(None, "dp", "mp"),
            P(None, "dp", "mp"),
            P(None, None, "mp", "dp"),
            P("dp", "mp"),
            P("dp", "mp"),
            P("dp"),
            P("mp", "dp"),
            P("dp"),
            P("dp"),
            P(None, "dp", "mp"),
            P("mp", "dp"),
        ),
        check_vma=False,
    )
```

```python
import jax
import jax.numpy as jnp
from jax import lax
from jax.experimental import pallas as pl
from jax.experimental.pallas import tpu as pltpu
from jax.sharding import PartitionSpec as P

DK = 128
KW = 4
PAD = 8

eps_norm = 1e-06
eps_unit = 1e-06

f32 = jnp.float32
bf16 = jnp.bfloat16


def split(v):
    if v.dtype == bf16:
        return v, None
    high = v.astype(bf16)
    return high, (v - high.astype(f32)).astype(bf16)


def mm(a, b, ca=1, cb=0, passes=3):
    def one(x, y):
        return lax.dot_general(x, y, (((ca,), (cb,)), ((), ())), preferred_element_type=f32)

    if passes == 1:
        return one(a.astype(bf16), b.astype(bf16))
    (ah, al), (bh, bl) = split(a), split(b)
    out = one(ah, bh)
    if bl is not None:
        out = out + one(ah, bl)
    if al is not None:
        out = out + one(al, bh)
    return out


def places(rows, cols):
    return (
        lax.broadcasted_iota(jnp.int32, (rows, cols), 0),
        lax.broadcasted_iota(jnp.int32, (rows, cols), 1),
    )


def unit_lower_inverses(blocks):
    size = blocks[0].shape[0]
    if size > 128:
        half = size // 2
        parts = unit_lower_inverses(
            [a[:half, :half] for a in blocks] + [a[half:, half:] for a in blocks]
        )
        firsts, seconds = parts[: len(blocks)], parts[len(blocks) :]
        inner = [mm(a[half:, :half], x) for a, x in zip(blocks, firsts)]
        lower = [-mm(x, y) for x, y in zip(seconds, inner)]
        zero = jnp.zeros((half, half), f32)
        return [
            jnp.concatenate(
                [jnp.concatenate([x, zero], 1), jnp.concatenate([y, z], 1)], 0
            )
            for x, y, z in zip(firsts, lower, seconds)
        ]
    rows, cols = places(size, size)
    eye = (rows == cols).astype(f32)
    level = 0
    inverses = None
    while (1 << level) < size:
        mask = (
            ((rows >> (level + 1)) == (cols >> (level + 1)))
            & (((rows >> level) & 1) == 1)
            & (((cols >> level) & 1) == 0)
        ).astype(f32)
        lows = [a * mask for a in blocks]
        if level == 0:
            inverses = [eye - low for low in lows]
        else:
            inner = [mm(low, x) for low, x in zip(lows, inverses)]
            inverses = [x - mm(x, y) for x, y in zip(inverses, inner)]
        level += 1
    return inverses


def head_slice(h):
    return slice(h * DK, (h + 1) * DK)


def convolve(rows, before, taps, i, h, inner):
    lanes = slice(i * inner + h * DK, i * inner + (h + 1) * DK)
    own = rows[:, lanes].astype(bf16).astype(f32)
    ext = jnp.concatenate([before[:, lanes], own], 0)
    length = own.shape[0]
    shifts = [ext[PAD - KW + 1 + j : PAD - KW + 1 + j + length] for j in range(KW)]
    out = None
    for j in range(KW):
        tap = taps[i * KW + j : i * KW + j + 1, head_slice(h)]
        out = tap * shifts[j] if out is None else out + tap * shifts[j]
    sig = jax.nn.sigmoid(out)
    return shifts, out, sig, out * sig


def unit(acts):
    inv = lax.rsqrt(jnp.sum(acts * acts, -1, keepdims=True) + eps_unit)
    return acts * inv, inv


def rule_inputs(rows, before, taps, h, inner):
    parts = [convolve(rows, before, taps, i, h, inner) for i in range(3)]
    q, q_inv = unit(parts[0][3])
    k, k_inv = unit(parts[1][3])
    return parts, (q, q_inv), (k, k_inv), parts[2][3]


def pre_kernel(cat_ref, before_ref, taps_ref, beta_ref, x_ref, wu_ref, qo_ref, to_ref):
    heads = to_ref.shape[1]
    inner = heads * DK
    rows, before, taps = cat_ref[0], before_ref[0], taps_ref[...]
    length = rows.shape[0]
    r, c = places(length, length)
    strict = (r > c).astype(f32)
    full = (r >= c).astype(f32)
    saved, blocks = [], []
    for h in range(heads):
        _, (q, _), (k, _), v = rule_inputs(rows, before, taps, h, inner)
        q, k, v = q.astype(bf16), k.astype(bf16), v.astype(bf16)
        beta = beta_ref[0, :, h : h + 1]
        gram = mm(k, k, 1, 1)
        blocks.append(beta * gram * strict)
        saved.append((q, k, v, beta))
    inverses = unit_lower_inverses(blocks)
    r, c = places(DK, DK)
    eye = (r == c).astype(f32)
    for h in range(heads):
        q, k, v, beta = saved[h]
        x = inverses[h]
        x_ref[0, h] = x
        kv = jnp.concatenate([k.astype(f32), v.astype(f32)], 1) * beta
        wu = mm(x, kv)
        wu_ref[0, h] = wu
        scores = mm(q, k, 1, 1) * full
        pwu = mm(scores, wu)
        qo_ref[0, h, :, :DK] = q.astype(f32) - pwu[:, :DK]
        qo_ref[0, h, :, DK:] = pwu[:, DK:]
        kwu = mm(k, wu, 0, 0)
        to_ref[0, h, :, :DK] = (eye - kwu[:, :DK]).astype(bf16)
        to_ref[0, h, :, DK:] = kwu[:, DK:].astype(bf16)


def mix_kernel(*refs):
    near, (qo_ref, cat_ref, gain_ref, normed_ref, rule_ref, state_ref) = refs[:-6], refs[-6:]
    heads = state_ref.shape[1]
    inner = heads * DK
    for h in range(heads):
        state = jnp.zeros((DK, DK), f32)
        for ref in reversed(near):
            state = mm(ref[0, h, :, :DK], state) + ref[0, h, :, DK:].astype(f32)
        state_ref[0, h] = state
        qo = qo_ref[0, h]
        out = (mm(qo[:, :DK], state) + qo[:, DK:]) * DK ** (-0.5)
        rule_ref[0, :, head_slice(h)] = out
        gate = cat_ref[0, :, 3 * inner + h * DK : 3 * inner + (h + 1) * DK]
        factor = lax.rsqrt(jnp.mean(out * out, -1, keepdims=True) + eps_norm)
        normed = out * factor * gain_ref[...] * (gate * jax.nn.sigmoid(gate))
        normed_ref[0, :, head_slice(h)] = normed.astype(bf16)


def gate_back_kernel(
    grad_ref, rule_ref, cat_ref, gain_ref, qo_ref, drule_ref, dgate_ref, dgain_ref, direct_ref
):
    heads = direct_ref.shape[1]
    inner = heads * DK
    total = jnp.zeros((1, DK), f32)
    for h in range(heads):
        grad = grad_ref[0, :, head_slice(h)]
        out = rule_ref[0, :, head_slice(h)]
        gate = cat_ref[0, :, 3 * inner + h * DK : 3 * inner + (h + 1) * DK]
        gain = gain_ref[...]
        factor = lax.rsqrt(jnp.mean(out * out, -1, keepdims=True) + eps_norm)
        n = out * factor
        sig = jax.nn.sigmoid(gate)
        silu = gate * sig
        gg = grad * gain
        dn = gg * silu
        drule = factor * (dn - n * jnp.mean(dn * n, -1, keepdims=True))
        drule_ref[0, :, head_slice(h)] = drule
        dgate = gg * n * sig * (1.0 + gate * (1.0 - sig))
        dgate_ref[0, :, head_slice(h)] = dgate.astype(bf16)
        total = total + jnp.sum(grad * n * silu, 0, keepdims=True)
        direct = mm(qo_ref[0, h, :, :DK], drule, 0, 0) * DK ** (-0.5)
        direct_ref[0, h] = direct.astype(bf16)
    dgain_ref[0] = total


def back_kernel(*refs):
    (
        cat_ref,
        before_ref,
        taps_ref,
        beta_ref,
        x_ref,
        wu_ref,
        state_ref,
        drule_ref,
        dgate_ref,
    ) = refs[:9]
    dcat_ref, last_ref, first_ref, dtaps_ref, dlogit_ref = refs[-5:]
    others = refs[9:-5]
    count = (len(others) + 1) // 2
    directs, nexts = others[:count], others[count:]
    heads = state_ref.shape[1]
    inner = heads * DK
    rows, before, taps = cat_ref[0], before_ref[0], taps_ref[...]
    length = rows.shape[0]
    r, c = places(length, length)
    strict = (r > c).astype(f32)
    full = (r >= c).astype(f32)
    zeros = jnp.zeros((PAD, DK), f32)
    for h in range(heads):
        parts, (qu, q_inv), (ku, k_inv), vu = rule_inputs(rows, before, taps, h, inner)
        q, k, v = qu.astype(bf16), ku.astype(bf16), vu.astype(bf16)
        beta = beta_ref[0, :, h : h + 1]
        leave = jnp.zeros((DK, DK), f32)
        for j in reversed(range(count)):
            here = directs[j][0, h].astype(f32)
            leave = here if j == count - 1 else mm(nexts[j][0, h, :, :DK], leave, 0, 0) + here
        state = state_ref[0, h]
        wu = wu_ref[0, h]
        u = wu[:, DK:] - mm(wu[:, :DK], state)
        resid = v.astype(f32) - mm(k, state)
        dout = drule_ref[0, :, head_slice(h)] * DK ** (-0.5)
        gram = mm(k, k, 1, 1)
        scores = mm(q, k, 1, 1) * full
        du = mm(scores, dout, 0, 0) + mm(k, leave)
        y = mm(x_ref[0, h], du, 0, 0)
        by = beta * y
        da = -(mm(y, u, 1, 1) * strict)
        dbeta = jnp.sum(y * resid, -1, keepdims=True) + jnp.sum(da * gram, -1, keepdims=True)
        dgram = beta * da
        dscores = mm(dout, u, 1, 1) * full
        dq = mm(dout, state, 1, 1) + mm(dscores, k)
        dk = (
            mm(dgram, k)
            + mm(dgram, k, 0, 0)
            + mm(dscores, q, 0, 0)
            + mm(u, leave, 1, 1)
            - mm(by, state, 1, 1)
        )
        dlogit_ref[0, :, h : h + 1] = (dbeta * beta * (1.0 - beta)).astype(bf16)
        dq = (dq - qu * jnp.sum(qu * dq, -1, keepdims=True)) * q_inv
        dk = (dk - ku * jnp.sum(ku * dk, -1, keepdims=True)) * k_inv
        for i, dact in enumerate((dq, dk, by)):
            shifts, out, sig, _ = parts[i]
            dconv = dact * sig * (1.0 + out * (1.0 - sig))
            ext = jnp.concatenate([zeros, dconv, zeros], 0)
            total = None
            for j in range(KW):
                at = i * KW + j
                dtaps_ref[0, at : at + 1, head_slice(h)] = jnp.sum(
                    dconv * shifts[j], 0, keepdims=True
                )
                tap = taps[at : at + 1, head_slice(h)]
                term = tap * ext[KW - 1 - j : KW - 1 - j + PAD + length]
                total = term if total is None else total + term
            lanes = slice(i * inner + h * DK, i * inner + (h + 1) * DK)
            first_ref[0, :, lanes] = total[:PAD]
            last_ref[0, :, lanes] = total[length:]
            dcat_ref[0, :, lanes] = total[PAD:].astype(bf16)
    dcat_ref[0, :, 3 * inner :] = dgate_ref[0]


def per_sequence(kernel, ins, outs, shared=()):
    seqs = outs[0].shape[0]

    def spec(shape, whole):
        if whole:
            return pl.BlockSpec(shape, lambda s: (0,) * len(shape))
        return pl.BlockSpec((1,) + tuple(shape[1:]), lambda s: (s,) + (0,) * (len(shape) - 1))

    return pl.pallas_call(
        kernel,
        grid=(seqs,),
        in_specs=[spec(a.shape, n in shared) for n, a in enumerate(ins)],
        out_specs=[spec(o.shape, False) for o in outs],
        out_shape=outs,
        compiler_params=pltpu.CompilerParams(vmem_limit_bytes=48 * 2**20),
    )(*ins)


def shape_of(shape, dtype):
    return jax.ShapeDtypeStruct(shape, dtype)


def shifted(array, axis, by):
    devices = lax.axis_size(axis)
    pairs = [(i, i + by) for i in range(devices) if 0 <= i + by < devices]
    return lax.ppermute(array, axis, pairs)


def swap(array, bit):
    return lax.ppermute(array, "dp", [(i, i ^ bit) for i in range(4)])


def first_hop(own):
    return swap(own, 1), swap(own, 2)


def second_hop(hop):
    by_one, by_two = hop
    half = by_one.shape[0] // 2
    return swap(by_one[:half], 2), swap(by_two[half:], 1)


def together(own, hop, diagonal, axis):
    return jnp.concatenate([own, hop[0], hop[1], jnp.concatenate(diagonal, 0)], axis)


def cut(array, axis):
    return jnp.split(array, 4, axis)


def forward_sums(pieces):
    own, one, two, far = pieces
    half = far.shape[0] // 2
    low = swap(far[:half], 1)
    high = swap(far[half:], 2)

    def add(a, b):
        return (a.astype(f32) + b.astype(f32)).astype(bf16)

    one = jnp.concatenate([one[:half], add(one[half:], high)], 0)
    two = jnp.concatenate([add(two[:half], low), two[half:]], 0)
    return own, one, two


def finish_sums(parts):
    own, one, two = parts
    return own.astype(f32) + swap(one, 1).astype(f32) + swap(two, 2).astype(f32)


def pack(parts):
    return jnp.concatenate([p.reshape(-1) for p in parts])


def unpack(flat, shapes):
    out, at = [], 0
    for shape in shapes:
        size = 1
        for n in shape:
            size *= n
        out.append(flat[..., at : at + size].reshape(flat.shape[:-1] + tuple(shape)))
        at += size
    return out


def padded(flat, multiple=1024):
    return jnp.pad(flat, (0, -flat.shape[0] % multiple))


def rms_factor(values):
    return lax.rsqrt(jnp.mean(values * values, -1, keepdims=True) + eps_norm)


def body(
    tokens,
    out_grad,
    domain,
    group_weight,
    w_qkv,
    conv_weight,
    w_beta,
    w_outgate,
    head_gain,
    w_out,
    mixer_gain,
    mlp_gain,
    w_gateup,
    w_down,
):
    dp = lax.axis_size("dp")
    place = lax.axis_index("dp")
    seqs, block, local_width = tokens.shape
    count_rows = seqs * block
    heads = conv_weight.shape[2]
    inner = heads * DK
    column = lax.axis_index("mp") * local_width
    near_four = dp == 4

    def blocks_about(array, axis):
        if not near_four:
            return array
        size = array.shape[axis] // 4
        return jnp.concatenate(
            [lax.dynamic_slice_in_dim(array, (place ^ k) * size, size, axis) for k in range(4)],
            axis,
        )

    onehot = (domain[..., None] == jnp.arange(3, dtype=jnp.int32)).astype(f32)
    own_counts = jnp.sum(onehot, axis=(0, 1))
    high = jnp.floor(own_counts / 128.0)
    digits = jnp.concatenate([high, own_counts - 128.0 * high]).astype(bf16)
    small = [w_beta, conv_weight, head_gain, mixer_gain, mlp_gain, digits]
    gathered = lax.all_gather(padded(pack(small)), "dp")
    g_beta, g_conv, g_head, g_mix, g_mlp, g_digits = unpack(gathered, [a.shape for a in small])
    full_beta = g_beta.reshape(-1, heads)
    full_conv = jnp.moveaxis(g_conv, 0, 3).reshape(3 * KW, inner).astype(f32)
    gain_head = g_head.reshape(1, DK).astype(f32)
    full_beta = blocks_about(full_beta, 0)
    gain_one = blocks_about(g_mix.reshape(-1).astype(f32), 0)
    gain_two = blocks_about(g_mlp.reshape(-1).astype(f32), 0)
    sums = jnp.sum(g_digits.astype(f32), 0)
    counts = 128.0 * sums[:3] + sums[3:]

    rows = lax.all_gather(tokens, "mp", axis=2, tiled=True)
    cat_own = jnp.concatenate([w_qkv[0], w_qkv[1], w_qkv[2], w_outgate], 1)
    if near_four:
        cat_hop = first_hop(cat_own)
        (own_out, own_gateup, own_down), cat_hop = lax.optimization_barrier(
            ((w_out, w_gateup, w_down), cat_hop)
        )
        full_cat = together(cat_own, cat_hop, second_hop(cat_hop), 0)
        out_hop = first_hop(own_out)
        gateup_hop = first_hop(own_gateup)
        down_hop = first_hop(own_down)
        full_out = together(own_out, out_hop, second_hop(out_hop), 1)
        full_gateup = together(own_gateup, gateup_hop, second_hop(gateup_hop), 1)
        full_down = together(own_down, down_hop, second_hop(down_hop), 1)
    else:
        full_cat = lax.all_gather(cat_own, "dp", axis=0, tiled=True)
        full_out = lax.all_gather(w_out, "dp", axis=1, tiled=True)
        full_gateup = lax.all_gather(w_gateup, "dp", axis=1, tiled=True)
        full_down = lax.all_gather(w_down, "dp", axis=1, tiled=True)
    rows = blocks_about(rows, 2)

    width = rows.shape[2]
    rows_f = rows.astype(f32).reshape(count_rows, width)
    scale_one = rms_factor(rows_f)
    hidden_one = (rows_f * scale_one * gain_one).astype(bf16)
    cat = jnp.dot(hidden_one, full_cat, preferred_element_type=f32)
    cat = cat.reshape(seqs, block, 4 * inner)
    tail = cat[:, block - PAD :, : 3 * inner].astype(bf16)
    before = shifted(tail, "dp", 1).astype(f32)
    logits = jnp.dot(hidden_one, full_beta, preferred_element_type=f32)
    betas = jax.nn.sigmoid(logits).reshape(seqs, block, heads)

    pair = (seqs, heads)
    inverse, wu, qo, to = per_sequence(
        pre_kernel,
        [cat, before, full_conv, betas],
        [
            shape_of(pair + (block, block), f32),
            shape_of(pair + (block, 2 * DK), f32),
            shape_of(pair + (block, 2 * DK), f32),
            shape_of(pair + (DK, 2 * DK), bf16),
        ],
        shared=(2,),
    )
    near = [shifted(to, "dp", c) for c in range(1, dp)]
    normed, rule, state = per_sequence(
        mix_kernel,
        near + [qo, cat, gain_head],
        [
            shape_of((seqs, block, inner), bf16),
            shape_of((seqs, block, inner), f32),
            shape_of(pair + (DK, DK), f32),
        ],
        shared=(len(near) + 2,),
    )
    normed = normed.reshape(count_rows, inner)
    mixer_part = jnp.dot(normed, full_out, preferred_element_type=f32)
    mixer_total = lax.psum(mixer_part.astype(bf16), "mp").astype(f32)
    middle = rows_f + mixer_total
    scale_two = rms_factor(middle)
    normal_two = middle * scale_two
    hidden_two = (normal_two * gain_two).astype(bf16)
    gate_up = jnp.einsum("td,idf->itf", hidden_two, full_gateup, preferred_element_type=f32)
    gate_act, up_act = (gate_up[0], gate_up[1])
    sigmoid_gate = jax.nn.sigmoid(gate_act)
    silu_gate = gate_act * sigmoid_gate
    hidden_mlp = (silu_gate * up_act).astype(bf16)

    table = group_weight * (domain.shape[0] * domain.shape[1] * dp) / counts
    factor = jnp.sum(onehot * table, -1)
    cotangent = (blocks_about(out_grad, 2).astype(f32) * factor[..., None]).astype(bf16).reshape(count_rows, width)
    grad_hidden = jnp.einsum("td,fd->tf", cotangent, full_down, preferred_element_type=f32)
    grad_gate = grad_hidden * up_act * sigmoid_gate * (1.0 + gate_act * (1.0 - sigmoid_gate))
    grad_pair = jnp.stack([grad_gate, grad_hidden * silu_gate]).astype(bf16)
    grad_two_part = jnp.einsum("itf,idf->td", grad_pair, full_gateup, preferred_element_type=f32)
    grad_two = lax.psum(grad_two_part.astype(bf16), "mp")

    down_part = jnp.dot(hidden_mlp, full_down, preferred_element_type=f32)
    grad_down = jnp.einsum("tf,td->fd", hidden_mlp, cotangent, preferred_element_type=f32)
    grad_gateup = jnp.einsum("td,itf->idf", hidden_two, grad_pair, preferred_element_type=f32)
    grad_gateup, grad_down, down_part = (
        grad_gateup.astype(bf16),
        grad_down.astype(bf16),
        blocks_about(down_part.astype(bf16).reshape(seqs, block, width), 2),
    )
    if near_four:
        gateup_sums = forward_sums(cut(grad_gateup, 1))
        down_sums = forward_sums(cut(grad_down, 1))
        grad_two, gateup_sums, down_sums, down_part = lax.optimization_barrier(
            (grad_two, gateup_sums, down_sums, down_part)
        )
        sum_gateup = finish_sums(gateup_sums)
        sum_down = finish_sums(down_sums)
    else:
        sum_gateup = lax.psum_scatter(grad_gateup, "dp", scatter_dimension=1, tiled=True)
        sum_down = lax.psum_scatter(grad_down, "dp", scatter_dimension=1, tiled=True)
    grad_two = grad_two.astype(f32)
    mlp_share = lax.psum_scatter(down_part, "mp", scatter_dimension=2, tiled=True).astype(f32)

    def own(array):
        whole = blocks_about(array.reshape(seqs, block, width), 2)
        return lax.dynamic_slice_in_dim(whole, column, local_width, 2)

    mixed_out = (own(middle) + mlp_share).astype(bf16)

    scaled = grad_two * gain_two
    grad_middle = cotangent.astype(f32) + scale_two * (
        scaled - normal_two * jnp.mean(scaled * normal_two, -1, keepdims=True)
    )
    grad_mlpgain = jnp.sum(grad_two * normal_two, 0)
    grad_mix = grad_middle.astype(bf16)
    grad_normed = jnp.einsum("td,cd->tc", grad_mix, full_out, preferred_element_type=f32)
    grad_outproj = jnp.einsum("tc,td->cd", normed, grad_mix, preferred_element_type=f32)
    drule, dgate, dgain, direct = per_sequence(
        gate_back_kernel,
        [grad_normed.reshape(seqs, block, inner), rule, cat, gain_head, qo],
        [
            shape_of((seqs, block, inner), f32),
            shape_of((seqs, block, inner), bf16),
            shape_of((seqs, 1, DK), f32),
            shape_of(pair + (DK, DK), bf16),
        ],
        shared=(3,),
    )
    directs = [shifted(direct, "dp", -c) for c in range(1, dp)]
    nexts = [shifted(to, "dp", -c) for c in range(1, dp - 1)]
    dcat, last, first, dtaps, dlogits = per_sequence(
        back_kernel,
        [cat, before, full_conv, betas, inverse, wu, state, drule, dgate] + directs + nexts,
        [
            shape_of((seqs, block, 4 * inner), bf16),
            shape_of((seqs, PAD, 3 * inner), f32),
            shape_of((seqs, PAD, 3 * inner), f32),
            shape_of((seqs, 3 * KW, inner), f32),
            shape_of((seqs, block, heads), bf16),
        ],
        shared=(2,),
    )
    later = shifted(first, "dp", -1)
    dcat = lax.dynamic_update_slice(dcat, (last + later).astype(bf16), (0, block - PAD, 0))
    dcat = dcat.reshape(count_rows, 4 * inner)
    dlogits = dlogits.reshape(count_rows, heads)
    grad_one_part = jnp.einsum("tc,dc->td", dcat, full_cat, preferred_element_type=f32)
    grad_one_part = grad_one_part + jnp.einsum(
        "th,dh->td", dlogits, full_beta, preferred_element_type=f32
    )
    normal_one = rows_f * scale_one
    row_part = jnp.sum(grad_one_part * gain_one * normal_one, -1)
    gain_part = jnp.sum(grad_one_part * normal_one, 0)
    one_share = lax.psum_scatter(
        blocks_about(grad_one_part.astype(bf16).reshape(seqs, block, width), 2),
        "mp",
        scatter_dimension=2,
        tiled=True,
    ).astype(f32)
    stats = [row_part, gain_part, jnp.sum(dgain, (0, 1))]
    stat_sum = jnp.sum(lax.all_gather(pack(stats), "mp"), 0)
    row_sum, mixgain_sum, headgain_sum = unpack(stat_sum, [a.shape for a in stats])

    grad_cat = jnp.einsum("td,tc->dc", hidden_one, dcat, preferred_element_type=f32)
    grad_beta = jnp.einsum("td,th->dh", hidden_one, dlogits, preferred_element_type=f32)
    grad_cat, grad_outproj = grad_cat.astype(bf16), grad_outproj.astype(bf16)
    if near_four:
        sum_cat = finish_sums(forward_sums(cut(grad_cat, 0)))
        sum_out = finish_sums(forward_sums(cut(grad_outproj, 1)))
    else:
        sum_cat = lax.psum_scatter(grad_cat, "dp", scatter_dimension=0, tiled=True)
        sum_out = lax.psum_scatter(grad_outproj, "dp", scatter_dimension=1, tiled=True)

    row_mean = (row_sum / width).reshape(seqs, block, 1)
    gain_own = lax.dynamic_slice_in_dim(blocks_about(gain_one, 0), column, local_width, 0)
    normal_own = tokens.astype(f32) * scale_one.reshape(seqs, block, 1)
    tokens_grad = own(grad_middle) + scale_one.reshape(seqs, block, 1) * (
        one_share * gain_own - normal_own * row_mean
    )

    def pieces(array, axis):
        shape = array.shape
        cut = array.reshape(shape[:axis] + (dp, shape[axis] // dp) + shape[axis + 1 :])
        return jnp.moveaxis(cut, axis, 0).reshape(dp, -1)

    smalls = [
        pieces(jnp.sum(dtaps, 0).reshape(3, KW, heads, DK), 3),
        pieces(blocks_about(grad_beta, 0), 0),
        pieces(headgain_sum, 0),
        pieces(blocks_about(mixgain_sum, 0), 0),
        pieces(blocks_about(grad_mlpgain, 0), 0),
    ]
    everyone = lax.all_gather(jnp.concatenate(smalls, 1).astype(bf16), "dp")
    mine = jnp.sum(
        lax.dynamic_index_in_dim(everyone, place, 1, keepdims=False).astype(f32), 0
    )
    sum_conv, sum_beta, sum_head, sum_mix, sum_mlp = unpack(
        mine,
        [conv_weight.shape, w_beta.shape, head_gain.shape, mixer_gain.shape, mlp_gain.shape],
    )
    sum_cat = sum_cat.astype(f32)
    grad_qkv = jnp.stack([sum_cat[:, i * inner : (i + 1) * inner] for i in range(3)])
    return (
        mixed_out,
        tokens_grad.astype(bf16),
        grad_qkv,
        sum_conv,
        sum_beta,
        sum_cat[:, 3 * inner :],
        sum_head,
        sum_out.astype(f32),
        sum_mix,
        sum_mlp,
        sum_gateup.astype(f32),
        sum_down.astype(f32),
    )


def solution(mesh):
    return jax.shard_map(
        body,
        mesh=mesh,
        in_specs=(
            P(None, "dp", "mp"),
            P(None, "dp", None),
            P(None, "dp"),
            P(),
            P(None, "dp", "mp"),
            P(None, None, "mp", "dp"),
            P("dp", "mp"),
            P("dp", "mp"),
            P("dp"),
            P("mp", "dp"),
            P("dp"),
            P("dp"),
            P(None, "dp", "mp"),
            P("mp", "dp"),
        ),
        out_specs=(
            P(None, "dp", "mp"),
            P(None, "dp", "mp"),
            P(None, "dp", "mp"),
            P(None, None, "mp", "dp"),
            P("dp", "mp"),
            P("dp", "mp"),
            P("dp"),
            P("mp", "dp"),
            P("dp"),
            P("dp"),
            P(None, "dp", "mp"),
            P("mp", "dp"),
        ),
        check_vma=False,
    )
```

```python
import jax
import jax.numpy as jnp
from jax import lax
from jax.experimental import pallas as pl
from jax.experimental.pallas import tpu as pltpu
from jax.sharding import PartitionSpec as P

DK = 128
KW = 4
PAD = 8

eps_norm = 1e-06
eps_unit = 1e-06

f32 = jnp.float32
bf16 = jnp.bfloat16


def split(v):
    if v.dtype == bf16:
        return v, None
    high = v.astype(bf16)
    return high, (v - high.astype(f32)).astype(bf16)


def mm(a, b, ca=1, cb=0, passes=3):
    def one(x, y):
        return lax.dot_general(x, y, (((ca,), (cb,)), ((), ())), preferred_element_type=f32)

    if passes == 1:
        return one(a.astype(bf16), b.astype(bf16))
    (ah, al), (bh, bl) = split(a), split(b)
    out = one(ah, bh)
    if bl is not None:
        out = out + one(ah, bl)
    if al is not None:
        out = out + one(al, bh)
    return out


def places(rows, cols):
    return (
        lax.broadcasted_iota(jnp.int32, (rows, cols), 0),
        lax.broadcasted_iota(jnp.int32, (rows, cols), 1),
    )


def unit_lower_inverses(blocks):
    size = blocks[0].shape[0]
    if size > 128:
        half = size // 2
        parts = unit_lower_inverses(
            [a[:half, :half] for a in blocks] + [a[half:, half:] for a in blocks]
        )
        firsts, seconds = parts[: len(blocks)], parts[len(blocks) :]
        inner = [mm(a[half:, :half], x) for a, x in zip(blocks, firsts)]
        lower = [-mm(x, y) for x, y in zip(seconds, inner)]
        zero = jnp.zeros((half, half), f32)
        return [
            jnp.concatenate(
                [jnp.concatenate([x, zero], 1), jnp.concatenate([y, z], 1)], 0
            )
            for x, y, z in zip(firsts, lower, seconds)
        ]
    rows, cols = places(size, size)
    eye = (rows == cols).astype(f32)
    level = 0
    inverses = None
    while (1 << level) < size:
        mask = (
            ((rows >> (level + 1)) == (cols >> (level + 1)))
            & (((rows >> level) & 1) == 1)
            & (((cols >> level) & 1) == 0)
        ).astype(f32)
        lows = [a * mask for a in blocks]
        if level == 0:
            inverses = [eye - low for low in lows]
        else:
            inner = [mm(low, x) for low, x in zip(lows, inverses)]
            inverses = [x - mm(x, y) for x, y in zip(inverses, inner)]
        level += 1
    return inverses


def head_slice(h):
    return slice(h * DK, (h + 1) * DK)


def convolve(rows, before, taps, i, h):
    own = rows[i, 0, :, head_slice(h)].astype(f32)
    ext = jnp.concatenate([before[i, 0, :, head_slice(h)], own], 0)
    length = own.shape[0]
    shifts = [ext[PAD - KW + 1 + j : PAD - KW + 1 + j + length] for j in range(KW)]
    out = None
    for j in range(KW):
        tap = taps[i * KW + j : i * KW + j + 1, head_slice(h)]
        out = tap * shifts[j] if out is None else out + tap * shifts[j]
    sig = jax.nn.sigmoid(out)
    return shifts, out, sig, out * sig


def unit(acts):
    inv = lax.rsqrt(jnp.sum(acts * acts, -1, keepdims=True) + eps_unit)
    return acts * inv, inv


def rule_inputs(rows, before, taps, h):
    parts = [convolve(rows, before, taps, i, h) for i in range(3)]
    q, q_inv = unit(parts[0][3])
    k, k_inv = unit(parts[1][3])
    return parts, (q, q_inv), (k, k_inv), parts[2][3]


def pre_kernel(proj_ref, before_ref, taps_ref, beta_ref, x_ref, wu_ref, qo_ref, to_ref):
    heads = to_ref.shape[1]
    taps = taps_ref[...]
    length = proj_ref.shape[2]
    r, c = places(length, length)
    strict = (r > c).astype(f32)
    full = (r >= c).astype(f32)
    saved, blocks = [], []
    for h in range(heads):
        _, (q, _), (k, _), v = rule_inputs(proj_ref, before_ref, taps, h)
        q, k, v = q.astype(bf16), k.astype(bf16), v.astype(bf16)
        beta = beta_ref[0, :, h : h + 1]
        gram = mm(k, k, 1, 1)
        blocks.append(beta * gram * strict)
        saved.append((q, k, v, beta))
    inverses = unit_lower_inverses(blocks)
    r, c = places(DK, DK)
    eye = (r == c).astype(f32)
    for h in range(heads):
        q, k, v, beta = saved[h]
        x = inverses[h]
        x_ref[0, h] = x
        kv = jnp.concatenate([k.astype(f32), v.astype(f32)], 1) * beta
        wu = mm(x, kv)
        wu_ref[0, h] = wu
        scores = mm(q, k, 1, 1) * full
        pwu = mm(scores, wu)
        qo_ref[0, h, :, :DK] = q.astype(f32) - pwu[:, :DK]
        qo_ref[0, h, :, DK:] = pwu[:, DK:]
        kwu = mm(k, wu, 0, 0)
        to_ref[0, h, :, :DK] = (eye - kwu[:, :DK]).astype(bf16)
        to_ref[0, h, :, DK:] = kwu[:, DK:].astype(bf16)


def mix_kernel(*refs):
    near, (qo_ref, gate_ref, gain_ref, normed_ref, rule_ref, state_ref) = refs[:-6], refs[-6:]
    heads = state_ref.shape[1]
    for h in range(heads):
        state = jnp.zeros((DK, DK), f32)
        for ref in reversed(near):
            state = mm(ref[0, h, :, :DK], state) + ref[0, h, :, DK:].astype(f32)
        state_ref[0, h] = state
        qo = qo_ref[0, h]
        out = (mm(qo[:, :DK], state) + qo[:, DK:]) * DK ** (-0.5)
        rule_ref[0, :, head_slice(h)] = out
        gate = gate_ref[0, :, head_slice(h)]
        factor = lax.rsqrt(jnp.mean(out * out, -1, keepdims=True) + eps_norm)
        normed = out * factor * gain_ref[...] * (gate * jax.nn.sigmoid(gate))
        normed_ref[0, :, head_slice(h)] = normed.astype(bf16)


def gate_back_kernel(
    grad_ref, rule_ref, gate_ref, gain_ref, qo_ref, drule_ref, dgate_ref, dgain_ref, direct_ref
):
    heads = direct_ref.shape[1]
    total = jnp.zeros((1, DK), f32)
    for h in range(heads):
        grad = grad_ref[0, :, head_slice(h)]
        out = rule_ref[0, :, head_slice(h)]
        gate = gate_ref[0, :, head_slice(h)]
        gain = gain_ref[...]
        factor = lax.rsqrt(jnp.mean(out * out, -1, keepdims=True) + eps_norm)
        n = out * factor
        sig = jax.nn.sigmoid(gate)
        silu = gate * sig
        gg = grad * gain
        dn = gg * silu
        drule = factor * (dn - n * jnp.mean(dn * n, -1, keepdims=True))
        drule_ref[0, :, head_slice(h)] = drule
        dgate = gg * n * sig * (1.0 + gate * (1.0 - sig))
        dgate_ref[0, :, head_slice(h)] = dgate.astype(bf16)
        total = total + jnp.sum(grad * n * silu, 0, keepdims=True)
        direct = mm(qo_ref[0, h, :, :DK], drule, 0, 0) * DK ** (-0.5)
        direct_ref[0, h] = direct.astype(bf16)
    dgain_ref[0] = total


def back_kernel(*refs):
    (
        proj_ref,
        before_ref,
        taps_ref,
        beta_ref,
        x_ref,
        wu_ref,
        state_ref,
        drule_ref,
    ) = refs[:8]
    dproj_ref, last_ref, first_ref, dtaps_ref, dlogit_ref = refs[-5:]
    others = refs[8:-5]
    count = (len(others) + 1) // 2
    directs, nexts = others[:count], others[count:]
    heads = state_ref.shape[1]
    taps = taps_ref[...]
    length = proj_ref.shape[2]
    r, c = places(length, length)
    strict = (r > c).astype(f32)
    full = (r >= c).astype(f32)
    zeros = jnp.zeros((PAD, DK), f32)
    for h in range(heads):
        parts, (qu, q_inv), (ku, k_inv), vu = rule_inputs(proj_ref, before_ref, taps, h)
        q, k, v = qu.astype(bf16), ku.astype(bf16), vu.astype(bf16)
        beta = beta_ref[0, :, h : h + 1]
        leave = jnp.zeros((DK, DK), f32)
        for j in reversed(range(count)):
            here = directs[j][0, h].astype(f32)
            leave = here if j == count - 1 else mm(nexts[j][0, h, :, :DK], leave, 0, 0) + here
        state = state_ref[0, h]
        wu = wu_ref[0, h]
        u = wu[:, DK:] - mm(wu[:, :DK], state)
        resid = v.astype(f32) - mm(k, state)
        dout = drule_ref[0, :, head_slice(h)] * DK ** (-0.5)
        gram = mm(k, k, 1, 1)
        scores = mm(q, k, 1, 1) * full
        du = mm(scores, dout, 0, 0) + mm(k, leave)
        y = mm(x_ref[0, h], du, 0, 0)
        by = beta * y
        da = -(mm(y, u, 1, 1) * strict)
        dbeta = jnp.sum(y * resid, -1, keepdims=True) + jnp.sum(da * gram, -1, keepdims=True)
        dgram = beta * da
        dscores = mm(dout, u, 1, 1) * full
        dq = mm(dout, state, 1, 1) + mm(dscores, k)
        dk = (
            mm(dgram, k)
            + mm(dgram, k, 0, 0)
            + mm(dscores, q, 0, 0)
            + mm(u, leave, 1, 1)
            - mm(by, state, 1, 1)
        )
        dlogit_ref[0, :, h : h + 1] = (dbeta * beta * (1.0 - beta)).astype(bf16)
        dq = (dq - qu * jnp.sum(qu * dq, -1, keepdims=True)) * q_inv
        dk = (dk - ku * jnp.sum(ku * dk, -1, keepdims=True)) * k_inv
        for i, dact in enumerate((dq, dk, by)):
            shifts, out, sig, _ = parts[i]
            dconv = dact * sig * (1.0 + out * (1.0 - sig))
            ext = jnp.concatenate([zeros, dconv, zeros], 0)
            total = None
            for j in range(KW):
                at = i * KW + j
                dtaps_ref[0, at : at + 1, head_slice(h)] = jnp.sum(
                    dconv * shifts[j], 0, keepdims=True
                )
                tap = taps[at : at + 1, head_slice(h)]
                term = tap * ext[KW - 1 - j : KW - 1 - j + PAD + length]
                total = term if total is None else total + term
            first_ref[i, 0, :, head_slice(h)] = total[:PAD]
            last_ref[i, 0, :, head_slice(h)] = total[length:]
            dproj_ref[i, 0, :, head_slice(h)] = total[PAD:].astype(bf16)


def per_sequence(kernel, ins, outs):
    def spec(shape, axis):
        block = tuple(1 if n == axis else size for n, size in enumerate(shape))
        return pl.BlockSpec(block, lambda s: tuple(s if n == axis else 0 for n in range(len(shape))))

    shape, axis = outs[0]
    return pl.pallas_call(
        kernel,
        grid=(shape.shape[axis],),
        in_specs=[spec(a.shape, axis) for a, axis in ins],
        out_specs=[spec(o.shape, axis) for o, axis in outs],
        out_shape=[o for o, _ in outs],
        compiler_params=pltpu.CompilerParams(vmem_limit_bytes=48 * 2**20),
    )(*[a for a, _ in ins])


def shape_of(shape, dtype):
    return jax.ShapeDtypeStruct(shape, dtype)


def shifted(array, axis, by):
    devices = lax.axis_size(axis)
    pairs = [(i, i + by) for i in range(devices) if 0 <= i + by < devices]
    return lax.ppermute(array, axis, pairs)


def tie(value, *before):
    return lax.optimization_barrier((value, before))[0]


def swap(array, bits):
    return lax.ppermute(array, "dp", [(i, i ^ bits) for i in range(4)])


def first_hop(own):
    return swap(own, 1), swap(own, 2)


def second_hop(hop, axis):
    low, high = (jnp.split(part, 2, axis) for part in hop)
    return swap(low[0], 2), swap(high[1], 1)


def together(own, hop, diagonal, axis, split_axis):
    if axis == split_axis:
        return jnp.concatenate([own, *hop, *diagonal], axis)
    return jnp.concatenate([own, *hop, jnp.concatenate(diagonal, split_axis)], axis)


def add(a, b):
    return (a.astype(f32) + b.astype(f32)).astype(bf16)


def sum_first(array, axis, split_axis):
    own, one, two, far = jnp.split(array, 4, axis)
    low, high = jnp.split(far, 2, split_axis)
    low, high = swap(low, 1), swap(high, 2)
    one = jnp.split(one, 2, split_axis)
    two = jnp.split(two, 2, split_axis)
    one = jnp.concatenate([one[0], add(one[1], high)], split_axis)
    two = jnp.concatenate([add(two[0], low), two[1]], split_axis)
    return own, one, two


def sum_second(parts):
    own, one, two = parts
    return own, swap(one, 1), swap(two, 2)


def sum_last(parts):
    own, one, two = parts
    return own.astype(f32) + one.astype(f32) + two.astype(f32)


def pack(parts):
    return jnp.concatenate([p.reshape(-1) for p in parts])


def unpack(flat, shapes):
    out, at = [], 0
    for shape in shapes:
        size = 1
        for n in shape:
            size *= n
        out.append(flat[..., at : at + size].reshape(flat.shape[:-1] + tuple(shape)))
        at += size
    return out


def padded(flat, multiple=1024):
    return jnp.pad(flat, (0, -flat.shape[0] % multiple))


def rms_factor(values):
    return lax.rsqrt(jnp.mean(values * values, -1, keepdims=True) + eps_norm)


def body(
    tokens,
    out_grad,
    domain,
    group_weight,
    w_qkv,
    conv_weight,
    w_beta,
    w_outgate,
    head_gain,
    w_out,
    mixer_gain,
    mlp_gain,
    w_gateup,
    w_down,
):
    dp = lax.axis_size("dp")
    place = lax.axis_index("dp")
    seqs, block, local_width = tokens.shape
    count_rows = seqs * block
    heads = conv_weight.shape[2]
    inner = heads * DK
    column = lax.axis_index("mp") * local_width
    near_four = dp == 4

    def blocks_about(array, axis):
        if not near_four:
            return array
        size = array.shape[axis] // 4
        return jnp.concatenate(
            [lax.dynamic_slice_in_dim(array, (place ^ k) * size, size, axis) for k in range(4)],
            axis,
        )

    def own(array):
        at = column
        if near_four:
            size = width // 4
            at = ((column // size) ^ place) * size + column % size
        return lax.dynamic_slice_in_dim(array.reshape(seqs, block, width), at, local_width, 2)

    onehot = (domain[..., None] == jnp.arange(3, dtype=jnp.int32)).astype(f32)
    own_counts = jnp.sum(onehot, axis=(0, 1))
    high = jnp.floor(own_counts / 128.0)
    digits = jnp.concatenate([high, own_counts - 128.0 * high]).astype(bf16)
    small = [w_beta, conv_weight, head_gain, mixer_gain, mlp_gain, digits]
    packed = padded(pack(small))
    if near_four:
        gathered = jnp.stack([packed] + [swap(packed, bits) for bits in (1, 2, 3)])
    else:
        gathered = lax.all_gather(packed, "dp")
    g_beta, g_conv, g_head, g_mix, g_mlp, g_digits = unpack(gathered, [a.shape for a in small])
    full_beta = g_beta.reshape(-1, heads)
    full_conv = jnp.moveaxis(blocks_about(g_conv, 0), 0, 3).reshape(3 * KW, inner).astype(f32)
    gain_head = blocks_about(g_head, 0).reshape(1, DK).astype(f32)
    gain_one = g_mix.reshape(-1).astype(f32)
    gain_two = g_mlp.reshape(-1).astype(f32)
    sums = jnp.sum(g_digits.astype(f32), 0)
    counts = 128.0 * sums[:3] + sums[3:]

    rows = lax.all_gather(tokens, "mp", axis=2, tiled=True)
    width = rows.shape[2]
    if near_four:
        qkv_hop = first_hop(w_qkv)
        qkv_far = second_hop(qkv_hop, 1)
        full_qkv = together(w_qkv, qkv_hop, qkv_far, 1, 1)
        half = w_out.shape[1] // 2
        pair_own = jnp.stack(
            [w_outgate, jnp.concatenate([w_out[:, :half], w_out[:, half:]], 0)]
        )
        pair_hop = first_hop(tie(pair_own, qkv_hop))
    else:
        full_qkv = lax.all_gather(w_qkv, "dp", axis=1, tiled=True)
    rows = blocks_about(rows, 2)

    rows_f = rows.astype(f32).reshape(count_rows, width)
    scale_one = rms_factor(rows_f)
    hidden_one = (rows_f * scale_one * gain_one).astype(bf16)
    projected = jnp.einsum("td,idc->itc", hidden_one, full_qkv, preferred_element_type=f32)
    projected = projected.astype(bf16).reshape(3, seqs, block, inner)
    before = shifted(projected[:, :, block - PAD :], "dp", 1).astype(f32)
    logits = jnp.dot(hidden_one, full_beta, preferred_element_type=f32)
    betas = jax.nn.sigmoid(logits).reshape(seqs, block, heads)
    if near_four:
        before, pair_hop = lax.optimization_barrier((before, pair_hop))
        pair_far = second_hop(pair_hop, 0)

    square = (seqs, heads, DK, DK)
    inverse, wu, qo, to = per_sequence(
        pre_kernel,
        [(projected, 1), (before, 1), (full_conv, None), (betas, 0)],
        [
            (shape_of((seqs, heads, block, block), f32), 0),
            (shape_of((seqs, heads, block, 2 * DK), f32), 0),
            (shape_of((seqs, heads, block, 2 * DK), f32), 0),
            (shape_of((seqs, heads, DK, 2 * DK), bf16), 0),
        ],
    )
    near = [shifted(to, "dp", c) for c in range(1, dp)]
    if near_four:
        near, pair_far = lax.optimization_barrier((near, pair_far))
        full_outgate = jnp.concatenate(
            [w_outgate, pair_hop[0][0], pair_hop[1][0], pair_far[0][0]], 0
        )
        outs = [pair_hop[0][1], pair_hop[1][1], pair_far[1][0]]
        full_out = jnp.concatenate(
            [w_out] + [part for a in outs for part in jnp.split(a, 2, 0)], 1
        )
    else:
        full_outgate = lax.all_gather(w_outgate, "dp", axis=0, tiled=True)
        full_out = lax.all_gather(w_out, "dp", axis=1, tiled=True)
    gates = jnp.dot(hidden_one, full_outgate, preferred_element_type=f32)
    gates = gates.reshape(seqs, block, inner)
    normed, rule, state = per_sequence(
        mix_kernel,
        [(a, 0) for a in near] + [(qo, 0), (gates, 0), (gain_head, None)],
        [
            (shape_of((seqs, block, inner), bf16), 0),
            (shape_of((seqs, block, inner), f32), 0),
            (shape_of(square, f32), 0),
        ],
    )
    normed = normed.reshape(count_rows, inner)
    mixer_part = jnp.dot(normed, full_out, preferred_element_type=f32).astype(bf16)
    mixer_total = lax.psum(mixer_part, "mp").astype(f32)
    if near_four:
        own_gateup, own_down = tie((w_gateup, w_down), mixer_part)
        gateup_hop = first_hop(own_gateup)
        full_gateup = together(own_gateup, gateup_hop, second_hop(gateup_hop, 0), 1, 0)
        down_hop = first_hop(tie(own_down, gateup_hop))
        full_down = together(own_down, down_hop, second_hop(down_hop, 0), 1, 0)
    else:
        full_gateup = lax.all_gather(w_gateup, "dp", axis=1, tiled=True)
        full_down = lax.all_gather(w_down, "dp", axis=1, tiled=True)
    middle = rows_f + mixer_total
    scale_two = rms_factor(middle)
    normal_two = middle * scale_two
    hidden_two = (normal_two * gain_two).astype(bf16)
    gate_up = jnp.einsum("td,idf->itf", hidden_two, full_gateup, preferred_element_type=f32)
    gate_act, up_act = (gate_up[0], gate_up[1])
    sigmoid_gate = jax.nn.sigmoid(gate_act)
    silu_gate = gate_act * sigmoid_gate
    hidden_mlp = (silu_gate * up_act).astype(bf16)

    table = group_weight * (domain.shape[0] * domain.shape[1] * dp) / counts
    factor = jnp.sum(onehot * table, -1)
    cotangent = (blocks_about(out_grad, 2).astype(f32) * factor[..., None]).astype(bf16)
    cotangent = cotangent.reshape(count_rows, width)
    grad_hidden = jnp.einsum("td,fd->tf", cotangent, full_down, preferred_element_type=f32)
    grad_gate = grad_hidden * up_act * sigmoid_gate * (1.0 + gate_act * (1.0 - sigmoid_gate))
    grad_pair = jnp.stack([grad_gate, grad_hidden * silu_gate]).astype(bf16)
    grad_two_part = jnp.einsum("itf,idf->td", grad_pair, full_gateup, preferred_element_type=f32)
    grad_two_part = grad_two_part.astype(bf16)
    grad_two = lax.psum(grad_two_part, "mp")

    late_pair, late_mlp = tie((grad_pair, hidden_mlp), grad_two_part)
    grad_gateup = jnp.einsum("td,itf->idf", hidden_two, late_pair, preferred_element_type=f32)
    grad_gateup = grad_gateup.astype(bf16)
    grad_down = jnp.einsum("tf,td->fd", late_mlp, cotangent, preferred_element_type=f32)
    grad_down = grad_down.astype(bf16)
    down_part = jnp.dot(late_mlp, full_down, preferred_element_type=f32).astype(bf16)
    down_part = blocks_about(down_part.reshape(seqs, block, width), 2)
    if near_four:
        gateup_sums = sum_second(sum_first(grad_gateup, 1, 0))
        down_sums = sum_first(grad_down, 1, 0)
        grad_two, gateup_sums, down_sums, down_part = lax.optimization_barrier(
            (grad_two, gateup_sums, down_sums, down_part)
        )
        down_sums = sum_second(down_sums)
    grad_two = grad_two.astype(f32)
    mlp_share = lax.psum_scatter(down_part, "mp", scatter_dimension=2, tiled=True).astype(f32)

    scaled = grad_two * gain_two
    grad_middle = cotangent.astype(f32) + scale_two * (
        scaled - normal_two * jnp.mean(scaled * normal_two, -1, keepdims=True)
    )
    grad_mlpgain = jnp.sum(grad_two * normal_two, 0)
    grad_mix = grad_middle.astype(bf16)
    grad_normed = jnp.einsum("td,cd->tc", grad_mix, full_out, preferred_element_type=f32)
    drule, dgate, dgain, direct = per_sequence(
        gate_back_kernel,
        [
            (grad_normed.reshape(seqs, block, inner), 0),
            (rule, 0),
            (gates, 0),
            (gain_head, None),
            (qo, 0),
        ],
        [
            (shape_of((seqs, block, inner), f32), 0),
            (shape_of((seqs, block, inner), bf16), 0),
            (shape_of((seqs, 1, DK), f32), 0),
            (shape_of(square, bf16), 0),
        ],
    )
    directs = [shifted(direct, "dp", -c) for c in range(1, dp)]
    nexts = [shifted(to[..., :DK], "dp", -c) for c in range(1, dp - 1)]
    dgate = dgate.reshape(count_rows, inner)
    late_dgate, late_normed = tie((dgate, normed), direct)
    grad_outgate = jnp.einsum("td,tc->dc", hidden_one, late_dgate, preferred_element_type=f32)
    grad_outgate = grad_outgate.astype(bf16)
    grad_outproj = jnp.einsum("tc,td->cd", late_normed, grad_mix, preferred_element_type=f32)
    grad_outproj = grad_outproj.astype(bf16)
    if near_four:
        directs, down_sums, grad_outgate, grad_outproj = lax.optimization_barrier(
            (directs, down_sums, grad_outgate, grad_outproj)
        )
        parts = [jnp.split(a, 2, 1) for a in jnp.split(grad_outproj, 4, 1)]
        pair_grad = jnp.stack(
            [grad_outgate.reshape(4, -1, inner), jnp.stack([jnp.concatenate(p, 0) for p in parts])],
            1,
        )
        pair_sums = sum_first(pair_grad, 0, 1)
    dproj, last, first, dtaps, dlogits = per_sequence(
        back_kernel,
        [
            (projected, 1),
            (before, 1),
            (full_conv, None),
            (betas, 0),
            (inverse, 0),
            (wu, 0),
            (state, 0),
            (drule, 0),
        ]
        + [(a, 0) for a in directs + nexts],
        [
            (shape_of((3, seqs, block, inner), bf16), 1),
            (shape_of((3, seqs, PAD, inner), f32), 1),
            (shape_of((3, seqs, PAD, inner), f32), 1),
            (shape_of((seqs, 3 * KW, inner), f32), 0),
            (shape_of((seqs, block, heads), bf16), 0),
        ],
    )
    later = shifted(first, "dp", -1)
    if near_four:
        later, pair_sums = lax.optimization_barrier((later, pair_sums))
        pair_sums = sum_second(pair_sums)
    dproj = lax.dynamic_update_slice(dproj, (last + later).astype(bf16), (0, 0, block - PAD, 0))
    dproj = dproj.reshape(3, count_rows, inner)
    dlogits = dlogits.reshape(count_rows, heads)
    grad_one_part = jnp.einsum("itc,idc->td", dproj, full_qkv, preferred_element_type=f32)
    grad_one_part = grad_one_part + jnp.einsum(
        "tc,dc->td", dgate, full_outgate, preferred_element_type=f32
    )
    grad_one_part = grad_one_part + jnp.einsum(
        "th,dh->td", dlogits, full_beta, preferred_element_type=f32
    )
    normal_one = rows_f * scale_one
    row_part = jnp.sum(grad_one_part * gain_one * normal_one, -1)
    gain_part = jnp.sum(grad_one_part * normal_one, 0)
    one_low = blocks_about(grad_one_part.astype(bf16).reshape(seqs, block, width), 2)
    one_share = lax.psum_scatter(one_low, "mp", scatter_dimension=2, tiled=True).astype(f32)
    late_proj, late_logits, late_middle, late_tokens, mlp_share = tie(
        (dproj, dlogits, middle, tokens, mlp_share), one_low
    )
    grad_qkv = jnp.einsum("td,itc->idc", hidden_one, late_proj, preferred_element_type=f32)
    grad_qkv = grad_qkv.astype(bf16)
    if near_four:
        qkv_sums = sum_first(grad_qkv, 1, 1)
    grad_beta = jnp.einsum("td,th->dh", hidden_one, late_logits, preferred_element_type=f32)
    stats = [row_part, gain_part, jnp.sum(dgain, (0, 1))]
    stat_sum = jnp.sum(lax.all_gather(pack(stats), "mp"), 0)
    row_sum, mixgain_sum, headgain_sum = unpack(stat_sum, [a.shape for a in stats])

    def pieces(array, axis, about):
        shape = array.shape
        cut = array.reshape(shape[:axis] + (dp, shape[axis] // dp) + shape[axis + 1 :])
        cut = jnp.moveaxis(cut, axis, 0).reshape(dp, -1)
        return blocks_about(cut, 0) if about else cut

    smalls = jnp.concatenate(
        [
            pieces(jnp.sum(dtaps, 0).reshape(3, KW, heads, DK), 3, True),
            pieces(grad_beta, 0, False),
            pieces(headgain_sum, 0, True),
            pieces(mixgain_sum, 0, False),
            pieces(grad_mlpgain, 0, False),
        ],
        1,
    )
    if near_four:
        mine = smalls[0]
        for bits in (1, 2, 3):
            mine = mine + swap(padded(smalls[bits].astype(bf16)), bits)[: mine.shape[0]].astype(f32)
        sum_qkv = sum_last(sum_second(qkv_sums))
        sum_gateup, sum_down, sum_pair = (
            sum_last(gateup_sums),
            sum_last(down_sums),
            sum_last(pair_sums),
        )
        sum_outgate = sum_pair[0, 0]
        sum_out = jnp.concatenate(jnp.split(sum_pair[0, 1], 2, 0), 1)
    else:
        everyone = lax.all_gather(smalls.astype(bf16), "dp")
        mine = jnp.sum(
            lax.dynamic_index_in_dim(everyone, place, 1, keepdims=False).astype(f32), 0
        )

        def scattered(array, axis):
            return lax.psum_scatter(array, "dp", scatter_dimension=axis, tiled=True).astype(f32)

        sum_qkv, sum_outgate = scattered(grad_qkv, 1), scattered(grad_outgate, 0)
        sum_out, sum_gateup = scattered(grad_outproj, 1), scattered(grad_gateup, 1)
        sum_down = scattered(grad_down, 1)
    sum_conv, sum_beta, sum_head, sum_mix, sum_mlp = unpack(
        mine,
        [conv_weight.shape, w_beta.shape, head_gain.shape, mixer_gain.shape, mlp_gain.shape],
    )

    mixed_out = (own(late_middle) + mlp_share).astype(bf16)
    row_mean = (row_sum / width).reshape(seqs, block, 1)
    gain_own = lax.dynamic_slice_in_dim(blocks_about(gain_one, 0), column, local_width, 0)
    factor_one = scale_one.reshape(seqs, block, 1)
    tokens_grad = own(grad_middle) + factor_one * (
        one_share * gain_own - late_tokens.astype(f32) * factor_one * row_mean
    )
    return (
        mixed_out,
        tokens_grad.astype(bf16),
        sum_qkv,
        sum_conv,
        sum_beta,
        sum_outgate,
        sum_head,
        sum_out,
        sum_mix,
        sum_mlp,
        sum_gateup,
        sum_down,
    )


def solution(mesh):
    return jax.shard_map(
        body,
        mesh=mesh,
        in_specs=(
            P(None, "dp", "mp"),
            P(None, "dp", None),
            P(None, "dp"),
            P(),
            P(None, "dp", "mp"),
            P(None, None, "mp", "dp"),
            P("dp", "mp"),
            P("dp", "mp"),
            P("dp"),
            P("mp", "dp"),
            P("dp"),
            P("dp"),
            P(None, "dp", "mp"),
            P("mp", "dp"),
        ),
        out_specs=(
            P(None, "dp", "mp"),
            P(None, "dp", "mp"),
            P(None, "dp", "mp"),
            P(None, None, "mp", "dp"),
            P("dp", "mp"),
            P("dp", "mp"),
            P("dp"),
            P("mp", "dp"),
            P("dp"),
            P("dp"),
            P(None, "dp", "mp"),
            P("mp", "dp"),
        ),
        check_vma=False,
    )
```

```python
import jax
import jax.numpy as jnp
from jax import lax
from jax.experimental import pallas as pl
from jax.experimental.pallas import tpu as pltpu
from jax.sharding import PartitionSpec as P

DK = 128
KW = 4
PAD = 8

eps_norm = 1e-06
eps_unit = 1e-06

f32 = jnp.float32
bf16 = jnp.bfloat16


def split(v):
    if v.dtype == bf16:
        return v, None
    high = v.astype(bf16)
    return high, (v - high.astype(f32)).astype(bf16)


def mm(a, b, ca=1, cb=0, passes=3):
    def one(x, y):
        return lax.dot_general(x, y, (((ca,), (cb,)), ((), ())), preferred_element_type=f32)

    if passes == 1:
        return one(a.astype(bf16), b.astype(bf16))
    (ah, al), (bh, bl) = split(a), split(b)
    out = one(ah, bh)
    if bl is not None:
        out = out + one(ah, bl)
    if al is not None:
        out = out + one(al, bh)
    return out


def places(rows, cols):
    return (
        lax.broadcasted_iota(jnp.int32, (rows, cols), 0),
        lax.broadcasted_iota(jnp.int32, (rows, cols), 1),
    )


def unit_lower_inverses(blocks):
    size = blocks[0].shape[0]
    if size > 128:
        half = size // 2
        parts = unit_lower_inverses(
            [a[:half, :half] for a in blocks] + [a[half:, half:] for a in blocks]
        )
        firsts, seconds = parts[: len(blocks)], parts[len(blocks) :]
        inner = [mm(a[half:, :half], x) for a, x in zip(blocks, firsts)]
        lower = [-mm(x, y) for x, y in zip(seconds, inner)]
        zero = jnp.zeros((half, half), f32)
        return [
            jnp.concatenate(
                [jnp.concatenate([x, zero], 1), jnp.concatenate([y, z], 1)], 0
            )
            for x, y, z in zip(firsts, lower, seconds)
        ]
    rows, cols = places(size, size)
    eye = (rows == cols).astype(f32)
    level = 0
    inverses = None
    while (1 << level) < size:
        mask = (
            ((rows >> (level + 1)) == (cols >> (level + 1)))
            & (((rows >> level) & 1) == 1)
            & (((cols >> level) & 1) == 0)
        ).astype(f32)
        lows = [a * mask for a in blocks]
        if level == 0:
            inverses = [eye - low for low in lows]
        else:
            inner = [mm(low, x) for low, x in zip(lows, inverses)]
            inverses = [x - mm(x, y) for x, y in zip(inverses, inner)]
        level += 1
    return inverses


def head_slice(h):
    return slice(h * DK, (h + 1) * DK)


def convolve(rows, before, taps, i, h):
    own = rows[i, 0, :, head_slice(h)].astype(f32)
    ext = jnp.concatenate([before[i, 0, :, head_slice(h)], own], 0)
    length = own.shape[0]
    shifts = [ext[PAD - KW + 1 + j : PAD - KW + 1 + j + length] for j in range(KW)]
    out = None
    for j in range(KW):
        tap = taps[i * KW + j : i * KW + j + 1, head_slice(h)]
        out = tap * shifts[j] if out is None else out + tap * shifts[j]
    sig = jax.nn.sigmoid(out)
    return shifts, out, sig, out * sig


def unit(acts):
    inv = lax.rsqrt(jnp.sum(acts * acts, -1, keepdims=True) + eps_unit)
    return acts * inv, inv


def rule_inputs(rows, before, taps, h):
    parts = [convolve(rows, before, taps, i, h) for i in range(3)]
    q, q_inv = unit(parts[0][3])
    k, k_inv = unit(parts[1][3])
    return parts, (q, q_inv), (k, k_inv), parts[2][3]


def pre_kernel(proj_ref, before_ref, taps_ref, beta_ref, x_ref, wu_ref, qo_ref, to_ref):
    heads = to_ref.shape[1]
    taps = taps_ref[...]
    length = proj_ref.shape[2]
    r, c = places(length, length)
    strict = (r > c).astype(f32)
    full = (r >= c).astype(f32)
    saved, blocks = [], []
    for h in range(heads):
        _, (q, _), (k, _), v = rule_inputs(proj_ref, before_ref, taps, h)
        q, k, v = q.astype(bf16), k.astype(bf16), v.astype(bf16)
        beta = beta_ref[0, :, h : h + 1]
        gram = mm(k, k, 1, 1)
        blocks.append(beta * gram * strict)
        saved.append((q, k, v, beta))
    inverses = unit_lower_inverses(blocks)
    r, c = places(DK, DK)
    eye = (r == c).astype(f32)
    for h in range(heads):
        q, k, v, beta = saved[h]
        x = inverses[h]
        x_ref[0, h] = x
        kv = jnp.concatenate([k.astype(f32), v.astype(f32)], 1) * beta
        wu = mm(x, kv)
        wu_ref[0, h] = wu
        scores = mm(q, k, 1, 1) * full
        pwu = mm(scores, wu)
        qo_ref[0, h, :, :DK] = q.astype(f32) - pwu[:, :DK]
        qo_ref[0, h, :, DK:] = pwu[:, DK:]
        kwu = mm(k, wu, 0, 0)
        to_ref[0, h, :, :DK] = (eye - kwu[:, :DK]).astype(bf16)
        to_ref[0, h, :, DK:] = kwu[:, DK:].astype(bf16)


def mix_kernel(*refs):
    near, (qo_ref, gate_ref, gain_ref, normed_ref, rule_ref, state_ref) = refs[:-6], refs[-6:]
    heads = state_ref.shape[1]
    for h in range(heads):
        state = jnp.zeros((DK, DK), f32)
        for ref in reversed(near):
            state = mm(ref[0, h, :, :DK], state) + ref[0, h, :, DK:].astype(f32)
        state_ref[0, h] = state
        qo = qo_ref[0, h]
        out = (mm(qo[:, :DK], state) + qo[:, DK:]) * DK ** (-0.5)
        rule_ref[0, :, head_slice(h)] = out
        gate = gate_ref[0, :, head_slice(h)]
        factor = lax.rsqrt(jnp.mean(out * out, -1, keepdims=True) + eps_norm)
        normed = out * factor * gain_ref[...] * (gate * jax.nn.sigmoid(gate))
        normed_ref[0, :, head_slice(h)] = normed.astype(bf16)


def middle_back_kernel(
    at_ref,
    two_ref,
    cot_ref,
    middle_ref,
    gain_ref,
    out_ref,
    rule_ref,
    gate_ref,
    head_gain_ref,
    qo_ref,
    mix_ref,
    own_ref,
    mlpgain_ref,
    drule_ref,
    dgate_ref,
    dgain_ref,
    direct_ref,
    keep_ref,
):
    middle = middle_ref[0]
    factor = lax.rsqrt(jnp.mean(middle * middle, -1, keepdims=True) + eps_norm)
    normal = middle * factor
    two = two_ref[0].astype(f32)
    mlpgain_ref[0] = jnp.sum(two * normal, 0, keepdims=True)
    scaled = two * gain_ref[...]
    mean = jnp.mean(scaled * normal, -1, keepdims=True)
    keep_ref[...] = cot_ref[0].astype(f32) + factor * (scaled - normal * mean)
    width = own_ref.shape[2]
    own_ref[0] = keep_ref[:, pl.ds(pl.multiple_of(at_ref[0], 128), width)]
    mix = keep_ref[...].astype(bf16)
    mix_ref[0] = mix
    grads = mm(mix, out_ref[...], 1, 1)
    total = jnp.zeros((1, DK), f32)
    for h in range(direct_ref.shape[1]):
        grad = grads[:, head_slice(h)]
        out = rule_ref[0, :, head_slice(h)]
        gate = gate_ref[0, :, head_slice(h)]
        inv = lax.rsqrt(jnp.mean(out * out, -1, keepdims=True) + eps_norm)
        n = out * inv
        sig = jax.nn.sigmoid(gate)
        silu = gate * sig
        gg = grad * head_gain_ref[...]
        dn = gg * silu
        drule = inv * (dn - n * jnp.mean(dn * n, -1, keepdims=True))
        drule_ref[0, :, head_slice(h)] = drule
        dgate = gg * n * sig * (1.0 + gate * (1.0 - sig))
        dgate_ref[0, :, head_slice(h)] = dgate.astype(bf16)
        total = total + jnp.sum(grad * n * silu, 0, keepdims=True)
        direct = mm(qo_ref[0, h, :, :DK], drule, 0, 0) * DK ** (-0.5)
        direct_ref[0, h] = direct.astype(bf16)
    dgain_ref[0] = total


def first_back_kernel(
    place_ref,
    dproj_ref,
    dgate_ref,
    dlogit_ref,
    qkv_ref,
    outgate_ref,
    beta_ref,
    rows_ref,
    scale_ref,
    gain_ref,
    one_ref,
    rowsum_ref,
    gainsum_ref,
):
    grad = mm(dgate_ref[...], outgate_ref[...], 1, 1)
    for i in range(3):
        grad = grad + mm(dproj_ref[i], qkv_ref[i], 1, 1)
    for h in range(beta_ref.shape[0]):
        grad = grad + dlogit_ref[:, h : h + 1].astype(f32) * beta_ref[h : h + 1, :]
    one_ref[...] = grad.astype(bf16)
    against = grad * (rows_ref[...].astype(f32) * scale_ref[...])
    gainsum_ref[...] = jnp.sum(against, 0, keepdims=True)
    rowsum = jnp.sum(against * gain_ref[...], -1, keepdims=True)

    @pl.when(pl.program_id(0) == 0)
    def _():
        rowsum_ref[...] = rowsum

    @pl.when(pl.program_id(0) > 0)
    def _():
        rowsum_ref[...] += rowsum


def first_back(place, dproj, dgate, dlogits, full_qkv, full_outgate, beta_rows, rows, scale, gain):
    tokens, width = rows.shape
    inner, heads, size = dgate.shape[1], dlogits.shape[1], width // 4

    def whole(*shape):
        return pl.BlockSpec(shape, lambda k, at: (0,) * len(shape))

    return pl.pallas_call(
        first_back_kernel,
        grid_spec=pltpu.PrefetchScalarGridSpec(
            num_scalar_prefetch=1,
            grid=(4,),
            in_specs=[
                whole(3, tokens, inner),
                whole(tokens, inner),
                whole(tokens, heads),
                pl.BlockSpec((3, size, inner), lambda k, at: (0, k, 0)),
                pl.BlockSpec((size, inner), lambda k, at: (k, 0)),
                pl.BlockSpec((heads, size), lambda k, at: (0, k)),
                pl.BlockSpec((tokens, size), lambda k, at: (0, k)),
                whole(tokens, 1),
                pl.BlockSpec((1, size), lambda k, at: (0, k)),
            ],
            out_specs=[
                pl.BlockSpec((tokens, size), lambda k, at: (0, k ^ at[0])),
                whole(tokens, 1),
                pl.BlockSpec((1, size), lambda k, at: (0, k)),
            ],
        ),
        out_shape=[
            shape_of((tokens, width), bf16),
            shape_of((tokens, 1), f32),
            shape_of((1, width), f32),
        ],
        compiler_params=pltpu.CompilerParams(vmem_limit_bytes=48 * 2**20),
    )(place, dproj, dgate, dlogits, full_qkv, full_outgate, beta_rows, rows, scale, gain)


def back_kernel(*refs):
    (
        proj_ref,
        before_ref,
        taps_ref,
        beta_ref,
        x_ref,
        wu_ref,
        state_ref,
        drule_ref,
    ) = refs[:8]
    dproj_ref, last_ref, first_ref, dtaps_ref, dlogit_ref = refs[-5:]
    others = refs[8:-5]
    count = (len(others) + 1) // 2
    directs, nexts = others[:count], others[count:]
    heads = state_ref.shape[1]
    taps = taps_ref[...]
    length = proj_ref.shape[2]
    r, c = places(length, length)
    strict = (r > c).astype(f32)
    full = (r >= c).astype(f32)
    zeros = jnp.zeros((PAD, DK), f32)
    for h in range(heads):
        parts, (qu, q_inv), (ku, k_inv), vu = rule_inputs(proj_ref, before_ref, taps, h)
        q, k, v = qu.astype(bf16), ku.astype(bf16), vu.astype(bf16)
        beta = beta_ref[0, :, h : h + 1]
        leave = jnp.zeros((DK, DK), f32)
        for j in reversed(range(count)):
            here = directs[j][0, h].astype(f32)
            leave = here if j == count - 1 else mm(nexts[j][0, h, :, :DK], leave, 0, 0) + here
        state = state_ref[0, h]
        wu = wu_ref[0, h]
        u = wu[:, DK:] - mm(wu[:, :DK], state)
        resid = v.astype(f32) - mm(k, state)
        dout = drule_ref[0, :, head_slice(h)] * DK ** (-0.5)
        gram = mm(k, k, 1, 1)
        scores = mm(q, k, 1, 1) * full
        du = mm(scores, dout, 0, 0) + mm(k, leave)
        y = mm(x_ref[0, h], du, 0, 0)
        by = beta * y
        da = -(mm(y, u, 1, 1) * strict)
        dbeta = jnp.sum(y * resid, -1, keepdims=True) + jnp.sum(da * gram, -1, keepdims=True)
        dgram = beta * da
        dscores = mm(dout, u, 1, 1) * full
        dq = mm(dout, state, 1, 1) + mm(dscores, k)
        dk = (
            mm(dgram, k)
            + mm(dgram, k, 0, 0)
            + mm(dscores, q, 0, 0)
            + mm(u, leave, 1, 1)
            - mm(by, state, 1, 1)
        )
        dlogit_ref[0, :, h : h + 1] = (dbeta * beta * (1.0 - beta)).astype(bf16)
        dq = (dq - qu * jnp.sum(qu * dq, -1, keepdims=True)) * q_inv
        dk = (dk - ku * jnp.sum(ku * dk, -1, keepdims=True)) * k_inv
        for i, dact in enumerate((dq, dk, by)):
            shifts, out, sig, _ = parts[i]
            dconv = dact * sig * (1.0 + out * (1.0 - sig))
            ext = jnp.concatenate([zeros, dconv, zeros], 0)
            total = None
            for j in range(KW):
                at = i * KW + j
                dtaps_ref[0, at : at + 1, head_slice(h)] = jnp.sum(
                    dconv * shifts[j], 0, keepdims=True
                )
                tap = taps[at : at + 1, head_slice(h)]
                term = tap * ext[KW - 1 - j : KW - 1 - j + PAD + length]
                total = term if total is None else total + term
            first_ref[i, 0, :, head_slice(h)] = total[:PAD]
            last_ref[i, 0, :, head_slice(h)] = total[length:]
            dproj_ref[i, 0, :, head_slice(h)] = total[PAD:].astype(bf16)


def per_sequence(kernel, ins, outs, scalar=None, scratch=()):
    def spec(shape, axis):
        block = tuple(1 if n == axis else size for n, size in enumerate(shape))
        return pl.BlockSpec(
            block, lambda s, *_: tuple(s if n == axis else 0 for n in range(len(shape)))
        )

    shape, axis = outs[0]
    given = [] if scalar is None else [scalar]
    return pl.pallas_call(
        kernel,
        grid_spec=pltpu.PrefetchScalarGridSpec(
            num_scalar_prefetch=len(given),
            grid=(shape.shape[axis],),
            in_specs=[spec(a.shape, axis) for a, axis in ins],
            out_specs=[spec(o.shape, axis) for o, axis in outs],
            scratch_shapes=scratch,
        ),
        out_shape=[o for o, _ in outs],
        compiler_params=pltpu.CompilerParams(vmem_limit_bytes=48 * 2**20),
    )(*given, *[a for a, _ in ins])


def shape_of(shape, dtype):
    return jax.ShapeDtypeStruct(shape, dtype)


def shifted(array, axis, by):
    devices = lax.axis_size(axis)
    pairs = [(i, i + by) for i in range(devices) if 0 <= i + by < devices]
    return lax.ppermute(array, axis, pairs)


def tie(value, *before):
    return lax.optimization_barrier((value, before))[0]


def swap(array, bits):
    return lax.ppermute(array, "dp", [(i, i ^ bits) for i in range(4)])


def first_hop(own):
    return swap(own, 1), swap(own, 2)


def second_hop(hop, axis):
    low, high = (jnp.split(part, 2, axis) for part in hop)
    return swap(low[0], 2), swap(high[1], 1)


def together(own, hop, diagonal, axis, split_axis):
    if axis == split_axis:
        return jnp.concatenate([own, *hop, *diagonal], axis)
    return jnp.concatenate([own, *hop, jnp.concatenate(diagonal, split_axis)], axis)


def add(a, b):
    return (a.astype(f32) + b.astype(f32)).astype(bf16)


def far_hop(far, split_axis):
    low, high = jnp.split(far, 2, split_axis)
    return swap(low, 1), swap(high, 2)


def near_sums(pieces, far_in, split_axis):
    own, one, two = pieces
    one = jnp.split(one, 2, split_axis)
    two = jnp.split(two, 2, split_axis)
    one = jnp.concatenate([one[0], add(one[1], far_in[1])], split_axis)
    two = jnp.concatenate([add(two[0], far_in[0]), two[1]], split_axis)
    return own, one, two


def sum_first(array, axis, split_axis):
    pieces = jnp.split(array, 4, axis)
    return near_sums(pieces[:3], far_hop(pieces[3], split_axis), split_axis)


def sum_second(parts):
    own, one, two = parts
    return own, swap(one, 1), swap(two, 2)


def sum_last(parts):
    own, one, two = parts
    return own.astype(f32) + one.astype(f32) + two.astype(f32)


def pack(parts):
    return jnp.concatenate([p.reshape(-1) for p in parts])


def unpack(flat, shapes):
    out, at = [], 0
    for shape in shapes:
        size = 1
        for n in shape:
            size *= n
        out.append(flat[..., at : at + size].reshape(flat.shape[:-1] + tuple(shape)))
        at += size
    return out


def padded(flat, multiple=1024):
    return jnp.pad(flat, (0, -flat.shape[0] % multiple))


def rms_factor(values):
    return lax.rsqrt(jnp.mean(values * values, -1, keepdims=True) + eps_norm)


def body(
    tokens,
    out_grad,
    domain,
    group_weight,
    w_qkv,
    conv_weight,
    w_beta,
    w_outgate,
    head_gain,
    w_out,
    mixer_gain,
    mlp_gain,
    w_gateup,
    w_down,
):
    dp = lax.axis_size("dp")
    place = lax.axis_index("dp")
    seqs, block, local_width = tokens.shape
    count_rows = seqs * block
    heads = conv_weight.shape[2]
    inner = heads * DK
    column = lax.axis_index("mp") * local_width
    near_four = dp == 4

    def blocks_about(array, axis):
        if not near_four:
            return array
        size = array.shape[axis] // 4
        return jnp.concatenate(
            [lax.dynamic_slice_in_dim(array, (place ^ k) * size, size, axis) for k in range(4)],
            axis,
        )

    width = out_grad.shape[2]
    turn = place if near_four else jnp.int32(0)
    column_about = ((column // (width // 4)) ^ turn) * (width // 4) + column % (width // 4)

    def own(array):
        array = array.reshape(seqs, block, width)
        return lax.dynamic_slice_in_dim(array, column_about, local_width, 2)

    onehot = (domain[..., None] == jnp.arange(3, dtype=jnp.int32)).astype(f32)
    own_counts = jnp.sum(onehot, axis=(0, 1))
    high = jnp.floor(own_counts / 128.0)
    digits = jnp.concatenate([high, own_counts - 128.0 * high]).astype(bf16)
    small = [w_beta, conv_weight, head_gain, mixer_gain, mlp_gain, digits]
    packed = padded(pack(small))
    if near_four:
        qkv_hop = first_hop(w_qkv)
        packed, qkv_hop = lax.optimization_barrier((packed, qkv_hop))
        gathered = jnp.stack([packed] + [swap(packed, bits) for bits in (1, 2, 3)])
    else:
        gathered = lax.all_gather(packed, "dp")
    g_beta, g_conv, g_head, g_mix, g_mlp, g_digits = unpack(gathered, [a.shape for a in small])
    full_beta = g_beta.reshape(-1, heads)
    full_conv = jnp.moveaxis(blocks_about(g_conv, 0), 0, 3).reshape(3 * KW, inner).astype(f32)
    gain_head = blocks_about(g_head, 0).reshape(1, DK).astype(f32)
    gain_one = g_mix.reshape(-1).astype(f32)
    gain_two = g_mlp.reshape(-1).astype(f32)
    sums = jnp.sum(g_digits.astype(f32), 0)
    counts = 128.0 * sums[:3] + sums[3:]

    rows = lax.all_gather(tokens, "mp", axis=2, tiled=True)
    if near_four:
        qkv_far = second_hop(qkv_hop, 1)
        full_qkv = together(w_qkv, qkv_hop, qkv_far, 1, 1)
        half = w_out.shape[1] // 2
        pair_own = jnp.stack(
            [w_outgate, jnp.concatenate([w_out[:, :half], w_out[:, half:]], 0)]
        )
        pair_hop = first_hop(tie(pair_own, qkv_hop))
        pair_far = second_hop(pair_hop, 0)
    else:
        full_qkv = lax.all_gather(w_qkv, "dp", axis=1, tiled=True)
    rows = blocks_about(rows, 2)

    rows_f = rows.astype(f32).reshape(count_rows, width)
    scale_one = rms_factor(rows_f)
    hidden_one = (rows_f * scale_one * gain_one).astype(bf16)
    projected = jnp.einsum("td,idc->itc", hidden_one, full_qkv, preferred_element_type=f32)
    projected = projected.astype(bf16).reshape(3, seqs, block, inner)
    before = shifted(projected[:, :, block - PAD :], "dp", 1).astype(f32)
    logits = jnp.dot(hidden_one, full_beta, preferred_element_type=f32)
    betas = jax.nn.sigmoid(logits).reshape(seqs, block, heads)
    if near_four:
        before, pair_far = lax.optimization_barrier((before, pair_far))

    square = (seqs, heads, DK, DK)
    inverse, wu, qo, to = per_sequence(
        pre_kernel,
        [(projected, 1), (before, 1), (full_conv, None), (betas, 0)],
        [
            (shape_of((seqs, heads, block, block), f32), 0),
            (shape_of((seqs, heads, block, 2 * DK), f32), 0),
            (shape_of((seqs, heads, block, 2 * DK), f32), 0),
            (shape_of((seqs, heads, DK, 2 * DK), bf16), 0),
        ],
    )
    near = [shifted(to, "dp", c) for c in range(1, dp)]
    nexts = [shifted(to[..., :DK], "dp", -c) for c in range(1, dp - 1)]
    if near_four:
        outgate_far, out_far = pair_far[0][0], pair_far[1][0]
        full_outgate = jnp.concatenate(
            [w_outgate, pair_hop[0][0], pair_hop[1][0], outgate_far], 0
        )
        outs = [pair_hop[0][1], pair_hop[1][1], out_far]
        full_out = jnp.concatenate(
            [w_out] + [part for a in outs for part in jnp.split(a, 2, 0)], 1
        )
    else:
        full_outgate = lax.all_gather(w_outgate, "dp", axis=0, tiled=True)
        full_out = lax.all_gather(w_out, "dp", axis=1, tiled=True)
    gates = jnp.dot(hidden_one, full_outgate, preferred_element_type=f32)
    gates = gates.reshape(seqs, block, inner)
    near, gates, full_out = lax.optimization_barrier((near, gates, full_out))
    normed, rule, state = per_sequence(
        mix_kernel,
        [(a, 0) for a in near] + [(qo, 0), (gates, 0), (gain_head, None)],
        [
            (shape_of((seqs, block, inner), bf16), 0),
            (shape_of((seqs, block, inner), f32), 0),
            (shape_of(square, f32), 0),
        ],
    )
    normed = normed.reshape(count_rows, inner)
    mixer_part = jnp.dot(normed, full_out, preferred_element_type=f32).astype(bf16)
    mixer_total = lax.psum(mixer_part, "mp").astype(f32)
    if near_four:
        own_gateup, own_down = tie((w_gateup, w_down), mixer_part)
        gateup_hop = first_hop(own_gateup)
        full_gateup = together(own_gateup, gateup_hop, second_hop(gateup_hop, 0), 1, 0)
        down_hop = first_hop(tie(own_down, gateup_hop))
        full_down = together(own_down, down_hop, second_hop(down_hop, 0), 1, 0)
    else:
        full_gateup = lax.all_gather(w_gateup, "dp", axis=1, tiled=True)
        full_down = lax.all_gather(w_down, "dp", axis=1, tiled=True)
    middle = rows_f + mixer_total
    scale_two = rms_factor(middle)
    normal_two = middle * scale_two
    hidden_two = (normal_two * gain_two).astype(bf16)
    gate_up = jnp.einsum("td,idf->itf", hidden_two, full_gateup, preferred_element_type=f32)
    gate_act, up_act = (gate_up[0], gate_up[1])
    sigmoid_gate = jax.nn.sigmoid(gate_act)
    silu_gate = gate_act * sigmoid_gate
    hidden_mlp = (silu_gate * up_act).astype(bf16)

    def down_gradient(columns):
        return jnp.einsum("tf,td->fd", hidden_mlp, columns, preferred_element_type=f32).astype(bf16)

    table = group_weight * (domain.shape[0] * domain.shape[1] * dp) / counts
    factor = jnp.sum(onehot * table, -1)
    cotangent = (blocks_about(out_grad, 2).astype(f32) * factor[..., None]).astype(bf16)
    cotangent = cotangent.reshape(count_rows, width)
    early_cotangent = cotangent
    if near_four:
        cut = 3 * width // 4
        down_far = down_gradient(cotangent[:, cut:])
        down_far_in = far_hop(down_far, 0)
        early_cotangent, down_far = lax.optimization_barrier((cotangent, down_far))
    grad_hidden = jnp.einsum("td,fd->tf", early_cotangent, full_down, preferred_element_type=f32)
    grad_gate = grad_hidden * up_act * sigmoid_gate * (1.0 + gate_act * (1.0 - sigmoid_gate))
    grad_pair = jnp.stack([grad_gate, grad_hidden * silu_gate]).astype(bf16)
    grad_two_part = jnp.einsum("itf,idf->td", grad_pair, full_gateup, preferred_element_type=f32)
    grad_two_part = grad_two_part.astype(bf16)
    if near_four:
        grad_two_part, down_far_in = lax.optimization_barrier((grad_two_part, down_far_in))
    grad_two = lax.psum(grad_two_part, "mp")

    late_pair, late_mlp, late_cotangent = tie((grad_pair, hidden_mlp, cotangent), grad_two_part)
    grad_gateup = jnp.einsum("td,itf->idf", hidden_two, late_pair, preferred_element_type=f32)
    grad_gateup = grad_gateup.astype(bf16)
    down_part = jnp.dot(late_mlp, full_down, preferred_element_type=f32).astype(bf16)
    down_part = blocks_about(down_part.reshape(seqs, block, width), 2)
    if near_four:
        gateup_sums = sum_second(sum_first(grad_gateup, 1, 0))
        grad_near = down_gradient(late_cotangent[:, :cut])
        down_sums = sum_second(near_sums(jnp.split(grad_near, 3, 1), down_far_in, 0))
        grad_two, gateup_sums, down_sums, down_part = lax.optimization_barrier(
            (grad_two, gateup_sums, down_sums, down_part)
        )
    else:
        grad_down = down_gradient(late_cotangent)
    mlp_share = lax.psum_scatter(down_part, "mp", scatter_dimension=2, tiled=True).astype(f32)

    grad_mix, middle_own, mlpgain, drule, dgate, dgain, direct = per_sequence(
        middle_back_kernel,
        [
            (grad_two.reshape(seqs, block, width), 0),
            (cotangent.reshape(seqs, block, width), 0),
            (middle.reshape(seqs, block, width), 0),
            (gain_two.reshape(1, width), None),
            (full_out, None),
            (rule, 0),
            (gates, 0),
            (gain_head, None),
            (qo, 0),
        ],
        [
            (shape_of((seqs, block, width), bf16), 0),
            (shape_of((seqs, block, local_width), f32), 0),
            (shape_of((seqs, 1, width), f32), 0),
            (shape_of((seqs, block, inner), f32), 0),
            (shape_of((seqs, block, inner), bf16), 0),
            (shape_of((seqs, 1, DK), f32), 0),
            (shape_of(square, bf16), 0),
        ],
        scalar=column_about.reshape(1),
        scratch=[pltpu.VMEM((block, width), f32)],
    )
    grad_mix = grad_mix.reshape(count_rows, width)
    directs = [shifted(direct, "dp", -c) for c in range(1, dp)]
    dgate = dgate.reshape(count_rows, inner)
    late_dgate, late_normed = tie((dgate, normed), direct)
    grad_outgate = jnp.einsum("td,tc->dc", hidden_one, late_dgate, preferred_element_type=f32)
    grad_outgate = grad_outgate.astype(bf16)
    grad_outproj = jnp.einsum("tc,td->cd", late_normed, grad_mix, preferred_element_type=f32)
    grad_outproj = grad_outproj.astype(bf16)
    if near_four:
        parts = [jnp.split(a, 2, 1) for a in jnp.split(grad_outproj, 4, 1)]
        pair_grad = jnp.stack(
            [grad_outgate.reshape(4, -1, inner), jnp.stack([jnp.concatenate(p, 0) for p in parts])],
            1,
        )
        directs, pair_grad = lax.optimization_barrier((directs, pair_grad))
    dproj, last, first, dtaps, dlogits = per_sequence(
        back_kernel,
        [
            (projected, 1),
            (before, 1),
            (full_conv, None),
            (betas, 0),
            (inverse, 0),
            (wu, 0),
            (state, 0),
            (drule, 0),
        ]
        + [(a, 0) for a in directs + nexts],
        [
            (shape_of((3, seqs, block, inner), bf16), 1),
            (shape_of((3, seqs, PAD, inner), f32), 1),
            (shape_of((3, seqs, PAD, inner), f32), 1),
            (shape_of((seqs, 3 * KW, inner), f32), 0),
            (shape_of((seqs, block, heads), bf16), 0),
        ],
    )
    later = shifted(first, "dp", -1)
    dproj = lax.dynamic_update_slice(dproj, (last + later).astype(bf16), (0, 0, block - PAD, 0))
    dproj = dproj.reshape(3, count_rows, inner)
    dlogits = dlogits.reshape(count_rows, heads)
    grad_qkv = jnp.einsum("td,itc->idc", hidden_one, dproj, preferred_element_type=f32)
    grad_qkv = grad_qkv.astype(bf16)
    if near_four:
        qkv_sums = sum_first(grad_qkv, 1, 1)
    late_proj = tie(dproj, grad_qkv)
    one_low, row_part, gain_part = first_back(
        turn.reshape(1),
        late_proj,
        dgate,
        dlogits,
        full_qkv,
        full_outgate,
        full_beta.T.astype(f32),
        rows.reshape(count_rows, width),
        scale_one,
        gain_one.reshape(1, width),
    )
    one_share = lax.psum_scatter(
        one_low.reshape(seqs, block, width), "mp", scatter_dimension=2, tiled=True
    ).astype(f32)
    late_logits, late_middle, late_tokens, mlp_share, late_stats = tie(
        (dlogits, middle, tokens, mlp_share, (row_part, gain_part, dgain)), one_low
    )
    if near_four:
        pair_sums = sum_second(sum_first(tie(pair_grad, one_low), 0, 1))
    grad_beta = jnp.einsum("td,th->dh", hidden_one, late_logits, preferred_element_type=f32)
    stats = [late_stats[0][:, 0], late_stats[1][0], jnp.sum(late_stats[2], (0, 1))]
    stat_sum = jnp.sum(lax.all_gather(pack(stats), "mp"), 0)
    row_sum, mixgain_sum, headgain_sum = unpack(stat_sum, [a.shape for a in stats])

    def pieces(array, axis, about):
        shape = array.shape
        cut = array.reshape(shape[:axis] + (dp, shape[axis] // dp) + shape[axis + 1 :])
        cut = jnp.moveaxis(cut, axis, 0).reshape(dp, -1)
        return blocks_about(cut, 0) if about else cut

    smalls = jnp.concatenate(
        [
            pieces(jnp.sum(dtaps, 0).reshape(3, KW, heads, DK), 3, True),
            pieces(grad_beta, 0, False),
            pieces(headgain_sum, 0, True),
            pieces(mixgain_sum, 0, False),
            pieces(jnp.sum(mlpgain, (0, 1)), 0, False),
        ],
        1,
    )
    if near_four:
        mine = smalls[0]
        for bits in (1, 2, 3):
            mine = mine + swap(padded(smalls[bits].astype(bf16)), bits)[: mine.shape[0]].astype(f32)
        sum_qkv = sum_last(sum_second(qkv_sums))
        sum_gateup, sum_down, sum_pair = (
            sum_last(gateup_sums),
            sum_last(down_sums),
            sum_last(pair_sums),
        )
        sum_outgate = sum_pair[0, 0]
        sum_out = jnp.concatenate(jnp.split(sum_pair[0, 1], 2, 0), 1)
    else:
        everyone = lax.all_gather(smalls.astype(bf16), "dp")
        mine = jnp.sum(
            lax.dynamic_index_in_dim(everyone, place, 1, keepdims=False).astype(f32), 0
        )

        def scattered(array, axis):
            return lax.psum_scatter(array, "dp", scatter_dimension=axis, tiled=True).astype(f32)

        sum_qkv, sum_outgate = scattered(grad_qkv, 1), scattered(grad_outgate, 0)
        sum_out, sum_gateup = scattered(grad_outproj, 1), scattered(grad_gateup, 1)
        sum_down = scattered(grad_down, 1)
    sum_conv, sum_beta, sum_head, sum_mix, sum_mlp = unpack(
        mine,
        [conv_weight.shape, w_beta.shape, head_gain.shape, mixer_gain.shape, mlp_gain.shape],
    )

    mixed_out = (own(late_middle) + mlp_share).astype(bf16)
    row_mean = (row_sum / width).reshape(seqs, block, 1)
    gain_own = lax.dynamic_slice_in_dim(blocks_about(gain_one, 0), column, local_width, 0)
    factor_one = scale_one.reshape(seqs, block, 1)
    tokens_grad = middle_own + factor_one * (
        one_share * gain_own - late_tokens.astype(f32) * factor_one * row_mean
    )
    return (
        mixed_out,
        tokens_grad.astype(bf16),
        sum_qkv,
        sum_conv,
        sum_beta,
        sum_outgate,
        sum_head,
        sum_out,
        sum_mix,
        sum_mlp,
        sum_gateup,
        sum_down,
    )


def solution(mesh):
    return jax.shard_map(
        body,
        mesh=mesh,
        in_specs=(
            P(None, "dp", "mp"),
            P(None, "dp", None),
            P(None, "dp"),
            P(),
            P(None, "dp", "mp"),
            P(None, None, "mp", "dp"),
            P("dp", "mp"),
            P("dp", "mp"),
            P("dp"),
            P("mp", "dp"),
            P("dp"),
            P("dp"),
            P(None, "dp", "mp"),
            P("mp", "dp"),
        ),
        out_specs=(
            P(None, "dp", "mp"),
            P(None, "dp", "mp"),
            P(None, "dp", "mp"),
            P(None, None, "mp", "dp"),
            P("dp", "mp"),
            P("dp", "mp"),
            P("dp"),
            P("mp", "dp"),
            P("dp"),
            P("dp"),
            P(None, "dp", "mp"),
            P("mp", "dp"),
        ),
        check_vma=False,
    )
```

```python
from functools import partial

import jax
import jax.numpy as jnp
from jax import lax
from jax.experimental import pallas as pl
from jax.experimental.pallas import tpu as pltpu
from jax.sharding import PartitionSpec as P

DK = 128
KW = 4
PAD = 8
HALO = 16
VMEM = 40 * 2**20

eps_norm = 1e-06
eps_unit = 1e-06

f32 = jnp.float32
bf16 = jnp.bfloat16


def split(v):
    if v.dtype == bf16:
        return v, None
    high = v.astype(bf16)
    return high, (v - high.astype(f32)).astype(bf16)


def mm(a, b, ca=1, cb=0, passes=3):
    def one(x, y):
        return lax.dot_general(x, y, (((ca,), (cb,)), ((), ())), preferred_element_type=f32)

    if passes == 1:
        return one(a.astype(bf16), b.astype(bf16))
    (ah, al), (bh, bl) = split(a), split(b)
    out = one(ah, bh)
    if bl is not None:
        out = out + one(ah, bl)
    if al is not None:
        out = out + one(al, bh)
    return out


def places(rows, cols):
    return (
        lax.broadcasted_iota(jnp.int32, (rows, cols), 0),
        lax.broadcasted_iota(jnp.int32, (rows, cols), 1),
    )


def unit_lower_inverses(blocks):
    size = blocks[0].shape[0]
    if size > 128:
        half = size // 2
        parts = unit_lower_inverses(
            [a[:half, :half] for a in blocks] + [a[half:, half:] for a in blocks]
        )
        firsts, seconds = parts[: len(blocks)], parts[len(blocks) :]
        inner = [mm(a[half:, :half], x) for a, x in zip(blocks, firsts)]
        lower = [-mm(x, y) for x, y in zip(seconds, inner)]
        zero = jnp.zeros((half, half), f32)
        return [
            jnp.concatenate(
                [jnp.concatenate([x, zero], 1), jnp.concatenate([y, z], 1)], 0
            )
            for x, y, z in zip(firsts, lower, seconds)
        ]
    rows, cols = places(size, size)
    eye = (rows == cols).astype(f32)
    level = 0
    inverses = None
    while (1 << level) < size:
        mask = (
            ((rows >> (level + 1)) == (cols >> (level + 1)))
            & (((rows >> level) & 1) == 1)
            & (((cols >> level) & 1) == 0)
        ).astype(f32)
        lows = [a * mask for a in blocks]
        if level == 0:
            inverses = [eye - low for low in lows]
        else:
            inner = [mm(low, x) for low, x in zip(lows, inverses)]
            inverses = [x - mm(x, y) for x, y in zip(inverses, inner)]
        level += 1
    return inverses


def head_slice(h):
    return slice(h * DK, (h + 1) * DK)


def convolve(proj_ref, taps, i, h):
    ext = proj_ref[i, 0, :, head_slice(h)].astype(f32)
    length = ext.shape[0] - HALO
    shifts = [ext[HALO - KW + 1 + j : HALO - KW + 1 + j + length] for j in range(KW)]
    out = None
    for j in range(KW):
        tap = taps[i * KW + j : i * KW + j + 1, head_slice(h)]
        out = tap * shifts[j] if out is None else out + tap * shifts[j]
    sig = jax.nn.sigmoid(out)
    return shifts, out, sig, out * sig


def unit(acts):
    inv = lax.rsqrt(jnp.sum(acts * acts, -1, keepdims=True) + eps_unit)
    return acts * inv, inv


def rule_inputs(proj_ref, taps, h):
    parts = [convolve(proj_ref, taps, i, h) for i in range(3)]
    q, q_inv = unit(parts[0][3])
    k, k_inv = unit(parts[1][3])
    return parts, (q, q_inv), (k, k_inv), parts[2][3]


def norm_factor(values):
    return lax.rsqrt(jnp.mean(values * values, -1, keepdims=True) + eps_norm)


def project_kernel(layout, *refs):
    place_ref, rows_ref, halo_ref, gain_ref, beta_ref = refs[:5]
    pieces = refs[5 : 5 + len(layout)]
    hidden_ref, proj_ref, logit_ref, scale_ref, keep_ref = refs[5 + len(layout) :]
    rows = jnp.concatenate([halo_ref[0], rows_ref[0]], 0).astype(f32)
    scale = norm_factor(rows)
    scale_ref[0] = scale[HALO:]
    keep_ref[...] = (rows * scale * gain_ref[...]).astype(bf16)
    logits = mm(keep_ref[HALO:, :], beta_ref[...])
    logit_ref[0] = logits[:, : logit_ref.shape[2]]
    sums = [None] * 3
    for (k, start, size, block), piece in zip(layout, pieces):
        at = pl.multiple_of((place_ref[0] ^ k) * block + start, 128)
        part = keep_ref[:, pl.ds(at, size)]
        hidden_ref[0, :, k * block + start : k * block + start + size] = part[HALO:]
        for i in range(3):
            term = mm(part, piece[i])
            sums[i] = term if sums[i] is None else sums[i] + term
    for i in range(3):
        proj_ref[i, 0] = sums[i].astype(bf16)


def pre_kernel(proj_ref, taps_ref, logit_ref, x_ref, wu_ref, qo_ref, to_ref):
    heads = to_ref.shape[1]
    taps = taps_ref[...]
    length = proj_ref.shape[2] - HALO
    betas = jax.nn.sigmoid(logit_ref[0])
    r, c = places(length, length)
    strict = (r > c).astype(f32)
    full = (r >= c).astype(f32)
    saved, blocks = [], []
    for h in range(heads):
        _, (q, _), (k, _), v = rule_inputs(proj_ref, taps, h)
        q, k, v = q.astype(bf16), k.astype(bf16), v.astype(bf16)
        beta = betas[:, h : h + 1]
        gram = mm(k, k, 1, 1)
        blocks.append(beta * gram * strict)
        saved.append((q, k, v, beta))
    inverses = unit_lower_inverses(blocks)
    r, c = places(DK, DK)
    eye = (r == c).astype(f32)
    for h in range(heads):
        q, k, v, beta = saved[h]
        x = inverses[h]
        x_ref[0, h] = x
        kv = jnp.concatenate([k.astype(f32), v.astype(f32)], 1) * beta
        wu = mm(x, kv)
        wu_ref[0, h] = wu
        scores = mm(q, k, 1, 1) * full
        pwu = mm(scores, wu)
        qo_ref[0, h, :, :DK] = q.astype(f32) - pwu[:, :DK]
        qo_ref[0, h, :, DK:] = pwu[:, DK:]
        kwu = mm(k, wu, 0, 0)
        to_ref[0, h, :, :DK] = (eye - kwu[:, :DK]).astype(bf16)
        to_ref[0, h, :, DK:] = kwu[:, DK:].astype(bf16)


def mix_kernel(*refs):
    near, rest = refs[:-8], refs[-8:]
    qo_ref, gate_ref, gain_ref, out_ref, part_ref, normed_ref, rule_ref, state_ref = rest
    heads = state_ref.shape[1]
    for h in range(heads):
        state = near[-1][0, h, :, DK:].astype(f32)
        for ref in reversed(near[:-1]):
            state = mm(ref[0, h, :, :DK], state) + ref[0, h, :, DK:].astype(f32)
        state_ref[0, h] = state
        qo = qo_ref[0, h]
        out = (mm(qo[:, :DK], state) + qo[:, DK:]) * DK ** (-0.5)
        rule_ref[0, :, head_slice(h)] = out
        gate = gate_ref[0, :, head_slice(h)]
        normed = out * norm_factor(out) * gain_ref[...] * (gate * jax.nn.sigmoid(gate))
        normed_ref[0, :, head_slice(h)] = normed.astype(bf16)
    part_ref[0] = mm(normed_ref[0], out_ref[...]).astype(bf16)


def feed_kernel(layout, *refs):
    rows_ref, total_ref, cot_ref, gain_ref = refs[:4]
    count = len(layout)
    gateups, downs = refs[4 : 4 + count], refs[4 + count : 4 + 2 * count]
    two_ref, hidden_ref, mlp_ref, pair_ref = refs[4 + 2 * count :]
    middle = rows_ref[0].astype(f32) + total_ref[0].astype(f32)
    hidden_ref[0] = (middle * norm_factor(middle) * gain_ref[...]).astype(bf16)
    gate, up, grad = None, None, None
    for (k, start, size, block), weights, down in zip(layout, gateups, downs):
        lanes = slice(k * block + start, k * block + start + size)
        hidden = hidden_ref[0, :, lanes]
        terms = (
            mm(hidden, weights[0]),
            mm(hidden, weights[1]),
            mm(cot_ref[0, :, lanes], down[...], 1, 1),
        )
        if gate is None:
            gate, up, grad = terms
        else:
            gate, up, grad = gate + terms[0], up + terms[1], grad + terms[2]
    sig = jax.nn.sigmoid(gate)
    silu = gate * sig
    mlp_ref[0] = (silu * up).astype(bf16)
    first = (grad * up * sig * (1.0 + gate * (1.0 - sig))).astype(bf16)
    second = (grad * silu).astype(bf16)
    pair_ref[0, 0] = first
    pair_ref[1, 0] = second
    for (k, start, size, block), weights in zip(layout, gateups):
        lanes = slice(k * block + start, k * block + start + size)
        two = mm(first, weights[0], 1, 1) + mm(second, weights[1], 1, 1)
        two_ref[0, :, lanes] = two.astype(bf16)


def middle_back_kernel(
    at_ref,
    two_ref,
    cot_ref,
    rows_ref,
    total_ref,
    gain_ref,
    out_ref,
    rule_ref,
    gate_ref,
    head_gain_ref,
    qo_ref,
    mix_ref,
    own_ref,
    mlpgain_ref,
    drule_ref,
    dgate_ref,
    dgain_ref,
    direct_ref,
    keep_ref,
):
    middle = rows_ref[0].astype(f32) + total_ref[0].astype(f32)
    factor = norm_factor(middle)
    normal = middle * factor
    two = two_ref[0].astype(f32)
    mlpgain_ref[0] = jnp.sum(two * normal, 0, keepdims=True)
    scaled = two * gain_ref[...]
    mean = jnp.mean(scaled * normal, -1, keepdims=True)
    keep_ref[...] = cot_ref[0].astype(f32) + factor * (scaled - normal * mean)
    width = own_ref.shape[2]
    own_ref[0] = keep_ref[:, pl.ds(pl.multiple_of(at_ref[0], 128), width)]
    mix = keep_ref[...].astype(bf16)
    mix_ref[0] = mix
    grads = mm(mix, out_ref[...], 1, 1)
    total = jnp.zeros((1, DK), f32)
    for h in range(direct_ref.shape[1]):
        grad = grads[:, head_slice(h)]
        out = rule_ref[0, :, head_slice(h)]
        gate = gate_ref[0, :, head_slice(h)]
        inv = norm_factor(out)
        n = out * inv
        sig = jax.nn.sigmoid(gate)
        silu = gate * sig
        gg = grad * head_gain_ref[...]
        dn = gg * silu
        drule = inv * (dn - n * jnp.mean(dn * n, -1, keepdims=True))
        drule_ref[0, :, head_slice(h)] = drule
        dgate = gg * n * sig * (1.0 + gate * (1.0 - sig))
        dgate_ref[0, :, head_slice(h)] = dgate.astype(bf16)
        total = total + jnp.sum(grad * n * silu, 0, keepdims=True)
        direct = mm(qo_ref[0, h, :, :DK], drule, 0, 0) * DK ** (-0.5)
        direct_ref[0, h] = direct.astype(bf16)
    dgain_ref[0] = total


def first_back_kernel(
    place_ref,
    dproj_ref,
    dgate_ref,
    dlogit_ref,
    proj_ref,
    gate_ref,
    logit_ref,
    qkv_ref,
    outgate_ref,
    beta_ref,
    rows_ref,
    scale_ref,
    one_ref,
    rowsum_ref,
    gainsum_ref,
):
    grad = mm(dgate_ref[...], outgate_ref[...], 1, 1)
    for i in range(3):
        grad = grad + mm(dproj_ref[i], qkv_ref[i], 1, 1)
    for h in range(beta_ref.shape[0]):
        grad = grad + dlogit_ref[:, h : h + 1].astype(f32) * beta_ref[h : h + 1, :]
    one_ref[...] = grad.astype(bf16)
    gainsum_ref[...] = jnp.sum(
        grad * (rows_ref[...].astype(f32) * scale_ref[...]), 0, keepdims=True
    )

    @pl.when(pl.program_id(0) == 0)
    def _():
        seqs = proj_ref.shape[1]
        block = proj_ref.shape[2] - HALO
        for s in range(seqs):
            own = slice(s * block, (s + 1) * block)
            total = dgate_ref[own, :].astype(f32) * gate_ref[own, :]
            for i in range(3):
                total = total + dproj_ref[i, own, :].astype(f32) * proj_ref[i, s, HALO:].astype(f32)
            total = jnp.sum(total, -1, keepdims=True)
            logits = dlogit_ref[own, :].astype(f32) * logit_ref[own, :]
            rowsum_ref[own, :] = total + jnp.sum(logits, -1, keepdims=True)


def first_back(place, dproj, dgate, dlogits, proj, gates, logits, full_qkv, full_outgate, beta_rows, rows, scale):
    tokens, width = rows.shape
    inner, heads, size = dgate.shape[1], dlogits.shape[1], width // 4

    def whole(*shape):
        return pl.BlockSpec(shape, lambda k, at: (0,) * len(shape))

    return pl.pallas_call(
        first_back_kernel,
        grid_spec=pltpu.PrefetchScalarGridSpec(
            num_scalar_prefetch=1,
            grid=(4,),
            in_specs=[
                whole(3, tokens, inner),
                whole(tokens, inner),
                whole(tokens, heads),
                whole(*proj.shape),
                whole(tokens, inner),
                whole(tokens, heads),
                pl.BlockSpec((3, size, inner), lambda k, at: (0, k, 0)),
                pl.BlockSpec((size, inner), lambda k, at: (k, 0)),
                pl.BlockSpec((heads, size), lambda k, at: (0, k)),
                pl.BlockSpec((tokens, size), lambda k, at: (0, k)),
                whole(tokens, 1),
            ],
            out_specs=[
                pl.BlockSpec((tokens, size), lambda k, at: (0, k ^ at[0])),
                whole(tokens, 1),
                pl.BlockSpec((1, size), lambda k, at: (0, k)),
            ],
        ),
        out_shape=[
            shape_of((tokens, width), bf16),
            shape_of((tokens, 1), f32),
            shape_of((1, width), f32),
        ],
        compiler_params=pltpu.CompilerParams(vmem_limit_bytes=VMEM),
    )(place, dproj, dgate, dlogits, proj, gates, logits, full_qkv, full_outgate, beta_rows, rows, scale)


def back_kernel(*refs):
    (
        proj_ref,
        taps_ref,
        logit_ref,
        x_ref,
        wu_ref,
        state_ref,
        drule_ref,
    ) = refs[:7]
    dproj_ref, last_ref, first_ref, dtaps_ref, dlogit_ref = refs[-5:]
    others = refs[7:-5]
    count = (len(others) + 1) // 2
    directs, nexts = others[:count], others[count:]
    heads = state_ref.shape[1]
    taps = taps_ref[...]
    length = proj_ref.shape[2] - HALO
    betas = jax.nn.sigmoid(logit_ref[0])
    r, c = places(length, length)
    strict = (r > c).astype(f32)
    full = (r >= c).astype(f32)
    zeros = jnp.zeros((PAD, DK), f32)
    for h in range(heads):
        parts, (qu, q_inv), (ku, k_inv), vu = rule_inputs(proj_ref, taps, h)
        q, k, v = qu.astype(bf16), ku.astype(bf16), vu.astype(bf16)
        beta = betas[:, h : h + 1]
        leave = jnp.zeros((DK, DK), f32)
        for j in reversed(range(count)):
            here = directs[j][0, h].astype(f32)
            leave = here if j == count - 1 else mm(nexts[j][0, h], leave, 0, 0) + here
        state = state_ref[0, h]
        wu = wu_ref[0, h]
        u = wu[:, DK:] - mm(wu[:, :DK], state)
        resid = v.astype(f32) - mm(k, state)
        dout = drule_ref[0, :, head_slice(h)] * DK ** (-0.5)
        gram = mm(k, k, 1, 1)
        scores = mm(q, k, 1, 1) * full
        du = mm(scores, dout, 0, 0) + mm(k, leave)
        y = mm(x_ref[0, h], du, 0, 0)
        by = beta * y
        da = -(mm(y, u, 1, 1) * strict)
        dbeta = jnp.sum(y * resid, -1, keepdims=True) + jnp.sum(da * gram, -1, keepdims=True)
        dgram = beta * da
        dscores = mm(dout, u, 1, 1) * full
        dq = mm(dout, state, 1, 1) + mm(dscores, k)
        dk = (
            mm(dgram, k)
            + mm(dgram, k, 0, 0)
            + mm(dscores, q, 0, 0)
            + mm(u, leave, 1, 1)
            - mm(by, state, 1, 1)
        )
        dlogit_ref[0, :, h : h + 1] = (dbeta * beta * (1.0 - beta)).astype(bf16)
        dq = (dq - qu * jnp.sum(qu * dq, -1, keepdims=True)) * q_inv
        dk = (dk - ku * jnp.sum(ku * dk, -1, keepdims=True)) * k_inv
        for i, dact in enumerate((dq, dk, by)):
            shifts, out, sig, _ = parts[i]
            dconv = dact * sig * (1.0 + out * (1.0 - sig))
            ext = jnp.concatenate([zeros, dconv, zeros], 0)
            total = None
            for j in range(KW):
                at = i * KW + j
                dtaps_ref[0, at : at + 1, head_slice(h)] = jnp.sum(
                    dconv * shifts[j], 0, keepdims=True
                )
                tap = taps[at : at + 1, head_slice(h)]
                term = tap * ext[KW - 1 - j : KW - 1 - j + PAD + length]
                total = term if total is None else total + term
            first_ref[i, 0, :, head_slice(h)] = total[:PAD]
            last_ref[i, 0, :, head_slice(h)] = total[length:]
            dproj_ref[i, 0, :, head_slice(h)] = total[PAD:].astype(bf16)


def per_sequence(kernel, ins, outs, scalar=None, scratch=(), limit=VMEM):
    def spec(shape, axis):
        block = tuple(1 if n == axis else size for n, size in enumerate(shape))
        where = lambda s, *_: tuple(s if n == axis else 0 for n in range(len(shape)))
        if axis is None:
            return pl.BlockSpec(block, where, pipeline_mode=pl.Buffered(1))
        return pl.BlockSpec(block, where)

    shape, axis = outs[0]
    given = [] if scalar is None else [scalar]
    return pl.pallas_call(
        kernel,
        grid_spec=pltpu.PrefetchScalarGridSpec(
            num_scalar_prefetch=len(given),
            grid=(shape.shape[axis],),
            in_specs=[spec(a.shape, axis) for a, axis in ins],
            out_specs=[spec(o.shape, axis) for o, axis in outs],
            scratch_shapes=scratch,
        ),
        out_shape=[o for o, _ in outs],
        compiler_params=pltpu.CompilerParams(vmem_limit_bytes=limit),
    )(*given, *[a for a, _ in ins])


def shape_of(shape, dtype):
    return jax.ShapeDtypeStruct(shape, dtype)


def shifted(array, axis, by):
    devices = lax.axis_size(axis)
    pairs = [(i, i + by) for i in range(devices) if 0 <= i + by < devices]
    return lax.ppermute(array, axis, pairs)


def tie(value, *before):
    return lax.optimization_barrier((value, before))[0]


def swap(array, bits):
    return lax.ppermute(array, "dp", [(i, i ^ bits) for i in range(4)])


def first_hop(own):
    return swap(own, 1), swap(own, 2)


def second_hop(hop, axis):
    low, high = (jnp.split(part, 2, axis) for part in hop)
    return swap(low[0], 2), swap(high[1], 1)


def gathered_pieces(own, axis, hop=None):
    hop = first_hop(own) if hop is None else hop
    return [own, *hop, *second_hop(hop, axis)]


def add(a, b):
    return (a.astype(f32) + b.astype(f32)).astype(bf16)


def far_hop(far, split_axis):
    low, high = jnp.split(far, 2, split_axis)
    return swap(low, 1), swap(high, 2)


def near_sums(pieces, far_in, split_axis):
    own, one, two = pieces
    one = jnp.split(one, 2, split_axis)
    two = jnp.split(two, 2, split_axis)
    one = jnp.concatenate([one[0], add(one[1], far_in[1])], split_axis)
    two = jnp.concatenate([add(two[0], far_in[0]), two[1]], split_axis)
    return own, one, two


def sum_first(array, axis, split_axis):
    pieces = jnp.split(array, 4, axis)
    return near_sums(pieces[:3], far_hop(pieces[3], split_axis), split_axis)


def sum_second(parts):
    own, one, two = parts
    return own, swap(one, 1), swap(two, 2)


def sum_last(parts):
    own, one, two = parts
    return own.astype(f32) + one.astype(f32) + two.astype(f32)


def pack(parts):
    return jnp.concatenate([p.reshape(-1) for p in parts])


def unpack(flat, shapes):
    out, at = [], 0
    for shape in shapes:
        size = 1
        for n in shape:
            size *= n
        out.append(flat[..., at : at + size].reshape(flat.shape[:-1] + tuple(shape)))
        at += size
    return out


def padded(flat, multiple=1024):
    return jnp.pad(flat, (0, -flat.shape[0] % multiple))


def body(
    tokens,
    out_grad,
    domain,
    group_weight,
    w_qkv,
    conv_weight,
    w_beta,
    w_outgate,
    head_gain,
    w_out,
    mixer_gain,
    mlp_gain,
    w_gateup,
    w_down,
):
    dp = lax.axis_size("dp")
    place = lax.axis_index("dp")
    seqs, block, local_width = tokens.shape
    count_rows = seqs * block
    heads = conv_weight.shape[2]
    inner = heads * DK
    column = lax.axis_index("mp") * local_width
    near_four = dp == 4

    def blocks_about(array, axis):
        if not near_four:
            return array
        size = array.shape[axis] // 4
        return jnp.concatenate(
            [lax.dynamic_slice_in_dim(array, (place ^ k) * size, size, axis) for k in range(4)],
            axis,
        )

    width = out_grad.shape[2]
    turn = place if near_four else jnp.int32(0)
    column_about = ((column // (width // 4)) ^ turn) * (width // 4) + column % (width // 4)

    def own(array):
        array = array.reshape(seqs, block, width)
        return lax.dynamic_slice_in_dim(array, column_about, local_width, 2)

    onehot = (domain[..., None] == jnp.arange(3, dtype=jnp.int32)).astype(f32)
    own_counts = jnp.sum(onehot, axis=(0, 1))
    high = jnp.floor(own_counts / 128.0)
    digits = jnp.concatenate([high, own_counts - 128.0 * high]).astype(bf16)
    small = [w_beta, conv_weight, head_gain, mixer_gain, mlp_gain, digits]
    packed = padded(pack(small))
    halo = shifted(tokens[:, block - HALO :], "dp", 1)
    if near_four:
        qkv_hop = first_hop(w_qkv)
        packed, qkv_hop = lax.optimization_barrier((packed, qkv_hop))
        gathered = jnp.stack([packed] + [swap(packed, bits) for bits in (1, 2, 3)])
        qkv = gathered_pieces(w_qkv, 1, qkv_hop)
        half = w_out.shape[1] // 2
        pair_own = jnp.stack(
            [w_outgate, jnp.concatenate([w_out[:, :half], w_out[:, half:]], 0)]
        )
        pair_own = tie(pair_own, qkv[-2:])
        pair_in = [swap(pair_own, bits) for bits in (1, 2, 3)]
        size = width // 4
        layout = [(0, 0, size, size), (1, 0, size, size), (2, 0, size, size)]
        layout += [(3, 0, size // 2, size), (3, size // 2, size // 2, size)]
    else:
        gathered = lax.all_gather(packed, "dp")
        qkv = [lax.all_gather(w_qkv, "dp", axis=1, tiled=True)]
        layout = [(0, 0, width, width)]
    g_beta, g_conv, g_head, g_mix, g_mlp, g_digits = unpack(gathered, [a.shape for a in small])
    about_beta = g_beta.reshape(-1, heads)
    full_beta = blocks_about(about_beta, 0)
    full_conv = jnp.moveaxis(blocks_about(g_conv, 0), 0, 3).reshape(3 * KW, inner).astype(f32)
    gain_head = blocks_about(g_head, 0).reshape(1, DK).astype(f32)
    gain_one = blocks_about(g_mix.reshape(1, -1).astype(f32), 1)
    gain_two = g_mlp.reshape(1, -1).astype(f32)
    sums = jnp.sum(g_digits.astype(f32), 0)
    counts = 128.0 * sums[:3] + sums[3:]

    halo = lax.all_gather(halo, "mp", axis=2, tiled=True)
    rows = lax.all_gather(tokens, "mp", axis=2, tiled=True)

    hidden_one, proj, logits, scale_one = per_sequence(
        partial(project_kernel, layout),
        [(rows, 0), (halo, 0), (gain_one, None), (jnp.pad(full_beta, ((0, 0), (0, 128 - heads))), None)]
        + [(a, None) for a in qkv],
        [
            (shape_of((seqs, block, width), bf16), 0),
            (shape_of((3, seqs, HALO + block, inner), bf16), 1),
            (shape_of((seqs, block, heads), f32), 0),
            (shape_of((seqs, block, 1), f32), 0),
        ],
        scalar=turn.reshape(1),
        scratch=[pltpu.VMEM((HALO + block, width), bf16)],
    )
    hidden_one = hidden_one.reshape(count_rows, width)
    square = (seqs, heads, DK, DK)
    inverse, wu, qo, to = per_sequence(
        pre_kernel,
        [(proj, 1), (full_conv, None), (logits, 0)],
        [
            (shape_of((seqs, heads, block, block), f32), 0),
            (shape_of((seqs, heads, block, 2 * DK), f32), 0),
            (shape_of((seqs, heads, block, 2 * DK), f32), 0),
            (shape_of((seqs, heads, DK, 2 * DK), bf16), 0),
        ],
    )
    if near_four:
        to, pair_in = lax.optimization_barrier((to, pair_in))
    near = [shifted(to, "dp", c) for c in range(1, dp)]
    late_rows = tie(rows, to)
    rows = blocks_about(late_rows, 2)
    if near_four:
        full_outgate = jnp.concatenate([w_outgate] + [a[0] for a in pair_in], 0)
        full_out = jnp.concatenate(
            [w_out] + [part for a in pair_in for part in jnp.split(a[1], 2, 0)], 1
        )
        full_qkv = jnp.concatenate(qkv, 1)
    else:
        full_outgate = lax.all_gather(w_outgate, "dp", axis=0, tiled=True)
        full_out = lax.all_gather(w_out, "dp", axis=1, tiled=True)
        full_qkv = qkv[0]
    gates = jnp.dot(hidden_one, full_outgate, preferred_element_type=f32)
    gates = gates.reshape(seqs, block, inner)
    near, gates, full_out = lax.optimization_barrier((near, gates, full_out))
    mixer_part, normed, rule, state = per_sequence(
        mix_kernel,
        [(a, 0) for a in near] + [(qo, 0), (gates, 0), (gain_head, None), (full_out, None)],
        [
            (shape_of((seqs, block, width), bf16), 0),
            (shape_of((seqs, block, inner), bf16), 0),
            (shape_of((seqs, block, inner), f32), 0),
            (shape_of(square, f32), 0),
        ],
    )
    normed = normed.reshape(count_rows, inner)
    total = lax.psum(mixer_part, "mp")
    late_grad, late_to = tie((out_grad, to), mixer_part)
    nexts = [shifted(late_to[..., :DK], "dp", -c) for c in range(1, dp - 1)]
    table = group_weight * (domain.shape[0] * domain.shape[1] * dp) / counts
    factor = jnp.sum(onehot * table, -1)
    cotangent = (blocks_about(late_grad, 2).astype(f32) * factor[..., None]).astype(bf16)
    if near_four:
        own_gateup, own_down = tie((w_gateup, w_down), mixer_part)
        gateup_hop = first_hop(own_gateup)
        gateup = gathered_pieces(own_gateup, 1, gateup_hop)
        down_hop = first_hop(tie(own_down, gateup_hop))
        total, down_hop, rows, cotangent, nexts, full_qkv = lax.optimization_barrier(
            (total, down_hop, rows, cotangent, nexts, full_qkv)
        )
        down = gathered_pieces(own_down, 1, down_hop)
    else:
        gateup = [lax.all_gather(w_gateup, "dp", axis=1, tiled=True)]
        down = [lax.all_gather(w_down, "dp", axis=1, tiled=True)]
    hidden_units = w_down.shape[0]
    two_part, hidden_two, hidden_mlp, grad_pair = per_sequence(
        partial(feed_kernel, layout),
        [(rows, 0), (total, 0), (cotangent, 0), (gain_two, None)]
        + [(a, None) for a in gateup + down],
        [
            (shape_of((seqs, block, width), bf16), 0),
            (shape_of((seqs, block, width), bf16), 0),
            (shape_of((seqs, block, hidden_units), bf16), 0),
            (shape_of((2, seqs, block, hidden_units), bf16), 1),
        ],
        limit=52 * 2**20,
    )
    grad_two = lax.psum(two_part, "mp")

    hidden_two, hidden_mlp, grad_pair, flat_cotangent, down = tie(
        (
            hidden_two.reshape(count_rows, width),
            hidden_mlp.reshape(count_rows, hidden_units),
            grad_pair.reshape(2, count_rows, hidden_units),
            cotangent.reshape(count_rows, width),
            down,
        ),
        two_part,
    )

    def gateup_gradient(columns):
        return jnp.einsum("td,itf->idf", columns, grad_pair, preferred_element_type=f32).astype(bf16)

    def down_gradient(columns):
        return jnp.einsum("tf,td->fd", hidden_mlp, columns, preferred_element_type=f32).astype(bf16)

    if near_four:
        cut = 3 * width // 4
        gateup_far = gateup_gradient(hidden_two[:, cut:])
        gateup_far_in = far_hop(gateup_far, 0)
        late_two, late_cotangent = tie((hidden_two, flat_cotangent), gateup_far)
        down_grad = down_gradient(late_cotangent)
        down_first = sum_first(down_grad, 1, 0)
        gateup_near = gateup_gradient(late_two[:, :cut])
        gateup_sums = sum_second(near_sums(jnp.split(gateup_near, 3, 1), gateup_far_in, 0))
        down_sums = sum_second(down_first)
        full_down = jnp.concatenate(down, 1)
    else:
        grad_gateup = gateup_gradient(hidden_two)
        grad_down = down_gradient(flat_cotangent)
        full_down = down[0]
    down_part = jnp.dot(hidden_mlp, full_down, preferred_element_type=f32).astype(bf16)
    down_part = blocks_about(down_part.reshape(seqs, block, width), 2)
    if near_four:
        grad_two, gateup_sums, down_sums, down_part, full_outgate = lax.optimization_barrier(
            (grad_two, gateup_sums, down_sums, down_part, full_outgate)
        )
    mlp_share = lax.psum_scatter(down_part, "mp", scatter_dimension=2, tiled=True).astype(f32)

    grad_mix, middle_own, mlpgain, drule, dgate, dgain, direct = per_sequence(
        middle_back_kernel,
        [
            (grad_two, 0),
            (cotangent, 0),
            (rows, 0),
            (total, 0),
            (gain_two, None),
            (full_out, None),
            (rule, 0),
            (gates, 0),
            (gain_head, None),
            (qo, 0),
        ],
        [
            (shape_of((seqs, block, width), bf16), 0),
            (shape_of((seqs, block, local_width), f32), 0),
            (shape_of((seqs, 1, width), f32), 0),
            (shape_of((seqs, block, inner), f32), 0),
            (shape_of((seqs, block, inner), bf16), 0),
            (shape_of((seqs, 1, DK), f32), 0),
            (shape_of(square, bf16), 0),
        ],
        scalar=column_about.reshape(1),
        scratch=[pltpu.VMEM((block, width), f32)],
    )
    grad_mix = grad_mix.reshape(count_rows, width)
    directs = [shifted(direct, "dp", -c) for c in range(1, dp)]
    dgate = dgate.reshape(count_rows, inner)
    late_dgate, late_normed = tie((dgate, normed), direct)
    grad_outgate = jnp.einsum("td,tc->dc", hidden_one, late_dgate, preferred_element_type=f32)
    grad_outgate = grad_outgate.astype(bf16)
    grad_outproj = jnp.einsum("tc,td->cd", late_normed, grad_mix, preferred_element_type=f32)
    grad_outproj = grad_outproj.astype(bf16)
    if near_four:
        parts = [jnp.split(a, 2, 1) for a in jnp.split(grad_outproj, 4, 1)]
        pair_grad = jnp.stack(
            [grad_outgate.reshape(4, -1, inner), jnp.stack([jnp.concatenate(p, 0) for p in parts])],
            1,
        )
        directs, pair_grad = lax.optimization_barrier((directs, pair_grad))
    dproj, last, first, dtaps, dlogits = per_sequence(
        back_kernel,
        [
            (proj, 1),
            (full_conv, None),
            (logits, 0),
            (inverse, 0),
            (wu, 0),
            (state, 0),
            (drule, 0),
        ]
        + [(a, 0) for a in directs + nexts],
        [
            (shape_of((3, seqs, block, inner), bf16), 1),
            (shape_of((3, seqs, PAD, inner), f32), 1),
            (shape_of((3, seqs, PAD, inner), f32), 1),
            (shape_of((seqs, 3 * KW, inner), f32), 0),
            (shape_of((seqs, block, heads), bf16), 0),
        ],
    )
    later = shifted(first, "dp", -1)
    dproj = lax.dynamic_update_slice(dproj, (last + later).astype(bf16), (0, 0, block - PAD, 0))
    dproj = dproj.reshape(3, count_rows, inner)
    dlogits = dlogits.reshape(count_rows, heads)
    grad_qkv = jnp.einsum("td,itc->idc", hidden_one, dproj, preferred_element_type=f32)
    grad_qkv = grad_qkv.astype(bf16)
    late_proj = tie(dproj, grad_qkv)
    one_low, row_part, gain_part = first_back(
        turn.reshape(1),
        late_proj,
        dgate,
        dlogits,
        proj,
        gates.reshape(count_rows, inner),
        logits.reshape(count_rows, heads),
        full_qkv,
        full_outgate,
        about_beta.T.astype(f32),
        rows.reshape(count_rows, width),
        scale_one.reshape(count_rows, 1),
    )
    one_share = lax.psum_scatter(
        one_low.reshape(seqs, block, width), "mp", scatter_dimension=2, tiled=True
    ).astype(f32)
    stats = [row_part[:, 0], gain_part[0], jnp.sum(dgain, (0, 1))]
    stat_own = tie(pack(stats), one_low)
    if near_four:
        qkv_first = sum_first(grad_qkv, 1, 1)
        stat_own, qkv_first = lax.optimization_barrier((stat_own, qkv_first))
    stat_sum = jnp.sum(lax.all_gather(stat_own, "mp"), 0)
    row_sum, mixgain_sum, headgain_sum = unpack(stat_sum, [a.shape for a in stats])
    late_logits, late_total, late_tokens, mlp_share = tie(
        (dlogits, total, tokens, mlp_share), one_low
    )
    if near_four:
        stat_sum, qkv_first = lax.optimization_barrier((stat_sum, qkv_first))
        qkv_sums = sum_second(qkv_first)
        pair_grad, gateup_sums, down_sums = tie((pair_grad, gateup_sums, down_sums), stat_sum)
        pair_sums = sum_second(sum_first(pair_grad, 0, 1))
    grad_beta = jnp.einsum("td,th->dh", hidden_one, late_logits, preferred_element_type=f32)

    def pieces(array, axis, about):
        shape = array.shape
        cut = array.reshape(shape[:axis] + (dp, shape[axis] // dp) + shape[axis + 1 :])
        cut = jnp.moveaxis(cut, axis, 0).reshape(dp, -1)
        return blocks_about(cut, 0) if about else cut

    smalls = jnp.concatenate(
        [
            pieces(jnp.sum(dtaps, 0).reshape(3, KW, heads, DK), 3, True),
            pieces(grad_beta, 0, False),
            pieces(headgain_sum, 0, True),
            pieces(mixgain_sum, 0, False),
            pieces(jnp.sum(mlpgain, (0, 1)), 0, False),
        ],
        1,
    )
    if near_four:
        mine = smalls[0]
        for bits in (1, 2, 3):
            mine = mine + swap(padded(smalls[bits].astype(bf16)), bits)[: mine.shape[0]].astype(f32)
        sum_qkv = sum_last(qkv_sums)
        sum_gateup, sum_down, sum_pair = (
            sum_last(gateup_sums),
            sum_last(down_sums),
            sum_last(pair_sums),
        )
        sum_outgate = sum_pair[0, 0]
        sum_out = jnp.concatenate(jnp.split(sum_pair[0, 1], 2, 0), 1)
    else:
        everyone = lax.all_gather(smalls.astype(bf16), "dp")
        mine = jnp.sum(
            lax.dynamic_index_in_dim(everyone, place, 1, keepdims=False).astype(f32), 0
        )

        def scattered(array, axis):
            return lax.psum_scatter(array, "dp", scatter_dimension=axis, tiled=True).astype(f32)

        sum_qkv, sum_outgate = scattered(grad_qkv, 1), scattered(grad_outgate, 0)
        sum_out, sum_gateup = scattered(grad_outproj, 1), scattered(grad_gateup, 1)
        sum_down = scattered(grad_down, 1)
    sum_conv, sum_beta, sum_head, sum_mix, sum_mlp = unpack(
        mine,
        [conv_weight.shape, w_beta.shape, head_gain.shape, mixer_gain.shape, mlp_gain.shape],
    )

    late_tokens = late_tokens.astype(f32)
    mixed_out = (late_tokens + own(late_total).astype(f32) + mlp_share).astype(bf16)
    row_mean = (row_sum / width).reshape(seqs, block, 1)
    gain_own = lax.dynamic_slice_in_dim(gain_one, column, local_width, 1)
    tokens_grad = middle_own + scale_one * (
        one_share * gain_own - late_tokens * scale_one * row_mean
    )
    return (
        mixed_out,
        tokens_grad.astype(bf16),
        sum_qkv,
        sum_conv,
        sum_beta,
        sum_outgate,
        sum_head,
        sum_out,
        sum_mix,
        sum_mlp,
        sum_gateup,
        sum_down,
    )


def solution(mesh):
    return jax.shard_map(
        body,
        mesh=mesh,
        in_specs=(
            P(None, "dp", "mp"),
            P(None, "dp", None),
            P(None, "dp"),
            P(),
            P(None, "dp", "mp"),
            P(None, None, "mp", "dp"),
            P("dp", "mp"),
            P("dp", "mp"),
            P("dp"),
            P("mp", "dp"),
            P("dp"),
            P("dp"),
            P(None, "dp", "mp"),
            P("mp", "dp"),
        ),
        out_specs=(
            P(None, "dp", "mp"),
            P(None, "dp", "mp"),
            P(None, "dp", "mp"),
            P(None, None, "mp", "dp"),
            P("dp", "mp"),
            P("dp", "mp"),
            P("dp"),
            P("mp", "dp"),
            P("dp"),
            P("dp"),
            P(None, "dp", "mp"),
            P("mp", "dp"),
        ),
        check_vma=False,
    )
```

```python
from functools import partial

import jax
import jax.numpy as jnp
from jax import lax
from jax.experimental import pallas as pl
from jax.experimental.pallas import tpu as pltpu
from jax.sharding import PartitionSpec as P

DK = 128
KW = 4
PAD = 8
HALO = 16
VMEM = 16 * 2**20

eps_norm = 1e-06
eps_unit = 1e-06

f32 = jnp.float32
bf16 = jnp.bfloat16


def split(v):
    if v.dtype == bf16:
        return v, None
    high = v.astype(bf16)
    return high, (v - high.astype(f32)).astype(bf16)


def mm(a, b, ca=1, cb=0, passes=3):
    def one(x, y):
        return lax.dot_general(x, y, (((ca,), (cb,)), ((), ())), preferred_element_type=f32)

    if passes == 1:
        return one(a.astype(bf16), b.astype(bf16))
    (ah, al), (bh, bl) = split(a), split(b)
    out = one(ah, bh)
    if bl is not None:
        out = out + one(ah, bl)
    if al is not None:
        out = out + one(al, bh)
    return out


def places(rows, cols):
    return (
        lax.broadcasted_iota(jnp.int32, (rows, cols), 0),
        lax.broadcasted_iota(jnp.int32, (rows, cols), 1),
    )


def unit_lower_inverses(blocks):
    size = blocks[0].shape[0]
    if size > 128:
        half = size // 2
        parts = unit_lower_inverses(
            [a[:half, :half] for a in blocks] + [a[half:, half:] for a in blocks]
        )
        firsts, seconds = parts[: len(blocks)], parts[len(blocks) :]
        inner = [mm(a[half:, :half], x) for a, x in zip(blocks, firsts)]
        lower = [-mm(x, y) for x, y in zip(seconds, inner)]
        zero = jnp.zeros((half, half), f32)
        return [
            jnp.concatenate(
                [jnp.concatenate([x, zero], 1), jnp.concatenate([y, z], 1)], 0
            )
            for x, y, z in zip(firsts, lower, seconds)
        ]
    rows, cols = places(size, size)
    eye = (rows == cols).astype(f32)
    level = 0
    inverses = None
    while (1 << level) < size:
        mask = (
            ((rows >> (level + 1)) == (cols >> (level + 1)))
            & (((rows >> level) & 1) == 1)
            & (((cols >> level) & 1) == 0)
        ).astype(f32)
        lows = [a * mask for a in blocks]
        if level == 0:
            inverses = [eye - low for low in lows]
        else:
            inner = [mm(low, x) for low, x in zip(lows, inverses)]
            inverses = [x - mm(x, y) for x, y in zip(inverses, inner)]
        level += 1
    return inverses


def head_slice(h):
    return slice(h * DK, (h + 1) * DK)


def convolve(proj_ref, taps, i, h):
    ext = proj_ref[i, 0, :, head_slice(h)].astype(f32)
    length = ext.shape[0] - HALO
    shifts = [ext[HALO - KW + 1 + j : HALO - KW + 1 + j + length] for j in range(KW)]
    out = None
    for j in range(KW):
        tap = taps[i * KW + j : i * KW + j + 1, head_slice(h)]
        out = tap * shifts[j] if out is None else out + tap * shifts[j]
    sig = jax.nn.sigmoid(out)
    return shifts, out, sig, out * sig


def unit(acts):
    inv = lax.rsqrt(jnp.sum(acts * acts, -1, keepdims=True) + eps_unit)
    return acts * inv, inv


def rule_inputs(proj_ref, taps, h):
    parts = [convolve(proj_ref, taps, i, h) for i in range(3)]
    q, q_inv = unit(parts[0][3])
    k, k_inv = unit(parts[1][3])
    return parts, (q, q_inv), (k, k_inv), parts[2][3]


def norm_factor(values):
    return lax.rsqrt(jnp.mean(values * values, -1, keepdims=True) + eps_norm)


def project_kernel(layout, *refs):
    place_ref, rows_ref, halo_ref, gain_ref, beta_ref = refs[:5]
    pieces = refs[5 : 5 + len(layout)]
    hidden_ref, proj_ref, logit_ref, scale_ref, keep_ref = refs[5 + len(layout) :]
    rows = jnp.concatenate([halo_ref[0], rows_ref[0]], 0).astype(f32)
    scale = norm_factor(rows)
    scale_ref[0] = scale[HALO:]
    keep_ref[...] = (rows * scale * gain_ref[...]).astype(bf16)
    logits = mm(keep_ref[HALO:, :], beta_ref[...])
    logit_ref[0] = logits[:, : logit_ref.shape[2]]
    sums = [None] * 3
    for (k, start, size, block), piece in zip(layout, pieces):
        at = pl.multiple_of((place_ref[0] ^ k) * block + start, 128)
        part = keep_ref[:, pl.ds(at, size)]
        hidden_ref[0, :, k * block + start : k * block + start + size] = part[HALO:]
        for i in range(3):
            term = mm(part, piece[i])
            sums[i] = term if sums[i] is None else sums[i] + term
    for i in range(3):
        proj_ref[i, 0] = sums[i].astype(bf16)


def pre_kernel(proj_ref, taps_ref, logit_ref, x_ref, wu_ref, qo_ref, to_ref):
    heads = to_ref.shape[1]
    taps = taps_ref[...]
    length = proj_ref.shape[2] - HALO
    betas = jax.nn.sigmoid(logit_ref[0])
    r, c = places(length, length)
    strict = (r > c).astype(f32)
    full = (r >= c).astype(f32)
    saved, blocks = [], []
    for h in range(heads):
        _, (q, _), (k, _), v = rule_inputs(proj_ref, taps, h)
        q, k, v = q.astype(bf16), k.astype(bf16), v.astype(bf16)
        beta = betas[:, h : h + 1]
        gram = mm(k, k, 1, 1)
        blocks.append(beta * gram * strict)
        saved.append((q, k, v, beta))
    inverses = unit_lower_inverses(blocks)
    r, c = places(DK, DK)
    eye = (r == c).astype(f32)
    for h in range(heads):
        q, k, v, beta = saved[h]
        x = inverses[h]
        x_ref[0, h] = x
        kv = jnp.concatenate([k.astype(f32), v.astype(f32)], 1) * beta
        wu = mm(x, kv)
        wu_ref[0, h] = wu
        scores = mm(q, k, 1, 1) * full
        pwu = mm(scores, wu)
        qo_ref[0, h, :, :DK] = q.astype(f32) - pwu[:, :DK]
        qo_ref[0, h, :, DK:] = pwu[:, DK:]
        kwu = mm(k, wu, 0, 0)
        to_ref[0, h, :, :DK] = (eye - kwu[:, :DK]).astype(bf16)
        to_ref[0, h, :, DK:] = kwu[:, DK:].astype(bf16)


def mix_kernel(*refs):
    near, rest = refs[:-8], refs[-8:]
    qo_ref, gate_ref, gain_ref, out_ref, part_ref, normed_ref, rule_ref, state_ref = rest
    heads = state_ref.shape[1]
    for h in range(heads):
        state = near[-1][0, h, :, DK:].astype(f32)
        for ref in reversed(near[:-1]):
            state = mm(ref[0, h, :, :DK], state) + ref[0, h, :, DK:].astype(f32)
        state_ref[0, h] = state
        qo = qo_ref[0, h]
        out = (mm(qo[:, :DK], state) + qo[:, DK:]) * DK ** (-0.5)
        rule_ref[0, :, head_slice(h)] = out
        gate = gate_ref[0, :, head_slice(h)]
        normed = out * norm_factor(out) * gain_ref[...] * (gate * jax.nn.sigmoid(gate))
        normed_ref[0, :, head_slice(h)] = normed.astype(bf16)
    part_ref[0] = mm(normed_ref[0], out_ref[...]).astype(bf16)


def feed_kernel(layout, *refs):
    rows_ref, total_ref, cot_ref, gain_ref = refs[:4]
    count = len(layout)
    gateups, downs = refs[4 : 4 + count], refs[4 + count : 4 + 2 * count]
    two_ref, hidden_ref, mlp_ref, pair_ref = refs[4 + 2 * count :]
    middle = rows_ref[0].astype(f32) + total_ref[0].astype(f32)
    hidden_ref[0] = (middle * norm_factor(middle) * gain_ref[...]).astype(bf16)
    gate, up, grad = None, None, None
    for (k, start, size, block), weights, down in zip(layout, gateups, downs):
        lanes = slice(k * block + start, k * block + start + size)
        hidden = hidden_ref[0, :, lanes]
        terms = (
            mm(hidden, weights[0], 1, 1),
            mm(hidden, weights[1], 1, 1),
            mm(cot_ref[0, :, lanes], down[...], 1, 1),
        )
        if gate is None:
            gate, up, grad = terms
        else:
            gate, up, grad = gate + terms[0], up + terms[1], grad + terms[2]
    sig = jax.nn.sigmoid(gate)
    silu = gate * sig
    mlp_ref[0] = (silu * up).astype(bf16)
    first = (grad * up * sig * (1.0 + gate * (1.0 - sig))).astype(bf16)
    second = (grad * silu).astype(bf16)
    pair_ref[0, 0] = first
    pair_ref[1, 0] = second
    for (k, start, size, block), weights in zip(layout, gateups):
        lanes = slice(k * block + start, k * block + start + size)
        two = mm(first, weights[0]) + mm(second, weights[1])
        two_ref[0, :, lanes] = two.astype(bf16)


def middle_back_kernel(
    at_ref,
    two_ref,
    cot_ref,
    rows_ref,
    total_ref,
    gain_ref,
    out_ref,
    rule_ref,
    gate_ref,
    head_gain_ref,
    qo_ref,
    mix_ref,
    own_ref,
    mlpgain_ref,
    drule_ref,
    dgate_ref,
    dgain_ref,
    direct_ref,
    keep_ref,
):
    middle = rows_ref[0].astype(f32) + total_ref[0].astype(f32)
    factor = norm_factor(middle)
    normal = middle * factor
    two = two_ref[0].astype(f32)
    mlpgain_ref[0] = jnp.sum(two * normal, 0, keepdims=True)
    scaled = two * gain_ref[...]
    mean = jnp.mean(scaled * normal, -1, keepdims=True)
    keep_ref[...] = cot_ref[0].astype(f32) + factor * (scaled - normal * mean)
    width = own_ref.shape[2]
    own_ref[0] = keep_ref[:, pl.ds(pl.multiple_of(at_ref[0], 128), width)]
    mix = keep_ref[...].astype(bf16)
    mix_ref[0] = mix
    grads = mm(mix, out_ref[...], 1, 1)
    total = jnp.zeros((1, DK), f32)
    for h in range(direct_ref.shape[1]):
        grad = grads[:, head_slice(h)]
        out = rule_ref[0, :, head_slice(h)]
        gate = gate_ref[0, :, head_slice(h)]
        inv = norm_factor(out)
        n = out * inv
        sig = jax.nn.sigmoid(gate)
        silu = gate * sig
        gg = grad * head_gain_ref[...]
        dn = gg * silu
        drule = inv * (dn - n * jnp.mean(dn * n, -1, keepdims=True))
        drule_ref[0, :, head_slice(h)] = drule
        dgate = gg * n * sig * (1.0 + gate * (1.0 - sig))
        dgate_ref[0, :, head_slice(h)] = dgate.astype(bf16)
        total = total + jnp.sum(grad * n * silu, 0, keepdims=True)
        direct = mm(qo_ref[0, h, :, :DK], drule, 0, 0) * DK ** (-0.5)
        direct_ref[0, h] = direct.astype(bf16)
    dgain_ref[0] = total


def first_back_kernel(
    place_ref,
    dproj_ref,
    dgate_ref,
    dlogit_ref,
    proj_ref,
    gate_ref,
    logit_ref,
    qkv_ref,
    outgate_ref,
    beta_ref,
    rows_ref,
    scale_ref,
    one_ref,
    rowsum_ref,
    gainsum_ref,
):
    grad = mm(dgate_ref[...], outgate_ref[...], 1, 1)
    for i in range(3):
        grad = grad + mm(dproj_ref[i], qkv_ref[i], 1, 1)
    for h in range(beta_ref.shape[0]):
        grad = grad + dlogit_ref[:, h : h + 1].astype(f32) * beta_ref[h : h + 1, :]
    one_ref[...] = grad.astype(bf16)
    gainsum_ref[...] = jnp.sum(
        grad * (rows_ref[...].astype(f32) * scale_ref[...]), 0, keepdims=True
    )

    @pl.when(pl.program_id(0) == 0)
    def _():
        seqs = proj_ref.shape[1]
        block = proj_ref.shape[2] - HALO
        for s in range(seqs):
            own = slice(s * block, (s + 1) * block)
            total = dgate_ref[own, :].astype(f32) * gate_ref[own, :]
            for i in range(3):
                total = total + dproj_ref[i, own, :].astype(f32) * proj_ref[i, s, HALO:].astype(f32)
            total = jnp.sum(total, -1, keepdims=True)
            logits = dlogit_ref[own, :].astype(f32) * logit_ref[own, :]
            rowsum_ref[own, :] = total + jnp.sum(logits, -1, keepdims=True)


def first_back(place, dproj, dgate, dlogits, proj, gates, logits, full_qkv, full_outgate, beta_rows, rows, scale):
    tokens, width = rows.shape
    inner, heads, size = dgate.shape[1], dlogits.shape[1], width // 4

    def whole(*shape):
        return pl.BlockSpec(shape, lambda k, at: (0,) * len(shape))

    return pl.pallas_call(
        first_back_kernel,
        grid_spec=pltpu.PrefetchScalarGridSpec(
            num_scalar_prefetch=1,
            grid=(4,),
            in_specs=[
                whole(3, tokens, inner),
                whole(tokens, inner),
                whole(tokens, heads),
                whole(*proj.shape),
                whole(tokens, inner),
                whole(tokens, heads),
                pl.BlockSpec((3, size, inner), lambda k, at: (0, k, 0)),
                pl.BlockSpec((size, inner), lambda k, at: (k, 0)),
                pl.BlockSpec((heads, size), lambda k, at: (0, k)),
                pl.BlockSpec((tokens, size), lambda k, at: (0, k)),
                whole(tokens, 1),
            ],
            out_specs=[
                pl.BlockSpec((tokens, size), lambda k, at: (0, k ^ at[0])),
                whole(tokens, 1),
                pl.BlockSpec((1, size), lambda k, at: (0, k)),
            ],
        ),
        out_shape=[
            shape_of((tokens, width), bf16),
            shape_of((tokens, 1), f32),
            shape_of((1, width), f32),
        ],
        compiler_params=pltpu.CompilerParams(vmem_limit_bytes=VMEM),
    )(place, dproj, dgate, dlogits, proj, gates, logits, full_qkv, full_outgate, beta_rows, rows, scale)


def back_kernel(*refs):
    (
        proj_ref,
        taps_ref,
        logit_ref,
        x_ref,
        wu_ref,
        state_ref,
        drule_ref,
    ) = refs[:7]
    dproj_ref, last_ref, first_ref, dtaps_ref, dlogit_ref = refs[-5:]
    others = refs[7:-5]
    count = (len(others) + 1) // 2
    directs, nexts = others[:count], others[count:]
    heads = state_ref.shape[1]
    taps = taps_ref[...]
    length = proj_ref.shape[2] - HALO
    betas = jax.nn.sigmoid(logit_ref[0])
    r, c = places(length, length)
    strict = (r > c).astype(f32)
    full = (r >= c).astype(f32)
    zeros = jnp.zeros((PAD, DK), f32)
    for h in range(heads):
        parts, (qu, q_inv), (ku, k_inv), vu = rule_inputs(proj_ref, taps, h)
        q, k, v = qu.astype(bf16), ku.astype(bf16), vu.astype(bf16)
        beta = betas[:, h : h + 1]
        leave = jnp.zeros((DK, DK), f32)
        for j in reversed(range(count)):
            here = directs[j][0, h].astype(f32)
            leave = here if j == count - 1 else mm(nexts[j][0, h], leave, 0, 0) + here
        state = state_ref[0, h]
        wu = wu_ref[0, h]
        u = wu[:, DK:] - mm(wu[:, :DK], state)
        resid = v.astype(f32) - mm(k, state)
        dout = drule_ref[0, :, head_slice(h)] * DK ** (-0.5)
        gram = mm(k, k, 1, 1)
        scores = mm(q, k, 1, 1) * full
        du = mm(scores, dout, 0, 0) + mm(k, leave)
        y = mm(x_ref[0, h], du, 0, 0)
        by = beta * y
        da = -(mm(y, u, 1, 1) * strict)
        dbeta = jnp.sum(y * resid, -1, keepdims=True) + jnp.sum(da * gram, -1, keepdims=True)
        dgram = beta * da
        dscores = mm(dout, u, 1, 1) * full
        dq = mm(dout, state, 1, 1) + mm(dscores, k)
        dk = (
            mm(dgram, k)
            + mm(dgram, k, 0, 0)
            + mm(dscores, q, 0, 0)
            + mm(u, leave, 1, 1)
            - mm(by, state, 1, 1)
        )
        dlogit_ref[0, :, h : h + 1] = (dbeta * beta * (1.0 - beta)).astype(bf16)
        dq = (dq - qu * jnp.sum(qu * dq, -1, keepdims=True)) * q_inv
        dk = (dk - ku * jnp.sum(ku * dk, -1, keepdims=True)) * k_inv
        for i, dact in enumerate((dq, dk, by)):
            shifts, out, sig, _ = parts[i]
            dconv = dact * sig * (1.0 + out * (1.0 - sig))
            ext = jnp.concatenate([zeros, dconv, zeros], 0)
            total = None
            for j in range(KW):
                at = i * KW + j
                dtaps_ref[0, at : at + 1, head_slice(h)] = jnp.sum(
                    dconv * shifts[j], 0, keepdims=True
                )
                tap = taps[at : at + 1, head_slice(h)]
                term = tap * ext[KW - 1 - j : KW - 1 - j + PAD + length]
                total = term if total is None else total + term
            first_ref[i, 0, :, head_slice(h)] = total[:PAD]
            last_ref[i, 0, :, head_slice(h)] = total[length:]
            dproj_ref[i, 0, :, head_slice(h)] = total[PAD:].astype(bf16)


def per_sequence(kernel, ins, outs, scalar=None, scratch=(), limit=VMEM):
    def spec(shape, axis):
        block = tuple(1 if n == axis else size for n, size in enumerate(shape))
        where = lambda s, *_: tuple(s if n == axis else 0 for n in range(len(shape)))
        if axis is None:
            return pl.BlockSpec(block, where, pipeline_mode=pl.Buffered(1))
        return pl.BlockSpec(block, where)

    shape, axis = outs[0]
    given = [] if scalar is None else [scalar]
    return pl.pallas_call(
        kernel,
        grid_spec=pltpu.PrefetchScalarGridSpec(
            num_scalar_prefetch=len(given),
            grid=(shape.shape[axis],),
            in_specs=[spec(a.shape, axis) for a, axis in ins],
            out_specs=[spec(o.shape, axis) for o, axis in outs],
            scratch_shapes=scratch,
        ),
        out_shape=[o for o, _ in outs],
        compiler_params=pltpu.CompilerParams(vmem_limit_bytes=limit),
    )(*given, *[a for a, _ in ins])


def shape_of(shape, dtype):
    return jax.ShapeDtypeStruct(shape, dtype)


def shifted(array, axis, by):
    devices = lax.axis_size(axis)
    pairs = [(i, i + by) for i in range(devices) if 0 <= i + by < devices]
    return lax.ppermute(array, axis, pairs)


def after(values, *others):
    flat, tree = jax.tree.flatten(values)
    others = jax.tree.leaves(others)
    here = pl.BlockSpec(memory_space=pl.ANY)
    out = pl.pallas_call(
        lambda *refs: None,
        in_specs=[here] * (len(flat) + len(others)),
        out_specs=[here] * len(flat),
        out_shape=[shape_of(a.shape, a.dtype) for a in flat],
        input_output_aliases={n: n for n in range(len(flat))},
    )(*flat, *others)
    return jax.tree.unflatten(tree, out)


def swap(array, bits):
    return lax.ppermute(array, "dp", [(i, i ^ bits) for i in range(4)])


def first_hop(own):
    return swap(own, 1), swap(own, 2)


def gathered_pieces(own, axis, hop, *others):
    low, high = (jnp.split(part, 2, axis) for part in hop)
    low, high = low[0], high[1]
    if others:
        low, high = after((low, high), *others)
    return [own, *hop, swap(low, 2), swap(high, 1)]


def add(a, b):
    return (a.astype(f32) + b.astype(f32)).astype(bf16)


def far_hop(far, split_axis, *others):
    low, high = jnp.split(far, 2, split_axis)
    if others:
        low, high = after((low, high), *others)
    return swap(low, 1), swap(high, 2)


def near_sums(pieces, far_in, split_axis):
    own, one, two = pieces
    one = jnp.split(one, 2, split_axis)
    two = jnp.split(two, 2, split_axis)
    one = jnp.concatenate([one[0], add(one[1], far_in[1])], split_axis)
    two = jnp.concatenate([add(two[0], far_in[0]), two[1]], split_axis)
    return own, one, two


def sum_first(array, axis, split_axis, *others):
    pieces = jnp.split(array, 4, axis)
    return near_sums(pieces[:3], far_hop(pieces[3], split_axis, *others), split_axis)


def sum_second(parts, *others):
    own, one, two = parts
    if others:
        one, two = after((one, two), *others)
    return own, swap(one, 1), swap(two, 2)


def sum_last(parts, *others):
    own, one, two = parts
    if others:
        one, two = after((one, two), *others)
    return own.astype(f32) + one.astype(f32) + two.astype(f32)


def pack(parts):
    return jnp.concatenate([p.reshape(-1) for p in parts])


def unpack(flat, shapes):
    out, at = [], 0
    for shape in shapes:
        size = 1
        for n in shape:
            size *= n
        out.append(flat[..., at : at + size].reshape(flat.shape[:-1] + tuple(shape)))
        at += size
    return out


def padded(flat, multiple=1024):
    return jnp.pad(flat, (0, -flat.shape[0] % multiple))


def body(
    tokens,
    out_grad,
    domain,
    group_weight,
    w_qkv,
    conv_weight,
    w_beta,
    w_outgate,
    head_gain,
    w_out,
    mixer_gain,
    mlp_gain,
    w_gateup,
    w_down,
):
    dp = lax.axis_size("dp")
    place = lax.axis_index("dp")
    seqs, block, local_width = tokens.shape
    count_rows = seqs * block
    heads = conv_weight.shape[2]
    inner = heads * DK
    column = lax.axis_index("mp") * local_width
    near_four = dp == 4

    def blocks_about(array, axis):
        if not near_four:
            return array
        size = array.shape[axis] // 4
        return jnp.concatenate(
            [lax.dynamic_slice_in_dim(array, (place ^ k) * size, size, axis) for k in range(4)],
            axis,
        )

    width = out_grad.shape[2]
    turn = place if near_four else jnp.int32(0)
    column_about = ((column // (width // 4)) ^ turn) * (width // 4) + column % (width // 4)

    def own(array):
        array = array.reshape(seqs, block, width)
        return lax.dynamic_slice_in_dim(array, column_about, local_width, 2)

    onehot = (domain[..., None] == jnp.arange(3, dtype=jnp.int32)).astype(f32)
    own_counts = jnp.sum(onehot, axis=(0, 1))
    high = jnp.floor(own_counts / 128.0)
    digits = jnp.concatenate([high, own_counts - 128.0 * high]).astype(bf16)
    small = [w_beta, conv_weight, head_gain, mixer_gain, mlp_gain, digits]
    packed = padded(pack(small))
    halo = shifted(tokens[:, block - HALO :], "dp", 1)
    if near_four:
        qkv_hop = first_hop(w_qkv)
        halo = lax.all_gather(halo, "mp", axis=2, tiled=True)
        qkv = gathered_pieces(w_qkv, 1, qkv_hop, halo)
        packed = after(packed, halo)
        gathered = jnp.stack([packed] + [swap(packed, bits) for bits in (1, 2, 3)])
        half = w_out.shape[1] // 2
        pair_own = jnp.stack(
            [w_outgate, jnp.concatenate([w_out[:, :half], w_out[:, half:]], 0)]
        )
        pair_own = after(pair_own, qkv[-2:])
        pair_in = [swap(pair_own, bits) for bits in (1, 2, 3)]
        size = width // 4
        layout = [(0, 0, size, size), (1, 0, size, size), (2, 0, size, size)]
        layout += [(3, 0, size // 2, size), (3, size // 2, size // 2, size)]
    else:
        halo = lax.all_gather(halo, "mp", axis=2, tiled=True)
        gathered = lax.all_gather(packed, "dp")
        qkv = [lax.all_gather(w_qkv, "dp", axis=1, tiled=True)]
        layout = [(0, 0, width, width)]
    g_beta, g_conv, g_head, g_mix, g_mlp, g_digits = unpack(gathered, [a.shape for a in small])
    about_beta = g_beta.reshape(-1, heads)
    full_beta = blocks_about(about_beta, 0)
    full_conv = jnp.moveaxis(blocks_about(g_conv, 0), 0, 3).reshape(3 * KW, inner).astype(f32)
    gain_head = blocks_about(g_head, 0).reshape(1, DK).astype(f32)
    gain_one = blocks_about(g_mix.reshape(1, -1).astype(f32), 1)
    gain_two = g_mlp.reshape(1, -1).astype(f32)
    sums = jnp.sum(g_digits.astype(f32), 0)
    counts = 128.0 * sums[:3] + sums[3:]

    rows = lax.all_gather(tokens, "mp", axis=2, tiled=True)

    hidden_one, proj, logits, scale_one = per_sequence(
        partial(project_kernel, layout),
        [(rows, 0), (halo, 0), (gain_one, None), (jnp.pad(full_beta, ((0, 0), (0, 128 - heads))), None)]
        + [(a, None) for a in qkv],
        [
            (shape_of((seqs, block, width), bf16), 0),
            (shape_of((3, seqs, HALO + block, inner), bf16), 1),
            (shape_of((seqs, block, heads), f32), 0),
            (shape_of((seqs, block, 1), f32), 0),
        ],
        scalar=turn.reshape(1),
        scratch=[pltpu.VMEM((HALO + block, width), bf16)],
    )
    hidden_one = hidden_one.reshape(count_rows, width)
    square = (seqs, heads, DK, DK)
    inverse, wu, qo, to = per_sequence(
        pre_kernel,
        [(proj, 1), (full_conv, None), (logits, 0)],
        [
            (shape_of((seqs, heads, block, block), f32), 0),
            (shape_of((seqs, heads, block, 2 * DK), f32), 0),
            (shape_of((seqs, heads, block, 2 * DK), f32), 0),
            (shape_of((seqs, heads, DK, 2 * DK), bf16), 0),
        ],
    )
    near = [shifted(to, "dp", c) for c in range(1, dp)]
    rows = blocks_about(rows, 2)
    if near_four:
        full_outgate = jnp.concatenate([w_outgate] + [a[0] for a in pair_in], 0)
        full_out = jnp.concatenate(
            [w_out] + [part for a in pair_in for part in jnp.split(a[1], 2, 0)], 1
        )
        full_qkv = jnp.concatenate(qkv, 1)
    else:
        full_outgate = lax.all_gather(w_outgate, "dp", axis=0, tiled=True)
        full_out = lax.all_gather(w_out, "dp", axis=1, tiled=True)
        full_qkv = qkv[0]
    gates = jnp.dot(hidden_one, full_outgate, preferred_element_type=f32)
    gates = gates.reshape(seqs, block, inner)
    mixer_part, normed, rule, state = per_sequence(
        mix_kernel,
        [(a, 0) for a in near] + [(qo, 0), (gates, 0), (gain_head, None), (full_out, None)],
        [
            (shape_of((seqs, block, width), bf16), 0),
            (shape_of((seqs, block, inner), bf16), 0),
            (shape_of((seqs, block, inner), f32), 0),
            (shape_of(square, f32), 0),
        ],
    )
    normed = normed.reshape(count_rows, inner)
    total = lax.psum(mixer_part, "mp")
    nexts = [shifted(after(to[..., :DK], mixer_part), "dp", -c) for c in range(1, dp - 1)]
    table = group_weight * (domain.shape[0] * domain.shape[1] * dp) / counts
    factor = jnp.sum(onehot * table, -1)
    cotangent = (blocks_about(out_grad, 2).astype(f32) * factor[..., None]).astype(bf16)
    if near_four:
        own_gateup = after(jnp.swapaxes(w_gateup, 1, 2), mixer_part)
        gateup_hop = first_hop(own_gateup)
        gateup = gathered_pieces(own_gateup, 2, gateup_hop)
        own_down = after(w_down, gateup_hop)
        down = gathered_pieces(own_down, 1, first_hop(own_down))
    else:
        gateup = [lax.all_gather(jnp.swapaxes(w_gateup, 1, 2), "dp", axis=2, tiled=True)]
        down = [lax.all_gather(w_down, "dp", axis=1, tiled=True)]
    hidden_units = w_down.shape[0]
    two_part, hidden_two, hidden_mlp, grad_pair = per_sequence(
        partial(feed_kernel, layout),
        [(rows, 0), (total, 0), (cotangent, 0), (gain_two, None)]
        + [(a, None) for a in gateup + down],
        [
            (shape_of((seqs, block, width), bf16), 0),
            (shape_of((seqs, block, width), bf16), 0),
            (shape_of((seqs, block, hidden_units), bf16), 0),
            (shape_of((2, seqs, block, hidden_units), bf16), 1),
        ],
        limit=36 * 2**20,
    )
    grad_two = lax.psum(two_part, "mp")

    hidden_two = hidden_two.reshape(count_rows, width)
    hidden_mlp = hidden_mlp.reshape(count_rows, hidden_units)
    grad_pair = grad_pair.reshape(2, count_rows, hidden_units)

    def gateup_gradient(columns):
        return jnp.einsum("itf,td->ifd", grad_pair, columns, preferred_element_type=f32).astype(bf16)

    grad_down = jnp.einsum(
        "tf,td->fd", hidden_mlp, cotangent.reshape(count_rows, width), preferred_element_type=f32
    ).astype(bf16)
    if near_four:
        cut = 3 * width // 4
        gateup_far_in = far_hop(gateup_gradient(hidden_two[:, cut:]), 0)
        down_first = sum_first(grad_down, 1, 0, gateup_far_in)
        gateup_near = jnp.split(gateup_gradient(hidden_two[:, :cut]), 3, 2)
        gateup_sums = sum_second(near_sums(gateup_near, gateup_far_in, 0))
        full_down = jnp.concatenate(down, 1)
    else:
        grad_gateup = gateup_gradient(hidden_two)
        full_down = down[0]
    down_part = jnp.dot(hidden_mlp, full_down, preferred_element_type=f32).astype(bf16)
    down_part = blocks_about(down_part.reshape(seqs, block, width), 2)
    mlp_share = lax.psum_scatter(down_part, "mp", scatter_dimension=2, tiled=True).astype(f32)

    grad_mix, middle_own, mlpgain, drule, dgate, dgain, direct = per_sequence(
        middle_back_kernel,
        [
            (grad_two, 0),
            (cotangent, 0),
            (rows, 0),
            (total, 0),
            (gain_two, None),
            (full_out, None),
            (rule, 0),
            (gates, 0),
            (gain_head, None),
            (qo, 0),
        ],
        [
            (shape_of((seqs, block, width), bf16), 0),
            (shape_of((seqs, block, local_width), f32), 0),
            (shape_of((seqs, 1, width), f32), 0),
            (shape_of((seqs, block, inner), f32), 0),
            (shape_of((seqs, block, inner), bf16), 0),
            (shape_of((seqs, 1, DK), f32), 0),
            (shape_of(square, bf16), 0),
        ],
        scalar=column_about.reshape(1),
        scratch=[pltpu.VMEM((block, width), f32)],
    )
    grad_mix = grad_mix.reshape(count_rows, width)
    directs = [shifted(direct, "dp", -c) for c in range(1, dp)]
    dgate = dgate.reshape(count_rows, inner)
    grad_outgate = jnp.einsum("td,tc->dc", hidden_one, dgate, preferred_element_type=f32)
    grad_outgate = grad_outgate.astype(bf16)
    grad_outproj = jnp.einsum("tc,td->cd", normed, grad_mix, preferred_element_type=f32)
    grad_outproj = grad_outproj.astype(bf16)
    if near_four:
        parts = [jnp.split(a, 2, 1) for a in jnp.split(grad_outproj, 4, 1)]
        pair_grad = jnp.stack(
            [grad_outgate.reshape(4, -1, inner), jnp.stack([jnp.concatenate(p, 0) for p in parts])],
            1,
        )
        down_sums = sum_second(down_first, directs)
    dproj, last, first, dtaps, dlogits = per_sequence(
        back_kernel,
        [
            (proj, 1),
            (full_conv, None),
            (logits, 0),
            (inverse, 0),
            (wu, 0),
            (state, 0),
            (drule, 0),
        ]
        + [(a, 0) for a in directs + nexts],
        [
            (shape_of((3, seqs, block, inner), bf16), 1),
            (shape_of((3, seqs, PAD, inner), f32), 1),
            (shape_of((3, seqs, PAD, inner), f32), 1),
            (shape_of((seqs, 3 * KW, inner), f32), 0),
            (shape_of((seqs, block, heads), bf16), 0),
        ],
    )
    later = shifted(first, "dp", -1)
    dproj = lax.dynamic_update_slice(dproj, (last + later).astype(bf16), (0, 0, block - PAD, 0))
    dproj = dproj.reshape(3, count_rows, inner)
    dlogits = dlogits.reshape(count_rows, heads)
    grad_qkv = jnp.einsum("td,itc->idc", hidden_one, dproj, preferred_element_type=f32)
    grad_qkv = grad_qkv.astype(bf16)
    late_proj = after(dproj, grad_qkv)
    one_low, row_part, gain_part = first_back(
        turn.reshape(1),
        late_proj,
        dgate,
        dlogits,
        proj,
        gates.reshape(count_rows, inner),
        logits.reshape(count_rows, heads),
        full_qkv,
        full_outgate,
        about_beta.T.astype(f32),
        rows.reshape(count_rows, width),
        scale_one.reshape(count_rows, 1),
    )
    one_share = lax.psum_scatter(
        one_low.reshape(seqs, block, width), "mp", scatter_dimension=2, tiled=True
    ).astype(f32)
    stats = [row_part[:, 0], gain_part[0], jnp.sum(dgain, (0, 1))]
    stat_sum = jnp.sum(lax.all_gather(pack(stats), "mp"), 0)
    row_sum, mixgain_sum, headgain_sum = unpack(stat_sum, [a.shape for a in stats])
    if near_four:
        qkv_sums = sum_second(sum_first(grad_qkv, 1, 1), stat_sum)
        pair_sums = sum_second(sum_first(pair_grad, 0, 1, stat_sum))
    grad_beta = jnp.einsum("td,th->dh", hidden_one, dlogits, preferred_element_type=f32)

    def pieces(array, axis, about):
        shape = array.shape
        cut = array.reshape(shape[:axis] + (dp, shape[axis] // dp) + shape[axis + 1 :])
        cut = jnp.moveaxis(cut, axis, 0).reshape(dp, -1)
        return blocks_about(cut, 0) if about else cut

    smalls = jnp.concatenate(
        [
            pieces(jnp.sum(dtaps, 0).reshape(3, KW, heads, DK), 3, True),
            pieces(grad_beta, 0, False),
            pieces(headgain_sum, 0, True),
            pieces(mixgain_sum, 0, False),
            pieces(jnp.sum(mlpgain, (0, 1)), 0, False),
        ],
        1,
    )
    if near_four:
        mine = smalls[0]
        for bits in (1, 2, 3):
            mine = mine + swap(padded(smalls[bits].astype(bf16)), bits)[: mine.shape[0]].astype(f32)
        sum_qkv = sum_last(qkv_sums)
        sum_gateup, sum_down, sum_pair = (
            jnp.swapaxes(sum_last(gateup_sums, stat_sum), 1, 2),
            sum_last(down_sums, stat_sum),
            sum_last(pair_sums),
        )
        sum_outgate = sum_pair[0, 0]
        sum_out = jnp.concatenate(jnp.split(sum_pair[0, 1], 2, 0), 1)
    else:
        everyone = lax.all_gather(smalls.astype(bf16), "dp")
        mine = jnp.sum(
            lax.dynamic_index_in_dim(everyone, place, 1, keepdims=False).astype(f32), 0
        )

        def scattered(array, axis):
            return lax.psum_scatter(array, "dp", scatter_dimension=axis, tiled=True).astype(f32)

        sum_qkv, sum_outgate = scattered(grad_qkv, 1), scattered(grad_outgate, 0)
        sum_out = scattered(grad_outproj, 1)
        sum_gateup = jnp.swapaxes(scattered(grad_gateup, 2), 1, 2)
        sum_down = scattered(grad_down, 1)
    sum_conv, sum_beta, sum_head, sum_mix, sum_mlp = unpack(
        mine,
        [conv_weight.shape, w_beta.shape, head_gain.shape, mixer_gain.shape, mlp_gain.shape],
    )

    own_tokens = tokens.astype(f32)
    mixed_out = (own_tokens + own(total).astype(f32) + mlp_share).astype(bf16)
    row_mean = (row_sum / width).reshape(seqs, block, 1)
    gain_own = lax.dynamic_slice_in_dim(gain_one, column, local_width, 1)
    tokens_grad = middle_own + scale_one * (
        one_share * gain_own - own_tokens * scale_one * row_mean
    )
    return (
        mixed_out,
        tokens_grad.astype(bf16),
        sum_qkv,
        sum_conv,
        sum_beta,
        sum_outgate,
        sum_head,
        sum_out,
        sum_mix,
        sum_mlp,
        sum_gateup,
        sum_down,
    )


def solution(mesh):
    return jax.shard_map(
        body,
        mesh=mesh,
        in_specs=(
            P(None, "dp", "mp"),
            P(None, "dp", None),
            P(None, "dp"),
            P(),
            P(None, "dp", "mp"),
            P(None, None, "mp", "dp"),
            P("dp", "mp"),
            P("dp", "mp"),
            P("dp"),
            P("mp", "dp"),
            P("dp"),
            P("dp"),
            P(None, "dp", "mp"),
            P("mp", "dp"),
        ),
        out_specs=(
            P(None, "dp", "mp"),
            P(None, "dp", "mp"),
            P(None, "dp", "mp"),
            P(None, None, "mp", "dp"),
            P("dp", "mp"),
            P("dp", "mp"),
            P("dp"),
            P("mp", "dp"),
            P("dp"),
            P("dp"),
            P(None, "dp", "mp"),
            P("mp", "dp"),
        ),
        check_vma=False,
    )
```

```python
from functools import partial

import jax
import jax.numpy as jnp
from jax import lax
from jax.experimental import pallas as pl
from jax.experimental.pallas import tpu as pltpu
from jax.sharding import PartitionSpec as P

DK = 128
KW = 4
PAD = 8
HALO = 16
VMEM = 58 * 2**20

eps_norm = 1e-06
eps_unit = 1e-06

f32 = jnp.float32
bf16 = jnp.bfloat16


def split(v):
    if v.dtype == bf16:
        return v, None
    high = v.astype(bf16)
    return high, (v - high.astype(f32)).astype(bf16)


def mm(a, b, ca=1, cb=0, passes=3):
    def one(x, y):
        return lax.dot_general(x, y, (((ca,), (cb,)), ((), ())), preferred_element_type=f32)

    if passes == 1:
        return one(a.astype(bf16), b.astype(bf16))
    (ah, al), (bh, bl) = split(a), split(b)
    out = one(ah, bh)
    if bl is not None:
        out = out + one(ah, bl)
    if al is not None:
        out = out + one(al, bh)
    return out


def places(rows, cols):
    return (
        lax.broadcasted_iota(jnp.int32, (rows, cols), 0),
        lax.broadcasted_iota(jnp.int32, (rows, cols), 1),
    )


def unit_lower_inverses(blocks):
    size = blocks[0].shape[0]
    if size > 128:
        half = size // 2
        parts = unit_lower_inverses(
            [a[:half, :half] for a in blocks] + [a[half:, half:] for a in blocks]
        )
        firsts, seconds = parts[: len(blocks)], parts[len(blocks) :]
        inner = [mm(a[half:, :half], x) for a, x in zip(blocks, firsts)]
        lower = [-mm(x, y) for x, y in zip(seconds, inner)]
        zero = jnp.zeros((half, half), f32)
        return [
            jnp.concatenate(
                [jnp.concatenate([x, zero], 1), jnp.concatenate([y, z], 1)], 0
            )
            for x, y, z in zip(firsts, lower, seconds)
        ]
    rows, cols = places(size, size)
    eye = (rows == cols).astype(f32)
    level = 0
    inverses = None
    while (1 << level) < size:
        mask = (
            ((rows >> (level + 1)) == (cols >> (level + 1)))
            & (((rows >> level) & 1) == 1)
            & (((cols >> level) & 1) == 0)
        ).astype(f32)
        lows = [a * mask for a in blocks]
        if level == 0:
            inverses = [eye - low for low in lows]
        else:
            inner = [mm(low, x) for low, x in zip(lows, inverses)]
            inverses = [x - mm(x, y) for x, y in zip(inverses, inner)]
        level += 1
    return inverses


def head_slice(h):
    return slice(h * DK, (h + 1) * DK)


def convolve(proj_ref, before_ref, taps, i, h):
    own = proj_ref[i, 0, :, head_slice(h)].astype(f32)
    length = own.shape[0]
    ext = jnp.concatenate([before_ref[i, 0, :, head_slice(h)].astype(f32), own], 0)
    shifts = [ext[HALO - KW + 1 + j : HALO - KW + 1 + j + length] for j in range(KW)]
    out = None
    for j in range(KW):
        tap = taps[i * KW + j : i * KW + j + 1, head_slice(h)]
        out = tap * shifts[j] if out is None else out + tap * shifts[j]
    sig = jax.nn.sigmoid(out)
    return shifts, out, sig, out * sig


def unit(acts):
    inv = lax.rsqrt(jnp.sum(acts * acts, -1, keepdims=True) + eps_unit)
    return acts * inv, inv


def rule_inputs(proj_ref, before_ref, taps, h):
    parts = [convolve(proj_ref, before_ref, taps, i, h) for i in range(3)]
    q, q_inv = unit(parts[0][3])
    k, k_inv = unit(parts[1][3])
    return parts, (q, q_inv), (k, k_inv), parts[2][3]


def norm_factor(values):
    return lax.rsqrt(jnp.mean(values * values, -1, keepdims=True) + eps_norm)


def project_kernel(layout, *refs):
    place_ref, rows_ref, gain_ref, beta_ref = refs[:4]
    pieces = refs[4 : 4 + len(layout)]
    hidden_ref, proj_ref, tail_ref, logit_ref, scale_ref, keep_ref = refs[4 + len(layout) :]
    rows = rows_ref[0].astype(f32)
    scale = norm_factor(rows)
    scale_ref[0] = scale
    keep_ref[...] = (rows * scale * gain_ref[...]).astype(bf16)
    logits = mm(keep_ref[...], beta_ref[...])
    logit_ref[0] = logits[:, : logit_ref.shape[2]]
    sums = [None] * 3
    for (k, start, size, block), piece in zip(layout, pieces):
        at = pl.multiple_of((place_ref[0] ^ k) * block + start, 128)
        part = keep_ref[:, pl.ds(at, size)]
        hidden_ref[0, :, k * block + start : k * block + start + size] = part
        for i in range(3):
            term = mm(part, piece[i])
            sums[i] = term if sums[i] is None else sums[i] + term
    for i in range(3):
        low = sums[i].astype(bf16)
        proj_ref[i, 0] = low
        tail_ref[i, 0] = low[low.shape[0] - HALO :]


def pre_kernel(proj_ref, before_ref, taps_ref, logit_ref, x_ref, wu_ref, qo_ref, to_ref):
    heads = to_ref.shape[1]
    taps = taps_ref[...]
    length = proj_ref.shape[2]
    betas = jax.nn.sigmoid(logit_ref[0])
    r, c = places(length, length)
    strict = (r > c).astype(f32)
    full = (r >= c).astype(f32)
    saved, blocks = [], []
    for h in range(heads):
        _, (q, _), (k, _), v = rule_inputs(proj_ref, before_ref, taps, h)
        q, k, v = q.astype(bf16), k.astype(bf16), v.astype(bf16)
        beta = betas[:, h : h + 1]
        gram = mm(k, k, 1, 1)
        blocks.append(beta * gram * strict)
        saved.append((q, k, v, beta))
    inverses = unit_lower_inverses(blocks)
    r, c = places(DK, DK)
    eye = (r == c).astype(f32)
    for h in range(heads):
        q, k, v, beta = saved[h]
        x = inverses[h]
        x_ref[0, h] = x
        kv = jnp.concatenate([k.astype(f32), v.astype(f32)], 1) * beta
        wu = mm(x, kv)
        wu_ref[0, h] = wu
        scores = mm(q, k, 1, 1) * full
        pwu = mm(scores, wu)
        qo_ref[0, h, :, :DK] = q.astype(f32) - pwu[:, :DK]
        qo_ref[0, h, :, DK:] = pwu[:, DK:]
        kwu = mm(k, wu, 0, 0)
        to_ref[0, h, :, :DK] = (eye - kwu[:, :DK]).astype(bf16)
        to_ref[0, h, :, DK:] = kwu[:, DK:].astype(bf16)


def gate_kernel(layout, hidden_ref, *refs):
    gate_ref = refs[-1]
    total = None
    for (k, start, size, block), ref in zip(layout, refs[:-1]):
        at = k * block + start
        term = mm(hidden_ref[0, :, at : at + size], gate_part(ref)[...])
        total = term if total is None else total + term
    gate_ref[0] = total


def gate_part(ref):
    return ref.at[0] if len(ref.shape) == 3 else ref


def out_columns(layout, refs):
    for (k, start, size, block), ref in zip(layout, refs):
        at, half = k * block + start, size // 2
        if len(ref.shape) == 2:
            yield at, size, ref
            continue
        inner = ref.shape[1] // 2
        yield at, half, ref.at[1, :inner]
        yield at + half, half, ref.at[1, inner:]


def mix_kernel(layout, count, *refs):
    near, rest = refs[:count], refs[count:]
    qo_ref, gate_ref, gain_ref = rest[:3]
    outs, (_, part_ref, normed_ref, rule_ref, state_ref) = rest[3 : 3 + len(layout)], rest[3 + len(layout) :]
    heads = state_ref.shape[1]
    for h in range(heads):
        state = near[-1][0, h, :, DK:].astype(f32)
        for ref in reversed(near[:-1]):
            state = mm(ref[0, h, :, :DK], state) + ref[0, h, :, DK:].astype(f32)
        state_ref[0, h] = state
        qo = qo_ref[0, h]
        out = (mm(qo[:, :DK], state) + qo[:, DK:]) * DK ** (-0.5)
        rule_ref[0, :, head_slice(h)] = out
        gate = gate_ref[0, :, head_slice(h)]
        normed = out * norm_factor(out) * gain_ref[...] * (gate * jax.nn.sigmoid(gate))
        normed_ref[0, :, head_slice(h)] = normed.astype(bf16)
    for at, size, ref in out_columns(layout, outs):
        part_ref[0, :, at : at + size] = mm(normed_ref[0], ref[...]).astype(bf16)


def prepare_kernel(layout, place_ref, rows_ref, grad_ref, factor_ref, about_ref, cot_ref):
    for k, start, size, block in layout:
        at = pl.multiple_of((place_ref[0] ^ k) * block + start, 128)
        to = slice(k * block + start, k * block + start + size)
        about_ref[0, :, to] = rows_ref[0, :, pl.ds(at, size)]
        grad = grad_ref[0, :, pl.ds(at, size)].astype(f32) * factor_ref[0]
        cot_ref[0, :, to] = grad.astype(bf16)


def down_kernel(layout, place_ref, mlp_ref, *refs):
    part_ref = refs[-1]
    for (k, start, size, block), ref in zip(layout, refs[:-1]):
        at = pl.multiple_of((place_ref[0] ^ k) * block + start, 128)
        part_ref[0, :, pl.ds(at, size)] = mm(mlp_ref[0], ref[...]).astype(bf16)


def feed_gradient_kernel(ranges, hidden_ref, cot_ref, pair_ref, mlp_ref, *outs):
    for n, (start, size) in enumerate(ranges):
        hidden = hidden_ref[:, start : start + size]
        outs[2 * n][0] = mm(pair_ref[0], hidden, 0, 0).astype(bf16)
        outs[2 * n][1] = mm(pair_ref[1], hidden, 0, 0).astype(bf16)
        outs[2 * n + 1][0] = mm(mlp_ref[...], cot_ref[:, start : start + size], 0, 0).astype(bf16)


def qkv_gradient_kernel(ranges, hidden_ref, dproj_ref, dlogit_ref, *outs):
    outs = outs[-len(ranges) - 1 :]
    for (start, size), out in zip(ranges, outs[:-1]):
        hidden = hidden_ref[:, start : start + size]
        for i in range(3):
            out[i] = mm(hidden, dproj_ref[i], 0, 0).astype(bf16)
    outs[-1][...] = mm(dlogit_ref[...], hidden_ref[...], 0, 0)


def pair_gradient_kernel(ranges, hidden_ref, dgate_ref, normed_ref, mix_ref, *outs):
    inner = normed_ref.shape[1]
    for (start, size), out in zip(ranges, outs):
        out[0] = mm(hidden_ref[:, start : start + size], dgate_ref[...], 0, 0).astype(bf16)
        for n in range(2):
            at = start + n * size // 2
            mix = mix_ref[:, at : at + size // 2]
            out[1, n * inner : (n + 1) * inner] = mm(normed_ref[...], mix, 0, 0).astype(bf16)


def add_halves_kernel(one_ref, two_ref, low_ref, high_ref, one_out, two_out):
    def add(a, b):
        return (a.astype(f32) + b.astype(f32)).astype(bf16)

    half = low_ref.shape
    rows = slice(0, half[1])
    if half[1] < one_ref.shape[1]:
        late, lanes, late_lanes = slice(half[1], 2 * half[1]), slice(None), slice(None)
    else:
        late, lanes, late_lanes = rows, slice(0, half[2]), slice(half[2], 2 * half[2])
    one_out[...] = one_ref[...]
    two_out[...] = two_ref[...]
    one_out[0, late, late_lanes] = add(one_ref[0, late, late_lanes], high_ref[0])
    two_out[0, rows, lanes] = add(two_ref[0, rows, lanes], low_ref[0])


def add_last_kernel(*refs):
    own_ref, one_ref, two_ref, out_ref = refs[:3] + refs[-1:]
    out_ref[...] = own_ref[...].astype(f32) + one_ref[...].astype(f32) + two_ref[...].astype(f32)


def feed_kernel(layout, *refs):
    rows_ref, total_ref, cot_ref, gain_ref = refs[:4]
    count = len(layout)
    gateups, downs = (refs[4 + n * count : 4 + (n + 1) * count] for n in range(2))
    two_ref, hidden_ref, mlp_ref, pair_ref = refs[4 + 2 * count :]
    middle = rows_ref[0].astype(f32) + total_ref[0].astype(f32)
    hidden_ref[0] = (middle * norm_factor(middle) * gain_ref[...]).astype(bf16)
    gate, up, grad = None, None, None
    for (k, start, size, block), w_gateup, w_down in zip(layout, gateups, downs):
        lanes = slice(k * block + start, k * block + start + size)
        hidden = hidden_ref[0, :, lanes]
        terms = (
            mm(hidden, w_gateup[0], 1, 1),
            mm(hidden, w_gateup[1], 1, 1),
            mm(cot_ref[0, :, lanes], w_down[...], 1, 1),
        )
        if gate is None:
            gate, up, grad = terms
        else:
            gate, up, grad = gate + terms[0], up + terms[1], grad + terms[2]
    sig = jax.nn.sigmoid(gate)
    silu = gate * sig
    mlp_ref[0] = (silu * up).astype(bf16)
    first = (grad * up * sig * (1.0 + gate * (1.0 - sig))).astype(bf16)
    second = (grad * silu).astype(bf16)
    pair_ref[0, 0] = first
    pair_ref[1, 0] = second
    for (k, start, size, block), w_gateup in zip(layout, gateups):
        lanes = slice(k * block + start, k * block + start + size)
        two = mm(first, w_gateup[0]) + mm(second, w_gateup[1])
        two_ref[0, :, lanes] = two.astype(bf16)


def middle_back_kernel(layout, at_ref, *refs):
    two_ref, cot_ref, rows_ref, total_ref, gain_ref, rule_ref, gate_ref, head_gain_ref, qo_ref = refs[:9]
    outs = refs[9 : 9 + len(layout)]
    mix_ref, own_ref, mlpgain_ref, drule_ref, dgate_ref, dgain_ref, direct_ref, keep_ref = refs[-8:]
    middle = rows_ref[0].astype(f32) + total_ref[0].astype(f32)
    factor = norm_factor(middle)
    normal = middle * factor
    two = two_ref[0].astype(f32)
    mlpgain_ref[0] = jnp.sum(two * normal, 0, keepdims=True)
    scaled = two * gain_ref[...]
    mean = jnp.mean(scaled * normal, -1, keepdims=True)
    keep_ref[...] = cot_ref[0].astype(f32) + factor * (scaled - normal * mean)
    width = own_ref.shape[2]
    own_ref[0] = keep_ref[:, pl.ds(pl.multiple_of(at_ref[0], 128), width)]
    mix = keep_ref[...].astype(bf16)
    mix_ref[0] = mix
    grads = None
    for at, size, ref in out_columns(layout, outs):
        term = mm(mix_ref[0, :, at : at + size], ref[...], 1, 1)
        grads = term if grads is None else grads + term
    total = jnp.zeros((1, DK), f32)
    for h in range(direct_ref.shape[1]):
        grad = grads[:, head_slice(h)]
        out = rule_ref[0, :, head_slice(h)]
        gate = gate_ref[0, :, head_slice(h)]
        inv = norm_factor(out)
        n = out * inv
        sig = jax.nn.sigmoid(gate)
        silu = gate * sig
        gg = grad * head_gain_ref[...]
        dn = gg * silu
        drule = inv * (dn - n * jnp.mean(dn * n, -1, keepdims=True))
        drule_ref[0, :, head_slice(h)] = drule
        dgate = gg * n * sig * (1.0 + gate * (1.0 - sig))
        dgate_ref[0, :, head_slice(h)] = dgate.astype(bf16)
        total = total + jnp.sum(grad * n * silu, 0, keepdims=True)
        direct = mm(qo_ref[0, h, :, :DK], drule, 0, 0) * DK ** (-0.5)
        direct_ref[0, h] = direct.astype(bf16)
    dgain_ref[0] = total


def first_back_kernel(layout, pair_layout, place_ref, *refs):
    dproj_ref, dgate_ref, dlogit_ref, proj_ref, gate_ref, logit_ref, beta_ref, rows_ref, scale_ref = refs[:9]
    pieces = refs[9 : 9 + len(layout)]
    pairs = refs[9 + len(layout) : 9 + len(layout) + len(pair_layout)]
    one_ref, rowsum_ref, gainsum_ref = refs[-3:]
    gates = {}
    for (k, start, size, block), ref in zip(pair_layout, pairs):
        gates[k] = ref
    for (k, start, size, block), piece in zip(layout, pieces):
        lanes = slice(k * block + start, k * block + start + size)
        grad = mm(dgate_ref[...], gate_part(gates[k])[start : start + size], 1, 1)
        for i in range(3):
            grad = grad + mm(dproj_ref[i], piece[i], 1, 1)
        for h in range(beta_ref.shape[0]):
            grad = grad + dlogit_ref[:, h : h + 1].astype(f32) * beta_ref[h : h + 1, lanes]
        at = pl.multiple_of((place_ref[0] ^ k) * block + start, 128)
        one_ref[:, pl.ds(at, size)] = grad.astype(bf16)
        gainsum_ref[:, lanes] = jnp.sum(
            grad * (rows_ref[:, lanes].astype(f32) * scale_ref[...]), 0, keepdims=True
        )
    total = dgate_ref[...].astype(f32) * gate_ref[...]
    for i in range(3):
        total = total + dproj_ref[i].astype(f32) * proj_ref[i].astype(f32)
    total = jnp.sum(total, -1, keepdims=True)
    logits = dlogit_ref[...].astype(f32) * logit_ref[...]
    rowsum_ref[...] = total + jnp.sum(logits, -1, keepdims=True)


def back_kernel(*refs):
    (
        proj_ref,
        before_ref,
        taps_ref,
        logit_ref,
        x_ref,
        wu_ref,
        state_ref,
        drule_ref,
    ) = refs[:8]
    dproj_ref, last_ref, first_ref, dtaps_ref, dlogit_ref = refs[-5:]
    others = refs[8:-5]
    count = (len(others) + 1) // 2
    directs, nexts = others[:count], others[count:]
    heads = state_ref.shape[1]
    taps = taps_ref[...]
    length = proj_ref.shape[2]
    betas = jax.nn.sigmoid(logit_ref[0])
    r, c = places(length, length)
    strict = (r > c).astype(f32)
    full = (r >= c).astype(f32)
    zeros = jnp.zeros((PAD, DK), f32)
    for h in range(heads):
        parts, (qu, q_inv), (ku, k_inv), vu = rule_inputs(proj_ref, before_ref, taps, h)
        q, k, v = qu.astype(bf16), ku.astype(bf16), vu.astype(bf16)
        beta = betas[:, h : h + 1]
        leave = jnp.zeros((DK, DK), f32)
        for j in reversed(range(count)):
            here = directs[j][0, h].astype(f32)
            leave = here if j == count - 1 else mm(nexts[j][0, h], leave, 0, 0) + here
        state = state_ref[0, h]
        wu = wu_ref[0, h]
        u = wu[:, DK:] - mm(wu[:, :DK], state)
        resid = v.astype(f32) - mm(k, state)
        dout = drule_ref[0, :, head_slice(h)] * DK ** (-0.5)
        gram = mm(k, k, 1, 1)
        scores = mm(q, k, 1, 1) * full
        du = mm(scores, dout, 0, 0) + mm(k, leave)
        y = mm(x_ref[0, h], du, 0, 0)
        by = beta * y
        da = -(mm(y, u, 1, 1) * strict)
        dbeta = jnp.sum(y * resid, -1, keepdims=True) + jnp.sum(da * gram, -1, keepdims=True)
        dgram = beta * da
        dscores = mm(dout, u, 1, 1) * full
        dq = mm(dout, state, 1, 1) + mm(dscores, k)
        dk = (
            mm(dgram, k)
            + mm(dgram, k, 0, 0)
            + mm(dscores, q, 0, 0)
            + mm(u, leave, 1, 1)
            - mm(by, state, 1, 1)
        )
        dlogit_ref[0, :, h : h + 1] = (dbeta * beta * (1.0 - beta)).astype(bf16)
        dq = (dq - qu * jnp.sum(qu * dq, -1, keepdims=True)) * q_inv
        dk = (dk - ku * jnp.sum(ku * dk, -1, keepdims=True)) * k_inv
        for i, dact in enumerate((dq, dk, by)):
            shifts, out, sig, _ = parts[i]
            dconv = dact * sig * (1.0 + out * (1.0 - sig))
            ext = jnp.concatenate([zeros, dconv, zeros], 0)
            total = None
            for j in range(KW):
                at = i * KW + j
                dtaps_ref[0, at : at + 1, head_slice(h)] = jnp.sum(
                    dconv * shifts[j], 0, keepdims=True
                )
                tap = taps[at : at + 1, head_slice(h)]
                term = tap * ext[KW - 1 - j : KW - 1 - j + PAD + length]
                total = term if total is None else total + term
            first_ref[i, 0, :, head_slice(h)] = total[:PAD]
            last_ref[i, 0, :, head_slice(h)] = total[length:]
            dproj_ref[i, 0, :, head_slice(h)] = total[PAD:].astype(bf16)


def call(kernel, ins, outs, steps, scalar=None, scratch=(), limit=VMEM, alias=None):
    def spec(shape, axis):
        if axis == "any":
            return pl.BlockSpec(memory_space=pl.ANY)
        block = tuple(1 if n == axis else size for n, size in enumerate(shape))
        where = lambda s, *_: tuple(s if n == axis else 0 for n in range(len(shape)))
        if axis is None:
            return pl.BlockSpec(block, where, pipeline_mode=pl.Buffered(1))
        return pl.BlockSpec(block, where)

    given = [] if scalar is None else [scalar]
    return pl.pallas_call(
        kernel,
        grid_spec=pltpu.PrefetchScalarGridSpec(
            num_scalar_prefetch=len(given),
            grid=(steps,),
            in_specs=[spec(a.shape, axis) for a, axis in ins],
            out_specs=[spec(o.shape, axis) for o, axis in outs],
            scratch_shapes=scratch,
        ),
        out_shape=[o for o, _ in outs],
        input_output_aliases=alias or {},
        compiler_params=pltpu.CompilerParams(vmem_limit_bytes=limit),
    )(*given, *[a for a, _ in ins])


def shape_of(shape, dtype):
    return jax.ShapeDtypeStruct(shape, dtype)


def shifted(array, axis, by):
    devices = lax.axis_size(axis)
    pairs = [(i, i + by) for i in range(devices) if 0 <= i + by < devices]
    return lax.ppermute(array, axis, pairs)


def after(values, *others):
    flat, tree = jax.tree.flatten(values)
    others = jax.tree.leaves(others)
    here = pl.BlockSpec(memory_space=pl.ANY)
    out = pl.pallas_call(
        lambda *refs: None,
        in_specs=[here] * (len(flat) + len(others)),
        out_specs=[here] * len(flat),
        out_shape=[shape_of(a.shape, a.dtype) for a in flat],
        input_output_aliases={n: n for n in range(len(flat))},
    )(*flat, *others)
    return jax.tree.unflatten(tree, out)


def swap(array, bits):
    return lax.ppermute(array, "dp", [(i, i ^ bits) for i in range(4)])


def first_hop(own):
    return swap(own, 1), swap(own, 2)


def gathered_pieces(own, axis):
    hop = first_hop(own)
    low, high = (jnp.split(part, 2, axis) for part in hop)
    return [own, *hop, swap(low[0], 2), swap(high[1], 1)]


def far_hop(low, high):
    return swap(low, 1), swap(high, 2)


def near_sums(pieces, far_in):
    own, one, two = pieces
    specs = [(one, 0), (two, 0), (far_in[0], 0), (far_in[1], 0)]
    outs = [(shape_of(a.shape, a.dtype), 0) for a in (one, two)]
    return own, *call(add_halves_kernel, specs, outs, one.shape[0])


def near_hop(pieces):
    own, one, two = pieces
    return own, swap(one, 1), swap(two, 2)


def sum_last(parts, *others):
    own = parts[0]
    ins = [(a, 0) for a in parts] + [(a, "any") for a in others]
    [total] = call(add_last_kernel, ins, [(shape_of(own.shape, f32), 0)], own.shape[0])
    return total


def pack(parts):
    return jnp.concatenate([p.reshape(-1) for p in parts])


def unpack(flat, shapes):
    out, at = [], 0
    for shape in shapes:
        size = 1
        for n in shape:
            size *= n
        out.append(flat[..., at : at + size].reshape(flat.shape[:-1] + tuple(shape)))
        at += size
    return out


def padded(flat, multiple=1024):
    return jnp.pad(flat, (0, -flat.shape[0] % multiple))


def body(
    tokens,
    out_grad,
    domain,
    group_weight,
    w_qkv,
    conv_weight,
    w_beta,
    w_outgate,
    head_gain,
    w_out,
    mixer_gain,
    mlp_gain,
    w_gateup,
    w_down,
):
    dp = lax.axis_size("dp")
    place = lax.axis_index("dp")
    seqs, block, local_width = tokens.shape
    count_rows = seqs * block
    heads = conv_weight.shape[2]
    inner = heads * DK
    column = lax.axis_index("mp") * local_width
    near_four = dp == 4

    def blocks_about(array, axis):
        if not near_four:
            return array
        size = array.shape[axis] // 4
        return jnp.concatenate(
            [lax.dynamic_slice_in_dim(array, (place ^ k) * size, size, axis) for k in range(4)],
            axis,
        )

    width = out_grad.shape[2]
    turn = place if near_four else jnp.int32(0)
    column_about = ((column // (width // 4)) ^ turn) * (width // 4) + column % (width // 4)

    def own(array):
        array = array.reshape(seqs, block, width)
        return lax.dynamic_slice_in_dim(array, column_about, local_width, 2)

    onehot = (domain[..., None] == jnp.arange(3, dtype=jnp.int32)).astype(f32)
    own_counts = jnp.sum(onehot, axis=(0, 1))
    high = jnp.floor(own_counts / 128.0)
    digits = jnp.concatenate([high, own_counts - 128.0 * high]).astype(bf16)
    small = [w_beta, conv_weight, head_gain, mixer_gain, mlp_gain, digits]
    packed = padded(pack(small))
    size = width // 4
    if near_four:
        qkv = gathered_pieces(w_qkv, 1)
        packed = after(packed, qkv[1:3])
        gathered = jnp.stack([packed] + [swap(packed, bits) for bits in (1, 2, 3)])
        half = w_out.shape[1] // 2
        pair_own = jnp.stack(
            [w_outgate, jnp.concatenate([w_out[:, :half], w_out[:, half:]], 0)]
        )
        pair_layout = [(k, 0, size, size) for k in range(4)]
        layout = pair_layout[:3] + [(3, 0, size // 2, size), (3, size // 2, size // 2, size)]
    else:
        gathered = lax.all_gather(packed, "dp")
        qkv = [lax.all_gather(w_qkv, "dp", axis=1, tiled=True)]
        gate_pieces = [lax.all_gather(w_outgate, "dp", axis=0, tiled=True)]
        out_pieces = [lax.all_gather(w_out, "dp", axis=1, tiled=True)]
        layout = pair_layout = [(0, 0, width, width)]
    ranges = [(k * step + start, n) for k, start, n, step in layout]
    g_beta, g_conv, g_head, g_mix, g_mlp, g_digits = unpack(gathered, [a.shape for a in small])
    about_beta = g_beta.reshape(-1, heads)
    full_beta = blocks_about(about_beta, 0)
    full_conv = jnp.moveaxis(blocks_about(g_conv, 0), 0, 3).reshape(3 * KW, inner).astype(f32)
    gain_head = blocks_about(g_head, 0).reshape(1, DK).astype(f32)
    gain_one = blocks_about(g_mix.reshape(1, -1).astype(f32), 1)
    gain_two = g_mlp.reshape(1, -1).astype(f32)
    sums = jnp.sum(g_digits.astype(f32), 0)
    counts = 128.0 * sums[:3] + sums[3:]
    table = group_weight * (domain.shape[0] * domain.shape[1] * dp) / counts
    factor = jnp.sum(onehot * table, -1)[..., None]

    def flat(array):
        return array.reshape(array.shape[:-3] + (count_rows, array.shape[-1]))

    rows = lax.all_gather(tokens, "mp", axis=2, tiled=True)
    turn_one = turn.reshape(1)
    per_token = (seqs, block)
    square = (seqs, heads, DK, DK)
    hidden_one, proj, tail, logits, scale_one = call(
        partial(project_kernel, layout),
        [(rows, 0), (gain_one, None), (jnp.pad(full_beta, ((0, 0), (0, 128 - heads))), None)]
        + [(a, None) for a in qkv],
        [
            (shape_of(per_token + (width,), bf16), 0),
            (shape_of((3,) + per_token + (inner,), bf16), 1),
            (shape_of((3, seqs, HALO, inner), bf16), 1),
            (shape_of(per_token + (heads,), f32), 0),
            (shape_of(per_token + (1,), f32), 0),
        ],
        seqs,
        scalar=turn_one,
        scratch=[pltpu.VMEM((block, width), bf16)],
    )
    before = shifted(tail, "dp", 1)
    if near_four:
        pair_late = after(pair_own, tail)
        gate_pieces = [pair_own] + [swap(pair_late, bits) for bits in (1, 2, 3)]
        out_pieces = gate_pieces
    inverse, wu, qo, to = call(
        pre_kernel,
        [(proj, 1), (before, 1), (full_conv, None), (logits, 0)],
        [
            (shape_of((seqs, heads, block, block), f32), 0),
            (shape_of((seqs, heads, block, 2 * DK), f32), 0),
            (shape_of((seqs, heads, block, 2 * DK), f32), 0),
            (shape_of((seqs, heads, DK, 2 * DK), bf16), 0),
        ],
        seqs,
    )
    near = [shifted(to, "dp", c) for c in range(1, dp)]
    [gates] = call(
        partial(gate_kernel, pair_layout),
        [(hidden_one, 0)] + [(a, None) for a in gate_pieces],
        [(shape_of(per_token + (inner,), f32), 0)],
        seqs,
    )
    rows_about, cotangent = call(
        partial(prepare_kernel, layout),
        [(rows, 0), (out_grad, 0), (factor, 0)],
        [(shape_of(per_token + (width,), bf16), 0)] * 2,
        seqs,
        scalar=turn_one,
    )
    turned = jnp.swapaxes(w_gateup, 1, 2)
    feed_own = [turned, w_down]
    mixer_part, normed, rule, state = call(
        partial(mix_kernel, pair_layout, len(near)),
        [(a, 0) for a in near]
        + [(qo, 0), (gates, 0), (gain_head, None)]
        + [(a, None) for a in out_pieces]
        + [(cotangent, "any")],
        [
            (shape_of(per_token + (width,), bf16), 0),
            (shape_of(per_token + (inner,), bf16), 0),
            (shape_of(per_token + (inner,), f32), 0),
            (shape_of(square, f32), 0),
        ],
        seqs,
    )
    total = lax.psum(mixer_part, "mp")
    nexts = [shifted(to[..., :DK], "dp", -c) for c in range(1, dp - 1)]
    if near_four:
        gateup, down = (gathered_pieces(a, a.ndim - 1) for a in after(feed_own, mixer_part))
    else:
        gateup, down = (
            [lax.all_gather(a, "dp", axis=a.ndim - 1, tiled=True)] for a in feed_own
        )
    units = w_down.shape[0]
    two_part, hidden_two, hidden_mlp, grad_pair = call(
        partial(feed_kernel, layout),
        [(rows_about, 0), (total, 0), (cotangent, 0), (gain_two, None)]
        + [(a, None) for a in gateup + down],
        [
            (shape_of(per_token + (width,), bf16), 0),
            (shape_of(per_token + (width,), bf16), 0),
            (shape_of(per_token + (units,), bf16), 0),
            (shape_of((2,) + per_token + (units,), bf16), 1),
        ],
        seqs,
    )
    grad_two = lax.psum(two_part, "mp")

    def feed_gradients(some):
        outs = [(shape_of((m, units, n), bf16), None) for _, n in some for m in (2, 1)]
        ins = [flat(hidden_two), flat(cotangent), flat(grad_pair), flat(hidden_mlp)]
        made = call(partial(feed_gradient_kernel, some), [(a, None) for a in ins], outs, 1)
        return made[::2], made[1::2]

    if near_four:
        feed_in = [far_hop(*far) for far in feed_gradients(ranges[3:])]
        gateup_near, down_near = (
            near_sums(n, got) for n, got in zip(feed_gradients(ranges[:3]), feed_in)
        )
        gateup_sums, down_sums = near_hop(gateup_near), near_hop(down_near)
        held = [(a, "any") for a in gateup_sums[1:] + down_near[1:]]
    else:
        [grad_gateup], [grad_down] = feed_gradients(ranges)
        held = []
    [down_part] = call(
        partial(down_kernel, layout),
        [(hidden_mlp, 0)] + [(a, None) for a in down],
        [(shape_of(per_token + (width,), bf16), 0)],
        seqs,
        scalar=turn_one,
    )
    mlp_share = lax.psum_scatter(down_part, "mp", scatter_dimension=2, tiled=True).astype(f32)
    grad_mix, middle_own, mlpgain, drule, dgate, dgain, direct = call(
        partial(middle_back_kernel, pair_layout),
        [
            (grad_two, 0),
            (cotangent, 0),
            (rows_about, 0),
            (total, 0),
            (gain_two, None),
            (rule, 0),
            (gates, 0),
            (gain_head, None),
            (qo, 0),
        ]
        + [(a, None) for a in out_pieces]
        + [(down_part, "any")]
        + held,
        [
            (shape_of(per_token + (width,), bf16), 0),
            (shape_of(per_token + (local_width,), f32), 0),
            (shape_of((seqs, 1, width), f32), 0),
            (shape_of(per_token + (inner,), f32), 0),
            (shape_of(per_token + (inner,), bf16), 0),
            (shape_of((seqs, 1, DK), f32), 0),
            (shape_of(square, bf16), 0),
        ],
        seqs,
        scalar=column_about.reshape(1),
        scratch=[pltpu.VMEM((block, width), f32)],
    )
    directs = [shifted(direct, "dp", -c) for c in range(1, dp)]
    if near_four:
        pair_grads = call(
            partial(pair_gradient_kernel, [(k * size, size) for k in range(4)]),
            [(flat(a), None) for a in (hidden_one, dgate, normed, grad_mix)],
            [(shape_of((2, size, inner), bf16), None)] * 4,
            1,
        )
        held = [(pair_grads[3], "any")]
    else:
        grad_outgate = jnp.einsum(
            "td,tc->dc", flat(hidden_one), flat(dgate), preferred_element_type=f32
        )
        grad_outproj = jnp.einsum(
            "tc,td->cd", flat(normed), flat(grad_mix), preferred_element_type=f32
        )
        held = []
    dproj, last, first, dtaps, dlogits = call(
        back_kernel,
        [
            (proj, 1),
            (before, 1),
            (full_conv, None),
            (logits, 0),
            (inverse, 0),
            (wu, 0),
            (state, 0),
            (drule, 0),
        ]
        + [(a, 0) for a in directs + nexts],
        [
            (shape_of((3,) + per_token + (inner,), bf16), 1),
            (shape_of((3, seqs, PAD, inner), f32), 1),
            (shape_of((3, seqs, PAD, inner), f32), 1),
            (shape_of((seqs, 3 * KW, inner), f32), 0),
            (shape_of(per_token + (heads,), bf16), 0),
        ],
        seqs,
    )
    later = shifted(first, "dp", -1)
    dproj = lax.dynamic_update_slice(dproj, (last + later).astype(bf16), (0, 0, block - PAD, 0))
    one_low, row_part, gain_part = call(
        partial(first_back_kernel, layout, pair_layout),
        [
            (flat(dproj), None),
            (flat(dgate), None),
            (flat(dlogits), None),
            (flat(proj), None),
            (flat(gates), None),
            (flat(logits), None),
            (about_beta.T.astype(f32), None),
            (flat(rows_about), None),
            (flat(scale_one), None),
        ]
        + [(a, None) for a in qkv + gate_pieces]
        + held,
        [
            (shape_of((count_rows, width), bf16), None),
            (shape_of((count_rows, 1), f32), None),
            (shape_of((1, width), f32), None),
        ],
        1,
        scalar=turn_one,
    )
    one_share = lax.psum_scatter(
        one_low.reshape(seqs, block, width), "mp", scatter_dimension=2, tiled=True
    ).astype(f32)
    made = call(
        partial(qkv_gradient_kernel, ranges),
        [(flat(hidden_one), None), (flat(dproj), None), (flat(dlogits), None), (row_part, "any")],
        [(shape_of((3, n, inner), bf16), None) for _, n in ranges]
        + [(shape_of((heads, width), f32), None)],
        1,
    )

    smalls = [
        jnp.sum(dtaps, 0).reshape(3, KW, heads, DK),
        blocks_about(made[-1], 1).T,
        jnp.sum(dgain, (0, 1)),
        blocks_about(gain_part[0], 0),
        blocks_about(jnp.sum(mlpgain, (0, 1)), 0),
    ]
    small_sum = lax.psum(padded(pack(smalls)).astype(bf16), "dp")
    sum_conv, sum_beta, sum_head, sum_mix, sum_mlp = (
        lax.dynamic_slice_in_dim(a, place * (a.shape[axis] // dp), a.shape[axis] // dp, axis)
        for a, axis in zip(unpack(small_sum.astype(f32), [a.shape for a in smalls]), (3, 0, 0, 0, 0))
    )
    rest = pack([row_part[:, 0], sum_head, sum_mix])
    if near_four:
        own_qkv, *near_qkv = near_sums(made[:3], far_hop(made[3], made[4]))
        near_qkv = after(near_qkv, small_sum)
        rest = after(rest, near_qkv)
        late = near_qkv[0]
        pair_sums = near_hop(near_sums(pair_grads[:3], far_hop(*jnp.split(pair_grads[3], 2, 1))))
        sum_qkv = sum_last(near_hop((own_qkv, *near_qkv)))
        sum_gateup = jnp.swapaxes(sum_last(gateup_sums, late), 1, 2)
        sum_down = sum_last(down_sums, late)[0]
        sum_pair = sum_last(pair_sums)
        sum_outgate = sum_pair[0]
        sum_out = jnp.concatenate(jnp.split(sum_pair[1], 2, 0), 1)
    else:

        def scattered(array, axis):
            return lax.psum_scatter(array, "dp", scatter_dimension=axis, tiled=True).astype(f32)

        sum_qkv = scattered(made[0], 1)
        sum_outgate = scattered(grad_outgate.astype(bf16), 0)
        sum_out = scattered(grad_outproj.astype(bf16), 1)
        sum_gateup = jnp.swapaxes(scattered(grad_gateup, 2), 1, 2)
        sum_down = scattered(grad_down[0], 1)
    row_sum, sum_head, sum_mix = unpack(
        lax.psum(rest, "mp"), [(count_rows,), sum_head.shape, sum_mix.shape]
    )

    own_tokens = tokens.astype(f32)
    mixed_out = (own_tokens + own(total).astype(f32) + mlp_share).astype(bf16)
    row_mean = (row_sum / width).reshape(seqs, block, 1)
    gain_own = lax.dynamic_slice_in_dim(gain_one, column, local_width, 1)
    tokens_grad = middle_own + scale_one * (
        one_share * gain_own - own_tokens * scale_one * row_mean
    )
    return (
        mixed_out,
        tokens_grad.astype(bf16),
        sum_qkv,
        sum_conv,
        sum_beta,
        sum_outgate,
        sum_head,
        sum_out,
        sum_mix,
        sum_mlp,
        sum_gateup,
        sum_down,
    )


def solution(mesh):
    return jax.shard_map(
        body,
        mesh=mesh,
        in_specs=(
            P(None, "dp", "mp"),
            P(None, "dp", None),
            P(None, "dp"),
            P(),
            P(None, "dp", "mp"),
            P(None, None, "mp", "dp"),
            P("dp", "mp"),
            P("dp", "mp"),
            P("dp"),
            P("mp", "dp"),
            P("dp"),
            P("dp"),
            P(None, "dp", "mp"),
            P("mp", "dp"),
        ),
        out_specs=(
            P(None, "dp", "mp"),
            P(None, "dp", "mp"),
            P(None, "dp", "mp"),
            P(None, None, "mp", "dp"),
            P("dp", "mp"),
            P("dp", "mp"),
            P("dp"),
            P("mp", "dp"),
            P("dp"),
            P("dp"),
            P(None, "dp", "mp"),
            P("mp", "dp"),
        ),
        check_vma=False,
    )
```

```python
from functools import partial

import jax
import jax.numpy as jnp
from jax import lax
from jax.experimental import pallas as pl
from jax.experimental.pallas import tpu as pltpu
from jax.sharding import PartitionSpec as P

DK = 128
KW = 4
PAD = 8
HALO = 16
VMEM = 58 * 2**20

eps_norm = 1e-06
eps_unit = 1e-06

f32 = jnp.float32
bf16 = jnp.bfloat16


def split(v):
    if v.dtype == bf16:
        return v, None
    high = v.astype(bf16)
    return high, (v - high.astype(f32)).astype(bf16)


def mm(a, b, ca=1, cb=0, passes=3):
    def one(x, y):
        return lax.dot_general(x, y, (((ca,), (cb,)), ((), ())), preferred_element_type=f32)

    if passes == 1:
        return one(a.astype(bf16), b.astype(bf16))
    (ah, al), (bh, bl) = split(a), split(b)
    out = one(ah, bh)
    if bl is not None:
        out = out + one(ah, bl)
    if al is not None:
        out = out + one(al, bh)
    return out


def places(rows, cols):
    return (
        lax.broadcasted_iota(jnp.int32, (rows, cols), 0),
        lax.broadcasted_iota(jnp.int32, (rows, cols), 1),
    )


def unit_lower_inverses(blocks):
    size = blocks[0].shape[0]
    if size > 128:
        half = size // 2
        parts = unit_lower_inverses(
            [a[:half, :half] for a in blocks] + [a[half:, half:] for a in blocks]
        )
        firsts, seconds = parts[: len(blocks)], parts[len(blocks) :]
        inner = [mm(a[half:, :half], x) for a, x in zip(blocks, firsts)]
        lower = [-mm(x, y) for x, y in zip(seconds, inner)]
        zero = jnp.zeros((half, half), f32)
        return [
            jnp.concatenate(
                [jnp.concatenate([x, zero], 1), jnp.concatenate([y, z], 1)], 0
            )
            for x, y, z in zip(firsts, lower, seconds)
        ]
    rows, cols = places(size, size)
    eye = (rows == cols).astype(f32)
    level = 0
    inverses = None
    while (1 << level) < size:
        mask = (
            ((rows >> (level + 1)) == (cols >> (level + 1)))
            & (((rows >> level) & 1) == 1)
            & (((cols >> level) & 1) == 0)
        ).astype(f32)
        lows = [a * mask for a in blocks]
        if level == 0:
            inverses = [eye - low for low in lows]
        else:
            inner = [mm(low, x) for low, x in zip(lows, inverses)]
            inverses = [x - mm(x, y) for x, y in zip(inverses, inner)]
        level += 1
    return inverses


def head_slice(h):
    return slice(h * DK, (h + 1) * DK)


def convolve(proj_ref, before_ref, taps, i, h):
    own = proj_ref[i, 0, :, head_slice(h)].astype(f32)
    length = own.shape[0]
    ext = jnp.concatenate([before_ref[i, 0, :, head_slice(h)].astype(f32), own], 0)
    shifts = [ext[HALO - KW + 1 + j : HALO - KW + 1 + j + length] for j in range(KW)]
    out = None
    for j in range(KW):
        tap = taps[i * KW + j : i * KW + j + 1, head_slice(h)]
        out = tap * shifts[j] if out is None else out + tap * shifts[j]
    sig = jax.nn.sigmoid(out)
    return shifts, out, sig, out * sig


def unit(acts):
    inv = lax.rsqrt(jnp.sum(acts * acts, -1, keepdims=True) + eps_unit)
    return acts * inv, inv


def rule_inputs(proj_ref, before_ref, taps, h):
    parts = [convolve(proj_ref, before_ref, taps, i, h) for i in range(3)]
    q, q_inv = unit(parts[0][3])
    k, k_inv = unit(parts[1][3])
    return parts, (q, q_inv), (k, k_inv), parts[2][3]


def norm_factor(values):
    return lax.rsqrt(jnp.mean(values * values, -1, keepdims=True) + eps_norm)


def project_kernel(layout, *refs):
    place_ref, rows_ref, gain_ref, beta_ref = refs[:4]
    pieces = refs[4 : 4 + len(layout)]
    hidden_ref, proj_ref, tail_ref, logit_ref, scale_ref, keep_ref = refs[4 + len(layout) :]
    rows = rows_ref[0].astype(f32)
    scale = norm_factor(rows)
    scale_ref[0] = scale
    keep_ref[...] = (rows * scale * gain_ref[...]).astype(bf16)
    logits = mm(keep_ref[...], beta_ref[...])
    logit_ref[0] = logits[:, : logit_ref.shape[2]]
    sums = [None] * 3
    for (k, start, size, block), piece in zip(layout, pieces):
        at = pl.multiple_of((place_ref[0] ^ k) * block + start, 128)
        part = keep_ref[:, pl.ds(at, size)]
        hidden_ref[0, :, k * block + start : k * block + start + size] = part
        for i in range(3):
            term = mm(part, piece[i])
            sums[i] = term if sums[i] is None else sums[i] + term
    for i in range(3):
        low = sums[i].astype(bf16)
        proj_ref[i, 0] = low
        tail_ref[i, 0] = low[low.shape[0] - HALO :]


def pre_kernel(proj_ref, before_ref, taps_ref, logit_ref, x_ref, wu_ref, qo_ref, to_ref):
    heads = to_ref.shape[1]
    taps = taps_ref[...]
    length = proj_ref.shape[2]
    betas = jax.nn.sigmoid(logit_ref[0])
    r, c = places(length, length)
    strict = (r > c).astype(f32)
    full = (r >= c).astype(f32)
    saved, blocks = [], []
    for h in range(heads):
        _, (q, _), (k, _), v = rule_inputs(proj_ref, before_ref, taps, h)
        q, k, v = q.astype(bf16), k.astype(bf16), v.astype(bf16)
        beta = betas[:, h : h + 1]
        gram = mm(k, k, 1, 1)
        blocks.append(beta * gram * strict)
        saved.append((q, k, v, beta))
    inverses = unit_lower_inverses(blocks)
    r, c = places(DK, DK)
    eye = (r == c).astype(f32)
    for h in range(heads):
        q, k, v, beta = saved[h]
        x = inverses[h]
        x_ref[0, h] = x
        kv = jnp.concatenate([k.astype(f32), v.astype(f32)], 1) * beta
        wu = mm(x, kv)
        wu_ref[0, h] = wu
        scores = mm(q, k, 1, 1) * full
        pwu = mm(scores, wu)
        qo_ref[0, h, :, :DK] = q.astype(f32) - pwu[:, :DK]
        qo_ref[0, h, :, DK:] = pwu[:, DK:]
        kwu = mm(k, wu, 0, 0)
        to_ref[0, h, :, :DK] = (eye - kwu[:, :DK]).astype(bf16)
        to_ref[0, h, :, DK:] = kwu[:, DK:].astype(bf16)


def by_piece(place_ref, refs):
    if len(refs) > 1 or len(refs[0].shape) < 4:
        return refs
    return [refs[0].at[place_ref[0] ^ k] for k in range(4)]


def gate_kernel(layout, place_ref, hidden_ref, *refs):
    gate_ref = refs[-1]
    refs = by_piece(place_ref, refs[:-1])
    total = None
    for (k, start, size, block), ref in zip(layout, refs):
        at = k * block + start
        term = mm(hidden_ref[0, :, at : at + size], gate_part(ref)[...])
        total = term if total is None else total + term
    gate_ref[0] = total


def gate_part(ref):
    return ref.at[0] if len(ref.shape) == 3 else ref


def out_columns(layout, refs):
    for (k, start, size, block), ref in zip(layout, refs):
        at, half = k * block + start, size // 2
        if len(ref.shape) == 2:
            yield at, size, ref
            continue
        inner = ref.shape[1] // 2
        yield at, half, ref.at[1, :inner]
        yield at + half, half, ref.at[1, inner:]


def mix_kernel(layout, count, place_ref, *refs):
    near, rest = refs[:count], refs[count:]
    qo_ref, gate_ref, gain_ref = rest[:3]
    outs = by_piece(place_ref, rest[3:-5])
    part_ref, normed_ref, rule_ref, state_ref = rest[-4:]
    heads = state_ref.shape[1]
    for h in range(heads):
        state = near[-1][0, h, :, DK:].astype(f32)
        for ref in reversed(near[:-1]):
            state = mm(ref[0, h, :, :DK], state) + ref[0, h, :, DK:].astype(f32)
        state_ref[0, h] = state
        qo = qo_ref[0, h]
        out = (mm(qo[:, :DK], state) + qo[:, DK:]) * DK ** (-0.5)
        rule_ref[0, :, head_slice(h)] = out
        gate = gate_ref[0, :, head_slice(h)]
        normed = out * norm_factor(out) * gain_ref[...] * (gate * jax.nn.sigmoid(gate))
        normed_ref[0, :, head_slice(h)] = normed.astype(bf16)
    for at, size, ref in out_columns(layout, outs):
        part_ref[0, :, at : at + size] = mm(normed_ref[0], ref[...]).astype(bf16)


def prepare_kernel(layout, place_ref, rows_ref, grad_ref, factor_ref, about_ref, cot_ref):
    for k, start, size, block in layout:
        at = pl.multiple_of((place_ref[0] ^ k) * block + start, 128)
        to = slice(k * block + start, k * block + start + size)
        about_ref[0, :, to] = rows_ref[0, :, pl.ds(at, size)]
        grad = grad_ref[0, :, pl.ds(at, size)].astype(f32) * factor_ref[0]
        cot_ref[0, :, to] = grad.astype(bf16)


def down_kernel(layout, place_ref, mlp_ref, *refs):
    part_ref = refs[-1]
    for (k, start, size, block), ref in zip(layout, refs[:-1]):
        at = pl.multiple_of((place_ref[0] ^ k) * block + start, 128)
        part_ref[0, :, pl.ds(at, size)] = mm(mlp_ref[0], ref[...]).astype(bf16)


def feed_gradient_kernel(ranges, hidden_ref, cot_ref, pair_ref, mlp_ref, *outs):
    for n, (start, size) in enumerate(ranges):
        hidden = hidden_ref[:, start : start + size]
        outs[2 * n][0] = mm(pair_ref[0], hidden, 0, 0).astype(bf16)
        outs[2 * n][1] = mm(pair_ref[1], hidden, 0, 0).astype(bf16)
        outs[2 * n + 1][0] = mm(mlp_ref[...], cot_ref[:, start : start + size], 0, 0).astype(bf16)


def qkv_gradient_kernel(ranges, hidden_ref, dproj_ref, dlogit_ref, *outs):
    outs = outs[-len(ranges) - 1 :]
    for (start, size), out in zip(ranges, outs[:-1]):
        hidden = hidden_ref[:, start : start + size]
        for i in range(3):
            out[i] = mm(hidden, dproj_ref[i], 0, 0).astype(bf16)
    outs[-1][...] = mm(dlogit_ref[...], hidden_ref[...], 0, 0)


def pair_gradient_kernel(ranges, hidden_ref, dgate_ref, normed_ref, mix_ref, *outs):
    inner = normed_ref.shape[1]
    for (start, size), out in zip(ranges, outs):
        out[0] = mm(hidden_ref[:, start : start + size], dgate_ref[...], 0, 0).astype(bf16)
        for n in range(2):
            at = start + n * size // 2
            mix = mix_ref[:, at : at + size // 2]
            out[1, n * inner : (n + 1) * inner] = mm(normed_ref[...], mix, 0, 0).astype(bf16)


def add_halves_kernel(*refs):
    one_ref, two_ref, low_ref, high_ref, one_out, two_out = refs[:4] + refs[-2:]

    def add(a, b):
        return (a.astype(f32) + b.astype(f32)).astype(bf16)

    half = low_ref.shape
    rows = slice(0, half[1])
    if half[1] < one_ref.shape[1]:
        late, lanes, late_lanes = slice(half[1], 2 * half[1]), slice(None), slice(None)
    else:
        late, lanes, late_lanes = rows, slice(0, half[2]), slice(half[2], 2 * half[2])
    one_out[...] = one_ref[...]
    two_out[...] = two_ref[...]
    one_out[0, late, late_lanes] = add(one_ref[0, late, late_lanes], high_ref[0])
    two_out[0, rows, lanes] = add(two_ref[0, rows, lanes], low_ref[0])


def add_last_kernel(*refs):
    own_ref, one_ref, two_ref, out_ref = refs[:3] + refs[-1:]
    out_ref[...] = own_ref[...].astype(f32) + one_ref[...].astype(f32) + two_ref[...].astype(f32)


def feed_kernel(layout, *refs):
    rows_ref, total_ref, cot_ref, gain_ref = refs[:4]
    count = len(layout)
    gateups, downs = (refs[4 + n * count : 4 + (n + 1) * count] for n in range(2))
    two_ref, hidden_ref, mlp_ref, pair_ref = refs[-4:]
    middle = rows_ref[0].astype(f32) + total_ref[0].astype(f32)
    hidden_ref[0] = (middle * norm_factor(middle) * gain_ref[...]).astype(bf16)
    gate, up, grad = None, None, None
    for (k, start, size, block), w_gateup, w_down in zip(layout, gateups, downs):
        lanes = slice(k * block + start, k * block + start + size)
        hidden = hidden_ref[0, :, lanes]
        terms = (
            mm(hidden, w_gateup[0], 1, 1),
            mm(hidden, w_gateup[1], 1, 1),
            mm(cot_ref[0, :, lanes], w_down[...], 1, 1),
        )
        if gate is None:
            gate, up, grad = terms
        else:
            gate, up, grad = gate + terms[0], up + terms[1], grad + terms[2]
    sig = jax.nn.sigmoid(gate)
    silu = gate * sig
    mlp_ref[0] = (silu * up).astype(bf16)
    first = (grad * up * sig * (1.0 + gate * (1.0 - sig))).astype(bf16)
    second = (grad * silu).astype(bf16)
    pair_ref[0, 0] = first
    pair_ref[1, 0] = second
    for (k, start, size, block), w_gateup in zip(layout, gateups):
        lanes = slice(k * block + start, k * block + start + size)
        two = mm(first, w_gateup[0]) + mm(second, w_gateup[1])
        two_ref[0, :, lanes] = two.astype(bf16)


def middle_back_kernel(layout, pieces, at_ref, *refs):
    two_ref, cot_ref, rows_ref, total_ref, gain_ref, rule_ref, gate_ref, head_gain_ref, qo_ref = refs[:9]
    outs = by_piece(at_ref, refs[9 : 9 + pieces])
    mix_ref, own_ref, mlpgain_ref, drule_ref, dgate_ref, dgain_ref, direct_ref, keep_ref = refs[-8:]
    middle = rows_ref[0].astype(f32) + total_ref[0].astype(f32)
    factor = norm_factor(middle)
    normal = middle * factor
    two = two_ref[0].astype(f32)
    mlpgain_ref[0] = jnp.sum(two * normal, 0, keepdims=True)
    scaled = two * gain_ref[...]
    mean = jnp.mean(scaled * normal, -1, keepdims=True)
    keep_ref[...] = cot_ref[0].astype(f32) + factor * (scaled - normal * mean)
    width = own_ref.shape[2]
    own_ref[0] = keep_ref[:, pl.ds(pl.multiple_of(at_ref[1], 128), width)]
    mix = keep_ref[...].astype(bf16)
    mix_ref[0] = mix
    grads = None
    for at, size, ref in out_columns(layout, outs):
        term = mm(mix_ref[0, :, at : at + size], ref[...], 1, 1)
        grads = term if grads is None else grads + term
    total = jnp.zeros((1, DK), f32)
    for h in range(direct_ref.shape[1]):
        grad = grads[:, head_slice(h)]
        out = rule_ref[0, :, head_slice(h)]
        gate = gate_ref[0, :, head_slice(h)]
        inv = norm_factor(out)
        n = out * inv
        sig = jax.nn.sigmoid(gate)
        silu = gate * sig
        gg = grad * head_gain_ref[...]
        dn = gg * silu
        drule = inv * (dn - n * jnp.mean(dn * n, -1, keepdims=True))
        drule_ref[0, :, head_slice(h)] = drule
        dgate = gg * n * sig * (1.0 + gate * (1.0 - sig))
        dgate_ref[0, :, head_slice(h)] = dgate.astype(bf16)
        total = total + jnp.sum(grad * n * silu, 0, keepdims=True)
        direct = mm(qo_ref[0, h, :, :DK], drule, 0, 0) * DK ** (-0.5)
        direct_ref[0, h] = direct.astype(bf16)
    dgain_ref[0] = total


def first_back_kernel(layout, pair_layout, count, place_ref, *refs):
    dproj_ref, dgate_ref, dlogit_ref, proj_ref, gate_ref, logit_ref, beta_ref, rows_ref, scale_ref = refs[:9]
    pieces = refs[9 : 9 + len(layout)]
    pairs = by_piece(place_ref, refs[9 + len(layout) : 9 + len(layout) + count])
    one_ref, rowsum_ref, gainsum_ref = refs[-3:]
    gates = {}
    for (k, start, size, block), ref in zip(pair_layout, pairs):
        gates[k] = ref
    for (k, start, size, block), piece in zip(layout, pieces):
        lanes = slice(k * block + start, k * block + start + size)
        grad = mm(dgate_ref[...], gate_part(gates[k])[start : start + size], 1, 1)
        for i in range(3):
            grad = grad + mm(dproj_ref[i], piece[i], 1, 1)
        for h in range(beta_ref.shape[0]):
            grad = grad + dlogit_ref[:, h : h + 1].astype(f32) * beta_ref[h : h + 1, lanes]
        at = pl.multiple_of((place_ref[0] ^ k) * block + start, 128)
        one_ref[:, pl.ds(at, size)] = grad.astype(bf16)
        gainsum_ref[:, lanes] = jnp.sum(
            grad * (rows_ref[:, lanes].astype(f32) * scale_ref[...]), 0, keepdims=True
        )
    total = dgate_ref[...].astype(f32) * gate_ref[...]
    for i in range(3):
        total = total + dproj_ref[i].astype(f32) * proj_ref[i].astype(f32)
    total = jnp.sum(total, -1, keepdims=True)
    logits = dlogit_ref[...].astype(f32) * logit_ref[...]
    rowsum_ref[...] = total + jnp.sum(logits, -1, keepdims=True)


def back_kernel(count, *refs):
    (
        proj_ref,
        before_ref,
        taps_ref,
        logit_ref,
        x_ref,
        wu_ref,
        state_ref,
        drule_ref,
    ) = refs[:8]
    dproj_ref, last_ref, first_ref, dtaps_ref, dlogit_ref = refs[-5:]
    others = refs[8 : 8 + 2 * count - 1]
    directs, nexts = others[:count], others[count:]
    heads = state_ref.shape[1]
    taps = taps_ref[...]
    length = proj_ref.shape[2]
    betas = jax.nn.sigmoid(logit_ref[0])
    r, c = places(length, length)
    strict = (r > c).astype(f32)
    full = (r >= c).astype(f32)
    zeros = jnp.zeros((PAD, DK), f32)
    for h in range(heads):
        parts, (qu, q_inv), (ku, k_inv), vu = rule_inputs(proj_ref, before_ref, taps, h)
        q, k, v = qu.astype(bf16), ku.astype(bf16), vu.astype(bf16)
        beta = betas[:, h : h + 1]
        leave = jnp.zeros((DK, DK), f32)
        for j in reversed(range(count)):
            here = directs[j][0, h].astype(f32)
            leave = here if j == count - 1 else mm(nexts[j][0, h], leave, 0, 0) + here
        state = state_ref[0, h]
        wu = wu_ref[0, h]
        u = wu[:, DK:] - mm(wu[:, :DK], state)
        resid = v.astype(f32) - mm(k, state)
        dout = drule_ref[0, :, head_slice(h)] * DK ** (-0.5)
        gram = mm(k, k, 1, 1)
        scores = mm(q, k, 1, 1) * full
        du = mm(scores, dout, 0, 0) + mm(k, leave)
        y = mm(x_ref[0, h], du, 0, 0)
        by = beta * y
        da = -(mm(y, u, 1, 1) * strict)
        dbeta = jnp.sum(y * resid, -1, keepdims=True) + jnp.sum(da * gram, -1, keepdims=True)
        dgram = beta * da
        dscores = mm(dout, u, 1, 1) * full
        dq = mm(dout, state, 1, 1) + mm(dscores, k)
        dk = (
            mm(dgram, k)
            + mm(dgram, k, 0, 0)
            + mm(dscores, q, 0, 0)
            + mm(u, leave, 1, 1)
            - mm(by, state, 1, 1)
        )
        dlogit_ref[0, :, h : h + 1] = (dbeta * beta * (1.0 - beta)).astype(bf16)
        dq = (dq - qu * jnp.sum(qu * dq, -1, keepdims=True)) * q_inv
        dk = (dk - ku * jnp.sum(ku * dk, -1, keepdims=True)) * k_inv
        for i, dact in enumerate((dq, dk, by)):
            shifts, out, sig, _ = parts[i]
            dconv = dact * sig * (1.0 + out * (1.0 - sig))
            ext = jnp.concatenate([zeros, dconv, zeros], 0)
            total = None
            for j in range(KW):
                at = i * KW + j
                dtaps_ref[0, at : at + 1, head_slice(h)] = jnp.sum(
                    dconv * shifts[j], 0, keepdims=True
                )
                tap = taps[at : at + 1, head_slice(h)]
                term = tap * ext[KW - 1 - j : KW - 1 - j + PAD + length]
                total = term if total is None else total + term
            first_ref[i, 0, :, head_slice(h)] = total[:PAD]
            last_ref[i, 0, :, head_slice(h)] = total[length:]
            dproj_ref[i, 0, :, head_slice(h)] = total[PAD:].astype(bf16)


def call(kernel, ins, outs, steps, scalar=None, scratch=(), limit=VMEM, alias=None):
    def spec(shape, axis):
        if axis == "any":
            return pl.BlockSpec(memory_space=pl.ANY)
        block = tuple(1 if n == axis else size for n, size in enumerate(shape))
        where = lambda s, *_: tuple(s if n == axis else 0 for n in range(len(shape)))
        if axis is None:
            return pl.BlockSpec(block, where, pipeline_mode=pl.Buffered(1))
        return pl.BlockSpec(block, where)

    given = [] if scalar is None else [scalar]
    return pl.pallas_call(
        kernel,
        grid_spec=pltpu.PrefetchScalarGridSpec(
            num_scalar_prefetch=len(given),
            grid=(steps,),
            in_specs=[spec(a.shape, axis) for a, axis in ins],
            out_specs=[spec(o.shape, axis) for o, axis in outs],
            scratch_shapes=scratch,
        ),
        out_shape=[o for o, _ in outs],
        input_output_aliases=alias or {},
        compiler_params=pltpu.CompilerParams(vmem_limit_bytes=limit),
    )(*given, *[a for a, _ in ins])


def shape_of(shape, dtype):
    return jax.ShapeDtypeStruct(shape, dtype)


def shifted(array, axis, by):
    devices = lax.axis_size(axis)
    pairs = [(i, i + by) for i in range(devices) if 0 <= i + by < devices]
    return lax.ppermute(array, axis, pairs)


def after(values, *others):
    flat, tree = jax.tree.flatten(values)
    others = jax.tree.leaves(others)
    here = pl.BlockSpec(memory_space=pl.ANY)
    out = pl.pallas_call(
        lambda *refs: None,
        in_specs=[here] * (len(flat) + len(others)),
        out_specs=[here] * len(flat),
        out_shape=[shape_of(a.shape, a.dtype) for a in flat],
        input_output_aliases={n: n for n in range(len(flat))},
    )(*flat, *others)
    return jax.tree.unflatten(tree, out)


def copied_after(values, *others):
    others = jax.tree.leaves(others)
    count = len(values)
    here = pl.BlockSpec(memory_space=pl.ANY)

    def kernel(*refs):
        outs, sems = refs[-count - 1 : -1], refs[-1]
        copies = [
            pltpu.make_async_copy(refs[n], outs[n], sems.at[n]) for n in range(count)
        ]
        for copy in copies:
            copy.start()
        for copy in copies:
            copy.wait()

    return pl.pallas_call(
        kernel,
        in_specs=[here] * (count + len(others)),
        out_specs=[here] * count,
        out_shape=[shape_of(a.shape, a.dtype) for a in values],
        scratch_shapes=[pltpu.SemaphoreType.DMA((count,))],
    )(*values, *others)


def swap(array, bits):
    return lax.ppermute(array, "dp", [(i, i ^ bits) for i in range(4)])


def first_hop(own):
    return swap(own, 1), swap(own, 2)


def halves_of(hop, axis):
    low, high = (jnp.split(part, 2, axis) for part in hop)
    return low[0], high[1]


def gathered_pieces(own, axis, hop=None, halves=None):
    hop = hop or first_hop(own)
    low, high = halves or halves_of(hop, axis)
    return [own, *hop, swap(low, 2), swap(high, 1)]


def far_hop(low, high):
    return swap(low, 1), swap(high, 2)


def near_sums(pieces, far_in, *others):
    own, one, two = pieces
    specs = [(one, 0), (two, 0), (far_in[0], 0), (far_in[1], 0)]
    specs += [(a, "any") for a in others]
    outs = [(shape_of(a.shape, a.dtype), 0) for a in (one, two)]
    return own, *call(add_halves_kernel, specs, outs, one.shape[0])


def near_hop(pieces):
    own, one, two = pieces
    return own, swap(one, 1), swap(two, 2)


def sum_last(parts, *others):
    own = parts[0]
    ins = [(a, 0) for a in parts] + [(a, "any") for a in others]
    [total] = call(add_last_kernel, ins, [(shape_of(own.shape, f32), 0)], own.shape[0])
    return total


def pack(parts):
    return jnp.concatenate([p.reshape(-1) for p in parts])


def unpack(flat, shapes):
    out, at = [], 0
    for shape in shapes:
        size = 1
        for n in shape:
            size *= n
        out.append(flat[..., at : at + size].reshape(flat.shape[:-1] + tuple(shape)))
        at += size
    return out


def padded(flat, multiple=1024):
    return jnp.pad(flat, (0, -flat.shape[0] % multiple))


def body(
    tokens,
    out_grad,
    domain,
    group_weight,
    w_qkv,
    conv_weight,
    w_beta,
    w_outgate,
    head_gain,
    w_out,
    mixer_gain,
    mlp_gain,
    w_gateup,
    w_down,
):
    dp = lax.axis_size("dp")
    place = lax.axis_index("dp")
    seqs, block, local_width = tokens.shape
    count_rows = seqs * block
    heads = conv_weight.shape[2]
    inner = heads * DK
    column = lax.axis_index("mp") * local_width
    near_four = dp == 4

    def blocks_about(array, axis):
        if not near_four:
            return array
        size = array.shape[axis] // 4
        return jnp.concatenate(
            [lax.dynamic_slice_in_dim(array, (place ^ k) * size, size, axis) for k in range(4)],
            axis,
        )

    width = out_grad.shape[2]
    turn = place if near_four else jnp.int32(0)
    column_about = ((column // (width // 4)) ^ turn) * (width // 4) + column % (width // 4)

    def own(array):
        array = array.reshape(seqs, block, width)
        return lax.dynamic_slice_in_dim(array, column_about, local_width, 2)

    onehot = (domain[..., None] == jnp.arange(3, dtype=jnp.int32)).astype(f32)
    own_counts = jnp.sum(onehot, axis=(0, 1))
    high = jnp.floor(own_counts / 128.0)
    digits = jnp.concatenate([high, own_counts - 128.0 * high]).astype(bf16)
    small = [w_beta, conv_weight, head_gain, mixer_gain, mlp_gain, digits]
    packed = padded(pack(small))
    size = width // 4
    if near_four:
        qkv_hop = first_hop(w_qkv)
        qkv_halves = halves_of(qkv_hop, 1)
        qkv = gathered_pieces(w_qkv, 1, qkv_hop, qkv_halves)
        packed = after(packed, qkv_halves)
        gathered = jnp.stack([packed] + [swap(packed, bits) for bits in (1, 2, 3)])
        half = w_out.shape[1] // 2
        pair_own = jnp.stack(
            [w_outgate, jnp.concatenate([w_out[:, :half], w_out[:, half:]], 0)]
        )
        pair_layout = [(k, 0, size, size) for k in range(4)]
        layout = pair_layout[:3] + [(3, 0, size // 2, size), (3, size // 2, size // 2, size)]
    else:
        gathered = lax.all_gather(packed, "dp")
        qkv = [lax.all_gather(w_qkv, "dp", axis=1, tiled=True)]
        gate_pieces = [lax.all_gather(w_outgate, "dp", axis=0, tiled=True)]
        out_pieces = [lax.all_gather(w_out, "dp", axis=1, tiled=True)]
        layout = pair_layout = [(0, 0, width, width)]
    ranges = [(k * step + start, n) for k, start, n, step in layout]
    g_beta, g_conv, g_head, g_mix, g_mlp, g_digits = unpack(gathered, [a.shape for a in small])
    about_beta = g_beta.reshape(-1, heads)
    full_beta = blocks_about(about_beta, 0)
    full_conv = jnp.moveaxis(blocks_about(g_conv, 0), 0, 3).reshape(3 * KW, inner).astype(f32)
    gain_head = blocks_about(g_head, 0).reshape(1, DK).astype(f32)
    gain_one = blocks_about(g_mix.reshape(1, -1).astype(f32), 1)
    gain_two = g_mlp.reshape(1, -1).astype(f32)
    sums = jnp.sum(g_digits.astype(f32), 0)
    counts = 128.0 * sums[:3] + sums[3:]
    table = group_weight * (domain.shape[0] * domain.shape[1] * dp) / counts
    factor = jnp.sum(onehot * table, -1)[..., None]

    def flat(array):
        return array.reshape(array.shape[:-3] + (count_rows, array.shape[-1]))

    rows = lax.all_gather(tokens, "mp", axis=2, tiled=True)
    if near_four:
        gate_pieces = out_pieces = [lax.all_gather(after(pair_own, packed), "dp")]
    turn_one = turn.reshape(1)
    per_token = (seqs, block)
    square = (seqs, heads, DK, DK)
    hidden_one, proj, tail, logits, scale_one = call(
        partial(project_kernel, layout),
        [(rows, 0), (gain_one, None), (jnp.pad(full_beta, ((0, 0), (0, 128 - heads))), None)]
        + [(a, None) for a in qkv],
        [
            (shape_of(per_token + (width,), bf16), 0),
            (shape_of((3,) + per_token + (inner,), bf16), 1),
            (shape_of((3, seqs, HALO, inner), bf16), 1),
            (shape_of(per_token + (heads,), f32), 0),
            (shape_of(per_token + (1,), f32), 0),
        ],
        seqs,
        scalar=turn_one,
        scratch=[pltpu.VMEM((block, width), bf16)],
    )
    before = shifted(tail, "dp", 1)
    inverse, wu, qo, to = call(
        pre_kernel,
        [(proj, 1), (before, 1), (full_conv, None), (logits, 0)],
        [
            (shape_of((seqs, heads, block, block), f32), 0),
            (shape_of((seqs, heads, block, 2 * DK), f32), 0),
            (shape_of((seqs, heads, block, 2 * DK), f32), 0),
            (shape_of((seqs, heads, DK, 2 * DK), bf16), 0),
        ],
        seqs,
    )
    near = [shifted(to, "dp", c) for c in range(1, dp)]
    [gates] = call(
        partial(gate_kernel, pair_layout),
        [(hidden_one, 0)] + [(a, None) for a in gate_pieces],
        [(shape_of(per_token + (inner,), f32), 0)],
        seqs,
        scalar=turn_one,
    )
    rows_about, cotangent = call(
        partial(prepare_kernel, layout),
        [(rows, 0), (out_grad, 0), (factor, 0)],
        [(shape_of(per_token + (width,), bf16), 0)] * 2,
        seqs,
        scalar=turn_one,
    )
    turned = jnp.swapaxes(w_gateup, 1, 2)
    feed_own = [turned, w_down]
    mixer_part, normed, rule, state = call(
        partial(mix_kernel, pair_layout, len(near)),
        [(a, 0) for a in near]
        + [(qo, 0), (gates, 0), (gain_head, None)]
        + [(a, None) for a in out_pieces]
        + [(cotangent, "any")],
        [
            (shape_of(per_token + (width,), bf16), 0),
            (shape_of(per_token + (inner,), bf16), 0),
            (shape_of(per_token + (inner,), f32), 0),
            (shape_of(square, f32), 0),
        ],
        seqs,
        scalar=turn_one,
    )
    total = lax.psum(mixer_part, "mp")
    nexts = [shifted(after(to[..., :DK], mixer_part), "dp", -1)]
    for _ in range(dp - 3):
        nexts.append(shifted(nexts[-1], "dp", -1))
    if near_four:
        gateup, down = (gathered_pieces(a, a.ndim - 1) for a in copied_after(feed_own, mixer_part))
    else:
        gateup, down = (
            [lax.all_gather(a, "dp", axis=a.ndim - 1, tiled=True)] for a in feed_own
        )
    units = w_down.shape[0]
    two_part, hidden_two, hidden_mlp, grad_pair = call(
        partial(feed_kernel, layout),
        [(rows_about, 0), (total, 0), (cotangent, 0), (gain_two, None)]
        + [(a, None) for a in gateup + down]
        + [(nexts[0], "any")],
        [
            (shape_of(per_token + (width,), bf16), 0),
            (shape_of(per_token + (width,), bf16), 0),
            (shape_of(per_token + (units,), bf16), 0),
            (shape_of((2,) + per_token + (units,), bf16), 1),
        ],
        seqs,
    )
    grad_two = lax.psum(two_part, "mp")

    def feed_gradients(some):
        outs = [(shape_of((m, units, n), bf16), None) for _, n in some for m in (2, 1)]
        ins = [flat(hidden_two), flat(cotangent), flat(grad_pair), flat(hidden_mlp)]
        made = call(partial(feed_gradient_kernel, some), [(a, None) for a in ins], outs, 1)
        return made[::2], made[1::2]

    if near_four:
        feed_in = [far_hop(*far) for far in feed_gradients(ranges[3:])]
        near_gateup, near_down = feed_gradients(ranges[:3])
        gateup_sums = near_hop(near_sums(near_gateup, feed_in[0], *feed_in[1]))
        down_sums = near_hop(near_sums(near_down, feed_in[1]))
        held = [(a, "any") for a in (*gateup_sums[1:], *nexts)]
    else:
        [grad_gateup], [grad_down] = feed_gradients(ranges)
        held = []
    [down_part] = call(
        partial(down_kernel, layout),
        [(hidden_mlp, 0)] + [(a, None) for a in down],
        [(shape_of(per_token + (width,), bf16), 0)],
        seqs,
        scalar=turn_one,
    )
    mlp_share = lax.psum_scatter(down_part, "mp", scatter_dimension=2, tiled=True).astype(f32)
    grad_mix, middle_own, mlpgain, drule, dgate, dgain, direct = call(
        partial(middle_back_kernel, pair_layout, len(out_pieces)),
        [
            (grad_two, 0),
            (cotangent, 0),
            (rows_about, 0),
            (total, 0),
            (gain_two, None),
            (rule, 0),
            (gates, 0),
            (gain_head, None),
            (qo, 0),
        ]
        + [(a, None) for a in out_pieces]
        + [(down_part, "any")]
        + held,
        [
            (shape_of(per_token + (width,), bf16), 0),
            (shape_of(per_token + (local_width,), f32), 0),
            (shape_of((seqs, 1, width), f32), 0),
            (shape_of(per_token + (inner,), f32), 0),
            (shape_of(per_token + (inner,), bf16), 0),
            (shape_of((seqs, 1, DK), f32), 0),
            (shape_of(square, bf16), 0),
        ],
        seqs,
        scalar=jnp.stack([turn, column_about]),
        scratch=[pltpu.VMEM((block, width), f32)],
    )
    directs = [shifted(direct, "dp", -c) for c in range(1, dp)]
    if near_four:
        pair_grads = call(
            partial(pair_gradient_kernel, [(k * size, size) for k in range(4)]),
            [(flat(a), None) for a in (hidden_one, dgate, normed, grad_mix)],
            [(shape_of((2, size, inner), bf16), None)] * 4,
            1,
        )
        held = [(a, "any") for a in (pair_grads[3], *down_sums[1:])]
    else:
        grad_outgate = jnp.einsum(
            "td,tc->dc", flat(hidden_one), flat(dgate), preferred_element_type=f32
        )
        grad_outproj = jnp.einsum(
            "tc,td->cd", flat(normed), flat(grad_mix), preferred_element_type=f32
        )
        held = []
    dproj, last, first, dtaps, dlogits = call(
        partial(back_kernel, len(directs)),
        [
            (proj, 1),
            (before, 1),
            (full_conv, None),
            (logits, 0),
            (inverse, 0),
            (wu, 0),
            (state, 0),
            (drule, 0),
        ]
        + [(a, 0) for a in directs + nexts]
        + held,
        [
            (shape_of((3,) + per_token + (inner,), bf16), 1),
            (shape_of((3, seqs, PAD, inner), f32), 1),
            (shape_of((3, seqs, PAD, inner), f32), 1),
            (shape_of((seqs, 3 * KW, inner), f32), 0),
            (shape_of(per_token + (heads,), bf16), 0),
        ],
        seqs,
    )
    later = shifted(first, "dp", -1)
    dproj = lax.dynamic_update_slice(dproj, (last + later).astype(bf16), (0, 0, block - PAD, 0))
    one_low, row_part, gain_part = call(
        partial(first_back_kernel, layout, pair_layout, len(gate_pieces)),
        [
            (flat(dproj), None),
            (flat(dgate), None),
            (flat(dlogits), None),
            (flat(proj), None),
            (flat(gates), None),
            (flat(logits), None),
            (about_beta.T.astype(f32), None),
            (flat(rows_about), None),
            (flat(scale_one), None),
        ]
        + [(a, None) for a in qkv + gate_pieces],
        [
            (shape_of((count_rows, width), bf16), None),
            (shape_of((count_rows, 1), f32), None),
            (shape_of((1, width), f32), None),
        ],
        1,
        scalar=turn_one,
    )
    one_share = lax.psum_scatter(
        one_low.reshape(seqs, block, width), "mp", scatter_dimension=2, tiled=True
    ).astype(f32)
    made = call(
        partial(qkv_gradient_kernel, ranges),
        [(flat(hidden_one), None), (flat(dproj), None), (flat(dlogits), None), (row_part, "any")],
        [(shape_of((3, n, inner), bf16), None) for _, n in ranges]
        + [(shape_of((heads, width), f32), None)],
        1,
    )

    shared = [row_part[:, 0], gain_part[0], jnp.sum(dgain, (0, 1))]
    packed_shared = after(pack(shared), made[0])
    row_sum, mixgain, headgain = unpack(
        lax.psum(packed_shared, "mp"), [a.shape for a in shared]
    )
    smalls = [
        jnp.sum(dtaps, 0).reshape(3, KW, heads, DK),
        blocks_about(made[-1], 1).T,
        headgain,
        blocks_about(mixgain, 0),
        blocks_about(jnp.sum(mlpgain, (0, 1)), 0),
    ]
    packed_smalls = padded(pack(smalls)).astype(bf16)
    if near_four:
        own_qkv, *near_qkv = near_sums(made[:3], far_hop(made[3], made[4]))
        packed_smalls = after(packed_smalls, near_qkv)
    small_sum = lax.psum(packed_smalls, "dp").astype(f32)
    sum_conv, sum_beta, sum_head, sum_mix, sum_mlp = (
        lax.dynamic_slice_in_dim(a, place * (a.shape[axis] // dp), a.shape[axis] // dp, axis)
        for a, axis in zip(unpack(small_sum, [a.shape for a in smalls]), (3, 0, 0, 0, 0))
    )
    if near_four:
        late = near_qkv[0]
        pair_sums = near_hop(near_sums(pair_grads[:3], far_hop(*jnp.split(pair_grads[3], 2, 1))))
        sum_qkv = sum_last(near_hop((own_qkv, *near_qkv)))
        sum_gateup = jnp.swapaxes(sum_last(gateup_sums, late), 1, 2)
        sum_down = sum_last(down_sums, late)[0]
        sum_pair = sum_last(pair_sums)
        sum_outgate = sum_pair[0]
        sum_out = jnp.concatenate(jnp.split(sum_pair[1], 2, 0), 1)
    else:

        def scattered(array, axis):
            return lax.psum_scatter(array, "dp", scatter_dimension=axis, tiled=True).astype(f32)

        sum_qkv = scattered(made[0], 1)
        sum_outgate = scattered(grad_outgate.astype(bf16), 0)
        sum_out = scattered(grad_outproj.astype(bf16), 1)
        sum_gateup = jnp.swapaxes(scattered(grad_gateup, 2), 1, 2)
        sum_down = scattered(grad_down[0], 1)
    own_tokens = tokens.astype(f32)
    mixed_out = (own_tokens + own(total).astype(f32) + mlp_share).astype(bf16)
    row_mean = (row_sum / width).reshape(seqs, block, 1)
    gain_own = lax.dynamic_slice_in_dim(gain_one, column, local_width, 1)
    tokens_grad = middle_own + scale_one * (
        one_share * gain_own - own_tokens * scale_one * row_mean
    )
    return (
        mixed_out,
        tokens_grad.astype(bf16),
        sum_qkv,
        sum_conv,
        sum_beta,
        sum_outgate,
        sum_head,
        sum_out,
        sum_mix,
        sum_mlp,
        sum_gateup,
        sum_down,
    )


def solution(mesh):
    return jax.shard_map(
        body,
        mesh=mesh,
        in_specs=(
            P(None, "dp", "mp"),
            P(None, "dp", None),
            P(None, "dp"),
            P(),
            P(None, "dp", "mp"),
            P(None, None, "mp", "dp"),
            P("dp", "mp"),
            P("dp", "mp"),
            P("dp"),
            P("mp", "dp"),
            P("dp"),
            P("dp"),
            P(None, "dp", "mp"),
            P("mp", "dp"),
        ),
        out_specs=(
            P(None, "dp", "mp"),
            P(None, "dp", "mp"),
            P(None, "dp", "mp"),
            P(None, None, "mp", "dp"),
            P("dp", "mp"),
            P("dp", "mp"),
            P("dp"),
            P("mp", "dp"),
            P("dp"),
            P("dp"),
            P(None, "dp", "mp"),
            P("mp", "dp"),
        ),
        check_vma=False,
    )
```

```python
from functools import partial

import jax
import jax.numpy as jnp
from jax import lax
from jax.experimental import pallas as pl
from jax.experimental.pallas import tpu as pltpu
from jax.sharding import PartitionSpec as P

DK = 128
KW = 4
PAD = 8
HALO = 16
VMEM = 58 * 2**20

eps_norm = 1e-06
eps_unit = 1e-06

f32 = jnp.float32
bf16 = jnp.bfloat16


def split(v):
    if v.dtype == bf16:
        return v, None
    high = v.astype(bf16)
    return high, (v - high.astype(f32)).astype(bf16)


def mm(a, b, ca=1, cb=0, passes=3):
    def one(x, y):
        return lax.dot_general(x, y, (((ca,), (cb,)), ((), ())), preferred_element_type=f32)

    if passes == 1:
        return one(a.astype(bf16), b.astype(bf16))
    (ah, al), (bh, bl) = split(a), split(b)
    out = one(ah, bh)
    if bl is not None:
        out = out + one(ah, bl)
    if al is not None:
        out = out + one(al, bh)
    return out


def places(rows, cols):
    return (
        lax.broadcasted_iota(jnp.int32, (rows, cols), 0),
        lax.broadcasted_iota(jnp.int32, (rows, cols), 1),
    )


def unit_lower_inverses(blocks):
    size = blocks[0].shape[0]
    if size > 128:
        half = size // 2
        parts = unit_lower_inverses(
            [a[:half, :half] for a in blocks] + [a[half:, half:] for a in blocks]
        )
        firsts, seconds = parts[: len(blocks)], parts[len(blocks) :]
        inner = [mm(a[half:, :half], x) for a, x in zip(blocks, firsts)]
        lower = [-mm(x, y) for x, y in zip(seconds, inner)]
        zero = jnp.zeros((half, half), f32)
        return [
            jnp.concatenate(
                [jnp.concatenate([x, zero], 1), jnp.concatenate([y, z], 1)], 0
            )
            for x, y, z in zip(firsts, lower, seconds)
        ]
    rows, cols = places(size, size)
    eye = (rows == cols).astype(f32)
    level = 0
    inverses = None
    while (1 << level) < size:
        mask = (
            ((rows >> (level + 1)) == (cols >> (level + 1)))
            & (((rows >> level) & 1) == 1)
            & (((cols >> level) & 1) == 0)
        ).astype(f32)
        lows = [a * mask for a in blocks]
        if level == 0:
            inverses = [eye - low for low in lows]
        else:
            inner = [mm(low, x) for low, x in zip(lows, inverses)]
            inverses = [x - mm(x, y) for x, y in zip(inverses, inner)]
        level += 1
    return inverses


def head_slice(h):
    return slice(h * DK, (h + 1) * DK)


def convolve(proj_ref, before_ref, taps, i, h):
    own = proj_ref[i, 0, :, head_slice(h)].astype(f32)
    length = own.shape[0]
    ext = jnp.concatenate([before_ref[i, 0, :, head_slice(h)].astype(f32), own], 0)
    shifts = [ext[HALO - KW + 1 + j : HALO - KW + 1 + j + length] for j in range(KW)]
    out = None
    for j in range(KW):
        tap = taps[i * KW + j : i * KW + j + 1, head_slice(h)]
        out = tap * shifts[j] if out is None else out + tap * shifts[j]
    sig = jax.nn.sigmoid(out)
    return shifts, out, sig, out * sig


def unit(acts):
    inv = lax.rsqrt(jnp.sum(acts * acts, -1, keepdims=True) + eps_unit)
    return acts * inv, inv


def rule_inputs(proj_ref, before_ref, taps, h):
    parts = [convolve(proj_ref, before_ref, taps, i, h) for i in range(3)]
    q, q_inv = unit(parts[0][3])
    k, k_inv = unit(parts[1][3])
    return parts, (q, q_inv), (k, k_inv), parts[2][3]


def norm_factor(values):
    return lax.rsqrt(jnp.mean(values * values, -1, keepdims=True) + eps_norm)


def project_kernel(layout, *refs):
    place_ref, rows_ref, gain_ref, beta_ref = refs[:4]
    pieces = refs[4 : 4 + len(layout)]
    hidden_ref, proj_ref, tail_ref, logit_ref, scale_ref, keep_ref = refs[4 + len(layout) :]
    rows = rows_ref[0].astype(f32)
    scale = norm_factor(rows)
    scale_ref[0] = scale
    keep_ref[...] = (rows * scale * gain_ref[...]).astype(bf16)
    logits = mm(keep_ref[...], beta_ref[...])
    logit_ref[0] = logits[:, : logit_ref.shape[2]]
    sums = [None] * 3
    for (k, start, size, block), piece in zip(layout, pieces):
        at = pl.multiple_of((place_ref[0] ^ k) * block + start, 128)
        part = keep_ref[:, pl.ds(at, size)]
        hidden_ref[0, :, k * block + start : k * block + start + size] = part
        for i in range(3):
            term = mm(part, piece[i])
            sums[i] = term if sums[i] is None else sums[i] + term
    for i in range(3):
        low = sums[i].astype(bf16)
        proj_ref[i, 0] = low
        tail_ref[i, 0] = low[low.shape[0] - HALO :]


def pre_kernel(proj_ref, before_ref, taps_ref, logit_ref, x_ref, wu_ref, qo_ref, to_ref):
    heads = to_ref.shape[1]
    taps = taps_ref[...]
    length = proj_ref.shape[2]
    betas = jax.nn.sigmoid(logit_ref[0])
    r, c = places(length, length)
    strict = (r > c).astype(f32)
    full = (r >= c).astype(f32)
    saved, blocks = [], []
    for h in range(heads):
        _, (q, _), (k, _), v = rule_inputs(proj_ref, before_ref, taps, h)
        q, k, v = q.astype(bf16), k.astype(bf16), v.astype(bf16)
        beta = betas[:, h : h + 1]
        gram = mm(k, k, 1, 1)
        blocks.append(beta * gram * strict)
        saved.append((q, k, v, beta))
    inverses = unit_lower_inverses(blocks)
    r, c = places(DK, DK)
    eye = (r == c).astype(f32)
    for h in range(heads):
        q, k, v, beta = saved[h]
        x = inverses[h]
        x_ref[0, h] = x
        kv = jnp.concatenate([k.astype(f32), v.astype(f32)], 1) * beta
        wu = mm(x, kv)
        wu_ref[0, h] = wu
        scores = mm(q, k, 1, 1) * full
        pwu = mm(scores, wu)
        qo_ref[0, h, :, :DK] = q.astype(f32) - pwu[:, :DK]
        qo_ref[0, h, :, DK:] = pwu[:, DK:]
        kwu = mm(k, wu, 0, 0)
        to_ref[0, h, :, :DK] = (eye - kwu[:, :DK]).astype(bf16)
        to_ref[0, h, :, DK:] = kwu[:, DK:].astype(bf16)


def by_piece(place_ref, refs):
    if len(refs) > 1 or len(refs[0].shape) < 4:
        return refs
    return [refs[0].at[place_ref[0] ^ k] for k in range(4)]


def gate_kernel(layout, place_ref, hidden_ref, *refs):
    gate_ref = refs[-1]
    refs = by_piece(place_ref, refs[:-1])
    total = None
    for (k, start, size, block), ref in zip(layout, refs):
        at = k * block + start
        term = mm(hidden_ref[0, :, at : at + size], gate_part(ref)[...])
        total = term if total is None else total + term
    gate_ref[0] = total


def gate_part(ref):
    return ref.at[0] if len(ref.shape) == 3 else ref


def out_columns(layout, refs):
    for (k, start, size, block), ref in zip(layout, refs):
        at, half = k * block + start, size // 2
        if len(ref.shape) == 2:
            yield at, size, ref
            continue
        inner = ref.shape[1] // 2
        yield at, half, ref.at[1, :inner]
        yield at + half, half, ref.at[1, inner:]


def mix_kernel(layout, count, place_ref, *refs):
    near, rest = refs[:count], refs[count:]
    qo_ref, gate_ref, gain_ref = rest[:3]
    outs = by_piece(place_ref, rest[3:-5])
    part_ref, normed_ref, rule_ref, state_ref = rest[-4:]
    heads = state_ref.shape[1]
    for h in range(heads):
        state = near[-1][0, h, :, DK:].astype(f32)
        for ref in reversed(near[:-1]):
            state = mm(ref[0, h, :, :DK], state) + ref[0, h, :, DK:].astype(f32)
        state_ref[0, h] = state
        qo = qo_ref[0, h]
        out = (mm(qo[:, :DK], state) + qo[:, DK:]) * DK ** (-0.5)
        rule_ref[0, :, head_slice(h)] = out
        gate = gate_ref[0, :, head_slice(h)]
        normed = out * norm_factor(out) * gain_ref[...] * (gate * jax.nn.sigmoid(gate))
        normed_ref[0, :, head_slice(h)] = normed.astype(bf16)
    for at, size, ref in out_columns(layout, outs):
        part_ref[0, :, at : at + size] = mm(normed_ref[0], ref[...]).astype(bf16)


def prepare_kernel(layout, place_ref, rows_ref, grad_ref, factor_ref, about_ref, cot_ref):
    for k, start, size, block in layout:
        at = pl.multiple_of((place_ref[0] ^ k) * block + start, 128)
        to = slice(k * block + start, k * block + start + size)
        about_ref[0, :, to] = rows_ref[0, :, pl.ds(at, size)]
        grad = grad_ref[0, :, pl.ds(at, size)].astype(f32) * factor_ref[0]
        cot_ref[0, :, to] = grad.astype(bf16)


def down_kernel(layout, place_ref, mlp_ref, *refs):
    part_ref = refs[-1]
    for (k, start, size, block), ref in zip(layout, refs):
        at = pl.multiple_of((place_ref[0] ^ k) * block + start, 128)
        part_ref[0, :, pl.ds(at, size)] = mm(mlp_ref[0], ref[...]).astype(bf16)


def feed_gradient_kernel(ranges, hidden_ref, cot_ref, pair_ref, mlp_ref, *outs):
    for n, (start, size) in enumerate(ranges):
        hidden = hidden_ref[:, start : start + size]
        outs[2 * n][0] = mm(pair_ref[0], hidden, 0, 0).astype(bf16)
        outs[2 * n][1] = mm(pair_ref[1], hidden, 0, 0).astype(bf16)
        outs[2 * n + 1][0] = mm(mlp_ref[...], cot_ref[:, start : start + size], 0, 0).astype(bf16)


def qkv_gradient_kernel(ranges, hidden_ref, dproj_ref, dlogit_ref, *outs):
    outs = outs[-len(ranges) - 1 :]
    for (start, size), out in zip(ranges, outs[:-1]):
        hidden = hidden_ref[:, start : start + size]
        for i in range(3):
            out[i] = mm(hidden, dproj_ref[i], 0, 0).astype(bf16)
    outs[-1][...] = mm(dlogit_ref[...], hidden_ref[...], 0, 0)


def pair_gradient_kernel(ranges, hidden_ref, dgate_ref, normed_ref, mix_ref, *outs):
    inner = normed_ref.shape[1]
    for (start, size), out in zip(ranges, outs):
        out[0] = mm(hidden_ref[:, start : start + size], dgate_ref[...], 0, 0).astype(bf16)
        for n in range(2):
            at = start + n * size // 2
            mix = mix_ref[:, at : at + size // 2]
            out[1, n * inner : (n + 1) * inner] = mm(normed_ref[...], mix, 0, 0).astype(bf16)


def add_halves_kernel(*refs):
    one_ref, two_ref, low_ref, high_ref, one_out, two_out = refs[:4] + refs[-2:]

    def add(a, b):
        return (a.astype(f32) + b.astype(f32)).astype(bf16)

    half = low_ref.shape
    rows = slice(0, half[1])
    if half[1] < one_ref.shape[1]:
        late, lanes, late_lanes = slice(half[1], 2 * half[1]), slice(None), slice(None)
    else:
        late, lanes, late_lanes = rows, slice(0, half[2]), slice(half[2], 2 * half[2])
    one_out[...] = one_ref[...]
    two_out[...] = two_ref[...]
    one_out[0, late, late_lanes] = add(one_ref[0, late, late_lanes], high_ref[0])
    two_out[0, rows, lanes] = add(two_ref[0, rows, lanes], low_ref[0])


def add_last_kernel(*refs):
    own_ref, one_ref, two_ref, out_ref = refs[:3] + refs[-1:]
    out_ref[...] = own_ref[...].astype(f32) + one_ref[...].astype(f32) + two_ref[...].astype(f32)


def feed_kernel(layout, *refs):
    rows_ref, total_ref, cot_ref, gain_ref = refs[:4]
    count = len(layout)
    gateups, downs = (refs[4 + n * count : 4 + (n + 1) * count] for n in range(2))
    two_ref, hidden_ref, mlp_ref, pair_ref = refs[-4:]
    middle = rows_ref[0].astype(f32) + total_ref[0].astype(f32)
    hidden_ref[0] = (middle * norm_factor(middle) * gain_ref[...]).astype(bf16)
    gate, up, grad = None, None, None
    for (k, start, size, block), w_gateup, w_down in zip(layout, gateups, downs):
        lanes = slice(k * block + start, k * block + start + size)
        hidden = hidden_ref[0, :, lanes]
        terms = (
            mm(hidden, w_gateup[0], 1, 1),
            mm(hidden, w_gateup[1], 1, 1),
            mm(cot_ref[0, :, lanes], w_down[...], 1, 1),
        )
        if gate is None:
            gate, up, grad = terms
        else:
            gate, up, grad = gate + terms[0], up + terms[1], grad + terms[2]
    sig = jax.nn.sigmoid(gate)
    silu = gate * sig
    mlp_ref[0] = (silu * up).astype(bf16)
    first = (grad * up * sig * (1.0 + gate * (1.0 - sig))).astype(bf16)
    second = (grad * silu).astype(bf16)
    pair_ref[0, 0] = first
    pair_ref[1, 0] = second
    for (k, start, size, block), w_gateup in zip(layout, gateups):
        lanes = slice(k * block + start, k * block + start + size)
        two = mm(first, w_gateup[0]) + mm(second, w_gateup[1])
        two_ref[0, :, lanes] = two.astype(bf16)


def middle_back_kernel(layout, pieces, at_ref, *refs):
    two_ref, cot_ref, rows_ref, total_ref, gain_ref, rule_ref, gate_ref, head_gain_ref, qo_ref = refs[:9]
    outs = by_piece(at_ref, refs[9 : 9 + pieces])
    mix_ref, own_ref, mlpgain_ref, drule_ref, dgate_ref, dgain_ref, direct_ref, keep_ref = refs[-8:]
    middle = rows_ref[0].astype(f32) + total_ref[0].astype(f32)
    factor = norm_factor(middle)
    normal = middle * factor
    two = two_ref[0].astype(f32)
    mlpgain_ref[0] = jnp.sum(two * normal, 0, keepdims=True)
    scaled = two * gain_ref[...]
    mean = jnp.mean(scaled * normal, -1, keepdims=True)
    keep_ref[...] = cot_ref[0].astype(f32) + factor * (scaled - normal * mean)
    width = own_ref.shape[2]
    own_ref[0] = keep_ref[:, pl.ds(pl.multiple_of(at_ref[1], 128), width)]
    mix = keep_ref[...].astype(bf16)
    mix_ref[0] = mix
    grads = None
    for at, size, ref in out_columns(layout, outs):
        term = mm(mix_ref[0, :, at : at + size], ref[...], 1, 1)
        grads = term if grads is None else grads + term
    total = jnp.zeros((1, DK), f32)
    for h in range(direct_ref.shape[1]):
        grad = grads[:, head_slice(h)]
        out = rule_ref[0, :, head_slice(h)]
        gate = gate_ref[0, :, head_slice(h)]
        inv = norm_factor(out)
        n = out * inv
        sig = jax.nn.sigmoid(gate)
        silu = gate * sig
        gg = grad * head_gain_ref[...]
        dn = gg * silu
        drule = inv * (dn - n * jnp.mean(dn * n, -1, keepdims=True))
        drule_ref[0, :, head_slice(h)] = drule
        dgate = gg * n * sig * (1.0 + gate * (1.0 - sig))
        dgate_ref[0, :, head_slice(h)] = dgate.astype(bf16)
        total = total + jnp.sum(grad * n * silu, 0, keepdims=True)
        direct = mm(qo_ref[0, h, :, :DK], drule, 0, 0) * DK ** (-0.5)
        direct_ref[0, h] = direct.astype(bf16)
    dgain_ref[0] = total


def first_back_kernel(layout, pair_layout, count, place_ref, *refs):
    dproj_ref, dgate_ref, dlogit_ref, proj_ref, gate_ref, logit_ref, beta_ref, rows_ref, scale_ref = refs[:9]
    pieces = refs[9 : 9 + len(layout)]
    pairs = by_piece(place_ref, refs[9 + len(layout) : 9 + len(layout) + count])
    one_ref, rowsum_ref, gainsum_ref = refs[-3:]
    gates = {}
    for (k, start, size, block), ref in zip(pair_layout, pairs):
        gates[k] = ref
    for (k, start, size, block), piece in zip(layout, pieces):
        lanes = slice(k * block + start, k * block + start + size)
        grad = mm(dgate_ref[...], gate_part(gates[k])[start : start + size], 1, 1)
        for i in range(3):
            grad = grad + mm(dproj_ref[i], piece[i], 1, 1)
        for h in range(beta_ref.shape[0]):
            grad = grad + dlogit_ref[:, h : h + 1].astype(f32) * beta_ref[h : h + 1, lanes]
        at = pl.multiple_of((place_ref[0] ^ k) * block + start, 128)
        one_ref[:, pl.ds(at, size)] = grad.astype(bf16)
        gainsum_ref[:, lanes] = jnp.sum(
            grad * (rows_ref[:, lanes].astype(f32) * scale_ref[...]), 0, keepdims=True
        )
    total = dgate_ref[...].astype(f32) * gate_ref[...]
    for i in range(3):
        total = total + dproj_ref[i].astype(f32) * proj_ref[i].astype(f32)
    total = jnp.sum(total, -1, keepdims=True)
    logits = dlogit_ref[...].astype(f32) * logit_ref[...]
    rowsum_ref[...] = total + jnp.sum(logits, -1, keepdims=True)


def back_kernel(count, *refs):
    (
        proj_ref,
        before_ref,
        taps_ref,
        logit_ref,
        x_ref,
        wu_ref,
        state_ref,
        drule_ref,
    ) = refs[:8]
    dproj_ref, last_ref, first_ref, dtaps_ref, dlogit_ref = refs[-5:]
    others = refs[8 : 8 + 2 * count - 1]
    directs, nexts = others[:count], others[count:]
    heads = state_ref.shape[1]
    taps = taps_ref[...]
    length = proj_ref.shape[2]
    betas = jax.nn.sigmoid(logit_ref[0])
    r, c = places(length, length)
    strict = (r > c).astype(f32)
    full = (r >= c).astype(f32)
    zeros = jnp.zeros((PAD, DK), f32)
    for h in range(heads):
        parts, (qu, q_inv), (ku, k_inv), vu = rule_inputs(proj_ref, before_ref, taps, h)
        q, k, v = qu.astype(bf16), ku.astype(bf16), vu.astype(bf16)
        beta = betas[:, h : h + 1]
        leave = jnp.zeros((DK, DK), f32)
        for j in reversed(range(count)):
            here = directs[j][0, h].astype(f32)
            leave = here if j == count - 1 else mm(nexts[j][0, h], leave, 0, 0) + here
        state = state_ref[0, h]
        wu = wu_ref[0, h]
        u = wu[:, DK:] - mm(wu[:, :DK], state)
        resid = v.astype(f32) - mm(k, state)
        dout = drule_ref[0, :, head_slice(h)] * DK ** (-0.5)
        gram = mm(k, k, 1, 1)
        scores = mm(q, k, 1, 1) * full
        du = mm(scores, dout, 0, 0) + mm(k, leave)
        y = mm(x_ref[0, h], du, 0, 0)
        by = beta * y
        da = -(mm(y, u, 1, 1) * strict)
        dbeta = jnp.sum(y * resid, -1, keepdims=True) + jnp.sum(da * gram, -1, keepdims=True)
        dgram = beta * da
        dscores = mm(dout, u, 1, 1) * full
        dq = mm(dout, state, 1, 1) + mm(dscores, k)
        dk = (
            mm(dgram, k)
            + mm(dgram, k, 0, 0)
            + mm(dscores, q, 0, 0)
            + mm(u, leave, 1, 1)
            - mm(by, state, 1, 1)
        )
        dlogit_ref[0, :, h : h + 1] = (dbeta * beta * (1.0 - beta)).astype(bf16)
        dq = (dq - qu * jnp.sum(qu * dq, -1, keepdims=True)) * q_inv
        dk = (dk - ku * jnp.sum(ku * dk, -1, keepdims=True)) * k_inv
        for i, dact in enumerate((dq, dk, by)):
            shifts, out, sig, _ = parts[i]
            dconv = dact * sig * (1.0 + out * (1.0 - sig))
            ext = jnp.concatenate([zeros, dconv, zeros], 0)
            total = None
            for j in range(KW):
                at = i * KW + j
                dtaps_ref[0, at : at + 1, head_slice(h)] = jnp.sum(
                    dconv * shifts[j], 0, keepdims=True
                )
                tap = taps[at : at + 1, head_slice(h)]
                term = tap * ext[KW - 1 - j : KW - 1 - j + PAD + length]
                total = term if total is None else total + term
            first_ref[i, 0, :, head_slice(h)] = total[:PAD]
            last_ref[i, 0, :, head_slice(h)] = total[length:]
            dproj_ref[i, 0, :, head_slice(h)] = total[PAD:].astype(bf16)


def call(kernel, ins, outs, steps, scalar=None, scratch=(), limit=VMEM, alias=None):
    def spec(shape, axis):
        if axis == "any":
            return pl.BlockSpec(memory_space=pl.ANY)
        block = tuple(1 if n == axis else size for n, size in enumerate(shape))
        where = lambda s, *_: tuple(s if n == axis else 0 for n in range(len(shape)))
        if axis is None:
            return pl.BlockSpec(block, where, pipeline_mode=pl.Buffered(1))
        return pl.BlockSpec(block, where)

    given = [] if scalar is None else [scalar]
    return pl.pallas_call(
        kernel,
        grid_spec=pltpu.PrefetchScalarGridSpec(
            num_scalar_prefetch=len(given),
            grid=(steps,),
            in_specs=[spec(a.shape, axis) for a, axis in ins],
            out_specs=[spec(o.shape, axis) for o, axis in outs],
            scratch_shapes=scratch,
        ),
        out_shape=[o for o, _ in outs],
        input_output_aliases=alias or {},
        compiler_params=pltpu.CompilerParams(vmem_limit_bytes=limit),
    )(*given, *[a for a, _ in ins])


def shape_of(shape, dtype):
    return jax.ShapeDtypeStruct(shape, dtype)


def shifted(array, axis, by):
    devices = lax.axis_size(axis)
    pairs = [(i, i + by) for i in range(devices) if 0 <= i + by < devices]
    return lax.ppermute(array, axis, pairs)


def after(values, *others):
    flat, tree = jax.tree.flatten(values)
    others = jax.tree.leaves(others)
    here = pl.BlockSpec(memory_space=pl.ANY)
    out = pl.pallas_call(
        lambda *refs: None,
        in_specs=[here] * (len(flat) + len(others)),
        out_specs=[here] * len(flat),
        out_shape=[shape_of(a.shape, a.dtype) for a in flat],
        input_output_aliases={n: n for n in range(len(flat))},
    )(*flat, *others)
    return jax.tree.unflatten(tree, out)


def copied_after(values, *others):
    count = len(values)

    def kernel(*refs):
        for n in range(count):
            refs[n - count][...] = refs[n][...]

    ins = [(a, None) for a in values] + [(a, "any") for a in others]
    return call(kernel, ins, [(shape_of(a.shape, a.dtype), None) for a in values], 1)


def swap(array, bits):
    return lax.ppermute(array, "dp", [(i, i ^ bits) for i in range(4)])


def first_hop(own):
    return swap(own, 1), swap(own, 2)


def halves_of(hop, axis):
    low, high = (jnp.split(part, 2, axis) for part in hop)
    return low[0], high[1]


def gathered_pieces(own, axis, hop=None, halves=None):
    hop = hop or first_hop(own)
    low, high = halves or halves_of(hop, axis)
    return [own, *hop, swap(low, 2), swap(high, 1)]


def far_hop(low, high):
    return swap(low, 1), swap(high, 2)


def near_sums(pieces, far_in, *others):
    own, one, two = pieces
    specs = [(one, 0), (two, 0), (far_in[0], 0), (far_in[1], 0)]
    specs += [(a, "any") for a in others]
    outs = [(shape_of(a.shape, a.dtype), 0) for a in (one, two)]
    return own, *call(add_halves_kernel, specs, outs, one.shape[0])


def near_hop(pieces):
    own, one, two = pieces
    return own, swap(one, 1), swap(two, 2)


def sum_last(parts, *others):
    own = parts[0]
    ins = [(a, 0) for a in parts] + [(a, "any") for a in others]
    [total] = call(add_last_kernel, ins, [(shape_of(own.shape, f32), 0)], own.shape[0])
    return total


def pack(parts):
    return jnp.concatenate([p.reshape(-1) for p in parts])


def unpack(flat, shapes):
    out, at = [], 0
    for shape in shapes:
        size = 1
        for n in shape:
            size *= n
        out.append(flat[..., at : at + size].reshape(flat.shape[:-1] + tuple(shape)))
        at += size
    return out


def padded(flat, multiple=1024):
    return jnp.pad(flat, (0, -flat.shape[0] % multiple))


def body(
    tokens,
    out_grad,
    domain,
    group_weight,
    w_qkv,
    conv_weight,
    w_beta,
    w_outgate,
    head_gain,
    w_out,
    mixer_gain,
    mlp_gain,
    w_gateup,
    w_down,
):
    dp = lax.axis_size("dp")
    place = lax.axis_index("dp")
    seqs, block, local_width = tokens.shape
    count_rows = seqs * block
    heads = conv_weight.shape[2]
    inner = heads * DK
    column = lax.axis_index("mp") * local_width
    near_four = dp == 4

    def blocks_about(array, axis):
        if not near_four:
            return array
        size = array.shape[axis] // 4
        return jnp.concatenate(
            [lax.dynamic_slice_in_dim(array, (place ^ k) * size, size, axis) for k in range(4)],
            axis,
        )

    width = out_grad.shape[2]
    turn = place if near_four else jnp.int32(0)
    column_about = ((column // (width // 4)) ^ turn) * (width // 4) + column % (width // 4)

    def own(array):
        array = array.reshape(seqs, block, width)
        return lax.dynamic_slice_in_dim(array, column_about, local_width, 2)

    onehot = (domain[..., None] == jnp.arange(3, dtype=jnp.int32)).astype(f32)
    own_counts = jnp.sum(onehot, axis=(0, 1))
    high = jnp.floor(own_counts / 128.0)
    digits = jnp.concatenate([high, own_counts - 128.0 * high]).astype(bf16)
    small = [w_beta, conv_weight, head_gain, mixer_gain, mlp_gain, digits]
    packed = padded(pack(small))
    size = width // 4
    if near_four:
        qkv_hop = first_hop(w_qkv)
        qkv_halves = halves_of(qkv_hop, 1)
        qkv = gathered_pieces(w_qkv, 1, qkv_hop, qkv_halves)
        packed = after(packed, qkv_halves)
        gathered = jnp.stack([packed] + [swap(packed, bits) for bits in (1, 2, 3)])
        half = w_out.shape[1] // 2
        pair_own = jnp.stack(
            [w_outgate, jnp.concatenate([w_out[:, :half], w_out[:, half:]], 0)]
        )
        pair_layout = [(k, 0, size, size) for k in range(4)]
        layout = pair_layout[:3] + [(3, 0, size // 2, size), (3, size // 2, size // 2, size)]
    else:
        gathered = lax.all_gather(packed, "dp")
        qkv = [lax.all_gather(w_qkv, "dp", axis=1, tiled=True)]
        gate_pieces = [lax.all_gather(w_outgate, "dp", axis=0, tiled=True)]
        out_pieces = [lax.all_gather(w_out, "dp", axis=1, tiled=True)]
        layout = pair_layout = [(0, 0, width, width)]
    ranges = [(k * step + start, n) for k, start, n, step in layout]
    g_beta, g_conv, g_head, g_mix, g_mlp, g_digits = unpack(gathered, [a.shape for a in small])
    about_beta = g_beta.reshape(-1, heads)
    full_beta = blocks_about(about_beta, 0)
    full_conv = jnp.moveaxis(blocks_about(g_conv, 0), 0, 3).reshape(3 * KW, inner).astype(f32)
    gain_head = blocks_about(g_head, 0).reshape(1, DK).astype(f32)
    gain_one = blocks_about(g_mix.reshape(1, -1).astype(f32), 1)
    gain_two = g_mlp.reshape(1, -1).astype(f32)
    sums = jnp.sum(g_digits.astype(f32), 0)
    counts = 128.0 * sums[:3] + sums[3:]
    table = group_weight * (domain.shape[0] * domain.shape[1] * dp) / counts
    factor = jnp.sum(onehot * table, -1)[..., None]

    def flat(array):
        return array.reshape(array.shape[:-3] + (count_rows, array.shape[-1]))

    rows = lax.all_gather(tokens, "mp", axis=2, tiled=True)
    if near_four:
        gate_pieces = out_pieces = [lax.all_gather(after(pair_own, packed), "dp")]
    turn_one = turn.reshape(1)
    per_token = (seqs, block)
    square = (seqs, heads, DK, DK)
    hidden_one, proj, tail, logits, scale_one = call(
        partial(project_kernel, layout),
        [(rows, 0), (gain_one, None), (jnp.pad(full_beta, ((0, 0), (0, 128 - heads))), None)]
        + [(a, None) for a in qkv],
        [
            (shape_of(per_token + (width,), bf16), 0),
            (shape_of((3,) + per_token + (inner,), bf16), 1),
            (shape_of((3, seqs, HALO, inner), bf16), 1),
            (shape_of(per_token + (heads,), f32), 0),
            (shape_of(per_token + (1,), f32), 0),
        ],
        seqs,
        scalar=turn_one,
        scratch=[pltpu.VMEM((block, width), bf16)],
    )
    before = shifted(tail, "dp", 1)
    inverse, wu, qo, to = call(
        pre_kernel,
        [(proj, 1), (before, 1), (full_conv, None), (logits, 0)],
        [
            (shape_of((seqs, heads, block, block), f32), 0),
            (shape_of((seqs, heads, block, 2 * DK), f32), 0),
            (shape_of((seqs, heads, block, 2 * DK), f32), 0),
            (shape_of((seqs, heads, DK, 2 * DK), bf16), 0),
        ],
        seqs,
    )
    near = [shifted(to, "dp", c) for c in range(1, dp)]
    [gates] = call(
        partial(gate_kernel, pair_layout),
        [(hidden_one, 0)] + [(a, None) for a in gate_pieces],
        [(shape_of(per_token + (inner,), f32), 0)],
        seqs,
        scalar=turn_one,
    )
    rows_about, cotangent = call(
        partial(prepare_kernel, layout),
        [(rows, 0), (out_grad, 0), (factor, 0)],
        [(shape_of(per_token + (width,), bf16), 0)] * 2,
        seqs,
        scalar=turn_one,
    )
    turned = jnp.swapaxes(w_gateup, 1, 2)
    feed_own = [turned, w_down]
    mixer_part, normed, rule, state = call(
        partial(mix_kernel, pair_layout, len(near)),
        [(a, 0) for a in near]
        + [(qo, 0), (gates, 0), (gain_head, None)]
        + [(a, None) for a in out_pieces]
        + [(cotangent, "any")],
        [
            (shape_of(per_token + (width,), bf16), 0),
            (shape_of(per_token + (inner,), bf16), 0),
            (shape_of(per_token + (inner,), f32), 0),
            (shape_of(square, f32), 0),
        ],
        seqs,
        scalar=turn_one,
    )
    total = lax.psum(mixer_part, "mp")
    nexts = [shifted(to[..., :DK], "dp", -c) for c in range(1, dp - 1)]
    if near_four:
        gateup, down = (gathered_pieces(a, a.ndim - 1) for a in copied_after(feed_own, mixer_part, *nexts))
    else:
        gateup, down = (
            [lax.all_gather(a, "dp", axis=a.ndim - 1, tiled=True)] for a in feed_own
        )
    units = w_down.shape[0]
    two_part, hidden_two, hidden_mlp, grad_pair = call(
        partial(feed_kernel, layout),
        [(rows_about, 0), (total, 0), (cotangent, 0), (gain_two, None)]
        + [(a, None) for a in gateup + down],
        [
            (shape_of(per_token + (width,), bf16), 0),
            (shape_of(per_token + (width,), bf16), 0),
            (shape_of(per_token + (units,), bf16), 0),
            (shape_of((2,) + per_token + (units,), bf16), 1),
        ],
        seqs,
    )
    grad_two = lax.psum(two_part, "mp")

    def feed_gradients(some):
        outs = [(shape_of((m, units, n), bf16), None) for _, n in some for m in (2, 1)]
        ins = [flat(hidden_two), flat(cotangent), flat(grad_pair), flat(hidden_mlp)]
        made = call(partial(feed_gradient_kernel, some), [(a, None) for a in ins], outs, 1)
        return made[::2], made[1::2]

    if near_four:
        feed_in = [far_hop(*far) for far in feed_gradients(ranges[3:])]
        near_gateup, near_down = feed_gradients(ranges[:3])
        gateup_sums = near_hop(near_sums(near_gateup, feed_in[0], *feed_in[1]))
        down_sums = near_hop(near_sums(near_down, feed_in[1]))
        held = [(a, "any") for a in gateup_sums[1:]]
    else:
        [grad_gateup], [grad_down] = feed_gradients(ranges)
        held = []
    [down_part] = call(
        partial(down_kernel, layout),
        [(hidden_mlp, 0)] + [(a, None) for a in down],
        [(shape_of(per_token + (width,), bf16), 0)],
        seqs,
        scalar=turn_one,
    )
    mlp_share = lax.psum_scatter(down_part, "mp", scatter_dimension=2, tiled=True)
    grad_mix, middle_own, mlpgain, drule, dgate, dgain, direct = call(
        partial(middle_back_kernel, pair_layout, len(out_pieces)),
        [
            (grad_two, 0),
            (cotangent, 0),
            (rows_about, 0),
            (total, 0),
            (gain_two, None),
            (rule, 0),
            (gates, 0),
            (gain_head, None),
            (qo, 0),
        ]
        + [(a, None) for a in out_pieces]
        + [(down_part, "any")]
        + held,
        [
            (shape_of(per_token + (width,), bf16), 0),
            (shape_of(per_token + (local_width,), f32), 0),
            (shape_of((seqs, 1, width), f32), 0),
            (shape_of(per_token + (inner,), f32), 0),
            (shape_of(per_token + (inner,), bf16), 0),
            (shape_of((seqs, 1, DK), f32), 0),
            (shape_of(square, bf16), 0),
        ],
        seqs,
        scalar=jnp.stack([turn, column_about]),
        scratch=[pltpu.VMEM((block, width), f32)],
    )
    directs = [shifted(direct, "dp", -c) for c in range(1, dp)]
    if near_four:
        pair_grads = call(
            partial(pair_gradient_kernel, [(k * size, size) for k in range(4)]),
            [(flat(a), None) for a in (hidden_one, dgate, normed, grad_mix)],
            [(shape_of((2, size, inner), bf16), None)] * 4,
            1,
        )
        held = [(a, "any") for a in (pair_grads[3], *down_sums[1:])]
    else:
        grad_outgate = jnp.einsum(
            "td,tc->dc", flat(hidden_one), flat(dgate), preferred_element_type=f32
        )
        grad_outproj = jnp.einsum(
            "tc,td->cd", flat(normed), flat(grad_mix), preferred_element_type=f32
        )
        held = []
    dproj, last, first, dtaps, dlogits = call(
        partial(back_kernel, len(directs)),
        [
            (proj, 1),
            (before, 1),
            (full_conv, None),
            (logits, 0),
            (inverse, 0),
            (wu, 0),
            (state, 0),
            (drule, 0),
        ]
        + [(a, 0) for a in directs + nexts]
        + held,
        [
            (shape_of((3,) + per_token + (inner,), bf16), 1),
            (shape_of((3, seqs, PAD, inner), f32), 1),
            (shape_of((3, seqs, PAD, inner), f32), 1),
            (shape_of((seqs, 3 * KW, inner), f32), 0),
            (shape_of(per_token + (heads,), bf16), 0),
        ],
        seqs,
    )
    later = shifted(first, "dp", -1)
    dproj = lax.dynamic_update_slice(dproj, (last + later).astype(bf16), (0, 0, block - PAD, 0))
    one_low, row_part, gain_part = call(
        partial(first_back_kernel, layout, pair_layout, len(gate_pieces)),
        [
            (flat(dproj), None),
            (flat(dgate), None),
            (flat(dlogits), None),
            (flat(proj), None),
            (flat(gates), None),
            (flat(logits), None),
            (about_beta.T.astype(f32), None),
            (flat(rows_about), None),
            (flat(scale_one), None),
        ]
        + [(a, None) for a in qkv + gate_pieces]
        + [(mlp_share, "any")],
        [
            (shape_of((count_rows, width), bf16), None),
            (shape_of((count_rows, 1), f32), None),
            (shape_of((1, width), f32), None),
        ],
        1,
        scalar=turn_one,
    )
    one_share = lax.psum_scatter(
        one_low.reshape(seqs, block, width), "mp", scatter_dimension=2, tiled=True
    ).astype(f32)
    made = call(
        partial(qkv_gradient_kernel, ranges),
        [(flat(hidden_one), None), (flat(dproj), None), (flat(dlogits), None), (row_part, "any")],
        [(shape_of((3, n, inner), bf16), None) for _, n in ranges]
        + [(shape_of((heads, width), f32), None)],
        1,
    )

    shared = [row_part[:, 0], gain_part[0], jnp.sum(dgain, (0, 1))]
    packed_shared = after(pack(shared), made[0])
    everyone = lax.optimization_barrier(lax.all_gather(packed_shared, "mp"))
    row_sum, mixgain, headgain = unpack(jnp.sum(everyone, 0), [a.shape for a in shared])
    def pieces(array, axis, about):
        shape = array.shape
        cut = array.reshape(shape[:axis] + (dp, shape[axis] // dp) + shape[axis + 1 :])
        cut = jnp.moveaxis(cut, axis, 0).reshape(dp, -1)
        return blocks_about(cut, 0) if about else cut

    smalls = jnp.concatenate(
        [
            pieces(jnp.sum(dtaps, 0).reshape(3, KW, heads, DK), 3, True),
            pieces(made[-1].T, 0, False),
            pieces(headgain, 0, True),
            pieces(mixgain, 0, False),
            pieces(jnp.sum(mlpgain, (0, 1)), 0, False),
        ],
        1,
    )
    if near_four:
        own_qkv, *near_qkv = near_sums(made[:3], far_hop(made[3], made[4]), everyone)
        sent = [padded(smalls[k].astype(bf16)) for k in (1, 2, 3)]
        mine = smalls[0]
        for bits, part in zip((1, 2, 3), after(sent, near_qkv)):
            mine = mine + swap(part, bits)[: mine.shape[0]].astype(f32)
    else:
        gathered = lax.all_gather(smalls.astype(bf16), "dp")
        mine = jnp.sum(
            lax.dynamic_index_in_dim(gathered, place, 1, keepdims=False).astype(f32), 0
        )
    sum_conv, sum_beta, sum_head, sum_mix, sum_mlp = unpack(
        mine,
        [conv_weight.shape, w_beta.shape, head_gain.shape, mixer_gain.shape, mlp_gain.shape],
    )
    if near_four:
        late = near_qkv[0]
        pair_sums = near_hop(near_sums(pair_grads[:3], far_hop(*jnp.split(pair_grads[3], 2, 1))))
        sum_qkv = sum_last(near_hop((own_qkv, *near_qkv)))
        sum_gateup = jnp.swapaxes(sum_last(gateup_sums, late), 1, 2)
        sum_down = sum_last(down_sums, late)[0]
        sum_pair = sum_last(pair_sums)
        sum_outgate = sum_pair[0]
        sum_out = jnp.concatenate(jnp.split(sum_pair[1], 2, 0), 1)
    else:

        def scattered(array, axis):
            return lax.psum_scatter(array, "dp", scatter_dimension=axis, tiled=True).astype(f32)

        sum_qkv = scattered(made[0], 1)
        sum_outgate = scattered(grad_outgate.astype(bf16), 0)
        sum_out = scattered(grad_outproj.astype(bf16), 1)
        sum_gateup = jnp.swapaxes(scattered(grad_gateup, 2), 1, 2)
        sum_down = scattered(grad_down[0], 1)
    own_tokens = tokens.astype(f32)
    mixed_out = (own_tokens + own(total).astype(f32) + mlp_share.astype(f32)).astype(bf16)
    row_mean = (row_sum / width).reshape(seqs, block, 1)
    gain_own = lax.dynamic_slice_in_dim(gain_one, column, local_width, 1)
    tokens_grad = middle_own + scale_one * (
        one_share * gain_own - own_tokens * scale_one * row_mean
    )
    return (
        mixed_out,
        tokens_grad.astype(bf16),
        sum_qkv,
        sum_conv,
        sum_beta,
        sum_outgate,
        sum_head,
        sum_out,
        sum_mix,
        sum_mlp,
        sum_gateup,
        sum_down,
    )


def solution(mesh):
    return jax.shard_map(
        body,
        mesh=mesh,
        in_specs=(
            P(None, "dp", "mp"),
            P(None, "dp", None),
            P(None, "dp"),
            P(),
            P(None, "dp", "mp"),
            P(None, None, "mp", "dp"),
            P("dp", "mp"),
            P("dp", "mp"),
            P("dp"),
            P("mp", "dp"),
            P("dp"),
            P("dp"),
            P(None, "dp", "mp"),
            P("mp", "dp"),
        ),
        out_specs=(
            P(None, "dp", "mp"),
            P(None, "dp", "mp"),
            P(None, "dp", "mp"),
            P(None, None, "mp", "dp"),
            P("dp", "mp"),
            P("dp", "mp"),
            P("dp"),
            P("mp", "dp"),
            P("dp"),
            P("dp"),
            P(None, "dp", "mp"),
            P("mp", "dp"),
        ),
        check_vma=False,
    )
```

```python
from functools import partial

import jax
import jax.numpy as jnp
from jax import lax
from jax.experimental import pallas as pl
from jax.experimental.pallas import tpu as pltpu
from jax.sharding import PartitionSpec as P

DK = 128
KW = 4
PAD = 8
HALO = 16
VMEM = 58 * 2**20

eps_norm = 1e-06
eps_unit = 1e-06

f32 = jnp.float32
bf16 = jnp.bfloat16


def split(v):
    if v.dtype == bf16:
        return v, None
    high = v.astype(bf16)
    return high, (v - high.astype(f32)).astype(bf16)


def mm(a, b, ca=1, cb=0, passes=3):
    def one(x, y):
        return lax.dot_general(x, y, (((ca,), (cb,)), ((), ())), preferred_element_type=f32)

    if passes == 1:
        return one(a.astype(bf16), b.astype(bf16))
    (ah, al), (bh, bl) = split(a), split(b)
    out = one(ah, bh)
    if bl is not None:
        out = out + one(ah, bl)
    if al is not None:
        out = out + one(al, bh)
    return out


def places(rows, cols):
    return (
        lax.broadcasted_iota(jnp.int32, (rows, cols), 0),
        lax.broadcasted_iota(jnp.int32, (rows, cols), 1),
    )


def unit_lower_inverses(blocks):
    size = blocks[0].shape[0]
    if size > 128:
        half = size // 2
        parts = unit_lower_inverses(
            [a[:half, :half] for a in blocks] + [a[half:, half:] for a in blocks]
        )
        firsts, seconds = parts[: len(blocks)], parts[len(blocks) :]
        inner = [mm(a[half:, :half], x) for a, x in zip(blocks, firsts)]
        lower = [-mm(x, y) for x, y in zip(seconds, inner)]
        zero = jnp.zeros((half, half), f32)
        return [
            jnp.concatenate(
                [jnp.concatenate([x, zero], 1), jnp.concatenate([y, z], 1)], 0
            )
            for x, y, z in zip(firsts, lower, seconds)
        ]
    rows, cols = places(size, size)
    eye = (rows == cols).astype(f32)
    level = 0
    inverses = None
    while (1 << level) < size:
        mask = (
            ((rows >> (level + 1)) == (cols >> (level + 1)))
            & (((rows >> level) & 1) == 1)
            & (((cols >> level) & 1) == 0)
        ).astype(f32)
        lows = [a * mask for a in blocks]
        if level == 0:
            inverses = [eye - low for low in lows]
        else:
            inner = [mm(low, x) for low, x in zip(lows, inverses)]
            inverses = [x - mm(x, y) for x, y in zip(inverses, inner)]
        level += 1
    return inverses


def head_slice(h):
    return slice(h * DK, (h + 1) * DK)


def convolve(proj_ref, before_ref, taps, i, h):
    own = proj_ref[i, 0, :, head_slice(h)].astype(f32)
    length = own.shape[0]
    ext = jnp.concatenate([before_ref[i, 0, :, head_slice(h)].astype(f32), own], 0)
    shifts = [ext[HALO - KW + 1 + j : HALO - KW + 1 + j + length] for j in range(KW)]
    out = None
    for j in range(KW):
        tap = taps[i * KW + j : i * KW + j + 1, head_slice(h)]
        out = tap * shifts[j] if out is None else out + tap * shifts[j]
    sig = jax.nn.sigmoid(out)
    return shifts, out, sig, out * sig


def unit(acts):
    inv = lax.rsqrt(jnp.sum(acts * acts, -1, keepdims=True) + eps_unit)
    return acts * inv, inv


def rule_inputs(proj_ref, before_ref, taps, h):
    parts = [convolve(proj_ref, before_ref, taps, i, h) for i in range(3)]
    q, q_inv = unit(parts[0][3])
    k, k_inv = unit(parts[1][3])
    return parts, (q, q_inv), (k, k_inv), parts[2][3]


def norm_factor(values):
    return lax.rsqrt(jnp.mean(values * values, -1, keepdims=True) + eps_norm)


def project_kernel(layout, *refs):
    place_ref, rows_ref, gain_ref, beta_ref = refs[:4]
    pieces = refs[4 : 4 + len(layout)]
    hidden_ref, proj_ref, tail_ref, logit_ref, scale_ref, keep_ref = refs[4 + len(layout) :]
    rows = rows_ref[0].astype(f32)
    scale = norm_factor(rows)
    scale_ref[0] = scale
    keep_ref[...] = (rows * scale * gain_ref[...]).astype(bf16)
    logits = mm(keep_ref[...], beta_ref[...])
    logit_ref[0] = logits[:, : logit_ref.shape[2]]
    sums = [None] * 3
    for (k, start, size, block), piece in zip(layout, pieces):
        at = pl.multiple_of((place_ref[0] ^ k) * block + start, 128)
        part = keep_ref[:, pl.ds(at, size)]
        hidden_ref[0, :, k * block + start : k * block + start + size] = part
        for i in range(3):
            term = mm(part, piece[i])
            sums[i] = term if sums[i] is None else sums[i] + term
    for i in range(3):
        low = sums[i].astype(bf16)
        proj_ref[i, 0] = low
        tail_ref[i, 0] = low[low.shape[0] - HALO :]


def pre_kernel(proj_ref, before_ref, taps_ref, logit_ref, x_ref, wu_ref, qo_ref, to_ref):
    heads = to_ref.shape[1]
    taps = taps_ref[...]
    length = proj_ref.shape[2]
    betas = jax.nn.sigmoid(logit_ref[0])
    r, c = places(length, length)
    strict = (r > c).astype(f32)
    full = (r >= c).astype(f32)
    saved, blocks = [], []
    for h in range(heads):
        _, (q, _), (k, _), v = rule_inputs(proj_ref, before_ref, taps, h)
        q, k, v = q.astype(bf16), k.astype(bf16), v.astype(bf16)
        beta = betas[:, h : h + 1]
        gram = mm(k, k, 1, 1)
        blocks.append(beta * gram * strict)
        saved.append((q, k, v, beta))
    inverses = unit_lower_inverses(blocks)
    r, c = places(DK, DK)
    eye = (r == c).astype(f32)
    for h in range(heads):
        q, k, v, beta = saved[h]
        x = inverses[h]
        x_ref[0, h] = x
        kv = jnp.concatenate([k.astype(f32), v.astype(f32)], 1) * beta
        wu = mm(x, kv)
        wu_ref[0, h] = wu
        scores = mm(q, k, 1, 1) * full
        pwu = mm(scores, wu)
        qo_ref[0, h, :, :DK] = q.astype(f32) - pwu[:, :DK]
        qo_ref[0, h, :, DK:] = pwu[:, DK:]
        kwu = mm(k, wu, 0, 0)
        to_ref[0, h, :, :DK] = (eye - kwu[:, :DK]).astype(bf16)
        to_ref[0, h, :, DK:] = kwu[:, DK:].astype(bf16)


def by_piece(place_ref, refs):
    if len(refs) > 1 or len(refs[0].shape) < 4:
        return refs
    return [refs[0].at[place_ref[0] ^ k] for k in range(4)]


def gate_kernel(layout, place_ref, hidden_ref, *refs):
    gate_ref = refs[-1]
    refs = by_piece(place_ref, refs[:-1])
    total = None
    for (k, start, size, block), ref in zip(layout, refs):
        at = k * block + start
        term = mm(hidden_ref[0, :, at : at + size], gate_part(ref)[...])
        total = term if total is None else total + term
    gate_ref[0] = total


def gate_part(ref):
    return ref.at[0] if len(ref.shape) == 3 else ref


def out_columns(layout, refs):
    for (k, start, size, block), ref in zip(layout, refs):
        at, half = k * block + start, size // 2
        if len(ref.shape) == 2:
            yield at, size, ref
            continue
        inner = ref.shape[1] // 2
        yield at, half, ref.at[1, :inner]
        yield at + half, half, ref.at[1, inner:]


def mix_kernel(layout, count, place_ref, *refs):
    near, rest = refs[:count], refs[count:]
    qo_ref, gate_ref, gain_ref = rest[:3]
    outs = by_piece(place_ref, rest[3:-5])
    part_ref, normed_ref, rule_ref, state_ref = rest[-4:]
    heads = state_ref.shape[1]
    for h in range(heads):
        state = near[-1][0, h, :, DK:].astype(f32)
        for ref in reversed(near[:-1]):
            state = mm(ref[0, h, :, :DK], state) + ref[0, h, :, DK:].astype(f32)
        state_ref[0, h] = state
        qo = qo_ref[0, h]
        out = (mm(qo[:, :DK], state) + qo[:, DK:]) * DK ** (-0.5)
        rule_ref[0, :, head_slice(h)] = out
        gate = gate_ref[0, :, head_slice(h)]
        normed = out * norm_factor(out) * gain_ref[...] * (gate * jax.nn.sigmoid(gate))
        normed_ref[0, :, head_slice(h)] = normed.astype(bf16)
    for at, size, ref in out_columns(layout, outs):
        part_ref[0, :, at : at + size] = mm(normed_ref[0], ref[...]).astype(bf16)


def prepare_kernel(layout, place_ref, rows_ref, grad_ref, factor_ref, about_ref, cot_ref):
    for k, start, size, block in layout:
        at = pl.multiple_of((place_ref[0] ^ k) * block + start, 128)
        to = slice(k * block + start, k * block + start + size)
        about_ref[0, :, to] = rows_ref[0, :, pl.ds(at, size)]
        grad = grad_ref[0, :, pl.ds(at, size)].astype(f32) * factor_ref[0]
        cot_ref[0, :, to] = grad.astype(bf16)


def down_kernel(layout, place_ref, mlp_ref, *refs):
    part_ref = refs[-1]
    for (k, start, size, block), ref in zip(layout, refs):
        at = pl.multiple_of((place_ref[0] ^ k) * block + start, 128)
        part_ref[0, :, pl.ds(at, size)] = mm(mlp_ref[0], ref[...]).astype(bf16)


def feed_gradient_kernel(ranges, hidden_ref, cot_ref, pair_ref, mlp_ref, *outs):
    for n, (start, size) in enumerate(ranges):
        hidden = hidden_ref[:, start : start + size]
        outs[2 * n][0] = mm(pair_ref[0], hidden, 0, 0).astype(bf16)
        outs[2 * n][1] = mm(pair_ref[1], hidden, 0, 0).astype(bf16)
        outs[2 * n + 1][0] = mm(mlp_ref[...], cot_ref[:, start : start + size], 0, 0).astype(bf16)


def qkv_gradient_kernel(ranges, hidden_ref, dproj_ref, dlogit_ref, *outs):
    outs = outs[-len(ranges) - 1 :]
    for (start, size), out in zip(ranges, outs[:-1]):
        hidden = hidden_ref[:, start : start + size]
        for i in range(3):
            out[i] = mm(hidden, dproj_ref[i], 0, 0).astype(bf16)
    outs[-1][...] = mm(dlogit_ref[...], hidden_ref[...], 0, 0)


def pair_gradient_kernel(ranges, hidden_ref, dgate_ref, normed_ref, mix_ref, *outs):
    inner = normed_ref.shape[1]
    for (start, size), out in zip(ranges, outs):
        out[0] = mm(hidden_ref[:, start : start + size], dgate_ref[...], 0, 0).astype(bf16)
        for n in range(2):
            at = start + n * size // 2
            mix = mix_ref[:, at : at + size // 2]
            out[1, n * inner : (n + 1) * inner] = mm(normed_ref[...], mix, 0, 0).astype(bf16)


def add_halves_kernel(*refs):
    one_ref, two_ref, low_ref, high_ref, one_out, two_out = refs[:4] + refs[-2:]

    def add(a, b):
        return (a.astype(f32) + b.astype(f32)).astype(bf16)

    half = low_ref.shape
    rows = slice(0, half[1])
    if half[1] < one_ref.shape[1]:
        late, lanes, late_lanes = slice(half[1], 2 * half[1]), slice(None), slice(None)
    else:
        late, lanes, late_lanes = rows, slice(0, half[2]), slice(half[2], 2 * half[2])
    one_out[...] = one_ref[...]
    two_out[...] = two_ref[...]
    one_out[0, late, late_lanes] = add(one_ref[0, late, late_lanes], high_ref[0])
    two_out[0, rows, lanes] = add(two_ref[0, rows, lanes], low_ref[0])


def add_last_kernel(*refs):
    own_ref, one_ref, two_ref, out_ref = refs[:3] + refs[-1:]
    out_ref[...] = own_ref[...].astype(f32) + one_ref[...].astype(f32) + two_ref[...].astype(f32)


def feed_kernel(layout, *refs):
    rows_ref, total_ref, cot_ref, gain_ref = refs[:4]
    count = len(layout)
    gateups, downs = (refs[4 + n * count : 4 + (n + 1) * count] for n in range(2))
    two_ref, hidden_ref, mlp_ref, pair_ref = refs[-4:]
    middle = rows_ref[0].astype(f32) + total_ref[0].astype(f32)
    hidden_ref[0] = (middle * norm_factor(middle) * gain_ref[...]).astype(bf16)
    gate, up, grad = None, None, None
    for (k, start, size, block), w_gateup, w_down in zip(layout, gateups, downs):
        lanes = slice(k * block + start, k * block + start + size)
        hidden = hidden_ref[0, :, lanes]
        terms = (
            mm(hidden, w_gateup[0], 1, 1),
            mm(hidden, w_gateup[1], 1, 1),
            mm(cot_ref[0, :, lanes], w_down[...], 1, 1),
        )
        if gate is None:
            gate, up, grad = terms
        else:
            gate, up, grad = gate + terms[0], up + terms[1], grad + terms[2]
    sig = jax.nn.sigmoid(gate)
    silu = gate * sig
    mlp_ref[0] = (silu * up).astype(bf16)
    first = (grad * up * sig * (1.0 + gate * (1.0 - sig))).astype(bf16)
    second = (grad * silu).astype(bf16)
    pair_ref[0, 0] = first
    pair_ref[1, 0] = second
    for (k, start, size, block), w_gateup in zip(layout, gateups):
        lanes = slice(k * block + start, k * block + start + size)
        two = mm(first, w_gateup[0]) + mm(second, w_gateup[1])
        two_ref[0, :, lanes] = two.astype(bf16)


def middle_back_kernel(layout, pieces, at_ref, *refs):
    two_ref, cot_ref, rows_ref, total_ref, gain_ref, rule_ref, gate_ref, head_gain_ref, qo_ref = refs[:9]
    outs = by_piece(at_ref, refs[9 : 9 + pieces])
    mix_ref, own_ref, mlpgain_ref, drule_ref, dgate_ref, dgain_ref, direct_ref, keep_ref = refs[-8:]
    middle = rows_ref[0].astype(f32) + total_ref[0].astype(f32)
    factor = norm_factor(middle)
    normal = middle * factor
    two = two_ref[0].astype(f32)
    mlpgain_ref[0] = jnp.sum(two * normal, 0, keepdims=True)
    scaled = two * gain_ref[...]
    mean = jnp.mean(scaled * normal, -1, keepdims=True)
    keep_ref[...] = cot_ref[0].astype(f32) + factor * (scaled - normal * mean)
    width = own_ref.shape[2]
    own_ref[0] = keep_ref[:, pl.ds(pl.multiple_of(at_ref[1], 128), width)]
    mix = keep_ref[...].astype(bf16)
    mix_ref[0] = mix
    grads = None
    for at, size, ref in out_columns(layout, outs):
        term = mm(mix_ref[0, :, at : at + size], ref[...], 1, 1)
        grads = term if grads is None else grads + term
    total = jnp.zeros((1, DK), f32)
    for h in range(direct_ref.shape[1]):
        grad = grads[:, head_slice(h)]
        out = rule_ref[0, :, head_slice(h)]
        gate = gate_ref[0, :, head_slice(h)]
        inv = norm_factor(out)
        n = out * inv
        sig = jax.nn.sigmoid(gate)
        silu = gate * sig
        gg = grad * head_gain_ref[...]
        dn = gg * silu
        drule = inv * (dn - n * jnp.mean(dn * n, -1, keepdims=True))
        drule_ref[0, :, head_slice(h)] = drule
        dgate = gg * n * sig * (1.0 + gate * (1.0 - sig))
        dgate_ref[0, :, head_slice(h)] = dgate.astype(bf16)
        total = total + jnp.sum(grad * n * silu, 0, keepdims=True)
        direct = mm(qo_ref[0, h, :, :DK], drule, 0, 0) * DK ** (-0.5)
        direct_ref[0, h] = direct.astype(bf16)
    dgain_ref[0] = total


def first_back_kernel(layout, pair_layout, count, place_ref, *refs):
    dproj_ref, dgate_ref, dlogit_ref, proj_ref, gate_ref, logit_ref, beta_ref, rows_ref, scale_ref = refs[:9]
    pieces = refs[9 : 9 + len(layout)]
    pairs = by_piece(place_ref, refs[9 + len(layout) : 9 + len(layout) + count])
    one_ref, rowsum_ref, gainsum_ref = refs[-3:]
    gates = {}
    for (k, start, size, block), ref in zip(pair_layout, pairs):
        gates[k] = ref
    for (k, start, size, block), piece in zip(layout, pieces):
        lanes = slice(k * block + start, k * block + start + size)
        grad = mm(dgate_ref[...], gate_part(gates[k])[start : start + size], 1, 1)
        for i in range(3):
            grad = grad + mm(dproj_ref[i], piece[i], 1, 1)
        for h in range(beta_ref.shape[0]):
            grad = grad + dlogit_ref[:, h : h + 1].astype(f32) * beta_ref[h : h + 1, lanes]
        at = pl.multiple_of((place_ref[0] ^ k) * block + start, 128)
        one_ref[:, pl.ds(at, size)] = grad.astype(bf16)
        gainsum_ref[:, lanes] = jnp.sum(
            grad * (rows_ref[:, lanes].astype(f32) * scale_ref[...]), 0, keepdims=True
        )
    total = dgate_ref[...].astype(f32) * gate_ref[...]
    for i in range(3):
        total = total + dproj_ref[i].astype(f32) * proj_ref[i].astype(f32)
    total = jnp.sum(total, -1, keepdims=True)
    logits = dlogit_ref[...].astype(f32) * logit_ref[...]
    rowsum_ref[...] = total + jnp.sum(logits, -1, keepdims=True)


def back_kernel(count, *refs):
    (
        proj_ref,
        before_ref,
        taps_ref,
        logit_ref,
        x_ref,
        wu_ref,
        state_ref,
        drule_ref,
    ) = refs[:8]
    dproj_ref, last_ref, first_ref, dtaps_ref, dlogit_ref = refs[-5:]
    others = refs[8 : 8 + 2 * count - 1]
    directs, nexts = others[:count], others[count:]
    heads = state_ref.shape[1]
    taps = taps_ref[...]
    length = proj_ref.shape[2]
    betas = jax.nn.sigmoid(logit_ref[0])
    r, c = places(length, length)
    strict = (r > c).astype(f32)
    full = (r >= c).astype(f32)
    zeros = jnp.zeros((PAD, DK), f32)
    for h in range(heads):
        parts, (qu, q_inv), (ku, k_inv), vu = rule_inputs(proj_ref, before_ref, taps, h)
        q, k, v = qu.astype(bf16), ku.astype(bf16), vu.astype(bf16)
        beta = betas[:, h : h + 1]
        leave = jnp.zeros((DK, DK), f32)
        for j in reversed(range(count)):
            here = directs[j][0, h].astype(f32)
            leave = here if j == count - 1 else mm(nexts[j][0, h], leave, 0, 0) + here
        state = state_ref[0, h]
        wu = wu_ref[0, h]
        u = wu[:, DK:] - mm(wu[:, :DK], state)
        resid = v.astype(f32) - mm(k, state)
        dout = drule_ref[0, :, head_slice(h)] * DK ** (-0.5)
        gram = mm(k, k, 1, 1)
        scores = mm(q, k, 1, 1) * full
        du = mm(scores, dout, 0, 0) + mm(k, leave)
        y = mm(x_ref[0, h], du, 0, 0)
        by = beta * y
        da = -(mm(y, u, 1, 1) * strict)
        dbeta = jnp.sum(y * resid, -1, keepdims=True) + jnp.sum(da * gram, -1, keepdims=True)
        dgram = beta * da
        dscores = mm(dout, u, 1, 1) * full
        dq = mm(dout, state, 1, 1) + mm(dscores, k)
        dk = (
            mm(dgram, k)
            + mm(dgram, k, 0, 0)
            + mm(dscores, q, 0, 0)
            + mm(u, leave, 1, 1)
            - mm(by, state, 1, 1)
        )
        dlogit_ref[0, :, h : h + 1] = (dbeta * beta * (1.0 - beta)).astype(bf16)
        dq = (dq - qu * jnp.sum(qu * dq, -1, keepdims=True)) * q_inv
        dk = (dk - ku * jnp.sum(ku * dk, -1, keepdims=True)) * k_inv
        for i, dact in enumerate((dq, dk, by)):
            shifts, out, sig, _ = parts[i]
            dconv = dact * sig * (1.0 + out * (1.0 - sig))
            ext = jnp.concatenate([zeros, dconv, zeros], 0)
            total = None
            for j in range(KW):
                at = i * KW + j
                dtaps_ref[0, at : at + 1, head_slice(h)] = jnp.sum(
                    dconv * shifts[j], 0, keepdims=True
                )
                tap = taps[at : at + 1, head_slice(h)]
                term = tap * ext[KW - 1 - j : KW - 1 - j + PAD + length]
                total = term if total is None else total + term
            first_ref[i, 0, :, head_slice(h)] = total[:PAD]
            last_ref[i, 0, :, head_slice(h)] = total[length:]
            dproj_ref[i, 0, :, head_slice(h)] = total[PAD:].astype(bf16)


def call(kernel, ins, outs, steps, scalar=None, scratch=(), limit=VMEM, alias=None):
    def spec(shape, axis):
        if axis == "any":
            return pl.BlockSpec(memory_space=pl.ANY)
        block = tuple(1 if n == axis else size for n, size in enumerate(shape))
        where = lambda s, *_: tuple(s if n == axis else 0 for n in range(len(shape)))
        if axis is None:
            return pl.BlockSpec(block, where, pipeline_mode=pl.Buffered(1))
        return pl.BlockSpec(block, where)

    given = [] if scalar is None else [scalar]
    return pl.pallas_call(
        kernel,
        grid_spec=pltpu.PrefetchScalarGridSpec(
            num_scalar_prefetch=len(given),
            grid=(steps,),
            in_specs=[spec(a.shape, axis) for a, axis in ins],
            out_specs=[spec(o.shape, axis) for o, axis in outs],
            scratch_shapes=scratch,
        ),
        out_shape=[o for o, _ in outs],
        input_output_aliases=alias or {},
        compiler_params=pltpu.CompilerParams(vmem_limit_bytes=limit),
    )(*given, *[a for a, _ in ins])


def shape_of(shape, dtype):
    return jax.ShapeDtypeStruct(shape, dtype)


def shifted(array, axis, by):
    devices = lax.axis_size(axis)
    pairs = [(i, i + by) for i in range(devices) if 0 <= i + by < devices]
    return lax.ppermute(array, axis, pairs)


def after(values, *others):
    flat, tree = jax.tree.flatten(values)
    others = jax.tree.leaves(others)
    here = pl.BlockSpec(memory_space=pl.ANY)
    out = pl.pallas_call(
        lambda *refs: None,
        in_specs=[here] * (len(flat) + len(others)),
        out_specs=[here] * len(flat),
        out_shape=[shape_of(a.shape, a.dtype) for a in flat],
        input_output_aliases={n: n for n in range(len(flat))},
    )(*flat, *others)
    return jax.tree.unflatten(tree, out)


def copies(values):
    count = len(values)

    def kernel(*refs):
        for n in range(count):
            refs[n - count][...] = refs[n][...]

    outs = [(shape_of(a.shape, a.dtype), None) for a in values]
    return call(kernel, [(a, None) for a in values], outs, 1)


def swap(array, bits):
    return lax.ppermute(array, "dp", [(i, i ^ bits) for i in range(4)])


def first_hop(own):
    return swap(own, 1), swap(own, 2)


def halves_of(hop, axis):
    low, high = (jnp.split(part, 2, axis) for part in hop)
    return low[0], high[1]


def gathered_pieces(own, axis, hop=None, halves=None):
    hop = hop or first_hop(own)
    low, high = halves or halves_of(hop, axis)
    return [own, *hop, swap(low, 2), swap(high, 1)]


def far_hop(low, high):
    return swap(low, 1), swap(high, 2)


def near_sums(pieces, far_in, *others):
    own, one, two = pieces
    specs = [(one, 0), (two, 0), (far_in[0], 0), (far_in[1], 0)]
    specs += [(a, "any") for a in others]
    outs = [(shape_of(a.shape, a.dtype), 0) for a in (one, two)]
    return own, *call(add_halves_kernel, specs, outs, one.shape[0])


def near_hop(pieces):
    own, one, two = pieces
    return own, swap(one, 1), swap(two, 2)


def sum_last(parts, *others):
    own = parts[0]
    ins = [(a, 0) for a in parts] + [(a, "any") for a in others]
    [total] = call(add_last_kernel, ins, [(shape_of(own.shape, f32), 0)], own.shape[0])
    return total


def pack(parts):
    return jnp.concatenate([p.reshape(-1) for p in parts])


def unpack(flat, shapes):
    out, at = [], 0
    for shape in shapes:
        size = 1
        for n in shape:
            size *= n
        out.append(flat[..., at : at + size].reshape(flat.shape[:-1] + tuple(shape)))
        at += size
    return out


def padded(flat, multiple=1024):
    return jnp.pad(flat, (0, -flat.shape[0] % multiple))


def body(
    tokens,
    out_grad,
    domain,
    group_weight,
    w_qkv,
    conv_weight,
    w_beta,
    w_outgate,
    head_gain,
    w_out,
    mixer_gain,
    mlp_gain,
    w_gateup,
    w_down,
):
    dp = lax.axis_size("dp")
    place = lax.axis_index("dp")
    seqs, block, local_width = tokens.shape
    count_rows = seqs * block
    heads = conv_weight.shape[2]
    inner = heads * DK
    column = lax.axis_index("mp") * local_width
    near_four = dp == 4

    def blocks_about(array, axis):
        if not near_four:
            return array
        size = array.shape[axis] // 4
        return jnp.concatenate(
            [lax.dynamic_slice_in_dim(array, (place ^ k) * size, size, axis) for k in range(4)],
            axis,
        )

    width = out_grad.shape[2]
    turn = place if near_four else jnp.int32(0)
    column_about = ((column // (width // 4)) ^ turn) * (width // 4) + column % (width // 4)

    def own(array):
        array = array.reshape(seqs, block, width)
        return lax.dynamic_slice_in_dim(array, column_about, local_width, 2)

    onehot = (domain[..., None] == jnp.arange(3, dtype=jnp.int32)).astype(f32)
    own_counts = jnp.sum(onehot, axis=(0, 1))
    high = jnp.floor(own_counts / 128.0)
    digits = jnp.concatenate([high, own_counts - 128.0 * high]).astype(bf16)
    small = [w_beta, conv_weight, head_gain, mixer_gain, mlp_gain, digits]
    packed = padded(pack(small))
    size = width // 4
    if near_four:
        qkv_hop = first_hop(w_qkv)
        qkv_halves = halves_of(qkv_hop, 1)
        qkv = gathered_pieces(w_qkv, 1, qkv_hop, qkv_halves)
        packed = after(packed, qkv_halves)
        gathered = jnp.stack([packed] + [swap(packed, bits) for bits in (1, 2, 3)])
        half = w_out.shape[1] // 2
        pair_own = jnp.stack(
            [w_outgate, jnp.concatenate([w_out[:, :half], w_out[:, half:]], 0)]
        )
        pair_layout = [(k, 0, size, size) for k in range(4)]
        layout = pair_layout[:3] + [(3, 0, size // 2, size), (3, size // 2, size // 2, size)]
    else:
        gathered = lax.all_gather(packed, "dp")
        qkv = [lax.all_gather(w_qkv, "dp", axis=1, tiled=True)]
        gate_pieces = [lax.all_gather(w_outgate, "dp", axis=0, tiled=True)]
        out_pieces = [lax.all_gather(w_out, "dp", axis=1, tiled=True)]
        layout = pair_layout = [(0, 0, width, width)]
    ranges = [(k * step + start, n) for k, start, n, step in layout]
    g_beta, g_conv, g_head, g_mix, g_mlp, g_digits = unpack(gathered, [a.shape for a in small])
    about_beta = g_beta.reshape(-1, heads)
    full_beta = blocks_about(about_beta, 0)
    full_conv = jnp.moveaxis(blocks_about(g_conv, 0), 0, 3).reshape(3 * KW, inner).astype(f32)
    gain_head = blocks_about(g_head, 0).reshape(1, DK).astype(f32)
    gain_one = blocks_about(g_mix.reshape(1, -1).astype(f32), 1)
    gain_two = g_mlp.reshape(1, -1).astype(f32)
    sums = jnp.sum(g_digits.astype(f32), 0)
    counts = 128.0 * sums[:3] + sums[3:]
    table = group_weight * (domain.shape[0] * domain.shape[1] * dp) / counts
    factor = jnp.sum(onehot * table, -1)[..., None]

    def flat(array):
        return array.reshape(array.shape[:-3] + (count_rows, array.shape[-1]))

    rows = lax.all_gather(tokens, "mp", axis=2, tiled=True)
    if near_four:
        gate_pieces = out_pieces = [lax.all_gather(after(pair_own, packed), "dp")]
    turn_one = turn.reshape(1)
    per_token = (seqs, block)
    square = (seqs, heads, DK, DK)
    hidden_one, proj, tail, logits, scale_one = call(
        partial(project_kernel, layout),
        [(rows, 0), (gain_one, None), (jnp.pad(full_beta, ((0, 0), (0, 128 - heads))), None)]
        + [(a, None) for a in qkv],
        [
            (shape_of(per_token + (width,), bf16), 0),
            (shape_of((3,) + per_token + (inner,), bf16), 1),
            (shape_of((3, seqs, HALO, inner), bf16), 1),
            (shape_of(per_token + (heads,), f32), 0),
            (shape_of(per_token + (1,), f32), 0),
        ],
        seqs,
        scalar=turn_one,
        scratch=[pltpu.VMEM((block, width), bf16)],
    )
    before = shifted(tail, "dp", 1)
    inverse, wu, qo, to = call(
        pre_kernel,
        [(proj, 1), (before, 1), (full_conv, None), (logits, 0)],
        [
            (shape_of((seqs, heads, block, block), f32), 0),
            (shape_of((seqs, heads, block, 2 * DK), f32), 0),
            (shape_of((seqs, heads, block, 2 * DK), f32), 0),
            (shape_of((seqs, heads, DK, 2 * DK), bf16), 0),
        ],
        seqs,
    )
    near = [shifted(to, "dp", c) for c in range(1, dp)]
    [gates] = call(
        partial(gate_kernel, pair_layout),
        [(hidden_one, 0)] + [(a, None) for a in gate_pieces],
        [(shape_of(per_token + (inner,), f32), 0)],
        seqs,
        scalar=turn_one,
    )
    rows_about, cotangent = call(
        partial(prepare_kernel, layout),
        [(rows, 0), (out_grad, 0), (factor, 0)],
        [(shape_of(per_token + (width,), bf16), 0)] * 2,
        seqs,
        scalar=turn_one,
    )
    turned = jnp.swapaxes(w_gateup, 1, 2)
    feed_own = [turned, w_down]
    mixer_part, normed, rule, state = call(
        partial(mix_kernel, pair_layout, len(near)),
        [(a, 0) for a in near]
        + [(qo, 0), (gates, 0), (gain_head, None)]
        + [(a, None) for a in out_pieces]
        + [(cotangent, "any")],
        [
            (shape_of(per_token + (width,), bf16), 0),
            (shape_of(per_token + (inner,), bf16), 0),
            (shape_of(per_token + (inner,), f32), 0),
            (shape_of(square, f32), 0),
        ],
        seqs,
        scalar=turn_one,
    )
    total = lax.psum(mixer_part, "mp")
    nexts = [shifted(to[..., :DK], "dp", -c) for c in range(1, dp - 1)]
    if near_four:
        gateup, down = (gathered_pieces(a, a.ndim - 1) for a in after(copies(feed_own), mixer_part, nexts))
    else:
        gateup, down = (
            [lax.all_gather(a, "dp", axis=a.ndim - 1, tiled=True)] for a in feed_own
        )
    units = w_down.shape[0]
    two_part, hidden_two, hidden_mlp, grad_pair = call(
        partial(feed_kernel, layout),
        [(rows_about, 0), (total, 0), (cotangent, 0), (gain_two, None)]
        + [(a, None) for a in gateup + down],
        [
            (shape_of(per_token + (width,), bf16), 0),
            (shape_of(per_token + (width,), bf16), 0),
            (shape_of(per_token + (units,), bf16), 0),
            (shape_of((2,) + per_token + (units,), bf16), 1),
        ],
        seqs,
    )
    grad_two = lax.psum(two_part, "mp")

    def feed_gradients(some):
        outs = [(shape_of((m, units, n), bf16), None) for _, n in some for m in (2, 1)]
        ins = [flat(hidden_two), flat(cotangent), flat(grad_pair), flat(hidden_mlp)]
        made = call(partial(feed_gradient_kernel, some), [(a, None) for a in ins], outs, 1)
        return made[::2], made[1::2]

    if near_four:
        feed_far = feed_gradients(ranges[3:])
        feed_in = [far_hop(*far) for far in feed_far]
        first_made = [(feed_far[0][0], "any")]
        near_gateup, near_down = feed_gradients(ranges[:3])
        gateup_sums = near_hop(near_sums(near_gateup, feed_in[0], *feed_in[1]))
        down_sums = near_hop(near_sums(near_down, feed_in[1]))
        held = [(a, "any") for a in gateup_sums[1:]]
    else:
        [grad_gateup], [grad_down] = feed_gradients(ranges)
        held = first_made = []
    [down_part] = call(
        partial(down_kernel, layout),
        [(hidden_mlp, 0)] + [(a, None) for a in down] + first_made,
        [(shape_of(per_token + (width,), bf16), 0)],
        seqs,
        scalar=turn_one,
    )
    mlp_share = lax.psum_scatter(down_part, "mp", scatter_dimension=2, tiled=True)
    grad_mix, middle_own, mlpgain, drule, dgate, dgain, direct = call(
        partial(middle_back_kernel, pair_layout, len(out_pieces)),
        [
            (grad_two, 0),
            (cotangent, 0),
            (rows_about, 0),
            (total, 0),
            (gain_two, None),
            (rule, 0),
            (gates, 0),
            (gain_head, None),
            (qo, 0),
        ]
        + [(a, None) for a in out_pieces]
        + [(down_part, "any")]
        + held,
        [
            (shape_of(per_token + (width,), bf16), 0),
            (shape_of(per_token + (local_width,), f32), 0),
            (shape_of((seqs, 1, width), f32), 0),
            (shape_of(per_token + (inner,), f32), 0),
            (shape_of(per_token + (inner,), bf16), 0),
            (shape_of((seqs, 1, DK), f32), 0),
            (shape_of(square, bf16), 0),
        ],
        seqs,
        scalar=jnp.stack([turn, column_about]),
        scratch=[pltpu.VMEM((block, width), f32)],
    )
    directs = [shifted(direct, "dp", -c) for c in range(1, dp)]
    if near_four:
        pair_grads = call(
            partial(pair_gradient_kernel, [(k * size, size) for k in range(4)]),
            [(flat(a), None) for a in (hidden_one, dgate, normed, grad_mix)],
            [(shape_of((2, size, inner), bf16), None)] * 4,
            1,
        )
        pair_in = far_hop(*jnp.split(pair_grads[3], 2, 1))
        held = [(a, "any") for a in (pair_grads[3], *down_sums[1:])]
    else:
        grad_outgate = jnp.einsum(
            "td,tc->dc", flat(hidden_one), flat(dgate), preferred_element_type=f32
        )
        grad_outproj = jnp.einsum(
            "tc,td->cd", flat(normed), flat(grad_mix), preferred_element_type=f32
        )
        held = []
    dproj, last, first, dtaps, dlogits = call(
        partial(back_kernel, len(directs)),
        [
            (proj, 1),
            (before, 1),
            (full_conv, None),
            (logits, 0),
            (inverse, 0),
            (wu, 0),
            (state, 0),
            (drule, 0),
        ]
        + [(a, 0) for a in directs + nexts]
        + held,
        [
            (shape_of((3,) + per_token + (inner,), bf16), 1),
            (shape_of((3, seqs, PAD, inner), f32), 1),
            (shape_of((3, seqs, PAD, inner), f32), 1),
            (shape_of((seqs, 3 * KW, inner), f32), 0),
            (shape_of(per_token + (heads,), bf16), 0),
        ],
        seqs,
    )
    later = shifted(first, "dp", -1)
    dproj = lax.dynamic_update_slice(dproj, (last + later).astype(bf16), (0, 0, block - PAD, 0))
    one_low, row_part, gain_part = call(
        partial(first_back_kernel, layout, pair_layout, len(gate_pieces)),
        [
            (flat(dproj), None),
            (flat(dgate), None),
            (flat(dlogits), None),
            (flat(proj), None),
            (flat(gates), None),
            (flat(logits), None),
            (about_beta.T.astype(f32), None),
            (flat(rows_about), None),
            (flat(scale_one), None),
        ]
        + [(a, None) for a in qkv + gate_pieces]
        + [(mlp_share, "any")]
        + ([(a, "any") for a in pair_in] if near_four else []),
        [
            (shape_of((count_rows, width), bf16), None),
            (shape_of((count_rows, 1), f32), None),
            (shape_of((1, width), f32), None),
        ],
        1,
        scalar=turn_one,
    )
    one_share = lax.psum_scatter(
        one_low.reshape(seqs, block, width), "mp", scatter_dimension=2, tiled=True
    ).astype(f32)
    made = call(
        partial(qkv_gradient_kernel, ranges),
        [(flat(hidden_one), None), (flat(dproj), None), (flat(dlogits), None), (row_part, "any")],
        [(shape_of((3, n, inner), bf16), None) for _, n in ranges]
        + [(shape_of((heads, width), f32), None)],
        1,
    )

    def pieces(array, axis, about):
        shape = array.shape
        cut = array.reshape(shape[:axis] + (dp, shape[axis] // dp) + shape[axis + 1 :])
        cut = jnp.moveaxis(cut, axis, 0).reshape(dp, -1)
        return blocks_about(cut, 0) if about else cut

    smalls = jnp.concatenate(
        [
            pieces(jnp.sum(dtaps, 0).reshape(3, KW, heads, DK), 3, True),
            pieces(made[-1].T, 0, False),
            pieces(jnp.sum(dgain, (0, 1)), 0, True),
            pieces(gain_part[0], 0, False),
            pieces(jnp.sum(mlpgain, (0, 1)), 0, False),
        ],
        1,
    )
    if near_four:
        own_qkv, *near_qkv = near_sums(made[:3], far_hop(made[3], made[4]))
        mine = smalls[0]
        for bits in (1, 2, 3):
            mine = mine + swap(padded(smalls[bits].astype(bf16)), bits)[: mine.shape[0]].astype(f32)
        late = near_qkv[0]
        sum_qkv = sum_last(near_hop((own_qkv, *near_qkv)))
        sum_gateup = jnp.swapaxes(sum_last(gateup_sums, late), 1, 2)
        sum_down = sum_last(down_sums, late)[0]
        pair_near = after(near_sums(pair_grads[:3], pair_in)[1:], near_qkv)
        sum_pair = sum_last(near_hop((pair_grads[0], *pair_near)), late)
        sum_outgate = sum_pair[0]
        sum_out = jnp.concatenate(jnp.split(sum_pair[1], 2, 0), 1)
    else:
        gathered = lax.all_gather(smalls.astype(bf16), "dp")
        mine = jnp.sum(
            lax.dynamic_index_in_dim(gathered, place, 1, keepdims=False).astype(f32), 0
        )

        def scattered(array, axis):
            return lax.psum_scatter(array, "dp", scatter_dimension=axis, tiled=True).astype(f32)

        sum_qkv = scattered(made[0], 1)
        sum_outgate = scattered(grad_outgate.astype(bf16), 0)
        sum_out = scattered(grad_outproj.astype(bf16), 1)
        sum_gateup = jnp.swapaxes(scattered(grad_gateup, 2), 1, 2)
        sum_down = scattered(grad_down[0], 1)
    sum_conv, sum_beta, sum_head, sum_mix, sum_mlp = unpack(
        mine,
        [conv_weight.shape, w_beta.shape, head_gain.shape, mixer_gain.shape, mlp_gain.shape],
    )
    rest = [row_part[:, 0], sum_head, sum_mix]
    packed_rest = padded(pack(rest), 128)
    if near_four:
        packed_rest = after(packed_rest, near_qkv)
    everyone = lax.optimization_barrier(lax.all_gather(packed_rest, "mp"))
    row_sum, sum_head, sum_mix = unpack(jnp.sum(everyone, 0), [a.shape for a in rest])

    own_tokens = tokens.astype(f32)
    mixed_out = (own_tokens + own(total).astype(f32) + mlp_share.astype(f32)).astype(bf16)
    row_mean = (row_sum / width).reshape(seqs, block, 1)
    gain_own = lax.dynamic_slice_in_dim(gain_one, column, local_width, 1)
    tokens_grad = middle_own + scale_one * (
        one_share * gain_own - own_tokens * scale_one * row_mean
    )
    return (
        mixed_out,
        tokens_grad.astype(bf16),
        sum_qkv,
        sum_conv,
        sum_beta,
        sum_outgate,
        sum_head,
        sum_out,
        sum_mix,
        sum_mlp,
        sum_gateup,
        sum_down,
    )


def solution(mesh):
    return jax.shard_map(
        body,
        mesh=mesh,
        in_specs=(
            P(None, "dp", "mp"),
            P(None, "dp", None),
            P(None, "dp"),
            P(),
            P(None, "dp", "mp"),
            P(None, None, "mp", "dp"),
            P("dp", "mp"),
            P("dp", "mp"),
            P("dp"),
            P("mp", "dp"),
            P("dp"),
            P("dp"),
            P(None, "dp", "mp"),
            P("mp", "dp"),
        ),
        out_specs=(
            P(None, "dp", "mp"),
            P(None, "dp", "mp"),
            P(None, "dp", "mp"),
            P(None, None, "mp", "dp"),
            P("dp", "mp"),
            P("dp", "mp"),
            P("dp"),
            P("mp", "dp"),
            P("dp"),
            P("dp"),
            P(None, "dp", "mp"),
            P("mp", "dp"),
        ),
        check_vma=False,
    )
```

```python
from functools import partial

import jax
import jax.numpy as jnp
from jax import lax
from jax.experimental import pallas as pl
from jax.experimental.pallas import tpu as pltpu
from jax.sharding import PartitionSpec as P

DK = 128
KW = 4
PAD = 8
HALO = 16
VMEM = 58 * 2**20

eps_norm = 1e-06
eps_unit = 1e-06

f32 = jnp.float32
bf16 = jnp.bfloat16


def split(v):
    if v.dtype == bf16:
        return v, None
    high = v.astype(bf16)
    return high, (v - high.astype(f32)).astype(bf16)


def mm(a, b, ca=1, cb=0, passes=3):
    def one(x, y):
        return lax.dot_general(x, y, (((ca,), (cb,)), ((), ())), preferred_element_type=f32)

    if passes == 1:
        return one(a.astype(bf16), b.astype(bf16))
    (ah, al), (bh, bl) = split(a), split(b)
    out = one(ah, bh)
    if bl is not None:
        out = out + one(ah, bl)
    if al is not None:
        out = out + one(al, bh)
    return out


def places(rows, cols):
    return (
        lax.broadcasted_iota(jnp.int32, (rows, cols), 0),
        lax.broadcasted_iota(jnp.int32, (rows, cols), 1),
    )


def unit_lower_inverses(blocks):
    size = blocks[0].shape[0]
    if size > 128:
        half = size // 2
        parts = unit_lower_inverses(
            [a[:half, :half] for a in blocks] + [a[half:, half:] for a in blocks]
        )
        firsts, seconds = parts[: len(blocks)], parts[len(blocks) :]
        inner = [mm(a[half:, :half], x) for a, x in zip(blocks, firsts)]
        lower = [-mm(x, y) for x, y in zip(seconds, inner)]
        zero = jnp.zeros((half, half), f32)
        return [
            jnp.concatenate(
                [jnp.concatenate([x, zero], 1), jnp.concatenate([y, z], 1)], 0
            )
            for x, y, z in zip(firsts, lower, seconds)
        ]
    rows, cols = places(size, size)
    eye = (rows == cols).astype(f32)
    level = 0
    inverses = None
    while (1 << level) < size:
        mask = (
            ((rows >> (level + 1)) == (cols >> (level + 1)))
            & (((rows >> level) & 1) == 1)
            & (((cols >> level) & 1) == 0)
        ).astype(f32)
        lows = [a * mask for a in blocks]
        if level == 0:
            inverses = [eye - low for low in lows]
        else:
            inner = [mm(low, x) for low, x in zip(lows, inverses)]
            inverses = [x - mm(x, y) for x, y in zip(inverses, inner)]
        level += 1
    return inverses


def head_slice(h):
    return slice(h * DK, (h + 1) * DK)


def convolve(proj_ref, before_ref, taps, i, h):
    own = proj_ref[i, 0, :, head_slice(h)].astype(f32)
    length = own.shape[0]
    ext = jnp.concatenate([before_ref[i, 0, :, head_slice(h)].astype(f32), own], 0)
    shifts = [ext[HALO - KW + 1 + j : HALO - KW + 1 + j + length] for j in range(KW)]
    out = None
    for j in range(KW):
        tap = taps[i * KW + j : i * KW + j + 1, head_slice(h)]
        out = tap * shifts[j] if out is None else out + tap * shifts[j]
    sig = jax.nn.sigmoid(out)
    return shifts, out, sig, out * sig


def unit(acts):
    inv = lax.rsqrt(jnp.sum(acts * acts, -1, keepdims=True) + eps_unit)
    return acts * inv, inv


def rule_inputs(proj_ref, before_ref, taps, h):
    parts = [convolve(proj_ref, before_ref, taps, i, h) for i in range(3)]
    q, q_inv = unit(parts[0][3])
    k, k_inv = unit(parts[1][3])
    return parts, (q, q_inv), (k, k_inv), parts[2][3]


def norm_factor(values):
    return lax.rsqrt(jnp.mean(values * values, -1, keepdims=True) + eps_norm)


def project_kernel(layout, *refs):
    place_ref, rows_ref, gain_ref, beta_ref = refs[:4]
    pieces = refs[4 : 4 + len(layout)]
    hidden_ref, proj_ref, tail_ref, logit_ref, scale_ref, keep_ref = refs[4 + len(layout) :]
    rows = rows_ref[0].astype(f32)
    scale = norm_factor(rows)
    scale_ref[0] = scale
    keep_ref[...] = (rows * scale * gain_ref[...]).astype(bf16)
    logits = mm(keep_ref[...], beta_ref[...])
    logit_ref[0] = logits[:, : logit_ref.shape[2]]
    sums = [None] * 3
    for (k, start, size, block), piece in zip(layout, pieces):
        at = pl.multiple_of((place_ref[0] ^ k) * block + start, 128)
        part = keep_ref[:, pl.ds(at, size)]
        hidden_ref[0, :, k * block + start : k * block + start + size] = part
        for i in range(3):
            term = mm(part, piece[i])
            sums[i] = term if sums[i] is None else sums[i] + term
    for i in range(3):
        low = sums[i].astype(bf16)
        proj_ref[i, 0] = low
        tail_ref[i, 0] = low[low.shape[0] - HALO :]


def pre_kernel(proj_ref, before_ref, taps_ref, logit_ref, x_ref, wu_ref, qo_ref, to_ref):
    seqs, heads = to_ref.shape[:2]
    taps = taps_ref[...]
    length = proj_ref.shape[2]
    r, c = places(length, length)
    strict = (r > c).astype(f32)
    full = (r >= c).astype(f32)
    saved, blocks = [], []
    for s in range(seqs):
        betas = jax.nn.sigmoid(logit_ref[s])
        rows, before = proj_ref.at[:, s : s + 1], before_ref.at[:, s : s + 1]
        for h in range(heads):
            _, (q, _), (k, _), v = rule_inputs(rows, before, taps, h)
            q, k, v = q.astype(bf16), k.astype(bf16), v.astype(bf16)
            beta = betas[:, h : h + 1]
            blocks.append(beta * mm(k, k, 1, 1) * strict)
            saved.append((s, h, q, k, v, beta))
    inverses = unit_lower_inverses(blocks)
    r, c = places(DK, DK)
    eye = (r == c).astype(f32)
    for (s, h, q, k, v, beta), x in zip(saved, inverses):
        x_ref[s, h] = x
        kv = jnp.concatenate([k.astype(f32), v.astype(f32)], 1) * beta
        wu = mm(x, kv)
        wu_ref[s, h] = wu
        scores = mm(q, k, 1, 1) * full
        pwu = mm(scores, wu)
        qo_ref[s, h, :, :DK] = q.astype(f32) - pwu[:, :DK]
        qo_ref[s, h, :, DK:] = pwu[:, DK:]
        kwu = mm(k, wu, 0, 0)
        to_ref[s, h, :, :DK] = (eye - kwu[:, :DK]).astype(bf16)
        to_ref[s, h, :, DK:] = kwu[:, DK:].astype(bf16)


def by_piece(place_ref, refs):
    if len(refs) > 1 or len(refs[0].shape) < 4:
        return refs
    return [refs[0].at[place_ref[0] ^ k] for k in range(4)]


def gate_kernel(layout, place_ref, hidden_ref, *refs):
    gate_ref = refs[-1]
    refs = by_piece(place_ref, refs[:-1])
    total = None
    for (k, start, size, block), ref in zip(layout, refs):
        at = k * block + start
        term = mm(hidden_ref[0, :, at : at + size], gate_part(ref)[...])
        total = term if total is None else total + term
    gate_ref[0] = total


def gate_part(ref):
    return ref.at[0] if len(ref.shape) == 3 else ref


def out_columns(layout, refs):
    for (k, start, size, block), ref in zip(layout, refs):
        at, half = k * block + start, size // 2
        if len(ref.shape) == 2:
            yield at, size, ref
            continue
        inner = ref.shape[1] // 2
        yield at, half, ref.at[1, :inner]
        yield at + half, half, ref.at[1, inner:]


def mix_kernel(layout, count, place_ref, *refs):
    near, rest = refs[:count], refs[count:]
    qo_ref, gate_ref, gain_ref = rest[:3]
    outs = by_piece(place_ref, rest[3:-5])
    part_ref, normed_ref, rule_ref, state_ref = rest[-4:]
    heads = state_ref.shape[1]
    for h in range(heads):
        state = near[-1][0, h, :, DK:].astype(f32)
        for ref in reversed(near[:-1]):
            state = mm(ref[0, h, :, :DK], state) + ref[0, h, :, DK:].astype(f32)
        state_ref[0, h] = state
        qo = qo_ref[0, h]
        out = (mm(qo[:, :DK], state) + qo[:, DK:]) * DK ** (-0.5)
        rule_ref[0, :, head_slice(h)] = out
        gate = gate_ref[0, :, head_slice(h)]
        normed = out * norm_factor(out) * gain_ref[...] * (gate * jax.nn.sigmoid(gate))
        normed_ref[0, :, head_slice(h)] = normed.astype(bf16)
    for at, size, ref in out_columns(layout, outs):
        part_ref[0, :, at : at + size] = mm(normed_ref[0], ref[...]).astype(bf16)


def prepare_kernel(layout, place_ref, rows_ref, grad_ref, factor_ref, about_ref, cot_ref):
    for k, start, size, block in layout:
        at = pl.multiple_of((place_ref[0] ^ k) * block + start, 128)
        to = slice(k * block + start, k * block + start + size)
        about_ref[0, :, to] = rows_ref[0, :, pl.ds(at, size)]
        grad = grad_ref[0, :, pl.ds(at, size)].astype(f32) * factor_ref[0]
        cot_ref[0, :, to] = grad.astype(bf16)


def down_kernel(layout, place_ref, mlp_ref, *refs):
    part_ref = refs[-1]
    for (k, start, size, block), ref in zip(layout, refs):
        at = pl.multiple_of((place_ref[0] ^ k) * block + start, 128)
        part_ref[0, :, pl.ds(at, size)] = mm(mlp_ref[0], ref[...]).astype(bf16)


def feed_gradient_kernel(base, ranges, hidden_ref, cot_ref, pair_ref, mlp_ref, *outs):
    for n, (start, size) in enumerate(ranges):
        start = start - base
        hidden = hidden_ref[:, start : start + size]
        outs[2 * n][0] = mm(pair_ref[0], hidden, 0, 0).astype(bf16)
        outs[2 * n][1] = mm(pair_ref[1], hidden, 0, 0).astype(bf16)
        outs[2 * n + 1][0] = mm(mlp_ref[...], cot_ref[:, start : start + size], 0, 0).astype(bf16)


def qkv_gradient_kernel(ranges, hidden_ref, dproj_ref, dlogit_ref, *outs):
    outs = outs[-len(ranges) - 1 :]
    for (start, size), out in zip(ranges, outs[:-1]):
        hidden = hidden_ref[:, start : start + size]
        for i in range(3):
            out[i] = mm(hidden, dproj_ref[i], 0, 0).astype(bf16)
    outs[-1][...] = mm(dlogit_ref[...], hidden_ref[...], 0, 0)


def pair_gradient_kernel(ranges, hidden_ref, dgate_ref, normed_ref, mix_ref, *outs):
    inner = normed_ref.shape[1]
    for (start, size), out in zip(ranges, outs):
        out[0] = mm(hidden_ref[:, start : start + size], dgate_ref[...], 0, 0).astype(bf16)
        for n in range(2):
            at = start + n * size // 2
            mix = mix_ref[:, at : at + size // 2]
            out[1, n * inner : (n + 1) * inner] = mm(normed_ref[...], mix, 0, 0).astype(bf16)


def add_halves_kernel(*refs):
    one_ref, two_ref, low_ref, high_ref, one_out, two_out = refs[:4] + refs[-2:]
    one_out[...] = (one_ref[...].astype(f32) + high_ref[...].astype(f32)).astype(bf16)
    two_out[...] = (two_ref[...].astype(f32) + low_ref[...].astype(f32)).astype(bf16)


def add_last_kernel(*refs):
    own_ref, one_ref, two_ref, out_ref = refs[:3] + refs[-1:]
    out_ref[...] = own_ref[...].astype(f32) + one_ref[...].astype(f32) + two_ref[...].astype(f32)


def feed_kernel(layout, *refs):
    rows_ref, total_ref, cot_ref, gain_ref = refs[:4]
    count = len(layout)
    gateups, downs = (refs[4 + n * count : 4 + (n + 1) * count] for n in range(2))
    two_ref, hidden_ref, mlp_ref, pair_ref = refs[-4:]
    middle = rows_ref[0].astype(f32) + total_ref[0].astype(f32)
    hidden_ref[0] = (middle * norm_factor(middle) * gain_ref[...]).astype(bf16)
    gate, up, grad = None, None, None
    for (k, start, size, block), w_gateup, w_down in zip(layout, gateups, downs):
        lanes = slice(k * block + start, k * block + start + size)
        hidden = hidden_ref[0, :, lanes]
        terms = (
            mm(hidden, w_gateup[0], 1, 1),
            mm(hidden, w_gateup[1], 1, 1),
            mm(cot_ref[0, :, lanes], w_down[...], 1, 1),
        )
        if gate is None:
            gate, up, grad = terms
        else:
            gate, up, grad = gate + terms[0], up + terms[1], grad + terms[2]
    sig = jax.nn.sigmoid(gate)
    silu = gate * sig
    mlp_ref[0] = (silu * up).astype(bf16)
    first = (grad * up * sig * (1.0 + gate * (1.0 - sig))).astype(bf16)
    second = (grad * silu).astype(bf16)
    pair_ref[0, 0] = first
    pair_ref[1, 0] = second
    for (k, start, size, block), w_gateup in zip(layout, gateups):
        lanes = slice(k * block + start, k * block + start + size)
        two = mm(first, w_gateup[0]) + mm(second, w_gateup[1])
        two_ref[0, :, lanes] = two.astype(bf16)


def middle_back_kernel(layout, pieces, at_ref, *refs):
    two_ref, cot_ref, rows_ref, total_ref, gain_ref, rule_ref, gate_ref, head_gain_ref, qo_ref = refs[:9]
    outs = by_piece(at_ref, refs[9 : 9 + pieces])
    mix_ref, own_ref, mlpgain_ref, drule_ref, dgate_ref, dgain_ref, direct_ref, keep_ref = refs[-8:]
    middle = rows_ref[0].astype(f32) + total_ref[0].astype(f32)
    factor = norm_factor(middle)
    normal = middle * factor
    two = two_ref[0].astype(f32)
    mlpgain_ref[0] = jnp.sum(two * normal, 0, keepdims=True)
    scaled = two * gain_ref[...]
    mean = jnp.mean(scaled * normal, -1, keepdims=True)
    keep_ref[...] = cot_ref[0].astype(f32) + factor * (scaled - normal * mean)
    width = own_ref.shape[2]
    own_ref[0] = keep_ref[:, pl.ds(pl.multiple_of(at_ref[1], 128), width)]
    mix = keep_ref[...].astype(bf16)
    mix_ref[0] = mix
    grads = None
    for at, size, ref in out_columns(layout, outs):
        term = mm(mix_ref[0, :, at : at + size], ref[...], 1, 1)
        grads = term if grads is None else grads + term
    total = jnp.zeros((1, DK), f32)
    for h in range(direct_ref.shape[1]):
        grad = grads[:, head_slice(h)]
        out = rule_ref[0, :, head_slice(h)]
        gate = gate_ref[0, :, head_slice(h)]
        inv = norm_factor(out)
        n = out * inv
        sig = jax.nn.sigmoid(gate)
        silu = gate * sig
        gg = grad * head_gain_ref[...]
        dn = gg * silu
        drule = inv * (dn - n * jnp.mean(dn * n, -1, keepdims=True))
        drule_ref[0, :, head_slice(h)] = drule
        dgate = gg * n * sig * (1.0 + gate * (1.0 - sig))
        dgate_ref[0, :, head_slice(h)] = dgate.astype(bf16)
        total = total + jnp.sum(grad * n * silu, 0, keepdims=True)
        direct = mm(qo_ref[0, h, :, :DK], drule, 0, 0) * DK ** (-0.5)
        direct_ref[0, h] = direct.astype(bf16)
    dgain_ref[0] = total


def first_back_kernel(layout, pair_layout, count, place_ref, *refs):
    dproj_ref, dgate_ref, dlogit_ref, proj_ref, gate_ref, logit_ref, beta_ref, rows_ref, scale_ref = refs[:9]
    pieces = refs[9 : 9 + len(layout)]
    pairs = by_piece(place_ref, refs[9 + len(layout) : 9 + len(layout) + count])
    one_ref, rowsum_ref, gainsum_ref = refs[-3:]
    gates = {}
    for (k, start, size, block), ref in zip(pair_layout, pairs):
        gates[k] = ref
    for (k, start, size, block), piece in zip(layout, pieces):
        lanes = slice(k * block + start, k * block + start + size)
        grad = mm(dgate_ref[...], gate_part(gates[k])[start : start + size], 1, 1)
        for i in range(3):
            grad = grad + mm(dproj_ref[i], piece[i], 1, 1)
        for h in range(beta_ref.shape[0]):
            grad = grad + dlogit_ref[:, h : h + 1].astype(f32) * beta_ref[h : h + 1, lanes]
        at = pl.multiple_of((place_ref[0] ^ k) * block + start, 128)
        one_ref[:, pl.ds(at, size)] = grad.astype(bf16)
        gainsum_ref[:, lanes] = jnp.sum(
            grad * (rows_ref[:, lanes].astype(f32) * scale_ref[...]), 0, keepdims=True
        )
    total = dgate_ref[...].astype(f32) * gate_ref[...]
    for i in range(3):
        total = total + dproj_ref[i].astype(f32) * proj_ref[i].astype(f32)
    total = jnp.sum(total, -1, keepdims=True)
    logits = dlogit_ref[...].astype(f32) * logit_ref[...]
    rowsum_ref[...] = total + jnp.sum(logits, -1, keepdims=True)


def back_kernel(count, *refs):
    (
        proj_ref,
        before_ref,
        taps_ref,
        logit_ref,
        x_ref,
        wu_ref,
        state_ref,
        drule_ref,
    ) = refs[:8]
    dproj_ref, last_ref, first_ref, dtaps_ref, dlogit_ref = refs[-5:]
    others = refs[8 : 8 + 2 * count - 1]
    directs, nexts = others[:count], others[count:]
    heads = state_ref.shape[1]
    taps = taps_ref[...]
    length = proj_ref.shape[2]
    betas = jax.nn.sigmoid(logit_ref[0])
    r, c = places(length, length)
    strict = (r > c).astype(f32)
    full = (r >= c).astype(f32)
    zeros = jnp.zeros((PAD, DK), f32)
    for h in range(heads):
        parts, (qu, q_inv), (ku, k_inv), vu = rule_inputs(proj_ref, before_ref, taps, h)
        q, k, v = qu.astype(bf16), ku.astype(bf16), vu.astype(bf16)
        beta = betas[:, h : h + 1]
        leave = jnp.zeros((DK, DK), f32)
        for j in reversed(range(count)):
            here = directs[j][0, h].astype(f32)
            leave = here if j == count - 1 else mm(nexts[j][0, h], leave, 0, 0) + here
        state = state_ref[0, h]
        wu = wu_ref[0, h]
        u = wu[:, DK:] - mm(wu[:, :DK], state)
        resid = v.astype(f32) - mm(k, state)
        dout = drule_ref[0, :, head_slice(h)] * DK ** (-0.5)
        gram = mm(k, k, 1, 1)
        scores = mm(q, k, 1, 1) * full
        du = mm(scores, dout, 0, 0) + mm(k, leave)
        y = mm(x_ref[0, h], du, 0, 0)
        by = beta * y
        da = -(mm(y, u, 1, 1, 1) * strict)
        dbeta = jnp.sum(y * resid, -1, keepdims=True) + jnp.sum(da * gram, -1, keepdims=True)
        dgram = beta * da
        dscores = mm(dout, u, 1, 1, 1) * full
        dq = mm(dout, state, 1, 1, 1) + mm(dscores, k, 1, 0, 1)
        dk = (
            mm(dgram, k, 1, 0, 1)
            + mm(dgram, k, 0, 0, 1)
            + mm(dscores, q, 0, 0, 1)
            + mm(u, leave, 1, 1, 1)
            - mm(by, state, 1, 1, 1)
        )
        dlogit_ref[0, :, h : h + 1] = (dbeta * beta * (1.0 - beta)).astype(bf16)
        dq = (dq - qu * jnp.sum(qu * dq, -1, keepdims=True)) * q_inv
        dk = (dk - ku * jnp.sum(ku * dk, -1, keepdims=True)) * k_inv
        for i, dact in enumerate((dq, dk, by)):
            shifts, out, sig, _ = parts[i]
            dconv = dact * sig * (1.0 + out * (1.0 - sig))
            ext = jnp.concatenate([zeros, dconv, zeros], 0)
            total = None
            for j in range(KW):
                at = i * KW + j
                dtaps_ref[0, at : at + 1, head_slice(h)] = jnp.sum(
                    dconv * shifts[j], 0, keepdims=True
                )
                tap = taps[at : at + 1, head_slice(h)]
                term = tap * ext[KW - 1 - j : KW - 1 - j + PAD + length]
                total = term if total is None else total + term
            first_ref[i, 0, :, head_slice(h)] = total[:PAD]
            last_ref[i, 0, :, head_slice(h)] = total[length:]
            dproj_ref[i, 0, :, head_slice(h)] = total[PAD:].astype(bf16)


def call(kernel, ins, outs, steps, scalar=None, scratch=(), limit=VMEM, alias=None):
    def spec(shape, axis):
        if axis == "any":
            return pl.BlockSpec(memory_space=pl.ANY)
        block = tuple(1 if n == axis else size for n, size in enumerate(shape))
        where = lambda s, *_: tuple(s if n == axis else 0 for n in range(len(shape)))
        if axis is None:
            return pl.BlockSpec(block, where, pipeline_mode=pl.Buffered(1))
        return pl.BlockSpec(block, where)

    given = [] if scalar is None else [scalar]
    return pl.pallas_call(
        kernel,
        grid_spec=pltpu.PrefetchScalarGridSpec(
            num_scalar_prefetch=len(given),
            grid=(steps,),
            in_specs=[spec(a.shape, axis) for a, axis in ins],
            out_specs=[spec(o.shape, axis) for o, axis in outs],
            scratch_shapes=scratch,
        ),
        out_shape=[o for o, _ in outs],
        input_output_aliases=alias or {},
        compiler_params=pltpu.CompilerParams(vmem_limit_bytes=limit),
    )(*given, *[a for a, _ in ins])


def shape_of(shape, dtype):
    return jax.ShapeDtypeStruct(shape, dtype)


def shifted(array, axis, by):
    devices = lax.axis_size(axis)
    pairs = [(i, i + by) for i in range(devices) if 0 <= i + by < devices]
    return lax.ppermute(array, axis, pairs)


def after(values, *others):
    flat, tree = jax.tree.flatten(values)
    others = jax.tree.leaves(others)
    here = pl.BlockSpec(memory_space=pl.ANY)
    out = pl.pallas_call(
        lambda *refs: None,
        in_specs=[here] * (len(flat) + len(others)),
        out_specs=[here] * len(flat),
        out_shape=[shape_of(a.shape, a.dtype) for a in flat],
        input_output_aliases={n: n for n in range(len(flat))},
    )(*flat, *others)
    return jax.tree.unflatten(tree, out)


def copies(values):
    count = len(values)

    def kernel(*refs):
        for n in range(count):
            refs[n - count][...] = refs[n][...]

    outs = [(shape_of(a.shape, a.dtype), None) for a in values]
    return call(kernel, [(a, None) for a in values], outs, 1)


def swap(array, bits):
    return lax.ppermute(array, "dp", [(i, i ^ bits) for i in range(4)])


def first_hop(own):
    return swap(own, 1), swap(own, 2)


def halves_of(hop, axis):
    low, high = (jnp.split(part, 2, axis) for part in hop)
    return low[0], high[1]


def gathered_pieces(own, axis, hop=None, halves=None):
    hop = hop or first_hop(own)
    low, high = halves or halves_of(hop, axis)
    return [own, *hop, swap(low, 2), swap(high, 1)]


def far_hop(low, high):
    return swap(low, 1), swap(high, 2)


def near_sums(pieces, far_in, *others):
    own, one, two = pieces
    half = (1,) + far_in[0].shape[1:]
    along = 1 if half[1] < one.shape[1] else 2

    def spec(place):
        where = tuple(place if n == along else 0 for n in (1, 2))
        return pl.BlockSpec(half, lambda s: (s,) + where)

    first, second = spec(0), spec(1)
    here = pl.BlockSpec(memory_space=pl.ANY)
    one, two = pl.pallas_call(
        add_halves_kernel,
        grid=(one.shape[0],),
        in_specs=[second, first, first, first] + [here] * len(others),
        out_specs=[second, first],
        out_shape=[shape_of(a.shape, a.dtype) for a in (one, two)],
        input_output_aliases={0: 0, 1: 1},
        compiler_params=pltpu.CompilerParams(vmem_limit_bytes=VMEM),
    )(one, two, *far_in, *others)
    return own, one, two


def near_hop(pieces):
    own, one, two = pieces
    return own, swap(one, 1), swap(two, 2)


def sum_last(parts, *others):
    own = parts[0]
    ins = [(a, 0) for a in parts] + [(a, "any") for a in others]
    [total] = call(add_last_kernel, ins, [(shape_of(own.shape, f32), 0)], own.shape[0])
    return total


def pack(parts):
    return jnp.concatenate([p.reshape(-1) for p in parts])


def unpack(flat, shapes):
    out, at = [], 0
    for shape in shapes:
        size = 1
        for n in shape:
            size *= n
        out.append(flat[..., at : at + size].reshape(flat.shape[:-1] + tuple(shape)))
        at += size
    return out


def padded(flat, multiple=1024):
    return jnp.pad(flat, (0, -flat.shape[0] % multiple))


def body(
    tokens,
    out_grad,
    domain,
    group_weight,
    w_qkv,
    conv_weight,
    w_beta,
    w_outgate,
    head_gain,
    w_out,
    mixer_gain,
    mlp_gain,
    w_gateup,
    w_down,
):
    dp = lax.axis_size("dp")
    place = lax.axis_index("dp")
    seqs, block, local_width = tokens.shape
    count_rows = seqs * block
    heads = conv_weight.shape[2]
    inner = heads * DK
    column = lax.axis_index("mp") * local_width
    near_four = dp == 4

    def blocks_about(array, axis):
        if not near_four:
            return array
        size = array.shape[axis] // 4
        return jnp.concatenate(
            [lax.dynamic_slice_in_dim(array, (place ^ k) * size, size, axis) for k in range(4)],
            axis,
        )

    width = out_grad.shape[2]
    turn = place if near_four else jnp.int32(0)
    column_about = ((column // (width // 4)) ^ turn) * (width // 4) + column % (width // 4)

    def own(array):
        array = array.reshape(seqs, block, width)
        return lax.dynamic_slice_in_dim(array, column_about, local_width, 2)

    onehot = (domain[..., None] == jnp.arange(3, dtype=jnp.int32)).astype(f32)
    own_counts = jnp.sum(onehot, axis=(0, 1))
    high = jnp.floor(own_counts / 128.0)
    digits = jnp.concatenate([high, own_counts - 128.0 * high]).astype(bf16)
    small = [w_beta, conv_weight, head_gain, mixer_gain, mlp_gain, digits]
    packed = padded(pack(small))
    size = width // 4
    if near_four:
        qkv_hop = first_hop(w_qkv)
        qkv_halves = halves_of(qkv_hop, 1)
        qkv = gathered_pieces(w_qkv, 1, qkv_hop, qkv_halves)
        packed = after(packed, qkv_halves)
        gathered = jnp.stack([packed] + [swap(packed, bits) for bits in (1, 2, 3)])
        half = w_out.shape[1] // 2
        pair_own = jnp.stack(
            [w_outgate, jnp.concatenate([w_out[:, :half], w_out[:, half:]], 0)]
        )
        pair_layout = [(k, 0, size, size) for k in range(4)]
        layout = pair_layout[:3] + [(3, 0, size // 2, size), (3, size // 2, size // 2, size)]
    else:
        gathered = lax.all_gather(packed, "dp")
        qkv = [lax.all_gather(w_qkv, "dp", axis=1, tiled=True)]
        gate_pieces = [lax.all_gather(w_outgate, "dp", axis=0, tiled=True)]
        out_pieces = [lax.all_gather(w_out, "dp", axis=1, tiled=True)]
        layout = pair_layout = [(0, 0, width, width)]
    ranges = [(k * step + start, n) for k, start, n, step in layout]
    g_beta, g_conv, g_head, g_mix, g_mlp, g_digits = unpack(gathered, [a.shape for a in small])
    about_beta = g_beta.reshape(-1, heads)
    full_beta = blocks_about(about_beta, 0)
    full_conv = jnp.moveaxis(blocks_about(g_conv, 0), 0, 3).reshape(3 * KW, inner).astype(f32)
    gain_head = blocks_about(g_head, 0).reshape(1, DK).astype(f32)
    gain_one = blocks_about(g_mix.reshape(1, -1).astype(f32), 1)
    gain_two = g_mlp.reshape(1, -1).astype(f32)
    sums = jnp.sum(g_digits.astype(f32), 0)
    counts = 128.0 * sums[:3] + sums[3:]
    table = group_weight * (domain.shape[0] * domain.shape[1] * dp) / counts
    factor = jnp.sum(onehot * table, -1)[..., None]

    def flat(array):
        return array.reshape(array.shape[:-3] + (count_rows, array.shape[-1]))

    rows = lax.all_gather(tokens, "mp", axis=2, tiled=True)
    if near_four:
        gate_pieces = out_pieces = [lax.all_gather(after(pair_own, packed), "dp")]
    turn_one = turn.reshape(1)
    per_token = (seqs, block)
    square = (seqs, heads, DK, DK)
    hidden_one, proj, tail, logits, scale_one = call(
        partial(project_kernel, layout),
        [(rows, 0), (gain_one, None), (jnp.pad(full_beta, ((0, 0), (0, 128 - heads))), None)]
        + [(a, None) for a in qkv],
        [
            (shape_of(per_token + (width,), bf16), 0),
            (shape_of((3,) + per_token + (inner,), bf16), 1),
            (shape_of((3, seqs, HALO, inner), bf16), 1),
            (shape_of(per_token + (heads,), f32), 0),
            (shape_of(per_token + (1,), f32), 0),
        ],
        seqs,
        scalar=turn_one,
        scratch=[pltpu.VMEM((block, width), bf16)],
    )
    before = shifted(tail, "dp", 1)
    inverse, wu, qo, to = call(
        pre_kernel,
        [(proj, None), (before, None), (full_conv, None), (logits, None)],
        [
            (shape_of((seqs, heads, block, block), f32), None),
            (shape_of((seqs, heads, block, 2 * DK), f32), None),
            (shape_of((seqs, heads, block, 2 * DK), f32), None),
            (shape_of((seqs, heads, DK, 2 * DK), bf16), None),
        ],
        1,
    )
    near = [shifted(to, "dp", c) for c in range(1, dp)]
    [gates] = call(
        partial(gate_kernel, pair_layout),
        [(hidden_one, 0)] + [(a, None) for a in gate_pieces],
        [(shape_of(per_token + (inner,), f32), 0)],
        seqs,
        scalar=turn_one,
    )
    rows_about, cotangent = call(
        partial(prepare_kernel, layout),
        [(rows, 0), (out_grad, 0), (factor, 0)],
        [(shape_of(per_token + (width,), bf16), 0)] * 2,
        seqs,
        scalar=turn_one,
    )
    turned = jnp.swapaxes(w_gateup, 1, 2)
    feed_own = [turned, w_down]
    mixer_part, normed, rule, state = call(
        partial(mix_kernel, pair_layout, len(near)),
        [(a, 0) for a in near]
        + [(qo, 0), (gates, 0), (gain_head, None)]
        + [(a, None) for a in out_pieces]
        + [(cotangent, "any")],
        [
            (shape_of(per_token + (width,), bf16), 0),
            (shape_of(per_token + (inner,), bf16), 0),
            (shape_of(per_token + (inner,), f32), 0),
            (shape_of(square, f32), 0),
        ],
        seqs,
        scalar=turn_one,
    )
    total = lax.psum(mixer_part, "mp")
    nexts = [shifted(to[..., :DK], "dp", -c) for c in range(1, dp - 1)]
    if near_four:
        gateup, down = (gathered_pieces(a, a.ndim - 1) for a in after(copies(feed_own), mixer_part, nexts))
    else:
        gateup, down = (
            [lax.all_gather(a, "dp", axis=a.ndim - 1, tiled=True)] for a in feed_own
        )
    units = w_down.shape[0]
    two_part, hidden_two, hidden_mlp, grad_pair = call(
        partial(feed_kernel, layout),
        [(rows_about, 0), (total, 0), (cotangent, 0), (gain_two, None)]
        + [(a, None) for a in gateup + down],
        [
            (shape_of(per_token + (width,), bf16), 0),
            (shape_of(per_token + (width,), bf16), 0),
            (shape_of(per_token + (units,), bf16), 0),
            (shape_of((2,) + per_token + (units,), bf16), 1),
        ],
        seqs,
    )
    grad_two = lax.psum(two_part, "mp")

    def feed_gradients(some):
        outs = [(shape_of((m, units, n), bf16), None) for _, n in some for m in (2, 1)]
        base, span = some[0][0], sum(n for _, n in some)
        aligned = base % span == 0
        at = base // span if aligned else 0
        cols = pl.BlockSpec((count_rows, span if aligned else width), lambda s: (0, at))
        made = pl.pallas_call(
            partial(feed_gradient_kernel, base if aligned else 0, some),
            grid=(1,),
            in_specs=[
                cols,
                cols,
                pl.BlockSpec((2, count_rows, units), lambda s: (0, 0, 0)),
                pl.BlockSpec((count_rows, units), lambda s: (0, 0)),
            ],
            out_specs=[pl.BlockSpec(o.shape, lambda s: (0, 0, 0)) for o, _ in outs],
            out_shape=[o for o, _ in outs],
            compiler_params=pltpu.CompilerParams(vmem_limit_bytes=VMEM),
        )(flat(hidden_two), flat(cotangent), flat(grad_pair), flat(hidden_mlp))
        return made[::2], made[1::2]

    if near_four:
        feed_far = feed_gradients(ranges[3:])
        feed_in = [far_hop(*far) for far in feed_far]
        near_gateup, near_down = feed_gradients(ranges[:3])
        first_made = [(near_gateup[0], "any")]
        gateup_sums = near_hop(near_sums(near_gateup, feed_in[0], *feed_in[1]))
        down_sums = near_hop(near_sums(near_down, feed_in[1]))
        held = [(a, "any") for a in gateup_sums[1:]]
    else:
        [grad_gateup], [grad_down] = feed_gradients(ranges)
        held = first_made = []
    [down_part] = call(
        partial(down_kernel, layout),
        [(hidden_mlp, 0)] + [(a, None) for a in down] + first_made,
        [(shape_of(per_token + (width,), bf16), 0)],
        seqs,
        scalar=turn_one,
    )
    mlp_share = lax.psum_scatter(down_part, "mp", scatter_dimension=2, tiled=True)
    grad_mix, middle_own, mlpgain, drule, dgate, dgain, direct = call(
        partial(middle_back_kernel, pair_layout, len(out_pieces)),
        [
            (grad_two, 0),
            (cotangent, 0),
            (rows_about, 0),
            (total, 0),
            (gain_two, None),
            (rule, 0),
            (gates, 0),
            (gain_head, None),
            (qo, 0),
        ]
        + [(a, None) for a in out_pieces]
        + [(down_part, "any")]
        + held,
        [
            (shape_of(per_token + (width,), bf16), 0),
            (shape_of(per_token + (local_width,), f32), 0),
            (shape_of((seqs, 1, width), f32), 0),
            (shape_of(per_token + (inner,), f32), 0),
            (shape_of(per_token + (inner,), bf16), 0),
            (shape_of((seqs, 1, DK), f32), 0),
            (shape_of(square, bf16), 0),
        ],
        seqs,
        scalar=jnp.stack([turn, column_about]),
        scratch=[pltpu.VMEM((block, width), f32)],
    )
    directs = [shifted(direct, "dp", -c) for c in range(1, dp)]
    if near_four:
        pair_grads = call(
            partial(pair_gradient_kernel, [(k * size, size) for k in range(4)]),
            [(flat(a), None) for a in (hidden_one, dgate, normed, grad_mix)],
            [(shape_of((2, size, inner), bf16), None)] * 4,
            1,
        )
        pair_in = far_hop(*jnp.split(pair_grads[3], 2, 1))
        held = [(a, "any") for a in (pair_grads[3], *down_sums[1:])]
    else:
        grad_outgate = jnp.einsum(
            "td,tc->dc", flat(hidden_one), flat(dgate), preferred_element_type=f32
        )
        grad_outproj = jnp.einsum(
            "tc,td->cd", flat(normed), flat(grad_mix), preferred_element_type=f32
        )
        held = []
    dproj, last, first, dtaps, dlogits = call(
        partial(back_kernel, len(directs)),
        [
            (proj, 1),
            (before, 1),
            (full_conv, None),
            (logits, 0),
            (inverse, 0),
            (wu, 0),
            (state, 0),
            (drule, 0),
        ]
        + [(a, 0) for a in directs + nexts]
        + held,
        [
            (shape_of((3,) + per_token + (inner,), bf16), 1),
            (shape_of((3, seqs, PAD, inner), f32), 1),
            (shape_of((3, seqs, PAD, inner), f32), 1),
            (shape_of((seqs, 3 * KW, inner), f32), 0),
            (shape_of(per_token + (heads,), bf16), 0),
        ],
        seqs,
    )
    later = shifted(first, "dp", -1)
    dproj = lax.dynamic_update_slice(dproj, (last + later).astype(bf16), (0, 0, block - PAD, 0))
    one_low, row_part, gain_part = call(
        partial(first_back_kernel, layout, pair_layout, len(gate_pieces)),
        [
            (flat(dproj), None),
            (flat(dgate), None),
            (flat(dlogits), None),
            (flat(proj), None),
            (flat(gates), None),
            (flat(logits), None),
            (about_beta.T.astype(f32), None),
            (flat(rows_about), None),
            (flat(scale_one), None),
        ]
        + [(a, None) for a in qkv + gate_pieces]
        + [(mlp_share, "any")]
        + ([(a, "any") for a in pair_in] if near_four else []),
        [
            (shape_of((count_rows, width), bf16), None),
            (shape_of((count_rows, 1), f32), None),
            (shape_of((1, width), f32), None),
        ],
        1,
        scalar=turn_one,
    )
    one_share = lax.psum_scatter(
        one_low.reshape(seqs, block, width), "mp", scatter_dimension=2, tiled=True
    ).astype(f32)
    made = call(
        partial(qkv_gradient_kernel, ranges),
        [(flat(hidden_one), None), (flat(dproj), None), (flat(dlogits), None), (row_part, "any")],
        [(shape_of((3, n, inner), bf16), None) for _, n in ranges]
        + [(shape_of((heads, width), f32), None)],
        1,
    )

    def pieces(array, axis, about):
        shape = array.shape
        cut = array.reshape(shape[:axis] + (dp, shape[axis] // dp) + shape[axis + 1 :])
        cut = jnp.moveaxis(cut, axis, 0).reshape(dp, -1)
        return blocks_about(cut, 0) if about else cut

    smalls = jnp.concatenate(
        [
            pieces(jnp.sum(dtaps, 0).reshape(3, KW, heads, DK), 3, True),
            pieces(made[-1].T, 0, False),
            pieces(jnp.sum(dgain, (0, 1)), 0, True),
            pieces(gain_part[0], 0, False),
            pieces(jnp.sum(mlpgain, (0, 1)), 0, False),
        ],
        1,
    )
    if near_four:
        qkv_in = far_hop(made[3], made[4])
        own_qkv, *near_qkv = near_sums(made[:3], qkv_in)
        mine = smalls[0]
        for bits in (1, 2, 3):
            mine = mine + swap(padded(smalls[bits].astype(bf16)), bits)[: mine.shape[0]].astype(f32)
        late = near_qkv[0]
        sum_qkv = sum_last(near_hop((own_qkv, *near_qkv)))
        sum_gateup = jnp.swapaxes(sum_last(gateup_sums, late), 1, 2)
        sum_down = sum_last(down_sums, late)[0]
        pair_near = near_sums(pair_grads[:3], pair_in, *near_qkv)[1:]
        sum_pair = sum_last(near_hop((pair_grads[0], *pair_near)), late)
        sum_outgate = sum_pair[0]
        sum_out = jnp.concatenate(jnp.split(sum_pair[1], 2, 0), 1)
    else:
        gathered = lax.all_gather(smalls.astype(bf16), "dp")
        mine = jnp.sum(
            lax.dynamic_index_in_dim(gathered, place, 1, keepdims=False).astype(f32), 0
        )

        def scattered(array, axis):
            return lax.psum_scatter(array, "dp", scatter_dimension=axis, tiled=True).astype(f32)

        sum_qkv = scattered(made[0], 1)
        sum_outgate = scattered(grad_outgate.astype(bf16), 0)
        sum_out = scattered(grad_outproj.astype(bf16), 1)
        sum_gateup = jnp.swapaxes(scattered(grad_gateup, 2), 1, 2)
        sum_down = scattered(grad_down[0], 1)
    sum_conv, sum_beta, sum_head, sum_mix, sum_mlp = unpack(
        mine,
        [conv_weight.shape, w_beta.shape, head_gain.shape, mixer_gain.shape, mlp_gain.shape],
    )
    rest = [row_part[:, 0], sum_head, sum_mix]
    packed_rest = padded(pack(rest), 128)
    if near_four:
        packed_rest = after(packed_rest, near_qkv)
    everyone = lax.optimization_barrier(lax.all_gather(packed_rest, "mp"))
    row_sum, sum_head, sum_mix = unpack(jnp.sum(everyone, 0), [a.shape for a in rest])

    own_tokens = tokens.astype(f32)
    mixed_out = (own_tokens + own(total).astype(f32) + mlp_share.astype(f32)).astype(bf16)
    row_mean = (row_sum / width).reshape(seqs, block, 1)
    gain_own = lax.dynamic_slice_in_dim(gain_one, column, local_width, 1)
    tokens_grad = middle_own + scale_one * (
        one_share * gain_own - own_tokens * scale_one * row_mean
    )
    return (
        mixed_out,
        tokens_grad.astype(bf16),
        sum_qkv,
        sum_conv,
        sum_beta,
        sum_outgate,
        sum_head,
        sum_out,
        sum_mix,
        sum_mlp,
        sum_gateup,
        sum_down,
    )


def solution(mesh):
    return jax.shard_map(
        body,
        mesh=mesh,
        in_specs=(
            P(None, "dp", "mp"),
            P(None, "dp", None),
            P(None, "dp"),
            P(),
            P(None, "dp", "mp"),
            P(None, None, "mp", "dp"),
            P("dp", "mp"),
            P("dp", "mp"),
            P("dp"),
            P("mp", "dp"),
            P("dp"),
            P("dp"),
            P(None, "dp", "mp"),
            P("mp", "dp"),
        ),
        out_specs=(
            P(None, "dp", "mp"),
            P(None, "dp", "mp"),
            P(None, "dp", "mp"),
            P(None, None, "mp", "dp"),
            P("dp", "mp"),
            P("dp", "mp"),
            P("dp"),
            P("mp", "dp"),
            P("dp"),
            P("dp"),
            P(None, "dp", "mp"),
            P("mp", "dp"),
        ),
        check_vma=False,
    )
```

```python
from functools import partial

import jax
import jax.numpy as jnp
from jax import lax
from jax.experimental import pallas as pl
from jax.experimental.pallas import tpu as pltpu
from jax.sharding import PartitionSpec as P

DK = 128
KW = 4
PAD = 8
HALO = 16
CHUNK = 16
VMEM = 58 * 2**20

eps_norm = 1e-06
eps_unit = 1e-06

f32 = jnp.float32
bf16 = jnp.bfloat16


def split(v):
    if v.dtype == bf16:
        return v, None
    high = v.astype(bf16)
    return high, (v - high.astype(f32)).astype(bf16)


def mm(a, b, ca=1, cb=0, passes=3):
    def one(x, y):
        return lax.dot_general(x, y, (((ca,), (cb,)), ((), ())), preferred_element_type=f32)

    if passes == 1:
        return one(a.astype(bf16), b.astype(bf16))
    (ah, al), (bh, bl) = split(a), split(b)
    out = one(ah, bh)
    if bl is not None:
        out = out + one(ah, bl)
    if al is not None:
        out = out + one(al, bh)
    return out


def places(rows, cols):
    return (
        lax.broadcasted_iota(jnp.int32, (rows, cols), 0),
        lax.broadcasted_iota(jnp.int32, (rows, cols), 1),
    )


def unit_lower_inverses(blocks):
    size = blocks[0].shape[0]
    if size > 128:
        half = size // 2
        parts = unit_lower_inverses(
            [a[:half, :half] for a in blocks] + [a[half:, half:] for a in blocks]
        )
        firsts, seconds = parts[: len(blocks)], parts[len(blocks) :]
        inner = [mm(a[half:, :half], x) for a, x in zip(blocks, firsts)]
        lower = [-mm(x, y) for x, y in zip(seconds, inner)]
        zero = jnp.zeros((half, half), f32)
        return [
            jnp.concatenate(
                [jnp.concatenate([x, zero], 1), jnp.concatenate([y, z], 1)], 0
            )
            for x, y, z in zip(firsts, lower, seconds)
        ]
    rows, cols = places(size, size)
    eye = (rows == cols).astype(f32)
    level = 0
    inverses = None
    while (1 << level) < size:
        mask = (
            ((rows >> (level + 1)) == (cols >> (level + 1)))
            & (((rows >> level) & 1) == 1)
            & (((cols >> level) & 1) == 0)
        ).astype(f32)
        lows = [a * mask for a in blocks]
        if level == 0:
            inverses = [eye - low for low in lows]
        else:
            inner = [mm(low, x) for low, x in zip(lows, inverses)]
            inverses = [x - mm(x, y) for x, y in zip(inverses, inner)]
        level += 1
    return inverses


def head_slice(h):
    return slice(h * DK, (h + 1) * DK)


def convolve(proj_ref, before_ref, taps, i, h):
    own = proj_ref[i, 0, :, head_slice(h)].astype(f32)
    length = own.shape[0]
    ext = jnp.concatenate([before_ref[i, 0, :, head_slice(h)].astype(f32), own], 0)
    shifts = [ext[HALO - KW + 1 + j : HALO - KW + 1 + j + length] for j in range(KW)]
    out = None
    for j in range(KW):
        tap = taps[i * KW + j : i * KW + j + 1, head_slice(h)]
        out = tap * shifts[j] if out is None else out + tap * shifts[j]
    sig = jax.nn.sigmoid(out)
    return shifts, out, sig, out * sig


def unit(acts):
    inv = lax.rsqrt(jnp.sum(acts * acts, -1, keepdims=True) + eps_unit)
    return acts * inv, inv


def rule_inputs(proj_ref, before_ref, taps, h):
    parts = [convolve(proj_ref, before_ref, taps, i, h) for i in range(3)]
    q, q_inv = unit(parts[0][3])
    k, k_inv = unit(parts[1][3])
    return parts, (q, q_inv), (k, k_inv), parts[2][3]


def norm_factor(values):
    return lax.rsqrt(jnp.mean(values * values, -1, keepdims=True) + eps_norm)


def project_kernel(layout, *refs):
    place_ref, rows_ref, gain_ref, beta_ref = refs[:4]
    pieces = refs[4 : 4 + len(layout)]
    hidden_ref, proj_ref, tail_ref, logit_ref, scale_ref, keep_ref = refs[4 + len(layout) :]
    rows = rows_ref[0].astype(f32)
    scale = norm_factor(rows)
    scale_ref[0] = scale
    keep_ref[...] = (rows * scale * gain_ref[...]).astype(bf16)
    logits = mm(keep_ref[...], beta_ref[...])
    logit_ref[0] = logits[:, : logit_ref.shape[2]]
    sums = [None] * 3
    for (k, start, size, block), piece in zip(layout, pieces):
        at = pl.multiple_of((place_ref[0] ^ k) * block + start, 128)
        part = keep_ref[:, pl.ds(at, size)]
        hidden_ref[0, :, k * block + start : k * block + start + size] = part
        for i in range(3):
            term = mm(part, piece[i])
            sums[i] = term if sums[i] is None else sums[i] + term
    for i in range(3):
        low = sums[i].astype(bf16)
        proj_ref[i, 0] = low
        tail_ref[i, 0] = low[low.shape[0] - HALO :]


def pre_kernel(proj_ref, before_ref, taps_ref, logit_ref, x_ref, wu_ref, qo_ref, to_ref):
    seqs, heads = to_ref.shape[:2]
    taps = taps_ref[...]
    length = proj_ref.shape[2]
    r, c = places(length, length)
    strict = (r > c).astype(f32)
    full = (r >= c).astype(f32)
    saved, blocks = [], []
    for s in range(seqs):
        betas = jax.nn.sigmoid(logit_ref[s])
        rows, before = proj_ref.at[:, s : s + 1], before_ref.at[:, s : s + 1]
        for h in range(heads):
            _, (q, _), (k, _), v = rule_inputs(rows, before, taps, h)
            q, k, v = q.astype(bf16), k.astype(bf16), v.astype(bf16)
            beta = betas[:, h : h + 1]
            blocks.append(beta * mm(k, k, 1, 1) * strict)
            saved.append((s, h, q, k, v, beta))
    inverses = unit_lower_inverses(blocks)
    r, c = places(DK, DK)
    eye = (r == c).astype(f32)
    for (s, h, q, k, v, beta), x in zip(saved, inverses):
        x_ref[s, h] = x
        kv = jnp.concatenate([k.astype(f32), v.astype(f32)], 1) * beta
        wu = mm(x, kv)
        wu_ref[s, h] = wu
        scores = mm(q, k, 1, 1) * full
        pwu = mm(scores, wu)
        qo_ref[s, h, :, :DK] = q.astype(f32) - pwu[:, :DK]
        qo_ref[s, h, :, DK:] = pwu[:, DK:]
        kwu = mm(k, wu, 0, 0)
        to_ref[s, h, :, :DK] = (eye - kwu[:, :DK]).astype(bf16)
        to_ref[s, h, :, DK:] = kwu[:, DK:].astype(bf16)


def by_piece(place_ref, refs):
    if len(refs) > 1 or len(refs[0].shape) < 4:
        return refs
    return [refs[0].at[place_ref[0] ^ k] for k in range(4)]


def gate_part(ref):
    return ref.at[0] if len(ref.shape) == 3 else ref


def out_columns(layout, refs):
    for (k, start, size, block), ref in zip(layout, refs):
        at, half = k * block + start, size // 2
        if len(ref.shape) == 2:
            yield at, size, ref
            continue
        inner = ref.shape[1] // 2
        yield at, half, ref.at[1, :inner]
        yield at + half, half, ref.at[1, inner:]


def mix_kernel(layout, count, pieces, place_ref, *refs):
    near, rest = refs[:count], refs[count:]
    qo_ref, hidden_ref, gain_ref = rest[:3]
    gate_pieces = by_piece(place_ref, rest[3 : 3 + pieces])
    outs = by_piece(place_ref, rest[3 + pieces : 3 + 2 * pieces])
    part_ref, normed_ref, rule_ref, state_ref, gate_ref = rest[-5:]
    gates = None
    for (k, start, size, block), ref in zip(layout, gate_pieces):
        at = k * block + start
        term = mm(hidden_ref[0, :, at : at + size], gate_part(ref)[...])
        gates = term if gates is None else gates + term
    gate_ref[0] = gates
    heads = state_ref.shape[1]
    for h in range(heads):
        state = near[-1][0, h, :, DK:].astype(f32)
        for ref in reversed(near[:-1]):
            state = mm(ref[0, h, :, :DK], state) + ref[0, h, :, DK:].astype(f32)
        state_ref[0, h] = state
        qo = qo_ref[0, h]
        out = (mm(qo[:, :DK], state) + qo[:, DK:]) * DK ** (-0.5)
        rule_ref[0, :, head_slice(h)] = out
        gate = gate_ref[0, :, head_slice(h)]
        normed = out * norm_factor(out) * gain_ref[...] * (gate * jax.nn.sigmoid(gate))
        normed_ref[0, :, head_slice(h)] = normed.astype(bf16)
    for at, size, ref in out_columns(layout, outs):
        part_ref[0, :, at : at + size] = mm(normed_ref[0], ref[...]).astype(bf16)


def prepare_kernel(layout, place_ref, rows_ref, grad_ref, factor_ref, about_ref, cot_ref):
    for k, start, size, block in layout:
        at = pl.multiple_of((place_ref[0] ^ k) * block + start, 128)
        to = slice(k * block + start, k * block + start + size)
        about_ref[0, :, to] = rows_ref[0, :, pl.ds(at, size)]
        grad = grad_ref[0, :, pl.ds(at, size)].astype(f32) * factor_ref[0]
        cot_ref[0, :, to] = grad.astype(bf16)


def down_kernel(layout, place_ref, mlp_ref, *refs):
    part_ref = refs[-1]
    for (k, start, size, block), ref in zip(layout, refs):
        at = pl.multiple_of((place_ref[0] ^ k) * block + start, 128)
        part_ref[0, :, pl.ds(at, size)] = mm(mlp_ref[0], ref[...]).astype(bf16)


def feed_gradient_kernel(base, ranges, hidden_ref, cot_ref, pair_ref, mlp_ref, *outs):
    outs = outs[-2 * len(ranges) :]
    for n, (start, size) in enumerate(ranges):
        start = start - base
        hidden = hidden_ref[:, start : start + size]
        outs[2 * n][0] = mm(pair_ref[0], hidden, 0, 0).astype(bf16)
        outs[2 * n][1] = mm(pair_ref[1], hidden, 0, 0).astype(bf16)
        outs[2 * n + 1][0] = mm(mlp_ref[...], cot_ref[:, start : start + size], 0, 0).astype(bf16)


def qkv_gradient_kernel(ranges, hidden_ref, dproj_ref, dlogit_ref, *outs):
    outs = outs[-len(ranges) - 1 :]
    for (start, size), out in zip(ranges, outs[:-1]):
        hidden = hidden_ref[:, start : start + size]
        for i in range(3):
            out[i] = mm(hidden, dproj_ref[i], 0, 0).astype(bf16)
    outs[-1][...] = mm(dlogit_ref[...], hidden_ref[...], 0, 0)


def pair_gradient_kernel(ranges, hidden_ref, dgate_ref, normed_ref, mix_ref, *outs):
    inner = normed_ref.shape[1]
    for (start, size), out in zip(ranges, outs):
        out[0] = mm(hidden_ref[:, start : start + size], dgate_ref[...], 0, 0).astype(bf16)
        for n in range(2):
            at = start + n * size // 2
            mix = mix_ref[:, at : at + size // 2]
            out[1, n * inner : (n + 1) * inner] = mm(normed_ref[...], mix, 0, 0).astype(bf16)


def add_halves_kernel(*refs):
    one_ref, two_ref, low_ref, high_ref, one_out, two_out = refs[:4] + refs[-2:]
    one_out[...] = (one_ref[...].astype(f32) + high_ref[...].astype(f32)).astype(bf16)
    two_out[...] = (two_ref[...].astype(f32) + low_ref[...].astype(f32)).astype(bf16)


def add_small_kernel(*refs):
    refs[-1][...] = sum(ref[...].astype(f32) for ref in refs[:-1])


def add_last_kernel(*refs):
    own_ref, one_ref, two_ref, out_ref = refs[:3] + refs[-1:]
    out_ref[...] = own_ref[...].astype(f32) + one_ref[...].astype(f32) + two_ref[...].astype(f32)


def feed_kernel(layout, *refs):
    rows_ref, total_ref, cot_ref, gain_ref = refs[:4]
    count = len(layout)
    gateups, downs = (refs[4 + n * count : 4 + (n + 1) * count] for n in range(2))
    two_ref, hidden_ref, mlp_ref, pair_ref, gates_ref, ups_ref, grads_ref = refs[-7:]
    chunks = rows_ref.shape[1] // CHUNK

    def norm(c, carry):
        at = pl.ds(pl.multiple_of(c * CHUNK, CHUNK), CHUNK)
        middle = rows_ref[0, at, :].astype(f32) + total_ref[0, at, :].astype(f32)
        hidden_ref[0, at, :] = (middle * norm_factor(middle) * gain_ref[...]).astype(bf16)
        return carry

    lax.fori_loop(0, chunks, norm, 0)
    gate, up, grad = None, None, None
    for (k, start, size, block), w_gateup, w_down in zip(layout, gateups, downs):
        lanes = slice(k * block + start, k * block + start + size)
        hidden = hidden_ref[0, :, lanes]
        terms = (
            mm(hidden, w_gateup[0], 1, 1),
            mm(hidden, w_gateup[1], 1, 1),
            mm(cot_ref[0, :, lanes], w_down[...], 1, 1),
        )
        if gate is None:
            gate, up, grad = terms
        else:
            gate, up, grad = gate + terms[0], up + terms[1], grad + terms[2]
    gates_ref[...], ups_ref[...], grads_ref[...] = gate, up, grad

    def gated(c, carry):
        at = pl.ds(pl.multiple_of(c * CHUNK, CHUNK), CHUNK)
        gate, up, grad = gates_ref[at, :], ups_ref[at, :], grads_ref[at, :]
        sig = jax.nn.sigmoid(gate)
        silu = gate * sig
        mlp_ref[0, at, :] = (silu * up).astype(bf16)
        pair_ref[0, 0, at, :] = (grad * up * (sig + silu * (1.0 - sig))).astype(bf16)
        pair_ref[1, 0, at, :] = (grad * silu).astype(bf16)
        return carry

    lax.fori_loop(0, chunks, gated, 0)
    first, second = pair_ref[0, 0], pair_ref[1, 0]
    for (k, start, size, block), w_gateup in zip(layout, gateups):
        lanes = slice(k * block + start, k * block + start + size)
        two = mm(first, w_gateup[0]) + mm(second, w_gateup[1])
        two_ref[0, :, lanes] = two.astype(bf16)


def middle_back_kernel(layout, pieces, at_ref, *refs):
    two_ref, cot_ref, rows_ref, total_ref, gain_ref, rule_ref, gate_ref, head_gain_ref, qo_ref = refs[:9]
    outs = by_piece(at_ref, refs[9 : 9 + pieces])
    mix_ref, own_ref, mlpgain_ref, drule_ref, dgate_ref, dgain_ref, direct_ref, keep_ref, sum_ref = refs[-9:]
    sum_ref[...] = jnp.zeros_like(sum_ref)
    full = rows_ref.shape[2]

    def chunk(c, carry):
        at = pl.ds(pl.multiple_of(c * CHUNK, CHUNK), CHUNK)
        middle = rows_ref[0, at, :].astype(f32) + total_ref[0, at, :].astype(f32)
        two = two_ref[0, at, :].astype(f32)
        factor = norm_factor(middle)
        normal = middle * factor
        sum_ref[...] += two * normal
        scaled = two * gain_ref[...]
        mean = jnp.sum(scaled * normal, -1, keepdims=True) * (1.0 / full)
        keep = cot_ref[0, at, :].astype(f32) + factor * (scaled - normal * mean)
        keep_ref[at, :] = keep
        mix_ref[0, at, :] = keep.astype(bf16)
        return carry

    lax.fori_loop(0, rows_ref.shape[1] // CHUNK, chunk, 0)
    mlpgain_ref[0] = jnp.sum(sum_ref[...], 0, keepdims=True)
    width = own_ref.shape[2]
    own_ref[0] = keep_ref[:, pl.ds(pl.multiple_of(at_ref[1], 128), width)]
    grads = None
    for at, size, ref in out_columns(layout, outs):
        term = mm(mix_ref[0, :, at : at + size], ref[...], 1, 1)
        grads = term if grads is None else grads + term
    total = jnp.zeros((1, DK), f32)
    for h in range(direct_ref.shape[1]):
        grad = grads[:, head_slice(h)]
        out = rule_ref[0, :, head_slice(h)]
        gate = gate_ref[0, :, head_slice(h)]
        inv = norm_factor(out)
        n = out * inv
        sig = jax.nn.sigmoid(gate)
        silu = gate * sig
        gg = grad * head_gain_ref[...]
        dn = gg * silu
        drule = inv * (dn - n * jnp.mean(dn * n, -1, keepdims=True))
        drule_ref[0, :, head_slice(h)] = drule
        dgate = gg * n * sig * (1.0 + gate * (1.0 - sig))
        dgate_ref[0, :, head_slice(h)] = dgate.astype(bf16)
        total = total + jnp.sum(grad * n * silu, 0, keepdims=True)
        direct = mm(qo_ref[0, h, :, :DK], drule, 0, 0) * DK ** (-0.5)
        direct_ref[0, h] = direct.astype(bf16)
    dgain_ref[0] = total


def first_back_kernel(layout, pair_layout, count, place_ref, *refs):
    dproj_ref, dgate_ref, dlogit_ref, proj_ref, gate_ref, logit_ref, beta_ref, rows_ref, scale_ref = refs[:9]
    pieces = refs[9 : 9 + len(layout)]
    pairs = by_piece(place_ref, refs[9 + len(layout) : 9 + len(layout) + count])
    one_ref, rowsum_ref, gainsum_ref = refs[-3:]
    gates = {}
    for (k, start, size, block), ref in zip(pair_layout, pairs):
        gates[k] = ref
    for (k, start, size, block), piece in zip(layout, pieces):
        lanes = slice(k * block + start, k * block + start + size)
        grad = mm(dgate_ref[...], gate_part(gates[k])[start : start + size], 1, 1)
        for i in range(3):
            grad = grad + mm(dproj_ref[i], piece[i], 1, 1)
        for h in range(beta_ref.shape[0]):
            grad = grad + dlogit_ref[:, h : h + 1].astype(f32) * beta_ref[h : h + 1, lanes]
        at = pl.multiple_of((place_ref[0] ^ k) * block + start, 128)
        one_ref[:, pl.ds(at, size)] = grad.astype(bf16)
        gainsum_ref[:, lanes] = jnp.sum(
            grad * (rows_ref[:, lanes].astype(f32) * scale_ref[...]), 0, keepdims=True
        )
    total = dgate_ref[...].astype(f32) * gate_ref[...]
    for i in range(3):
        total = total + dproj_ref[i].astype(f32) * proj_ref[i].astype(f32)
    total = jnp.sum(total, -1, keepdims=True)
    logits = dlogit_ref[...].astype(f32) * logit_ref[...]
    rowsum_ref[...] = total + jnp.sum(logits, -1, keepdims=True)


def back_kernel(count, *refs):
    (
        proj_ref,
        before_ref,
        taps_ref,
        logit_ref,
        x_ref,
        wu_ref,
        state_ref,
        drule_ref,
    ) = refs[:8]
    dproj_ref, last_ref, first_ref, dtaps_ref, dlogit_ref = refs[-5:]
    others = refs[8 : 8 + 2 * count - 1]
    directs, nexts = others[:count], others[count:]
    heads = state_ref.shape[1]
    taps = taps_ref[...]
    length = proj_ref.shape[2]
    betas = jax.nn.sigmoid(logit_ref[0])
    r, c = places(length, length)
    strict = (r > c).astype(f32)
    full = (r >= c).astype(f32)
    zeros = jnp.zeros((PAD, DK), f32)
    for h in range(heads):
        parts, (qu, q_inv), (ku, k_inv), vu = rule_inputs(proj_ref, before_ref, taps, h)
        q, k, v = qu.astype(bf16), ku.astype(bf16), vu.astype(bf16)
        beta = betas[:, h : h + 1]
        leave = jnp.zeros((DK, DK), f32)
        for j in reversed(range(count)):
            here = directs[j][0, h].astype(f32)
            leave = here if j == count - 1 else mm(nexts[j][0, h], leave, 0, 0) + here
        state = state_ref[0, h]
        wu = wu_ref[0, h]
        u = wu[:, DK:] - mm(wu[:, :DK], state)
        resid = v.astype(f32) - mm(k, state)
        dout = drule_ref[0, :, head_slice(h)] * DK ** (-0.5)
        gram = mm(k, k, 1, 1)
        scores = mm(q, k, 1, 1) * full
        du = mm(scores, dout, 0, 0) + mm(k, leave)
        y = mm(x_ref[0, h], du, 0, 0)
        by = beta * y
        da = -(mm(y, u, 1, 1, 1) * strict)
        dbeta = jnp.sum(y * resid, -1, keepdims=True) + jnp.sum(da * gram, -1, keepdims=True)
        dgram = beta * da
        dscores = mm(dout, u, 1, 1, 1) * full
        dq = mm(dout, state, 1, 1, 1) + mm(dscores, k, 1, 0, 1)
        dk = (
            mm(dgram, k, 1, 0, 1)
            + mm(dgram, k, 0, 0, 1)
            + mm(dscores, q, 0, 0, 1)
            + mm(u, leave, 1, 1, 1)
            - mm(by, state, 1, 1, 1)
        )
        dlogit_ref[0, :, h : h + 1] = (dbeta * beta * (1.0 - beta)).astype(bf16)
        dq = (dq - qu * jnp.sum(qu * dq, -1, keepdims=True)) * q_inv
        dk = (dk - ku * jnp.sum(ku * dk, -1, keepdims=True)) * k_inv
        for i, dact in enumerate((dq, dk, by)):
            shifts, out, sig, _ = parts[i]
            dconv = dact * sig * (1.0 + out * (1.0 - sig))
            ext = jnp.concatenate([zeros, dconv, zeros], 0)
            total = None
            for j in range(KW):
                at = i * KW + j
                dtaps_ref[0, at : at + 1, head_slice(h)] = jnp.sum(
                    dconv * shifts[j], 0, keepdims=True
                )
                tap = taps[at : at + 1, head_slice(h)]
                term = tap * ext[KW - 1 - j : KW - 1 - j + PAD + length]
                total = term if total is None else total + term
            first_ref[i, 0, :, head_slice(h)] = total[:PAD]
            last_ref[i, 0, :, head_slice(h)] = total[length:]
            dproj_ref[i, 0, :, head_slice(h)] = total[PAD:].astype(bf16)


def call(kernel, ins, outs, steps, scalar=None, scratch=(), limit=VMEM, alias=None):
    def spec(shape, axis):
        if axis == "any":
            return pl.BlockSpec(memory_space=pl.ANY)
        block = tuple(1 if n == axis else size for n, size in enumerate(shape))
        where = lambda s, *_: tuple(s if n == axis else 0 for n in range(len(shape)))
        if axis is None:
            return pl.BlockSpec(block, where, pipeline_mode=pl.Buffered(1))
        return pl.BlockSpec(block, where)

    given = [] if scalar is None else [scalar]
    return pl.pallas_call(
        kernel,
        grid_spec=pltpu.PrefetchScalarGridSpec(
            num_scalar_prefetch=len(given),
            grid=(steps,),
            in_specs=[spec(a.shape, axis) for a, axis in ins],
            out_specs=[spec(o.shape, axis) for o, axis in outs],
            scratch_shapes=scratch,
        ),
        out_shape=[o for o, _ in outs],
        input_output_aliases=alias or {},
        compiler_params=pltpu.CompilerParams(vmem_limit_bytes=limit),
    )(*given, *[a for a, _ in ins])


def shape_of(shape, dtype):
    return jax.ShapeDtypeStruct(shape, dtype)


def shifted(array, axis, by):
    devices = lax.axis_size(axis)
    pairs = [(i, i + by) for i in range(devices) if 0 <= i + by < devices]
    return lax.ppermute(array, axis, pairs)


def after(values, *others):
    flat, tree = jax.tree.flatten(values)
    others = jax.tree.leaves(others)
    here = pl.BlockSpec(memory_space=pl.ANY)
    out = pl.pallas_call(
        lambda *refs: None,
        in_specs=[here] * (len(flat) + len(others)),
        out_specs=[here] * len(flat),
        out_shape=[shape_of(a.shape, a.dtype) for a in flat],
        input_output_aliases={n: n for n in range(len(flat))},
    )(*flat, *others)
    return jax.tree.unflatten(tree, out)


def copies(values):
    count = len(values)

    def kernel(*refs):
        for n in range(count):
            refs[n - count][...] = refs[n][...]

    outs = [(shape_of(a.shape, a.dtype), None) for a in values]
    return call(kernel, [(a, None) for a in values], outs, 1)


def swap(array, bits):
    return lax.ppermute(array, "dp", [(i, i ^ bits) for i in range(4)])


def first_hop(own):
    return swap(own, 1), swap(own, 2)


def halves_of(hop, axis):
    low, high = (jnp.split(part, 2, axis) for part in hop)
    return low[0], high[1]


def gathered_pieces(own, axis, hop=None, halves=None):
    hop = hop or first_hop(own)
    low, high = halves or halves_of(hop, axis)
    return [own, *hop, swap(low, 2), swap(high, 1)]


def far_hop(low, high):
    return swap(low, 1), swap(high, 2)


def near_sums(pieces, far_in, *others):
    own, one, two = pieces
    half = (1,) + far_in[0].shape[1:]
    along = 1 if half[1] < one.shape[1] else 2

    def spec(place):
        where = tuple(place if n == along else 0 for n in (1, 2))
        return pl.BlockSpec(half, lambda s: (s,) + where)

    first, second = spec(0), spec(1)
    here = pl.BlockSpec(memory_space=pl.ANY)
    one, two = pl.pallas_call(
        add_halves_kernel,
        grid=(one.shape[0],),
        in_specs=[second, first, first, first] + [here] * len(others),
        out_specs=[second, first],
        out_shape=[shape_of(a.shape, a.dtype) for a in (one, two)],
        input_output_aliases={0: 0, 1: 1},
        compiler_params=pltpu.CompilerParams(vmem_limit_bytes=VMEM),
    )(one, two, *far_in, *others)
    return own, one, two


def near_hop(pieces):
    own, one, two = pieces
    return own, swap(one, 1), swap(two, 2)


def add_pair_kernel(own_ref, one_ref, two_ref, *refs):
    gate_ref, out_ref = refs[-2:]
    inner = out_ref.shape[0]

    def added(i, rows):
        parts = (ref[i, rows].astype(f32) for ref in (own_ref, one_ref, two_ref))
        return sum(parts)

    gate_ref[...] = added(0, slice(None))
    for n in range(2):
        out_ref[:, n * inner : (n + 1) * inner] = added(1, slice(n * inner, (n + 1) * inner))


def sum_last(parts, *others):
    own = parts[0]
    ins = [(a, 0) for a in parts] + [(a, "any") for a in others]
    [total] = call(add_last_kernel, ins, [(shape_of(own.shape, f32), 0)], own.shape[0])
    return total


def pack(parts):
    return jnp.concatenate([p.reshape(-1) for p in parts])


def unpack(flat, shapes):
    out, at = [], 0
    for shape in shapes:
        size = 1
        for n in shape:
            size *= n
        out.append(flat[..., at : at + size].reshape(flat.shape[:-1] + tuple(shape)))
        at += size
    return out


def padded(flat, multiple=1024):
    return jnp.pad(flat, (0, -flat.shape[0] % multiple))


def body(
    tokens,
    out_grad,
    domain,
    group_weight,
    w_qkv,
    conv_weight,
    w_beta,
    w_outgate,
    head_gain,
    w_out,
    mixer_gain,
    mlp_gain,
    w_gateup,
    w_down,
):
    dp = lax.axis_size("dp")
    place = lax.axis_index("dp")
    seqs, block, local_width = tokens.shape
    count_rows = seqs * block
    heads = conv_weight.shape[2]
    inner = heads * DK
    column = lax.axis_index("mp") * local_width
    near_four = dp == 4

    def blocks_about(array, axis):
        if not near_four:
            return array
        size = array.shape[axis] // 4
        return jnp.concatenate(
            [lax.dynamic_slice_in_dim(array, (place ^ k) * size, size, axis) for k in range(4)],
            axis,
        )

    width = out_grad.shape[2]
    turn = place if near_four else jnp.int32(0)
    column_about = ((column // (width // 4)) ^ turn) * (width // 4) + column % (width // 4)

    def own(array):
        array = array.reshape(seqs, block, width)
        return lax.dynamic_slice_in_dim(array, column_about, local_width, 2)

    onehot = (domain[..., None] == jnp.arange(3, dtype=jnp.int32)).astype(f32)
    own_counts = jnp.sum(onehot, axis=(0, 1))
    high = jnp.floor(own_counts / 128.0)
    digits = jnp.concatenate([high, own_counts - 128.0 * high]).astype(bf16)
    small = [w_beta, conv_weight, head_gain, mixer_gain, mlp_gain, digits]
    packed = padded(pack(small))
    size = width // 4
    if near_four:
        qkv_hop = first_hop(w_qkv)
        qkv_halves = halves_of(qkv_hop, 1)
        qkv = gathered_pieces(w_qkv, 1, qkv_hop, qkv_halves)
        packed = after(packed, qkv_halves)
        gathered = jnp.stack([packed] + [swap(packed, bits) for bits in (1, 2, 3)])
        half = w_out.shape[1] // 2
        pair_own = jnp.stack(
            [w_outgate, jnp.concatenate([w_out[:, :half], w_out[:, half:]], 0)]
        )
        pair_layout = [(k, 0, size, size) for k in range(4)]
        layout = pair_layout[:3] + [(3, 0, size // 2, size), (3, size // 2, size // 2, size)]
    else:
        gathered = lax.all_gather(packed, "dp")
        qkv = [lax.all_gather(w_qkv, "dp", axis=1, tiled=True)]
        gate_pieces = [lax.all_gather(w_outgate, "dp", axis=0, tiled=True)]
        out_pieces = [lax.all_gather(w_out, "dp", axis=1, tiled=True)]
        layout = pair_layout = [(0, 0, width, width)]
    ranges = [(k * step + start, n) for k, start, n, step in layout]
    g_beta, g_conv, g_head, g_mix, g_mlp, g_digits = unpack(gathered, [a.shape for a in small])
    about_beta = g_beta.reshape(-1, heads)
    full_beta = blocks_about(about_beta, 0)
    full_conv = jnp.moveaxis(blocks_about(g_conv, 0), 0, 3).reshape(3 * KW, inner).astype(f32)
    gain_head = blocks_about(g_head, 0).reshape(1, DK).astype(f32)
    gain_one = blocks_about(g_mix.reshape(1, -1).astype(f32), 1)
    gain_two = g_mlp.reshape(1, -1).astype(f32)
    sums = jnp.sum(g_digits.astype(f32), 0)
    counts = 128.0 * sums[:3] + sums[3:]
    table = group_weight * (domain.shape[0] * domain.shape[1] * dp) / counts
    factor = jnp.sum(onehot * table, -1)[..., None]

    def flat(array):
        return array.reshape(array.shape[:-3] + (count_rows, array.shape[-1]))

    rows = lax.all_gather(tokens, "mp", axis=2, tiled=True)
    if near_four:
        gate_pieces = out_pieces = [lax.all_gather(after(pair_own, packed), "dp")]
    turn_one = turn.reshape(1)
    per_token = (seqs, block)
    square = (seqs, heads, DK, DK)
    hidden_one, proj, tail, logits, scale_one = call(
        partial(project_kernel, layout),
        [(rows, 0), (gain_one, None), (jnp.pad(full_beta, ((0, 0), (0, 128 - heads))), None)]
        + [(a, None) for a in qkv],
        [
            (shape_of(per_token + (width,), bf16), 0),
            (shape_of((3,) + per_token + (inner,), bf16), 1),
            (shape_of((3, seqs, HALO, inner), bf16), 1),
            (shape_of(per_token + (heads,), f32), 0),
            (shape_of(per_token + (1,), f32), 0),
        ],
        seqs,
        scalar=turn_one,
        scratch=[pltpu.VMEM((block, width), bf16)],
    )
    before = shifted(tail, "dp", 1)
    inverse, wu, qo, to = call(
        pre_kernel,
        [(proj, None), (before, None), (full_conv, None), (logits, None)],
        [
            (shape_of((seqs, heads, block, block), f32), None),
            (shape_of((seqs, heads, block, 2 * DK), f32), None),
            (shape_of((seqs, heads, block, 2 * DK), f32), None),
            (shape_of((seqs, heads, DK, 2 * DK), bf16), None),
        ],
        1,
    )
    near = [shifted(to, "dp", c) for c in range(1, dp)]
    rows_about, cotangent = call(
        partial(prepare_kernel, layout),
        [(rows, 0), (out_grad, 0), (factor, 0)],
        [(shape_of(per_token + (width,), bf16), 0)] * 2,
        seqs,
        scalar=turn_one,
    )
    turned = jnp.swapaxes(w_gateup, 1, 2)
    feed_own = [turned, w_down]
    mixer_part, normed, rule, state, gates = call(
        partial(mix_kernel, pair_layout, len(near), len(out_pieces)),
        [(a, 0) for a in near]
        + [(qo, 0), (hidden_one, 0), (gain_head, None)]
        + [(a, None) for a in gate_pieces + out_pieces]
        + [(cotangent, "any")],
        [
            (shape_of(per_token + (width,), bf16), 0),
            (shape_of(per_token + (inner,), bf16), 0),
            (shape_of(per_token + (inner,), f32), 0),
            (shape_of(square, f32), 0),
            (shape_of(per_token + (inner,), f32), 0),
        ],
        seqs,
        scalar=turn_one,
    )
    total = lax.psum(mixer_part, "mp")
    nexts = [shifted(to[..., :DK], "dp", -c) for c in range(1, dp - 1)]
    if near_four:
        gateup, down = (gathered_pieces(a, a.ndim - 1) for a in after(copies(feed_own), mixer_part, nexts))
    else:
        gateup, down = (
            [lax.all_gather(a, "dp", axis=a.ndim - 1, tiled=True)] for a in feed_own
        )
    units = w_down.shape[0]
    two_part, hidden_two, hidden_mlp, grad_pair = call(
        partial(feed_kernel, layout),
        [(rows_about, 0), (total, 0), (cotangent, 0), (gain_two, None)]
        + [(a, None) for a in gateup + down],
        [
            (shape_of(per_token + (width,), bf16), 0),
            (shape_of(per_token + (width,), bf16), 0),
            (shape_of(per_token + (units,), bf16), 0),
            (shape_of((2,) + per_token + (units,), bf16), 1),
        ],
        seqs,
        scratch=[pltpu.VMEM((block, units), f32)] * 3,
    )
    grad_two = lax.psum(two_part, "mp")

    def feed_gradients(some, *others):
        outs = [(shape_of((m, units, n), bf16), None) for _, n in some for m in (2, 1)]
        base, span = some[0][0], sum(n for _, n in some)
        aligned = base % span == 0
        at = base // span if aligned else 0
        cols = pl.BlockSpec((count_rows, span if aligned else width), lambda s: (0, at))
        made = pl.pallas_call(
            partial(feed_gradient_kernel, base if aligned else 0, some),
            grid=(1,),
            in_specs=[
                cols,
                cols,
                pl.BlockSpec((2, count_rows, units), lambda s: (0, 0, 0)),
                pl.BlockSpec((count_rows, units), lambda s: (0, 0)),
            ]
            + [pl.BlockSpec(memory_space=pl.ANY)] * len(others),
            out_specs=[pl.BlockSpec(o.shape, lambda s: (0, 0, 0)) for o, _ in outs],
            out_shape=[o for o, _ in outs],
            compiler_params=pltpu.CompilerParams(vmem_limit_bytes=VMEM),
        )(flat(hidden_two), flat(cotangent), flat(grad_pair), flat(hidden_mlp), *others)
        return made[::2], made[1::2]

    if near_four:
        feed_far = feed_gradients(ranges[3:])
        feed_in = [far_hop(*far) for far in feed_far]
        near_gateup, near_down = feed_gradients(ranges[:3], feed_far[0][0])
        first_made = [(near_gateup[0], "any")]
        gateup_sums = near_hop(near_sums(near_gateup, feed_in[0], *feed_in[1]))
        down_sums = near_hop(near_sums(near_down, feed_in[1]))
        held = [(a, "any") for a in gateup_sums[1:]]
    else:
        [grad_gateup], [grad_down] = feed_gradients(ranges)
        held = first_made = []
    [down_part] = call(
        partial(down_kernel, layout),
        [(hidden_mlp, 0)] + [(a, None) for a in down] + first_made,
        [(shape_of(per_token + (width,), bf16), 0)],
        seqs,
        scalar=turn_one,
    )
    mlp_share = lax.psum_scatter(down_part, "mp", scatter_dimension=2, tiled=True)
    grad_mix, middle_own, mlpgain, drule, dgate, dgain, direct = call(
        partial(middle_back_kernel, pair_layout, len(out_pieces)),
        [
            (grad_two, 0),
            (cotangent, 0),
            (rows_about, 0),
            (total, 0),
            (gain_two, None),
            (rule, 0),
            (gates, 0),
            (gain_head, None),
            (qo, 0),
        ]
        + [(a, None) for a in out_pieces]
        + [(down_part, "any")]
        + held,
        [
            (shape_of(per_token + (width,), bf16), 0),
            (shape_of(per_token + (local_width,), f32), 0),
            (shape_of((seqs, 1, width), f32), 0),
            (shape_of(per_token + (inner,), f32), 0),
            (shape_of(per_token + (inner,), bf16), 0),
            (shape_of((seqs, 1, DK), f32), 0),
            (shape_of(square, bf16), 0),
        ],
        seqs,
        scalar=jnp.stack([turn, column_about]),
        scratch=[pltpu.VMEM((block, width), f32), pltpu.VMEM((CHUNK, width), f32)],
    )
    directs = [shifted(direct, "dp", -c) for c in range(1, dp)]
    if near_four:
        pair_grads = call(
            partial(pair_gradient_kernel, [(k * size, size) for k in range(4)]),
            [(flat(a), None) for a in (hidden_one, dgate, normed, grad_mix)],
            [(shape_of((2, size, inner), bf16), None)] * 4,
            1,
        )
        pair_in = far_hop(*jnp.split(pair_grads[3], 2, 1))
        held = [(a, "any") for a in (pair_grads[3], *down_sums[1:])]
    else:
        grad_outgate = jnp.einsum(
            "td,tc->dc", flat(hidden_one), flat(dgate), preferred_element_type=f32
        )
        grad_outproj = jnp.einsum(
            "tc,td->cd", flat(normed), flat(grad_mix), preferred_element_type=f32
        )
        held = []
    dproj, last, first, dtaps, dlogits = call(
        partial(back_kernel, len(directs)),
        [
            (proj, 1),
            (before, 1),
            (full_conv, None),
            (logits, 0),
            (inverse, 0),
            (wu, 0),
            (state, 0),
            (drule, 0),
        ]
        + [(a, 0) for a in directs + nexts]
        + held,
        [
            (shape_of((3,) + per_token + (inner,), bf16), 1),
            (shape_of((3, seqs, PAD, inner), f32), 1),
            (shape_of((3, seqs, PAD, inner), f32), 1),
            (shape_of((seqs, 3 * KW, inner), f32), 0),
            (shape_of(per_token + (heads,), bf16), 0),
        ],
        seqs,
    )
    later = shifted(first, "dp", -1)
    dproj = lax.dynamic_update_slice(dproj, (last + later).astype(bf16), (0, 0, block - PAD, 0))
    one_low, row_part, gain_part = call(
        partial(first_back_kernel, layout, pair_layout, len(gate_pieces)),
        [
            (flat(dproj), None),
            (flat(dgate), None),
            (flat(dlogits), None),
            (flat(proj), None),
            (flat(gates), None),
            (flat(logits), None),
            (about_beta.T.astype(f32), None),
            (flat(rows_about), None),
            (flat(scale_one), None),
        ]
        + [(a, None) for a in qkv + gate_pieces]
        + [(mlp_share, "any")]
        + ([(a, "any") for a in pair_in] if near_four else []),
        [
            (shape_of((count_rows, width), bf16), None),
            (shape_of((count_rows, 1), f32), None),
            (shape_of((1, width), f32), None),
        ],
        1,
        scalar=turn_one,
    )
    one_share = lax.psum_scatter(
        one_low.reshape(seqs, block, width), "mp", scatter_dimension=2, tiled=True
    ).astype(f32)
    made = call(
        partial(qkv_gradient_kernel, ranges),
        [(flat(hidden_one), None), (flat(dproj), None), (flat(dlogits), None), (row_part, "any")],
        [(shape_of((3, n, inner), bf16), None) for _, n in ranges]
        + [(shape_of((heads, width), f32), None)],
        1,
    )

    def pieces(array, axis, about):
        shape = array.shape
        cut = array.reshape(shape[:axis] + (dp, shape[axis] // dp) + shape[axis + 1 :])
        cut = jnp.moveaxis(cut, axis, 0).reshape(dp, -1)
        return blocks_about(cut, 0) if about else cut

    smalls = jnp.concatenate(
        [
            pieces(jnp.sum(dtaps, 0).reshape(3, KW, heads, DK), 3, True),
            pieces(made[-1].T, 0, False),
            pieces(jnp.sum(dgain, (0, 1)), 0, True),
            pieces(gain_part[0], 0, False),
            pieces(jnp.sum(mlpgain, (0, 1)), 0, False),
        ],
        1,
    )
    if near_four:
        qkv_in = far_hop(made[3], made[4])
        gateup_total = sum_last(gateup_sums, made[0])
        down_total = sum_last(down_sums, made[0])
        own_qkv, *near_qkv = near_sums(made[:3], qkv_in, gateup_total, down_total)
        smalls = jnp.pad(smalls, ((0, 0), (0, -smalls.shape[1] % 1024))).reshape(dp, -1, 128)
        sent = smalls.astype(bf16)
        got = [swap(sent[bits], bits) for bits in (1, 2, 3)]
        [mine] = call(
            add_small_kernel,
            [(a, None) for a in [smalls[0]] + got],
            [(shape_of(smalls.shape[1:], f32), None)],
            1,
        )
        mine = mine.reshape(-1)
        sum_qkv = sum_last(near_hop((own_qkv, *near_qkv)))
        sum_gateup = jnp.swapaxes(gateup_total, 1, 2)
        sum_down = down_total[0]
        pair_near = near_sums(pair_grads[:3], pair_in, *near_qkv)[1:]
        sum_outgate, sum_out = call(
            add_pair_kernel,
            [(a, None) for a in near_hop((pair_grads[0], *pair_near))],
            [(shape_of(w_outgate.shape, f32), None), (shape_of(w_out.shape, f32), None)],
            1,
        )
    else:
        gathered = lax.all_gather(smalls.astype(bf16), "dp")
        mine = jnp.sum(
            lax.dynamic_index_in_dim(gathered, place, 1, keepdims=False).astype(f32), 0
        )

        def scattered(array, axis):
            return lax.psum_scatter(array, "dp", scatter_dimension=axis, tiled=True).astype(f32)

        sum_qkv = scattered(made[0], 1)
        sum_outgate = scattered(grad_outgate.astype(bf16), 0)
        sum_out = scattered(grad_outproj.astype(bf16), 1)
        sum_gateup = jnp.swapaxes(scattered(grad_gateup, 2), 1, 2)
        sum_down = scattered(grad_down[0], 1)
    sum_conv, sum_beta, sum_head, sum_mix, sum_mlp = unpack(
        mine,
        [conv_weight.shape, w_beta.shape, head_gain.shape, mixer_gain.shape, mlp_gain.shape],
    )
    rest = [row_part[:, 0], sum_head, sum_mix]
    packed_rest = padded(pack(rest), 128)
    if near_four:
        packed_rest = after(packed_rest, near_qkv)
    everyone = lax.optimization_barrier(lax.all_gather(packed_rest, "mp"))
    row_sum, sum_head, sum_mix = unpack(jnp.sum(everyone, 0), [a.shape for a in rest])

    own_tokens = tokens.astype(f32)
    mixed_out = (own_tokens + own(total).astype(f32) + mlp_share.astype(f32)).astype(bf16)
    row_mean = (row_sum / width).reshape(seqs, block, 1)
    gain_own = lax.dynamic_slice_in_dim(gain_one, column, local_width, 1)
    tokens_grad = middle_own + scale_one * (
        one_share * gain_own - own_tokens * scale_one * row_mean
    )
    return (
        mixed_out,
        tokens_grad.astype(bf16),
        sum_qkv,
        sum_conv,
        sum_beta,
        sum_outgate,
        sum_head,
        sum_out,
        sum_mix,
        sum_mlp,
        sum_gateup,
        sum_down,
    )


def solution(mesh):
    return jax.shard_map(
        body,
        mesh=mesh,
        in_specs=(
            P(None, "dp", "mp"),
            P(None, "dp", None),
            P(None, "dp"),
            P(),
            P(None, "dp", "mp"),
            P(None, None, "mp", "dp"),
            P("dp", "mp"),
            P("dp", "mp"),
            P("dp"),
            P("mp", "dp"),
            P("dp"),
            P("dp"),
            P(None, "dp", "mp"),
            P("mp", "dp"),
        ),
        out_specs=(
            P(None, "dp", "mp"),
            P(None, "dp", "mp"),
            P(None, "dp", "mp"),
            P(None, None, "mp", "dp"),
            P("dp", "mp"),
            P("dp", "mp"),
            P("dp"),
            P("mp", "dp"),
            P("dp"),
            P("dp"),
            P(None, "dp", "mp"),
            P("mp", "dp"),
        ),
        check_vma=False,
    )
```

```python
from functools import partial

import jax
import jax.numpy as jnp
from jax import lax
from jax.experimental import pallas as pl
from jax.experimental.pallas import tpu as pltpu
from jax.sharding import PartitionSpec as P

DK = 128
KW = 4
PAD = 8
HALO = 16
VMEM = 58 * 2**20

eps_norm = 1e-06
eps_unit = 1e-06

f32 = jnp.float32
bf16 = jnp.bfloat16


def split(v):
    if v.dtype == bf16:
        return v, None
    high = v.astype(bf16)
    return high, (v - high.astype(f32)).astype(bf16)


def mm(a, b, ca=1, cb=0, passes=3):
    def one(x, y):
        return lax.dot_general(x, y, (((ca,), (cb,)), ((), ())), preferred_element_type=f32)

    if passes == 1:
        return one(a.astype(bf16), b.astype(bf16))
    (ah, al), (bh, bl) = split(a), split(b)
    out = one(ah, bh)
    if bl is not None:
        out = out + one(ah, bl)
    if al is not None:
        out = out + one(al, bh)
    return out


def places(rows, cols):
    return (
        lax.broadcasted_iota(jnp.int32, (rows, cols), 0),
        lax.broadcasted_iota(jnp.int32, (rows, cols), 1),
    )


def unit_lower_inverses(blocks):
    size = blocks[0].shape[0]
    if size > 128:
        half = size // 2
        parts = unit_lower_inverses(
            [a[:half, :half] for a in blocks] + [a[half:, half:] for a in blocks]
        )
        firsts, seconds = parts[: len(blocks)], parts[len(blocks) :]
        inner = [mm(a[half:, :half], x) for a, x in zip(blocks, firsts)]
        lower = [-mm(x, y) for x, y in zip(seconds, inner)]
        zero = jnp.zeros((half, half), f32)
        return [
            jnp.concatenate(
                [jnp.concatenate([x, zero], 1), jnp.concatenate([y, z], 1)], 0
            )
            for x, y, z in zip(firsts, lower, seconds)
        ]
    rows, cols = places(size, size)
    eye = (rows == cols).astype(f32)
    level = 0
    inverses = None
    while (1 << level) < size:
        mask = (
            ((rows >> (level + 1)) == (cols >> (level + 1)))
            & (((rows >> level) & 1) == 1)
            & (((cols >> level) & 1) == 0)
        ).astype(f32)
        lows = [a * mask for a in blocks]
        if level == 0:
            inverses = [eye - low for low in lows]
        else:
            inner = [mm(low, x) for low, x in zip(lows, inverses)]
            inverses = [x - mm(x, y) for x, y in zip(inverses, inner)]
        level += 1
    return inverses


def head_slice(h):
    return slice(h * DK, (h + 1) * DK)


def convolve(proj_ref, before_ref, taps, i, h):
    own = proj_ref[i, 0, :, head_slice(h)].astype(f32)
    length = own.shape[0]
    ext = jnp.concatenate([before_ref[i, 0, :, head_slice(h)].astype(f32), own], 0)
    shifts = [ext[HALO - KW + 1 + j : HALO - KW + 1 + j + length] for j in range(KW)]
    out = None
    for j in range(KW):
        tap = taps[i * KW + j : i * KW + j + 1, head_slice(h)]
        out = tap * shifts[j] if out is None else out + tap * shifts[j]
    sig = jax.nn.sigmoid(out)
    return shifts, out, sig, out * sig


def unit(acts):
    inv = lax.rsqrt(jnp.sum(acts * acts, -1, keepdims=True) + eps_unit)
    return acts * inv, inv


def rule_inputs(proj_ref, before_ref, taps, h):
    parts = [convolve(proj_ref, before_ref, taps, i, h) for i in range(3)]
    q, q_inv = unit(parts[0][3])
    k, k_inv = unit(parts[1][3])
    return parts, (q, q_inv), (k, k_inv), parts[2][3]


def norm_factor(values):
    return lax.rsqrt(jnp.mean(values * values, -1, keepdims=True) + eps_norm)


def project_kernel(layout, *refs):
    place_ref, rows_ref, gain_ref, beta_ref = refs[:4]
    pieces = refs[4 : 4 + len(layout)]
    hidden_ref, proj_ref, tail_ref, logit_ref, scale_ref, keep_ref = refs[4 + len(layout) :]
    rows = rows_ref[0].astype(f32)
    scale = norm_factor(rows)
    scale_ref[0] = scale
    keep_ref[...] = (rows * scale * gain_ref[...]).astype(bf16)
    logits = mm(keep_ref[...], beta_ref[...])
    logit_ref[0] = logits[:, : logit_ref.shape[2]]
    sums = [None] * 3
    for (k, start, size, block), piece in zip(layout, pieces):
        at = pl.multiple_of((place_ref[0] ^ k) * block + start, 128)
        part = keep_ref[:, pl.ds(at, size)]
        hidden_ref[0, :, k * block + start : k * block + start + size] = part
        for i in range(3):
            term = mm(part, piece[i])
            sums[i] = term if sums[i] is None else sums[i] + term
    for i in range(3):
        low = sums[i].astype(bf16)
        proj_ref[i, 0] = low
        tail_ref[i, 0] = low[low.shape[0] - HALO :]


def pre_kernel(proj_ref, before_ref, taps_ref, logit_ref, x_ref, wu_ref, qo_ref, to_ref):
    seqs, heads = to_ref.shape[:2]
    taps = taps_ref[...]
    length = proj_ref.shape[2]
    r, c = places(length, length)
    strict = (r > c).astype(f32)
    full = (r >= c).astype(f32)
    saved, blocks = [], []
    for s in range(seqs):
        betas = jax.nn.sigmoid(logit_ref[s])
        rows, before = proj_ref.at[:, s : s + 1], before_ref.at[:, s : s + 1]
        for h in range(heads):
            _, (q, _), (k, _), v = rule_inputs(rows, before, taps, h)
            q, k, v = q.astype(bf16), k.astype(bf16), v.astype(bf16)
            beta = betas[:, h : h + 1]
            blocks.append(beta * mm(k, k, 1, 1) * strict)
            saved.append((s, h, q, k, v, beta))
    inverses = unit_lower_inverses(blocks)
    r, c = places(DK, DK)
    eye = (r == c).astype(f32)
    for (s, h, q, k, v, beta), x in zip(saved, inverses):
        x_ref[s, h] = x
        kv = jnp.concatenate([k.astype(f32), v.astype(f32)], 1) * beta
        wu = mm(x, kv)
        wu_ref[s, h] = wu
        scores = mm(q, k, 1, 1) * full
        pwu = mm(scores, wu)
        qo_ref[s, h, :, :DK] = q.astype(f32) - pwu[:, :DK]
        qo_ref[s, h, :, DK:] = pwu[:, DK:]
        kwu = mm(k, wu, 0, 0)
        to_ref[s, h, :, :DK] = (eye - kwu[:, :DK]).astype(bf16)
        to_ref[s, h, :, DK:] = kwu[:, DK:].astype(bf16)


def by_piece(place_ref, refs):
    if len(refs) > 1 or len(refs[0].shape) < 4:
        return refs
    return [refs[0].at[place_ref[0] ^ k] for k in range(4)]


def gate_part(ref):
    return ref.at[0] if len(ref.shape) == 3 else ref


def out_columns(layout, refs):
    for (k, start, size, block), ref in zip(layout, refs):
        at, half = k * block + start, size // 2
        if len(ref.shape) == 2:
            yield at, size, ref
            continue
        inner = ref.shape[1] // 2
        yield at, half, ref.at[1, :inner]
        yield at + half, half, ref.at[1, inner:]


def mix_kernel(layout, count, pieces, place_ref, *refs):
    near, rest = refs[:count], refs[count:]
    qo_ref, hidden_ref, gain_ref = rest[:3]
    gate_pieces = by_piece(place_ref, rest[3 : 3 + pieces])
    outs = by_piece(place_ref, rest[3 + pieces : 3 + 2 * pieces])
    part_ref, normed_ref, rule_ref, state_ref, gate_ref = rest[-5:]
    gates = None
    for (k, start, size, block), ref in zip(layout, gate_pieces):
        at = k * block + start
        term = mm(hidden_ref[0, :, at : at + size], gate_part(ref)[...])
        gates = term if gates is None else gates + term
    gate_ref[0] = gates
    heads = state_ref.shape[1]
    for h in range(heads):
        state = near[-1][0, h, :, DK:].astype(f32)
        for ref in reversed(near[:-1]):
            state = mm(ref[0, h, :, :DK], state) + ref[0, h, :, DK:].astype(f32)
        state_ref[0, h] = state
        qo = qo_ref[0, h]
        out = (mm(qo[:, :DK], state) + qo[:, DK:]) * DK ** (-0.5)
        rule_ref[0, :, head_slice(h)] = out
        gate = gate_ref[0, :, head_slice(h)]
        normed = out * norm_factor(out) * gain_ref[...] * (gate * jax.nn.sigmoid(gate))
        normed_ref[0, :, head_slice(h)] = normed.astype(bf16)
    for at, size, ref in out_columns(layout, outs):
        part_ref[0, :, at : at + size] = mm(normed_ref[0], ref[...]).astype(bf16)


def prepare_kernel(layout, place_ref, rows_ref, grad_ref, factor_ref, about_ref, cot_ref):
    for k, start, size, block in layout:
        at = pl.multiple_of((place_ref[0] ^ k) * block + start, 128)
        to = slice(k * block + start, k * block + start + size)
        about_ref[0, :, to] = rows_ref[0, :, pl.ds(at, size)]
        grad = grad_ref[0, :, pl.ds(at, size)].astype(f32) * factor_ref[0]
        cot_ref[0, :, to] = grad.astype(bf16)


def down_kernel(layout, place_ref, mlp_ref, *refs):
    part_ref = refs[-1]
    for (k, start, size, block), ref in zip(layout, refs):
        at = pl.multiple_of((place_ref[0] ^ k) * block + start, 128)
        part_ref[0, :, pl.ds(at, size)] = mm(mlp_ref[0], ref[...]).astype(bf16)


def plus(value, came):
    return (value.astype(bf16).astype(f32) + came.astype(f32)).astype(bf16)


def feed_gradient_kernel(ranges, arrivals, left_ref, right_ref, *refs):
    came, outs = refs[:arrivals], refs[-len(ranges) :]
    for n, (start, size) in enumerate(ranges):
        for m in range(left_ref.shape[0]):
            piece = mm(left_ref[m], right_ref[:, start : start + size], 0, 0)
            half = size // 2
            if came and n == 1:
                outs[n][m, :, :half] = piece[:, :half].astype(bf16)
                outs[n][m, :, half:] = plus(piece[:, half:], came[1][m])
            elif came and n == 2:
                outs[n][m, :, :half] = plus(piece[:, :half], came[0][m])
                outs[n][m, :, half:] = piece[:, half:].astype(bf16)
            else:
                outs[n][m] = piece.astype(bf16)


def qkv_gradient_kernel(ranges, hidden_ref, dproj_ref, dlogit_ref, *outs):
    outs = outs[-len(ranges) - 1 :]
    for (start, size), out in zip(ranges, outs[:-1]):
        hidden = hidden_ref[:, start : start + size]
        for i in range(3):
            out[i] = mm(hidden, dproj_ref[i], 0, 0).astype(bf16)
    outs[-1][...] = mm(dlogit_ref[...], hidden_ref[...], 0, 0)


def pair_gradient_kernel(ranges, hidden_ref, dgate_ref, normed_ref, mix_ref, *outs):
    inner = normed_ref.shape[1]
    for (start, size), out in zip(ranges, outs):
        out[0] = mm(hidden_ref[:, start : start + size], dgate_ref[...], 0, 0).astype(bf16)
        for n in range(2):
            at = start + n * size // 2
            mix = mix_ref[:, at : at + size // 2]
            out[1, n * inner : (n + 1) * inner] = mm(normed_ref[...], mix, 0, 0).astype(bf16)


def add_halves_kernel(*refs):
    one_ref, two_ref, low_ref, high_ref, one_out, two_out = refs[:4] + refs[-2:]
    one_out[...] = (one_ref[...].astype(f32) + high_ref[...].astype(f32)).astype(bf16)
    two_out[...] = (two_ref[...].astype(f32) + low_ref[...].astype(f32)).astype(bf16)


def add_small_kernel(*refs):
    refs[-1][...] = sum(ref[...].astype(f32) for ref in refs[:4])


def add_last_kernel(*refs):
    own_ref, one_ref, two_ref, out_ref = refs[:3] + refs[-1:]
    out_ref[...] = own_ref[...].astype(f32) + one_ref[...].astype(f32) + two_ref[...].astype(f32)


def feed_kernel(layout, *refs):
    rows_ref, total_ref, cot_ref, gain_ref = refs[:4]
    count = len(layout)
    gateups, downs = (refs[4 + n * count : 4 + (n + 1) * count] for n in range(2))
    two_ref, hidden_ref, mlp_ref, pair_ref = refs[-4:]
    middle = rows_ref[0].astype(f32) + total_ref[0].astype(f32)
    hidden_ref[0] = (middle * norm_factor(middle) * gain_ref[...]).astype(bf16)
    gate, up, grad = None, None, None
    for (k, start, size, block), w_gateup, w_down in zip(layout, gateups, downs):
        lanes = slice(k * block + start, k * block + start + size)
        hidden = hidden_ref[0, :, lanes]
        terms = (
            mm(hidden, w_gateup[0], 1, 1),
            mm(hidden, w_gateup[1], 1, 1),
            mm(cot_ref[0, :, lanes], w_down[...], 1, 1),
        )
        if gate is None:
            gate, up, grad = terms
        else:
            gate, up, grad = gate + terms[0], up + terms[1], grad + terms[2]
    sig = jax.nn.sigmoid(gate)
    silu = gate * sig
    mlp_ref[0] = (silu * up).astype(bf16)
    first = (grad * up * (sig + silu * (1.0 - sig))).astype(bf16)
    second = (grad * silu).astype(bf16)
    pair_ref[0, 0] = first
    pair_ref[1, 0] = second
    for (k, start, size, block), w_gateup in zip(layout, gateups):
        lanes = slice(k * block + start, k * block + start + size)
        two = mm(first, w_gateup[0]) + mm(second, w_gateup[1])
        two_ref[0, :, lanes] = two.astype(bf16)


def middle_back_kernel(layout, pieces, at_ref, *refs):
    two_ref, cot_ref, rows_ref, total_ref, gain_ref, rule_ref, gate_ref, head_gain_ref, qo_ref = refs[:9]
    outs = by_piece(at_ref, refs[9 : 9 + pieces])
    mix_ref, own_ref, mlpgain_ref, drule_ref, dgate_ref, dgain_ref, direct_ref, keep_ref = refs[-8:]
    middle = rows_ref[0].astype(f32) + total_ref[0].astype(f32)
    factor = norm_factor(middle)
    normal = middle * factor
    two = two_ref[0].astype(f32)
    mlpgain_ref[0] = jnp.sum(two * normal, 0, keepdims=True)
    scaled = two * gain_ref[...]
    mean = jnp.mean(scaled * normal, -1, keepdims=True)
    keep_ref[...] = cot_ref[0].astype(f32) + factor * (scaled - normal * mean)
    width = own_ref.shape[2]
    own_ref[0] = keep_ref[:, pl.ds(pl.multiple_of(at_ref[1], 128), width)]
    mix_ref[0] = keep_ref[...].astype(bf16)
    grads = None
    for at, size, ref in out_columns(layout, outs):
        term = mm(mix_ref[0, :, at : at + size], ref[...], 1, 1)
        grads = term if grads is None else grads + term
    total = jnp.zeros((1, DK), f32)
    for h in range(direct_ref.shape[1]):
        grad = grads[:, head_slice(h)]
        out = rule_ref[0, :, head_slice(h)]
        gate = gate_ref[0, :, head_slice(h)]
        inv = norm_factor(out)
        n = out * inv
        sig = jax.nn.sigmoid(gate)
        silu = gate * sig
        gg = grad * head_gain_ref[...]
        dn = gg * silu
        drule = inv * (dn - n * jnp.mean(dn * n, -1, keepdims=True))
        drule_ref[0, :, head_slice(h)] = drule
        dgate = gg * n * sig * (1.0 + gate * (1.0 - sig))
        dgate_ref[0, :, head_slice(h)] = dgate.astype(bf16)
        total = total + jnp.sum(grad * n * silu, 0, keepdims=True)
        direct = mm(qo_ref[0, h, :, :DK], drule, 0, 0) * DK ** (-0.5)
        direct_ref[0, h] = direct.astype(bf16)
    dgain_ref[0] = total


def first_back_kernel(layout, pair_layout, count, place_ref, *refs):
    dproj_ref, dgate_ref, dlogit_ref, proj_ref, gate_ref, logit_ref, beta_ref, rows_ref, scale_ref = refs[:9]
    pieces = refs[9 : 9 + len(layout)]
    pairs = by_piece(place_ref, refs[9 + len(layout) : 9 + len(layout) + count])
    one_ref, rowsum_ref, gainsum_ref = refs[-3:]
    gates = {}
    for (k, start, size, block), ref in zip(pair_layout, pairs):
        gates[k] = ref
    for (k, start, size, block), piece in zip(layout, pieces):
        lanes = slice(k * block + start, k * block + start + size)
        grad = mm(dgate_ref[...], gate_part(gates[k])[start : start + size], 1, 1)
        for i in range(3):
            grad = grad + mm(dproj_ref[i], piece[i], 1, 1)
        for h in range(beta_ref.shape[0]):
            grad = grad + dlogit_ref[:, h : h + 1].astype(f32) * beta_ref[h : h + 1, lanes]
        at = pl.multiple_of((place_ref[0] ^ k) * block + start, 128)
        one_ref[:, pl.ds(at, size)] = grad.astype(bf16)
        gainsum_ref[:, lanes] = jnp.sum(
            grad * (rows_ref[:, lanes].astype(f32) * scale_ref[...]), 0, keepdims=True
        )
    total = dgate_ref[...].astype(f32) * gate_ref[...]
    for i in range(3):
        total = total + dproj_ref[i].astype(f32) * proj_ref[i].astype(f32)
    total = jnp.sum(total, -1, keepdims=True)
    logits = dlogit_ref[...].astype(f32) * logit_ref[...]
    rowsum_ref[...] = total + jnp.sum(logits, -1, keepdims=True)


def back_kernel(count, *refs):
    (
        proj_ref,
        before_ref,
        taps_ref,
        logit_ref,
        x_ref,
        wu_ref,
        state_ref,
        drule_ref,
    ) = refs[:8]
    dproj_ref, last_ref, first_ref, dtaps_ref, dlogit_ref = refs[-5:]
    others = refs[8 : 8 + 2 * count - 1]
    directs, nexts = others[:count], others[count:]
    heads = state_ref.shape[1]
    taps = taps_ref[...]
    length = proj_ref.shape[2]
    betas = jax.nn.sigmoid(logit_ref[0])
    r, c = places(length, length)
    strict = (r > c).astype(f32)
    full = (r >= c).astype(f32)
    zeros = jnp.zeros((PAD, DK), f32)
    for h in range(heads):
        parts, (qu, q_inv), (ku, k_inv), vu = rule_inputs(proj_ref, before_ref, taps, h)
        q, k, v = qu.astype(bf16), ku.astype(bf16), vu.astype(bf16)
        beta = betas[:, h : h + 1]
        leave = jnp.zeros((DK, DK), f32)
        for j in reversed(range(count)):
            here = directs[j][0, h].astype(f32)
            leave = here if j == count - 1 else mm(nexts[j][0, h], leave, 0, 0) + here
        state = state_ref[0, h]
        wu = wu_ref[0, h]
        u = wu[:, DK:] - mm(wu[:, :DK], state)
        resid = v.astype(f32) - mm(k, state)
        dout = drule_ref[0, :, head_slice(h)] * DK ** (-0.5)
        gram = mm(k, k, 1, 1)
        scores = mm(q, k, 1, 1) * full
        du = mm(scores, dout, 0, 0) + mm(k, leave)
        y = mm(x_ref[0, h], du, 0, 0)
        by = beta * y
        da = -(mm(y, u, 1, 1, 1) * strict)
        dbeta = jnp.sum(y * resid, -1, keepdims=True) + jnp.sum(da * gram, -1, keepdims=True)
        dgram = beta * da
        dscores = mm(dout, u, 1, 1, 1) * full
        dq = mm(dout, state, 1, 1, 1) + mm(dscores, k, 1, 0, 1)
        dk = (
            mm(dgram, k, 1, 0, 1)
            + mm(dgram, k, 0, 0, 1)
            + mm(dscores, q, 0, 0, 1)
            + mm(u, leave, 1, 1, 1)
            - mm(by, state, 1, 1, 1)
        )
        dlogit_ref[0, :, h : h + 1] = (dbeta * beta * (1.0 - beta)).astype(bf16)
        dq = (dq - qu * jnp.sum(qu * dq, -1, keepdims=True)) * q_inv
        dk = (dk - ku * jnp.sum(ku * dk, -1, keepdims=True)) * k_inv
        for i, dact in enumerate((dq, dk, by)):
            shifts, out, sig, _ = parts[i]
            dconv = dact * sig * (1.0 + out * (1.0 - sig))
            ext = jnp.concatenate([zeros, dconv, zeros], 0)
            total = None
            for j in range(KW):
                at = i * KW + j
                dtaps_ref[0, at : at + 1, head_slice(h)] = jnp.sum(
                    dconv * shifts[j], 0, keepdims=True
                )
                tap = taps[at : at + 1, head_slice(h)]
                term = tap * ext[KW - 1 - j : KW - 1 - j + PAD + length]
                total = term if total is None else total + term
            first_ref[i, 0, :, head_slice(h)] = total[:PAD]
            last_ref[i, 0, :, head_slice(h)] = total[length:]
            dproj_ref[i, 0, :, head_slice(h)] = total[PAD:].astype(bf16)


def call(kernel, ins, outs, steps, scalar=None, scratch=(), limit=VMEM, alias=None):
    def spec(shape, axis):
        if axis == "any":
            return pl.BlockSpec(memory_space=pl.ANY)
        block = tuple(1 if n == axis else size for n, size in enumerate(shape))
        where = lambda s, *_: tuple(s if n == axis else 0 for n in range(len(shape)))
        if axis is None:
            return pl.BlockSpec(block, where, pipeline_mode=pl.Buffered(1))
        return pl.BlockSpec(block, where)

    given = [] if scalar is None else [scalar]
    return pl.pallas_call(
        kernel,
        grid_spec=pltpu.PrefetchScalarGridSpec(
            num_scalar_prefetch=len(given),
            grid=(steps,),
            in_specs=[spec(a.shape, axis) for a, axis in ins],
            out_specs=[spec(o.shape, axis) for o, axis in outs],
            scratch_shapes=scratch,
        ),
        out_shape=[o for o, _ in outs],
        input_output_aliases=alias or {},
        compiler_params=pltpu.CompilerParams(vmem_limit_bytes=limit),
    )(*given, *[a for a, _ in ins])


def shape_of(shape, dtype):
    return jax.ShapeDtypeStruct(shape, dtype)


def shifted(array, axis, by):
    devices = lax.axis_size(axis)
    pairs = [(i, i + by) for i in range(devices) if 0 <= i + by < devices]
    return lax.ppermute(array, axis, pairs)


def after(values, *others):
    flat, tree = jax.tree.flatten(values)
    others = jax.tree.leaves(others)
    here = pl.BlockSpec(memory_space=pl.ANY)
    out = pl.pallas_call(
        lambda *refs: None,
        in_specs=[here] * (len(flat) + len(others)),
        out_specs=[here] * len(flat),
        out_shape=[shape_of(a.shape, a.dtype) for a in flat],
        input_output_aliases={n: n for n in range(len(flat))},
    )(*flat, *others)
    return jax.tree.unflatten(tree, out)


def copies(values):
    count = len(values)

    def kernel(*refs):
        for n in range(count):
            refs[n - count][...] = refs[n][...]

    outs = [(shape_of(a.shape, a.dtype), None) for a in values]
    return call(kernel, [(a, None) for a in values], outs, 1)


def swap(array, bits):
    return lax.ppermute(array, "dp", [(i, i ^ bits) for i in range(4)])


def first_hop(own):
    return swap(own, 1), swap(own, 2)


def halves_of(hop, axis):
    low, high = (jnp.split(part, 2, axis) for part in hop)
    return low[0], high[1]


def gathered_pieces(own, axis, hop=None, halves=None):
    hop = hop or first_hop(own)
    low, high = halves or halves_of(hop, axis)
    return [own, *hop, swap(low, 2), swap(high, 1)]


def far_hop(low, high):
    return swap(low, 1), swap(high, 2)


def near_sums(pieces, far_in, *others):
    own, one, two = pieces
    half = far_in[0].shape
    along = 1 if half[1] < one.shape[1] else 2

    def spec(place):
        where = tuple(place if n == along else 0 for n in range(3))
        return pl.BlockSpec(half, lambda s: where)

    first, second = spec(0), spec(1)
    here = pl.BlockSpec(memory_space=pl.ANY)
    one, two = pl.pallas_call(
        add_halves_kernel,
        grid=(1,),
        in_specs=[second, first, first, first] + [here] * len(others),
        out_specs=[second, first],
        out_shape=[shape_of(a.shape, a.dtype) for a in (one, two)],
        input_output_aliases={0: 0, 1: 1},
        compiler_params=pltpu.CompilerParams(vmem_limit_bytes=VMEM),
    )(one, two, *far_in, *others)
    return own, one, two


def near_hop(pieces):
    own, one, two = pieces
    return own, swap(one, 1), swap(two, 2)


def add_pair_kernel(own_ref, one_ref, two_ref, *refs):
    gate_ref, out_ref = refs[-2:]
    inner = out_ref.shape[0]

    def added(i, rows):
        parts = (ref[i, rows].astype(f32) for ref in (own_ref, one_ref, two_ref))
        return sum(parts)

    gate_ref[...] = added(0, slice(None))
    for n in range(2):
        out_ref[:, n * inner : (n + 1) * inner] = added(1, slice(n * inner, (n + 1) * inner))


def sum_last(parts, *others):
    own = parts[0]
    ins = [(a, 0) for a in parts] + [(a, "any") for a in others]
    [total] = call(add_last_kernel, ins, [(shape_of(own.shape, f32), 0)], own.shape[0])
    return total


def pack(parts):
    return jnp.concatenate([p.reshape(-1) for p in parts])


def unpack(flat, shapes):
    out, at = [], 0
    for shape in shapes:
        size = 1
        for n in shape:
            size *= n
        out.append(flat[..., at : at + size].reshape(flat.shape[:-1] + tuple(shape)))
        at += size
    return out


def padded(flat, multiple=1024):
    return jnp.pad(flat, (0, -flat.shape[0] % multiple))


def body(
    tokens,
    out_grad,
    domain,
    group_weight,
    w_qkv,
    conv_weight,
    w_beta,
    w_outgate,
    head_gain,
    w_out,
    mixer_gain,
    mlp_gain,
    w_gateup,
    w_down,
):
    dp = lax.axis_size("dp")
    place = lax.axis_index("dp")
    seqs, block, local_width = tokens.shape
    count_rows = seqs * block
    heads = conv_weight.shape[2]
    inner = heads * DK
    column = lax.axis_index("mp") * local_width
    near_four = dp == 4

    def blocks_about(array, axis):
        if not near_four:
            return array
        size = array.shape[axis] // 4
        return jnp.concatenate(
            [lax.dynamic_slice_in_dim(array, (place ^ k) * size, size, axis) for k in range(4)],
            axis,
        )

    width = out_grad.shape[2]
    turn = place if near_four else jnp.int32(0)
    column_about = ((column // (width // 4)) ^ turn) * (width // 4) + column % (width // 4)

    def own(array):
        array = array.reshape(seqs, block, width)
        return lax.dynamic_slice_in_dim(array, column_about, local_width, 2)

    onehot = (domain[..., None] == jnp.arange(3, dtype=jnp.int32)).astype(f32)
    own_counts = jnp.sum(onehot, axis=(0, 1))
    high = jnp.floor(own_counts / 128.0)
    digits = jnp.concatenate([high, own_counts - 128.0 * high]).astype(bf16)
    small = [w_beta, conv_weight, head_gain, mixer_gain, mlp_gain, digits]
    packed = padded(pack(small))
    size = width // 4
    if near_four:
        qkv_hop = first_hop(w_qkv)
        qkv_halves = halves_of(qkv_hop, 1)
        qkv = gathered_pieces(w_qkv, 1, qkv_hop, qkv_halves)
        packed = after(packed, qkv_halves)
        gathered = jnp.stack([packed] + [swap(packed, bits) for bits in (1, 2, 3)])
        half = w_out.shape[1] // 2
        pair_own = jnp.stack(
            [w_outgate, jnp.concatenate([w_out[:, :half], w_out[:, half:]], 0)]
        )
        pair_layout = [(k, 0, size, size) for k in range(4)]
        layout = pair_layout[:3] + [(3, 0, size // 2, size), (3, size // 2, size // 2, size)]
    else:
        gathered = lax.all_gather(packed, "dp")
        qkv = [lax.all_gather(w_qkv, "dp", axis=1, tiled=True)]
        gate_pieces = [lax.all_gather(w_outgate, "dp", axis=0, tiled=True)]
        out_pieces = [lax.all_gather(w_out, "dp", axis=1, tiled=True)]
        layout = pair_layout = [(0, 0, width, width)]
    ranges = [(k * step + start, n) for k, start, n, step in layout]
    g_beta, g_conv, g_head, g_mix, g_mlp, g_digits = unpack(gathered, [a.shape for a in small])
    about_beta = g_beta.reshape(-1, heads)
    full_beta = blocks_about(about_beta, 0)
    full_conv = jnp.moveaxis(blocks_about(g_conv, 0), 0, 3).reshape(3 * KW, inner).astype(f32)
    gain_head = blocks_about(g_head, 0).reshape(1, DK).astype(f32)
    gain_one = blocks_about(g_mix.reshape(1, -1).astype(f32), 1)
    gain_two = g_mlp.reshape(1, -1).astype(f32)
    sums = jnp.sum(g_digits.astype(f32), 0)
    counts = 128.0 * sums[:3] + sums[3:]
    table = group_weight * (domain.shape[0] * domain.shape[1] * dp) / counts
    factor = jnp.sum(onehot * table, -1)[..., None]

    def flat(array):
        return array.reshape(array.shape[:-3] + (count_rows, array.shape[-1]))

    rows = lax.all_gather(tokens, "mp", axis=2, tiled=True)
    if near_four:
        gate_pieces = out_pieces = [lax.all_gather(after(pair_own, packed), "dp")]
    turn_one = turn.reshape(1)
    per_token = (seqs, block)
    square = (seqs, heads, DK, DK)
    hidden_one, proj, tail, logits, scale_one = call(
        partial(project_kernel, layout),
        [(rows, 0), (gain_one, None), (jnp.pad(full_beta, ((0, 0), (0, 128 - heads))), None)]
        + [(a, None) for a in qkv],
        [
            (shape_of(per_token + (width,), bf16), 0),
            (shape_of((3,) + per_token + (inner,), bf16), 1),
            (shape_of((3, seqs, HALO, inner), bf16), 1),
            (shape_of(per_token + (heads,), f32), 0),
            (shape_of(per_token + (1,), f32), 0),
        ],
        seqs,
        scalar=turn_one,
        scratch=[pltpu.VMEM((block, width), bf16)],
    )
    before = shifted(tail, "dp", 1)
    inverse, wu, qo, to = call(
        pre_kernel,
        [(proj, None), (before, None), (full_conv, None), (logits, None)],
        [
            (shape_of((seqs, heads, block, block), f32), None),
            (shape_of((seqs, heads, block, 2 * DK), f32), None),
            (shape_of((seqs, heads, block, 2 * DK), f32), None),
            (shape_of((seqs, heads, DK, 2 * DK), bf16), None),
        ],
        1,
    )
    near = [shifted(to, "dp", c) for c in range(1, dp)]
    rows_about, cotangent = call(
        partial(prepare_kernel, layout),
        [(rows, 0), (out_grad, 0), (factor, 0)],
        [(shape_of(per_token + (width,), bf16), 0)] * 2,
        seqs,
        scalar=turn_one,
    )
    turned = jnp.swapaxes(w_gateup, 1, 2)
    feed_own = [turned, w_down]
    mixer_part, normed, rule, state, gates = call(
        partial(mix_kernel, pair_layout, len(near), len(out_pieces)),
        [(a, 0) for a in near]
        + [(qo, 0), (hidden_one, 0), (gain_head, None)]
        + [(a, None) for a in gate_pieces + out_pieces]
        + [(cotangent, "any")],
        [
            (shape_of(per_token + (width,), bf16), 0),
            (shape_of(per_token + (inner,), bf16), 0),
            (shape_of(per_token + (inner,), f32), 0),
            (shape_of(square, f32), 0),
            (shape_of(per_token + (inner,), f32), 0),
        ],
        seqs,
        scalar=turn_one,
    )
    total = lax.psum(mixer_part, "mp")
    nexts = [shifted(to[..., :DK], "dp", -c) for c in range(1, dp - 1)]
    if near_four:
        gateup, down = (gathered_pieces(a, a.ndim - 1) for a in after(copies(feed_own), mixer_part, nexts))
    else:
        gateup, down = (
            [lax.all_gather(a, "dp", axis=a.ndim - 1, tiled=True)] for a in feed_own
        )
    units = w_down.shape[0]
    two_part, hidden_two, hidden_mlp, grad_pair = call(
        partial(feed_kernel, layout),
        [(rows_about, 0), (total, 0), (cotangent, 0), (gain_two, None)]
        + [(a, None) for a in gateup + down],
        [
            (shape_of(per_token + (width,), bf16), 0),
            (shape_of(per_token + (width,), bf16), 0),
            (shape_of(per_token + (units,), bf16), 0),
            (shape_of((2,) + per_token + (units,), bf16), 1),
        ],
        seqs,
    )
    grad_two = lax.psum(two_part, "mp")

    def feed_gradients(some, left, right, came=(), others=()):
        base, span = some[0][0], sum(n for _, n in some)
        aligned = base % span == 0
        at = base // span if aligned else 0
        some = [(start - (base if aligned else 0), n) for start, n in some]
        parts, units = left.shape[0], left.shape[2]
        outs = [shape_of((parts, units, n), bf16) for _, n in some]
        return pl.pallas_call(
            partial(feed_gradient_kernel, some, len(came)),
            grid=(1,),
            in_specs=[
                pl.BlockSpec(left.shape, lambda s: (0, 0, 0)),
                pl.BlockSpec((count_rows, span if aligned else width), lambda s: (0, at)),
            ]
            + [pl.BlockSpec(a.shape, lambda s: (0, 0, 0)) for a in came]
            + [pl.BlockSpec(memory_space=pl.ANY)] * len(others),
            out_specs=[pl.BlockSpec(o.shape, lambda s: (0, 0, 0)) for o in outs],
            out_shape=outs,
            compiler_params=pltpu.CompilerParams(vmem_limit_bytes=VMEM),
        )(left, right, *came, *others)

    pair_left, mlp_left = flat(grad_pair), flat(hidden_mlp)[None]
    if near_four:
        far = [
            feed_gradients(ranges[3:], pair_left, flat(hidden_two)),
            feed_gradients(ranges[3:], mlp_left, flat(cotangent)),
        ]
        gateup_in, down_in = (far_hop(*part) for part in far)
        near_gateup = feed_gradients(
            ranges[:3], pair_left, flat(hidden_two), gateup_in, down_in
        )
        near_down = feed_gradients(
            ranges[:3], mlp_left, flat(cotangent), down_in, near_gateup[:1]
        )
        first_made = [(near_down[0], "any")]
        gateup_sums, down_sums = near_hop(near_gateup), near_hop(near_down)
        held = [(a, "any") for a in gateup_sums[1:]]
    else:
        [grad_gateup] = feed_gradients(ranges, pair_left, flat(hidden_two))
        [grad_down] = feed_gradients(ranges, mlp_left, flat(cotangent))
        held = first_made = []
    [down_part] = call(
        partial(down_kernel, layout),
        [(hidden_mlp, 0)] + [(a, None) for a in down] + first_made,
        [(shape_of(per_token + (width,), bf16), 0)],
        seqs,
        scalar=turn_one,
    )
    mlp_share = lax.psum_scatter(down_part, "mp", scatter_dimension=2, tiled=True)
    grad_mix, middle_own, mlpgain, drule, dgate, dgain, direct = call(
        partial(middle_back_kernel, pair_layout, len(out_pieces)),
        [
            (grad_two, 0),
            (cotangent, 0),
            (rows_about, 0),
            (total, 0),
            (gain_two, None),
            (rule, 0),
            (gates, 0),
            (gain_head, None),
            (qo, 0),
        ]
        + [(a, None) for a in out_pieces]
        + [(down_part, "any")]
        + held,
        [
            (shape_of(per_token + (width,), bf16), 0),
            (shape_of(per_token + (local_width,), f32), 0),
            (shape_of((seqs, 1, width), f32), 0),
            (shape_of(per_token + (inner,), f32), 0),
            (shape_of(per_token + (inner,), bf16), 0),
            (shape_of((seqs, 1, DK), f32), 0),
            (shape_of(square, bf16), 0),
        ],
        seqs,
        scalar=jnp.stack([turn, column_about]),
        scratch=[pltpu.VMEM((block, width), f32)],
    )
    directs = [shifted(direct, "dp", -c) for c in range(1, dp)]
    if near_four:
        pair_grads = call(
            partial(pair_gradient_kernel, [(k * size, size) for k in range(4)]),
            [(flat(a), None) for a in (hidden_one, dgate, normed, grad_mix)],
            [(shape_of((2, size, inner), bf16), None)] * 4,
            1,
        )
        pair_in = far_hop(*jnp.split(pair_grads[3], 2, 1))
        held = [(a, "any") for a in (pair_grads[3], *down_sums[1:])]
    else:
        grad_outgate = jnp.einsum(
            "td,tc->dc", flat(hidden_one), flat(dgate), preferred_element_type=f32
        )
        grad_outproj = jnp.einsum(
            "tc,td->cd", flat(normed), flat(grad_mix), preferred_element_type=f32
        )
        held = []
    dproj, last, first, dtaps, dlogits = call(
        partial(back_kernel, len(directs)),
        [
            (proj, 1),
            (before, 1),
            (full_conv, None),
            (logits, 0),
            (inverse, 0),
            (wu, 0),
            (state, 0),
            (drule, 0),
        ]
        + [(a, 0) for a in directs + nexts]
        + held,
        [
            (shape_of((3,) + per_token + (inner,), bf16), 1),
            (shape_of((3, seqs, PAD, inner), f32), 1),
            (shape_of((3, seqs, PAD, inner), f32), 1),
            (shape_of((seqs, 3 * KW, inner), f32), 0),
            (shape_of(per_token + (heads,), bf16), 0),
        ],
        seqs,
    )
    later = shifted(first, "dp", -1)
    dproj = lax.dynamic_update_slice(dproj, (last + later).astype(bf16), (0, 0, block - PAD, 0))
    one_low, row_part, gain_part = call(
        partial(first_back_kernel, layout, pair_layout, len(gate_pieces)),
        [
            (flat(dproj), None),
            (flat(dgate), None),
            (flat(dlogits), None),
            (flat(proj), None),
            (flat(gates), None),
            (flat(logits), None),
            (about_beta.T.astype(f32), None),
            (flat(rows_about), None),
            (flat(scale_one), None),
        ]
        + [(a, None) for a in qkv + gate_pieces]
        + [(mlp_share, "any")]
        + ([(a, "any") for a in pair_in] if near_four else []),
        [
            (shape_of((count_rows, width), bf16), None),
            (shape_of((count_rows, 1), f32), None),
            (shape_of((1, width), f32), None),
        ],
        1,
        scalar=turn_one,
    )
    one_share = lax.psum_scatter(
        one_low.reshape(seqs, block, width), "mp", scatter_dimension=2, tiled=True
    ).astype(f32)
    made = call(
        partial(qkv_gradient_kernel, ranges),
        [(flat(hidden_one), None), (flat(dproj), None), (flat(dlogits), None), (row_part, "any")],
        [(shape_of((3, n, inner), bf16), None) for _, n in ranges]
        + [(shape_of((heads, width), f32), None)],
        1,
    )

    def pieces(array, axis, about):
        shape = array.shape
        cut = array.reshape(shape[:axis] + (dp, shape[axis] // dp) + shape[axis + 1 :])
        cut = jnp.moveaxis(cut, axis, 0).reshape(dp, -1)
        return blocks_about(cut, 0) if about else cut

    shared = [row_part[:, 0], gain_part[0], jnp.sum(dgain, (0, 1))]
    packed_shared = pack(shared)
    if near_four:
        gateup_total = sum_last(gateup_sums, made[0])
        down_total = sum_last(down_sums, made[0])
        own_qkv, *near_qkv = near_sums(made[:3], far_hop(made[3], made[4]), gateup_total, down_total)
        packed_shared = after(packed_shared, near_qkv)
    everyone = lax.optimization_barrier(lax.all_gather(packed_shared, "mp"))
    row_sum, mixgain, headgain = unpack(jnp.sum(everyone, 0), [a.shape for a in shared])
    smalls = jnp.concatenate(
        [
            pieces(jnp.sum(dtaps, 0).reshape(3, KW, heads, DK), 3, True),
            pieces(made[-1].T, 0, False),
            pieces(headgain, 0, True),
            pieces(mixgain, 0, False),
            pieces(jnp.sum(mlpgain, (0, 1)), 0, False),
        ],
        1,
    )
    if near_four:
        smalls = jnp.pad(smalls, ((0, 0), (0, -smalls.shape[1] % 1024))).reshape(dp, -1, 128)
        sent = smalls.astype(bf16)
        got = [swap(sent[bits], bits) for bits in (1, 2, 3)]
        sum_qkv = sum_last(near_hop((own_qkv, *near_qkv)))
        [mine] = call(
            add_small_kernel,
            [(a, None) for a in [smalls[0]] + got] + [(sum_qkv, "any")],
            [(shape_of(smalls.shape[1:], f32), None)],
            1,
        )
        mine = mine.reshape(-1)
        sum_gateup = jnp.swapaxes(gateup_total, 1, 2)
        sum_down = down_total[0]
        pair_near = near_sums(pair_grads[:3], pair_in, *near_qkv)[1:]
        sum_outgate, sum_out = call(
            add_pair_kernel,
            [(a, None) for a in near_hop((pair_grads[0], *pair_near))],
            [(shape_of(w_outgate.shape, f32), None), (shape_of(w_out.shape, f32), None)],
            1,
        )
    else:
        gathered = lax.all_gather(smalls.astype(bf16), "dp")
        mine = jnp.sum(
            lax.dynamic_index_in_dim(gathered, place, 1, keepdims=False).astype(f32), 0
        )

        def scattered(array, axis):
            return lax.psum_scatter(array, "dp", scatter_dimension=axis, tiled=True).astype(f32)

        sum_qkv = scattered(made[0], 1)
        sum_outgate = scattered(grad_outgate.astype(bf16), 0)
        sum_out = scattered(grad_outproj.astype(bf16), 1)
        sum_gateup = jnp.swapaxes(scattered(grad_gateup, 2), 1, 2)
        sum_down = scattered(grad_down[0], 1)
    sum_conv, sum_beta, sum_head, sum_mix, sum_mlp = unpack(
        mine,
        [conv_weight.shape, w_beta.shape, head_gain.shape, mixer_gain.shape, mlp_gain.shape],
    )

    own_tokens = tokens.astype(f32)
    mixed_out = (own_tokens + own(total).astype(f32) + mlp_share.astype(f32)).astype(bf16)
    row_mean = (row_sum / width).reshape(seqs, block, 1)
    gain_own = lax.dynamic_slice_in_dim(gain_one, column, local_width, 1)
    tokens_grad = middle_own + scale_one * (
        one_share * gain_own - own_tokens * scale_one * row_mean
    )
    return (
        mixed_out,
        tokens_grad.astype(bf16),
        sum_qkv,
        sum_conv,
        sum_beta,
        sum_outgate,
        sum_head,
        sum_out,
        sum_mix,
        sum_mlp,
        sum_gateup,
        sum_down,
    )


def solution(mesh):
    return jax.shard_map(
        body,
        mesh=mesh,
        in_specs=(
            P(None, "dp", "mp"),
            P(None, "dp", None),
            P(None, "dp"),
            P(),
            P(None, "dp", "mp"),
            P(None, None, "mp", "dp"),
            P("dp", "mp"),
            P("dp", "mp"),
            P("dp"),
            P("mp", "dp"),
            P("dp"),
            P("dp"),
            P(None, "dp", "mp"),
            P("mp", "dp"),
        ),
        out_specs=(
            P(None, "dp", "mp"),
            P(None, "dp", "mp"),
            P(None, "dp", "mp"),
            P(None, None, "mp", "dp"),
            P("dp", "mp"),
            P("dp", "mp"),
            P("dp"),
            P("mp", "dp"),
            P("dp"),
            P("dp"),
            P(None, "dp", "mp"),
            P("mp", "dp"),
        ),
        check_vma=False,
    )
```

```python
from functools import partial

import jax
import jax.numpy as jnp
from jax import lax
from jax.experimental import pallas as pl
from jax.experimental.pallas import tpu as pltpu
from jax.sharding import PartitionSpec as P

DK = 128
KW = 4
PAD = 8
HALO = 16
VMEM = 58 * 2**20
FREE = pl.CostEstimate(flops=0, transcendentals=0, bytes_accessed=0)

eps_norm = 1e-06
eps_unit = 1e-06

f32 = jnp.float32
bf16 = jnp.bfloat16


def split(v):
    if v.dtype == bf16:
        return v, None
    high = v.astype(bf16)
    return high, (v - high.astype(f32)).astype(bf16)


def mm(a, b, ca=1, cb=0, passes=3):
    def one(x, y):
        return lax.dot_general(x, y, (((ca,), (cb,)), ((), ())), preferred_element_type=f32)

    if passes == 1:
        return one(a.astype(bf16), b.astype(bf16))
    (ah, al), (bh, bl) = split(a), split(b)
    out = one(ah, bh)
    if bl is not None:
        out = out + one(ah, bl)
    if al is not None:
        out = out + one(al, bh)
    return out


def places(rows, cols):
    return (
        lax.broadcasted_iota(jnp.int32, (rows, cols), 0),
        lax.broadcasted_iota(jnp.int32, (rows, cols), 1),
    )


def unit_lower_inverses(blocks):
    size = blocks[0].shape[0]
    if size > 128:
        half = size // 2
        parts = unit_lower_inverses(
            [a[:half, :half] for a in blocks] + [a[half:, half:] for a in blocks]
        )
        firsts, seconds = parts[: len(blocks)], parts[len(blocks) :]
        inner = [mm(a[half:, :half], x) for a, x in zip(blocks, firsts)]
        lower = [-mm(x, y) for x, y in zip(seconds, inner)]
        zero = jnp.zeros((half, half), f32)
        return [
            jnp.concatenate(
                [jnp.concatenate([x, zero], 1), jnp.concatenate([y, z], 1)], 0
            )
            for x, y, z in zip(firsts, lower, seconds)
        ]
    rows, cols = places(size, size)
    eye = (rows == cols).astype(f32)
    level = 0
    inverses = None
    while (1 << level) < size:
        mask = (
            ((rows >> (level + 1)) == (cols >> (level + 1)))
            & (((rows >> level) & 1) == 1)
            & (((cols >> level) & 1) == 0)
        ).astype(f32)
        lows = [a * mask for a in blocks]
        if level == 0:
            inverses = [eye - low for low in lows]
        else:
            inner = [mm(low, x) for low, x in zip(lows, inverses)]
            inverses = [x - mm(x, y) for x, y in zip(inverses, inner)]
        level += 1
    return inverses


def head_slice(h):
    return slice(h * DK, (h + 1) * DK)


def convolve(proj_ref, before_ref, taps, i, h):
    own = proj_ref[i, 0, :, head_slice(h)].astype(f32)
    length = own.shape[0]
    ext = jnp.concatenate([before_ref[i, 0, :, head_slice(h)].astype(f32), own], 0)
    shifts = [ext[HALO - KW + 1 + j : HALO - KW + 1 + j + length] for j in range(KW)]
    out = None
    for j in range(KW):
        tap = taps[i * KW + j : i * KW + j + 1, head_slice(h)]
        out = tap * shifts[j] if out is None else out + tap * shifts[j]
    sig = jax.nn.sigmoid(out)
    return shifts, out, sig, out * sig


def unit(acts):
    inv = lax.rsqrt(jnp.sum(acts * acts, -1, keepdims=True) + eps_unit)
    return acts * inv, inv


def rule_inputs(proj_ref, before_ref, taps, h):
    parts = [convolve(proj_ref, before_ref, taps, i, h) for i in range(3)]
    q, q_inv = unit(parts[0][3])
    k, k_inv = unit(parts[1][3])
    return parts, (q, q_inv), (k, k_inv), parts[2][3]


def norm_factor(values):
    return lax.rsqrt(jnp.mean(values * values, -1, keepdims=True) + eps_norm)


def project_kernel(layout, *refs):
    place_ref, rows_ref, gain_ref, beta_ref = refs[:4]
    pieces = refs[4 : 4 + len(layout)]
    hidden_ref, proj_ref, tail_ref, logit_ref, scale_ref, keep_ref = refs[4 + len(layout) :]
    rows = rows_ref[0].astype(f32)
    scale = norm_factor(rows)
    scale_ref[0] = scale
    keep_ref[...] = (rows * scale * gain_ref[...]).astype(bf16)
    logits = mm(keep_ref[...], beta_ref[...])
    logit_ref[0] = logits[:, : logit_ref.shape[2]]
    sums = [None] * 3
    for (k, start, size, block), piece in zip(layout, pieces):
        at = pl.multiple_of((place_ref[0] ^ k) * block + start, 128)
        part = keep_ref[:, pl.ds(at, size)]
        hidden_ref[0, :, k * block + start : k * block + start + size] = part
        for i in range(3):
            term = mm(part, piece[i])
            sums[i] = term if sums[i] is None else sums[i] + term
    for i in range(3):
        low = sums[i].astype(bf16)
        proj_ref[i, 0] = low
        tail_ref[i, 0] = low[low.shape[0] - HALO :]


def pre_kernel(proj_ref, before_ref, taps_ref, logit_ref, x_ref, wu_ref, qo_ref, to_ref):
    seqs, heads = to_ref.shape[:2]
    taps = taps_ref[...]
    length = proj_ref.shape[2]
    r, c = places(length, length)
    strict = (r > c).astype(f32)
    full = (r >= c).astype(f32)
    saved, blocks = [], []
    for s in range(seqs):
        betas = jax.nn.sigmoid(logit_ref[s])
        rows, before = proj_ref.at[:, s : s + 1], before_ref.at[:, s : s + 1]
        for h in range(heads):
            _, (q, _), (k, _), v = rule_inputs(rows, before, taps, h)
            q, k, v = q.astype(bf16), k.astype(bf16), v.astype(bf16)
            beta = betas[:, h : h + 1]
            blocks.append(beta * mm(k, k, 1, 1) * strict)
            saved.append((s, h, q, k, v, beta))
    inverses = unit_lower_inverses(blocks)
    r, c = places(DK, DK)
    eye = (r == c).astype(f32)
    for (s, h, q, k, v, beta), x in zip(saved, inverses):
        x_ref[s, h] = x
        kv = jnp.concatenate([k.astype(f32), v.astype(f32)], 1) * beta
        wu = mm(x, kv)
        wu_ref[s, h] = wu
        scores = mm(q, k, 1, 1) * full
        pwu = mm(scores, wu)
        qo_ref[s, h, :, :DK] = q.astype(f32) - pwu[:, :DK]
        qo_ref[s, h, :, DK:] = pwu[:, DK:]
        kwu = mm(k, wu, 0, 0)
        to_ref[s, h, :, :DK] = (eye - kwu[:, :DK]).astype(bf16)
        to_ref[s, h, :, DK:] = kwu[:, DK:].astype(bf16)


def by_piece(place_ref, refs):
    if len(refs) > 1 or len(refs[0].shape) < 4:
        return refs
    return [refs[0].at[place_ref[0] ^ k] for k in range(4)]


def gate_part(ref):
    return ref.at[0] if len(ref.shape) == 3 else ref


def out_columns(layout, refs):
    for (k, start, size, block), ref in zip(layout, refs):
        at, half = k * block + start, size // 2
        if len(ref.shape) == 2:
            yield at, size, ref
            continue
        inner = ref.shape[1] // 2
        yield at, half, ref.at[1, :inner]
        yield at + half, half, ref.at[1, inner:]


def mix_kernel(layout, count, pieces, place_ref, *refs):
    near, rest = refs[:count], refs[count:]
    qo_ref, hidden_ref, gain_ref = rest[:3]
    gate_pieces = by_piece(place_ref, rest[3 : 3 + pieces])
    outs = by_piece(place_ref, rest[3 + pieces : 3 + 2 * pieces])
    part_ref, normed_ref, rule_ref, state_ref, gate_ref = rest[-5:]
    gates = None
    for (k, start, size, block), ref in zip(layout, gate_pieces):
        at = k * block + start
        term = mm(hidden_ref[0, :, at : at + size], gate_part(ref)[...])
        gates = term if gates is None else gates + term
    gate_ref[0] = gates
    heads = state_ref.shape[1]
    for h in range(heads):
        state = near[-1][0, h, :, DK:].astype(f32)
        for ref in reversed(near[:-1]):
            state = mm(ref[0, h, :, :DK], state) + ref[0, h, :, DK:].astype(f32)
        state_ref[0, h] = state
        qo = qo_ref[0, h]
        out = (mm(qo[:, :DK], state) + qo[:, DK:]) * DK ** (-0.5)
        rule_ref[0, :, head_slice(h)] = out
        gate = gate_ref[0, :, head_slice(h)]
        normed = out * norm_factor(out) * gain_ref[...] * (gate * jax.nn.sigmoid(gate))
        normed_ref[0, :, head_slice(h)] = normed.astype(bf16)
    for at, size, ref in out_columns(layout, outs):
        part_ref[0, :, at : at + size] = mm(normed_ref[0], ref[...]).astype(bf16)


def prepare_kernel(layout, place_ref, rows_ref, grad_ref, factor_ref, about_ref, cot_ref):
    for k, start, size, block in layout:
        at = pl.multiple_of((place_ref[0] ^ k) * block + start, 128)
        to = slice(k * block + start, k * block + start + size)
        about_ref[0, :, to] = rows_ref[0, :, pl.ds(at, size)]
        grad = grad_ref[0, :, pl.ds(at, size)].astype(f32) * factor_ref[0]
        cot_ref[0, :, to] = grad.astype(bf16)


def down_kernel(layout, place_ref, mlp_ref, *refs):
    part_ref = refs[-1]
    for (k, start, size, block), ref in zip(layout, refs):
        at = pl.multiple_of((place_ref[0] ^ k) * block + start, 128)
        part_ref[0, :, pl.ds(at, size)] = mm(mlp_ref[0], ref[...]).astype(bf16)


def feed_gradient_kernel(base, ranges, hidden_ref, cot_ref, pair_ref, mlp_ref, *outs):
    outs = outs[-2 * len(ranges) :]
    for n, (start, size) in enumerate(ranges):
        start = start - base
        hidden = hidden_ref[:, start : start + size]
        outs[2 * n][0] = mm(pair_ref[0], hidden, 0, 0).astype(bf16)
        outs[2 * n][1] = mm(pair_ref[1], hidden, 0, 0).astype(bf16)
        outs[2 * n + 1][0] = mm(mlp_ref[...], cot_ref[:, start : start + size], 0, 0).astype(bf16)


def qkv_gradient_kernel(ranges, hidden_ref, dproj_ref, dlogit_ref, *outs):
    outs = outs[-len(ranges) - 1 :]
    for (start, size), out in zip(ranges, outs[:-1]):
        hidden = hidden_ref[:, start : start + size]
        for i in range(3):
            out[i] = mm(hidden, dproj_ref[i], 0, 0).astype(bf16)
    outs[-1][...] = mm(dlogit_ref[...], hidden_ref[...], 0, 0)


def pair_gradient_kernel(ranges, hidden_ref, dgate_ref, normed_ref, mix_ref, *outs):
    inner = normed_ref.shape[1]
    for (start, size), out in zip(ranges, outs):
        out[0] = mm(hidden_ref[:, start : start + size], dgate_ref[...], 0, 0).astype(bf16)
        for n in range(2):
            at = start + n * size // 2
            mix = mix_ref[:, at : at + size // 2]
            out[1, n * inner : (n + 1) * inner] = mm(normed_ref[...], mix, 0, 0).astype(bf16)


def add_halves_kernel(*refs):
    one_ref, two_ref, low_ref, high_ref, one_out, two_out = refs[:4] + refs[-2:]
    one_out[...] = (one_ref[...].astype(f32) + high_ref[...].astype(f32)).astype(bf16)
    two_out[...] = (two_ref[...].astype(f32) + low_ref[...].astype(f32)).astype(bf16)


def add_small_kernel(*refs):
    refs[-1][...] = sum(ref[...].astype(f32) for ref in refs[:-1])


def add_last_kernel(*refs):
    own_ref, one_ref, two_ref, out_ref = refs[:3] + refs[-1:]
    out_ref[...] = own_ref[...].astype(f32) + one_ref[...].astype(f32) + two_ref[...].astype(f32)


def feed_kernel(layout, *refs):
    rows_ref, total_ref, cot_ref, gain_ref = refs[:4]
    count = len(layout)
    gateups, downs = (refs[4 + n * count : 4 + (n + 1) * count] for n in range(2))
    two_ref, hidden_ref, mlp_ref, pair_ref = refs[-4:]
    middle = rows_ref[0].astype(f32) + total_ref[0].astype(f32)
    hidden_ref[0] = (middle * norm_factor(middle) * gain_ref[...]).astype(bf16)
    gate, up, grad = None, None, None
    for (k, start, size, block), w_gateup, w_down in zip(layout, gateups, downs):
        lanes = slice(k * block + start, k * block + start + size)
        hidden = hidden_ref[0, :, lanes]
        terms = (
            mm(hidden, w_gateup[0], 1, 1),
            mm(hidden, w_gateup[1], 1, 1),
            mm(cot_ref[0, :, lanes], w_down[...], 1, 1),
        )
        if gate is None:
            gate, up, grad = terms
        else:
            gate, up, grad = gate + terms[0], up + terms[1], grad + terms[2]
    sig = jax.nn.sigmoid(gate)
    silu = gate * sig
    mlp_ref[0] = (silu * up).astype(bf16)
    first = (grad * up * (sig + silu * (1.0 - sig))).astype(bf16)
    second = (grad * silu).astype(bf16)
    pair_ref[0, 0] = first
    pair_ref[1, 0] = second
    for (k, start, size, block), w_gateup in zip(layout, gateups):
        lanes = slice(k * block + start, k * block + start + size)
        two = mm(first, w_gateup[0]) + mm(second, w_gateup[1])
        two_ref[0, :, lanes] = two.astype(bf16)


def middle_back_kernel(layout, pieces, at_ref, *refs):
    two_ref, cot_ref, rows_ref, total_ref, gain_ref, rule_ref, gate_ref, head_gain_ref, qo_ref = refs[:9]
    outs = by_piece(at_ref, refs[9 : 9 + pieces])
    mix_ref, own_ref, mlpgain_ref, drule_ref, dgate_ref, dgain_ref, direct_ref, keep_ref = refs[-8:]
    middle = rows_ref[0].astype(f32) + total_ref[0].astype(f32)
    factor = norm_factor(middle)
    normal = middle * factor
    two = two_ref[0].astype(f32)
    mlpgain_ref[0] = jnp.sum(two * normal, 0, keepdims=True)
    scaled = two * gain_ref[...]
    mean = jnp.mean(scaled * normal, -1, keepdims=True)
    keep_ref[...] = cot_ref[0].astype(f32) + factor * (scaled - normal * mean)
    width = own_ref.shape[2]
    own_ref[0] = keep_ref[:, pl.ds(pl.multiple_of(at_ref[1], 128), width)]
    mix_ref[0] = keep_ref[...].astype(bf16)
    grads = None
    for at, size, ref in out_columns(layout, outs):
        term = mm(mix_ref[0, :, at : at + size], ref[...], 1, 1)
        grads = term if grads is None else grads + term
    total = jnp.zeros((1, DK), f32)
    for h in range(direct_ref.shape[1]):
        grad = grads[:, head_slice(h)]
        out = rule_ref[0, :, head_slice(h)]
        gate = gate_ref[0, :, head_slice(h)]
        inv = norm_factor(out)
        n = out * inv
        sig = jax.nn.sigmoid(gate)
        silu = gate * sig
        gg = grad * head_gain_ref[...]
        dn = gg * silu
        drule = inv * (dn - n * jnp.mean(dn * n, -1, keepdims=True))
        drule_ref[0, :, head_slice(h)] = drule
        dgate = gg * n * sig * (1.0 + gate * (1.0 - sig))
        dgate_ref[0, :, head_slice(h)] = dgate.astype(bf16)
        total = total + jnp.sum(grad * n * silu, 0, keepdims=True)
        direct = mm(qo_ref[0, h, :, :DK], drule, 0, 0) * DK ** (-0.5)
        direct_ref[0, h] = direct.astype(bf16)
    dgain_ref[0] = total


def first_back_kernel(layout, pair_layout, count, place_ref, *refs):
    dproj_ref, dgate_ref, dlogit_ref, proj_ref, gate_ref, logit_ref, beta_ref, rows_ref, scale_ref = refs[:9]
    pieces = refs[9 : 9 + len(layout)]
    pairs = by_piece(place_ref, refs[9 + len(layout) : 9 + len(layout) + count])
    one_ref, rowsum_ref, gainsum_ref = refs[-3:]
    gates = {}
    for (k, start, size, block), ref in zip(pair_layout, pairs):
        gates[k] = ref
    for (k, start, size, block), piece in zip(layout, pieces):
        lanes = slice(k * block + start, k * block + start + size)
        grad = mm(dgate_ref[...], gate_part(gates[k])[start : start + size], 1, 1)
        for i in range(3):
            grad = grad + mm(dproj_ref[i], piece[i], 1, 1)
        for h in range(beta_ref.shape[0]):
            grad = grad + dlogit_ref[:, h : h + 1].astype(f32) * beta_ref[h : h + 1, lanes]
        at = pl.multiple_of((place_ref[0] ^ k) * block + start, 128)
        one_ref[:, pl.ds(at, size)] = grad.astype(bf16)
        gainsum_ref[:, lanes] = jnp.sum(
            grad * (rows_ref[:, lanes].astype(f32) * scale_ref[...]), 0, keepdims=True
        )
    total = dgate_ref[...].astype(f32) * gate_ref[...]
    for i in range(3):
        total = total + dproj_ref[i].astype(f32) * proj_ref[i].astype(f32)
    total = jnp.sum(total, -1, keepdims=True)
    logits = dlogit_ref[...].astype(f32) * logit_ref[...]
    rowsum_ref[...] = total + jnp.sum(logits, -1, keepdims=True)


def back_kernel(count, *refs):
    (
        proj_ref,
        before_ref,
        taps_ref,
        logit_ref,
        x_ref,
        wu_ref,
        state_ref,
        drule_ref,
    ) = refs[:8]
    dproj_ref, last_ref, first_ref, dtaps_ref, dlogit_ref = refs[-5:]
    others = refs[8 : 8 + 2 * count - 1]
    directs, nexts = others[:count], others[count:]
    heads = state_ref.shape[1]
    taps = taps_ref[...]
    length = proj_ref.shape[2]
    betas = jax.nn.sigmoid(logit_ref[0])
    r, c = places(length, length)
    strict = (r > c).astype(f32)
    full = (r >= c).astype(f32)
    zeros = jnp.zeros((PAD, DK), f32)
    for h in range(heads):
        parts, (qu, q_inv), (ku, k_inv), vu = rule_inputs(proj_ref, before_ref, taps, h)
        q, k, v = qu.astype(bf16), ku.astype(bf16), vu.astype(bf16)
        beta = betas[:, h : h + 1]
        leave = jnp.zeros((DK, DK), f32)
        for j in reversed(range(count)):
            here = directs[j][0, h].astype(f32)
            leave = here if j == count - 1 else mm(nexts[j][0, h], leave, 0, 0) + here
        state = state_ref[0, h]
        wu = wu_ref[0, h]
        u = wu[:, DK:] - mm(wu[:, :DK], state)
        resid = v.astype(f32) - mm(k, state)
        dout = drule_ref[0, :, head_slice(h)] * DK ** (-0.5)
        gram = mm(k, k, 1, 1)
        scores = mm(q, k, 1, 1) * full
        du = mm(scores, dout, 0, 0) + mm(k, leave)
        y = mm(x_ref[0, h], du, 0, 0)
        by = beta * y
        da = -(mm(y, u, 1, 1, 1) * strict)
        dbeta = jnp.sum(y * resid, -1, keepdims=True) + jnp.sum(da * gram, -1, keepdims=True)
        dgram = beta * da
        dscores = mm(dout, u, 1, 1, 1) * full
        dq = mm(dout, state, 1, 1, 1) + mm(dscores, k, 1, 0, 1)
        dk = (
            mm(dgram, k, 1, 0, 1)
            + mm(dgram, k, 0, 0, 1)
            + mm(dscores, q, 0, 0, 1)
            + mm(u, leave, 1, 1, 1)
            - mm(by, state, 1, 1, 1)
        )
        dlogit_ref[0, :, h : h + 1] = (dbeta * beta * (1.0 - beta)).astype(bf16)
        dq = (dq - qu * jnp.sum(qu * dq, -1, keepdims=True)) * q_inv
        dk = (dk - ku * jnp.sum(ku * dk, -1, keepdims=True)) * k_inv
        for i, dact in enumerate((dq, dk, by)):
            shifts, out, sig, _ = parts[i]
            dconv = dact * sig * (1.0 + out * (1.0 - sig))
            ext = jnp.concatenate([zeros, dconv, zeros], 0)
            total = None
            for j in range(KW):
                at = i * KW + j
                dtaps_ref[0, at : at + 1, head_slice(h)] = jnp.sum(
                    dconv * shifts[j], 0, keepdims=True
                )
                tap = taps[at : at + 1, head_slice(h)]
                term = tap * ext[KW - 1 - j : KW - 1 - j + PAD + length]
                total = term if total is None else total + term
            first_ref[i, 0, :, head_slice(h)] = total[:PAD]
            last_ref[i, 0, :, head_slice(h)] = total[length:]
            dproj_ref[i, 0, :, head_slice(h)] = total[PAD:].astype(bf16)


def call(kernel, ins, outs, steps, scalar=None, scratch=(), limit=VMEM, alias=None):
    def spec(shape, axis):
        if axis == "any":
            return pl.BlockSpec(memory_space=pl.ANY)
        block = tuple(1 if n == axis else size for n, size in enumerate(shape))
        where = lambda s, *_: tuple(s if n == axis else 0 for n in range(len(shape)))
        if axis is None:
            return pl.BlockSpec(block, where, pipeline_mode=pl.Buffered(1))
        return pl.BlockSpec(block, where)

    given = [] if scalar is None else [scalar]
    return pl.pallas_call(
        kernel,
        cost_estimate=FREE,
        grid_spec=pltpu.PrefetchScalarGridSpec(
            num_scalar_prefetch=len(given),
            grid=(steps,),
            in_specs=[spec(a.shape, axis) for a, axis in ins],
            out_specs=[spec(o.shape, axis) for o, axis in outs],
            scratch_shapes=scratch,
        ),
        out_shape=[o for o, _ in outs],
        input_output_aliases=alias or {},
        compiler_params=pltpu.CompilerParams(vmem_limit_bytes=limit),
    )(*given, *[a for a, _ in ins])


def shape_of(shape, dtype):
    return jax.ShapeDtypeStruct(shape, dtype)


def shifted(array, axis, by):
    devices = lax.axis_size(axis)
    pairs = [(i, i + by) for i in range(devices) if 0 <= i + by < devices]
    return lax.ppermute(array, axis, pairs)


def after(values, *others):
    flat, tree = jax.tree.flatten(values)
    others = jax.tree.leaves(others)
    here = pl.BlockSpec(memory_space=pl.ANY)
    out = pl.pallas_call(
        lambda *refs: None,
        cost_estimate=FREE,
        in_specs=[here] * (len(flat) + len(others)),
        out_specs=[here] * len(flat),
        out_shape=[shape_of(a.shape, a.dtype) for a in flat],
        input_output_aliases={n: n for n in range(len(flat))},
    )(*flat, *others)
    return jax.tree.unflatten(tree, out)


def copies(values):
    count = len(values)

    def kernel(*refs):
        for n in range(count):
            refs[n - count][...] = refs[n][...]

    outs = [(shape_of(a.shape, a.dtype), None) for a in values]
    return call(kernel, [(a, None) for a in values], outs, 1)


def swap(array, bits):
    return lax.ppermute(array, "dp", [(i, i ^ bits) for i in range(4)])


def first_hop(own):
    return swap(own, 1), swap(own, 2)


def halves_of(hop, axis):
    low, high = (jnp.split(part, 2, axis) for part in hop)
    return low[0], high[1]


def gathered_pieces(own, axis, hop=None, halves=None):
    hop = hop or first_hop(own)
    low, high = halves or halves_of(hop, axis)
    return [own, *hop, swap(low, 2), swap(high, 1)]


def far_hop(low, high):
    return swap(low, 1), swap(high, 2)


def near_sums(pieces, far_in, *others):
    own, one, two = pieces
    half = far_in[0].shape
    along = 1 if half[1] < one.shape[1] else 2

    def spec(place):
        where = tuple(place if n == along else 0 for n in range(3))
        return pl.BlockSpec(half, lambda s: where)

    first, second = spec(0), spec(1)
    here = pl.BlockSpec(memory_space=pl.ANY)
    one, two = pl.pallas_call(
        add_halves_kernel,
        cost_estimate=FREE,
        grid=(1,),
        in_specs=[second, first, first, first] + [here] * len(others),
        out_specs=[second, first],
        out_shape=[shape_of(a.shape, a.dtype) for a in (one, two)],
        input_output_aliases={0: 0, 1: 1},
        compiler_params=pltpu.CompilerParams(vmem_limit_bytes=VMEM),
    )(one, two, *far_in, *others)
    return own, one, two


def near_hop(pieces):
    own, one, two = pieces
    return own, swap(one, 1), swap(two, 2)


def add_pair_kernel(own_ref, one_ref, two_ref, *refs):
    gate_ref, out_ref = refs[-2:]
    inner = out_ref.shape[0]

    def added(i, rows):
        parts = (ref[i, rows].astype(f32) for ref in (own_ref, one_ref, two_ref))
        return sum(parts)

    gate_ref[...] = added(0, slice(None))
    for n in range(2):
        out_ref[:, n * inner : (n + 1) * inner] = added(1, slice(n * inner, (n + 1) * inner))


def sum_last(parts, *others):
    own = parts[0]
    ins = [(a, 0) for a in parts] + [(a, "any") for a in others]
    [total] = call(add_last_kernel, ins, [(shape_of(own.shape, f32), 0)], own.shape[0])
    return total


def pack(parts):
    return jnp.concatenate([p.reshape(-1) for p in parts])


def unpack(flat, shapes):
    out, at = [], 0
    for shape in shapes:
        size = 1
        for n in shape:
            size *= n
        out.append(flat[..., at : at + size].reshape(flat.shape[:-1] + tuple(shape)))
        at += size
    return out


def padded(flat, multiple=1024):
    return jnp.pad(flat, (0, -flat.shape[0] % multiple))


def body(
    tokens,
    out_grad,
    domain,
    group_weight,
    w_qkv,
    conv_weight,
    w_beta,
    w_outgate,
    head_gain,
    w_out,
    mixer_gain,
    mlp_gain,
    w_gateup,
    w_down,
):
    dp = lax.axis_size("dp")
    place = lax.axis_index("dp")
    seqs, block, local_width = tokens.shape
    count_rows = seqs * block
    heads = conv_weight.shape[2]
    inner = heads * DK
    column = lax.axis_index("mp") * local_width
    near_four = dp == 4

    def blocks_about(array, axis):
        if not near_four:
            return array
        size = array.shape[axis] // 4
        return jnp.concatenate(
            [lax.dynamic_slice_in_dim(array, (place ^ k) * size, size, axis) for k in range(4)],
            axis,
        )

    width = out_grad.shape[2]
    turn = place if near_four else jnp.int32(0)
    column_about = ((column // (width // 4)) ^ turn) * (width // 4) + column % (width // 4)

    def own(array):
        array = array.reshape(seqs, block, width)
        return lax.dynamic_slice_in_dim(array, column_about, local_width, 2)

    onehot = (domain[..., None] == jnp.arange(3, dtype=jnp.int32)).astype(f32)
    own_counts = jnp.sum(onehot, axis=(0, 1))
    high = jnp.floor(own_counts / 128.0)
    digits = jnp.concatenate([high, own_counts - 128.0 * high]).astype(bf16)
    small = [w_beta, conv_weight, head_gain, mixer_gain, mlp_gain, digits]
    packed = padded(pack(small))
    size = width // 4
    if near_four:
        qkv_hop = first_hop(w_qkv)
        qkv_halves = halves_of(qkv_hop, 1)
        qkv = gathered_pieces(w_qkv, 1, qkv_hop, qkv_halves)
        packed = after(packed, qkv_halves)
        gathered = jnp.stack([packed] + [swap(packed, bits) for bits in (1, 2, 3)])
        half = w_out.shape[1] // 2
        pair_own = jnp.stack(
            [w_outgate, jnp.concatenate([w_out[:, :half], w_out[:, half:]], 0)]
        )
        pair_layout = [(k, 0, size, size) for k in range(4)]
        layout = pair_layout[:3] + [(3, 0, size // 2, size), (3, size // 2, size // 2, size)]
    else:
        gathered = lax.all_gather(packed, "dp")
        qkv = [lax.all_gather(w_qkv, "dp", axis=1, tiled=True)]
        gate_pieces = [lax.all_gather(w_outgate, "dp", axis=0, tiled=True)]
        out_pieces = [lax.all_gather(w_out, "dp", axis=1, tiled=True)]
        layout = pair_layout = [(0, 0, width, width)]
    ranges = [(k * step + start, n) for k, start, n, step in layout]
    g_beta, g_conv, g_head, g_mix, g_mlp, g_digits = unpack(gathered, [a.shape for a in small])
    about_beta = g_beta.reshape(-1, heads)
    full_beta = blocks_about(about_beta, 0)
    full_conv = jnp.moveaxis(blocks_about(g_conv, 0), 0, 3).reshape(3 * KW, inner).astype(f32)
    gain_head = blocks_about(g_head, 0).reshape(1, DK).astype(f32)
    gain_one = blocks_about(g_mix.reshape(1, -1).astype(f32), 1)
    gain_two = g_mlp.reshape(1, -1).astype(f32)
    sums = jnp.sum(g_digits.astype(f32), 0)
    counts = 128.0 * sums[:3] + sums[3:]
    table = group_weight * (domain.shape[0] * domain.shape[1] * dp) / counts
    factor = jnp.sum(onehot * table, -1)[..., None]

    def flat(array):
        return array.reshape(array.shape[:-3] + (count_rows, array.shape[-1]))

    rows = lax.all_gather(tokens, "mp", axis=2, tiled=True)
    if near_four:
        gate_pieces = out_pieces = [lax.all_gather(after(pair_own, packed), "dp")]
    turn_one = turn.reshape(1)
    per_token = (seqs, block)
    square = (seqs, heads, DK, DK)
    hidden_one, proj, tail, logits, scale_one = call(
        partial(project_kernel, layout),
        [(rows, 0), (gain_one, None), (jnp.pad(full_beta, ((0, 0), (0, 128 - heads))), None)]
        + [(a, None) for a in qkv],
        [
            (shape_of(per_token + (width,), bf16), 0),
            (shape_of((3,) + per_token + (inner,), bf16), 1),
            (shape_of((3, seqs, HALO, inner), bf16), 1),
            (shape_of(per_token + (heads,), f32), 0),
            (shape_of(per_token + (1,), f32), 0),
        ],
        seqs,
        scalar=turn_one,
        scratch=[pltpu.VMEM((block, width), bf16)],
    )
    before = shifted(tail, "dp", 1)
    inverse, wu, qo, to = call(
        pre_kernel,
        [(proj, None), (before, None), (full_conv, None), (logits, None)],
        [
            (shape_of((seqs, heads, block, block), f32), None),
            (shape_of((seqs, heads, block, 2 * DK), f32), None),
            (shape_of((seqs, heads, block, 2 * DK), f32), None),
            (shape_of((seqs, heads, DK, 2 * DK), bf16), None),
        ],
        1,
    )
    near = [shifted(to, "dp", c) for c in range(1, dp)]
    rows_about, cotangent = call(
        partial(prepare_kernel, layout),
        [(rows, 0), (out_grad, 0), (factor, 0)],
        [(shape_of(per_token + (width,), bf16), 0)] * 2,
        seqs,
        scalar=turn_one,
    )
    turned = jnp.swapaxes(w_gateup, 1, 2)
    feed_own = [turned, w_down]
    mixer_part, normed, rule, state, gates = call(
        partial(mix_kernel, pair_layout, len(near), len(out_pieces)),
        [(a, 0) for a in near]
        + [(qo, 0), (hidden_one, 0), (gain_head, None)]
        + [(a, None) for a in gate_pieces + out_pieces]
        + [(cotangent, "any")],
        [
            (shape_of(per_token + (width,), bf16), 0),
            (shape_of(per_token + (inner,), bf16), 0),
            (shape_of(per_token + (inner,), f32), 0),
            (shape_of(square, f32), 0),
            (shape_of(per_token + (inner,), f32), 0),
        ],
        seqs,
        scalar=turn_one,
    )
    total = lax.psum(mixer_part, "mp")
    nexts = [shifted(to[..., :DK], "dp", -c) for c in range(1, dp - 1)]
    if near_four:
        gateup, down = (gathered_pieces(a, a.ndim - 1) for a in after(copies(feed_own), mixer_part, nexts))
    else:
        gateup, down = (
            [lax.all_gather(a, "dp", axis=a.ndim - 1, tiled=True)] for a in feed_own
        )
    units = w_down.shape[0]
    two_part, hidden_two, hidden_mlp, grad_pair = call(
        partial(feed_kernel, layout),
        [(rows_about, 0), (total, 0), (cotangent, 0), (gain_two, None)]
        + [(a, None) for a in gateup + down],
        [
            (shape_of(per_token + (width,), bf16), 0),
            (shape_of(per_token + (width,), bf16), 0),
            (shape_of(per_token + (units,), bf16), 0),
            (shape_of((2,) + per_token + (units,), bf16), 1),
        ],
        seqs,
    )
    grad_two = lax.psum(two_part, "mp")

    def feed_gradients(some, *others):
        outs = [(shape_of((m, units, n), bf16), None) for _, n in some for m in (2, 1)]
        base, span = some[0][0], sum(n for _, n in some)
        aligned = base % span == 0
        at = base // span if aligned else 0
        cols = pl.BlockSpec((count_rows, span if aligned else width), lambda s: (0, at))
        made = pl.pallas_call(
            partial(feed_gradient_kernel, base if aligned else 0, some),
            cost_estimate=FREE,
            grid=(1,),
            in_specs=[
                cols,
                cols,
                pl.BlockSpec((2, count_rows, units), lambda s: (0, 0, 0)),
                pl.BlockSpec((count_rows, units), lambda s: (0, 0)),
            ]
            + [pl.BlockSpec(memory_space=pl.ANY)] * len(others),
            out_specs=[pl.BlockSpec(o.shape, lambda s: (0, 0, 0)) for o, _ in outs],
            out_shape=[o for o, _ in outs],
            compiler_params=pltpu.CompilerParams(vmem_limit_bytes=VMEM),
        )(flat(hidden_two), flat(cotangent), flat(grad_pair), flat(hidden_mlp), *others)
        return made[::2], made[1::2]

    if near_four:
        feed_far = feed_gradients(ranges[3:])
        feed_in = [far_hop(*far) for far in feed_far]
        near_gateup, near_down = feed_gradients(ranges[:3], feed_far[0][0])
        gateup_added = near_sums(near_gateup, feed_in[0], *feed_in[1])
        down_added = near_sums(near_down, feed_in[1], gateup_added[1])
        first_made = [(down_added[1], "any")]
        gateup_sums, down_sums = near_hop(gateup_added), near_hop(down_added)
        held = [(a, "any") for a in gateup_sums[1:]]
    else:
        [grad_gateup], [grad_down] = feed_gradients(ranges)
        held = first_made = []
    [down_part] = call(
        partial(down_kernel, layout),
        [(hidden_mlp, 0)] + [(a, None) for a in down] + first_made,
        [(shape_of(per_token + (width,), bf16), 0)],
        seqs,
        scalar=turn_one,
    )
    mlp_share = lax.psum_scatter(down_part, "mp", scatter_dimension=2, tiled=True)
    grad_mix, middle_own, mlpgain, drule, dgate, dgain, direct = call(
        partial(middle_back_kernel, pair_layout, len(out_pieces)),
        [
            (grad_two, 0),
            (cotangent, 0),
            (rows_about, 0),
            (total, 0),
            (gain_two, None),
            (rule, 0),
            (gates, 0),
            (gain_head, None),
            (qo, 0),
        ]
        + [(a, None) for a in out_pieces]
        + [(down_part, "any")]
        + held,
        [
            (shape_of(per_token + (width,), bf16), 0),
            (shape_of(per_token + (local_width,), f32), 0),
            (shape_of((seqs, 1, width), f32), 0),
            (shape_of(per_token + (inner,), f32), 0),
            (shape_of(per_token + (inner,), bf16), 0),
            (shape_of((seqs, 1, DK), f32), 0),
            (shape_of(square, bf16), 0),
        ],
        seqs,
        scalar=jnp.stack([turn, column_about]),
        scratch=[pltpu.VMEM((block, width), f32)],
    )
    directs = [shifted(direct, "dp", -c) for c in range(1, dp)]
    if near_four:
        pair_grads = call(
            partial(pair_gradient_kernel, [(k * size, size) for k in range(4)]),
            [(flat(a), None) for a in (hidden_one, dgate, normed, grad_mix)],
            [(shape_of((2, size, inner), bf16), None)] * 4,
            1,
        )
        pair_in = far_hop(*jnp.split(pair_grads[3], 2, 1))
        held = [(a, "any") for a in (pair_grads[3], *down_sums[1:])]
    else:
        grad_outgate = jnp.einsum(
            "td,tc->dc", flat(hidden_one), flat(dgate), preferred_element_type=f32
        )
        grad_outproj = jnp.einsum(
            "tc,td->cd", flat(normed), flat(grad_mix), preferred_element_type=f32
        )
        held = []
    dproj, last, first, dtaps, dlogits = call(
        partial(back_kernel, len(directs)),
        [
            (proj, 1),
            (before, 1),
            (full_conv, None),
            (logits, 0),
            (inverse, 0),
            (wu, 0),
            (state, 0),
            (drule, 0),
        ]
        + [(a, 0) for a in directs + nexts]
        + held,
        [
            (shape_of((3,) + per_token + (inner,), bf16), 1),
            (shape_of((3, seqs, PAD, inner), f32), 1),
            (shape_of((3, seqs, PAD, inner), f32), 1),
            (shape_of((seqs, 3 * KW, inner), f32), 0),
            (shape_of(per_token + (heads,), bf16), 0),
        ],
        seqs,
    )
    later = shifted(first, "dp", -1)
    dproj = lax.dynamic_update_slice(dproj, (last + later).astype(bf16), (0, 0, block - PAD, 0))
    one_low, row_part, gain_part = call(
        partial(first_back_kernel, layout, pair_layout, len(gate_pieces)),
        [
            (flat(dproj), None),
            (flat(dgate), None),
            (flat(dlogits), None),
            (flat(proj), None),
            (flat(gates), None),
            (flat(logits), None),
            (about_beta.T.astype(f32), None),
            (flat(rows_about), None),
            (flat(scale_one), None),
        ]
        + [(a, None) for a in qkv + gate_pieces],
        [
            (shape_of((count_rows, width), bf16), None),
            (shape_of((count_rows, 1), f32), None),
            (shape_of((1, width), f32), None),
        ],
        1,
        scalar=turn_one,
    )
    one_share = lax.psum_scatter(
        one_low.reshape(seqs, block, width), "mp", scatter_dimension=2, tiled=True
    ).astype(f32)
    made = call(
        partial(qkv_gradient_kernel, ranges),
        [(flat(hidden_one), None), (flat(dproj), None), (flat(dlogits), None), (row_part, "any")],
        [(shape_of((3, n, inner), bf16), None) for _, n in ranges]
        + [(shape_of((heads, width), f32), None)],
        1,
    )

    def pieces(array, axis, about):
        shape = array.shape
        cut = array.reshape(shape[:axis] + (dp, shape[axis] // dp) + shape[axis + 1 :])
        cut = jnp.moveaxis(cut, axis, 0).reshape(dp, -1)
        return blocks_about(cut, 0) if about else cut

    smalls = jnp.concatenate(
        [
            pieces(jnp.sum(dtaps, 0).reshape(3, KW, heads, DK), 3, True),
            pieces(made[-1].T, 0, False),
            pieces(jnp.sum(mlpgain, (0, 1)), 0, False),
        ],
        1,
    )
    shared = [row_part[:, 0], blocks_about(gain_part[0], 0), jnp.sum(dgain, (0, 1))]
    packed_shared = pack(shared)
    if near_four:
        gateup_total = sum_last(gateup_sums, made[0])
        down_total = sum_last(down_sums, made[0])
        own_qkv, *near_qkv = near_sums(made[:3], far_hop(made[3], made[4]), gateup_total, down_total)
        pair_near = near_sums(pair_grads[:3], pair_in, *near_qkv)[1:]
        packed_shared = after(packed_shared, (*near_qkv, *pair_near))
        smalls = jnp.pad(smalls, ((0, 0), (0, -smalls.shape[1] % 1024))).reshape(dp, -1, 128)
        sent = smalls.astype(bf16)
        got = [swap(sent[bits], bits) for bits in (1, 2, 3)]
        [mine] = call(
            add_small_kernel,
            [(a, None) for a in [smalls[0]] + got],
            [(shape_of(smalls.shape[1:], f32), None)],
            1,
        )
        mine = mine.reshape(-1)
        sum_qkv = sum_last(near_hop((own_qkv, *near_qkv)))
        sum_gateup = jnp.swapaxes(gateup_total, 1, 2)
        sum_down = down_total[0]
        sum_outgate, sum_out = call(
            add_pair_kernel,
            [(a, None) for a in near_hop((pair_grads[0], *pair_near))],
            [(shape_of(w_outgate.shape, f32), None), (shape_of(w_out.shape, f32), None)],
            1,
        )
    else:
        gathered = lax.all_gather(smalls.astype(bf16), "dp")
        mine = jnp.sum(
            lax.dynamic_index_in_dim(gathered, place, 1, keepdims=False).astype(f32), 0
        )

        def scattered(array, axis):
            return lax.psum_scatter(array, "dp", scatter_dimension=axis, tiled=True).astype(f32)

        sum_qkv = scattered(made[0], 1)
        sum_outgate = scattered(grad_outgate.astype(bf16), 0)
        sum_out = scattered(grad_outproj.astype(bf16), 1)
        sum_gateup = jnp.swapaxes(scattered(grad_gateup, 2), 1, 2)
        sum_down = scattered(grad_down[0], 1)
    sum_conv, sum_beta, sum_mlp = unpack(
        mine, [conv_weight.shape, w_beta.shape, mlp_gain.shape]
    )
    everyone = lax.optimization_barrier(lax.all_gather(packed_shared, ("dp", "mp")))
    everyone = everyone.reshape(dp, -1, everyone.shape[1])
    group = lax.dynamic_index_in_dim(everyone, place, 0, keepdims=False)
    row_sum = jnp.sum(group[:, :count_rows], 0)
    _, mixgain, headgain = unpack(everyone, [a.shape for a in shared])

    def own_block(array):
        size = array.shape[2] // dp
        return jnp.sum(lax.dynamic_slice_in_dim(array, place * size, size, 2), (0, 1))

    sum_mix, sum_head = own_block(mixgain), own_block(headgain)

    own_tokens = tokens.astype(f32)
    mixed_out = (own_tokens + own(total).astype(f32) + mlp_share.astype(f32)).astype(bf16)
    row_mean = (row_sum / width).reshape(seqs, block, 1)
    gain_own = lax.dynamic_slice_in_dim(gain_one, column, local_width, 1)
    tokens_grad = middle_own + scale_one * (
        one_share * gain_own - own_tokens * scale_one * row_mean
    )
    return (
        mixed_out,
        tokens_grad.astype(bf16),
        sum_qkv,
        sum_conv,
        sum_beta,
        sum_outgate,
        sum_head,
        sum_out,
        sum_mix,
        sum_mlp,
        sum_gateup,
        sum_down,
    )


def solution(mesh):
    return jax.shard_map(
        body,
        mesh=mesh,
        in_specs=(
            P(None, "dp", "mp"),
            P(None, "dp", None),
            P(None, "dp"),
            P(),
            P(None, "dp", "mp"),
            P(None, None, "mp", "dp"),
            P("dp", "mp"),
            P("dp", "mp"),
            P("dp"),
            P("mp", "dp"),
            P("dp"),
            P("dp"),
            P(None, "dp", "mp"),
            P("mp", "dp"),
        ),
        out_specs=(
            P(None, "dp", "mp"),
            P(None, "dp", "mp"),
            P(None, "dp", "mp"),
            P(None, None, "mp", "dp"),
            P("dp", "mp"),
            P("dp", "mp"),
            P("dp"),
            P("mp", "dp"),
            P("dp"),
            P("dp"),
            P(None, "dp", "mp"),
            P("mp", "dp"),
        ),
        check_vma=False,
    )
```

```python
from functools import partial

import jax
import jax.numpy as jnp
from jax import lax
from jax.experimental import pallas as pl
from jax.experimental.pallas import tpu as pltpu
from jax.sharding import PartitionSpec as P

DK = 128
KW = 4
PAD = 8
HALO = 16
VMEM = 58 * 2**20
FREE = pl.CostEstimate(flops=0, transcendentals=0, bytes_accessed=0)

eps_norm = 1e-06
eps_unit = 1e-06

f32 = jnp.float32
bf16 = jnp.bfloat16


def split(v):
    if v.dtype == bf16:
        return v, None
    high = v.astype(bf16)
    return high, (v - high.astype(f32)).astype(bf16)


def mm(a, b, ca=1, cb=0, passes=3):
    def one(x, y):
        return lax.dot_general(x, y, (((ca,), (cb,)), ((), ())), preferred_element_type=f32)

    if passes == 1:
        return one(a.astype(bf16), b.astype(bf16))
    (ah, al), (bh, bl) = split(a), split(b)
    out = one(ah, bh)
    if bl is not None:
        out = out + one(ah, bl)
    if al is not None:
        out = out + one(al, bh)
    return out


def places(rows, cols):
    return (
        lax.broadcasted_iota(jnp.int32, (rows, cols), 0),
        lax.broadcasted_iota(jnp.int32, (rows, cols), 1),
    )


def unit_lower_inverses(blocks):
    size = blocks[0].shape[0]
    if size > 128:
        half = size // 2
        parts = unit_lower_inverses(
            [a[:half, :half] for a in blocks] + [a[half:, half:] for a in blocks]
        )
        firsts, seconds = parts[: len(blocks)], parts[len(blocks) :]
        inner = [mm(a[half:, :half], x) for a, x in zip(blocks, firsts)]
        lower = [-mm(x, y) for x, y in zip(seconds, inner)]
        zero = jnp.zeros((half, half), f32)
        return [
            jnp.concatenate(
                [jnp.concatenate([x, zero], 1), jnp.concatenate([y, z], 1)], 0
            )
            for x, y, z in zip(firsts, lower, seconds)
        ]
    rows, cols = places(size, size)
    eye = (rows == cols).astype(f32)
    level = 0
    inverses = None
    while (1 << level) < size:
        mask = (
            ((rows >> (level + 1)) == (cols >> (level + 1)))
            & (((rows >> level) & 1) == 1)
            & (((cols >> level) & 1) == 0)
        ).astype(f32)
        lows = [a * mask for a in blocks]
        if level == 0:
            inverses = [eye - low for low in lows]
        else:
            inner = [mm(low, x) for low, x in zip(lows, inverses)]
            inverses = [x - mm(x, y) for x, y in zip(inverses, inner)]
        level += 1
    return inverses


def head_slice(h):
    return slice(h * DK, (h + 1) * DK)


def convolve(proj_ref, before_ref, taps, i, h):
    own = proj_ref[i, 0, :, head_slice(h)].astype(f32)
    length = own.shape[0]
    ext = jnp.concatenate([before_ref[i, 0, :, head_slice(h)].astype(f32), own], 0)
    shifts = [ext[HALO - KW + 1 + j : HALO - KW + 1 + j + length] for j in range(KW)]
    out = None
    for j in range(KW):
        tap = taps[i * KW + j : i * KW + j + 1, head_slice(h)]
        out = tap * shifts[j] if out is None else out + tap * shifts[j]
    sig = jax.nn.sigmoid(out)
    return shifts, out, sig, out * sig


def unit(acts):
    inv = lax.rsqrt(jnp.sum(acts * acts, -1, keepdims=True) + eps_unit)
    return acts * inv, inv


def rule_inputs(proj_ref, before_ref, taps, h):
    parts = [convolve(proj_ref, before_ref, taps, i, h) for i in range(3)]
    q, q_inv = unit(parts[0][3])
    k, k_inv = unit(parts[1][3])
    return parts, (q, q_inv), (k, k_inv), parts[2][3]


def norm_factor(values):
    return lax.rsqrt(jnp.mean(values * values, -1, keepdims=True) + eps_norm)


def project_kernel(layout, *refs):
    place_ref, rows_ref, gain_ref, beta_ref = refs[:4]
    pieces = refs[4 : 4 + len(layout)]
    hidden_ref, proj_ref, tail_ref, logit_ref, scale_ref, keep_ref = refs[4 + len(layout) :]
    rows = rows_ref[0].astype(f32)
    scale = norm_factor(rows)
    scale_ref[0] = scale
    keep_ref[...] = (rows * scale * gain_ref[...]).astype(bf16)
    logits = mm(keep_ref[...], beta_ref[...])
    logit_ref[0] = logits[:, : logit_ref.shape[2]]
    sums = [None] * 3
    for (k, start, size, block), piece in zip(layout, pieces):
        at = pl.multiple_of((place_ref[0] ^ k) * block + start, 128)
        part = keep_ref[:, pl.ds(at, size)]
        hidden_ref[0, :, k * block + start : k * block + start + size] = part
        for i in range(3):
            term = mm(part, piece[i])
            sums[i] = term if sums[i] is None else sums[i] + term
    for i in range(3):
        low = sums[i].astype(bf16)
        proj_ref[i, 0] = low
        tail_ref[i, 0] = low[low.shape[0] - HALO :]


def pre_kernel(proj_ref, before_ref, taps_ref, logit_ref, x_ref, wu_ref, qo_ref, to_ref):
    seqs, heads = to_ref.shape[:2]
    taps = taps_ref[...]
    length = proj_ref.shape[2]
    r, c = places(length, length)
    strict = (r > c).astype(f32)
    full = (r >= c).astype(f32)
    saved, blocks = [], []
    for s in range(seqs):
        betas = jax.nn.sigmoid(logit_ref[s])
        rows, before = proj_ref.at[:, s : s + 1], before_ref.at[:, s : s + 1]
        for h in range(heads):
            _, (q, _), (k, _), v = rule_inputs(rows, before, taps, h)
            q, k, v = q.astype(bf16), k.astype(bf16), v.astype(bf16)
            beta = betas[:, h : h + 1]
            blocks.append(beta * mm(k, k, 1, 1) * strict)
            saved.append((s, h, q, k, v, beta))
    inverses = unit_lower_inverses(blocks)
    r, c = places(DK, DK)
    eye = (r == c).astype(f32)
    for (s, h, q, k, v, beta), x in zip(saved, inverses):
        x_ref[s, h] = x
        kv = jnp.concatenate([k.astype(f32), v.astype(f32)], 1) * beta
        wu = mm(x, kv)
        wu_ref[s, h] = wu
        scores = mm(q, k, 1, 1) * full
        pwu = mm(scores, wu)
        qo_ref[s, h, :, :DK] = q.astype(f32) - pwu[:, :DK]
        qo_ref[s, h, :, DK:] = pwu[:, DK:]
        kwu = mm(k, wu, 0, 0)
        to_ref[s, h, :, :DK] = (eye - kwu[:, :DK]).astype(bf16)
        to_ref[s, h, :, DK:] = kwu[:, DK:].astype(bf16)


def by_piece(place_ref, refs):
    if len(refs) > 1 or len(refs[0].shape) < 4:
        return refs
    return [refs[0].at[place_ref[0] ^ k] for k in range(4)]


def gate_part(ref):
    return ref.at[0] if len(ref.shape) == 3 else ref


def out_columns(layout, refs):
    for (k, start, size, block), ref in zip(layout, refs):
        at, half = k * block + start, size // 2
        if len(ref.shape) == 2:
            yield at, size, ref
            continue
        inner = ref.shape[1] // 2
        yield at, half, ref.at[1, :inner]
        yield at + half, half, ref.at[1, inner:]


def mix_kernel(layout, count, pieces, place_ref, *refs):
    near, rest = refs[:count], refs[count:]
    qo_ref, hidden_ref, gain_ref = rest[:3]
    gate_pieces = by_piece(place_ref, rest[3 : 3 + pieces])
    outs = by_piece(place_ref, rest[3 + pieces : 3 + 2 * pieces])
    part_ref, normed_ref, rule_ref, state_ref, gate_ref = rest[-5:]
    gates = None
    for (k, start, size, block), ref in zip(layout, gate_pieces):
        at = k * block + start
        term = mm(hidden_ref[0, :, at : at + size], gate_part(ref)[...])
        gates = term if gates is None else gates + term
    gate_ref[0] = gates
    heads = state_ref.shape[1]
    for h in range(heads):
        state = near[-1][0, h, :, DK:].astype(f32)
        for ref in reversed(near[:-1]):
            state = mm(ref[0, h, :, :DK], state) + ref[0, h, :, DK:].astype(f32)
        state_ref[0, h] = state
        qo = qo_ref[0, h]
        out = (mm(qo[:, :DK], state) + qo[:, DK:]) * DK ** (-0.5)
        rule_ref[0, :, head_slice(h)] = out
        gate = gate_ref[0, :, head_slice(h)]
        normed = out * norm_factor(out) * gain_ref[...] * (gate * jax.nn.sigmoid(gate))
        normed_ref[0, :, head_slice(h)] = normed.astype(bf16)
    for at, size, ref in out_columns(layout, outs):
        part_ref[0, :, at : at + size] = mm(normed_ref[0], ref[...]).astype(bf16)


def prepare_kernel(layout, place_ref, rows_ref, grad_ref, factor_ref, about_ref, cot_ref):
    for k, start, size, block in layout:
        at = pl.multiple_of((place_ref[0] ^ k) * block + start, 128)
        to = slice(k * block + start, k * block + start + size)
        about_ref[0, :, to] = rows_ref[0, :, pl.ds(at, size)]
        grad = grad_ref[0, :, pl.ds(at, size)].astype(f32) * factor_ref[0]
        cot_ref[0, :, to] = grad.astype(bf16)


def down_kernel(layout, place_ref, mlp_ref, *refs):
    part_ref = refs[-1]
    for (k, start, size, block), ref in zip(layout, refs):
        at = pl.multiple_of((place_ref[0] ^ k) * block + start, 128)
        part_ref[0, :, pl.ds(at, size)] = mm(mlp_ref[0], ref[...]).astype(bf16)


def feed_gradient_kernel(base, ranges, hidden_ref, cot_ref, pair_ref, mlp_ref, *outs):
    outs = outs[-2 * len(ranges) :]
    for n, (start, size) in enumerate(ranges):
        start = start - base
        hidden = hidden_ref[:, start : start + size]
        outs[2 * n][0] = mm(pair_ref[0], hidden, 0, 0).astype(bf16)
        outs[2 * n][1] = mm(pair_ref[1], hidden, 0, 0).astype(bf16)
        outs[2 * n + 1][0] = mm(mlp_ref[...], cot_ref[:, start : start + size], 0, 0).astype(bf16)


def qkv_gradient_kernel(ranges, hidden_ref, dproj_ref, dlogit_ref, *outs):
    outs = outs[-len(ranges) - 1 :]
    for (start, size), out in zip(ranges, outs[:-1]):
        hidden = hidden_ref[:, start : start + size]
        for i in range(3):
            out[i] = mm(hidden, dproj_ref[i], 0, 0).astype(bf16)
    outs[-1][...] = mm(dlogit_ref[...], hidden_ref[...], 0, 0)


def pair_gradient_kernel(ranges, hidden_ref, dgate_ref, normed_ref, mix_ref, *outs):
    inner = normed_ref.shape[1]
    for (start, size), out in zip(ranges, outs):
        out[0] = mm(hidden_ref[:, start : start + size], dgate_ref[...], 0, 0).astype(bf16)
        for n in range(2):
            at = start + n * size // 2
            mix = mix_ref[:, at : at + size // 2]
            out[1, n * inner : (n + 1) * inner] = mm(normed_ref[...], mix, 0, 0).astype(bf16)


def add_halves_kernel(*refs):
    one_ref, two_ref, low_ref, high_ref, one_out, two_out = refs[:4] + refs[-2:]
    one_out[...] = (one_ref[...].astype(f32) + high_ref[...].astype(f32)).astype(bf16)
    two_out[...] = (two_ref[...].astype(f32) + low_ref[...].astype(f32)).astype(bf16)


def add_small_kernel(*refs):
    refs[-1][...] = sum(ref[...].astype(f32) for ref in refs[:-1])


def add_last_kernel(*refs):
    own_ref, one_ref, two_ref, out_ref = refs[:3] + refs[-1:]
    out_ref[...] = own_ref[...].astype(f32) + one_ref[...].astype(f32) + two_ref[...].astype(f32)


def feed_kernel(layout, *refs):
    rows_ref, total_ref, cot_ref, gain_ref = refs[:4]
    count = len(layout)
    gateups, downs = (refs[4 + n * count : 4 + (n + 1) * count] for n in range(2))
    two_ref, hidden_ref, mlp_ref, pair_ref = refs[-4:]
    middle = rows_ref[0].astype(f32) + total_ref[0].astype(f32)
    hidden_ref[0] = (middle * norm_factor(middle) * gain_ref[...]).astype(bf16)
    gate, up, grad = None, None, None
    for (k, start, size, block), w_gateup, w_down in zip(layout, gateups, downs):
        lanes = slice(k * block + start, k * block + start + size)
        hidden = hidden_ref[0, :, lanes]
        terms = (
            mm(hidden, w_gateup[0], 1, 1),
            mm(hidden, w_gateup[1], 1, 1),
            mm(cot_ref[0, :, lanes], w_down[...], 1, 1),
        )
        if gate is None:
            gate, up, grad = terms
        else:
            gate, up, grad = gate + terms[0], up + terms[1], grad + terms[2]
    sig = jax.nn.sigmoid(gate)
    silu = gate * sig
    mlp_ref[0] = (silu * up).astype(bf16)
    first = (grad * up * (sig + silu * (1.0 - sig))).astype(bf16)
    second = (grad * silu).astype(bf16)
    pair_ref[0, 0] = first
    pair_ref[1, 0] = second
    for (k, start, size, block), w_gateup in zip(layout, gateups):
        lanes = slice(k * block + start, k * block + start + size)
        two = mm(first, w_gateup[0]) + mm(second, w_gateup[1])
        two_ref[0, :, lanes] = two.astype(bf16)


def middle_back_kernel(layout, pieces, at_ref, *refs):
    two_ref, cot_ref, rows_ref, total_ref, gain_ref, rule_ref, gate_ref, head_gain_ref, qo_ref = refs[:9]
    outs = by_piece(at_ref, refs[9 : 9 + pieces])
    mix_ref, own_ref, mlpgain_ref, drule_ref, dgate_ref, dgain_ref, direct_ref, keep_ref = refs[-8:]
    middle = rows_ref[0].astype(f32) + total_ref[0].astype(f32)
    factor = norm_factor(middle)
    normal = middle * factor
    two = two_ref[0].astype(f32)
    mlpgain_ref[0] = jnp.sum(two * normal, 0, keepdims=True)
    scaled = two * gain_ref[...]
    mean = jnp.mean(scaled * normal, -1, keepdims=True)
    keep_ref[...] = cot_ref[0].astype(f32) + factor * (scaled - normal * mean)
    width = own_ref.shape[2]
    own_ref[0] = keep_ref[:, pl.ds(pl.multiple_of(at_ref[1], 128), width)]
    mix_ref[0] = keep_ref[...].astype(bf16)
    grads = None
    for at, size, ref in out_columns(layout, outs):
        term = mm(mix_ref[0, :, at : at + size], ref[...], 1, 1)
        grads = term if grads is None else grads + term
    total = jnp.zeros((1, DK), f32)
    for h in range(direct_ref.shape[1]):
        grad = grads[:, head_slice(h)]
        out = rule_ref[0, :, head_slice(h)]
        gate = gate_ref[0, :, head_slice(h)]
        inv = norm_factor(out)
        n = out * inv
        sig = jax.nn.sigmoid(gate)
        silu = gate * sig
        gg = grad * head_gain_ref[...]
        dn = gg * silu
        drule = inv * (dn - n * jnp.mean(dn * n, -1, keepdims=True))
        drule_ref[0, :, head_slice(h)] = drule
        dgate = gg * n * sig * (1.0 + gate * (1.0 - sig))
        dgate_ref[0, :, head_slice(h)] = dgate.astype(bf16)
        total = total + jnp.sum(grad * n * silu, 0, keepdims=True)
        direct = mm(qo_ref[0, h, :, :DK], drule, 0, 0) * DK ** (-0.5)
        direct_ref[0, h] = direct.astype(bf16)
    dgain_ref[0] = total


def first_back_kernel(layout, pair_layout, count, place_ref, *refs):
    dproj_ref, dgate_ref, dlogit_ref, proj_ref, gate_ref, logit_ref, beta_ref, rows_ref, scale_ref = refs[:9]
    pieces = refs[9 : 9 + len(layout)]
    pairs = by_piece(place_ref, refs[9 + len(layout) : 9 + len(layout) + count])
    one_ref, rowsum_ref, gainsum_ref = refs[-3:]
    gates = {}
    for (k, start, size, block), ref in zip(pair_layout, pairs):
        gates[k] = ref
    for (k, start, size, block), piece in zip(layout, pieces):
        lanes = slice(k * block + start, k * block + start + size)
        grad = mm(dgate_ref[...], gate_part(gates[k])[start : start + size], 1, 1)
        for i in range(3):
            grad = grad + mm(dproj_ref[i], piece[i], 1, 1)
        for h in range(beta_ref.shape[0]):
            grad = grad + dlogit_ref[:, h : h + 1].astype(f32) * beta_ref[h : h + 1, lanes]
        at = pl.multiple_of((place_ref[0] ^ k) * block + start, 128)
        one_ref[:, pl.ds(at, size)] = grad.astype(bf16)
        gainsum_ref[:, lanes] = jnp.sum(
            grad * (rows_ref[:, lanes].astype(f32) * scale_ref[...]), 0, keepdims=True
        )
    total = dgate_ref[...].astype(f32) * gate_ref[...]
    for i in range(3):
        total = total + dproj_ref[i].astype(f32) * proj_ref[i].astype(f32)
    total = jnp.sum(total, -1, keepdims=True)
    logits = dlogit_ref[...].astype(f32) * logit_ref[...]
    rowsum_ref[...] = total + jnp.sum(logits, -1, keepdims=True)


def back_kernel(count, *refs):
    (
        proj_ref,
        before_ref,
        taps_ref,
        logit_ref,
        x_ref,
        wu_ref,
        state_ref,
        drule_ref,
    ) = refs[:8]
    dproj_ref, last_ref, first_ref, dtaps_ref, dlogit_ref = refs[-5:]
    others = refs[8 : 8 + 2 * count - 1]
    directs, nexts = others[:count], others[count:]
    heads = state_ref.shape[1]
    taps = taps_ref[...]
    length = proj_ref.shape[2]
    betas = jax.nn.sigmoid(logit_ref[0])
    r, c = places(length, length)
    strict = (r > c).astype(f32)
    full = (r >= c).astype(f32)
    zeros = jnp.zeros((PAD, DK), f32)
    for h in range(heads):
        parts, (qu, q_inv), (ku, k_inv), vu = rule_inputs(proj_ref, before_ref, taps, h)
        q, k, v = qu.astype(bf16), ku.astype(bf16), vu.astype(bf16)
        beta = betas[:, h : h + 1]
        leave = jnp.zeros((DK, DK), f32)
        for j in reversed(range(count)):
            here = directs[j][0, h].astype(f32)
            leave = here if j == count - 1 else mm(nexts[j][0, h], leave, 0, 0) + here
        state = state_ref[0, h]
        wu = wu_ref[0, h]
        u = wu[:, DK:] - mm(wu[:, :DK], state)
        resid = v.astype(f32) - mm(k, state)
        dout = drule_ref[0, :, head_slice(h)] * DK ** (-0.5)
        gram = mm(k, k, 1, 1)
        scores = mm(q, k, 1, 1) * full
        du = mm(scores, dout, 0, 0) + mm(k, leave)
        y = mm(x_ref[0, h], du, 0, 0)
        by = beta * y
        da = -(mm(y, u, 1, 1, 1) * strict)
        dbeta = jnp.sum(y * resid, -1, keepdims=True) + jnp.sum(da * gram, -1, keepdims=True)
        dgram = beta * da
        dscores = mm(dout, u, 1, 1, 1) * full
        dq = mm(dout, state, 1, 1, 1) + mm(dscores, k, 1, 0, 1)
        dk = (
            mm(dgram, k, 1, 0, 1)
            + mm(dgram, k, 0, 0, 1)
            + mm(dscores, q, 0, 0, 1)
            + mm(u, leave, 1, 1, 1)
            - mm(by, state, 1, 1, 1)
        )
        dlogit_ref[0, :, h : h + 1] = (dbeta * beta * (1.0 - beta)).astype(bf16)
        dq = (dq - qu * jnp.sum(qu * dq, -1, keepdims=True)) * q_inv
        dk = (dk - ku * jnp.sum(ku * dk, -1, keepdims=True)) * k_inv
        for i, dact in enumerate((dq, dk, by)):
            shifts, out, sig, _ = parts[i]
            dconv = dact * sig * (1.0 + out * (1.0 - sig))
            ext = jnp.concatenate([zeros, dconv, zeros], 0)
            total = None
            for j in range(KW):
                at = i * KW + j
                dtaps_ref[0, at : at + 1, head_slice(h)] = jnp.sum(
                    dconv * shifts[j], 0, keepdims=True
                )
                tap = taps[at : at + 1, head_slice(h)]
                term = tap * ext[KW - 1 - j : KW - 1 - j + PAD + length]
                total = term if total is None else total + term
            first_ref[i, 0, :, head_slice(h)] = total[:PAD]
            last_ref[i, 0, :, head_slice(h)] = total[length:]
            dproj_ref[i, 0, :, head_slice(h)] = total[PAD:].astype(bf16)


def call(kernel, ins, outs, steps, scalar=None, scratch=(), limit=VMEM, alias=None):
    def spec(shape, axis):
        if axis == "any":
            return pl.BlockSpec(memory_space=pl.ANY)
        block = tuple(1 if n == axis else size for n, size in enumerate(shape))
        where = lambda s, *_: tuple(s if n == axis else 0 for n in range(len(shape)))
        if axis is None:
            return pl.BlockSpec(block, where, pipeline_mode=pl.Buffered(1))
        return pl.BlockSpec(block, where)

    given = [] if scalar is None else [scalar]
    return pl.pallas_call(
        kernel,
        cost_estimate=FREE,
        grid_spec=pltpu.PrefetchScalarGridSpec(
            num_scalar_prefetch=len(given),
            grid=(steps,),
            in_specs=[spec(a.shape, axis) for a, axis in ins],
            out_specs=[spec(o.shape, axis) for o, axis in outs],
            scratch_shapes=scratch,
        ),
        out_shape=[o for o, _ in outs],
        input_output_aliases=alias or {},
        compiler_params=pltpu.CompilerParams(vmem_limit_bytes=limit),
    )(*given, *[a for a, _ in ins])


def shape_of(shape, dtype):
    return jax.ShapeDtypeStruct(shape, dtype)


def shifted(array, axis, by):
    devices = lax.axis_size(axis)
    pairs = [(i, i + by) for i in range(devices) if 0 <= i + by < devices]
    return lax.ppermute(array, axis, pairs)


def after(values, *others):
    flat, tree = jax.tree.flatten(values)
    others = jax.tree.leaves(others)
    here = pl.BlockSpec(memory_space=pl.ANY)
    out = pl.pallas_call(
        lambda *refs: None,
        cost_estimate=FREE,
        in_specs=[here] * (len(flat) + len(others)),
        out_specs=[here] * len(flat),
        out_shape=[shape_of(a.shape, a.dtype) for a in flat],
        input_output_aliases={n: n for n in range(len(flat))},
    )(*flat, *others)
    return jax.tree.unflatten(tree, out)


def copies(values):
    count = len(values)

    def kernel(*refs):
        for n in range(count):
            refs[n - count][...] = refs[n][...]

    outs = [(shape_of(a.shape, a.dtype), None) for a in values]
    return call(kernel, [(a, None) for a in values], outs, 1)


def swap(array, bits):
    return lax.ppermute(array, "dp", [(i, i ^ bits) for i in range(4)])


def first_hop(own):
    return swap(own, 1), swap(own, 2)


def halves_of(hop, axis):
    low, high = (jnp.split(part, 2, axis) for part in hop)
    return low[0], high[1]


def gathered_pieces(own, axis, hop=None, halves=None):
    hop = hop or first_hop(own)
    low, high = halves or halves_of(hop, axis)
    return [own, *hop, swap(low, 2), swap(high, 1)]


def far_hop(low, high):
    return swap(low, 1), swap(high, 2)


def near_sums(pieces, far_in, *others):
    own, one, two = pieces
    half = far_in[0].shape
    along = 1 if half[1] < one.shape[1] else 2

    def spec(place):
        where = tuple(place if n == along else 0 for n in range(3))
        return pl.BlockSpec(half, lambda s: where)

    first, second = spec(0), spec(1)
    here = pl.BlockSpec(memory_space=pl.ANY)
    one, two = pl.pallas_call(
        add_halves_kernel,
        cost_estimate=FREE,
        grid=(1,),
        in_specs=[second, first, first, first] + [here] * len(others),
        out_specs=[second, first],
        out_shape=[shape_of(a.shape, a.dtype) for a in (one, two)],
        input_output_aliases={0: 0, 1: 1},
        compiler_params=pltpu.CompilerParams(vmem_limit_bytes=VMEM),
    )(one, two, *far_in, *others)
    return own, one, two


def near_hop(pieces):
    own, one, two = pieces
    return own, swap(one, 1), swap(two, 2)


def add_pair_kernel(own_ref, one_ref, two_ref, *refs):
    gate_ref, out_ref = refs[-2:]
    inner = out_ref.shape[0]

    def added(i, rows):
        parts = (ref[i, rows].astype(f32) for ref in (own_ref, one_ref, two_ref))
        return sum(parts)

    gate_ref[...] = added(0, slice(None))
    for n in range(2):
        out_ref[:, n * inner : (n + 1) * inner] = added(1, slice(n * inner, (n + 1) * inner))


def sum_last(parts, *others):
    own = parts[0]
    ins = [(a, 0) for a in parts] + [(a, "any") for a in others]
    [total] = call(add_last_kernel, ins, [(shape_of(own.shape, f32), 0)], own.shape[0])
    return total


def pack(parts):
    return jnp.concatenate([p.reshape(-1) for p in parts])


def unpack(flat, shapes):
    out, at = [], 0
    for shape in shapes:
        size = 1
        for n in shape:
            size *= n
        out.append(flat[..., at : at + size].reshape(flat.shape[:-1] + tuple(shape)))
        at += size
    return out


def padded(flat, multiple=1024):
    return jnp.pad(flat, (0, -flat.shape[0] % multiple))


def body(
    tokens,
    out_grad,
    domain,
    group_weight,
    w_qkv,
    conv_weight,
    w_beta,
    w_outgate,
    head_gain,
    w_out,
    mixer_gain,
    mlp_gain,
    w_gateup,
    w_down,
):
    dp = lax.axis_size("dp")
    place = lax.axis_index("dp")
    seqs, block, local_width = tokens.shape
    count_rows = seqs * block
    heads = conv_weight.shape[2]
    inner = heads * DK
    column = lax.axis_index("mp") * local_width
    near_four = dp == 4

    def blocks_about(array, axis):
        if not near_four:
            return array
        size = array.shape[axis] // 4
        return jnp.concatenate(
            [lax.dynamic_slice_in_dim(array, (place ^ k) * size, size, axis) for k in range(4)],
            axis,
        )

    width = out_grad.shape[2]
    turn = place if near_four else jnp.int32(0)
    column_about = ((column // (width // 4)) ^ turn) * (width // 4) + column % (width // 4)

    def own(array):
        array = array.reshape(seqs, block, width)
        return lax.dynamic_slice_in_dim(array, column_about, local_width, 2)

    onehot = (domain[..., None] == jnp.arange(3, dtype=jnp.int32)).astype(f32)
    own_counts = jnp.sum(onehot, axis=(0, 1))
    high = jnp.floor(own_counts / 128.0)
    digits = jnp.concatenate([high, own_counts - 128.0 * high]).astype(bf16)
    small = [w_beta, conv_weight, head_gain, mixer_gain, mlp_gain, digits]
    packed = padded(pack(small))
    size = width // 4
    if near_four:
        qkv_hop = first_hop(w_qkv)
        qkv_halves = halves_of(qkv_hop, 1)
        qkv = gathered_pieces(w_qkv, 1, qkv_hop, qkv_halves)
        packed = after(packed, qkv_halves)
        gathered = jnp.stack([packed] + [swap(packed, bits) for bits in (1, 2, 3)])
        half = w_out.shape[1] // 2
        pair_own = jnp.stack(
            [w_outgate, jnp.concatenate([w_out[:, :half], w_out[:, half:]], 0)]
        )
        pair_layout = [(k, 0, size, size) for k in range(4)]
        layout = pair_layout[:3] + [(3, 0, size // 2, size), (3, size // 2, size // 2, size)]
    else:
        gathered = lax.all_gather(packed, "dp")
        qkv = [lax.all_gather(w_qkv, "dp", axis=1, tiled=True)]
        gate_pieces = [lax.all_gather(w_outgate, "dp", axis=0, tiled=True)]
        out_pieces = [lax.all_gather(w_out, "dp", axis=1, tiled=True)]
        layout = pair_layout = [(0, 0, width, width)]
    ranges = [(k * step + start, n) for k, start, n, step in layout]
    g_beta, g_conv, g_head, g_mix, g_mlp, g_digits = unpack(gathered, [a.shape for a in small])
    about_beta = g_beta.reshape(-1, heads)
    full_beta = blocks_about(about_beta, 0)
    full_conv = jnp.moveaxis(blocks_about(g_conv, 0), 0, 3).reshape(3 * KW, inner).astype(f32)
    gain_head = blocks_about(g_head, 0).reshape(1, DK).astype(f32)
    gain_one = blocks_about(g_mix.reshape(1, -1).astype(f32), 1)
    gain_two = g_mlp.reshape(1, -1).astype(f32)
    sums = jnp.sum(g_digits.astype(f32), 0)
    counts = 128.0 * sums[:3] + sums[3:]
    table = group_weight * (domain.shape[0] * domain.shape[1] * dp) / counts
    factor = jnp.sum(onehot * table, -1)[..., None]

    def flat(array):
        return array.reshape(array.shape[:-3] + (count_rows, array.shape[-1]))

    rows = lax.all_gather(tokens, "mp", axis=2, tiled=True)
    if near_four:
        gate_pieces = out_pieces = [lax.all_gather(after(pair_own, packed), "dp")]
    turn_one = turn.reshape(1)
    per_token = (seqs, block)
    square = (seqs, heads, DK, DK)
    hidden_one, proj, tail, logits, scale_one = call(
        partial(project_kernel, layout),
        [(rows, 0), (gain_one, None), (jnp.pad(full_beta, ((0, 0), (0, 128 - heads))), None)]
        + [(a, None) for a in qkv],
        [
            (shape_of(per_token + (width,), bf16), 0),
            (shape_of((3,) + per_token + (inner,), bf16), 1),
            (shape_of((3, seqs, HALO, inner), bf16), 1),
            (shape_of(per_token + (heads,), f32), 0),
            (shape_of(per_token + (1,), f32), 0),
        ],
        seqs,
        scalar=turn_one,
        scratch=[pltpu.VMEM((block, width), bf16)],
    )
    before = shifted(tail, "dp", 1)
    inverse, wu, qo, to = call(
        pre_kernel,
        [(proj, None), (before, None), (full_conv, None), (logits, None)],
        [
            (shape_of((seqs, heads, block, block), f32), None),
            (shape_of((seqs, heads, block, 2 * DK), f32), None),
            (shape_of((seqs, heads, block, 2 * DK), f32), None),
            (shape_of((seqs, heads, DK, 2 * DK), bf16), None),
        ],
        1,
    )
    near = [shifted(to, "dp", c) for c in range(1, dp)]
    rows_about, cotangent = call(
        partial(prepare_kernel, layout),
        [(rows, 0), (out_grad, 0), (factor, 0)],
        [(shape_of(per_token + (width,), bf16), 0)] * 2,
        seqs,
        scalar=turn_one,
    )
    turned = jnp.swapaxes(w_gateup, 1, 2)
    feed_own = [turned, w_down]
    mixer_part, normed, rule, state, gates = call(
        partial(mix_kernel, pair_layout, len(near), len(out_pieces)),
        [(a, 0) for a in near]
        + [(qo, 0), (hidden_one, 0), (gain_head, None)]
        + [(a, None) for a in gate_pieces + out_pieces]
        + [(cotangent, "any")],
        [
            (shape_of(per_token + (width,), bf16), 0),
            (shape_of(per_token + (inner,), bf16), 0),
            (shape_of(per_token + (inner,), f32), 0),
            (shape_of(square, f32), 0),
            (shape_of(per_token + (inner,), f32), 0),
        ],
        seqs,
        scalar=turn_one,
    )
    total = lax.psum(mixer_part, "mp")
    nexts = [shifted(to[..., :DK], "dp", -c) for c in range(1, dp - 1)]
    if near_four:
        gateup, down = (gathered_pieces(a, a.ndim - 1) for a in after(copies(feed_own), mixer_part, nexts))
    else:
        gateup, down = (
            [lax.all_gather(a, "dp", axis=a.ndim - 1, tiled=True)] for a in feed_own
        )
    units = w_down.shape[0]
    two_part, hidden_two, hidden_mlp, grad_pair = call(
        partial(feed_kernel, layout),
        [(rows_about, 0), (total, 0), (cotangent, 0), (gain_two, None)]
        + [(a, None) for a in gateup + down],
        [
            (shape_of(per_token + (width,), bf16), 0),
            (shape_of(per_token + (width,), bf16), 0),
            (shape_of(per_token + (units,), bf16), 0),
            (shape_of((2,) + per_token + (units,), bf16), 1),
        ],
        seqs,
    )
    grad_two = lax.psum(two_part, "mp")

    def feed_gradients(some, *others):
        outs = [(shape_of((m, units, n), bf16), None) for _, n in some for m in (2, 1)]
        base, span = some[0][0], sum(n for _, n in some)
        aligned = base % span == 0
        at = base // span if aligned else 0
        cols = pl.BlockSpec((count_rows, span if aligned else width), lambda s: (0, at))
        made = pl.pallas_call(
            partial(feed_gradient_kernel, base if aligned else 0, some),
            cost_estimate=FREE,
            grid=(1,),
            in_specs=[
                cols,
                cols,
                pl.BlockSpec((2, count_rows, units), lambda s: (0, 0, 0)),
                pl.BlockSpec((count_rows, units), lambda s: (0, 0)),
            ]
            + [pl.BlockSpec(memory_space=pl.ANY)] * len(others),
            out_specs=[pl.BlockSpec(o.shape, lambda s: (0, 0, 0)) for o, _ in outs],
            out_shape=[o for o, _ in outs],
            compiler_params=pltpu.CompilerParams(vmem_limit_bytes=VMEM),
        )(flat(hidden_two), flat(cotangent), flat(grad_pair), flat(hidden_mlp), *others)
        return made[::2], made[1::2]

    if near_four:
        feed_far = feed_gradients(ranges[3:])
        feed_in = [far_hop(*far) for far in feed_far]
        near_gateup, near_down = feed_gradients(ranges[:3], feed_far[0][0])
        gateup_added = near_sums(near_gateup, feed_in[0], *feed_in[1])
        down_added = near_sums(near_down, feed_in[1], gateup_added[1])
        first_made = [(down_added[1], "any")]
        gateup_sums, down_sums = near_hop(gateup_added), near_hop(down_added)
        held = [(a, "any") for a in gateup_sums[1:]]
    else:
        [grad_gateup], [grad_down] = feed_gradients(ranges)
        held = first_made = []
    [down_part] = call(
        partial(down_kernel, layout),
        [(hidden_mlp, 0)] + [(a, None) for a in down] + first_made,
        [(shape_of(per_token + (width,), bf16), 0)],
        seqs,
        scalar=turn_one,
    )
    mlp_share = lax.psum_scatter(down_part, "mp", scatter_dimension=2, tiled=True)
    grad_mix, middle_own, mlpgain, drule, dgate, dgain, direct = call(
        partial(middle_back_kernel, pair_layout, len(out_pieces)),
        [
            (grad_two, 0),
            (cotangent, 0),
            (rows_about, 0),
            (total, 0),
            (gain_two, None),
            (rule, 0),
            (gates, 0),
            (gain_head, None),
            (qo, 0),
        ]
        + [(a, None) for a in out_pieces]
        + [(down_part, "any")]
        + held,
        [
            (shape_of(per_token + (width,), bf16), 0),
            (shape_of(per_token + (local_width,), f32), 0),
            (shape_of((seqs, 1, width), f32), 0),
            (shape_of(per_token + (inner,), f32), 0),
            (shape_of(per_token + (inner,), bf16), 0),
            (shape_of((seqs, 1, DK), f32), 0),
            (shape_of(square, bf16), 0),
        ],
        seqs,
        scalar=jnp.stack([turn, column_about]),
        scratch=[pltpu.VMEM((block, width), f32)],
    )
    directs = [shifted(direct, "dp", -c) for c in range(1, dp)]
    if near_four:
        pair_grads = call(
            partial(pair_gradient_kernel, [(k * size, size) for k in range(4)]),
            [(flat(a), None) for a in (hidden_one, dgate, normed, grad_mix)],
            [(shape_of((2, size, inner), bf16), None)] * 4,
            1,
        )
        held = [(a, "any") for a in (pair_grads[3], *down_sums[1:])]
    else:
        grad_outgate = jnp.einsum(
            "td,tc->dc", flat(hidden_one), flat(dgate), preferred_element_type=f32
        )
        grad_outproj = jnp.einsum(
            "tc,td->cd", flat(normed), flat(grad_mix), preferred_element_type=f32
        )
        held = []
    dproj, last, first, dtaps, dlogits = call(
        partial(back_kernel, len(directs)),
        [
            (proj, 1),
            (before, 1),
            (full_conv, None),
            (logits, 0),
            (inverse, 0),
            (wu, 0),
            (state, 0),
            (drule, 0),
        ]
        + [(a, 0) for a in directs + nexts]
        + held,
        [
            (shape_of((3,) + per_token + (inner,), bf16), 1),
            (shape_of((3, seqs, PAD, inner), f32), 1),
            (shape_of((3, seqs, PAD, inner), f32), 1),
            (shape_of((seqs, 3 * KW, inner), f32), 0),
            (shape_of(per_token + (heads,), bf16), 0),
        ],
        seqs,
    )
    later = shifted(first, "dp", -1)
    dproj = lax.dynamic_update_slice(dproj, (last + later).astype(bf16), (0, 0, block - PAD, 0))
    one_low, row_part, gain_part = call(
        partial(first_back_kernel, layout, pair_layout, len(gate_pieces)),
        [
            (flat(dproj), None),
            (flat(dgate), None),
            (flat(dlogits), None),
            (flat(proj), None),
            (flat(gates), None),
            (flat(logits), None),
            (about_beta.T.astype(f32), None),
            (flat(rows_about), None),
            (flat(scale_one), None),
        ]
        + [(a, None) for a in qkv + gate_pieces],
        [
            (shape_of((count_rows, width), bf16), None),
            (shape_of((count_rows, 1), f32), None),
            (shape_of((1, width), f32), None),
        ],
        1,
        scalar=turn_one,
    )
    one_share = lax.psum_scatter(
        one_low.reshape(seqs, block, width), "mp", scatter_dimension=2, tiled=True
    ).astype(f32)
    made = call(
        partial(qkv_gradient_kernel, ranges),
        [(flat(hidden_one), None), (flat(dproj), None), (flat(dlogits), None), (row_part, "any")],
        [(shape_of((3, n, inner), bf16), None) for _, n in ranges]
        + [(shape_of((heads, width), f32), None)],
        1,
    )

    def pieces(array, axis, about):
        shape = array.shape
        cut = array.reshape(shape[:axis] + (dp, shape[axis] // dp) + shape[axis + 1 :])
        cut = jnp.moveaxis(cut, axis, 0).reshape(dp, -1)
        return blocks_about(cut, 0) if about else cut

    smalls = jnp.concatenate(
        [
            pieces(jnp.sum(dtaps, 0).reshape(3, KW, heads, DK), 3, True),
            pieces(made[-1].T, 0, False),
            pieces(jnp.sum(dgain, (0, 1)), 0, True),
            pieces(gain_part[0], 0, False),
            pieces(jnp.sum(mlpgain, (0, 1)), 0, False),
        ],
        1,
    )
    if near_four:
        own_qkv, *near_qkv = near_sums(made[:3], far_hop(made[3], made[4]))
        gateup_total = sum_last(gateup_sums, *near_qkv)
        down_total = sum_last(down_sums, *near_qkv)
        smalls = jnp.pad(smalls, ((0, 0), (0, -smalls.shape[1] % 1024))).reshape(dp, -1, 128)
        sent = smalls.astype(bf16)
        got = [swap(sent[bits], bits) for bits in (1, 2, 3)]
        [mine] = call(
            add_small_kernel,
            [(a, None) for a in [smalls[0]] + got],
            [(shape_of(smalls.shape[1:], f32), None)],
            1,
        )
        pair_far = after(jnp.split(pair_grads[3], 2, 1), mine)
        pair_near = near_sums(pair_grads[:3], far_hop(*pair_far))[1:]
        mine = mine.reshape(-1)
        sum_qkv = sum_last(near_hop((own_qkv, *near_qkv)))
        sum_gateup = jnp.swapaxes(gateup_total, 1, 2)
        sum_down = down_total[0]
        sum_outgate, sum_out = call(
            add_pair_kernel,
            [(a, None) for a in near_hop((pair_grads[0], *pair_near))],
            [(shape_of(w_outgate.shape, f32), None), (shape_of(w_out.shape, f32), None)],
            1,
        )
    else:
        gathered = lax.all_gather(smalls.astype(bf16), "dp")
        mine = jnp.sum(
            lax.dynamic_index_in_dim(gathered, place, 1, keepdims=False).astype(f32), 0
        )

        def scattered(array, axis):
            return lax.psum_scatter(array, "dp", scatter_dimension=axis, tiled=True).astype(f32)

        sum_qkv = scattered(made[0], 1)
        sum_outgate = scattered(grad_outgate.astype(bf16), 0)
        sum_out = scattered(grad_outproj.astype(bf16), 1)
        sum_gateup = jnp.swapaxes(scattered(grad_gateup, 2), 1, 2)
        sum_down = scattered(grad_down[0], 1)
    sum_conv, sum_beta, sum_head, sum_mix, sum_mlp = unpack(
        mine,
        [conv_weight.shape, w_beta.shape, head_gain.shape, mixer_gain.shape, mlp_gain.shape],
    )
    rest = [row_part[:, 0], sum_head, sum_mix]
    packed_rest = padded(pack(rest), 128)
    if near_four:
        packed_rest = after(packed_rest, near_qkv)
    everyone = lax.optimization_barrier(lax.all_gather(packed_rest, "mp"))
    row_sum, sum_head, sum_mix = unpack(jnp.sum(everyone, 0), [a.shape for a in rest])

    own_tokens = tokens.astype(f32)
    mixed_out = (own_tokens + own(total).astype(f32) + mlp_share.astype(f32)).astype(bf16)
    row_mean = (row_sum / width).reshape(seqs, block, 1)
    gain_own = lax.dynamic_slice_in_dim(gain_one, column, local_width, 1)
    tokens_grad = middle_own + scale_one * (
        one_share * gain_own - own_tokens * scale_one * row_mean
    )
    return (
        mixed_out,
        tokens_grad.astype(bf16),
        sum_qkv,
        sum_conv,
        sum_beta,
        sum_outgate,
        sum_head,
        sum_out,
        sum_mix,
        sum_mlp,
        sum_gateup,
        sum_down,
    )


def solution(mesh):
    return jax.shard_map(
        body,
        mesh=mesh,
        in_specs=(
            P(None, "dp", "mp"),
            P(None, "dp", None),
            P(None, "dp"),
            P(),
            P(None, "dp", "mp"),
            P(None, None, "mp", "dp"),
            P("dp", "mp"),
            P("dp", "mp"),
            P("dp"),
            P("mp", "dp"),
            P("dp"),
            P("dp"),
            P(None, "dp", "mp"),
            P("mp", "dp"),
        ),
        out_specs=(
            P(None, "dp", "mp"),
            P(None, "dp", "mp"),
            P(None, "dp", "mp"),
            P(None, None, "mp", "dp"),
            P("dp", "mp"),
            P("dp", "mp"),
            P("dp"),
            P("mp", "dp"),
            P("dp"),
            P("dp"),
            P(None, "dp", "mp"),
            P("mp", "dp"),
        ),
        check_vma=False,
    )
```

```python
from functools import partial

import jax
import jax.numpy as jnp
from jax import lax
from jax.experimental import pallas as pl
from jax.experimental.pallas import tpu as pltpu
from jax.sharding import PartitionSpec as P

DK = 128
KW = 4
PAD = 8
HALO = 16
ROWS = 16
VMEM = 58 * 2**20
FREE = pl.CostEstimate(flops=0, transcendentals=0, bytes_accessed=0)

eps_norm = 1e-06
eps_unit = 1e-06

f32 = jnp.float32
bf16 = jnp.bfloat16


def split(v):
    if v.dtype == bf16:
        return v, None
    high = v.astype(bf16)
    return high, (v - high.astype(f32)).astype(bf16)


def mm(a, b, ca=1, cb=0, passes=3):
    def one(x, y):
        return lax.dot_general(x, y, (((ca,), (cb,)), ((), ())), preferred_element_type=f32)

    if passes == 1:
        return one(a.astype(bf16), b.astype(bf16))
    (ah, al), (bh, bl) = split(a), split(b)
    out = one(ah, bh)
    if bl is not None:
        out = out + one(ah, bl)
    if al is not None:
        out = out + one(al, bh)
    return out


def places(rows, cols):
    return (
        lax.broadcasted_iota(jnp.int32, (rows, cols), 0),
        lax.broadcasted_iota(jnp.int32, (rows, cols), 1),
    )


def unit_lower_inverses(blocks):
    size = blocks[0].shape[0]
    if size > 128:
        half = size // 2
        parts = unit_lower_inverses(
            [a[:half, :half] for a in blocks] + [a[half:, half:] for a in blocks]
        )
        firsts, seconds = parts[: len(blocks)], parts[len(blocks) :]
        inner = [mm(a[half:, :half], x) for a, x in zip(blocks, firsts)]
        lower = [-mm(x, y) for x, y in zip(seconds, inner)]
        zero = jnp.zeros((half, half), f32)
        return [
            jnp.concatenate(
                [jnp.concatenate([x, zero], 1), jnp.concatenate([y, z], 1)], 0
            )
            for x, y, z in zip(firsts, lower, seconds)
        ]
    rows, cols = places(size, size)
    eye = (rows == cols).astype(f32)
    level = 0
    inverses = None
    while (1 << level) < size:
        mask = (
            ((rows >> (level + 1)) == (cols >> (level + 1)))
            & (((rows >> level) & 1) == 1)
            & (((cols >> level) & 1) == 0)
        ).astype(f32)
        lows = [a * mask for a in blocks]
        if level == 0:
            inverses = [eye - low for low in lows]
        else:
            inner = [mm(low, x) for low, x in zip(lows, inverses)]
            inverses = [x - mm(x, y) for x, y in zip(inverses, inner)]
        level += 1
    return inverses


def head_slice(h):
    return slice(h * DK, (h + 1) * DK)


def convolve(proj_ref, before_ref, taps, i, h):
    own = proj_ref[i, 0, :, head_slice(h)].astype(f32)
    length = own.shape[0]
    ext = jnp.concatenate([before_ref[i, 0, :, head_slice(h)].astype(f32), own], 0)
    shifts = [ext[HALO - KW + 1 + j : HALO - KW + 1 + j + length] for j in range(KW)]
    out = None
    for j in range(KW):
        tap = taps[i * KW + j : i * KW + j + 1, head_slice(h)]
        out = tap * shifts[j] if out is None else out + tap * shifts[j]
    sig = jax.nn.sigmoid(out)
    return shifts, out, sig, out * sig


def unit(acts):
    inv = lax.rsqrt(jnp.sum(acts * acts, -1, keepdims=True) + eps_unit)
    return acts * inv, inv


def rule_inputs(proj_ref, before_ref, taps, h):
    parts = [convolve(proj_ref, before_ref, taps, i, h) for i in range(3)]
    q, q_inv = unit(parts[0][3])
    k, k_inv = unit(parts[1][3])
    return parts, (q, q_inv), (k, k_inv), parts[2][3]


def norm_factor(values):
    return lax.rsqrt(jnp.mean(values * values, -1, keepdims=True) + eps_norm)


def project_kernel(layout, *refs):
    place_ref, rows_ref, gain_ref, beta_ref = refs[:4]
    pieces = refs[4 : 4 + len(layout)]
    hidden_ref, proj_ref, tail_ref, logit_ref, scale_ref, keep_ref = refs[4 + len(layout) :]
    rows = rows_ref[0].astype(f32)
    scale = norm_factor(rows)
    scale_ref[0] = scale
    keep_ref[...] = (rows * scale * gain_ref[...]).astype(bf16)
    logits = mm(keep_ref[...], beta_ref[...])
    logit_ref[0] = logits[:, : logit_ref.shape[2]]
    sums = [None] * 3
    for (k, start, size, block), piece in zip(layout, pieces):
        at = pl.multiple_of((place_ref[0] ^ k) * block + start, 128)
        part = keep_ref[:, pl.ds(at, size)]
        hidden_ref[0, :, k * block + start : k * block + start + size] = part
        for i in range(3):
            term = mm(part, piece[i])
            sums[i] = term if sums[i] is None else sums[i] + term
    for i in range(3):
        low = sums[i].astype(bf16)
        proj_ref[i, 0] = low
        tail_ref[i, 0] = low[low.shape[0] - HALO :]


def pre_kernel(proj_ref, before_ref, taps_ref, logit_ref, x_ref, wu_ref, qo_ref, to_ref):
    seqs, heads = to_ref.shape[:2]
    taps = taps_ref[...]
    length = proj_ref.shape[2]
    r, c = places(length, length)
    strict = (r > c).astype(f32)
    full = (r >= c).astype(f32)
    saved, blocks = [], []
    for s in range(seqs):
        betas = jax.nn.sigmoid(logit_ref[s])
        rows, before = proj_ref.at[:, s : s + 1], before_ref.at[:, s : s + 1]
        for h in range(heads):
            _, (q, _), (k, _), v = rule_inputs(rows, before, taps, h)
            q, k, v = q.astype(bf16), k.astype(bf16), v.astype(bf16)
            beta = betas[:, h : h + 1]
            blocks.append(beta * mm(k, k, 1, 1) * strict)
            saved.append((s, h, q, k, v, beta))
    inverses = unit_lower_inverses(blocks)
    r, c = places(DK, DK)
    eye = (r == c).astype(f32)
    for (s, h, q, k, v, beta), x in zip(saved, inverses):
        x_ref[s, h] = x
        kv = jnp.concatenate([k.astype(f32), v.astype(f32)], 1) * beta
        wu = mm(x, kv)
        wu_ref[s, h] = wu
        scores = mm(q, k, 1, 1) * full
        pwu = mm(scores, wu)
        qo_ref[s, h, :, :DK] = q.astype(f32) - pwu[:, :DK]
        qo_ref[s, h, :, DK:] = pwu[:, DK:]
        kwu = mm(k, wu, 0, 0)
        to_ref[s, h, :, :DK] = (eye - kwu[:, :DK]).astype(bf16)
        to_ref[s, h, :, DK:] = kwu[:, DK:].astype(bf16)


def by_piece(place_ref, refs):
    if len(refs) > 1 or len(refs[0].shape) < 4:
        return refs
    return [refs[0].at[place_ref[0] ^ k] for k in range(4)]


def gate_part(ref):
    return ref.at[0] if len(ref.shape) == 3 else ref


def out_columns(layout, refs):
    for (k, start, size, block), ref in zip(layout, refs):
        at, half = k * block + start, size // 2
        if len(ref.shape) == 2:
            yield at, size, ref
            continue
        inner = ref.shape[1] // 2
        yield at, half, ref.at[1, :inner]
        yield at + half, half, ref.at[1, inner:]


def mix_kernel(layout, count, pieces, place_ref, *refs):
    near, rest = refs[:count], refs[count:]
    qo_ref, hidden_ref, gain_ref = rest[:3]
    gate_pieces = by_piece(place_ref, rest[3 : 3 + pieces])
    outs = by_piece(place_ref, rest[3 + pieces : 3 + 2 * pieces])
    part_ref, normed_ref, rule_ref, state_ref, gate_ref = rest[-5:]
    gates = None
    for (k, start, size, block), ref in zip(layout, gate_pieces):
        at = k * block + start
        term = mm(hidden_ref[0, :, at : at + size], gate_part(ref)[...])
        gates = term if gates is None else gates + term
    gate_ref[0] = gates
    heads = state_ref.shape[1]
    for h in range(heads):
        state = near[-1][0, h, :, DK:].astype(f32)
        for ref in reversed(near[:-1]):
            state = mm(ref[0, h, :, :DK], state) + ref[0, h, :, DK:].astype(f32)
        state_ref[0, h] = state
        qo = qo_ref[0, h]
        out = (mm(qo[:, :DK], state) + qo[:, DK:]) * DK ** (-0.5)
        rule_ref[0, :, head_slice(h)] = out
        gate = gate_ref[0, :, head_slice(h)]
        normed = out * norm_factor(out) * gain_ref[...] * (gate * jax.nn.sigmoid(gate))
        normed_ref[0, :, head_slice(h)] = normed.astype(bf16)
    for at, size, ref in out_columns(layout, outs):
        part_ref[0, :, at : at + size] = mm(normed_ref[0], ref[...]).astype(bf16)


def prepare_kernel(layout, place_ref, rows_ref, grad_ref, factor_ref, about_ref, cot_ref):
    for k, start, size, block in layout:
        at = pl.multiple_of((place_ref[0] ^ k) * block + start, 128)
        to = slice(k * block + start, k * block + start + size)
        about_ref[0, :, to] = rows_ref[0, :, pl.ds(at, size)]
        grad = grad_ref[0, :, pl.ds(at, size)].astype(f32) * factor_ref[0]
        cot_ref[0, :, to] = grad.astype(bf16)


def down_kernel(layout, place_ref, mlp_ref, *refs):
    part_ref = refs[-1]
    for (k, start, size, block), ref in zip(layout, refs):
        at = pl.multiple_of((place_ref[0] ^ k) * block + start, 128)
        part_ref[0, :, pl.ds(at, size)] = mm(mlp_ref[0], ref[...]).astype(bf16)


def feed_gradient_kernel(base, ranges, hidden_ref, cot_ref, pair_ref, mlp_ref, *outs):
    outs = outs[-2 * len(ranges) :]
    for n, (start, size) in enumerate(ranges):
        start = start - base
        hidden = hidden_ref[:, start : start + size]
        outs[2 * n][0] = mm(pair_ref[0], hidden, 0, 0).astype(bf16)
        outs[2 * n][1] = mm(pair_ref[1], hidden, 0, 0).astype(bf16)
        outs[2 * n + 1][0] = mm(mlp_ref[...], cot_ref[:, start : start + size], 0, 0).astype(bf16)


def qkv_gradient_kernel(ranges, hidden_ref, dproj_ref, dlogit_ref, *outs):
    outs = outs[-len(ranges) - 1 :]
    for (start, size), out in zip(ranges, outs[:-1]):
        hidden = hidden_ref[:, start : start + size]
        for i in range(3):
            out[i] = mm(hidden, dproj_ref[i], 0, 0).astype(bf16)
    outs[-1][...] = mm(dlogit_ref[...], hidden_ref[...], 0, 0)


def pair_gradient_kernel(ranges, hidden_ref, dgate_ref, normed_ref, mix_ref, *outs):
    inner = normed_ref.shape[1]
    for (start, size), out in zip(ranges, outs):
        out[0] = mm(hidden_ref[:, start : start + size], dgate_ref[...], 0, 0).astype(bf16)
        for n in range(2):
            at = start + n * size // 2
            mix = mix_ref[:, at : at + size // 2]
            out[1, n * inner : (n + 1) * inner] = mm(normed_ref[...], mix, 0, 0).astype(bf16)


def add_halves_kernel(*refs):
    one_ref, two_ref, low_ref, high_ref, one_out, two_out = refs[:4] + refs[-2:]
    one_out[...] = (one_ref[...].astype(f32) + high_ref[...].astype(f32)).astype(bf16)
    two_out[...] = (two_ref[...].astype(f32) + low_ref[...].astype(f32)).astype(bf16)


def add_small_kernel(mix_rows, head_row, *refs):
    *parts, row_ref, out_ref, rest_ref = refs
    total = sum(ref[...].astype(f32) for ref in parts)
    out_ref[...] = total
    lines = [row_ref[:, n * 128 : (n + 1) * 128] for n in range(row_ref.shape[1] // 128)]
    lines += [total[mix_rows], total[head_row : head_row + 1]]
    used = len(lines) - 2 + mix_rows.stop - mix_rows.start + 1
    lines.append(jnp.zeros((rest_ref.shape[0] - used, 128), f32))
    rest_ref[...] = jnp.concatenate(lines, 0)


def add_last_kernel(*refs):
    own_ref, one_ref, two_ref, out_ref = refs[:3] + refs[-1:]
    out_ref[...] = own_ref[...].astype(f32) + one_ref[...].astype(f32) + two_ref[...].astype(f32)


def feed_kernel(layout, *refs):
    rows_ref, total_ref, cot_ref, gain_ref = refs[:4]
    count = len(layout)
    gateups, downs = (refs[4 + n * count : 4 + (n + 1) * count] for n in range(2))
    two_ref, hidden_ref, mlp_ref, pair_ref = refs[-4:]
    middle = rows_ref[0].astype(f32) + total_ref[0].astype(f32)
    hidden_ref[0] = (middle * norm_factor(middle) * gain_ref[...]).astype(bf16)
    gate, up, grad = None, None, None
    for (k, start, size, block), w_gateup, w_down in zip(layout, gateups, downs):
        lanes = slice(k * block + start, k * block + start + size)
        hidden = hidden_ref[0, :, lanes]
        terms = (
            mm(hidden, w_gateup[0], 1, 1),
            mm(hidden, w_gateup[1], 1, 1),
            mm(cot_ref[0, :, lanes], w_down[...], 1, 1),
        )
        if gate is None:
            gate, up, grad = terms
        else:
            gate, up, grad = gate + terms[0], up + terms[1], grad + terms[2]
    sig = jax.nn.sigmoid(gate)
    silu = gate * sig
    mlp_ref[0] = (silu * up).astype(bf16)
    first = (grad * up * (sig + silu * (1.0 - sig))).astype(bf16)
    second = (grad * silu).astype(bf16)
    pair_ref[0, 0] = first
    pair_ref[1, 0] = second
    for (k, start, size, block), w_gateup in zip(layout, gateups):
        lanes = slice(k * block + start, k * block + start + size)
        two = mm(first, w_gateup[0]) + mm(second, w_gateup[1])
        two_ref[0, :, lanes] = two.astype(bf16)


def middle_back_kernel(layout, pieces, at_ref, *refs):
    two_ref, cot_ref, rows_ref, total_ref, gain_ref, rule_ref, gate_ref, head_gain_ref, qo_ref = refs[:9]
    outs = by_piece(at_ref, refs[9 : 9 + pieces])
    mix_ref, own_ref, mlpgain_ref, drule_ref, dgate_ref, dgain_ref, direct_ref, keep_ref = refs[-8:]
    full = rows_ref.shape[2]
    gain_sum = None
    for start in range(0, rows_ref.shape[1], ROWS):
        at = slice(start, start + ROWS)
        middle = rows_ref[0, at].astype(f32) + total_ref[0, at].astype(f32)
        two = two_ref[0, at].astype(f32)
        factor = norm_factor(middle)
        normal = middle * factor
        term = jnp.sum((two * normal).reshape(ROWS // 8, 8, full), 0)
        gain_sum = term if gain_sum is None else gain_sum + term
        scaled = two * gain_ref[...]
        mean = jnp.mean(scaled * normal, -1, keepdims=True)
        keep = cot_ref[0, at].astype(f32) + factor * (scaled - normal * mean)
        keep_ref[at] = keep
        mix_ref[0, at] = keep.astype(bf16)
    mlpgain_ref[0] = jnp.sum(gain_sum, 0, keepdims=True)
    width = own_ref.shape[2]
    own_ref[0] = keep_ref[:, pl.ds(pl.multiple_of(at_ref[1], 128), width)]
    grads = None
    for at, size, ref in out_columns(layout, outs):
        term = mm(mix_ref[0, :, at : at + size], ref[...], 1, 1)
        grads = term if grads is None else grads + term
    total = jnp.zeros((1, DK), f32)
    for h in range(direct_ref.shape[1]):
        grad = grads[:, head_slice(h)]
        out = rule_ref[0, :, head_slice(h)]
        gate = gate_ref[0, :, head_slice(h)]
        inv = norm_factor(out)
        n = out * inv
        sig = jax.nn.sigmoid(gate)
        silu = gate * sig
        gg = grad * head_gain_ref[...]
        dn = gg * silu
        drule = inv * (dn - n * jnp.mean(dn * n, -1, keepdims=True))
        drule_ref[0, :, head_slice(h)] = drule
        dgate = gg * n * sig * (1.0 + gate * (1.0 - sig))
        dgate_ref[0, :, head_slice(h)] = dgate.astype(bf16)
        total = total + jnp.sum(grad * n * silu, 0, keepdims=True)
        direct = mm(qo_ref[0, h, :, :DK], drule, 0, 0) * DK ** (-0.5)
        direct_ref[0, h] = direct.astype(bf16)
    dgain_ref[0] = total


def first_back_kernel(layout, pair_layout, count, place_ref, *refs):
    dproj_ref, dgate_ref, dlogit_ref, proj_ref, gate_ref, logit_ref, beta_ref, rows_ref, scale_ref = refs[:9]
    pieces = refs[9 : 9 + len(layout)]
    pairs = by_piece(place_ref, refs[9 + len(layout) : 9 + len(layout) + count])
    one_ref, rowsum_ref, gainsum_ref = refs[-3:]
    gates = {}
    for (k, start, size, block), ref in zip(pair_layout, pairs):
        gates[k] = ref
    for (k, start, size, block), piece in zip(layout, pieces):
        lanes = slice(k * block + start, k * block + start + size)
        grad = mm(dgate_ref[...], gate_part(gates[k])[start : start + size], 1, 1)
        for i in range(3):
            grad = grad + mm(dproj_ref[i], piece[i], 1, 1)
        for h in range(beta_ref.shape[0]):
            grad = grad + dlogit_ref[:, h : h + 1].astype(f32) * beta_ref[h : h + 1, lanes]
        at = pl.multiple_of((place_ref[0] ^ k) * block + start, 128)
        one_ref[:, pl.ds(at, size)] = grad.astype(bf16)
        gainsum_ref[:, lanes] = jnp.sum(
            grad * (rows_ref[:, lanes].astype(f32) * scale_ref[...]), 0, keepdims=True
        )
    total = dgate_ref[...].astype(f32) * gate_ref[...]
    for i in range(3):
        total = total + dproj_ref[i].astype(f32) * proj_ref[i].astype(f32)
    lane = lax.broadcasted_iota(jnp.int32, total.shape, 1) == 0
    logits = jnp.sum(dlogit_ref[...].astype(f32) * logit_ref[...], -1, keepdims=True)
    logits_sum = jnp.where(lane, logits, 0.0)
    total = total + logits_sum
    ones = jnp.ones((8, total.shape[1]), f32)
    rowsum_ref[...] = mm(ones, total, 1, 1)[:1]


def back_kernel(count, *refs):
    (
        proj_ref,
        before_ref,
        taps_ref,
        logit_ref,
        x_ref,
        wu_ref,
        state_ref,
        drule_ref,
    ) = refs[:8]
    dproj_ref, last_ref, first_ref, dtaps_ref, dlogit_ref = refs[-5:]
    others = refs[8 : 8 + 2 * count - 1]
    directs, nexts = others[:count], others[count:]
    heads = state_ref.shape[1]
    taps = taps_ref[...]
    length = proj_ref.shape[2]
    betas = jax.nn.sigmoid(logit_ref[0])
    r, c = places(length, length)
    strict = (r > c).astype(f32)
    full = (r >= c).astype(f32)
    zeros = jnp.zeros((PAD, DK), f32)
    for h in range(heads):
        parts, (qu, q_inv), (ku, k_inv), vu = rule_inputs(proj_ref, before_ref, taps, h)
        q, k, v = qu.astype(bf16), ku.astype(bf16), vu.astype(bf16)
        beta = betas[:, h : h + 1]
        leave = jnp.zeros((DK, DK), f32)
        for j in reversed(range(count)):
            here = directs[j][0, h].astype(f32)
            leave = here if j == count - 1 else mm(nexts[j][0, h], leave, 0, 0) + here
        state = state_ref[0, h]
        wu = wu_ref[0, h]
        u = wu[:, DK:] - mm(wu[:, :DK], state)
        resid = v.astype(f32) - mm(k, state)
        dout = drule_ref[0, :, head_slice(h)] * DK ** (-0.5)
        gram = mm(k, k, 1, 1)
        scores = mm(q, k, 1, 1) * full
        du = mm(scores, dout, 0, 0) + mm(k, leave)
        y = mm(x_ref[0, h], du, 0, 0)
        by = beta * y
        da = -(mm(y, u, 1, 1, 1) * strict)
        dbeta = jnp.sum(y * resid, -1, keepdims=True) + jnp.sum(da * gram, -1, keepdims=True)
        dgram = beta * da
        dscores = mm(dout, u, 1, 1, 1) * full
        dq = mm(dout, state, 1, 1, 1) + mm(dscores, k, 1, 0, 1)
        dk = (
            mm(dgram, k, 1, 0, 1)
            + mm(dgram, k, 0, 0, 1)
            + mm(dscores, q, 0, 0, 1)
            + mm(u, leave, 1, 1, 1)
            - mm(by, state, 1, 1, 1)
        )
        dlogit_ref[0, :, h : h + 1] = (dbeta * beta * (1.0 - beta)).astype(bf16)
        dq = (dq - qu * jnp.sum(qu * dq, -1, keepdims=True)) * q_inv
        dk = (dk - ku * jnp.sum(ku * dk, -1, keepdims=True)) * k_inv
        for i, dact in enumerate((dq, dk, by)):
            shifts, out, sig, _ = parts[i]
            dconv = dact * sig * (1.0 + out * (1.0 - sig))
            ext = jnp.concatenate([zeros, dconv, zeros], 0)
            total = None
            for j in range(KW):
                at = i * KW + j
                dtaps_ref[0, at : at + 1, head_slice(h)] = jnp.sum(
                    dconv * shifts[j], 0, keepdims=True
                )
                tap = taps[at : at + 1, head_slice(h)]
                term = tap * ext[KW - 1 - j : KW - 1 - j + PAD + length]
                total = term if total is None else total + term
            first_ref[i, 0, :, head_slice(h)] = total[:PAD]
            last_ref[i, 0, :, head_slice(h)] = total[length:]
            dproj_ref[i, 0, :, head_slice(h)] = total[PAD:].astype(bf16)


def call(kernel, ins, outs, steps, scalar=None, scratch=(), limit=VMEM, alias=None):
    def spec(shape, axis):
        if axis == "any":
            return pl.BlockSpec(memory_space=pl.ANY)
        block = tuple(1 if n == axis else size for n, size in enumerate(shape))
        where = lambda s, *_: tuple(s if n == axis else 0 for n in range(len(shape)))
        if axis is None:
            return pl.BlockSpec(block, where, pipeline_mode=pl.Buffered(1))
        return pl.BlockSpec(block, where)

    given = [] if scalar is None else [scalar]
    return pl.pallas_call(
        kernel,
        cost_estimate=FREE,
        grid_spec=pltpu.PrefetchScalarGridSpec(
            num_scalar_prefetch=len(given),
            grid=(steps,),
            in_specs=[spec(a.shape, axis) for a, axis in ins],
            out_specs=[spec(o.shape, axis) for o, axis in outs],
            scratch_shapes=scratch,
        ),
        out_shape=[o for o, _ in outs],
        input_output_aliases=alias or {},
        compiler_params=pltpu.CompilerParams(vmem_limit_bytes=limit),
    )(*given, *[a for a, _ in ins])


def shape_of(shape, dtype):
    return jax.ShapeDtypeStruct(shape, dtype)


def shifted(array, axis, by):
    devices = lax.axis_size(axis)
    pairs = [(i, i + by) for i in range(devices) if 0 <= i + by < devices]
    return lax.ppermute(array, axis, pairs)


def after(values, *others):
    flat, tree = jax.tree.flatten(values)
    others = jax.tree.leaves(others)
    here = pl.BlockSpec(memory_space=pl.ANY)
    out = pl.pallas_call(
        lambda *refs: None,
        cost_estimate=FREE,
        in_specs=[here] * (len(flat) + len(others)),
        out_specs=[here] * len(flat),
        out_shape=[shape_of(a.shape, a.dtype) for a in flat],
        input_output_aliases={n: n for n in range(len(flat))},
    )(*flat, *others)
    return jax.tree.unflatten(tree, out)


def copies(values):
    count = len(values)

    def kernel(*refs):
        for n in range(count):
            refs[n - count][...] = refs[n][...]

    outs = [(shape_of(a.shape, a.dtype), None) for a in values]
    return call(kernel, [(a, None) for a in values], outs, 1)


def swap(array, bits):
    return lax.ppermute(array, "dp", [(i, i ^ bits) for i in range(4)])


def first_hop(own):
    return swap(own, 1), swap(own, 2)


def halves_of(hop, axis):
    low, high = (jnp.split(part, 2, axis) for part in hop)
    return low[0], high[1]


def gathered_pieces(own, axis, hop=None, halves=None):
    hop = hop or first_hop(own)
    low, high = halves or halves_of(hop, axis)
    return [own, *hop, swap(low, 2), swap(high, 1)]


def far_hop(low, high):
    return swap(low, 1), swap(high, 2)


def near_sums(pieces, far_in, *others):
    own, one, two = pieces
    half = far_in[0].shape
    along = 1 if half[1] < one.shape[1] else 2

    def spec(place):
        where = tuple(place if n == along else 0 for n in range(3))
        return pl.BlockSpec(half, lambda s: where)

    first, second = spec(0), spec(1)
    here = pl.BlockSpec(memory_space=pl.ANY)
    one, two = pl.pallas_call(
        add_halves_kernel,
        cost_estimate=FREE,
        grid=(1,),
        in_specs=[second, first, first, first] + [here] * len(others),
        out_specs=[second, first],
        out_shape=[shape_of(a.shape, a.dtype) for a in (one, two)],
        input_output_aliases={0: 0, 1: 1},
        compiler_params=pltpu.CompilerParams(vmem_limit_bytes=VMEM),
    )(one, two, *far_in, *others)
    return own, one, two


def near_hop(pieces):
    own, one, two = pieces
    return own, swap(one, 1), swap(two, 2)


def add_pair_kernel(own_ref, one_ref, two_ref, *refs):
    gate_ref, out_ref = refs[-2:]
    inner = out_ref.shape[0]

    def added(i, rows):
        parts = (ref[i, rows].astype(f32) for ref in (own_ref, one_ref, two_ref))
        return sum(parts)

    gate_ref[...] = added(0, slice(None))
    for n in range(2):
        out_ref[:, n * inner : (n + 1) * inner] = added(1, slice(n * inner, (n + 1) * inner))


def sum_last(parts, *others):
    own = parts[0]
    ins = [(a, 0) for a in parts] + [(a, "any") for a in others]
    [total] = call(add_last_kernel, ins, [(shape_of(own.shape, f32), 0)], own.shape[0])
    return total


def pack(parts):
    return jnp.concatenate([p.reshape(-1) for p in parts])


def unpack(flat, shapes):
    out, at = [], 0
    for shape in shapes:
        size = 1
        for n in shape:
            size *= n
        out.append(flat[..., at : at + size].reshape(flat.shape[:-1] + tuple(shape)))
        at += size
    return out


def padded(flat, multiple=1024):
    return jnp.pad(flat, (0, -flat.shape[0] % multiple))


def body(
    tokens,
    out_grad,
    domain,
    group_weight,
    w_qkv,
    conv_weight,
    w_beta,
    w_outgate,
    head_gain,
    w_out,
    mixer_gain,
    mlp_gain,
    w_gateup,
    w_down,
):
    dp = lax.axis_size("dp")
    place = lax.axis_index("dp")
    seqs, block, local_width = tokens.shape
    count_rows = seqs * block
    heads = conv_weight.shape[2]
    inner = heads * DK
    column = lax.axis_index("mp") * local_width
    near_four = dp == 4

    def blocks_about(array, axis):
        if not near_four:
            return array
        size = array.shape[axis] // 4
        return jnp.concatenate(
            [lax.dynamic_slice_in_dim(array, (place ^ k) * size, size, axis) for k in range(4)],
            axis,
        )

    width = out_grad.shape[2]
    turn = place if near_four else jnp.int32(0)
    column_about = ((column // (width // 4)) ^ turn) * (width // 4) + column % (width // 4)

    def own(array):
        array = array.reshape(seqs, block, width)
        return lax.dynamic_slice_in_dim(array, column_about, local_width, 2)

    onehot = (domain[..., None] == jnp.arange(3, dtype=jnp.int32)).astype(f32)
    own_counts = jnp.sum(onehot, axis=(0, 1))
    high = jnp.floor(own_counts / 128.0)
    digits = jnp.concatenate([high, own_counts - 128.0 * high]).astype(bf16)
    small = [w_beta, conv_weight, head_gain, mixer_gain, mlp_gain, digits]
    packed = padded(pack(small))
    size = width // 4
    if near_four:
        qkv_hop = first_hop(w_qkv)
        qkv_halves = halves_of(qkv_hop, 1)
        qkv = gathered_pieces(w_qkv, 1, qkv_hop, qkv_halves)
        packed = after(packed, qkv_halves)
        gathered = jnp.stack([packed] + [swap(packed, bits) for bits in (1, 2, 3)])
        half = w_out.shape[1] // 2
        pair_own = jnp.stack(
            [w_outgate, jnp.concatenate([w_out[:, :half], w_out[:, half:]], 0)]
        )
        pair_layout = [(k, 0, size, size) for k in range(4)]
        layout = pair_layout[:3] + [(3, 0, size // 2, size), (3, size // 2, size // 2, size)]
    else:
        gathered = lax.all_gather(packed, "dp")
        qkv = [lax.all_gather(w_qkv, "dp", axis=1, tiled=True)]
        gate_pieces = [lax.all_gather(w_outgate, "dp", axis=0, tiled=True)]
        out_pieces = [lax.all_gather(w_out, "dp", axis=1, tiled=True)]
        layout = pair_layout = [(0, 0, width, width)]
    ranges = [(k * step + start, n) for k, start, n, step in layout]
    g_beta, g_conv, g_head, g_mix, g_mlp, g_digits = unpack(gathered, [a.shape for a in small])
    about_beta = g_beta.reshape(-1, heads)
    full_beta = blocks_about(about_beta, 0)
    full_conv = jnp.moveaxis(blocks_about(g_conv, 0), 0, 3).reshape(3 * KW, inner).astype(f32)
    gain_head = blocks_about(g_head, 0).reshape(1, DK).astype(f32)
    gain_one = blocks_about(g_mix.reshape(1, -1).astype(f32), 1)
    gain_two = g_mlp.reshape(1, -1).astype(f32)
    sums = jnp.sum(g_digits.astype(f32), 0)
    counts = 128.0 * sums[:3] + sums[3:]
    table = group_weight * (domain.shape[0] * domain.shape[1] * dp) / counts
    factor = jnp.sum(onehot * table, -1)[..., None]

    def flat(array):
        return array.reshape(array.shape[:-3] + (count_rows, array.shape[-1]))

    rows = lax.all_gather(tokens, "mp", axis=2, tiled=True)
    if near_four:
        gate_pieces = out_pieces = [lax.all_gather(after(pair_own, packed), "dp")]
    turn_one = turn.reshape(1)
    per_token = (seqs, block)
    square = (seqs, heads, DK, DK)
    hidden_one, proj, tail, logits, scale_one = call(
        partial(project_kernel, layout),
        [(rows, 0), (gain_one, None), (jnp.pad(full_beta, ((0, 0), (0, 128 - heads))), None)]
        + [(a, None) for a in qkv],
        [
            (shape_of(per_token + (width,), bf16), 0),
            (shape_of((3,) + per_token + (inner,), bf16), 1),
            (shape_of((3, seqs, HALO, inner), bf16), 1),
            (shape_of(per_token + (heads,), f32), 0),
            (shape_of(per_token + (1,), f32), 0),
        ],
        seqs,
        scalar=turn_one,
        scratch=[pltpu.VMEM((block, width), bf16)],
    )
    before = shifted(tail, "dp", 1)
    inverse, wu, qo, to = call(
        pre_kernel,
        [(proj, None), (before, None), (full_conv, None), (logits, None)],
        [
            (shape_of((seqs, heads, block, block), f32), None),
            (shape_of((seqs, heads, block, 2 * DK), f32), None),
            (shape_of((seqs, heads, block, 2 * DK), f32), None),
            (shape_of((seqs, heads, DK, 2 * DK), bf16), None),
        ],
        1,
    )
    near = [shifted(to, "dp", c) for c in range(1, dp)]
    rows_about, cotangent = call(
        partial(prepare_kernel, layout),
        [(rows, 0), (out_grad, 0), (factor, 0)],
        [(shape_of(per_token + (width,), bf16), 0)] * 2,
        seqs,
        scalar=turn_one,
    )
    turned = jnp.swapaxes(w_gateup, 1, 2)
    feed_own = [turned, w_down]
    mixer_part, normed, rule, state, gates = call(
        partial(mix_kernel, pair_layout, len(near), len(out_pieces)),
        [(a, 0) for a in near]
        + [(qo, 0), (hidden_one, 0), (gain_head, None)]
        + [(a, None) for a in gate_pieces + out_pieces]
        + [(cotangent, "any")],
        [
            (shape_of(per_token + (width,), bf16), 0),
            (shape_of(per_token + (inner,), bf16), 0),
            (shape_of(per_token + (inner,), f32), 0),
            (shape_of(square, f32), 0),
            (shape_of(per_token + (inner,), f32), 0),
        ],
        seqs,
        scalar=turn_one,
    )
    total = lax.psum(mixer_part, "mp")
    nexts = [shifted(to[..., :DK], "dp", -c) for c in range(1, dp - 1)]
    if near_four:
        gateup, down = (gathered_pieces(a, a.ndim - 1) for a in after(copies(feed_own), mixer_part, nexts))
    else:
        gateup, down = (
            [lax.all_gather(a, "dp", axis=a.ndim - 1, tiled=True)] for a in feed_own
        )
    units = w_down.shape[0]
    two_part, hidden_two, hidden_mlp, grad_pair = call(
        partial(feed_kernel, layout),
        [(rows_about, 0), (total, 0), (cotangent, 0), (gain_two, None)]
        + [(a, None) for a in gateup + down],
        [
            (shape_of(per_token + (width,), bf16), 0),
            (shape_of(per_token + (width,), bf16), 0),
            (shape_of(per_token + (units,), bf16), 0),
            (shape_of((2,) + per_token + (units,), bf16), 1),
        ],
        seqs,
    )
    grad_two = lax.psum(two_part, "mp")

    def feed_gradients(some, *others):
        outs = [(shape_of((m, units, n), bf16), None) for _, n in some for m in (2, 1)]
        base, span = some[0][0], sum(n for _, n in some)
        aligned = base % span == 0
        at = base // span if aligned else 0
        cols = pl.BlockSpec((count_rows, span if aligned else width), lambda s: (0, at))
        made = pl.pallas_call(
            partial(feed_gradient_kernel, base if aligned else 0, some),
            cost_estimate=FREE,
            grid=(1,),
            in_specs=[
                cols,
                cols,
                pl.BlockSpec((2, count_rows, units), lambda s: (0, 0, 0)),
                pl.BlockSpec((count_rows, units), lambda s: (0, 0)),
            ]
            + [pl.BlockSpec(memory_space=pl.ANY)] * len(others),
            out_specs=[pl.BlockSpec(o.shape, lambda s: (0, 0, 0)) for o, _ in outs],
            out_shape=[o for o, _ in outs],
            compiler_params=pltpu.CompilerParams(vmem_limit_bytes=VMEM),
        )(flat(hidden_two), flat(cotangent), flat(grad_pair), flat(hidden_mlp), *others)
        return made[::2], made[1::2]

    if near_four:
        feed_far = feed_gradients(ranges[3:])
        feed_in = [far_hop(*far) for far in feed_far]
        near_gateup, near_down = feed_gradients(ranges[:3], feed_far[0][0])
        first_made = [(near_gateup[0], "any")]
    else:
        [grad_gateup], [grad_down] = feed_gradients(ranges)
        held = first_made = []
    [down_part] = call(
        partial(down_kernel, layout),
        [(hidden_mlp, 0)] + [(a, None) for a in down] + first_made,
        [(shape_of(per_token + (width,), bf16), 0)],
        seqs,
        scalar=turn_one,
    )
    if near_four:
        gateup_added = near_sums(near_gateup, feed_in[0], *feed_in[1], down_part)
        down_added = near_sums(near_down, feed_in[1])
        gateup_sums, down_sums = near_hop(gateup_added), near_hop(down_added)
        down_part = after(down_part, gateup_added[1])
        held = [(a, "any") for a in gateup_sums[1:]]
    mlp_share = lax.psum_scatter(down_part, "mp", scatter_dimension=2, tiled=True)
    grad_mix, middle_own, mlpgain, drule, dgate, dgain, direct = call(
        partial(middle_back_kernel, pair_layout, len(out_pieces)),
        [
            (grad_two, 0),
            (cotangent, 0),
            (rows_about, 0),
            (total, 0),
            (gain_two, None),
            (rule, 0),
            (gates, 0),
            (gain_head, None),
            (qo, 0),
        ]
        + [(a, None) for a in out_pieces]
        + [(down_part, "any")]
        + held,
        [
            (shape_of(per_token + (width,), bf16), 0),
            (shape_of(per_token + (local_width,), f32), 0),
            (shape_of((seqs, 1, width), f32), 0),
            (shape_of(per_token + (inner,), f32), 0),
            (shape_of(per_token + (inner,), bf16), 0),
            (shape_of((seqs, 1, DK), f32), 0),
            (shape_of(square, bf16), 0),
        ],
        seqs,
        scalar=jnp.stack([turn, column_about]),
        scratch=[pltpu.VMEM((block, width), f32)],
    )
    directs = [shifted(direct, "dp", -c) for c in range(1, dp)]
    if near_four:
        pair_grads = call(
            partial(pair_gradient_kernel, [(k * size, size) for k in range(4)]),
            [(flat(a), None) for a in (hidden_one, dgate, normed, grad_mix)],
            [(shape_of((2, size, inner), bf16), None)] * 4,
            1,
        )
        held = [(a, "any") for a in (pair_grads[3], *down_sums[1:])]
    else:
        grad_outgate = jnp.einsum(
            "td,tc->dc", flat(hidden_one), flat(dgate), preferred_element_type=f32
        )
        grad_outproj = jnp.einsum(
            "tc,td->cd", flat(normed), flat(grad_mix), preferred_element_type=f32
        )
        held = []
    dproj, last, first, dtaps, dlogits = call(
        partial(back_kernel, len(directs)),
        [
            (proj, 1),
            (before, 1),
            (full_conv, None),
            (logits, 0),
            (inverse, 0),
            (wu, 0),
            (state, 0),
            (drule, 0),
        ]
        + [(a, 0) for a in directs + nexts]
        + held,
        [
            (shape_of((3,) + per_token + (inner,), bf16), 1),
            (shape_of((3, seqs, PAD, inner), f32), 1),
            (shape_of((3, seqs, PAD, inner), f32), 1),
            (shape_of((seqs, 3 * KW, inner), f32), 0),
            (shape_of(per_token + (heads,), bf16), 0),
        ],
        seqs,
    )
    later = shifted(first, "dp", -1)
    dproj = lax.dynamic_update_slice(dproj, (last + later).astype(bf16), (0, 0, block - PAD, 0))
    one_low, row_part, gain_part = call(
        partial(first_back_kernel, layout, pair_layout, len(gate_pieces)),
        [
            (flat(dproj), None),
            (flat(dgate), None),
            (flat(dlogits), None),
            (flat(proj), None),
            (flat(gates), None),
            (flat(logits), None),
            (about_beta.T.astype(f32), None),
            (flat(rows_about), None),
            (flat(scale_one), None),
        ]
        + [(a, None) for a in qkv + gate_pieces],
        [
            (shape_of((count_rows, width), bf16), None),
            (shape_of((1, count_rows), f32), None),
            (shape_of((1, width), f32), None),
        ],
        1,
        scalar=turn_one,
    )
    one_share = lax.psum_scatter(
        one_low.reshape(seqs, block, width), "mp", scatter_dimension=2, tiled=True
    ).astype(f32)
    made = call(
        partial(qkv_gradient_kernel, ranges),
        [(flat(hidden_one), None), (flat(dproj), None), (flat(dlogits), None), (row_part, "any")],
        [(shape_of((3, n, inner), bf16), None) for _, n in ranges]
        + [(shape_of((heads, width), f32), None)],
        1,
    )

    def pieces(array, axis, about):
        shape = array.shape
        cut = array.reshape(shape[:axis] + (dp, shape[axis] // dp) + shape[axis + 1 :])
        cut = jnp.moveaxis(cut, axis, 0).reshape(dp, -1)
        return blocks_about(cut, 0) if about else cut

    smalls = jnp.concatenate(
        [
            pieces(jnp.sum(dtaps, 0).reshape(3, KW, heads, DK), 3, True),
            pieces(made[-1].T, 0, False),
            pieces(gain_part[0], 0, False),
            pieces(jnp.sum(mlpgain, (0, 1)), 0, False),
            pieces(jnp.sum(dgain, (0, 1)), 0, True),
        ],
        1,
    )
    small_shapes = [a.shape for a in (conv_weight, w_beta, mixer_gain, mlp_gain, head_gain)]
    if near_four:
        gateup_total = sum_last(gateup_sums, made[0])
        down_total = sum_last(down_sums, made[0])
        own_qkv, *near_qkv = near_sums(made[:3], far_hop(made[3], made[4]), gateup_total, down_total)
        smalls = jnp.pad(smalls, ((0, 0), (0, -smalls.shape[1] % 1024))).reshape(dp, -1, 128)
        sent = after(smalls.astype(bf16), down_total)
        got = [swap(sent[bits], bits) for bits in (1, 2, 3)]
        first_mix = (conv_weight.size + w_beta.size) // 128
        last_mix = first_mix + mixer_gain.size // 128
        lines = count_rows // 128 + last_mix - first_mix
        mine, rest = call(
            partial(
                add_small_kernel,
                slice(first_mix, last_mix),
                last_mix + mlp_gain.size // 128,
            ),
            [(a, None) for a in [smalls[0]] + got + [row_part]],
            [
                (shape_of(smalls.shape[1:], f32), None),
                (shape_of((lines + 8 - lines % 8, 128), f32), None),
            ],
            1,
        )
        pair_far = after(jnp.split(pair_grads[3], 2, 1), mine)
        pair_near = near_sums(pair_grads[:3], far_hop(*pair_far))[1:]
        mine = mine.reshape(-1)
        sum_qkv = sum_last(near_hop((own_qkv, *near_qkv)))
        sum_gateup = jnp.swapaxes(gateup_total, 1, 2)
        sum_down = down_total[0]
        sum_outgate, sum_out = call(
            add_pair_kernel,
            [(a, None) for a in near_hop((pair_grads[0], *pair_near))],
            [(shape_of(w_outgate.shape, f32), None), (shape_of(w_out.shape, f32), None)],
            1,
        )
    else:
        gathered = lax.all_gather(smalls.astype(bf16), "dp")
        mine = jnp.sum(
            lax.dynamic_index_in_dim(gathered, place, 1, keepdims=False).astype(f32), 0
        )

        def scattered(array, axis):
            return lax.psum_scatter(array, "dp", scatter_dimension=axis, tiled=True).astype(f32)

        sum_qkv = scattered(made[0], 1)
        sum_outgate = scattered(grad_outgate.astype(bf16), 0)
        sum_out = scattered(grad_outproj.astype(bf16), 1)
        sum_gateup = jnp.swapaxes(scattered(grad_gateup, 2), 1, 2)
        sum_down = scattered(grad_down[0], 1)
    sum_conv, sum_beta, sum_mix, sum_mlp, sum_head = unpack(mine, small_shapes)
    if near_four:
        everyone = lax.optimization_barrier(lax.all_gather(after(rest, near_qkv), "mp"))
        rest_sum = jnp.sum(everyone, 0).reshape(-1)
    else:
        rest_sum = lax.psum(pack([row_part, sum_mix, sum_head]), "mp")
    row_sum, sum_mix, sum_head = unpack(rest_sum, [(count_rows,), sum_mix.shape, sum_head.shape])

    own_tokens = tokens.astype(f32)
    mixed_out = (own_tokens + own(total).astype(f32) + mlp_share.astype(f32)).astype(bf16)
    row_mean = (row_sum / width).reshape(seqs, block, 1)
    gain_own = lax.dynamic_slice_in_dim(gain_one, column, local_width, 1)
    tokens_grad = middle_own + scale_one * (
        one_share * gain_own - own_tokens * scale_one * row_mean
    )
    return (
        mixed_out,
        tokens_grad.astype(bf16),
        sum_qkv,
        sum_conv,
        sum_beta,
        sum_outgate,
        sum_head,
        sum_out,
        sum_mix,
        sum_mlp,
        sum_gateup,
        sum_down,
    )


def solution(mesh):
    return jax.shard_map(
        body,
        mesh=mesh,
        in_specs=(
            P(None, "dp", "mp"),
            P(None, "dp", None),
            P(None, "dp"),
            P(),
            P(None, "dp", "mp"),
            P(None, None, "mp", "dp"),
            P("dp", "mp"),
            P("dp", "mp"),
            P("dp"),
            P("mp", "dp"),
            P("dp"),
            P("dp"),
            P(None, "dp", "mp"),
            P("mp", "dp"),
        ),
        out_specs=(
            P(None, "dp", "mp"),
            P(None, "dp", "mp"),
            P(None, "dp", "mp"),
            P(None, None, "mp", "dp"),
            P("dp", "mp"),
            P("dp", "mp"),
            P("dp"),
            P("mp", "dp"),
            P("dp"),
            P("dp"),
            P(None, "dp", "mp"),
            P("mp", "dp"),
        ),
        check_vma=False,
    )
```

```python
from functools import partial

import jax
import jax.numpy as jnp
from jax import lax
from jax.experimental import pallas as pl
from jax.experimental.pallas import tpu as pltpu
from jax.sharding import PartitionSpec as P

DK = 128
KW = 4
PAD = 8
HALO = 16
ROWS = 16
VMEM = 58 * 2**20
FREE = pl.CostEstimate(flops=0, transcendentals=0, bytes_accessed=0)

eps_norm = 1e-06
eps_unit = 1e-06

f32 = jnp.float32
bf16 = jnp.bfloat16


def split(v):
    if v.dtype == bf16:
        return v, None
    high = v.astype(bf16)
    return high, (v - high.astype(f32)).astype(bf16)


def mm(a, b, ca=1, cb=0, passes=3):
    def one(x, y):
        return lax.dot_general(x, y, (((ca,), (cb,)), ((), ())), preferred_element_type=f32)

    if passes == 1:
        return one(a.astype(bf16), b.astype(bf16))
    (ah, al), (bh, bl) = split(a), split(b)
    out = one(ah, bh)
    if bl is not None:
        out = out + one(ah, bl)
    if al is not None:
        out = out + one(al, bh)
    return out


def places(rows, cols):
    return (
        lax.broadcasted_iota(jnp.int32, (rows, cols), 0),
        lax.broadcasted_iota(jnp.int32, (rows, cols), 1),
    )


def unit_lower_inverses(blocks):
    size = blocks[0].shape[0]
    if size > 128:
        half = size // 2
        parts = unit_lower_inverses(
            [a[:half, :half] for a in blocks] + [a[half:, half:] for a in blocks]
        )
        firsts, seconds = parts[: len(blocks)], parts[len(blocks) :]
        inner = [mm(a[half:, :half], x) for a, x in zip(blocks, firsts)]
        lower = [-mm(x, y) for x, y in zip(seconds, inner)]
        zero = jnp.zeros((half, half), f32)
        return [
            jnp.concatenate(
                [jnp.concatenate([x, zero], 1), jnp.concatenate([y, z], 1)], 0
            )
            for x, y, z in zip(firsts, lower, seconds)
        ]
    rows, cols = places(size, size)
    eye = (rows == cols).astype(f32)
    level = 0
    inverses = None
    while (1 << level) < size:
        mask = (
            ((rows >> (level + 1)) == (cols >> (level + 1)))
            & (((rows >> level) & 1) == 1)
            & (((cols >> level) & 1) == 0)
        ).astype(f32)
        lows = [a * mask for a in blocks]
        if level == 0:
            inverses = [eye - low for low in lows]
        else:
            inner = [mm(low, x) for low, x in zip(lows, inverses)]
            inverses = [x - mm(x, y) for x, y in zip(inverses, inner)]
        level += 1
    return inverses


def head_slice(h):
    return slice(h * DK, (h + 1) * DK)


def convolve(proj_ref, before_ref, taps, i, h):
    own = proj_ref[i, 0, :, head_slice(h)].astype(f32)
    length = own.shape[0]
    ext = jnp.concatenate([before_ref[i, 0, :, head_slice(h)].astype(f32), own], 0)
    shifts = [ext[HALO - KW + 1 + j : HALO - KW + 1 + j + length] for j in range(KW)]
    out = None
    for j in range(KW):
        tap = taps[i * KW + j : i * KW + j + 1, head_slice(h)]
        out = tap * shifts[j] if out is None else out + tap * shifts[j]
    sig = jax.nn.sigmoid(out)
    return shifts, out, sig, out * sig


def unit(acts):
    inv = lax.rsqrt(jnp.sum(acts * acts, -1, keepdims=True) + eps_unit)
    return acts * inv, inv


def rule_inputs(proj_ref, before_ref, taps, h):
    parts = [convolve(proj_ref, before_ref, taps, i, h) for i in range(3)]
    q, q_inv = unit(parts[0][3])
    k, k_inv = unit(parts[1][3])
    return parts, (q, q_inv), (k, k_inv), parts[2][3]


def norm_factor(values):
    return lax.rsqrt(jnp.mean(values * values, -1, keepdims=True) + eps_norm)


def project_kernel(layout, *refs):
    place_ref, rows_ref, gain_ref, beta_ref = refs[:4]
    pieces = refs[4 : 4 + len(layout)]
    hidden_ref, proj_ref, tail_ref, logit_ref, scale_ref, keep_ref = refs[4 + len(layout) :]
    rows = rows_ref[0].astype(f32)
    scale = norm_factor(rows)
    scale_ref[0] = scale
    keep_ref[...] = (rows * scale * gain_ref[...]).astype(bf16)
    logits = mm(keep_ref[...], beta_ref[...])
    logit_ref[0] = logits[:, : logit_ref.shape[2]]
    sums = [None] * 3
    for (k, start, size, block), piece in zip(layout, pieces):
        at = pl.multiple_of((place_ref[0] ^ k) * block + start, 128)
        part = keep_ref[:, pl.ds(at, size)]
        hidden_ref[0, :, k * block + start : k * block + start + size] = part
        for i in range(3):
            term = mm(part, piece[i])
            sums[i] = term if sums[i] is None else sums[i] + term
    for i in range(3):
        low = sums[i].astype(bf16)
        proj_ref[i, 0] = low
        tail_ref[i, 0] = low[low.shape[0] - HALO :]


def pre_kernel(proj_ref, before_ref, taps_ref, logit_ref, x_ref, wu_ref, qo_ref, to_ref):
    seqs, heads = to_ref.shape[:2]
    taps = taps_ref[...]
    length = proj_ref.shape[2]
    r, c = places(length, length)
    strict = (r > c).astype(f32)
    full = (r >= c).astype(f32)
    saved, blocks = [], []
    for s in range(seqs):
        betas = jax.nn.sigmoid(logit_ref[s])
        rows, before = proj_ref.at[:, s : s + 1], before_ref.at[:, s : s + 1]
        for h in range(heads):
            _, (q, _), (k, _), v = rule_inputs(rows, before, taps, h)
            q, k, v = q.astype(bf16), k.astype(bf16), v.astype(bf16)
            beta = betas[:, h : h + 1]
            blocks.append(beta * mm(k, k, 1, 1) * strict)
            saved.append((s, h, q, k, v, beta))
    inverses = unit_lower_inverses(blocks)
    r, c = places(DK, DK)
    eye = (r == c).astype(f32)
    for (s, h, q, k, v, beta), x in zip(saved, inverses):
        x_ref[s, h] = x
        kv = jnp.concatenate([k.astype(f32), v.astype(f32)], 1) * beta
        wu = mm(x, kv)
        wu_ref[s, h] = wu
        scores = mm(q, k, 1, 1) * full
        pwu = mm(scores, wu)
        qo_ref[s, h, :, :DK] = q.astype(f32) - pwu[:, :DK]
        qo_ref[s, h, :, DK:] = pwu[:, DK:]
        kwu = mm(k, wu, 0, 0)
        to_ref[s, h, :, :DK] = (eye - kwu[:, :DK]).astype(bf16)
        to_ref[s, h, :, DK:] = kwu[:, DK:].astype(bf16)


def by_piece(place_ref, refs):
    if len(refs) > 1 or len(refs[0].shape) < 4:
        return refs
    return [refs[0].at[place_ref[0] ^ k] for k in range(4)]


def gate_part(ref):
    return ref.at[0] if len(ref.shape) == 3 else ref


def out_columns(layout, refs):
    for (k, start, size, block), ref in zip(layout, refs):
        at, half = k * block + start, size // 2
        if len(ref.shape) == 2:
            yield at, size, ref
            continue
        inner = ref.shape[1] // 2
        yield at, half, ref.at[1, :inner]
        yield at + half, half, ref.at[1, inner:]


def mix_kernel(layout, count, pieces, place_ref, *refs):
    near, rest = refs[:count], refs[count:]
    qo_ref, hidden_ref, gain_ref = rest[:3]
    gate_pieces = by_piece(place_ref, rest[3 : 3 + pieces])
    outs = by_piece(place_ref, rest[3 + pieces : 3 + 2 * pieces])
    part_ref, normed_ref, rule_ref, state_ref, gate_ref = rest[-5:]
    gates = None
    for (k, start, size, block), ref in zip(layout, gate_pieces):
        at = k * block + start
        term = mm(hidden_ref[0, :, at : at + size], gate_part(ref)[...])
        gates = term if gates is None else gates + term
    gate_ref[0] = gates
    heads = state_ref.shape[1]
    for h in range(heads):
        state = near[-1][0, h, :, DK:].astype(f32)
        for ref in reversed(near[:-1]):
            state = mm(ref[0, h, :, :DK], state) + ref[0, h, :, DK:].astype(f32)
        state_ref[0, h] = state
        qo = qo_ref[0, h]
        out = (mm(qo[:, :DK], state) + qo[:, DK:]) * DK ** (-0.5)
        rule_ref[0, :, head_slice(h)] = out
        gate = gate_ref[0, :, head_slice(h)]
        normed = out * norm_factor(out) * gain_ref[...] * (gate * jax.nn.sigmoid(gate))
        normed_ref[0, :, head_slice(h)] = normed.astype(bf16)
    for at, size, ref in out_columns(layout, outs):
        part_ref[0, :, at : at + size] = mm(normed_ref[0], ref[...]).astype(bf16)


def prepare_kernel(layout, place_ref, rows_ref, grad_ref, factor_ref, about_ref, cot_ref):
    for k, start, size, block in layout:
        at = pl.multiple_of((place_ref[0] ^ k) * block + start, 128)
        to = slice(k * block + start, k * block + start + size)
        about_ref[0, :, to] = rows_ref[0, :, pl.ds(at, size)]
        grad = grad_ref[0, :, pl.ds(at, size)].astype(f32) * factor_ref[0]
        cot_ref[0, :, to] = grad.astype(bf16)


def down_kernel(layout, place_ref, mlp_ref, *refs):
    part_ref = refs[-1]
    for (k, start, size, block), ref in zip(layout, refs):
        at = pl.multiple_of((place_ref[0] ^ k) * block + start, 128)
        part_ref[0, :, pl.ds(at, size)] = mm(mlp_ref[0], ref[...]).astype(bf16)


def feed_gradient_kernel(base, ranges, hidden_ref, cot_ref, pair_ref, mlp_ref, *outs):
    outs = outs[-2 * len(ranges) :]
    for n, (start, size) in enumerate(ranges):
        start = start - base
        hidden = hidden_ref[:, start : start + size]
        outs[2 * n][0] = mm(pair_ref[0], hidden, 0, 0).astype(bf16)
        outs[2 * n][1] = mm(pair_ref[1], hidden, 0, 0).astype(bf16)
        outs[2 * n + 1][0] = mm(mlp_ref[...], cot_ref[:, start : start + size], 0, 0).astype(bf16)


def qkv_gradient_kernel(ranges, hidden_ref, dproj_ref, dlogit_ref, *outs):
    outs = outs[-len(ranges) - 1 :]
    for (start, size), out in zip(ranges, outs[:-1]):
        hidden = hidden_ref[:, start : start + size]
        for i in range(3):
            out[i] = mm(hidden, dproj_ref[i], 0, 0).astype(bf16)
    outs[-1][...] = mm(dlogit_ref[...], hidden_ref[...], 0, 0)


def pair_gradient_kernel(ranges, hidden_ref, dgate_ref, normed_ref, mix_ref, *outs):
    inner = normed_ref.shape[1]
    for (start, size), out in zip(ranges, outs):
        out[0] = mm(hidden_ref[:, start : start + size], dgate_ref[...], 0, 0).astype(bf16)
        for n in range(2):
            at = start + n * size // 2
            mix = mix_ref[:, at : at + size // 2]
            out[1, n * inner : (n + 1) * inner] = mm(normed_ref[...], mix, 0, 0).astype(bf16)


def add_halves_kernel(*refs):
    one_ref, two_ref, low_ref, high_ref, one_out, two_out = refs[:4] + refs[-2:]
    one_out[...] = (one_ref[...].astype(f32) + high_ref[...].astype(f32)).astype(bf16)
    two_out[...] = (two_ref[...].astype(f32) + low_ref[...].astype(f32)).astype(bf16)


def add_small_kernel(mix_rows, head_row, *refs):
    *parts, row_ref, out_ref, rest_ref = refs
    total = sum(ref[...].astype(f32) for ref in parts)
    out_ref[...] = total
    lines = [row_ref[:, n * 128 : (n + 1) * 128] for n in range(row_ref.shape[1] // 128)]
    lines += [total[mix_rows], total[head_row : head_row + 1]]
    used = len(lines) - 2 + mix_rows.stop - mix_rows.start + 1
    lines.append(jnp.zeros((rest_ref.shape[0] - used, 128), f32))
    rest_ref[...] = jnp.concatenate(lines, 0)


def add_last_kernel(*refs):
    own_ref, one_ref, two_ref, out_ref = refs[:3] + refs[-1:]
    out_ref[...] = own_ref[...].astype(f32) + one_ref[...].astype(f32) + two_ref[...].astype(f32)


def feed_kernel(layout, *refs):
    rows_ref, total_ref, cot_ref, gain_ref = refs[:4]
    count = len(layout)
    gateups, downs = (refs[4 + n * count : 4 + (n + 1) * count] for n in range(2))
    two_ref, hidden_ref, mlp_ref, pair_ref = refs[-4:]
    middle = rows_ref[0].astype(f32) + total_ref[0].astype(f32)
    hidden_ref[0] = (middle * norm_factor(middle) * gain_ref[...]).astype(bf16)
    gate, up, grad = None, None, None
    for (k, start, size, block), w_gateup, w_down in zip(layout, gateups, downs):
        lanes = slice(k * block + start, k * block + start + size)
        hidden = hidden_ref[0, :, lanes]
        terms = (
            mm(hidden, w_gateup[0], 1, 1),
            mm(hidden, w_gateup[1], 1, 1),
            mm(cot_ref[0, :, lanes], w_down[...], 1, 1),
        )
        if gate is None:
            gate, up, grad = terms
        else:
            gate, up, grad = gate + terms[0], up + terms[1], grad + terms[2]
    sig = jax.nn.sigmoid(gate)
    silu = gate * sig
    mlp_ref[0] = (silu * up).astype(bf16)
    first = (grad * up * (sig + silu * (1.0 - sig))).astype(bf16)
    second = (grad * silu).astype(bf16)
    pair_ref[0, 0] = first
    pair_ref[1, 0] = second
    for (k, start, size, block), w_gateup in zip(layout, gateups):
        lanes = slice(k * block + start, k * block + start + size)
        two = mm(first, w_gateup[0]) + mm(second, w_gateup[1])
        two_ref[0, :, lanes] = two.astype(bf16)


def middle_back_kernel(layout, pieces, at_ref, *refs):
    two_ref, cot_ref, rows_ref, total_ref, gain_ref, rule_ref, gate_ref, head_gain_ref, qo_ref = refs[:9]
    outs = by_piece(at_ref, refs[9 : 9 + pieces])
    mix_ref, own_ref, mlpgain_ref, drule_ref, dgate_ref, dgain_ref, direct_ref, keep_ref = refs[-8:]
    full = rows_ref.shape[2]
    gain_sum = None
    for start in range(0, rows_ref.shape[1], ROWS):
        at = slice(start, start + ROWS)
        middle = rows_ref[0, at].astype(f32) + total_ref[0, at].astype(f32)
        two = two_ref[0, at].astype(f32)
        factor = norm_factor(middle)
        normal = middle * factor
        term = jnp.sum((two * normal).reshape(ROWS // 8, 8, full), 0)
        gain_sum = term if gain_sum is None else gain_sum + term
        scaled = two * gain_ref[...]
        mean = jnp.mean(scaled * normal, -1, keepdims=True)
        keep = cot_ref[0, at].astype(f32) + factor * (scaled - normal * mean)
        keep_ref[at] = keep
        mix_ref[0, at] = keep.astype(bf16)
    mlpgain_ref[0] = jnp.sum(gain_sum, 0, keepdims=True)
    width = own_ref.shape[2]
    own_ref[0] = keep_ref[:, pl.ds(pl.multiple_of(at_ref[1], 128), width)]
    grads = None
    for at, size, ref in out_columns(layout, outs):
        term = mm(mix_ref[0, :, at : at + size], ref[...], 1, 1)
        grads = term if grads is None else grads + term
    total = jnp.zeros((1, DK), f32)
    for h in range(direct_ref.shape[1]):
        grad = grads[:, head_slice(h)]
        out = rule_ref[0, :, head_slice(h)]
        gate = gate_ref[0, :, head_slice(h)]
        inv = norm_factor(out)
        n = out * inv
        sig = jax.nn.sigmoid(gate)
        silu = gate * sig
        gg = grad * head_gain_ref[...]
        dn = gg * silu
        drule = inv * (dn - n * jnp.mean(dn * n, -1, keepdims=True))
        drule_ref[0, :, head_slice(h)] = drule
        dgate = gg * n * sig * (1.0 + gate * (1.0 - sig))
        dgate_ref[0, :, head_slice(h)] = dgate.astype(bf16)
        total = total + jnp.sum(grad * n * silu, 0, keepdims=True)
        direct = mm(qo_ref[0, h, :, :DK], drule, 0, 0) * DK ** (-0.5)
        direct_ref[0, h] = direct.astype(bf16)
    dgain_ref[0] = total


def first_back_kernel(layout, pair_layout, count, place_ref, *refs):
    dproj_ref, dgate_ref, dlogit_ref, proj_ref, gate_ref, logit_ref, beta_ref, rows_ref, scale_ref = refs[:9]
    pieces = refs[9 : 9 + len(layout)]
    pairs = by_piece(place_ref, refs[9 + len(layout) : 9 + len(layout) + count])
    one_ref, rowsum_ref, gainsum_ref = refs[-3:]
    gates = {}
    for (k, start, size, block), ref in zip(pair_layout, pairs):
        gates[k] = ref
    for (k, start, size, block), piece in zip(layout, pieces):
        lanes = slice(k * block + start, k * block + start + size)
        grad = mm(dgate_ref[...], gate_part(gates[k])[start : start + size], 1, 1)
        for i in range(3):
            grad = grad + mm(dproj_ref[i], piece[i], 1, 1)
        for h in range(beta_ref.shape[0]):
            grad = grad + dlogit_ref[:, h : h + 1].astype(f32) * beta_ref[h : h + 1, lanes]
        at = pl.multiple_of((place_ref[0] ^ k) * block + start, 128)
        one_ref[:, pl.ds(at, size)] = grad.astype(bf16)
        gainsum_ref[:, lanes] = jnp.sum(
            grad * (rows_ref[:, lanes].astype(f32) * scale_ref[...]), 0, keepdims=True
        )
    total = dgate_ref[...].astype(f32) * gate_ref[...]
    for i in range(3):
        total = total + dproj_ref[i].astype(f32) * proj_ref[i].astype(f32)
    lane = lax.broadcasted_iota(jnp.int32, total.shape, 1) == 0
    logits = jnp.sum(dlogit_ref[...].astype(f32) * logit_ref[...], -1, keepdims=True)
    logits_sum = jnp.where(lane, logits, 0.0)
    total = total + logits_sum
    ones = jnp.ones((8, total.shape[1]), f32)
    rowsum_ref[...] = mm(ones, total, 1, 1)[:1]


def back_kernel(count, *refs):
    (
        proj_ref,
        before_ref,
        taps_ref,
        logit_ref,
        x_ref,
        wu_ref,
        state_ref,
        drule_ref,
    ) = refs[:8]
    dproj_ref, last_ref, first_ref, dtaps_ref, dlogit_ref = refs[-5:]
    others = refs[8 : 8 + 2 * count - 1]
    directs, nexts = others[:count], others[count:]
    heads = state_ref.shape[1]
    taps = taps_ref[...]
    length = proj_ref.shape[2]
    betas = jax.nn.sigmoid(logit_ref[0])
    r, c = places(length, length)
    strict = (r > c).astype(f32)
    full = (r >= c).astype(f32)
    zeros = jnp.zeros((PAD, DK), f32)
    for h in range(heads):
        parts, (qu, q_inv), (ku, k_inv), vu = rule_inputs(proj_ref, before_ref, taps, h)
        q, k, v = qu.astype(bf16), ku.astype(bf16), vu.astype(bf16)
        beta = betas[:, h : h + 1]
        leave = jnp.zeros((DK, DK), f32)
        for j in reversed(range(count)):
            here = directs[j][0, h].astype(f32)
            leave = here if j == count - 1 else mm(nexts[j][0, h], leave, 0, 0) + here
        state = state_ref[0, h]
        wu = wu_ref[0, h]
        u = wu[:, DK:] - mm(wu[:, :DK], state)
        resid = v.astype(f32) - mm(k, state)
        dout = drule_ref[0, :, head_slice(h)] * DK ** (-0.5)
        gram = mm(k, k, 1, 1)
        scores = mm(q, k, 1, 1) * full
        du = mm(scores, dout, 0, 0) + mm(k, leave)
        y = mm(x_ref[0, h], du, 0, 0)
        by = beta * y
        da = -(mm(y, u, 1, 1, 1) * strict)
        dbeta = jnp.sum(y * resid, -1, keepdims=True) + jnp.sum(da * gram, -1, keepdims=True)
        dgram = beta * da
        dscores = mm(dout, u, 1, 1, 1) * full
        dq = mm(dout, state, 1, 1, 1) + mm(dscores, k, 1, 0, 1)
        dk = (
            mm(dgram, k, 1, 0, 1)
            + mm(dgram, k, 0, 0, 1)
            + mm(dscores, q, 0, 0, 1)
            + mm(u, leave, 1, 1, 1)
            - mm(by, state, 1, 1, 1)
        )
        dlogit_ref[0, :, h : h + 1] = (dbeta * beta * (1.0 - beta)).astype(bf16)
        dq = (dq - qu * jnp.sum(qu * dq, -1, keepdims=True)) * q_inv
        dk = (dk - ku * jnp.sum(ku * dk, -1, keepdims=True)) * k_inv
        for i, dact in enumerate((dq, dk, by)):
            shifts, out, sig, _ = parts[i]
            dconv = dact * sig * (1.0 + out * (1.0 - sig))
            ext = jnp.concatenate([zeros, dconv, zeros], 0)
            total = None
            for j in range(KW):
                at = i * KW + j
                dtaps_ref[0, at : at + 1, head_slice(h)] = jnp.sum(
                    dconv * shifts[j], 0, keepdims=True
                )
                tap = taps[at : at + 1, head_slice(h)]
                term = tap * ext[KW - 1 - j : KW - 1 - j + PAD + length]
                total = term if total is None else total + term
            first_ref[i, 0, :, head_slice(h)] = total[:PAD]
            last_ref[i, 0, :, head_slice(h)] = total[length:]
            dproj_ref[i, 0, :, head_slice(h)] = total[PAD:].astype(bf16)


def call(kernel, ins, outs, steps, scalar=None, scratch=(), limit=VMEM, alias=None):
    def spec(shape, axis):
        if axis == "any":
            return pl.BlockSpec(memory_space=pl.ANY)
        block = tuple(1 if n == axis else size for n, size in enumerate(shape))
        where = lambda s, *_: tuple(s if n == axis else 0 for n in range(len(shape)))
        if axis is None:
            return pl.BlockSpec(block, where, pipeline_mode=pl.Buffered(1))
        return pl.BlockSpec(block, where)

    given = [] if scalar is None else [scalar]
    return pl.pallas_call(
        kernel,
        cost_estimate=FREE,
        grid_spec=pltpu.PrefetchScalarGridSpec(
            num_scalar_prefetch=len(given),
            grid=(steps,),
            in_specs=[spec(a.shape, axis) for a, axis in ins],
            out_specs=[spec(o.shape, axis) for o, axis in outs],
            scratch_shapes=scratch,
        ),
        out_shape=[o for o, _ in outs],
        input_output_aliases=alias or {},
        compiler_params=pltpu.CompilerParams(vmem_limit_bytes=limit),
    )(*given, *[a for a, _ in ins])


def shape_of(shape, dtype):
    return jax.ShapeDtypeStruct(shape, dtype)


def shifted(array, axis, by):
    devices = lax.axis_size(axis)
    pairs = [(i, i + by) for i in range(devices) if 0 <= i + by < devices]
    return lax.ppermute(array, axis, pairs)


def after(values, *others):
    flat, tree = jax.tree.flatten(values)
    others = jax.tree.leaves(others)
    here = pl.BlockSpec(memory_space=pl.ANY)
    out = pl.pallas_call(
        lambda *refs: None,
        cost_estimate=FREE,
        in_specs=[here] * (len(flat) + len(others)),
        out_specs=[here] * len(flat),
        out_shape=[shape_of(a.shape, a.dtype) for a in flat],
        input_output_aliases={n: n for n in range(len(flat))},
    )(*flat, *others)
    return jax.tree.unflatten(tree, out)


def copies(values):
    count = len(values)

    def kernel(*refs):
        for n in range(count):
            refs[n - count][...] = refs[n][...]

    outs = [(shape_of(a.shape, a.dtype), None) for a in values]
    return call(kernel, [(a, None) for a in values], outs, 1)


def swap(array, bits):
    return lax.ppermute(array, "dp", [(i, i ^ bits) for i in range(4)])


def first_hop(own):
    return swap(own, 1), swap(own, 2)


def halves_of(hop, axis):
    low, high = (jnp.split(part, 2, axis) for part in hop)
    return low[0], high[1]


def gathered_pieces(own, axis, hop=None, halves=None):
    hop = hop or first_hop(own)
    low, high = halves or halves_of(hop, axis)
    return [own, *hop, swap(low, 2), swap(high, 1)]


def far_hop(low, high):
    return swap(low, 1), swap(high, 2)


def near_sums(pieces, far_in, *others):
    own, one, two = pieces
    half = far_in[0].shape
    along = 1 if half[1] < one.shape[1] else 2

    def spec(place):
        where = tuple(place if n == along else 0 for n in range(3))
        return pl.BlockSpec(half, lambda s: where)

    first, second = spec(0), spec(1)
    here = pl.BlockSpec(memory_space=pl.ANY)
    one, two = pl.pallas_call(
        add_halves_kernel,
        cost_estimate=FREE,
        grid=(1,),
        in_specs=[second, first, first, first] + [here] * len(others),
        out_specs=[second, first],
        out_shape=[shape_of(a.shape, a.dtype) for a in (one, two)],
        input_output_aliases={0: 0, 1: 1},
        compiler_params=pltpu.CompilerParams(vmem_limit_bytes=VMEM),
    )(one, two, *far_in, *others)
    return own, one, two


def near_hop(pieces):
    own, one, two = pieces
    return own, swap(one, 1), swap(two, 2)


def add_pair_kernel(own_ref, one_ref, two_ref, *refs):
    gate_ref, out_ref = refs[-2:]
    inner = out_ref.shape[0]

    def added(i, rows):
        parts = (ref[i, rows].astype(f32) for ref in (own_ref, one_ref, two_ref))
        return sum(parts)

    gate_ref[...] = added(0, slice(None))
    for n in range(2):
        out_ref[:, n * inner : (n + 1) * inner] = added(1, slice(n * inner, (n + 1) * inner))


def sum_last(parts, *others):
    own = parts[0]
    ins = [(a, 0) for a in parts] + [(a, "any") for a in others]
    [total] = call(add_last_kernel, ins, [(shape_of(own.shape, f32), 0)], own.shape[0])
    return total


def pack(parts):
    return jnp.concatenate([p.reshape(-1) for p in parts])


def unpack(flat, shapes):
    out, at = [], 0
    for shape in shapes:
        size = 1
        for n in shape:
            size *= n
        out.append(flat[..., at : at + size].reshape(flat.shape[:-1] + tuple(shape)))
        at += size
    return out


def padded(flat, multiple=1024):
    return jnp.pad(flat, (0, -flat.shape[0] % multiple))


def body(
    tokens,
    out_grad,
    domain,
    group_weight,
    w_qkv,
    conv_weight,
    w_beta,
    w_outgate,
    head_gain,
    w_out,
    mixer_gain,
    mlp_gain,
    w_gateup,
    w_down,
):
    dp = lax.axis_size("dp")
    place = lax.axis_index("dp")
    seqs, block, local_width = tokens.shape
    count_rows = seqs * block
    heads = conv_weight.shape[2]
    inner = heads * DK
    column = lax.axis_index("mp") * local_width
    near_four = dp == 4

    def blocks_about(array, axis):
        if not near_four:
            return array
        size = array.shape[axis] // 4
        return jnp.concatenate(
            [lax.dynamic_slice_in_dim(array, (place ^ k) * size, size, axis) for k in range(4)],
            axis,
        )

    width = out_grad.shape[2]
    turn = place if near_four else jnp.int32(0)
    column_about = ((column // (width // 4)) ^ turn) * (width // 4) + column % (width // 4)

    def own(array):
        array = array.reshape(seqs, block, width)
        return lax.dynamic_slice_in_dim(array, column_about, local_width, 2)

    onehot = (domain[..., None] == jnp.arange(3, dtype=jnp.int32)).astype(f32)
    own_counts = jnp.sum(onehot, axis=(0, 1))
    high = jnp.floor(own_counts / 128.0)
    digits = jnp.concatenate([high, own_counts - 128.0 * high]).astype(bf16)
    small = [w_beta, conv_weight, head_gain, mixer_gain, mlp_gain, digits]
    packed = padded(pack(small))
    size = width // 4
    if near_four:
        qkv_hop = first_hop(w_qkv)
        qkv_halves = halves_of(qkv_hop, 1)
        qkv = gathered_pieces(w_qkv, 1, qkv_hop, qkv_halves)
        packed = after(packed, qkv_halves)
        gathered = jnp.stack([packed] + [swap(packed, bits) for bits in (1, 2, 3)])
        half = w_out.shape[1] // 2
        pair_own = jnp.stack(
            [w_outgate, jnp.concatenate([w_out[:, :half], w_out[:, half:]], 0)]
        )
        pair_layout = [(k, 0, size, size) for k in range(4)]
        layout = pair_layout[:3] + [(3, 0, size // 2, size), (3, size // 2, size // 2, size)]
    else:
        gathered = lax.all_gather(packed, "dp")
        qkv = [lax.all_gather(w_qkv, "dp", axis=1, tiled=True)]
        gate_pieces = [lax.all_gather(w_outgate, "dp", axis=0, tiled=True)]
        out_pieces = [lax.all_gather(w_out, "dp", axis=1, tiled=True)]
        layout = pair_layout = [(0, 0, width, width)]
    ranges = [(k * step + start, n) for k, start, n, step in layout]
    g_beta, g_conv, g_head, g_mix, g_mlp, g_digits = unpack(gathered, [a.shape for a in small])
    about_beta = g_beta.reshape(-1, heads)
    full_beta = blocks_about(about_beta, 0)
    full_conv = jnp.moveaxis(blocks_about(g_conv, 0), 0, 3).reshape(3 * KW, inner).astype(f32)
    gain_head = blocks_about(g_head, 0).reshape(1, DK).astype(f32)
    gain_one = blocks_about(g_mix.reshape(1, -1).astype(f32), 1)
    gain_two = g_mlp.reshape(1, -1).astype(f32)
    sums = jnp.sum(g_digits.astype(f32), 0)
    counts = 128.0 * sums[:3] + sums[3:]
    table = group_weight * (domain.shape[0] * domain.shape[1] * dp) / counts
    factor = jnp.sum(onehot * table, -1)[..., None]

    def flat(array):
        return array.reshape(array.shape[:-3] + (count_rows, array.shape[-1]))

    rows = lax.all_gather(tokens, "mp", axis=2, tiled=True)
    if near_four:
        gate_pieces = out_pieces = [lax.all_gather(after(pair_own, packed), "dp")]
    turn_one = turn.reshape(1)
    per_token = (seqs, block)
    square = (seqs, heads, DK, DK)
    hidden_one, proj, tail, logits, scale_one = call(
        partial(project_kernel, layout),
        [(rows, 0), (gain_one, None), (jnp.pad(full_beta, ((0, 0), (0, 128 - heads))), None)]
        + [(a, None) for a in qkv],
        [
            (shape_of(per_token + (width,), bf16), 0),
            (shape_of((3,) + per_token + (inner,), bf16), 1),
            (shape_of((3, seqs, HALO, inner), bf16), 1),
            (shape_of(per_token + (heads,), f32), 0),
            (shape_of(per_token + (1,), f32), 0),
        ],
        seqs,
        scalar=turn_one,
        scratch=[pltpu.VMEM((block, width), bf16)],
    )
    before = shifted(tail, "dp", 1)
    inverse, wu, qo, to = call(
        pre_kernel,
        [(proj, None), (before, None), (full_conv, None), (logits, None)],
        [
            (shape_of((seqs, heads, block, block), f32), None),
            (shape_of((seqs, heads, block, 2 * DK), f32), None),
            (shape_of((seqs, heads, block, 2 * DK), f32), None),
            (shape_of((seqs, heads, DK, 2 * DK), bf16), None),
        ],
        1,
    )
    near = [shifted(to, "dp", c) for c in range(1, dp)]
    rows_about, cotangent = call(
        partial(prepare_kernel, layout),
        [(rows, 0), (out_grad, 0), (factor, 0)],
        [(shape_of(per_token + (width,), bf16), 0)] * 2,
        seqs,
        scalar=turn_one,
    )
    turned = jnp.swapaxes(w_gateup, 1, 2)
    feed_own = [turned, w_down]
    mixer_part, normed, rule, state, gates = call(
        partial(mix_kernel, pair_layout, len(near), len(out_pieces)),
        [(a, 0) for a in near]
        + [(qo, 0), (hidden_one, 0), (gain_head, None)]
        + [(a, None) for a in gate_pieces + out_pieces]
        + [(cotangent, "any")],
        [
            (shape_of(per_token + (width,), bf16), 0),
            (shape_of(per_token + (inner,), bf16), 0),
            (shape_of(per_token + (inner,), f32), 0),
            (shape_of(square, f32), 0),
            (shape_of(per_token + (inner,), f32), 0),
        ],
        seqs,
        scalar=turn_one,
    )
    total = lax.psum(mixer_part, "mp")
    nexts = [shifted(to[..., :DK], "dp", -c) for c in range(1, dp - 1)]
    if near_four:
        gateup, down = (gathered_pieces(a, a.ndim - 1) for a in after(copies(feed_own), mixer_part, nexts))
    else:
        gateup, down = (
            [lax.all_gather(a, "dp", axis=a.ndim - 1, tiled=True)] for a in feed_own
        )
    units = w_down.shape[0]
    two_part, hidden_two, hidden_mlp, grad_pair = call(
        partial(feed_kernel, layout),
        [(rows_about, 0), (total, 0), (cotangent, 0), (gain_two, None)]
        + [(a, None) for a in gateup + down],
        [
            (shape_of(per_token + (width,), bf16), 0),
            (shape_of(per_token + (width,), bf16), 0),
            (shape_of(per_token + (units,), bf16), 0),
            (shape_of((2,) + per_token + (units,), bf16), 1),
        ],
        seqs,
    )
    grad_two = lax.psum(two_part, "mp")

    def feed_gradients(some, *others):
        outs = [(shape_of((m, units, n), bf16), None) for _, n in some for m in (2, 1)]
        base, span = some[0][0], sum(n for _, n in some)
        aligned = base % span == 0
        at = base // span if aligned else 0
        cols = pl.BlockSpec((count_rows, span if aligned else width), lambda s: (0, at))
        made = pl.pallas_call(
            partial(feed_gradient_kernel, base if aligned else 0, some),
            cost_estimate=FREE,
            grid=(1,),
            in_specs=[
                cols,
                cols,
                pl.BlockSpec((2, count_rows, units), lambda s: (0, 0, 0)),
                pl.BlockSpec((count_rows, units), lambda s: (0, 0)),
            ]
            + [pl.BlockSpec(memory_space=pl.ANY)] * len(others),
            out_specs=[pl.BlockSpec(o.shape, lambda s: (0, 0, 0)) for o, _ in outs],
            out_shape=[o for o, _ in outs],
            compiler_params=pltpu.CompilerParams(vmem_limit_bytes=VMEM),
        )(flat(hidden_two), flat(cotangent), flat(grad_pair), flat(hidden_mlp), *others)
        return made[::2], made[1::2]

    if near_four:
        feed_far = feed_gradients(ranges[3:])
        feed_in = [far_hop(*far) for far in feed_far]
        near_gateup, near_down = feed_gradients(ranges[:3], feed_far[0][0])
        first_made = [(near_gateup[0], "any")]
    else:
        [grad_gateup], [grad_down] = feed_gradients(ranges)
        held = first_made = []
    [down_part] = call(
        partial(down_kernel, layout),
        [(hidden_mlp, 0)] + [(a, None) for a in down] + first_made,
        [(shape_of(per_token + (width,), bf16), 0)],
        seqs,
        scalar=turn_one,
    )
    if near_four:
        gateup_added = near_sums(near_gateup, feed_in[0], *feed_in[1], down_part)
        down_added = near_sums(near_down, feed_in[1])
        gateup_sums, down_sums = near_hop(gateup_added), near_hop(down_added)
        down_part = after(down_part, gateup_added[1])
        held = [(a, "any") for a in gateup_sums[1:]]
    mlp_share = lax.psum_scatter(down_part, "mp", scatter_dimension=2, tiled=True)
    grad_mix, middle_own, mlpgain, drule, dgate, dgain, direct = call(
        partial(middle_back_kernel, pair_layout, len(out_pieces)),
        [
            (grad_two, 0),
            (cotangent, 0),
            (rows_about, 0),
            (total, 0),
            (gain_two, None),
            (rule, 0),
            (gates, 0),
            (gain_head, None),
            (qo, 0),
        ]
        + [(a, None) for a in out_pieces]
        + [(down_part, "any")]
        + held,
        [
            (shape_of(per_token + (width,), bf16), 0),
            (shape_of(per_token + (local_width,), f32), 0),
            (shape_of((seqs, 1, width), f32), 0),
            (shape_of(per_token + (inner,), f32), 0),
            (shape_of(per_token + (inner,), bf16), 0),
            (shape_of((seqs, 1, DK), f32), 0),
            (shape_of(square, bf16), 0),
        ],
        seqs,
        scalar=jnp.stack([turn, column_about]),
        scratch=[pltpu.VMEM((block, width), f32)],
    )
    directs = [shifted(direct, "dp", -c) for c in range(1, dp)]
    if near_four:
        pair_grads = call(
            partial(pair_gradient_kernel, [(k * size, size) for k in range(4)]),
            [(flat(a), None) for a in (hidden_one, dgate, normed, grad_mix)],
            [(shape_of((2, size, inner), bf16), None)] * 4,
            1,
        )
        held = [(a, "any") for a in (pair_grads[3], *down_sums[1:])]
    else:
        grad_outgate = jnp.einsum(
            "td,tc->dc", flat(hidden_one), flat(dgate), preferred_element_type=f32
        )
        grad_outproj = jnp.einsum(
            "tc,td->cd", flat(normed), flat(grad_mix), preferred_element_type=f32
        )
        held = []
    dproj, last, first, dtaps, dlogits = call(
        partial(back_kernel, len(directs)),
        [
            (proj, 1),
            (before, 1),
            (full_conv, None),
            (logits, 0),
            (inverse, 0),
            (wu, 0),
            (state, 0),
            (drule, 0),
        ]
        + [(a, 0) for a in directs + nexts]
        + held,
        [
            (shape_of((3,) + per_token + (inner,), bf16), 1),
            (shape_of((3, seqs, PAD, inner), f32), 1),
            (shape_of((3, seqs, PAD, inner), f32), 1),
            (shape_of((seqs, 3 * KW, inner), f32), 0),
            (shape_of(per_token + (heads,), bf16), 0),
        ],
        seqs,
    )
    later = shifted(first, "dp", -1)
    dproj = lax.dynamic_update_slice(dproj, (last + later).astype(bf16), (0, 0, block - PAD, 0))
    one_low, row_part, gain_part = call(
        partial(first_back_kernel, layout, pair_layout, len(gate_pieces)),
        [
            (flat(dproj), None),
            (flat(dgate), None),
            (flat(dlogits), None),
            (flat(proj), None),
            (flat(gates), None),
            (flat(logits), None),
            (about_beta.T.astype(f32), None),
            (flat(rows_about), None),
            (flat(scale_one), None),
        ]
        + [(a, None) for a in qkv + gate_pieces],
        [
            (shape_of((count_rows, width), bf16), None),
            (shape_of((1, count_rows), f32), None),
            (shape_of((1, width), f32), None),
        ],
        1,
        scalar=turn_one,
    )
    one_share = lax.psum_scatter(
        one_low.reshape(seqs, block, width), "mp", scatter_dimension=2, tiled=True
    ).astype(f32)
    made = call(
        partial(qkv_gradient_kernel, ranges),
        [(flat(hidden_one), None), (flat(dproj), None), (flat(dlogits), None), (row_part, "any")],
        [(shape_of((3, n, inner), bf16), None) for _, n in ranges]
        + [(shape_of((heads, width), f32), None)],
        1,
    )

    def pieces(array, axis, about):
        shape = array.shape
        cut = array.reshape(shape[:axis] + (dp, shape[axis] // dp) + shape[axis + 1 :])
        cut = jnp.moveaxis(cut, axis, 0).reshape(dp, -1)
        return blocks_about(cut, 0) if about else cut

    smalls = jnp.concatenate(
        [
            pieces(jnp.sum(dtaps, 0).reshape(3, KW, heads, DK), 3, True),
            pieces(made[-1].T, 0, False),
            pieces(gain_part[0], 0, False),
            pieces(jnp.sum(mlpgain, (0, 1)), 0, False),
            pieces(jnp.sum(dgain, (0, 1)), 0, True),
        ],
        1,
    )
    small_shapes = [a.shape for a in (conv_weight, w_beta, mixer_gain, mlp_gain, head_gain)]
    if near_four:
        gateup_total = sum_last(gateup_sums, made[0])
        down_total = sum_last(down_sums, made[0])
        own_qkv, *near_qkv = near_sums(made[:3], far_hop(made[3], made[4]), gateup_total, down_total)
        smalls = jnp.pad(smalls, ((0, 0), (0, -smalls.shape[1] % 1024))).reshape(dp, -1, 128)
        sent = after(smalls.astype(bf16), down_total)
        got = [swap(sent[bits], bits) for bits in (1, 2, 3)]
        first_mix = (conv_weight.size + w_beta.size) // 128
        last_mix = first_mix + mixer_gain.size // 128
        lines = count_rows // 128 + last_mix - first_mix
        mine, rest = call(
            partial(
                add_small_kernel,
                slice(first_mix, last_mix),
                last_mix + mlp_gain.size // 128,
            ),
            [(a, None) for a in [smalls[0]] + got + [row_part]],
            [
                (shape_of(smalls.shape[1:], f32), None),
                (shape_of((lines + 8 - lines % 8, 128), f32), None),
            ],
            1,
        )
        pair_far = after(jnp.split(pair_grads[3], 2, 1), mine)
        pair_near = near_sums(pair_grads[:3], far_hop(*pair_far))[1:]
        mine = mine.reshape(-1)
        sum_qkv = sum_last(near_hop((own_qkv, *near_qkv)))
        sum_gateup = jnp.swapaxes(gateup_total, 1, 2)
        sum_down = down_total[0]
        sum_outgate, sum_out = call(
            add_pair_kernel,
            [(a, None) for a in near_hop((pair_grads[0], *pair_near))],
            [(shape_of(w_outgate.shape, f32), None), (shape_of(w_out.shape, f32), None)],
            1,
        )
    else:
        gathered = lax.all_gather(smalls.astype(bf16), "dp")
        mine = jnp.sum(
            lax.dynamic_index_in_dim(gathered, place, 1, keepdims=False).astype(f32), 0
        )

        def scattered(array, axis):
            return lax.psum_scatter(array, "dp", scatter_dimension=axis, tiled=True).astype(f32)

        sum_qkv = scattered(made[0], 1)
        sum_outgate = scattered(grad_outgate.astype(bf16), 0)
        sum_out = scattered(grad_outproj.astype(bf16), 1)
        sum_gateup = jnp.swapaxes(scattered(grad_gateup, 2), 1, 2)
        sum_down = scattered(grad_down[0], 1)
    sum_conv, sum_beta, sum_mix, sum_mlp, sum_head = unpack(mine, small_shapes)
    if near_four:
        bit = 1
        while bit < lax.axis_size("mp"):
            devices = lax.axis_size("mp")
            rest = rest + lax.ppermute(rest, "mp", [(i, i ^ bit) for i in range(devices)])
            bit *= 2
        rest_sum = rest.reshape(-1)
    else:
        rest_sum = lax.psum(pack([row_part, sum_mix, sum_head]), "mp")
    row_sum, sum_mix, sum_head = unpack(rest_sum, [(count_rows,), sum_mix.shape, sum_head.shape])

    own_tokens = tokens.astype(f32)
    mixed_out = (own_tokens + own(total).astype(f32) + mlp_share.astype(f32)).astype(bf16)
    row_mean = (row_sum / width).reshape(seqs, block, 1)
    gain_own = lax.dynamic_slice_in_dim(gain_one, column, local_width, 1)
    tokens_grad = middle_own + scale_one * (
        one_share * gain_own - own_tokens * scale_one * row_mean
    )
    return (
        mixed_out,
        tokens_grad.astype(bf16),
        sum_qkv,
        sum_conv,
        sum_beta,
        sum_outgate,
        sum_head,
        sum_out,
        sum_mix,
        sum_mlp,
        sum_gateup,
        sum_down,
    )


def solution(mesh):
    return jax.shard_map(
        body,
        mesh=mesh,
        in_specs=(
            P(None, "dp", "mp"),
            P(None, "dp", None),
            P(None, "dp"),
            P(),
            P(None, "dp", "mp"),
            P(None, None, "mp", "dp"),
            P("dp", "mp"),
            P("dp", "mp"),
            P("dp"),
            P("mp", "dp"),
            P("dp"),
            P("dp"),
            P(None, "dp", "mp"),
            P("mp", "dp"),
        ),
        out_specs=(
            P(None, "dp", "mp"),
            P(None, "dp", "mp"),
            P(None, "dp", "mp"),
            P(None, None, "mp", "dp"),
            P("dp", "mp"),
            P("dp", "mp"),
            P("dp"),
            P("mp", "dp"),
            P("dp"),
            P("dp"),
            P(None, "dp", "mp"),
            P("mp", "dp"),
        ),
        check_vma=False,
    )
```

```python
from functools import partial

import jax
import jax.numpy as jnp
from jax import lax
from jax.experimental import pallas as pl
from jax.experimental.pallas import tpu as pltpu
from jax.sharding import PartitionSpec as P

DK = 128
KW = 4
PAD = 8
HALO = 16
ROWS = 16
VMEM = 58 * 2**20
FREE = pl.CostEstimate(flops=0, transcendentals=0, bytes_accessed=0)

eps_norm = 1e-06
eps_unit = 1e-06

f32 = jnp.float32
bf16 = jnp.bfloat16


def split(v):
    if v.dtype == bf16:
        return v, None
    high = v.astype(bf16)
    return high, (v - high.astype(f32)).astype(bf16)


def mm(a, b, ca=1, cb=0, passes=3):
    def one(x, y):
        return lax.dot_general(x, y, (((ca,), (cb,)), ((), ())), preferred_element_type=f32)

    if passes == 1:
        return one(a.astype(bf16), b.astype(bf16))
    (ah, al), (bh, bl) = split(a), split(b)
    out = one(ah, bh)
    if bl is not None:
        out = out + one(ah, bl)
    if al is not None:
        out = out + one(al, bh)
    return out


def places(rows, cols):
    return (
        lax.broadcasted_iota(jnp.int32, (rows, cols), 0),
        lax.broadcasted_iota(jnp.int32, (rows, cols), 1),
    )


def unit_lower_inverses(blocks):
    size = blocks[0].shape[0]
    if size > 128:
        half = size // 2
        parts = unit_lower_inverses(
            [a[:half, :half] for a in blocks] + [a[half:, half:] for a in blocks]
        )
        firsts, seconds = parts[: len(blocks)], parts[len(blocks) :]
        inner = [mm(a[half:, :half], x) for a, x in zip(blocks, firsts)]
        lower = [-mm(x, y) for x, y in zip(seconds, inner)]
        zero = jnp.zeros((half, half), f32)
        return [
            jnp.concatenate(
                [jnp.concatenate([x, zero], 1), jnp.concatenate([y, z], 1)], 0
            )
            for x, y, z in zip(firsts, lower, seconds)
        ]
    rows, cols = places(size, size)
    eye = (rows == cols).astype(f32)
    level = 0
    inverses = None
    while (1 << level) < size:
        mask = (
            ((rows >> (level + 1)) == (cols >> (level + 1)))
            & (((rows >> level) & 1) == 1)
            & (((cols >> level) & 1) == 0)
        ).astype(f32)
        lows = [a * mask for a in blocks]
        if level == 0:
            inverses = [eye - low for low in lows]
        else:
            inner = [mm(low, x) for low, x in zip(lows, inverses)]
            inverses = [x - mm(x, y) for x, y in zip(inverses, inner)]
        level += 1
    return inverses


def head_slice(h):
    return slice(h * DK, (h + 1) * DK)


def convolve(proj_ref, before_ref, taps, i, h):
    own = proj_ref[i, 0, :, head_slice(h)].astype(f32)
    length = own.shape[0]
    ext = jnp.concatenate([before_ref[i, 0, :, head_slice(h)].astype(f32), own], 0)
    shifts = [ext[HALO - KW + 1 + j : HALO - KW + 1 + j + length] for j in range(KW)]
    out = None
    for j in range(KW):
        tap = taps[i * KW + j : i * KW + j + 1, head_slice(h)]
        out = tap * shifts[j] if out is None else out + tap * shifts[j]
    sig = jax.nn.sigmoid(out)
    return shifts, out, sig, out * sig


def unit(acts):
    inv = lax.rsqrt(jnp.sum(acts * acts, -1, keepdims=True) + eps_unit)
    return acts * inv, inv


def rule_inputs(proj_ref, before_ref, taps, h):
    parts = [convolve(proj_ref, before_ref, taps, i, h) for i in range(3)]
    q, q_inv = unit(parts[0][3])
    k, k_inv = unit(parts[1][3])
    return parts, (q, q_inv), (k, k_inv), parts[2][3]


def norm_factor(values):
    return lax.rsqrt(jnp.mean(values * values, -1, keepdims=True) + eps_norm)


def project_kernel(layout, *refs):
    place_ref, rows_ref, gain_ref, beta_ref = refs[:4]
    pieces = refs[4 : 4 + len(layout)]
    hidden_ref, proj_ref, tail_ref, logit_ref, scale_ref, keep_ref = refs[4 + len(layout) :]
    rows = rows_ref[0].astype(f32)
    scale = norm_factor(rows)
    scale_ref[0] = scale
    keep_ref[...] = (rows * scale * gain_ref[...]).astype(bf16)
    logits = mm(keep_ref[...], beta_ref[...])
    logit_ref[0] = logits[:, : logit_ref.shape[2]]
    sums = [None] * 3
    for (k, start, size, block), piece in zip(layout, pieces):
        at = pl.multiple_of((place_ref[0] ^ k) * block + start, 128)
        part = keep_ref[:, pl.ds(at, size)]
        hidden_ref[0, :, k * block + start : k * block + start + size] = part
        for i in range(3):
            term = mm(part, piece[i])
            sums[i] = term if sums[i] is None else sums[i] + term
    for i in range(3):
        low = sums[i].astype(bf16)
        proj_ref[i, 0] = low
        tail_ref[i, 0] = low[low.shape[0] - HALO :]


def pre_kernel(proj_ref, before_ref, taps_ref, logit_ref, x_ref, wu_ref, qo_ref, to_ref):
    seqs, heads = to_ref.shape[:2]
    taps = taps_ref[...]
    length = proj_ref.shape[2]
    r, c = places(length, length)
    strict = (r > c).astype(f32)
    full = (r >= c).astype(f32)
    saved, blocks = [], []
    for s in range(seqs):
        betas = jax.nn.sigmoid(logit_ref[s])
        rows, before = proj_ref.at[:, s : s + 1], before_ref.at[:, s : s + 1]
        for h in range(heads):
            _, (q, _), (k, _), v = rule_inputs(rows, before, taps, h)
            q, k, v = q.astype(bf16), k.astype(bf16), v.astype(bf16)
            beta = betas[:, h : h + 1]
            blocks.append(beta * mm(k, k, 1, 1) * strict)
            saved.append((s, h, q, k, v, beta))
    inverses = unit_lower_inverses(blocks)
    r, c = places(DK, DK)
    eye = (r == c).astype(f32)
    for (s, h, q, k, v, beta), x in zip(saved, inverses):
        x_ref[s, h] = x
        kv = jnp.concatenate([k.astype(f32), v.astype(f32)], 1) * beta
        wu = mm(x, kv)
        wu_ref[s, h] = wu
        scores = mm(q, k, 1, 1) * full
        pwu = mm(scores, wu)
        qo_ref[s, h, :, :DK] = q.astype(f32) - pwu[:, :DK]
        qo_ref[s, h, :, DK:] = pwu[:, DK:]
        kwu = mm(k, wu, 0, 0)
        to_ref[s, h, :, :DK] = (eye - kwu[:, :DK]).astype(bf16)
        to_ref[s, h, :, DK:] = kwu[:, DK:].astype(bf16)


def by_piece(place_ref, refs):
    if len(refs) > 1 or len(refs[0].shape) < 4:
        return refs
    return [refs[0].at[place_ref[0] ^ k] for k in range(4)]


def gate_part(ref):
    return ref.at[0] if len(ref.shape) == 3 else ref


def out_columns(layout, refs):
    for (k, start, size, block), ref in zip(layout, refs):
        at, half = k * block + start, size // 2
        if len(ref.shape) == 2:
            yield at, size, ref
            continue
        inner = ref.shape[1] // 2
        yield at, half, ref.at[1, :inner]
        yield at + half, half, ref.at[1, inner:]


def mix_kernel(layout, count, pieces, place_ref, *refs):
    near, rest = refs[:count], refs[count:]
    qo_ref, hidden_ref, gain_ref = rest[:3]
    gate_pieces = by_piece(place_ref, rest[3 : 3 + pieces])
    outs = by_piece(place_ref, rest[3 + pieces : 3 + 2 * pieces])
    part_ref, normed_ref, rule_ref, state_ref, gate_ref = rest[-5:]
    gates = None
    for (k, start, size, block), ref in zip(layout, gate_pieces):
        at = k * block + start
        term = mm(hidden_ref[0, :, at : at + size], gate_part(ref)[...])
        gates = term if gates is None else gates + term
    gate_ref[0] = gates
    heads = state_ref.shape[1]
    for h in range(heads):
        state = near[-1][0, h, :, DK:].astype(f32)
        for ref in reversed(near[:-1]):
            state = mm(ref[0, h, :, :DK], state) + ref[0, h, :, DK:].astype(f32)
        state_ref[0, h] = state
        qo = qo_ref[0, h]
        out = (mm(qo[:, :DK], state) + qo[:, DK:]) * DK ** (-0.5)
        rule_ref[0, :, head_slice(h)] = out
        gate = gate_ref[0, :, head_slice(h)]
        normed = out * norm_factor(out) * gain_ref[...] * (gate * jax.nn.sigmoid(gate))
        normed_ref[0, :, head_slice(h)] = normed.astype(bf16)
    for at, size, ref in out_columns(layout, outs):
        part_ref[0, :, at : at + size] = mm(normed_ref[0], ref[...]).astype(bf16)


def prepare_kernel(layout, place_ref, rows_ref, grad_ref, factor_ref, about_ref, cot_ref):
    for k, start, size, block in layout:
        at = pl.multiple_of((place_ref[0] ^ k) * block + start, 128)
        to = slice(k * block + start, k * block + start + size)
        about_ref[0, :, to] = rows_ref[0, :, pl.ds(at, size)]
        grad = grad_ref[0, :, pl.ds(at, size)].astype(f32) * factor_ref[0]
        cot_ref[0, :, to] = grad.astype(bf16)


def down_kernel(layout, place_ref, mlp_ref, *refs):
    part_ref = refs[-1]
    for (k, start, size, block), ref in zip(layout, refs):
        at = pl.multiple_of((place_ref[0] ^ k) * block + start, 128)
        part_ref[0, :, pl.ds(at, size)] = mm(mlp_ref[0], ref[...]).astype(bf16)


def feed_gradient_kernel(base, ranges, hidden_ref, cot_ref, pair_ref, mlp_ref, *outs):
    outs = outs[-2 * len(ranges) :]
    for n, (start, size) in enumerate(ranges):
        start = start - base
        hidden = hidden_ref[:, start : start + size]
        outs[2 * n][0] = mm(pair_ref[0], hidden, 0, 0).astype(bf16)
        outs[2 * n][1] = mm(pair_ref[1], hidden, 0, 0).astype(bf16)
        outs[2 * n + 1][0] = mm(mlp_ref[...], cot_ref[:, start : start + size], 0, 0).astype(bf16)


def qkv_gradient_kernel(ranges, hidden_ref, dproj_ref, dlogit_ref, *outs):
    outs = outs[-len(ranges) - 1 :]
    for (start, size), out in zip(ranges, outs[:-1]):
        hidden = hidden_ref[:, start : start + size]
        for i in range(3):
            out[i] = mm(hidden, dproj_ref[i], 0, 0).astype(bf16)
    outs[-1][...] = mm(dlogit_ref[...], hidden_ref[...], 0, 0)


def pair_gradient_kernel(ranges, hidden_ref, dgate_ref, normed_ref, mix_ref, *outs):
    inner = normed_ref.shape[1]
    for (start, size), out in zip(ranges, outs):
        out[0] = mm(hidden_ref[:, start : start + size], dgate_ref[...], 0, 0).astype(bf16)
        for n in range(2):
            at = start + n * size // 2
            mix = mix_ref[:, at : at + size // 2]
            out[1, n * inner : (n + 1) * inner] = mm(normed_ref[...], mix, 0, 0).astype(bf16)


def add_halves_kernel(*refs):
    one_ref, two_ref, low_ref, high_ref, one_out, two_out = refs[:4] + refs[-2:]
    one_out[...] = (one_ref[...].astype(f32) + high_ref[...].astype(f32)).astype(bf16)
    two_out[...] = (two_ref[...].astype(f32) + low_ref[...].astype(f32)).astype(bf16)


def add_small_kernel(mix_rows, head_row, *refs):
    *parts, row_ref, out_ref, rest_ref = refs
    total = sum(ref[...].astype(f32) for ref in parts)
    out_ref[...] = total
    lines = [row_ref[:, n * 128 : (n + 1) * 128] for n in range(row_ref.shape[1] // 128)]
    lines += [total[mix_rows], total[head_row : head_row + 1]]
    used = len(lines) - 2 + mix_rows.stop - mix_rows.start + 1
    lines.append(jnp.zeros((rest_ref.shape[0] - used, 128), f32))
    rest_ref[...] = jnp.concatenate(lines, 0)


def add_last_kernel(*refs):
    own_ref, one_ref, two_ref, out_ref = refs[:3] + refs[-1:]
    out_ref[...] = own_ref[...].astype(f32) + one_ref[...].astype(f32) + two_ref[...].astype(f32)


def feed_kernel(layout, *refs):
    rows_ref, total_ref, cot_ref, gain_ref = refs[:4]
    count = len(layout)
    gateups, downs = (refs[4 + n * count : 4 + (n + 1) * count] for n in range(2))
    two_ref, hidden_ref, mlp_ref, pair_ref = refs[-4:]
    middle = rows_ref[0].astype(f32) + total_ref[0].astype(f32)
    hidden_ref[0] = (middle * norm_factor(middle) * gain_ref[...]).astype(bf16)
    gate, up, grad = None, None, None
    for (k, start, size, block), w_gateup, w_down in zip(layout, gateups, downs):
        lanes = slice(k * block + start, k * block + start + size)
        hidden = hidden_ref[0, :, lanes]
        terms = (
            mm(hidden, w_gateup[0], 1, 1),
            mm(hidden, w_gateup[1], 1, 1),
            mm(cot_ref[0, :, lanes], w_down[...], 1, 1),
        )
        if gate is None:
            gate, up, grad = terms
        else:
            gate, up, grad = gate + terms[0], up + terms[1], grad + terms[2]
    sig = jax.nn.sigmoid(gate)
    silu = gate * sig
    mlp_ref[0] = (silu * up).astype(bf16)
    first = (grad * up * (sig + silu * (1.0 - sig))).astype(bf16)
    second = (grad * silu).astype(bf16)
    pair_ref[0, 0] = first
    pair_ref[1, 0] = second
    for (k, start, size, block), w_gateup in zip(layout, gateups):
        lanes = slice(k * block + start, k * block + start + size)
        two = mm(first, w_gateup[0]) + mm(second, w_gateup[1])
        two_ref[0, :, lanes] = two.astype(bf16)


def middle_back_kernel(layout, pieces, at_ref, *refs):
    two_ref, cot_ref, rows_ref, total_ref, gain_ref, rule_ref, gate_ref, head_gain_ref, qo_ref = refs[:9]
    outs = by_piece(at_ref, refs[9 : 9 + pieces])
    mix_ref, own_ref, mlpgain_ref, drule_ref, dgate_ref, dgain_ref, direct_ref, keep_ref = refs[-8:]
    full = rows_ref.shape[2]
    gain_sum = None
    for start in range(0, rows_ref.shape[1], ROWS):
        at = slice(start, start + ROWS)
        middle = rows_ref[0, at].astype(f32) + total_ref[0, at].astype(f32)
        two = two_ref[0, at].astype(f32)
        factor = norm_factor(middle)
        normal = middle * factor
        term = jnp.sum((two * normal).reshape(ROWS // 8, 8, full), 0)
        gain_sum = term if gain_sum is None else gain_sum + term
        scaled = two * gain_ref[...]
        mean = jnp.mean(scaled * normal, -1, keepdims=True)
        keep = cot_ref[0, at].astype(f32) + factor * (scaled - normal * mean)
        keep_ref[at] = keep
        mix_ref[0, at] = keep.astype(bf16)
    mlpgain_ref[0] = jnp.sum(gain_sum, 0, keepdims=True)
    width = own_ref.shape[2]
    own_ref[0] = keep_ref[:, pl.ds(pl.multiple_of(at_ref[1], 128), width)]
    grads = None
    for at, size, ref in out_columns(layout, outs):
        term = mm(mix_ref[0, :, at : at + size], ref[...], 1, 1)
        grads = term if grads is None else grads + term
    total = jnp.zeros((1, DK), f32)
    for h in range(direct_ref.shape[1]):
        grad = grads[:, head_slice(h)]
        out = rule_ref[0, :, head_slice(h)]
        gate = gate_ref[0, :, head_slice(h)]
        inv = norm_factor(out)
        n = out * inv
        sig = jax.nn.sigmoid(gate)
        silu = gate * sig
        gg = grad * head_gain_ref[...]
        dn = gg * silu
        drule = inv * (dn - n * jnp.mean(dn * n, -1, keepdims=True))
        drule_ref[0, :, head_slice(h)] = drule
        dgate = gg * n * sig * (1.0 + gate * (1.0 - sig))
        dgate_ref[0, :, head_slice(h)] = dgate.astype(bf16)
        total = total + jnp.sum(grad * n * silu, 0, keepdims=True)
        direct = mm(qo_ref[0, h, :, :DK], drule, 0, 0) * DK ** (-0.5)
        direct_ref[0, h] = direct.astype(bf16)
    dgain_ref[0] = total


def first_back_kernel(layout, pair_layout, count, place_ref, *refs):
    dproj_ref, dgate_ref, dlogit_ref, proj_ref, gate_ref, logit_ref, beta_ref, rows_ref, scale_ref = refs[:9]
    pieces = refs[9 : 9 + len(layout)]
    pairs = by_piece(place_ref, refs[9 + len(layout) : 9 + len(layout) + count])
    one_ref, rowsum_ref, gainsum_ref = refs[-3:]
    gates = {}
    for (k, start, size, block), ref in zip(pair_layout, pairs):
        gates[k] = ref
    for (k, start, size, block), piece in zip(layout, pieces):
        lanes = slice(k * block + start, k * block + start + size)
        grad = mm(dgate_ref[...], gate_part(gates[k])[start : start + size], 1, 1)
        for i in range(3):
            grad = grad + mm(dproj_ref[i], piece[i], 1, 1)
        for h in range(beta_ref.shape[0]):
            grad = grad + dlogit_ref[:, h : h + 1].astype(f32) * beta_ref[h : h + 1, lanes]
        at = pl.multiple_of((place_ref[0] ^ k) * block + start, 128)
        one_ref[:, pl.ds(at, size)] = grad.astype(bf16)
        gainsum_ref[:, lanes] = jnp.sum(
            grad * (rows_ref[:, lanes].astype(f32) * scale_ref[...]), 0, keepdims=True
        )
    total = dgate_ref[...].astype(f32) * gate_ref[...]
    for i in range(3):
        total = total + dproj_ref[i].astype(f32) * proj_ref[i].astype(f32)
    lane = lax.broadcasted_iota(jnp.int32, total.shape, 1) == 0
    logits = jnp.sum(dlogit_ref[...].astype(f32) * logit_ref[...], -1, keepdims=True)
    logits_sum = jnp.where(lane, logits, 0.0)
    total = total + logits_sum
    ones = jnp.ones((8, total.shape[1]), f32)
    rowsum_ref[...] = mm(ones, total, 1, 1)[:1]


def back_kernel(count, *refs):
    (
        proj_ref,
        before_ref,
        taps_ref,
        logit_ref,
        x_ref,
        wu_ref,
        state_ref,
        drule_ref,
    ) = refs[:8]
    dproj_ref, last_ref, first_ref, dtaps_ref, dlogit_ref = refs[-5:]
    others = refs[8 : 8 + 2 * count - 1]
    directs, nexts = others[:count], others[count:]
    heads = state_ref.shape[1]
    taps = taps_ref[...]
    length = proj_ref.shape[2]
    betas = jax.nn.sigmoid(logit_ref[0])
    r, c = places(length, length)
    strict = (r > c).astype(f32)
    full = (r >= c).astype(f32)
    zeros = jnp.zeros((PAD, DK), f32)
    for h in range(heads):
        parts, (qu, q_inv), (ku, k_inv), vu = rule_inputs(proj_ref, before_ref, taps, h)
        q, k, v = qu.astype(bf16), ku.astype(bf16), vu.astype(bf16)
        beta = betas[:, h : h + 1]
        leave = jnp.zeros((DK, DK), f32)
        for j in reversed(range(count)):
            here = directs[j][0, h].astype(f32)
            leave = here if j == count - 1 else mm(nexts[j][0, h], leave, 0, 0) + here
        state = state_ref[0, h]
        wu = wu_ref[0, h]
        u = wu[:, DK:] - mm(wu[:, :DK], state)
        resid = v.astype(f32) - mm(k, state)
        dout = drule_ref[0, :, head_slice(h)] * DK ** (-0.5)
        gram = mm(k, k, 1, 1)
        scores = mm(q, k, 1, 1) * full
        du = mm(scores, dout, 0, 0) + mm(k, leave)
        y = mm(x_ref[0, h], du, 0, 0)
        by = beta * y
        da = -(mm(y, u, 1, 1, 1) * strict)
        dbeta = jnp.sum(y * resid, -1, keepdims=True) + jnp.sum(da * gram, -1, keepdims=True)
        dgram = beta * da
        dscores = mm(dout, u, 1, 1, 1) * full
        dq = mm(dout, state, 1, 1, 1) + mm(dscores, k, 1, 0, 1)
        dk = (
            mm(dgram, k, 1, 0, 1)
            + mm(dgram, k, 0, 0, 1)
            + mm(dscores, q, 0, 0, 1)
            + mm(u, leave, 1, 1, 1)
            - mm(by, state, 1, 1, 1)
        )
        dlogit_ref[0, :, h : h + 1] = (dbeta * beta * (1.0 - beta)).astype(bf16)
        dq = (dq - qu * jnp.sum(qu * dq, -1, keepdims=True)) * q_inv
        dk = (dk - ku * jnp.sum(ku * dk, -1, keepdims=True)) * k_inv
        for i, dact in enumerate((dq, dk, by)):
            shifts, out, sig, _ = parts[i]
            dconv = dact * sig * (1.0 + out * (1.0 - sig))
            ext = jnp.concatenate([zeros, dconv, zeros], 0)
            total = None
            for j in range(KW):
                at = i * KW + j
                dtaps_ref[0, at : at + 1, head_slice(h)] = jnp.sum(
                    dconv * shifts[j], 0, keepdims=True
                )
                tap = taps[at : at + 1, head_slice(h)]
                term = tap * ext[KW - 1 - j : KW - 1 - j + PAD + length]
                total = term if total is None else total + term
            first_ref[i, 0, :, head_slice(h)] = total[:PAD]
            last_ref[i, 0, :, head_slice(h)] = total[length:]
            dproj_ref[i, 0, :, head_slice(h)] = total[PAD:].astype(bf16)


def call(kernel, ins, outs, steps, scalar=None, scratch=(), limit=VMEM, alias=None):
    def spec(shape, axis):
        if axis == "any":
            return pl.BlockSpec(memory_space=pl.ANY)
        block = tuple(1 if n == axis else size for n, size in enumerate(shape))
        where = lambda s, *_: tuple(s if n == axis else 0 for n in range(len(shape)))
        if axis is None:
            return pl.BlockSpec(block, where, pipeline_mode=pl.Buffered(1))
        return pl.BlockSpec(block, where)

    given = [] if scalar is None else [scalar]
    return pl.pallas_call(
        kernel,
        cost_estimate=FREE,
        grid_spec=pltpu.PrefetchScalarGridSpec(
            num_scalar_prefetch=len(given),
            grid=(steps,),
            in_specs=[spec(a.shape, axis) for a, axis in ins],
            out_specs=[spec(o.shape, axis) for o, axis in outs],
            scratch_shapes=scratch,
        ),
        out_shape=[o for o, _ in outs],
        input_output_aliases=alias or {},
        compiler_params=pltpu.CompilerParams(vmem_limit_bytes=limit),
    )(*given, *[a for a, _ in ins])


def shape_of(shape, dtype):
    return jax.ShapeDtypeStruct(shape, dtype)


def shifted(array, axis, by):
    devices = lax.axis_size(axis)
    pairs = [(i, i + by) for i in range(devices) if 0 <= i + by < devices]
    return lax.ppermute(array, axis, pairs)


def after(values, *others):
    flat, tree = jax.tree.flatten(values)
    others = jax.tree.leaves(others)
    here = pl.BlockSpec(memory_space=pl.ANY)
    out = pl.pallas_call(
        lambda *refs: None,
        cost_estimate=FREE,
        in_specs=[here] * (len(flat) + len(others)),
        out_specs=[here] * len(flat),
        out_shape=[shape_of(a.shape, a.dtype) for a in flat],
        input_output_aliases={n: n for n in range(len(flat))},
    )(*flat, *others)
    return jax.tree.unflatten(tree, out)


def copies(values):
    count = len(values)

    def kernel(*refs):
        for n in range(count):
            refs[n - count][...] = refs[n][...]

    outs = [(shape_of(a.shape, a.dtype), None) for a in values]
    return call(kernel, [(a, None) for a in values], outs, 1)


def swap(array, bits):
    return lax.ppermute(array, "dp", [(i, i ^ bits) for i in range(4)])


def first_hop(own):
    return swap(own, 1), swap(own, 2)


def halves_of(hop, axis):
    low, high = (jnp.split(part, 2, axis) for part in hop)
    return low[0], high[1]


def gathered_pieces(own, axis, hop=None, halves=None):
    hop = hop or first_hop(own)
    low, high = halves or halves_of(hop, axis)
    return [own, *hop, swap(low, 2), swap(high, 1)]


def far_hop(low, high):
    return swap(low, 1), swap(high, 2)


def near_sums(pieces, far_in, *others):
    own, one, two = pieces
    half = far_in[0].shape
    along = 1 if half[1] < one.shape[1] else 2

    def spec(place):
        where = tuple(place if n == along else 0 for n in range(3))
        return pl.BlockSpec(half, lambda s: where)

    first, second = spec(0), spec(1)
    here = pl.BlockSpec(memory_space=pl.ANY)
    one, two = pl.pallas_call(
        add_halves_kernel,
        cost_estimate=FREE,
        grid=(1,),
        in_specs=[second, first, first, first] + [here] * len(others),
        out_specs=[second, first],
        out_shape=[shape_of(a.shape, a.dtype) for a in (one, two)],
        input_output_aliases={0: 0, 1: 1},
        compiler_params=pltpu.CompilerParams(vmem_limit_bytes=VMEM),
    )(one, two, *far_in, *others)
    return own, one, two


def near_hop(pieces):
    own, one, two = pieces
    return own, swap(one, 1), swap(two, 2)


def add_pair_kernel(own_ref, one_ref, two_ref, *refs):
    gate_ref, out_ref = refs[-2:]
    inner = out_ref.shape[0]

    def added(i, rows):
        parts = (ref[i, rows].astype(f32) for ref in (own_ref, one_ref, two_ref))
        return sum(parts)

    gate_ref[...] = added(0, slice(None))
    for n in range(2):
        out_ref[:, n * inner : (n + 1) * inner] = added(1, slice(n * inner, (n + 1) * inner))


def sum_last(parts, *others):
    own = parts[0]
    ins = [(a, 0) for a in parts] + [(a, "any") for a in others]
    [total] = call(add_last_kernel, ins, [(shape_of(own.shape, f32), 0)], own.shape[0])
    return total


def pack(parts):
    return jnp.concatenate([p.reshape(-1) for p in parts])


def unpack(flat, shapes):
    out, at = [], 0
    for shape in shapes:
        size = 1
        for n in shape:
            size *= n
        out.append(flat[..., at : at + size].reshape(flat.shape[:-1] + tuple(shape)))
        at += size
    return out


def padded(flat, multiple=1024):
    return jnp.pad(flat, (0, -flat.shape[0] % multiple))


def body(
    tokens,
    out_grad,
    domain,
    group_weight,
    w_qkv,
    conv_weight,
    w_beta,
    w_outgate,
    head_gain,
    w_out,
    mixer_gain,
    mlp_gain,
    w_gateup,
    w_down,
):
    dp = lax.axis_size("dp")
    place = lax.axis_index("dp")
    seqs, block, local_width = tokens.shape
    count_rows = seqs * block
    heads = conv_weight.shape[2]
    inner = heads * DK
    column = lax.axis_index("mp") * local_width
    near_four = dp == 4

    def blocks_about(array, axis):
        if not near_four:
            return array
        size = array.shape[axis] // 4
        return jnp.concatenate(
            [lax.dynamic_slice_in_dim(array, (place ^ k) * size, size, axis) for k in range(4)],
            axis,
        )

    width = out_grad.shape[2]
    turn = place if near_four else jnp.int32(0)
    column_about = ((column // (width // 4)) ^ turn) * (width // 4) + column % (width // 4)

    def own(array):
        array = array.reshape(seqs, block, width)
        return lax.dynamic_slice_in_dim(array, column_about, local_width, 2)

    onehot = (domain[..., None] == jnp.arange(3, dtype=jnp.int32)).astype(f32)
    own_counts = jnp.sum(onehot, axis=(0, 1))
    high = jnp.floor(own_counts / 128.0)
    digits = jnp.concatenate([high, own_counts - 128.0 * high]).astype(bf16)
    small = [w_beta, conv_weight, head_gain, mixer_gain, mlp_gain, digits]
    packed = padded(pack(small))
    size = width // 4
    if near_four:
        qkv_hop = first_hop(w_qkv)
        qkv_halves = halves_of(qkv_hop, 1)
        qkv = gathered_pieces(w_qkv, 1, qkv_hop, qkv_halves)
        packed = after(packed, qkv_halves)
        gathered = jnp.stack([packed] + [swap(packed, bits) for bits in (1, 2, 3)])
        half = w_out.shape[1] // 2
        pair_own = jnp.stack(
            [w_outgate, jnp.concatenate([w_out[:, :half], w_out[:, half:]], 0)]
        )
        pair_layout = [(k, 0, size, size) for k in range(4)]
        layout = pair_layout[:3] + [(3, 0, size // 2, size), (3, size // 2, size // 2, size)]
    else:
        gathered = lax.all_gather(packed, "dp")
        qkv = [lax.all_gather(w_qkv, "dp", axis=1, tiled=True)]
        gate_pieces = [lax.all_gather(w_outgate, "dp", axis=0, tiled=True)]
        out_pieces = [lax.all_gather(w_out, "dp", axis=1, tiled=True)]
        layout = pair_layout = [(0, 0, width, width)]
    ranges = [(k * step + start, n) for k, start, n, step in layout]
    g_beta, g_conv, g_head, g_mix, g_mlp, g_digits = unpack(gathered, [a.shape for a in small])
    about_beta = g_beta.reshape(-1, heads)
    full_beta = blocks_about(about_beta, 0)
    full_conv = jnp.moveaxis(blocks_about(g_conv, 0), 0, 3).reshape(3 * KW, inner).astype(f32)
    gain_head = blocks_about(g_head, 0).reshape(1, DK).astype(f32)
    gain_one = blocks_about(g_mix.reshape(1, -1).astype(f32), 1)
    gain_two = g_mlp.reshape(1, -1).astype(f32)
    sums = jnp.sum(g_digits.astype(f32), 0)
    counts = 128.0 * sums[:3] + sums[3:]
    table = group_weight * (domain.shape[0] * domain.shape[1] * dp) / counts
    factor = jnp.sum(onehot * table, -1)[..., None]

    def flat(array):
        return array.reshape(array.shape[:-3] + (count_rows, array.shape[-1]))

    rows = lax.all_gather(tokens, "mp", axis=2, tiled=True)
    if near_four:
        gate_pieces = out_pieces = [lax.all_gather(after(pair_own, packed), "dp")]
    turn_one = turn.reshape(1)
    per_token = (seqs, block)
    square = (seqs, heads, DK, DK)
    hidden_one, proj, tail, logits, scale_one = call(
        partial(project_kernel, layout),
        [(rows, 0), (gain_one, None), (jnp.pad(full_beta, ((0, 0), (0, 128 - heads))), None)]
        + [(a, None) for a in qkv],
        [
            (shape_of(per_token + (width,), bf16), 0),
            (shape_of((3,) + per_token + (inner,), bf16), 1),
            (shape_of((3, seqs, HALO, inner), bf16), 1),
            (shape_of(per_token + (heads,), f32), 0),
            (shape_of(per_token + (1,), f32), 0),
        ],
        seqs,
        scalar=turn_one,
        scratch=[pltpu.VMEM((block, width), bf16)],
    )
    before = shifted(tail, "dp", 1)
    inverse, wu, qo, to = call(
        pre_kernel,
        [(proj, None), (before, None), (full_conv, None), (logits, None)],
        [
            (shape_of((seqs, heads, block, block), f32), None),
            (shape_of((seqs, heads, block, 2 * DK), f32), None),
            (shape_of((seqs, heads, block, 2 * DK), f32), None),
            (shape_of((seqs, heads, DK, 2 * DK), bf16), None),
        ],
        1,
    )
    near = [shifted(to, "dp", c) for c in range(1, dp)]
    rows_about, cotangent = call(
        partial(prepare_kernel, layout),
        [(rows, 0), (out_grad, 0), (factor, 0)],
        [(shape_of(per_token + (width,), bf16), 0)] * 2,
        seqs,
        scalar=turn_one,
    )
    turned = jnp.swapaxes(w_gateup, 1, 2)
    feed_own = [turned, w_down]
    mixer_part, normed, rule, state, gates = call(
        partial(mix_kernel, pair_layout, len(near), len(out_pieces)),
        [(a, 0) for a in near]
        + [(qo, 0), (hidden_one, 0), (gain_head, None)]
        + [(a, None) for a in gate_pieces + out_pieces]
        + [(cotangent, "any")],
        [
            (shape_of(per_token + (width,), bf16), 0),
            (shape_of(per_token + (inner,), bf16), 0),
            (shape_of(per_token + (inner,), f32), 0),
            (shape_of(square, f32), 0),
            (shape_of(per_token + (inner,), f32), 0),
        ],
        seqs,
        scalar=turn_one,
    )
    total = lax.psum(mixer_part, "mp")
    nexts = [shifted(to[..., :DK], "dp", -c) for c in range(1, dp - 1)]
    if near_four:
        gateup, down = (gathered_pieces(a, a.ndim - 1) for a in after(copies(feed_own), mixer_part, nexts))
    else:
        gateup, down = (
            [lax.all_gather(a, "dp", axis=a.ndim - 1, tiled=True)] for a in feed_own
        )
    units = w_down.shape[0]
    two_part, hidden_two, hidden_mlp, grad_pair = call(
        partial(feed_kernel, layout),
        [(rows_about, 0), (total, 0), (cotangent, 0), (gain_two, None)]
        + [(a, None) for a in gateup + down],
        [
            (shape_of(per_token + (width,), bf16), 0),
            (shape_of(per_token + (width,), bf16), 0),
            (shape_of(per_token + (units,), bf16), 0),
            (shape_of((2,) + per_token + (units,), bf16), 1),
        ],
        seqs,
    )
    grad_two = lax.psum(two_part, "mp")

    def feed_gradients(some, *others):
        outs = [(shape_of((m, units, n), bf16), None) for _, n in some for m in (2, 1)]
        base, span = some[0][0], sum(n for _, n in some)
        aligned = base % span == 0
        at = base // span if aligned else 0
        cols = pl.BlockSpec((count_rows, span if aligned else width), lambda s: (0, at))
        made = pl.pallas_call(
            partial(feed_gradient_kernel, base if aligned else 0, some),
            cost_estimate=FREE,
            grid=(1,),
            in_specs=[
                cols,
                cols,
                pl.BlockSpec((2, count_rows, units), lambda s: (0, 0, 0)),
                pl.BlockSpec((count_rows, units), lambda s: (0, 0)),
            ]
            + [pl.BlockSpec(memory_space=pl.ANY)] * len(others),
            out_specs=[pl.BlockSpec(o.shape, lambda s: (0, 0, 0)) for o, _ in outs],
            out_shape=[o for o, _ in outs],
            compiler_params=pltpu.CompilerParams(vmem_limit_bytes=VMEM),
        )(flat(hidden_two), flat(cotangent), flat(grad_pair), flat(hidden_mlp), *others)
        return made[::2], made[1::2]

    if near_four:
        feed_far = feed_gradients(ranges[3:])
        feed_in = [far_hop(*far) for far in feed_far]
        near_gateup, near_down = feed_gradients(ranges[:3], feed_far[0][0])
        first_made = [(near_gateup[0], "any")]
    else:
        [grad_gateup], [grad_down] = feed_gradients(ranges)
        held = first_made = []
    [down_part] = call(
        partial(down_kernel, layout),
        [(hidden_mlp, 0)] + [(a, None) for a in down] + first_made,
        [(shape_of(per_token + (width,), bf16), 0)],
        seqs,
        scalar=turn_one,
    )
    if near_four:
        gateup_added = near_sums(near_gateup, feed_in[0], *feed_in[1], down_part)
        down_added = near_sums(near_down, feed_in[1])
        gateup_sums, down_sums = near_hop(gateup_added), near_hop(down_added)
        down_part = after(down_part, gateup_added[1])
        held = [(a, "any") for a in gateup_sums[1:]]
    mlp_share = lax.psum_scatter(down_part, "mp", scatter_dimension=2, tiled=True)
    grad_mix, middle_own, mlpgain, drule, dgate, dgain, direct = call(
        partial(middle_back_kernel, pair_layout, len(out_pieces)),
        [
            (grad_two, 0),
            (cotangent, 0),
            (rows_about, 0),
            (total, 0),
            (gain_two, None),
            (rule, 0),
            (gates, 0),
            (gain_head, None),
            (qo, 0),
        ]
        + [(a, None) for a in out_pieces]
        + [(down_part, "any")]
        + held,
        [
            (shape_of(per_token + (width,), bf16), 0),
            (shape_of(per_token + (local_width,), f32), 0),
            (shape_of((seqs, 1, width), f32), 0),
            (shape_of(per_token + (inner,), f32), 0),
            (shape_of(per_token + (inner,), bf16), 0),
            (shape_of((seqs, 1, DK), f32), 0),
            (shape_of(square, bf16), 0),
        ],
        seqs,
        scalar=jnp.stack([turn, column_about]),
        scratch=[pltpu.VMEM((block, width), f32)],
    )
    directs = [shifted(direct, "dp", -c) for c in range(1, dp)]
    if near_four:
        pair_grads = call(
            partial(pair_gradient_kernel, [(k * size, size) for k in range(4)]),
            [(flat(a), None) for a in (hidden_one, dgate, normed, grad_mix)],
            [(shape_of((2, size, inner), bf16), None)] * 4,
            1,
        )
        held = [(a, "any") for a in (pair_grads[3], *down_sums[1:])]
    else:
        grad_outgate = jnp.einsum(
            "td,tc->dc", flat(hidden_one), flat(dgate), preferred_element_type=f32
        )
        grad_outproj = jnp.einsum(
            "tc,td->cd", flat(normed), flat(grad_mix), preferred_element_type=f32
        )
        held = []
    dproj, last, first, dtaps, dlogits = call(
        partial(back_kernel, len(directs)),
        [
            (proj, 1),
            (before, 1),
            (full_conv, None),
            (logits, 0),
            (inverse, 0),
            (wu, 0),
            (state, 0),
            (drule, 0),
        ]
        + [(a, 0) for a in directs + nexts]
        + held,
        [
            (shape_of((3,) + per_token + (inner,), bf16), 1),
            (shape_of((3, seqs, PAD, inner), f32), 1),
            (shape_of((3, seqs, PAD, inner), f32), 1),
            (shape_of((seqs, 3 * KW, inner), f32), 0),
            (shape_of(per_token + (heads,), bf16), 0),
        ],
        seqs,
    )
    later = shifted(first, "dp", -1)
    dproj = lax.dynamic_update_slice(dproj, (last + later).astype(bf16), (0, 0, block - PAD, 0))
    one_low, row_part, gain_part = call(
        partial(first_back_kernel, layout, pair_layout, len(gate_pieces)),
        [
            (flat(dproj), None),
            (flat(dgate), None),
            (flat(dlogits), None),
            (flat(proj), None),
            (flat(gates), None),
            (flat(logits), None),
            (about_beta.T.astype(f32), None),
            (flat(rows_about), None),
            (flat(scale_one), None),
        ]
        + [(a, None) for a in qkv + gate_pieces],
        [
            (shape_of((count_rows, width), bf16), None),
            (shape_of((1, count_rows), f32), None),
            (shape_of((1, width), f32), None),
        ],
        1,
        scalar=turn_one,
    )
    one_share = lax.psum_scatter(
        one_low.reshape(seqs, block, width), "mp", scatter_dimension=2, tiled=True
    ).astype(f32)
    made = call(
        partial(qkv_gradient_kernel, ranges),
        [(flat(hidden_one), None), (flat(dproj), None), (flat(dlogits), None), (row_part, "any")],
        [(shape_of((3, n, inner), bf16), None) for _, n in ranges]
        + [(shape_of((heads, width), f32), None)],
        1,
    )

    def pieces(array, axis, about):
        shape = array.shape
        cut = array.reshape(shape[:axis] + (dp, shape[axis] // dp) + shape[axis + 1 :])
        cut = jnp.moveaxis(cut, axis, 0).reshape(dp, -1)
        return blocks_about(cut, 0) if about else cut

    smalls = jnp.concatenate(
        [
            pieces(jnp.sum(dtaps, 0).reshape(3, KW, heads, DK), 3, True),
            pieces(made[-1].T, 0, False),
            pieces(gain_part[0], 0, False),
            pieces(jnp.sum(mlpgain, (0, 1)), 0, False),
            pieces(jnp.sum(dgain, (0, 1)), 0, True),
        ],
        1,
    )
    small_shapes = [a.shape for a in (conv_weight, w_beta, mixer_gain, mlp_gain, head_gain)]
    if near_four:
        own_qkv, *near_qkv = near_sums(made[:3], far_hop(made[3], made[4]))
        gateup_total = sum_last(gateup_sums, *near_qkv)
        down_total = sum_last(down_sums, *near_qkv)
        smalls = jnp.pad(smalls, ((0, 0), (0, -smalls.shape[1] % 1024))).reshape(dp, -1, 128)
        sent = smalls.astype(bf16)
        got = [swap(sent[bits], bits) for bits in (1, 2, 3)]
        first_mix = (conv_weight.size + w_beta.size) // 128
        last_mix = first_mix + mixer_gain.size // 128
        lines = count_rows // 128 + last_mix - first_mix
        mine, rest = call(
            partial(
                add_small_kernel,
                slice(first_mix, last_mix),
                last_mix + mlp_gain.size // 128,
            ),
            [(a, None) for a in [smalls[0]] + got + [row_part]],
            [
                (shape_of(smalls.shape[1:], f32), None),
                (shape_of((lines + 8 - lines % 8, 128), f32), None),
            ],
            1,
        )
        pair_far = after(jnp.split(pair_grads[3], 2, 1), made[0])
        pair_near = near_sums(pair_grads[:3], far_hop(*pair_far))[1:]
        mine = mine.reshape(-1)
        sum_qkv = sum_last(near_hop((own_qkv, *near_qkv)))
        sum_gateup = jnp.swapaxes(gateup_total, 1, 2)
        sum_down = down_total[0]
        pair_sums = near_hop((pair_grads[0], *pair_near))
    else:
        gathered = lax.all_gather(smalls.astype(bf16), "dp")
        mine = jnp.sum(
            lax.dynamic_index_in_dim(gathered, place, 1, keepdims=False).astype(f32), 0
        )

        def scattered(array, axis):
            return lax.psum_scatter(array, "dp", scatter_dimension=axis, tiled=True).astype(f32)

        sum_qkv = scattered(made[0], 1)
        sum_outgate = scattered(grad_outgate.astype(bf16), 0)
        sum_out = scattered(grad_outproj.astype(bf16), 1)
        sum_gateup = jnp.swapaxes(scattered(grad_gateup, 2), 1, 2)
        sum_down = scattered(grad_down[0], 1)
    sum_conv, sum_beta, sum_mix, sum_mlp, sum_head = unpack(mine, small_shapes)
    if near_four:
        bit = 1
        while bit < lax.axis_size("mp"):
            devices = lax.axis_size("mp")
            rest = rest + lax.ppermute(rest, "mp", [(i, i ^ bit) for i in range(devices)])
            bit *= 2
        rest_sum = rest.reshape(-1)
    else:
        rest_sum = lax.psum(pack([row_part, sum_mix, sum_head]), "mp")
    row_sum, sum_mix, sum_head = unpack(rest_sum, [(count_rows,), sum_mix.shape, sum_head.shape])

    own_tokens = tokens.astype(f32)
    mixed_out = (own_tokens + own(total).astype(f32) + mlp_share.astype(f32)).astype(bf16)
    row_mean = (row_sum / width).reshape(seqs, block, 1)
    gain_own = lax.dynamic_slice_in_dim(gain_one, column, local_width, 1)
    tokens_grad = middle_own + scale_one * (
        one_share * gain_own - own_tokens * scale_one * row_mean
    )
    tokens_grad = tokens_grad.astype(bf16)
    if near_four:
        done = [(a, "any") for a in (sum_qkv, tokens_grad, mixed_out, gateup_total, down_total)]
        sum_outgate, sum_out = call(
            add_pair_kernel,
            [(a, None) for a in pair_sums] + done,
            [(shape_of(w_outgate.shape, f32), None), (shape_of(w_out.shape, f32), None)],
            1,
        )
    return (
        mixed_out,
        tokens_grad,
        sum_qkv,
        sum_conv,
        sum_beta,
        sum_outgate,
        sum_head,
        sum_out,
        sum_mix,
        sum_mlp,
        sum_gateup,
        sum_down,
    )


def solution(mesh):
    return jax.shard_map(
        body,
        mesh=mesh,
        in_specs=(
            P(None, "dp", "mp"),
            P(None, "dp", None),
            P(None, "dp"),
            P(),
            P(None, "dp", "mp"),
            P(None, None, "mp", "dp"),
            P("dp", "mp"),
            P("dp", "mp"),
            P("dp"),
            P("mp", "dp"),
            P("dp"),
            P("dp"),
            P(None, "dp", "mp"),
            P("mp", "dp"),
        ),
        out_specs=(
            P(None, "dp", "mp"),
            P(None, "dp", "mp"),
            P(None, "dp", "mp"),
            P(None, None, "mp", "dp"),
            P("dp", "mp"),
            P("dp", "mp"),
            P("dp"),
            P("mp", "dp"),
            P("dp"),
            P("dp"),
            P(None, "dp", "mp"),
            P("mp", "dp"),
        ),
        check_vma=False,
    )
```

```python
from functools import partial

import jax
import jax.numpy as jnp
from jax import lax
from jax.experimental import pallas as pl
from jax.experimental.pallas import tpu as pltpu
from jax.sharding import PartitionSpec as P

DK = 128
KW = 4
PAD = 8
HALO = 16
ROWS = 16
VMEM = 58 * 2**20
FREE = pl.CostEstimate(flops=0, transcendentals=0, bytes_accessed=0)

eps_norm = 1e-06
eps_unit = 1e-06

f32 = jnp.float32
bf16 = jnp.bfloat16


def split(v):
    if v.dtype == bf16:
        return v, None
    high = v.astype(bf16)
    return high, (v - high.astype(f32)).astype(bf16)


def mm(a, b, ca=1, cb=0, passes=3):
    def one(x, y):
        return lax.dot_general(x, y, (((ca,), (cb,)), ((), ())), preferred_element_type=f32)

    if passes == 1:
        return one(a.astype(bf16), b.astype(bf16))
    (ah, al), (bh, bl) = split(a), split(b)
    out = one(ah, bh)
    if bl is not None:
        out = out + one(ah, bl)
    if al is not None:
        out = out + one(al, bh)
    return out


def places(rows, cols):
    return (
        lax.broadcasted_iota(jnp.int32, (rows, cols), 0),
        lax.broadcasted_iota(jnp.int32, (rows, cols), 1),
    )


def unit_lower_inverses(blocks):
    size = blocks[0].shape[0]
    if size > 128:
        half = size // 2
        parts = unit_lower_inverses(
            [a[:half, :half] for a in blocks] + [a[half:, half:] for a in blocks]
        )
        firsts, seconds = parts[: len(blocks)], parts[len(blocks) :]
        inner = [mm(a[half:, :half], x) for a, x in zip(blocks, firsts)]
        lower = [-mm(x, y) for x, y in zip(seconds, inner)]
        zero = jnp.zeros((half, half), f32)
        return [
            jnp.concatenate(
                [jnp.concatenate([x, zero], 1), jnp.concatenate([y, z], 1)], 0
            )
            for x, y, z in zip(firsts, lower, seconds)
        ]
    rows, cols = places(size, size)
    eye = (rows == cols).astype(f32)
    level = 0
    inverses = None
    while (1 << level) < size:
        mask = (
            ((rows >> (level + 1)) == (cols >> (level + 1)))
            & (((rows >> level) & 1) == 1)
            & (((cols >> level) & 1) == 0)
        ).astype(f32)
        lows = [a * mask for a in blocks]
        if level == 0:
            inverses = [eye - low for low in lows]
        else:
            inner = [mm(low, x) for low, x in zip(lows, inverses)]
            inverses = [x - mm(x, y) for x, y in zip(inverses, inner)]
        level += 1
    return inverses


def head_slice(h):
    return slice(h * DK, (h + 1) * DK)


def convolve(proj_ref, before_ref, taps, i, h):
    own = proj_ref[i, 0, :, head_slice(h)].astype(f32)
    length = own.shape[0]
    ext = jnp.concatenate([before_ref[i, 0, :, head_slice(h)].astype(f32), own], 0)
    shifts = [ext[HALO - KW + 1 + j : HALO - KW + 1 + j + length] for j in range(KW)]
    out = None
    for j in range(KW):
        tap = taps[i * KW + j : i * KW + j + 1, head_slice(h)]
        out = tap * shifts[j] if out is None else out + tap * shifts[j]
    sig = jax.nn.sigmoid(out)
    return shifts, out, sig, out * sig


def unit(acts):
    inv = lax.rsqrt(jnp.sum(acts * acts, -1, keepdims=True) + eps_unit)
    return acts * inv, inv


def rule_inputs(proj_ref, before_ref, taps, h):
    parts = [convolve(proj_ref, before_ref, taps, i, h) for i in range(3)]
    q, q_inv = unit(parts[0][3])
    k, k_inv = unit(parts[1][3])
    return parts, (q, q_inv), (k, k_inv), parts[2][3]


def norm_factor(values):
    return lax.rsqrt(jnp.mean(values * values, -1, keepdims=True) + eps_norm)


def project_kernel(layout, *refs):
    place_ref, rows_ref, gain_ref, beta_ref = refs[:4]
    pieces = refs[4 : 4 + len(layout)]
    hidden_ref, proj_ref, tail_ref, logit_ref, scale_ref, keep_ref = refs[4 + len(layout) :]
    rows = rows_ref[0].astype(f32)
    scale = norm_factor(rows)
    scale_ref[0] = scale
    keep_ref[...] = (rows * scale * gain_ref[...]).astype(bf16)
    logits = mm(keep_ref[...], beta_ref[...])
    logit_ref[0] = logits[:, : logit_ref.shape[2]]
    sums = [None] * 3
    for (k, start, size, block), piece in zip(layout, pieces):
        at = pl.multiple_of((place_ref[0] ^ k) * block + start, 128)
        part = keep_ref[:, pl.ds(at, size)]
        hidden_ref[0, :, k * block + start : k * block + start + size] = part
        for i in range(3):
            term = mm(part, piece[i])
            sums[i] = term if sums[i] is None else sums[i] + term
    for i in range(3):
        low = sums[i].astype(bf16)
        proj_ref[i, 0] = low
        tail_ref[i, 0] = low[low.shape[0] - HALO :]


def pre_kernel(proj_ref, before_ref, taps_ref, logit_ref, x_ref, wu_ref, qo_ref, to_ref):
    seqs, heads = to_ref.shape[:2]
    taps = taps_ref[...]
    length = proj_ref.shape[2]
    r, c = places(length, length)
    strict = (r > c).astype(f32)
    full = (r >= c).astype(f32)
    saved, blocks = [], []
    for s in range(seqs):
        betas = jax.nn.sigmoid(logit_ref[s])
        rows, before = proj_ref.at[:, s : s + 1], before_ref.at[:, s : s + 1]
        for h in range(heads):
            _, (q, _), (k, _), v = rule_inputs(rows, before, taps, h)
            q, k, v = q.astype(bf16), k.astype(bf16), v.astype(bf16)
            beta = betas[:, h : h + 1]
            blocks.append(beta * mm(k, k, 1, 1) * strict)
            saved.append((s, h, q, k, v, beta))
    inverses = unit_lower_inverses(blocks)
    r, c = places(DK, DK)
    eye = (r == c).astype(f32)
    for (s, h, q, k, v, beta), x in zip(saved, inverses):
        x_ref[s, h] = x
        kv = jnp.concatenate([k.astype(f32), v.astype(f32)], 1) * beta
        wu = mm(x, kv)
        wu_ref[s, h] = wu
        scores = mm(q, k, 1, 1) * full
        pwu = mm(scores, wu)
        qo_ref[s, h, :, :DK] = q.astype(f32) - pwu[:, :DK]
        qo_ref[s, h, :, DK:] = pwu[:, DK:]
        kwu = mm(k, wu, 0, 0)
        to_ref[s, h, :, :DK] = (eye - kwu[:, :DK]).astype(bf16)
        to_ref[s, h, :, DK:] = kwu[:, DK:].astype(bf16)


def by_piece(place_ref, refs):
    if len(refs) > 1 or len(refs[0].shape) < 4:
        return refs
    return [refs[0].at[place_ref[0] ^ k] for k in range(4)]


def gate_part(ref):
    return ref.at[0] if len(ref.shape) == 3 else ref


def out_columns(layout, refs):
    for (k, start, size, block), ref in zip(layout, refs):
        at, half = k * block + start, size // 2
        if len(ref.shape) == 2:
            yield at, size, ref
            continue
        inner = ref.shape[1] // 2
        yield at, half, ref.at[1, :inner]
        yield at + half, half, ref.at[1, inner:]


def mix_kernel(layout, count, pieces, place_ref, *refs):
    near, rest = refs[:count], refs[count:]
    qo_ref, hidden_ref, gain_ref = rest[:3]
    gate_pieces = by_piece(place_ref, rest[3 : 3 + pieces])
    outs = by_piece(place_ref, rest[3 + pieces : 3 + 2 * pieces])
    part_ref, normed_ref, rule_ref, state_ref, gate_ref = rest[-5:]
    gates = None
    for (k, start, size, block), ref in zip(layout, gate_pieces):
        at = k * block + start
        term = mm(hidden_ref[0, :, at : at + size], gate_part(ref)[...])
        gates = term if gates is None else gates + term
    gate_ref[0] = gates
    heads = state_ref.shape[1]
    for h in range(heads):
        state = near[-1][0, h, :, DK:].astype(f32)
        for ref in reversed(near[:-1]):
            state = mm(ref[0, h, :, :DK], state) + ref[0, h, :, DK:].astype(f32)
        state_ref[0, h] = state
        qo = qo_ref[0, h]
        out = (mm(qo[:, :DK], state) + qo[:, DK:]) * DK ** (-0.5)
        rule_ref[0, :, head_slice(h)] = out
        gate = gate_ref[0, :, head_slice(h)]
        normed = out * norm_factor(out) * gain_ref[...] * (gate * jax.nn.sigmoid(gate))
        normed_ref[0, :, head_slice(h)] = normed.astype(bf16)
    for at, size, ref in out_columns(layout, outs):
        part_ref[0, :, at : at + size] = mm(normed_ref[0], ref[...]).astype(bf16)


def prepare_kernel(layout, place_ref, rows_ref, grad_ref, factor_ref, about_ref, cot_ref):
    for k, start, size, block in layout:
        at = pl.multiple_of((place_ref[0] ^ k) * block + start, 128)
        to = slice(k * block + start, k * block + start + size)
        about_ref[0, :, to] = rows_ref[0, :, pl.ds(at, size)]
        grad = grad_ref[0, :, pl.ds(at, size)].astype(f32) * factor_ref[0]
        cot_ref[0, :, to] = grad.astype(bf16)


def down_kernel(layout, place_ref, mlp_ref, *refs):
    part_ref = refs[-1]
    for (k, start, size, block), ref in zip(layout, refs):
        at = pl.multiple_of((place_ref[0] ^ k) * block + start, 128)
        part_ref[0, :, pl.ds(at, size)] = mm(mlp_ref[0], ref[...]).astype(bf16)


def feed_gradient_kernel(base, ranges, hidden_ref, cot_ref, pair_ref, mlp_ref, *outs):
    outs = outs[-2 * len(ranges) :]
    for n, (start, size) in enumerate(ranges):
        start = start - base
        hidden = hidden_ref[:, start : start + size]
        outs[2 * n][0] = mm(pair_ref[0], hidden, 0, 0).astype(bf16)
        outs[2 * n][1] = mm(pair_ref[1], hidden, 0, 0).astype(bf16)
        outs[2 * n + 1][0] = mm(mlp_ref[...], cot_ref[:, start : start + size], 0, 0).astype(bf16)


def qkv_gradient_kernel(ranges, hidden_ref, dproj_ref, dlogit_ref, *outs):
    outs = outs[-len(ranges) - 1 :]
    for (start, size), out in zip(ranges, outs[:-1]):
        hidden = hidden_ref[:, start : start + size]
        for i in range(3):
            out[i] = mm(hidden, dproj_ref[i], 0, 0).astype(bf16)
    outs[-1][...] = mm(dlogit_ref[...], hidden_ref[...], 0, 0)


def pair_gradient_kernel(ranges, hidden_ref, dgate_ref, normed_ref, mix_ref, *outs):
    inner = normed_ref.shape[1]
    for (start, size), out in zip(ranges, outs):
        out[0] = mm(hidden_ref[:, start : start + size], dgate_ref[...], 0, 0).astype(bf16)
        for n in range(2):
            at = start + n * size // 2
            mix = mix_ref[:, at : at + size // 2]
            out[1, n * inner : (n + 1) * inner] = mm(normed_ref[...], mix, 0, 0).astype(bf16)


def add_halves_kernel(*refs):
    one_ref, two_ref, low_ref, high_ref, one_out, two_out = refs[:4] + refs[-2:]
    one_out[...] = (one_ref[...].astype(f32) + high_ref[...].astype(f32)).astype(bf16)
    two_out[...] = (two_ref[...].astype(f32) + low_ref[...].astype(f32)).astype(bf16)


def add_small_kernel(mix_rows, head_row, *refs):
    *parts, row_ref, out_ref, rest_ref = refs
    total = sum(ref[...].astype(f32) for ref in parts)
    out_ref[...] = total
    lines = [row_ref[:, n * 128 : (n + 1) * 128] for n in range(row_ref.shape[1] // 128)]
    lines += [total[mix_rows], total[head_row : head_row + 1]]
    used = len(lines) - 2 + mix_rows.stop - mix_rows.start + 1
    lines.append(jnp.zeros((rest_ref.shape[0] - used, 128), f32))
    rest_ref[...] = jnp.concatenate(lines, 0)


def add_last_kernel(*refs):
    own_ref, one_ref, two_ref, out_ref = refs[:3] + refs[-1:]
    out_ref[...] = own_ref[...].astype(f32) + one_ref[...].astype(f32) + two_ref[...].astype(f32)


def feed_kernel(layout, *refs):
    rows_ref, total_ref, cot_ref, gain_ref = refs[:4]
    count = len(layout)
    gateups, downs = (refs[4 + n * count : 4 + (n + 1) * count] for n in range(2))
    two_ref, hidden_ref, mlp_ref, pair_ref = refs[-4:]
    middle = rows_ref[0].astype(f32) + total_ref[0].astype(f32)
    hidden_ref[0] = (middle * norm_factor(middle) * gain_ref[...]).astype(bf16)
    gate, up, grad = None, None, None
    for (k, start, size, block), w_gateup, w_down in zip(layout, gateups, downs):
        lanes = slice(k * block + start, k * block + start + size)
        hidden = hidden_ref[0, :, lanes]
        terms = (
            mm(hidden, w_gateup[0], 1, 1),
            mm(hidden, w_gateup[1], 1, 1),
            mm(cot_ref[0, :, lanes], w_down[...], 1, 1),
        )
        if gate is None:
            gate, up, grad = terms
        else:
            gate, up, grad = gate + terms[0], up + terms[1], grad + terms[2]
    sig = jax.nn.sigmoid(gate)
    silu = gate * sig
    mlp_ref[0] = (silu * up).astype(bf16)
    first = (grad * up * (sig + silu * (1.0 - sig))).astype(bf16)
    second = (grad * silu).astype(bf16)
    pair_ref[0, 0] = first
    pair_ref[1, 0] = second
    for (k, start, size, block), w_gateup in zip(layout, gateups):
        lanes = slice(k * block + start, k * block + start + size)
        two = mm(first, w_gateup[0]) + mm(second, w_gateup[1])
        two_ref[0, :, lanes] = two.astype(bf16)


def middle_back_kernel(layout, pieces, at_ref, *refs):
    two_ref, cot_ref, rows_ref, total_ref, gain_ref, rule_ref, gate_ref, head_gain_ref, qo_ref = refs[:9]
    outs = by_piece(at_ref, refs[9 : 9 + pieces])
    mix_ref, own_ref, mlpgain_ref, drule_ref, dgate_ref, dgain_ref, direct_ref, keep_ref = refs[-8:]
    full = rows_ref.shape[2]
    gain_sum = None
    for start in range(0, rows_ref.shape[1], ROWS):
        at = slice(start, start + ROWS)
        middle = rows_ref[0, at].astype(f32) + total_ref[0, at].astype(f32)
        two = two_ref[0, at].astype(f32)
        factor = norm_factor(middle)
        normal = middle * factor
        term = jnp.sum((two * normal).reshape(ROWS // 8, 8, full), 0)
        gain_sum = term if gain_sum is None else gain_sum + term
        scaled = two * gain_ref[...]
        mean = jnp.mean(scaled * normal, -1, keepdims=True)
        keep = cot_ref[0, at].astype(f32) + factor * (scaled - normal * mean)
        keep_ref[at] = keep
        mix_ref[0, at] = keep.astype(bf16)
    mlpgain_ref[0] = jnp.sum(gain_sum, 0, keepdims=True)
    width = own_ref.shape[2]
    own_ref[0] = keep_ref[:, pl.ds(pl.multiple_of(at_ref[1], 128), width)]
    grads = None
    for at, size, ref in out_columns(layout, outs):
        term = mm(mix_ref[0, :, at : at + size], ref[...], 1, 1)
        grads = term if grads is None else grads + term
    total = jnp.zeros((1, DK), f32)
    for h in range(direct_ref.shape[1]):
        grad = grads[:, head_slice(h)]
        out = rule_ref[0, :, head_slice(h)]
        gate = gate_ref[0, :, head_slice(h)]
        inv = norm_factor(out)
        n = out * inv
        sig = jax.nn.sigmoid(gate)
        silu = gate * sig
        gg = grad * head_gain_ref[...]
        dn = gg * silu
        drule = inv * (dn - n * jnp.mean(dn * n, -1, keepdims=True))
        drule_ref[0, :, head_slice(h)] = drule
        dgate = gg * n * sig * (1.0 + gate * (1.0 - sig))
        dgate_ref[0, :, head_slice(h)] = dgate.astype(bf16)
        total = total + jnp.sum(grad * n * silu, 0, keepdims=True)
        direct = mm(qo_ref[0, h, :, :DK], drule, 0, 0) * DK ** (-0.5)
        direct_ref[0, h] = direct.astype(bf16)
    dgain_ref[0] = total


def first_back_kernel(layout, pair_layout, count, place_ref, *refs):
    dproj_ref, dgate_ref, dlogit_ref, proj_ref, gate_ref, logit_ref, beta_ref, rows_ref, scale_ref = refs[:9]
    pieces = refs[9 : 9 + len(layout)]
    pairs = by_piece(place_ref, refs[9 + len(layout) : 9 + len(layout) + count])
    one_ref, rowsum_ref, gainsum_ref = refs[-3:]
    gates = {}
    for (k, start, size, block), ref in zip(pair_layout, pairs):
        gates[k] = ref
    for (k, start, size, block), piece in zip(layout, pieces):
        lanes = slice(k * block + start, k * block + start + size)
        grad = mm(dgate_ref[...], gate_part(gates[k])[start : start + size], 1, 1)
        for i in range(3):
            grad = grad + mm(dproj_ref[i], piece[i], 1, 1)
        for h in range(beta_ref.shape[0]):
            grad = grad + dlogit_ref[:, h : h + 1].astype(f32) * beta_ref[h : h + 1, lanes]
        at = pl.multiple_of((place_ref[0] ^ k) * block + start, 128)
        one_ref[:, pl.ds(at, size)] = grad.astype(bf16)
        gainsum_ref[:, lanes] = jnp.sum(
            grad * (rows_ref[:, lanes].astype(f32) * scale_ref[...]), 0, keepdims=True
        )
    total = dgate_ref[...].astype(f32) * gate_ref[...]
    for i in range(3):
        total = total + dproj_ref[i].astype(f32) * proj_ref[i].astype(f32)
    lane = lax.broadcasted_iota(jnp.int32, total.shape, 1) == 0
    logits = jnp.sum(dlogit_ref[...].astype(f32) * logit_ref[...], -1, keepdims=True)
    logits_sum = jnp.where(lane, logits, 0.0)
    total = total + logits_sum
    ones = jnp.ones((8, total.shape[1]), f32)
    rowsum_ref[...] = mm(ones, total, 1, 1)[:1]


def back_kernel(count, *refs):
    (
        proj_ref,
        before_ref,
        taps_ref,
        logit_ref,
        x_ref,
        wu_ref,
        state_ref,
        drule_ref,
    ) = refs[:8]
    dproj_ref, last_ref, first_ref, dtaps_ref, dlogit_ref = refs[-5:]
    others = refs[8 : 8 + 2 * count - 1]
    directs, nexts = others[:count], others[count:]
    heads = state_ref.shape[1]
    taps = taps_ref[...]
    length = proj_ref.shape[2]
    betas = jax.nn.sigmoid(logit_ref[0])
    r, c = places(length, length)
    strict = (r > c).astype(f32)
    full = (r >= c).astype(f32)
    zeros = jnp.zeros((PAD, DK), f32)
    for h in range(heads):
        parts, (qu, q_inv), (ku, k_inv), vu = rule_inputs(proj_ref, before_ref, taps, h)
        q, k, v = qu.astype(bf16), ku.astype(bf16), vu.astype(bf16)
        beta = betas[:, h : h + 1]
        leave = jnp.zeros((DK, DK), f32)
        for j in reversed(range(count)):
            here = directs[j][0, h].astype(f32)
            leave = here if j == count - 1 else mm(nexts[j][0, h], leave, 0, 0) + here
        state = state_ref[0, h]
        wu = wu_ref[0, h]
        u = wu[:, DK:] - mm(wu[:, :DK], state)
        resid = v.astype(f32) - mm(k, state)
        dout = drule_ref[0, :, head_slice(h)] * DK ** (-0.5)
        gram = mm(k, k, 1, 1)
        scores = mm(q, k, 1, 1) * full
        du = mm(scores, dout, 0, 0) + mm(k, leave)
        y = mm(x_ref[0, h], du, 0, 0)
        by = beta * y
        da = -(mm(y, u, 1, 1, 1) * strict)
        dbeta = jnp.sum(y * resid, -1, keepdims=True) + jnp.sum(da * gram, -1, keepdims=True)
        dgram = beta * da
        dscores = mm(dout, u, 1, 1, 1) * full
        dq = mm(dout, state, 1, 1, 1) + mm(dscores, k, 1, 0, 1)
        dk = (
            mm(dgram, k, 1, 0, 1)
            + mm(dgram, k, 0, 0, 1)
            + mm(dscores, q, 0, 0, 1)
            + mm(u, leave, 1, 1, 1)
            - mm(by, state, 1, 1, 1)
        )
        dlogit_ref[0, :, h : h + 1] = (dbeta * beta * (1.0 - beta)).astype(bf16)
        dq = (dq - qu * jnp.sum(qu * dq, -1, keepdims=True)) * q_inv
        dk = (dk - ku * jnp.sum(ku * dk, -1, keepdims=True)) * k_inv
        for i, dact in enumerate((dq, dk, by)):
            shifts, out, sig, _ = parts[i]
            dconv = dact * sig * (1.0 + out * (1.0 - sig))
            ext = jnp.concatenate([zeros, dconv, zeros], 0)
            total = None
            for j in range(KW):
                at = i * KW + j
                dtaps_ref[0, at : at + 1, head_slice(h)] = jnp.sum(
                    dconv * shifts[j], 0, keepdims=True
                )
                tap = taps[at : at + 1, head_slice(h)]
                term = tap * ext[KW - 1 - j : KW - 1 - j + PAD + length]
                total = term if total is None else total + term
            first_ref[i, 0, :, head_slice(h)] = total[:PAD]
            last_ref[i, 0, :, head_slice(h)] = total[length:]
            dproj_ref[i, 0, :, head_slice(h)] = total[PAD:].astype(bf16)


def call(kernel, ins, outs, steps, scalar=None, scratch=(), limit=VMEM, alias=None):
    def spec(shape, axis):
        if axis == "any":
            return pl.BlockSpec(memory_space=pl.ANY)
        block = tuple(1 if n == axis else size for n, size in enumerate(shape))
        where = lambda s, *_: tuple(s if n == axis else 0 for n in range(len(shape)))
        if axis is None:
            return pl.BlockSpec(block, where, pipeline_mode=pl.Buffered(1))
        return pl.BlockSpec(block, where)

    given = [] if scalar is None else [scalar]
    return pl.pallas_call(
        kernel,
        cost_estimate=FREE,
        grid_spec=pltpu.PrefetchScalarGridSpec(
            num_scalar_prefetch=len(given),
            grid=(steps,),
            in_specs=[spec(a.shape, axis) for a, axis in ins],
            out_specs=[spec(o.shape, axis) for o, axis in outs],
            scratch_shapes=scratch,
        ),
        out_shape=[o for o, _ in outs],
        input_output_aliases=alias or {},
        compiler_params=pltpu.CompilerParams(vmem_limit_bytes=limit),
    )(*given, *[a for a, _ in ins])


def shape_of(shape, dtype):
    return jax.ShapeDtypeStruct(shape, dtype)


def shifted(array, axis, by):
    devices = lax.axis_size(axis)
    pairs = [(i, i + by) for i in range(devices) if 0 <= i + by < devices]
    return lax.ppermute(array, axis, pairs)


def after(values, *others):
    flat, tree = jax.tree.flatten(values)
    others = jax.tree.leaves(others)
    here = pl.BlockSpec(memory_space=pl.ANY)
    out = pl.pallas_call(
        lambda *refs: None,
        cost_estimate=FREE,
        in_specs=[here] * (len(flat) + len(others)),
        out_specs=[here] * len(flat),
        out_shape=[shape_of(a.shape, a.dtype) for a in flat],
        input_output_aliases={n: n for n in range(len(flat))},
    )(*flat, *others)
    return jax.tree.unflatten(tree, out)


def copies(values):
    count = len(values)

    def kernel(*refs):
        for n in range(count):
            refs[n - count][...] = refs[n][...]

    outs = [(shape_of(a.shape, a.dtype), None) for a in values]
    return call(kernel, [(a, None) for a in values], outs, 1)


def swap(array, bits):
    return lax.ppermute(array, "dp", [(i, i ^ bits) for i in range(4)])


def first_hop(own):
    return swap(own, 1), swap(own, 2)


def halves_of(hop, axis):
    low, high = (jnp.split(part, 2, axis) for part in hop)
    return low[0], high[1]


def gathered_pieces(own, axis, hop=None, halves=None):
    hop = hop or first_hop(own)
    low, high = halves or halves_of(hop, axis)
    return [own, *hop, swap(low, 2), swap(high, 1)]


def far_hop(low, high):
    return swap(low, 1), swap(high, 2)


def near_sums(pieces, far_in, *others):
    own, one, two = pieces
    half = far_in[0].shape
    along = 1 if half[1] < one.shape[1] else 2

    def spec(place):
        where = tuple(place if n == along else 0 for n in range(3))
        return pl.BlockSpec(half, lambda s: where)

    first, second = spec(0), spec(1)
    here = pl.BlockSpec(memory_space=pl.ANY)
    one, two = pl.pallas_call(
        add_halves_kernel,
        cost_estimate=FREE,
        grid=(1,),
        in_specs=[second, first, first, first] + [here] * len(others),
        out_specs=[second, first],
        out_shape=[shape_of(a.shape, a.dtype) for a in (one, two)],
        input_output_aliases={0: 0, 1: 1},
        compiler_params=pltpu.CompilerParams(vmem_limit_bytes=VMEM),
    )(one, two, *far_in, *others)
    return own, one, two


def near_hop(pieces):
    own, one, two = pieces
    return own, swap(one, 1), swap(two, 2)


def add_pair_kernel(own_ref, one_ref, two_ref, *refs):
    gate_ref, out_ref = refs[-2:]
    inner = out_ref.shape[0]

    def added(i, rows):
        parts = (ref[i, rows].astype(f32) for ref in (own_ref, one_ref, two_ref))
        return sum(parts)

    gate_ref[...] = added(0, slice(None))
    for n in range(2):
        out_ref[:, n * inner : (n + 1) * inner] = added(1, slice(n * inner, (n + 1) * inner))


def sum_last(parts, *others):
    own = parts[0]
    ins = [(a, 0) for a in parts] + [(a, "any") for a in others]
    [total] = call(add_last_kernel, ins, [(shape_of(own.shape, f32), 0)], own.shape[0])
    return total


def pack(parts):
    return jnp.concatenate([p.reshape(-1) for p in parts])


def unpack(flat, shapes):
    out, at = [], 0
    for shape in shapes:
        size = 1
        for n in shape:
            size *= n
        out.append(flat[..., at : at + size].reshape(flat.shape[:-1] + tuple(shape)))
        at += size
    return out


def padded(flat, multiple=1024):
    return jnp.pad(flat, (0, -flat.shape[0] % multiple))


def body(
    tokens,
    out_grad,
    domain,
    group_weight,
    w_qkv,
    conv_weight,
    w_beta,
    w_outgate,
    head_gain,
    w_out,
    mixer_gain,
    mlp_gain,
    w_gateup,
    w_down,
):
    dp = lax.axis_size("dp")
    place = lax.axis_index("dp")
    seqs, block, local_width = tokens.shape
    count_rows = seqs * block
    heads = conv_weight.shape[2]
    inner = heads * DK
    column = lax.axis_index("mp") * local_width
    near_four = dp == 4

    def blocks_about(array, axis):
        if not near_four:
            return array
        size = array.shape[axis] // 4
        return jnp.concatenate(
            [lax.dynamic_slice_in_dim(array, (place ^ k) * size, size, axis) for k in range(4)],
            axis,
        )

    width = out_grad.shape[2]
    turn = place if near_four else jnp.int32(0)
    column_about = ((column // (width // 4)) ^ turn) * (width // 4) + column % (width // 4)

    def own(array):
        array = array.reshape(seqs, block, width)
        return lax.dynamic_slice_in_dim(array, column_about, local_width, 2)

    onehot = (domain[..., None] == jnp.arange(3, dtype=jnp.int32)).astype(f32)
    own_counts = jnp.sum(onehot, axis=(0, 1))
    high = jnp.floor(own_counts / 128.0)
    digits = jnp.concatenate([high, own_counts - 128.0 * high]).astype(bf16)
    small = [w_beta, conv_weight, head_gain, mixer_gain, mlp_gain, digits]
    packed = padded(pack(small))
    size = width // 4
    if near_four:
        qkv_hop = first_hop(w_qkv)
        qkv_halves = halves_of(qkv_hop, 1)
        qkv = gathered_pieces(w_qkv, 1, qkv_hop, qkv_halves)
        packed = after(packed, qkv_halves)
        gathered = jnp.stack([packed] + [swap(packed, bits) for bits in (1, 2, 3)])
        half = w_out.shape[1] // 2
        pair_own = jnp.stack(
            [w_outgate, jnp.concatenate([w_out[:, :half], w_out[:, half:]], 0)]
        )
        pair_layout = [(k, 0, size, size) for k in range(4)]
        layout = pair_layout[:3] + [(3, 0, size // 2, size), (3, size // 2, size // 2, size)]
    else:
        gathered = lax.all_gather(packed, "dp")
        qkv = [lax.all_gather(w_qkv, "dp", axis=1, tiled=True)]
        gate_pieces = [lax.all_gather(w_outgate, "dp", axis=0, tiled=True)]
        out_pieces = [lax.all_gather(w_out, "dp", axis=1, tiled=True)]
        layout = pair_layout = [(0, 0, width, width)]
    ranges = [(k * step + start, n) for k, start, n, step in layout]
    g_beta, g_conv, g_head, g_mix, g_mlp, g_digits = unpack(gathered, [a.shape for a in small])
    about_beta = g_beta.reshape(-1, heads)
    full_beta = blocks_about(about_beta, 0)
    full_conv = jnp.moveaxis(blocks_about(g_conv, 0), 0, 3).reshape(3 * KW, inner).astype(f32)
    gain_head = blocks_about(g_head, 0).reshape(1, DK).astype(f32)
    gain_one = blocks_about(g_mix.reshape(1, -1).astype(f32), 1)
    gain_two = g_mlp.reshape(1, -1).astype(f32)
    sums = jnp.sum(g_digits.astype(f32), 0)
    counts = 128.0 * sums[:3] + sums[3:]
    table = group_weight * (domain.shape[0] * domain.shape[1] * dp) / counts
    factor = jnp.sum(onehot * table, -1)[..., None]

    def flat(array):
        return array.reshape(array.shape[:-3] + (count_rows, array.shape[-1]))

    rows = lax.all_gather(tokens, "mp", axis=2, tiled=True)
    if near_four:
        gate_pieces = out_pieces = [lax.all_gather(after(pair_own, packed), "dp")]
    turn_one = turn.reshape(1)
    per_token = (seqs, block)
    square = (seqs, heads, DK, DK)
    hidden_one, proj, tail, logits, scale_one = call(
        partial(project_kernel, layout),
        [(rows, 0), (gain_one, None), (jnp.pad(full_beta, ((0, 0), (0, 128 - heads))), None)]
        + [(a, None) for a in qkv],
        [
            (shape_of(per_token + (width,), bf16), 0),
            (shape_of((3,) + per_token + (inner,), bf16), 1),
            (shape_of((3, seqs, HALO, inner), bf16), 1),
            (shape_of(per_token + (heads,), f32), 0),
            (shape_of(per_token + (1,), f32), 0),
        ],
        seqs,
        scalar=turn_one,
        scratch=[pltpu.VMEM((block, width), bf16)],
    )
    before = shifted(tail, "dp", 1)
    inverse, wu, qo, to = call(
        pre_kernel,
        [(proj, None), (before, None), (full_conv, None), (logits, None)],
        [
            (shape_of((seqs, heads, block, block), f32), None),
            (shape_of((seqs, heads, block, 2 * DK), f32), None),
            (shape_of((seqs, heads, block, 2 * DK), f32), None),
            (shape_of((seqs, heads, DK, 2 * DK), bf16), None),
        ],
        1,
    )
    near = [shifted(to, "dp", c) for c in range(1, dp)]
    rows_about, cotangent = call(
        partial(prepare_kernel, layout),
        [(rows, 0), (out_grad, 0), (factor, 0)],
        [(shape_of(per_token + (width,), bf16), 0)] * 2,
        seqs,
        scalar=turn_one,
    )
    turned = jnp.swapaxes(w_gateup, 1, 2)
    feed_own = [turned, w_down]
    mixer_part, normed, rule, state, gates = call(
        partial(mix_kernel, pair_layout, len(near), len(out_pieces)),
        [(a, 0) for a in near]
        + [(qo, 0), (hidden_one, 0), (gain_head, None)]
        + [(a, None) for a in gate_pieces + out_pieces]
        + [(cotangent, "any")],
        [
            (shape_of(per_token + (width,), bf16), 0),
            (shape_of(per_token + (inner,), bf16), 0),
            (shape_of(per_token + (inner,), f32), 0),
            (shape_of(square, f32), 0),
            (shape_of(per_token + (inner,), f32), 0),
        ],
        seqs,
        scalar=turn_one,
    )
    total = lax.psum(mixer_part, "mp")
    nexts = [shifted(to[..., :DK], "dp", -c) for c in range(1, dp - 1)]
    if near_four:
        gateup, down = (gathered_pieces(a, a.ndim - 1) for a in after(copies(feed_own), mixer_part, nexts))
    else:
        gateup, down = (
            [lax.all_gather(a, "dp", axis=a.ndim - 1, tiled=True)] for a in feed_own
        )
    units = w_down.shape[0]
    two_part, hidden_two, hidden_mlp, grad_pair = call(
        partial(feed_kernel, layout),
        [(rows_about, 0), (total, 0), (cotangent, 0), (gain_two, None)]
        + [(a, None) for a in gateup + down],
        [
            (shape_of(per_token + (width,), bf16), 0),
            (shape_of(per_token + (width,), bf16), 0),
            (shape_of(per_token + (units,), bf16), 0),
            (shape_of((2,) + per_token + (units,), bf16), 1),
        ],
        seqs,
    )
    grad_two = lax.psum(two_part, "mp")

    def feed_gradients(some, *others):
        outs = [(shape_of((m, units, n), bf16), None) for _, n in some for m in (2, 1)]
        base, span = some[0][0], sum(n for _, n in some)
        aligned = base % span == 0
        at = base // span if aligned else 0
        cols = pl.BlockSpec((count_rows, span if aligned else width), lambda s: (0, at))
        made = pl.pallas_call(
            partial(feed_gradient_kernel, base if aligned else 0, some),
            cost_estimate=FREE,
            grid=(1,),
            in_specs=[
                cols,
                cols,
                pl.BlockSpec((2, count_rows, units), lambda s: (0, 0, 0)),
                pl.BlockSpec((count_rows, units), lambda s: (0, 0)),
            ]
            + [pl.BlockSpec(memory_space=pl.ANY)] * len(others),
            out_specs=[pl.BlockSpec(o.shape, lambda s: (0, 0, 0)) for o, _ in outs],
            out_shape=[o for o, _ in outs],
            compiler_params=pltpu.CompilerParams(vmem_limit_bytes=VMEM),
        )(flat(hidden_two), flat(cotangent), flat(grad_pair), flat(hidden_mlp), *others)
        return made[::2], made[1::2]

    if near_four:
        feed_far = feed_gradients(ranges[3:])
        feed_in = [far_hop(*far) for far in feed_far]
        near_gateup, near_down = feed_gradients(ranges[:3], feed_far[0][0])
        first_made = [(near_gateup[0], "any")]
    else:
        [grad_gateup], [grad_down] = feed_gradients(ranges)
        held = first_made = []
    [down_part] = call(
        partial(down_kernel, layout),
        [(hidden_mlp, 0)] + [(a, None) for a in down] + first_made,
        [(shape_of(per_token + (width,), bf16), 0)],
        seqs,
        scalar=turn_one,
    )
    if near_four:
        gateup_added = near_sums(near_gateup, feed_in[0], *feed_in[1], down_part)
        down_added = near_sums(near_down, feed_in[1])
        gateup_sums, down_sums = near_hop(gateup_added), near_hop(down_added)
        down_part = after(down_part, gateup_added[1])
        held = [(a, "any") for a in gateup_sums[1:]]
    mlp_share = lax.psum_scatter(down_part, "mp", scatter_dimension=2, tiled=True)
    grad_mix, middle_own, mlpgain, drule, dgate, dgain, direct = call(
        partial(middle_back_kernel, pair_layout, len(out_pieces)),
        [
            (grad_two, 0),
            (cotangent, 0),
            (rows_about, 0),
            (total, 0),
            (gain_two, None),
            (rule, 0),
            (gates, 0),
            (gain_head, None),
            (qo, 0),
        ]
        + [(a, None) for a in out_pieces]
        + [(down_part, "any")]
        + held,
        [
            (shape_of(per_token + (width,), bf16), 0),
            (shape_of(per_token + (local_width,), f32), 0),
            (shape_of((seqs, 1, width), f32), 0),
            (shape_of(per_token + (inner,), f32), 0),
            (shape_of(per_token + (inner,), bf16), 0),
            (shape_of((seqs, 1, DK), f32), 0),
            (shape_of(square, bf16), 0),
        ],
        seqs,
        scalar=jnp.stack([turn, column_about]),
        scratch=[pltpu.VMEM((block, width), f32)],
    )
    directs = [shifted(direct, "dp", -c) for c in range(1, dp)]
    if near_four:
        pair_grads = call(
            partial(pair_gradient_kernel, [(k * size, size) for k in range(4)]),
            [(flat(a), None) for a in (hidden_one, dgate, normed, grad_mix)],
            [(shape_of((2, size, inner), bf16), None)] * 4,
            1,
        )
        down_total = sum_last(down_sums, pair_grads[3])
        held = [(a, "any") for a in (pair_grads[3], down_total)]
    else:
        grad_outgate = jnp.einsum(
            "td,tc->dc", flat(hidden_one), flat(dgate), preferred_element_type=f32
        )
        grad_outproj = jnp.einsum(
            "tc,td->cd", flat(normed), flat(grad_mix), preferred_element_type=f32
        )
        held = []
    dproj, last, first, dtaps, dlogits = call(
        partial(back_kernel, len(directs)),
        [
            (proj, 1),
            (before, 1),
            (full_conv, None),
            (logits, 0),
            (inverse, 0),
            (wu, 0),
            (state, 0),
            (drule, 0),
        ]
        + [(a, 0) for a in directs + nexts]
        + held,
        [
            (shape_of((3,) + per_token + (inner,), bf16), 1),
            (shape_of((3, seqs, PAD, inner), f32), 1),
            (shape_of((3, seqs, PAD, inner), f32), 1),
            (shape_of((seqs, 3 * KW, inner), f32), 0),
            (shape_of(per_token + (heads,), bf16), 0),
        ],
        seqs,
    )
    late = []
    if near_four:
        gateup_total = sum_last(gateup_sums, dlogits)
        late = [(gateup_total, "any")]
    later = shifted(first, "dp", -1)
    dproj = lax.dynamic_update_slice(dproj, (last + later).astype(bf16), (0, 0, block - PAD, 0))
    one_low, row_part, gain_part = call(
        partial(first_back_kernel, layout, pair_layout, len(gate_pieces)),
        [
            (flat(dproj), None),
            (flat(dgate), None),
            (flat(dlogits), None),
            (flat(proj), None),
            (flat(gates), None),
            (flat(logits), None),
            (about_beta.T.astype(f32), None),
            (flat(rows_about), None),
            (flat(scale_one), None),
        ]
        + [(a, None) for a in qkv + gate_pieces]
        + late,
        [
            (shape_of((count_rows, width), bf16), None),
            (shape_of((1, count_rows), f32), None),
            (shape_of((1, width), f32), None),
        ],
        1,
        scalar=turn_one,
    )
    one_share = lax.psum_scatter(
        one_low.reshape(seqs, block, width), "mp", scatter_dimension=2, tiled=True
    ).astype(f32)
    made = call(
        partial(qkv_gradient_kernel, ranges),
        [(flat(hidden_one), None), (flat(dproj), None), (flat(dlogits), None), (row_part, "any")],
        [(shape_of((3, n, inner), bf16), None) for _, n in ranges]
        + [(shape_of((heads, width), f32), None)],
        1,
    )

    def pieces(array, axis, about):
        shape = array.shape
        cut = array.reshape(shape[:axis] + (dp, shape[axis] // dp) + shape[axis + 1 :])
        cut = jnp.moveaxis(cut, axis, 0).reshape(dp, -1)
        return blocks_about(cut, 0) if about else cut

    smalls = jnp.concatenate(
        [
            pieces(jnp.sum(dtaps, 0).reshape(3, KW, heads, DK), 3, True),
            pieces(made[-1].T, 0, False),
            pieces(gain_part[0], 0, False),
            pieces(jnp.sum(mlpgain, (0, 1)), 0, False),
            pieces(jnp.sum(dgain, (0, 1)), 0, True),
        ],
        1,
    )
    small_shapes = [a.shape for a in (conv_weight, w_beta, mixer_gain, mlp_gain, head_gain)]
    if near_four:
        own_qkv, *near_qkv = near_sums(made[:3], far_hop(made[3], made[4]))
        smalls = jnp.pad(smalls, ((0, 0), (0, -smalls.shape[1] % 1024))).reshape(dp, -1, 128)
        sent = smalls.astype(bf16)
        got = [swap(sent[bits], bits) for bits in (1, 2, 3)]
        first_mix = (conv_weight.size + w_beta.size) // 128
        last_mix = first_mix + mixer_gain.size // 128
        lines = count_rows // 128 + last_mix - first_mix
        mine, rest = call(
            partial(
                add_small_kernel,
                slice(first_mix, last_mix),
                last_mix + mlp_gain.size // 128,
            ),
            [(a, None) for a in [smalls[0]] + got + [row_part]],
            [
                (shape_of(smalls.shape[1:], f32), None),
                (shape_of((lines + 8 - lines % 8, 128), f32), None),
            ],
            1,
        )
        pair_far = after(jnp.split(pair_grads[3], 2, 1), made[0])
        pair_near = near_sums(pair_grads[:3], far_hop(*pair_far))[1:]
        mine = mine.reshape(-1)
        sum_qkv = sum_last(near_hop((own_qkv, *near_qkv)))
        sum_gateup = jnp.swapaxes(gateup_total, 1, 2)
        sum_down = down_total[0]
        pair_sums = near_hop((pair_grads[0], *pair_near))
    else:
        gathered = lax.all_gather(smalls.astype(bf16), "dp")
        mine = jnp.sum(
            lax.dynamic_index_in_dim(gathered, place, 1, keepdims=False).astype(f32), 0
        )

        def scattered(array, axis):
            return lax.psum_scatter(array, "dp", scatter_dimension=axis, tiled=True).astype(f32)

        sum_qkv = scattered(made[0], 1)
        sum_outgate = scattered(grad_outgate.astype(bf16), 0)
        sum_out = scattered(grad_outproj.astype(bf16), 1)
        sum_gateup = jnp.swapaxes(scattered(grad_gateup, 2), 1, 2)
        sum_down = scattered(grad_down[0], 1)
    sum_conv, sum_beta, sum_mix, sum_mlp, sum_head = unpack(mine, small_shapes)
    if near_four:
        bit = 1
        while bit < lax.axis_size("mp"):
            devices = lax.axis_size("mp")
            rest = rest + lax.ppermute(rest, "mp", [(i, i ^ bit) for i in range(devices)])
            bit *= 2
        rest_sum = rest.reshape(-1)
    else:
        rest_sum = lax.psum(pack([row_part, sum_mix, sum_head]), "mp")
    row_sum, sum_mix, sum_head = unpack(rest_sum, [(count_rows,), sum_mix.shape, sum_head.shape])

    own_tokens = tokens.astype(f32)
    mixed_out = (own_tokens + own(total).astype(f32) + mlp_share.astype(f32)).astype(bf16)
    row_mean = (row_sum / width).reshape(seqs, block, 1)
    gain_own = lax.dynamic_slice_in_dim(gain_one, column, local_width, 1)
    tokens_grad = middle_own + scale_one * (
        one_share * gain_own - own_tokens * scale_one * row_mean
    )
    tokens_grad = tokens_grad.astype(bf16)
    if near_four:
        done = [(a, "any") for a in (sum_qkv, tokens_grad, mixed_out)]
        sum_outgate, sum_out = call(
            add_pair_kernel,
            [(a, None) for a in pair_sums] + done,
            [(shape_of(w_outgate.shape, f32), None), (shape_of(w_out.shape, f32), None)],
            1,
        )
    return (
        mixed_out,
        tokens_grad,
        sum_qkv,
        sum_conv,
        sum_beta,
        sum_outgate,
        sum_head,
        sum_out,
        sum_mix,
        sum_mlp,
        sum_gateup,
        sum_down,
    )


def solution(mesh):
    return jax.shard_map(
        body,
        mesh=mesh,
        in_specs=(
            P(None, "dp", "mp"),
            P(None, "dp", None),
            P(None, "dp"),
            P(),
            P(None, "dp", "mp"),
            P(None, None, "mp", "dp"),
            P("dp", "mp"),
            P("dp", "mp"),
            P("dp"),
            P("mp", "dp"),
            P("dp"),
            P("dp"),
            P(None, "dp", "mp"),
            P("mp", "dp"),
        ),
        out_specs=(
            P(None, "dp", "mp"),
            P(None, "dp", "mp"),
            P(None, "dp", "mp"),
            P(None, None, "mp", "dp"),
            P("dp", "mp"),
            P("dp", "mp"),
            P("dp"),
            P("mp", "dp"),
            P("dp"),
            P("dp"),
            P(None, "dp", "mp"),
            P("mp", "dp"),
        ),
        check_vma=False,
    )
```

```python
from functools import partial

import jax
import jax.numpy as jnp
from jax import lax
from jax.experimental import pallas as pl
from jax.experimental.pallas import tpu as pltpu
from jax.sharding import PartitionSpec as P

DK = 128
KW = 4
PAD = 8
HALO = 16
ROWS = 16
VMEM = 58 * 2**20
FREE = pl.CostEstimate(flops=0, transcendentals=0, bytes_accessed=0)

eps_norm = 1e-06
eps_unit = 1e-06

f32 = jnp.float32
bf16 = jnp.bfloat16


def split(v):
    if v.dtype == bf16:
        return v, None
    high = v.astype(bf16)
    return high, (v - high.astype(f32)).astype(bf16)


def mm(a, b, ca=1, cb=0, passes=3):
    def one(x, y):
        return lax.dot_general(x, y, (((ca,), (cb,)), ((), ())), preferred_element_type=f32)

    if passes == 1:
        return one(a.astype(bf16), b.astype(bf16))
    (ah, al), (bh, bl) = split(a), split(b)
    out = one(ah, bh)
    if bl is not None:
        out = out + one(ah, bl)
    if al is not None:
        out = out + one(al, bh)
    return out


def places(rows, cols):
    return (
        lax.broadcasted_iota(jnp.int32, (rows, cols), 0),
        lax.broadcasted_iota(jnp.int32, (rows, cols), 1),
    )


def unit_lower_inverses(blocks):
    size = blocks[0].shape[0]
    if size > 128:
        half = size // 2
        parts = unit_lower_inverses(
            [a[:half, :half] for a in blocks] + [a[half:, half:] for a in blocks]
        )
        firsts, seconds = parts[: len(blocks)], parts[len(blocks) :]
        inner = [mm(a[half:, :half], x) for a, x in zip(blocks, firsts)]
        lower = [-mm(x, y) for x, y in zip(seconds, inner)]
        zero = jnp.zeros((half, half), f32)
        return [
            jnp.concatenate(
                [jnp.concatenate([x, zero], 1), jnp.concatenate([y, z], 1)], 0
            )
            for x, y, z in zip(firsts, lower, seconds)
        ]
    rows, cols = places(size, size)
    eye = (rows == cols).astype(f32)
    level = 0
    inverses = None
    while (1 << level) < size:
        mask = (
            ((rows >> (level + 1)) == (cols >> (level + 1)))
            & (((rows >> level) & 1) == 1)
            & (((cols >> level) & 1) == 0)
        ).astype(f32)
        lows = [a * mask for a in blocks]
        if level == 0:
            inverses = [eye - low for low in lows]
        else:
            inner = [mm(low, x) for low, x in zip(lows, inverses)]
            inverses = [x - mm(x, y) for x, y in zip(inverses, inner)]
        level += 1
    return inverses


def head_slice(h):
    return slice(h * DK, (h + 1) * DK)


def convolve(proj_ref, before_ref, taps, i, h):
    own = proj_ref[i, 0, :, head_slice(h)].astype(f32)
    length = own.shape[0]
    ext = jnp.concatenate([before_ref[i, 0, :, head_slice(h)].astype(f32), own], 0)
    shifts = [ext[HALO - KW + 1 + j : HALO - KW + 1 + j + length] for j in range(KW)]
    out = None
    for j in range(KW):
        tap = taps[i * KW + j : i * KW + j + 1, head_slice(h)]
        out = tap * shifts[j] if out is None else out + tap * shifts[j]
    sig = jax.nn.sigmoid(out)
    return shifts, out, sig, out * sig


def unit(acts):
    inv = lax.rsqrt(jnp.sum(acts * acts, -1, keepdims=True) + eps_unit)
    return acts * inv, inv


def rule_inputs(proj_ref, before_ref, taps, h):
    parts = [convolve(proj_ref, before_ref, taps, i, h) for i in range(3)]
    q, q_inv = unit(parts[0][3])
    k, k_inv = unit(parts[1][3])
    return parts, (q, q_inv), (k, k_inv), parts[2][3]


def norm_factor(values):
    return lax.rsqrt(jnp.mean(values * values, -1, keepdims=True) + eps_norm)


def project_kernel(layout, *refs):
    place_ref, rows_ref, gain_ref, beta_ref = refs[:4]
    pieces = refs[4 : 4 + len(layout)]
    hidden_ref, proj_ref, tail_ref, logit_ref, scale_ref, keep_ref = refs[4 + len(layout) :]
    rows = rows_ref[0].astype(f32)
    scale = norm_factor(rows)
    scale_ref[0] = scale
    keep_ref[...] = (rows * scale * gain_ref[...]).astype(bf16)
    logits = mm(keep_ref[...], beta_ref[...])
    logit_ref[0] = logits[:, : logit_ref.shape[2]]
    sums = [None] * 3
    for (k, start, size, block), piece in zip(layout, pieces):
        at = pl.multiple_of((place_ref[0] ^ k) * block + start, 128)
        part = keep_ref[:, pl.ds(at, size)]
        hidden_ref[0, :, k * block + start : k * block + start + size] = part
        for i in range(3):
            term = mm(part, piece[i])
            sums[i] = term if sums[i] is None else sums[i] + term
    for i in range(3):
        low = sums[i].astype(bf16)
        proj_ref[i, 0] = low
        tail_ref[i, 0] = low[low.shape[0] - HALO :]


def pre_kernel(proj_ref, before_ref, taps_ref, logit_ref, x_ref, wu_ref, qo_ref, to_ref):
    seqs, heads = to_ref.shape[:2]
    taps = taps_ref[...]
    length = proj_ref.shape[2]
    r, c = places(length, length)
    strict = (r > c).astype(f32)
    full = (r >= c).astype(f32)
    saved, blocks = [], []
    for s in range(seqs):
        betas = jax.nn.sigmoid(logit_ref[s])
        rows, before = proj_ref.at[:, s : s + 1], before_ref.at[:, s : s + 1]
        for h in range(heads):
            _, (q, _), (k, _), v = rule_inputs(rows, before, taps, h)
            q, k, v = q.astype(bf16), k.astype(bf16), v.astype(bf16)
            beta = betas[:, h : h + 1]
            blocks.append(beta * mm(k, k, 1, 1) * strict)
            saved.append((s, h, q, k, v, beta))
    inverses = unit_lower_inverses(blocks)
    r, c = places(DK, DK)
    eye = (r == c).astype(f32)
    for (s, h, q, k, v, beta), x in zip(saved, inverses):
        x_ref[s, h] = x
        kv = jnp.concatenate([k.astype(f32), v.astype(f32)], 1) * beta
        wu = mm(x, kv)
        wu_ref[s, h] = wu
        scores = mm(q, k, 1, 1) * full
        pwu = mm(scores, wu)
        qo_ref[s, h, :, :DK] = q.astype(f32) - pwu[:, :DK]
        qo_ref[s, h, :, DK:] = pwu[:, DK:]
        kwu = mm(k, wu, 0, 0)
        to_ref[s, h, :, :DK] = (eye - kwu[:, :DK]).astype(bf16)
        to_ref[s, h, :, DK:] = kwu[:, DK:].astype(bf16)


def by_piece(place_ref, refs):
    if len(refs) > 1 or len(refs[0].shape) < 4:
        return refs
    return [refs[0].at[place_ref[0] ^ k] for k in range(4)]


def gate_part(ref):
    return ref.at[0] if len(ref.shape) == 3 else ref


def out_columns(layout, refs):
    for (k, start, size, block), ref in zip(layout, refs):
        at, half = k * block + start, size // 2
        if len(ref.shape) == 2:
            yield at, size, ref
            continue
        inner = ref.shape[1] // 2
        yield at, half, ref.at[1, :inner]
        yield at + half, half, ref.at[1, inner:]


def mix_kernel(layout, count, pieces, place_ref, *refs):
    near, rest = refs[:count], refs[count:]
    qo_ref, hidden_ref, gain_ref = rest[:3]
    gate_pieces = by_piece(place_ref, rest[3 : 3 + pieces])
    outs = by_piece(place_ref, rest[3 + pieces : 3 + 2 * pieces])
    part_ref, normed_ref, rule_ref, state_ref, gate_ref = rest[-5:]
    gates = None
    for (k, start, size, block), ref in zip(layout, gate_pieces):
        at = k * block + start
        term = mm(hidden_ref[0, :, at : at + size], gate_part(ref)[...])
        gates = term if gates is None else gates + term
    gate_ref[0] = gates
    heads = state_ref.shape[1]
    for h in range(heads):
        state = near[-1][0, h, :, DK:].astype(f32)
        for ref in reversed(near[:-1]):
            state = mm(ref[0, h, :, :DK], state) + ref[0, h, :, DK:].astype(f32)
        state_ref[0, h] = state
        qo = qo_ref[0, h]
        out = (mm(qo[:, :DK], state) + qo[:, DK:]) * DK ** (-0.5)
        rule_ref[0, :, head_slice(h)] = out
        gate = gate_ref[0, :, head_slice(h)]
        normed = out * norm_factor(out) * gain_ref[...] * (gate * jax.nn.sigmoid(gate))
        normed_ref[0, :, head_slice(h)] = normed.astype(bf16)
    for at, size, ref in out_columns(layout, outs):
        part_ref[0, :, at : at + size] = mm(normed_ref[0], ref[...]).astype(bf16)


def prepare_kernel(layout, place_ref, rows_ref, grad_ref, factor_ref, about_ref, cot_ref):
    for k, start, size, block in layout:
        at = pl.multiple_of((place_ref[0] ^ k) * block + start, 128)
        to = slice(k * block + start, k * block + start + size)
        about_ref[0, :, to] = rows_ref[0, :, pl.ds(at, size)]
        grad = grad_ref[0, :, pl.ds(at, size)].astype(f32) * factor_ref[0]
        cot_ref[0, :, to] = grad.astype(bf16)


def down_kernel(layout, place_ref, mlp_ref, *refs):
    part_ref = refs[-1]
    for (k, start, size, block), ref in zip(layout, refs):
        at = pl.multiple_of((place_ref[0] ^ k) * block + start, 128)
        part_ref[0, :, pl.ds(at, size)] = mm(mlp_ref[0], ref[...]).astype(bf16)


def feed_gradient_kernel(base, ranges, hidden_ref, cot_ref, pair_ref, mlp_ref, *outs):
    outs = outs[-2 * len(ranges) :]
    for n, (start, size) in enumerate(ranges):
        start = start - base
        hidden = hidden_ref[:, start : start + size]
        outs[2 * n][0] = mm(pair_ref[0], hidden, 0, 0).astype(bf16)
        outs[2 * n][1] = mm(pair_ref[1], hidden, 0, 0).astype(bf16)
        outs[2 * n + 1][0] = mm(mlp_ref[...], cot_ref[:, start : start + size], 0, 0).astype(bf16)


def qkv_gradient_kernel(ranges, hidden_ref, dproj_ref, dlogit_ref, *outs):
    outs = outs[-len(ranges) - 1 :]
    for (start, size), out in zip(ranges, outs[:-1]):
        hidden = hidden_ref[:, start : start + size]
        for i in range(3):
            out[i] = mm(hidden, dproj_ref[i], 0, 0).astype(bf16)
    outs[-1][...] = mm(dlogit_ref[...], hidden_ref[...], 0, 0)


def pair_gradient_kernel(ranges, hidden_ref, dgate_ref, normed_ref, mix_ref, *outs):
    inner = normed_ref.shape[1]
    for (start, size), out in zip(ranges, outs):
        out[0] = mm(hidden_ref[:, start : start + size], dgate_ref[...], 0, 0).astype(bf16)
        for n in range(2):
            at = start + n * size // 2
            mix = mix_ref[:, at : at + size // 2]
            out[1, n * inner : (n + 1) * inner] = mm(normed_ref[...], mix, 0, 0).astype(bf16)


def add_halves_kernel(*refs):
    one_ref, two_ref, low_ref, high_ref, one_out, two_out = refs[:4] + refs[-2:]
    one_out[...] = (one_ref[...].astype(f32) + high_ref[...].astype(f32)).astype(bf16)
    two_out[...] = (two_ref[...].astype(f32) + low_ref[...].astype(f32)).astype(bf16)


def add_small_kernel(mix_rows, head_row, *refs):
    *parts, row_ref, out_ref, rest_ref = refs
    total = sum(ref[...].astype(f32) for ref in parts)
    out_ref[...] = total
    lines = [row_ref[:, n * 128 : (n + 1) * 128] for n in range(row_ref.shape[1] // 128)]
    lines += [total[mix_rows], total[head_row : head_row + 1]]
    used = len(lines) - 2 + mix_rows.stop - mix_rows.start + 1
    lines.append(jnp.zeros((rest_ref.shape[0] - used, 128), f32))
    rest_ref[...] = jnp.concatenate(lines, 0)


def add_last_kernel(*refs):
    own_ref, one_ref, two_ref, out_ref = refs[:3] + refs[-1:]
    out_ref[...] = own_ref[...].astype(f32) + one_ref[...].astype(f32) + two_ref[...].astype(f32)


def feed_kernel(layout, *refs):
    rows_ref, total_ref, cot_ref, gain_ref = refs[:4]
    count = len(layout)
    gateups, downs = (refs[4 + n * count : 4 + (n + 1) * count] for n in range(2))
    two_ref, hidden_ref, mlp_ref, pair_ref = refs[-4:]
    middle = rows_ref[0].astype(f32) + total_ref[0].astype(f32)
    hidden_ref[0] = (middle * norm_factor(middle) * gain_ref[...]).astype(bf16)
    gate, up, grad = None, None, None
    for (k, start, size, block), w_gateup, w_down in zip(layout, gateups, downs):
        lanes = slice(k * block + start, k * block + start + size)
        hidden = hidden_ref[0, :, lanes]
        terms = (
            mm(hidden, w_gateup[0], 1, 1),
            mm(hidden, w_gateup[1], 1, 1),
            mm(cot_ref[0, :, lanes], w_down[...], 1, 1),
        )
        if gate is None:
            gate, up, grad = terms
        else:
            gate, up, grad = gate + terms[0], up + terms[1], grad + terms[2]
    sig = jax.nn.sigmoid(gate)
    silu = gate * sig
    mlp_ref[0] = (silu * up).astype(bf16)
    first = (grad * up * (sig + silu * (1.0 - sig))).astype(bf16)
    second = (grad * silu).astype(bf16)
    pair_ref[0, 0] = first
    pair_ref[1, 0] = second
    for (k, start, size, block), w_gateup in zip(layout, gateups):
        lanes = slice(k * block + start, k * block + start + size)
        two = mm(first, w_gateup[0]) + mm(second, w_gateup[1])
        two_ref[0, :, lanes] = two.astype(bf16)


def middle_back_kernel(layout, pieces, at_ref, *refs):
    two_ref, cot_ref, rows_ref, total_ref, gain_ref, rule_ref, gate_ref, head_gain_ref, qo_ref = refs[:9]
    outs = by_piece(at_ref, refs[9 : 9 + pieces])
    mix_ref, own_ref, mlpgain_ref, drule_ref, dgate_ref, dgain_ref, direct_ref, keep_ref = refs[-8:]
    full = rows_ref.shape[2]
    gain_sum = None
    for start in range(0, rows_ref.shape[1], ROWS):
        at = slice(start, start + ROWS)
        middle = rows_ref[0, at].astype(f32) + total_ref[0, at].astype(f32)
        two = two_ref[0, at].astype(f32)
        factor = norm_factor(middle)
        normal = middle * factor
        term = jnp.sum((two * normal).reshape(ROWS // 8, 8, full), 0)
        gain_sum = term if gain_sum is None else gain_sum + term
        scaled = two * gain_ref[...]
        mean = jnp.mean(scaled * normal, -1, keepdims=True)
        keep = cot_ref[0, at].astype(f32) + factor * (scaled - normal * mean)
        keep_ref[at] = keep
        mix_ref[0, at] = keep.astype(bf16)
    mlpgain_ref[0] = jnp.sum(gain_sum, 0, keepdims=True)
    width = own_ref.shape[2]
    own_ref[0] = keep_ref[:, pl.ds(pl.multiple_of(at_ref[1], 128), width)]
    grads = None
    for at, size, ref in out_columns(layout, outs):
        term = mm(mix_ref[0, :, at : at + size], ref[...], 1, 1)
        grads = term if grads is None else grads + term
    total = jnp.zeros((1, DK), f32)
    for h in range(direct_ref.shape[1]):
        grad = grads[:, head_slice(h)]
        out = rule_ref[0, :, head_slice(h)]
        gate = gate_ref[0, :, head_slice(h)]
        inv = norm_factor(out)
        n = out * inv
        sig = jax.nn.sigmoid(gate)
        silu = gate * sig
        gg = grad * head_gain_ref[...]
        dn = gg * silu
        drule = inv * (dn - n * jnp.mean(dn * n, -1, keepdims=True))
        drule_ref[0, :, head_slice(h)] = drule
        dgate = gg * n * sig * (1.0 + gate * (1.0 - sig))
        dgate_ref[0, :, head_slice(h)] = dgate.astype(bf16)
        total = total + jnp.sum(grad * n * silu, 0, keepdims=True)
        direct = mm(qo_ref[0, h, :, :DK], drule, 0, 0) * DK ** (-0.5)
        direct_ref[0, h] = direct.astype(bf16)
    dgain_ref[0] = total


def first_back_kernel(layout, pair_layout, count, place_ref, *refs):
    dproj_ref, dgate_ref, dlogit_ref, proj_ref, gate_ref, logit_ref, beta_ref, rows_ref, scale_ref = refs[:9]
    pieces = refs[9 : 9 + len(layout)]
    pairs = by_piece(place_ref, refs[9 + len(layout) : 9 + len(layout) + count])
    one_ref, rowsum_ref, gainsum_ref = refs[-3:]
    gates = {}
    for (k, start, size, block), ref in zip(pair_layout, pairs):
        gates[k] = ref
    for (k, start, size, block), piece in zip(layout, pieces):
        lanes = slice(k * block + start, k * block + start + size)
        grad = mm(dgate_ref[...], gate_part(gates[k])[start : start + size], 1, 1)
        for i in range(3):
            grad = grad + mm(dproj_ref[i], piece[i], 1, 1)
        for h in range(beta_ref.shape[0]):
            grad = grad + dlogit_ref[:, h : h + 1].astype(f32) * beta_ref[h : h + 1, lanes]
        at = pl.multiple_of((place_ref[0] ^ k) * block + start, 128)
        one_ref[:, pl.ds(at, size)] = grad.astype(bf16)
        gainsum_ref[:, lanes] = jnp.sum(
            grad * (rows_ref[:, lanes].astype(f32) * scale_ref[...]), 0, keepdims=True
        )
    total = dgate_ref[...].astype(f32) * gate_ref[...]
    for i in range(3):
        total = total + dproj_ref[i].astype(f32) * proj_ref[i].astype(f32)
    lane = lax.broadcasted_iota(jnp.int32, total.shape, 1) == 0
    logits = jnp.sum(dlogit_ref[...].astype(f32) * logit_ref[...], -1, keepdims=True)
    logits_sum = jnp.where(lane, logits, 0.0)
    total = total + logits_sum
    ones = jnp.ones((8, total.shape[1]), f32)
    rowsum_ref[...] = mm(ones, total, 1, 1)[:1]


def back_kernel(count, *refs):
    (
        proj_ref,
        before_ref,
        taps_ref,
        logit_ref,
        x_ref,
        wu_ref,
        state_ref,
        drule_ref,
    ) = refs[:8]
    dproj_ref, last_ref, first_ref, dtaps_ref, dlogit_ref = refs[-5:]
    others = refs[8 : 8 + 2 * count - 1]
    directs, nexts = others[:count], others[count:]
    heads = state_ref.shape[1]
    taps = taps_ref[...]
    length = proj_ref.shape[2]
    betas = jax.nn.sigmoid(logit_ref[0])
    r, c = places(length, length)
    strict = (r > c).astype(f32)
    full = (r >= c).astype(f32)
    zeros = jnp.zeros((PAD, DK), f32)
    for h in range(heads):
        parts, (qu, q_inv), (ku, k_inv), vu = rule_inputs(proj_ref, before_ref, taps, h)
        q, k, v = qu.astype(bf16), ku.astype(bf16), vu.astype(bf16)
        beta = betas[:, h : h + 1]
        leave = jnp.zeros((DK, DK), f32)
        for j in reversed(range(count)):
            here = directs[j][0, h].astype(f32)
            leave = here if j == count - 1 else mm(nexts[j][0, h], leave, 0, 0) + here
        state = state_ref[0, h]
        wu = wu_ref[0, h]
        u = wu[:, DK:] - mm(wu[:, :DK], state)
        resid = v.astype(f32) - mm(k, state)
        dout = drule_ref[0, :, head_slice(h)] * DK ** (-0.5)
        gram = mm(k, k, 1, 1)
        scores = mm(q, k, 1, 1) * full
        du = mm(scores, dout, 0, 0) + mm(k, leave)
        y = mm(x_ref[0, h], du, 0, 0)
        by = beta * y
        da = -(mm(y, u, 1, 1, 1) * strict)
        dbeta = jnp.sum(y * resid, -1, keepdims=True) + jnp.sum(da * gram, -1, keepdims=True)
        dgram = beta * da
        dscores = mm(dout, u, 1, 1, 1) * full
        dq = mm(dout, state, 1, 1, 1) + mm(dscores, k, 1, 0, 1)
        dk = (
            mm(dgram, k, 1, 0, 1)
            + mm(dgram, k, 0, 0, 1)
            + mm(dscores, q, 0, 0, 1)
            + mm(u, leave, 1, 1, 1)
            - mm(by, state, 1, 1, 1)
        )
        dlogit_ref[0, :, h : h + 1] = (dbeta * beta * (1.0 - beta)).astype(bf16)
        dq = (dq - qu * jnp.sum(qu * dq, -1, keepdims=True)) * q_inv
        dk = (dk - ku * jnp.sum(ku * dk, -1, keepdims=True)) * k_inv
        for i, dact in enumerate((dq, dk, by)):
            shifts, out, sig, _ = parts[i]
            dconv = dact * sig * (1.0 + out * (1.0 - sig))
            ext = jnp.concatenate([zeros, dconv, zeros], 0)
            total = None
            for j in range(KW):
                at = i * KW + j
                dtaps_ref[0, at : at + 1, head_slice(h)] = jnp.sum(
                    dconv * shifts[j], 0, keepdims=True
                )
                tap = taps[at : at + 1, head_slice(h)]
                term = tap * ext[KW - 1 - j : KW - 1 - j + PAD + length]
                total = term if total is None else total + term
            first_ref[i, 0, :, head_slice(h)] = total[:PAD]
            last_ref[i, 0, :, head_slice(h)] = total[length:]
            dproj_ref[i, 0, :, head_slice(h)] = total[PAD:].astype(bf16)


def call(kernel, ins, outs, steps, scalar=None, scratch=(), limit=VMEM, alias=None):
    def spec(shape, axis):
        if axis == "any":
            return pl.BlockSpec(memory_space=pl.ANY)
        block = tuple(1 if n == axis else size for n, size in enumerate(shape))
        where = lambda s, *_: tuple(s if n == axis else 0 for n in range(len(shape)))
        if axis is None:
            return pl.BlockSpec(block, where, pipeline_mode=pl.Buffered(1))
        return pl.BlockSpec(block, where)

    given = [] if scalar is None else [scalar]
    return pl.pallas_call(
        kernel,
        cost_estimate=FREE,
        grid_spec=pltpu.PrefetchScalarGridSpec(
            num_scalar_prefetch=len(given),
            grid=(steps,),
            in_specs=[spec(a.shape, axis) for a, axis in ins],
            out_specs=[spec(o.shape, axis) for o, axis in outs],
            scratch_shapes=scratch,
        ),
        out_shape=[o for o, _ in outs],
        input_output_aliases=alias or {},
        compiler_params=pltpu.CompilerParams(vmem_limit_bytes=limit),
    )(*given, *[a for a, _ in ins])


def shape_of(shape, dtype):
    return jax.ShapeDtypeStruct(shape, dtype)


def shifted(array, axis, by):
    devices = lax.axis_size(axis)
    pairs = [(i, i + by) for i in range(devices) if 0 <= i + by < devices]
    return lax.ppermute(array, axis, pairs)


def after(values, *others):
    flat, tree = jax.tree.flatten(values)
    others = jax.tree.leaves(others)
    here = pl.BlockSpec(memory_space=pl.ANY)
    out = pl.pallas_call(
        lambda *refs: None,
        cost_estimate=FREE,
        in_specs=[here] * (len(flat) + len(others)),
        out_specs=[here] * len(flat),
        out_shape=[shape_of(a.shape, a.dtype) for a in flat],
        input_output_aliases={n: n for n in range(len(flat))},
    )(*flat, *others)
    return jax.tree.unflatten(tree, out)


def copies(values):
    count = len(values)

    def kernel(*refs):
        for n in range(count):
            refs[n - count][...] = refs[n][...]

    outs = [(shape_of(a.shape, a.dtype), None) for a in values]
    return call(kernel, [(a, None) for a in values], outs, 1)


def swap(array, bits):
    return lax.ppermute(array, "dp", [(i, i ^ bits) for i in range(4)])


def first_hop(own):
    return swap(own, 1), swap(own, 2)


def halves_of(hop, axis):
    low, high = (jnp.split(part, 2, axis) for part in hop)
    return low[0], high[1]


def gathered_pieces(own, axis, hop=None, halves=None):
    hop = hop or first_hop(own)
    low, high = halves or halves_of(hop, axis)
    return [own, *hop, swap(low, 2), swap(high, 1)]


def far_hop(low, high):
    return swap(low, 1), swap(high, 2)


def near_sums(pieces, far_in, *others):
    own, one, two = pieces
    half = far_in[0].shape
    along = 1 if half[1] < one.shape[1] else 2

    def spec(place):
        where = tuple(place if n == along else 0 for n in range(3))
        return pl.BlockSpec(half, lambda s: where)

    first, second = spec(0), spec(1)
    here = pl.BlockSpec(memory_space=pl.ANY)
    one, two = pl.pallas_call(
        add_halves_kernel,
        cost_estimate=FREE,
        grid=(1,),
        in_specs=[second, first, first, first] + [here] * len(others),
        out_specs=[second, first],
        out_shape=[shape_of(a.shape, a.dtype) for a in (one, two)],
        input_output_aliases={0: 0, 1: 1},
        compiler_params=pltpu.CompilerParams(vmem_limit_bytes=VMEM),
    )(one, two, *far_in, *others)
    return own, one, two


def near_hop(pieces):
    own, one, two = pieces
    return own, swap(one, 1), swap(two, 2)


def add_pair_kernel(own_ref, one_ref, two_ref, *refs):
    gate_ref, out_ref = refs[-2:]
    inner = out_ref.shape[0]

    def added(i, rows):
        parts = (ref[i, rows].astype(f32) for ref in (own_ref, one_ref, two_ref))
        return sum(parts)

    gate_ref[...] = added(0, slice(None))
    for n in range(2):
        out_ref[:, n * inner : (n + 1) * inner] = added(1, slice(n * inner, (n + 1) * inner))


def sum_last(parts, *others):
    own = parts[0]
    ins = [(a, 0) for a in parts] + [(a, "any") for a in others]
    [total] = call(add_last_kernel, ins, [(shape_of(own.shape, f32), 0)], own.shape[0])
    return total


def pack(parts):
    return jnp.concatenate([p.reshape(-1) for p in parts])


def unpack(flat, shapes):
    out, at = [], 0
    for shape in shapes:
        size = 1
        for n in shape:
            size *= n
        out.append(flat[..., at : at + size].reshape(flat.shape[:-1] + tuple(shape)))
        at += size
    return out


def padded(flat, multiple=1024):
    return jnp.pad(flat, (0, -flat.shape[0] % multiple))


def body(
    tokens,
    out_grad,
    domain,
    group_weight,
    w_qkv,
    conv_weight,
    w_beta,
    w_outgate,
    head_gain,
    w_out,
    mixer_gain,
    mlp_gain,
    w_gateup,
    w_down,
):
    dp = lax.axis_size("dp")
    place = lax.axis_index("dp")
    seqs, block, local_width = tokens.shape
    count_rows = seqs * block
    heads = conv_weight.shape[2]
    inner = heads * DK
    column = lax.axis_index("mp") * local_width
    near_four = dp == 4

    def blocks_about(array, axis):
        if not near_four:
            return array
        size = array.shape[axis] // 4
        return jnp.concatenate(
            [lax.dynamic_slice_in_dim(array, (place ^ k) * size, size, axis) for k in range(4)],
            axis,
        )

    width = out_grad.shape[2]
    turn = place if near_four else jnp.int32(0)
    column_about = ((column // (width // 4)) ^ turn) * (width // 4) + column % (width // 4)

    def own(array):
        array = array.reshape(seqs, block, width)
        return lax.dynamic_slice_in_dim(array, column_about, local_width, 2)

    onehot = (domain[..., None] == jnp.arange(3, dtype=jnp.int32)).astype(f32)
    own_counts = jnp.sum(onehot, axis=(0, 1))
    high = jnp.floor(own_counts / 128.0)
    digits = jnp.concatenate([high, own_counts - 128.0 * high]).astype(bf16)
    small = [w_beta, conv_weight, head_gain, mixer_gain, mlp_gain, digits]
    packed = padded(pack(small))
    size = width // 4
    if near_four:
        qkv_hop = first_hop(w_qkv)
        qkv_halves = halves_of(qkv_hop, 1)
        qkv = gathered_pieces(w_qkv, 1, qkv_hop, qkv_halves)
        packed = after(packed, qkv_halves)
        gathered = jnp.stack([packed] + [swap(packed, bits) for bits in (1, 2, 3)])
        half = w_out.shape[1] // 2
        pair_own = jnp.stack(
            [w_outgate, jnp.concatenate([w_out[:, :half], w_out[:, half:]], 0)]
        )
        pair_layout = [(k, 0, size, size) for k in range(4)]
        layout = pair_layout[:3] + [(3, 0, size // 2, size), (3, size // 2, size // 2, size)]
    else:
        gathered = lax.all_gather(packed, "dp")
        qkv = [lax.all_gather(w_qkv, "dp", axis=1, tiled=True)]
        gate_pieces = [lax.all_gather(w_outgate, "dp", axis=0, tiled=True)]
        out_pieces = [lax.all_gather(w_out, "dp", axis=1, tiled=True)]
        layout = pair_layout = [(0, 0, width, width)]
    ranges = [(k * step + start, n) for k, start, n, step in layout]
    g_beta, g_conv, g_head, g_mix, g_mlp, g_digits = unpack(gathered, [a.shape for a in small])
    about_beta = g_beta.reshape(-1, heads)
    full_beta = blocks_about(about_beta, 0)
    full_conv = jnp.moveaxis(blocks_about(g_conv, 0), 0, 3).reshape(3 * KW, inner).astype(f32)
    gain_head = blocks_about(g_head, 0).reshape(1, DK).astype(f32)
    gain_one = blocks_about(g_mix.reshape(1, -1).astype(f32), 1)
    gain_two = g_mlp.reshape(1, -1).astype(f32)
    sums = jnp.sum(g_digits.astype(f32), 0)
    counts = 128.0 * sums[:3] + sums[3:]
    table = group_weight * (domain.shape[0] * domain.shape[1] * dp) / counts
    factor = jnp.sum(onehot * table, -1)[..., None]

    def flat(array):
        return array.reshape(array.shape[:-3] + (count_rows, array.shape[-1]))

    rows = lax.all_gather(tokens, "mp", axis=2, tiled=True)
    if near_four:
        gate_pieces = out_pieces = [lax.all_gather(after(pair_own, packed), "dp")]
    turn_one = turn.reshape(1)
    per_token = (seqs, block)
    square = (seqs, heads, DK, DK)
    hidden_one, proj, tail, logits, scale_one = call(
        partial(project_kernel, layout),
        [(rows, 0), (gain_one, None), (jnp.pad(full_beta, ((0, 0), (0, 128 - heads))), None)]
        + [(a, None) for a in qkv],
        [
            (shape_of(per_token + (width,), bf16), 0),
            (shape_of((3,) + per_token + (inner,), bf16), 1),
            (shape_of((3, seqs, HALO, inner), bf16), 1),
            (shape_of(per_token + (heads,), f32), 0),
            (shape_of(per_token + (1,), f32), 0),
        ],
        seqs,
        scalar=turn_one,
        scratch=[pltpu.VMEM((block, width), bf16)],
    )
    before = shifted(tail, "dp", 1)
    inverse, wu, qo, to = call(
        pre_kernel,
        [(proj, None), (before, None), (full_conv, None), (logits, None)],
        [
            (shape_of((seqs, heads, block, block), f32), None),
            (shape_of((seqs, heads, block, 2 * DK), f32), None),
            (shape_of((seqs, heads, block, 2 * DK), f32), None),
            (shape_of((seqs, heads, DK, 2 * DK), bf16), None),
        ],
        1,
    )
    near = [shifted(to, "dp", c) for c in range(1, dp)]
    rows_about, cotangent = call(
        partial(prepare_kernel, layout),
        [(rows, 0), (out_grad, 0), (factor, 0)],
        [(shape_of(per_token + (width,), bf16), 0)] * 2,
        seqs,
        scalar=turn_one,
    )
    turned = jnp.swapaxes(w_gateup, 1, 2)
    feed_own = [turned, w_down]
    mixer_part, normed, rule, state, gates = call(
        partial(mix_kernel, pair_layout, len(near), len(out_pieces)),
        [(a, 0) for a in near]
        + [(qo, 0), (hidden_one, 0), (gain_head, None)]
        + [(a, None) for a in gate_pieces + out_pieces],
        [
            (shape_of(per_token + (width,), bf16), 0),
            (shape_of(per_token + (inner,), bf16), 0),
            (shape_of(per_token + (inner,), f32), 0),
            (shape_of(square, f32), 0),
            (shape_of(per_token + (inner,), f32), 0),
        ],
        seqs,
        scalar=turn_one,
    )
    total = lax.psum(mixer_part, "mp")
    nexts = [shifted(to[..., :DK], "dp", -c) for c in range(1, dp - 1)]
    if near_four:
        gateup, down = (gathered_pieces(a, a.ndim - 1) for a in after(copies(feed_own), mixer_part, nexts))
    else:
        gateup, down = (
            [lax.all_gather(a, "dp", axis=a.ndim - 1, tiled=True)] for a in feed_own
        )
    units = w_down.shape[0]
    two_part, hidden_two, hidden_mlp, grad_pair = call(
        partial(feed_kernel, layout),
        [(rows_about, 0), (total, 0), (cotangent, 0), (gain_two, None)]
        + [(a, None) for a in gateup + down],
        [
            (shape_of(per_token + (width,), bf16), 0),
            (shape_of(per_token + (width,), bf16), 0),
            (shape_of(per_token + (units,), bf16), 0),
            (shape_of((2,) + per_token + (units,), bf16), 1),
        ],
        seqs,
    )
    grad_two = lax.psum(two_part, "mp")

    def feed_gradients(some, *others):
        outs = [(shape_of((m, units, n), bf16), None) for _, n in some for m in (2, 1)]
        base, span = some[0][0], sum(n for _, n in some)
        aligned = base % span == 0
        at = base // span if aligned else 0
        cols = pl.BlockSpec((count_rows, span if aligned else width), lambda s: (0, at))
        made = pl.pallas_call(
            partial(feed_gradient_kernel, base if aligned else 0, some),
            cost_estimate=FREE,
            grid=(1,),
            in_specs=[
                cols,
                cols,
                pl.BlockSpec((2, count_rows, units), lambda s: (0, 0, 0)),
                pl.BlockSpec((count_rows, units), lambda s: (0, 0)),
            ]
            + [pl.BlockSpec(memory_space=pl.ANY)] * len(others),
            out_specs=[pl.BlockSpec(o.shape, lambda s: (0, 0, 0)) for o, _ in outs],
            out_shape=[o for o, _ in outs],
            compiler_params=pltpu.CompilerParams(vmem_limit_bytes=VMEM),
        )(flat(hidden_two), flat(cotangent), flat(grad_pair), flat(hidden_mlp), *others)
        return made[::2], made[1::2]

    if near_four:
        feed_far = feed_gradients(ranges[3:])
        feed_in = [far_hop(*far) for far in feed_far]
        near_gateup, near_down = feed_gradients(ranges[:3], feed_far[0][0])
        first_made = [(near_gateup[0], "any")]
    else:
        [grad_gateup], [grad_down] = feed_gradients(ranges)
        held = first_made = []
    [down_part] = call(
        partial(down_kernel, layout),
        [(hidden_mlp, 0)] + [(a, None) for a in down] + first_made,
        [(shape_of(per_token + (width,), bf16), 0)],
        seqs,
        scalar=turn_one,
    )
    if near_four:
        gateup_added = near_sums(near_gateup, feed_in[0], *feed_in[1], down_part)
        down_added = near_sums(near_down, feed_in[1])
        gateup_sums, down_sums = near_hop(gateup_added), near_hop(down_added)
        down_part = after(down_part, gateup_added[1])
        held = [(a, "any") for a in gateup_sums[1:]]
    mlp_share = lax.psum_scatter(down_part, "mp", scatter_dimension=2, tiled=True)
    grad_mix, middle_own, mlpgain, drule, dgate, dgain, direct = call(
        partial(middle_back_kernel, pair_layout, len(out_pieces)),
        [
            (grad_two, 0),
            (cotangent, 0),
            (rows_about, 0),
            (total, 0),
            (gain_two, None),
            (rule, 0),
            (gates, 0),
            (gain_head, None),
            (qo, 0),
        ]
        + [(a, None) for a in out_pieces]
        + [(down_part, "any")]
        + held,
        [
            (shape_of(per_token + (width,), bf16), 0),
            (shape_of(per_token + (local_width,), f32), 0),
            (shape_of((seqs, 1, width), f32), 0),
            (shape_of(per_token + (inner,), f32), 0),
            (shape_of(per_token + (inner,), bf16), 0),
            (shape_of((seqs, 1, DK), f32), 0),
            (shape_of(square, bf16), 0),
        ],
        seqs,
        scalar=jnp.stack([turn, column_about]),
        scratch=[pltpu.VMEM((block, width), f32)],
    )
    directs = [shifted(direct, "dp", -c) for c in range(1, dp)]
    if near_four:
        pair_grads = call(
            partial(pair_gradient_kernel, [(k * size, size) for k in range(4)]),
            [(flat(a), None) for a in (hidden_one, dgate, normed, grad_mix)],
            [(shape_of((2, size, inner), bf16), None)] * 4,
            1,
        )
        down_total = sum_last(down_sums, pair_grads[3])
        held = [(a, "any") for a in (pair_grads[3], down_total)]
    else:
        grad_outgate = jnp.einsum(
            "td,tc->dc", flat(hidden_one), flat(dgate), preferred_element_type=f32
        )
        grad_outproj = jnp.einsum(
            "tc,td->cd", flat(normed), flat(grad_mix), preferred_element_type=f32
        )
        held = []
    dproj, last, first, dtaps, dlogits = call(
        partial(back_kernel, len(directs)),
        [
            (proj, 1),
            (before, 1),
            (full_conv, None),
            (logits, 0),
            (inverse, 0),
            (wu, 0),
            (state, 0),
            (drule, 0),
        ]
        + [(a, 0) for a in directs + nexts]
        + held,
        [
            (shape_of((3,) + per_token + (inner,), bf16), 1),
            (shape_of((3, seqs, PAD, inner), f32), 1),
            (shape_of((3, seqs, PAD, inner), f32), 1),
            (shape_of((seqs, 3 * KW, inner), f32), 0),
            (shape_of(per_token + (heads,), bf16), 0),
        ],
        seqs,
    )
    late = []
    if near_four:
        gateup_total = sum_last(gateup_sums, dlogits)
        late = [(gateup_total, "any")]
    later = shifted(first, "dp", -1)
    dproj = lax.dynamic_update_slice(dproj, (last + later).astype(bf16), (0, 0, block - PAD, 0))
    one_low, row_part, gain_part = call(
        partial(first_back_kernel, layout, pair_layout, len(gate_pieces)),
        [
            (flat(dproj), None),
            (flat(dgate), None),
            (flat(dlogits), None),
            (flat(proj), None),
            (flat(gates), None),
            (flat(logits), None),
            (about_beta.T.astype(f32), None),
            (flat(rows_about), None),
            (flat(scale_one), None),
        ]
        + [(a, None) for a in qkv + gate_pieces]
        + late,
        [
            (shape_of((count_rows, width), bf16), None),
            (shape_of((1, count_rows), f32), None),
            (shape_of((1, width), f32), None),
        ],
        1,
        scalar=turn_one,
    )
    one_share = lax.psum_scatter(
        one_low.reshape(seqs, block, width), "mp", scatter_dimension=2, tiled=True
    ).astype(f32)
    made = call(
        partial(qkv_gradient_kernel, ranges),
        [(flat(hidden_one), None), (flat(dproj), None), (flat(dlogits), None), (row_part, "any")],
        [(shape_of((3, n, inner), bf16), None) for _, n in ranges]
        + [(shape_of((heads, width), f32), None)],
        1,
    )

    def pieces(array, axis, about):
        shape = array.shape
        cut = array.reshape(shape[:axis] + (dp, shape[axis] // dp) + shape[axis + 1 :])
        cut = jnp.moveaxis(cut, axis, 0).reshape(dp, -1)
        return blocks_about(cut, 0) if about else cut

    smalls = jnp.concatenate(
        [
            pieces(jnp.sum(dtaps, 0).reshape(3, KW, heads, DK), 3, True),
            pieces(made[-1].T, 0, False),
            pieces(gain_part[0], 0, False),
            pieces(jnp.sum(mlpgain, (0, 1)), 0, False),
            pieces(jnp.sum(dgain, (0, 1)), 0, True),
        ],
        1,
    )
    small_shapes = [a.shape for a in (conv_weight, w_beta, mixer_gain, mlp_gain, head_gain)]
    if near_four:
        own_qkv, *near_qkv = near_sums(made[:3], far_hop(made[3], made[4]))
        smalls = jnp.pad(smalls, ((0, 0), (0, -smalls.shape[1] % 1024))).reshape(dp, -1, 128)
        sent = smalls.astype(bf16)
        got = [swap(sent[bits], bits) for bits in (1, 2, 3)]
        first_mix = (conv_weight.size + w_beta.size) // 128
        last_mix = first_mix + mixer_gain.size // 128
        lines = count_rows // 128 + last_mix - first_mix
        mine, rest = call(
            partial(
                add_small_kernel,
                slice(first_mix, last_mix),
                last_mix + mlp_gain.size // 128,
            ),
            [(a, None) for a in [smalls[0]] + got + [row_part]],
            [
                (shape_of(smalls.shape[1:], f32), None),
                (shape_of((lines + 8 - lines % 8, 128), f32), None),
            ],
            1,
        )
        pair_far = after(jnp.split(pair_grads[3], 2, 1), made[0])
        pair_near = near_sums(pair_grads[:3], far_hop(*pair_far))[1:]
        mine = mine.reshape(-1)
        sum_qkv = sum_last(near_hop((own_qkv, *near_qkv)))
        sum_gateup = jnp.swapaxes(gateup_total, 1, 2)
        sum_down = down_total[0]
        pair_sums = near_hop((pair_grads[0], *pair_near))
    else:
        gathered = lax.all_gather(smalls.astype(bf16), "dp")
        mine = jnp.sum(
            lax.dynamic_index_in_dim(gathered, place, 1, keepdims=False).astype(f32), 0
        )

        def scattered(array, axis):
            return lax.psum_scatter(array, "dp", scatter_dimension=axis, tiled=True).astype(f32)

        sum_qkv = scattered(made[0], 1)
        sum_outgate = scattered(grad_outgate.astype(bf16), 0)
        sum_out = scattered(grad_outproj.astype(bf16), 1)
        sum_gateup = jnp.swapaxes(scattered(grad_gateup, 2), 1, 2)
        sum_down = scattered(grad_down[0], 1)
    sum_conv, sum_beta, sum_mix, sum_mlp, sum_head = unpack(mine, small_shapes)
    if near_four:
        bit = 1
        while bit < lax.axis_size("mp"):
            devices = lax.axis_size("mp")
            rest = rest + lax.ppermute(rest, "mp", [(i, i ^ bit) for i in range(devices)])
            bit *= 2
        rest_sum = rest.reshape(-1)
    else:
        rest_sum = lax.psum(pack([row_part, sum_mix, sum_head]), "mp")
    row_sum, sum_mix, sum_head = unpack(rest_sum, [(count_rows,), sum_mix.shape, sum_head.shape])

    own_tokens = tokens.astype(f32)
    mixed_out = (own_tokens + own(total).astype(f32) + mlp_share.astype(f32)).astype(bf16)
    row_mean = (row_sum / width).reshape(seqs, block, 1)
    gain_own = lax.dynamic_slice_in_dim(gain_one, column, local_width, 1)
    tokens_grad = middle_own + scale_one * (
        one_share * gain_own - own_tokens * scale_one * row_mean
    )
    tokens_grad = tokens_grad.astype(bf16)
    if near_four:
        done = [(a, "any") for a in (sum_qkv, tokens_grad, mixed_out)]
        sum_outgate, sum_out = call(
            add_pair_kernel,
            [(a, None) for a in pair_sums] + done,
            [(shape_of(w_outgate.shape, f32), None), (shape_of(w_out.shape, f32), None)],
            1,
        )
    return (
        mixed_out,
        tokens_grad,
        sum_qkv,
        sum_conv,
        sum_beta,
        sum_outgate,
        sum_head,
        sum_out,
        sum_mix,
        sum_mlp,
        sum_gateup,
        sum_down,
    )


def solution(mesh):
    return jax.shard_map(
        body,
        mesh=mesh,
        in_specs=(
            P(None, "dp", "mp"),
            P(None, "dp", None),
            P(None, "dp"),
            P(),
            P(None, "dp", "mp"),
            P(None, None, "mp", "dp"),
            P("dp", "mp"),
            P("dp", "mp"),
            P("dp"),
            P("mp", "dp"),
            P("dp"),
            P("dp"),
            P(None, "dp", "mp"),
            P("mp", "dp"),
        ),
        out_specs=(
            P(None, "dp", "mp"),
            P(None, "dp", "mp"),
            P(None, "dp", "mp"),
            P(None, None, "mp", "dp"),
            P("dp", "mp"),
            P("dp", "mp"),
            P("dp"),
            P("mp", "dp"),
            P("dp"),
            P("dp"),
            P(None, "dp", "mp"),
            P("mp", "dp"),
        ),
        check_vma=False,
    )
```

```python
from functools import partial

import jax
import jax.numpy as jnp
from jax import lax
from jax.experimental import pallas as pl
from jax.experimental.pallas import tpu as pltpu
from jax.sharding import PartitionSpec as P

DK = 128
KW = 4
PAD = 8
HALO = 16
ROWS = 16
VMEM = 58 * 2**20
FREE = pl.CostEstimate(flops=0, transcendentals=0, bytes_accessed=0)

eps_norm = 1e-06
eps_unit = 1e-06

f32 = jnp.float32
bf16 = jnp.bfloat16


def split(v):
    if v.dtype == bf16:
        return v, None
    high = v.astype(bf16)
    return high, (v - high.astype(f32)).astype(bf16)


def mm(a, b, ca=1, cb=0, passes=3):
    def one(x, y):
        return lax.dot_general(x, y, (((ca,), (cb,)), ((), ())), preferred_element_type=f32)

    if passes == 1:
        return one(a.astype(bf16), b.astype(bf16))
    (ah, al), (bh, bl) = split(a), split(b)
    out = one(ah, bh)
    if bl is not None:
        out = out + one(ah, bl)
    if al is not None:
        out = out + one(al, bh)
    return out


def places(rows, cols):
    return (
        lax.broadcasted_iota(jnp.int32, (rows, cols), 0),
        lax.broadcasted_iota(jnp.int32, (rows, cols), 1),
    )


def unit_lower_inverses(blocks):
    size = blocks[0].shape[0]
    if size > 128:
        half = size // 2
        parts = unit_lower_inverses(
            [a[:half, :half] for a in blocks] + [a[half:, half:] for a in blocks]
        )
        firsts, seconds = parts[: len(blocks)], parts[len(blocks) :]
        inner = [mm(a[half:, :half], x) for a, x in zip(blocks, firsts)]
        lower = [-mm(x, y) for x, y in zip(seconds, inner)]
        zero = jnp.zeros((half, half), f32)
        return [
            jnp.concatenate(
                [jnp.concatenate([x, zero], 1), jnp.concatenate([y, z], 1)], 0
            )
            for x, y, z in zip(firsts, lower, seconds)
        ]
    rows, cols = places(size, size)
    eye = (rows == cols).astype(f32)
    level = 0
    inverses = None
    while (1 << level) < size:
        mask = (
            ((rows >> (level + 1)) == (cols >> (level + 1)))
            & (((rows >> level) & 1) == 1)
            & (((cols >> level) & 1) == 0)
        ).astype(f32)
        lows = [a * mask for a in blocks]
        if level == 0:
            inverses = [eye - low for low in lows]
        else:
            inner = [mm(low, x) for low, x in zip(lows, inverses)]
            inverses = [x - mm(x, y) for x, y in zip(inverses, inner)]
        level += 1
    return inverses


def head_slice(h):
    return slice(h * DK, (h + 1) * DK)


def convolve(proj_ref, before_ref, taps, i, h):
    own = proj_ref[i, 0, :, head_slice(h)].astype(f32)
    length = own.shape[0]
    ext = jnp.concatenate([before_ref[i, 0, :, head_slice(h)].astype(f32), own], 0)
    shifts = [ext[HALO - KW + 1 + j : HALO - KW + 1 + j + length] for j in range(KW)]
    out = None
    for j in range(KW):
        tap = taps[i * KW + j : i * KW + j + 1, head_slice(h)]
        out = tap * shifts[j] if out is None else out + tap * shifts[j]
    sig = jax.nn.sigmoid(out)
    return shifts, out, sig, out * sig


def unit(acts):
    inv = lax.rsqrt(jnp.sum(acts * acts, -1, keepdims=True) + eps_unit)
    return acts * inv, inv


def rule_inputs(proj_ref, before_ref, taps, h):
    parts = [convolve(proj_ref, before_ref, taps, i, h) for i in range(3)]
    q, q_inv = unit(parts[0][3])
    k, k_inv = unit(parts[1][3])
    return parts, (q, q_inv), (k, k_inv), parts[2][3]


def norm_factor(values):
    return lax.rsqrt(jnp.mean(values * values, -1, keepdims=True) + eps_norm)


def project_kernel(layout, *refs):
    place_ref, rows_ref, gain_ref, beta_ref = refs[:4]
    pieces = refs[4 : 4 + len(layout)]
    hidden_ref, proj_ref, tail_ref, logit_ref, scale_ref, keep_ref = refs[4 + len(layout) :]
    rows = rows_ref[0].astype(f32)
    scale = norm_factor(rows)
    scale_ref[0] = scale
    keep_ref[...] = (rows * scale * gain_ref[...]).astype(bf16)
    logits = mm(keep_ref[...], beta_ref[...])
    logit_ref[0] = logits[:, : logit_ref.shape[2]]
    sums = [None] * 3
    for (k, start, size, block), piece in zip(layout, pieces):
        at = pl.multiple_of((place_ref[0] ^ k) * block + start, 128)
        part = keep_ref[:, pl.ds(at, size)]
        hidden_ref[0, :, k * block + start : k * block + start + size] = part
        for i in range(3):
            term = mm(part, piece[i])
            sums[i] = term if sums[i] is None else sums[i] + term
    for i in range(3):
        low = sums[i].astype(bf16)
        proj_ref[i, 0] = low
        tail_ref[i, 0] = low[low.shape[0] - HALO :]


def pre_kernel(proj_ref, before_ref, taps_ref, logit_ref, x_ref, wu_ref, qo_ref, to_ref, t_ref, o_ref):
    seqs, heads = to_ref.shape[:2]
    taps = taps_ref[...]
    length = proj_ref.shape[2]
    r, c = places(length, length)
    strict = (r > c).astype(f32)
    full = (r >= c).astype(f32)
    saved, blocks = [], []
    for s in range(seqs):
        betas = jax.nn.sigmoid(logit_ref[s])
        rows, before = proj_ref.at[:, s : s + 1], before_ref.at[:, s : s + 1]
        for h in range(heads):
            _, (q, _), (k, _), v = rule_inputs(rows, before, taps, h)
            q, k, v = q.astype(bf16), k.astype(bf16), v.astype(bf16)
            beta = betas[:, h : h + 1]
            blocks.append(beta * mm(k, k, 1, 1) * strict)
            saved.append((s, h, q, k, v, beta))
    inverses = unit_lower_inverses(blocks)
    r, c = places(DK, DK)
    eye = (r == c).astype(f32)
    for (s, h, q, k, v, beta), x in zip(saved, inverses):
        x_ref[s, h] = x
        kv = jnp.concatenate([k.astype(f32), v.astype(f32)], 1) * beta
        wu = mm(x, kv)
        wu_ref[s, h] = wu
        scores = mm(q, k, 1, 1) * full
        pwu = mm(scores, wu)
        qo_ref[s, h, :, :DK] = q.astype(f32) - pwu[:, :DK]
        qo_ref[s, h, :, DK:] = pwu[:, DK:]
        kwu = mm(k, wu, 0, 0)
        transfer, offset = (eye - kwu[:, :DK]).astype(bf16), kwu[:, DK:].astype(bf16)
        to_ref[s, h, :, :DK] = transfer
        to_ref[s, h, :, DK:] = offset
        t_ref[s, h] = transfer
        o_ref[s, h] = offset


def by_piece(place_ref, refs):
    if len(refs) > 1 or len(refs[0].shape) < 4:
        return refs
    return [refs[0].at[place_ref[0] ^ k] for k in range(4)]


def gate_part(ref):
    return ref.at[0] if len(ref.shape) == 3 else ref


def out_columns(layout, refs):
    for (k, start, size, block), ref in zip(layout, refs):
        at, half = k * block + start, size // 2
        if len(ref.shape) == 2:
            yield at, size, ref
            continue
        inner = ref.shape[1] // 2
        yield at, half, ref.at[1, :inner]
        yield at + half, half, ref.at[1, inner:]


def mix_kernel(layout, count, pieces, place_ref, *refs):
    near, rest = refs[:count], refs[count:]
    qo_ref, hidden_ref, gain_ref = rest[:3]
    gate_pieces = by_piece(place_ref, rest[3 : 3 + pieces])
    outs = by_piece(place_ref, rest[3 + pieces : 3 + 2 * pieces])
    part_ref, normed_ref, rule_ref, state_ref, gate_ref = rest[-5:]
    gates = None
    for (k, start, size, block), ref in zip(layout, gate_pieces):
        at = k * block + start
        term = mm(hidden_ref[0, :, at : at + size], gate_part(ref)[...])
        gates = term if gates is None else gates + term
    gate_ref[0] = gates
    heads = state_ref.shape[1]
    for h in range(heads):
        state = near[-1][0, h].astype(f32)
        for ref in reversed(near[:-1]):
            state = mm(ref[0, h, :, :DK], state) + ref[0, h, :, DK:].astype(f32)
        state_ref[0, h] = state
        qo = qo_ref[0, h]
        out = (mm(qo[:, :DK], state) + qo[:, DK:]) * DK ** (-0.5)
        rule_ref[0, :, head_slice(h)] = out
        gate = gate_ref[0, :, head_slice(h)]
        normed = out * norm_factor(out) * gain_ref[...] * (gate * jax.nn.sigmoid(gate))
        normed_ref[0, :, head_slice(h)] = normed.astype(bf16)
    for at, size, ref in out_columns(layout, outs):
        part_ref[0, :, at : at + size] = mm(normed_ref[0], ref[...]).astype(bf16)


def prepare_kernel(layout, place_ref, rows_ref, grad_ref, factor_ref, about_ref, cot_ref):
    for k, start, size, block in layout:
        at = pl.multiple_of((place_ref[0] ^ k) * block + start, 128)
        to = slice(k * block + start, k * block + start + size)
        about_ref[0, :, to] = rows_ref[0, :, pl.ds(at, size)]
        grad = grad_ref[0, :, pl.ds(at, size)].astype(f32) * factor_ref[0]
        cot_ref[0, :, to] = grad.astype(bf16)


def down_kernel(layout, place_ref, mlp_ref, *refs):
    part_ref = refs[-1]
    for (k, start, size, block), ref in zip(layout, refs):
        at = pl.multiple_of((place_ref[0] ^ k) * block + start, 128)
        part_ref[0, :, pl.ds(at, size)] = mm(mlp_ref[0], ref[...]).astype(bf16)


def feed_gradient_kernel(base, ranges, hidden_ref, cot_ref, pair_ref, mlp_ref, *outs):
    outs = outs[-2 * len(ranges) :]
    for n, (start, size) in enumerate(ranges):
        start = start - base
        hidden = hidden_ref[:, start : start + size]
        outs[2 * n][0] = mm(pair_ref[0], hidden, 0, 0).astype(bf16)
        outs[2 * n][1] = mm(pair_ref[1], hidden, 0, 0).astype(bf16)
        outs[2 * n + 1][0] = mm(mlp_ref[...], cot_ref[:, start : start + size], 0, 0).astype(bf16)


def qkv_gradient_kernel(ranges, hidden_ref, dproj_ref, dlogit_ref, *outs):
    outs = outs[-len(ranges) - 1 :]
    for (start, size), out in zip(ranges, outs[:-1]):
        hidden = hidden_ref[:, start : start + size]
        for i in range(3):
            out[i] = mm(hidden, dproj_ref[i], 0, 0).astype(bf16)
    outs[-1][...] = mm(dlogit_ref[...], hidden_ref[...], 0, 0)


def pair_gradient_kernel(ranges, hidden_ref, dgate_ref, normed_ref, mix_ref, *outs):
    inner = normed_ref.shape[1]
    for (start, size), out in zip(ranges, outs):
        out[0] = mm(hidden_ref[:, start : start + size], dgate_ref[...], 0, 0).astype(bf16)
        for n in range(2):
            at = start + n * size // 2
            mix = mix_ref[:, at : at + size // 2]
            out[1, n * inner : (n + 1) * inner] = mm(normed_ref[...], mix, 0, 0).astype(bf16)


def add_halves_kernel(*refs):
    one_ref, two_ref, low_ref, high_ref, one_out, two_out = refs[:4] + refs[-2:]
    one_out[...] = (one_ref[...].astype(f32) + high_ref[...].astype(f32)).astype(bf16)
    two_out[...] = (two_ref[...].astype(f32) + low_ref[...].astype(f32)).astype(bf16)


def add_small_kernel(mix_rows, head_row, *refs):
    *parts, row_ref, out_ref, rest_ref = refs
    total = sum(ref[...].astype(f32) for ref in parts)
    out_ref[...] = total
    lines = [row_ref[:, n * 128 : (n + 1) * 128] for n in range(row_ref.shape[1] // 128)]
    lines += [total[mix_rows], total[head_row : head_row + 1]]
    used = len(lines) - 2 + mix_rows.stop - mix_rows.start + 1
    lines.append(jnp.zeros((rest_ref.shape[0] - used, 128), f32))
    rest_ref[...] = jnp.concatenate(lines, 0)


def add_last_kernel(*refs):
    own_ref, one_ref, two_ref, out_ref = refs[:3] + refs[-1:]
    out_ref[...] = own_ref[...].astype(f32) + one_ref[...].astype(f32) + two_ref[...].astype(f32)


def feed_kernel(layout, *refs):
    rows_ref, total_ref, cot_ref, gain_ref = refs[:4]
    count = len(layout)
    gateups, downs = (refs[4 + n * count : 4 + (n + 1) * count] for n in range(2))
    two_ref, hidden_ref, mlp_ref, pair_ref = refs[-4:]
    middle = rows_ref[0].astype(f32) + total_ref[0].astype(f32)
    hidden_ref[0] = (middle * norm_factor(middle) * gain_ref[...]).astype(bf16)
    gate, up, grad = None, None, None
    for (k, start, size, block), w_gateup, w_down in zip(layout, gateups, downs):
        lanes = slice(k * block + start, k * block + start + size)
        hidden = hidden_ref[0, :, lanes]
        terms = (
            mm(hidden, w_gateup[0], 1, 1),
            mm(hidden, w_gateup[1], 1, 1),
            mm(cot_ref[0, :, lanes], w_down[...], 1, 1),
        )
        if gate is None:
            gate, up, grad = terms
        else:
            gate, up, grad = gate + terms[0], up + terms[1], grad + terms[2]
    sig = jax.nn.sigmoid(gate)
    silu = gate * sig
    mlp_ref[0] = (silu * up).astype(bf16)
    first = (grad * up * (sig + silu * (1.0 - sig))).astype(bf16)
    second = (grad * silu).astype(bf16)
    pair_ref[0, 0] = first
    pair_ref[1, 0] = second
    for (k, start, size, block), w_gateup in zip(layout, gateups):
        lanes = slice(k * block + start, k * block + start + size)
        two = mm(first, w_gateup[0]) + mm(second, w_gateup[1])
        two_ref[0, :, lanes] = two.astype(bf16)


def middle_back_kernel(layout, pieces, at_ref, *refs):
    two_ref, cot_ref, rows_ref, total_ref, gain_ref, rule_ref, gate_ref, head_gain_ref, qo_ref = refs[:9]
    outs = by_piece(at_ref, refs[9 : 9 + pieces])
    mix_ref, own_ref, mlpgain_ref, drule_ref, dgate_ref, dgain_ref, direct_ref, keep_ref = refs[-8:]
    full = rows_ref.shape[2]
    gain_sum = None
    for start in range(0, rows_ref.shape[1], ROWS):
        at = slice(start, start + ROWS)
        middle = rows_ref[0, at].astype(f32) + total_ref[0, at].astype(f32)
        two = two_ref[0, at].astype(f32)
        factor = norm_factor(middle)
        normal = middle * factor
        term = jnp.sum((two * normal).reshape(ROWS // 8, 8, full), 0)
        gain_sum = term if gain_sum is None else gain_sum + term
        scaled = two * gain_ref[...]
        mean = jnp.mean(scaled * normal, -1, keepdims=True)
        keep = cot_ref[0, at].astype(f32) + factor * (scaled - normal * mean)
        keep_ref[at] = keep
        mix_ref[0, at] = keep.astype(bf16)
    mlpgain_ref[0] = jnp.sum(gain_sum, 0, keepdims=True)
    width = own_ref.shape[2]
    own_ref[0] = keep_ref[:, pl.ds(pl.multiple_of(at_ref[1], 128), width)]
    grads = None
    for at, size, ref in out_columns(layout, outs):
        term = mm(mix_ref[0, :, at : at + size], ref[...], 1, 1)
        grads = term if grads is None else grads + term
    total = jnp.zeros((1, DK), f32)
    for h in range(direct_ref.shape[1]):
        grad = grads[:, head_slice(h)]
        out = rule_ref[0, :, head_slice(h)]
        gate = gate_ref[0, :, head_slice(h)]
        inv = norm_factor(out)
        n = out * inv
        sig = jax.nn.sigmoid(gate)
        silu = gate * sig
        gg = grad * head_gain_ref[...]
        dn = gg * silu
        drule = inv * (dn - n * jnp.mean(dn * n, -1, keepdims=True))
        drule_ref[0, :, head_slice(h)] = drule
        dgate = gg * n * sig * (1.0 + gate * (1.0 - sig))
        dgate_ref[0, :, head_slice(h)] = dgate.astype(bf16)
        total = total + jnp.sum(grad * n * silu, 0, keepdims=True)
        direct = mm(qo_ref[0, h, :, :DK], drule, 0, 0) * DK ** (-0.5)
        direct_ref[0, h] = direct.astype(bf16)
    dgain_ref[0] = total


def first_back_kernel(layout, pair_layout, count, place_ref, *refs):
    dproj_ref, dgate_ref, dlogit_ref, proj_ref, gate_ref, logit_ref, beta_ref, rows_ref, scale_ref = refs[:9]
    pieces = refs[9 : 9 + len(layout)]
    pairs = by_piece(place_ref, refs[9 + len(layout) : 9 + len(layout) + count])
    one_ref, rowsum_ref, gainsum_ref = refs[-3:]
    gates = {}
    for (k, start, size, block), ref in zip(pair_layout, pairs):
        gates[k] = ref
    for (k, start, size, block), piece in zip(layout, pieces):
        lanes = slice(k * block + start, k * block + start + size)
        grad = mm(dgate_ref[...], gate_part(gates[k])[start : start + size], 1, 1)
        for i in range(3):
            grad = grad + mm(dproj_ref[i], piece[i], 1, 1)
        for h in range(beta_ref.shape[0]):
            grad = grad + dlogit_ref[:, h : h + 1].astype(f32) * beta_ref[h : h + 1, lanes]
        at = pl.multiple_of((place_ref[0] ^ k) * block + start, 128)
        one_ref[:, pl.ds(at, size)] = grad.astype(bf16)
        gainsum_ref[:, lanes] = jnp.sum(
            grad * (rows_ref[:, lanes].astype(f32) * scale_ref[...]), 0, keepdims=True
        )
    total = dgate_ref[...].astype(f32) * gate_ref[...]
    for i in range(3):
        total = total + dproj_ref[i].astype(f32) * proj_ref[i].astype(f32)
    lane = lax.broadcasted_iota(jnp.int32, total.shape, 1) == 0
    logits = jnp.sum(dlogit_ref[...].astype(f32) * logit_ref[...], -1, keepdims=True)
    logits_sum = jnp.where(lane, logits, 0.0)
    total = total + logits_sum
    ones = jnp.ones((8, total.shape[1]), f32)
    rowsum_ref[...] = mm(ones, total, 1, 1)[:1]


def back_kernel(count, *refs):
    (
        proj_ref,
        before_ref,
        taps_ref,
        logit_ref,
        x_ref,
        wu_ref,
        state_ref,
        drule_ref,
    ) = refs[:8]
    dproj_ref, last_ref, first_ref, dtaps_ref, dlogit_ref = refs[-5:]
    others = refs[8 : 8 + 2 * count - 1]
    directs, nexts = others[:count], others[count:]
    heads = state_ref.shape[1]
    taps = taps_ref[...]
    length = proj_ref.shape[2]
    betas = jax.nn.sigmoid(logit_ref[0])
    r, c = places(length, length)
    strict = (r > c).astype(f32)
    full = (r >= c).astype(f32)
    zeros = jnp.zeros((PAD, DK), f32)
    for h in range(heads):
        parts, (qu, q_inv), (ku, k_inv), vu = rule_inputs(proj_ref, before_ref, taps, h)
        q, k, v = qu.astype(bf16), ku.astype(bf16), vu.astype(bf16)
        beta = betas[:, h : h + 1]
        leave = jnp.zeros((DK, DK), f32)
        for j in reversed(range(count)):
            here = directs[j][0, h].astype(f32)
            leave = here if j == count - 1 else mm(nexts[j][0, h], leave, 0, 0) + here
        state = state_ref[0, h]
        wu = wu_ref[0, h]
        u = wu[:, DK:] - mm(wu[:, :DK], state)
        resid = v.astype(f32) - mm(k, state)
        dout = drule_ref[0, :, head_slice(h)] * DK ** (-0.5)
        gram = mm(k, k, 1, 1)
        scores = mm(q, k, 1, 1) * full
        du = mm(scores, dout, 0, 0) + mm(k, leave)
        y = mm(x_ref[0, h], du, 0, 0)
        by = beta * y
        da = -(mm(y, u, 1, 1, 1) * strict)
        dbeta = jnp.sum(y * resid, -1, keepdims=True) + jnp.sum(da * gram, -1, keepdims=True)
        dgram = beta * da
        dscores = mm(dout, u, 1, 1, 1) * full
        dq = mm(dout, state, 1, 1, 1) + mm(dscores, k, 1, 0, 1)
        dk = (
            mm(dgram, k, 1, 0, 1)
            + mm(dgram, k, 0, 0, 1)
            + mm(dscores, q, 0, 0, 1)
            + mm(u, leave, 1, 1, 1)
            - mm(by, state, 1, 1, 1)
        )
        dlogit_ref[0, :, h : h + 1] = (dbeta * beta * (1.0 - beta)).astype(bf16)
        dq = (dq - qu * jnp.sum(qu * dq, -1, keepdims=True)) * q_inv
        dk = (dk - ku * jnp.sum(ku * dk, -1, keepdims=True)) * k_inv
        for i, dact in enumerate((dq, dk, by)):
            shifts, out, sig, _ = parts[i]
            dconv = dact * sig * (1.0 + out * (1.0 - sig))
            ext = jnp.concatenate([zeros, dconv, zeros], 0)
            total = None
            for j in range(KW):
                at = i * KW + j
                dtaps_ref[0, at : at + 1, head_slice(h)] = jnp.sum(
                    dconv * shifts[j], 0, keepdims=True
                )
                tap = taps[at : at + 1, head_slice(h)]
                term = tap * ext[KW - 1 - j : KW - 1 - j + PAD + length]
                total = term if total is None else total + term
            first_ref[i, 0, :, head_slice(h)] = total[:PAD]
            last_ref[i, 0, :, head_slice(h)] = total[length:]
            dproj_ref[i, 0, :, head_slice(h)] = total[PAD:].astype(bf16)


def call(kernel, ins, outs, steps, scalar=None, scratch=(), limit=VMEM, alias=None):
    def spec(shape, axis):
        if axis == "any":
            return pl.BlockSpec(memory_space=pl.ANY)
        block = tuple(1 if n == axis else size for n, size in enumerate(shape))
        where = lambda s, *_: tuple(s if n == axis else 0 for n in range(len(shape)))
        if axis is None:
            return pl.BlockSpec(block, where, pipeline_mode=pl.Buffered(1))
        return pl.BlockSpec(block, where)

    given = [] if scalar is None else [scalar]
    return pl.pallas_call(
        kernel,
        cost_estimate=FREE,
        grid_spec=pltpu.PrefetchScalarGridSpec(
            num_scalar_prefetch=len(given),
            grid=(steps,),
            in_specs=[spec(a.shape, axis) for a, axis in ins],
            out_specs=[spec(o.shape, axis) for o, axis in outs],
            scratch_shapes=scratch,
        ),
        out_shape=[o for o, _ in outs],
        input_output_aliases=alias or {},
        compiler_params=pltpu.CompilerParams(vmem_limit_bytes=limit),
    )(*given, *[a for a, _ in ins])


def shape_of(shape, dtype):
    return jax.ShapeDtypeStruct(shape, dtype)


def shifted(array, axis, by):
    devices = lax.axis_size(axis)
    pairs = [(i, i + by) for i in range(devices) if 0 <= i + by < devices]
    return lax.ppermute(array, axis, pairs)


def after(values, *others):
    flat, tree = jax.tree.flatten(values)
    others = jax.tree.leaves(others)
    here = pl.BlockSpec(memory_space=pl.ANY)
    out = pl.pallas_call(
        lambda *refs: None,
        cost_estimate=FREE,
        in_specs=[here] * (len(flat) + len(others)),
        out_specs=[here] * len(flat),
        out_shape=[shape_of(a.shape, a.dtype) for a in flat],
        input_output_aliases={n: n for n in range(len(flat))},
    )(*flat, *others)
    return jax.tree.unflatten(tree, out)


def copies(values):
    count = len(values)

    def kernel(*refs):
        for n in range(count):
            refs[n - count][...] = refs[n][...]

    outs = [(shape_of(a.shape, a.dtype), None) for a in values]
    return call(kernel, [(a, None) for a in values], outs, 1)


def swap(array, bits):
    return lax.ppermute(array, "dp", [(i, i ^ bits) for i in range(4)])


def first_hop(own):
    return swap(own, 1), swap(own, 2)


def halves_of(hop, axis):
    low, high = (jnp.split(part, 2, axis) for part in hop)
    return low[0], high[1]


def gathered_pieces(own, axis, hop=None, halves=None):
    hop = hop or first_hop(own)
    low, high = halves or halves_of(hop, axis)
    return [own, *hop, swap(low, 2), swap(high, 1)]


def far_hop(low, high):
    return swap(low, 1), swap(high, 2)


def near_sums(pieces, far_in, *others):
    own, one, two = pieces
    half = far_in[0].shape
    along = 1 if half[1] < one.shape[1] else 2

    def spec(place):
        where = tuple(place if n == along else 0 for n in range(3))
        return pl.BlockSpec(half, lambda s: where)

    first, second = spec(0), spec(1)
    here = pl.BlockSpec(memory_space=pl.ANY)
    one, two = pl.pallas_call(
        add_halves_kernel,
        cost_estimate=FREE,
        grid=(1,),
        in_specs=[second, first, first, first] + [here] * len(others),
        out_specs=[second, first],
        out_shape=[shape_of(a.shape, a.dtype) for a in (one, two)],
        input_output_aliases={0: 0, 1: 1},
        compiler_params=pltpu.CompilerParams(vmem_limit_bytes=VMEM),
    )(one, two, *far_in, *others)
    return own, one, two


def near_hop(pieces):
    own, one, two = pieces
    return own, swap(one, 1), swap(two, 2)


def add_pair_kernel(own_ref, one_ref, two_ref, *refs):
    gate_ref, out_ref = refs[-2:]
    inner = out_ref.shape[0]

    def added(i, rows):
        parts = (ref[i, rows].astype(f32) for ref in (own_ref, one_ref, two_ref))
        return sum(parts)

    gate_ref[...] = added(0, slice(None))
    for n in range(2):
        out_ref[:, n * inner : (n + 1) * inner] = added(1, slice(n * inner, (n + 1) * inner))


def sum_last(parts, *others):
    own = parts[0]
    ins = [(a, 0) for a in parts] + [(a, "any") for a in others]
    [total] = call(add_last_kernel, ins, [(shape_of(own.shape, f32), 0)], own.shape[0])
    return total


def pack(parts):
    return jnp.concatenate([p.reshape(-1) for p in parts])


def unpack(flat, shapes):
    out, at = [], 0
    for shape in shapes:
        size = 1
        for n in shape:
            size *= n
        out.append(flat[..., at : at + size].reshape(flat.shape[:-1] + tuple(shape)))
        at += size
    return out


def padded(flat, multiple=1024):
    return jnp.pad(flat, (0, -flat.shape[0] % multiple))


def body(
    tokens,
    out_grad,
    domain,
    group_weight,
    w_qkv,
    conv_weight,
    w_beta,
    w_outgate,
    head_gain,
    w_out,
    mixer_gain,
    mlp_gain,
    w_gateup,
    w_down,
):
    dp = lax.axis_size("dp")
    place = lax.axis_index("dp")
    seqs, block, local_width = tokens.shape
    count_rows = seqs * block
    heads = conv_weight.shape[2]
    inner = heads * DK
    column = lax.axis_index("mp") * local_width
    near_four = dp == 4

    def blocks_about(array, axis):
        if not near_four:
            return array
        size = array.shape[axis] // 4
        return jnp.concatenate(
            [lax.dynamic_slice_in_dim(array, (place ^ k) * size, size, axis) for k in range(4)],
            axis,
        )

    width = out_grad.shape[2]
    turn = place if near_four else jnp.int32(0)
    column_about = ((column // (width // 4)) ^ turn) * (width // 4) + column % (width // 4)

    def own(array):
        array = array.reshape(seqs, block, width)
        return lax.dynamic_slice_in_dim(array, column_about, local_width, 2)

    onehot = (domain[..., None] == jnp.arange(3, dtype=jnp.int32)).astype(f32)
    own_counts = jnp.sum(onehot, axis=(0, 1))
    high = jnp.floor(own_counts / 128.0)
    digits = jnp.concatenate([high, own_counts - 128.0 * high]).astype(bf16)
    small = [w_beta, conv_weight, head_gain, mixer_gain, mlp_gain, digits]
    packed = padded(pack(small))
    size = width // 4
    if near_four:
        qkv_hop = first_hop(w_qkv)
        qkv_halves = halves_of(qkv_hop, 1)
        qkv = gathered_pieces(w_qkv, 1, qkv_hop, qkv_halves)
        packed = after(packed, qkv_halves)
        gathered = jnp.stack([packed] + [swap(packed, bits) for bits in (1, 2, 3)])
        half = w_out.shape[1] // 2
        pair_own = jnp.stack(
            [w_outgate, jnp.concatenate([w_out[:, :half], w_out[:, half:]], 0)]
        )
        pair_layout = [(k, 0, size, size) for k in range(4)]
        layout = pair_layout[:3] + [(3, 0, size // 2, size), (3, size // 2, size // 2, size)]
    else:
        gathered = lax.all_gather(packed, "dp")
        qkv = [lax.all_gather(w_qkv, "dp", axis=1, tiled=True)]
        gate_pieces = [lax.all_gather(w_outgate, "dp", axis=0, tiled=True)]
        out_pieces = [lax.all_gather(w_out, "dp", axis=1, tiled=True)]
        layout = pair_layout = [(0, 0, width, width)]
    ranges = [(k * step + start, n) for k, start, n, step in layout]
    g_beta, g_conv, g_head, g_mix, g_mlp, g_digits = unpack(gathered, [a.shape for a in small])
    about_beta = g_beta.reshape(-1, heads)
    full_beta = blocks_about(about_beta, 0)
    full_conv = jnp.moveaxis(blocks_about(g_conv, 0), 0, 3).reshape(3 * KW, inner).astype(f32)
    gain_head = blocks_about(g_head, 0).reshape(1, DK).astype(f32)
    gain_one = blocks_about(g_mix.reshape(1, -1).astype(f32), 1)
    gain_two = g_mlp.reshape(1, -1).astype(f32)
    sums = jnp.sum(g_digits.astype(f32), 0)
    counts = 128.0 * sums[:3] + sums[3:]
    table = group_weight * (domain.shape[0] * domain.shape[1] * dp) / counts
    factor = jnp.sum(onehot * table, -1)[..., None]

    def flat(array):
        return array.reshape(array.shape[:-3] + (count_rows, array.shape[-1]))

    rows = lax.all_gather(tokens, "mp", axis=2, tiled=True)
    if near_four:
        gate_pieces = out_pieces = [lax.all_gather(after(pair_own, packed), "dp")]
    turn_one = turn.reshape(1)
    per_token = (seqs, block)
    square = (seqs, heads, DK, DK)
    hidden_one, proj, tail, logits, scale_one = call(
        partial(project_kernel, layout),
        [(rows, 0), (gain_one, None), (jnp.pad(full_beta, ((0, 0), (0, 128 - heads))), None)]
        + [(a, None) for a in qkv],
        [
            (shape_of(per_token + (width,), bf16), 0),
            (shape_of((3,) + per_token + (inner,), bf16), 1),
            (shape_of((3, seqs, HALO, inner), bf16), 1),
            (shape_of(per_token + (heads,), f32), 0),
            (shape_of(per_token + (1,), f32), 0),
        ],
        seqs,
        scalar=turn_one,
        scratch=[pltpu.VMEM((block, width), bf16)],
    )
    before = shifted(tail, "dp", 1)
    inverse, wu, qo, to, transfer, offset = call(
        pre_kernel,
        [(proj, None), (before, None), (full_conv, None), (logits, None)],
        [
            (shape_of((seqs, heads, block, block), f32), None),
            (shape_of((seqs, heads, block, 2 * DK), f32), None),
            (shape_of((seqs, heads, block, 2 * DK), f32), None),
            (shape_of((seqs, heads, DK, 2 * DK), bf16), None),
            (shape_of(square, bf16), None),
            (shape_of(square, bf16), None),
        ],
        1,
    )
    near = [shifted(to, "dp", c) for c in range(1, dp - 1)] + [shifted(offset, "dp", dp - 1)]
    rows_about, cotangent = call(
        partial(prepare_kernel, layout),
        [(rows, 0), (out_grad, 0), (factor, 0)],
        [(shape_of(per_token + (width,), bf16), 0)] * 2,
        seqs,
        scalar=turn_one,
    )
    turned = jnp.swapaxes(w_gateup, 1, 2)
    feed_own = [turned, w_down]
    mixer_part, normed, rule, state, gates = call(
        partial(mix_kernel, pair_layout, len(near), len(out_pieces)),
        [(a, 0) for a in near]
        + [(qo, 0), (hidden_one, 0), (gain_head, None)]
        + [(a, None) for a in gate_pieces + out_pieces],
        [
            (shape_of(per_token + (width,), bf16), 0),
            (shape_of(per_token + (inner,), bf16), 0),
            (shape_of(per_token + (inner,), f32), 0),
            (shape_of(square, f32), 0),
            (shape_of(per_token + (inner,), f32), 0),
        ],
        seqs,
        scalar=turn_one,
    )
    total = lax.psum(mixer_part, "mp")
    nexts = [shifted(transfer, "dp", -c) for c in range(1, dp - 1)]
    if near_four:
        gateup, down = (gathered_pieces(a, a.ndim - 1) for a in after(copies(feed_own), mixer_part, nexts))
    else:
        gateup, down = (
            [lax.all_gather(a, "dp", axis=a.ndim - 1, tiled=True)] for a in feed_own
        )
    units = w_down.shape[0]
    two_part, hidden_two, hidden_mlp, grad_pair = call(
        partial(feed_kernel, layout),
        [(rows_about, 0), (total, 0), (cotangent, 0), (gain_two, None)]
        + [(a, None) for a in gateup + down],
        [
            (shape_of(per_token + (width,), bf16), 0),
            (shape_of(per_token + (width,), bf16), 0),
            (shape_of(per_token + (units,), bf16), 0),
            (shape_of((2,) + per_token + (units,), bf16), 1),
        ],
        seqs,
    )
    grad_two = lax.psum(two_part, "mp")

    def feed_gradients(some, *others):
        outs = [(shape_of((m, units, n), bf16), None) for _, n in some for m in (2, 1)]
        base, span = some[0][0], sum(n for _, n in some)
        aligned = base % span == 0
        at = base // span if aligned else 0
        cols = pl.BlockSpec((count_rows, span if aligned else width), lambda s: (0, at))
        made = pl.pallas_call(
            partial(feed_gradient_kernel, base if aligned else 0, some),
            cost_estimate=FREE,
            grid=(1,),
            in_specs=[
                cols,
                cols,
                pl.BlockSpec((2, count_rows, units), lambda s: (0, 0, 0)),
                pl.BlockSpec((count_rows, units), lambda s: (0, 0)),
            ]
            + [pl.BlockSpec(memory_space=pl.ANY)] * len(others),
            out_specs=[pl.BlockSpec(o.shape, lambda s: (0, 0, 0)) for o, _ in outs],
            out_shape=[o for o, _ in outs],
            compiler_params=pltpu.CompilerParams(vmem_limit_bytes=VMEM),
        )(flat(hidden_two), flat(cotangent), flat(grad_pair), flat(hidden_mlp), *others)
        return made[::2], made[1::2]

    if near_four:
        feed_far = feed_gradients(ranges[3:])
        feed_in = [far_hop(*far) for far in feed_far]
        near_gateup, near_down = feed_gradients(ranges[:3], feed_far[0][0])
        first_made = [(near_gateup[0], "any")]
    else:
        [grad_gateup], [grad_down] = feed_gradients(ranges)
        held = first_made = []
    [down_part] = call(
        partial(down_kernel, layout),
        [(hidden_mlp, 0)] + [(a, None) for a in down] + first_made,
        [(shape_of(per_token + (width,), bf16), 0)],
        seqs,
        scalar=turn_one,
    )
    if near_four:
        gateup_added = near_sums(near_gateup, feed_in[0], *feed_in[1], down_part)
        down_added = near_sums(near_down, feed_in[1])
        gateup_sums, down_sums = near_hop(gateup_added), near_hop(down_added)
        down_part = after(down_part, gateup_added[1])
        held = [(a, "any") for a in gateup_sums[1:]]
    mlp_share = lax.psum_scatter(down_part, "mp", scatter_dimension=2, tiled=True)
    grad_mix, middle_own, mlpgain, drule, dgate, dgain, direct = call(
        partial(middle_back_kernel, pair_layout, len(out_pieces)),
        [
            (grad_two, 0),
            (cotangent, 0),
            (rows_about, 0),
            (total, 0),
            (gain_two, None),
            (rule, 0),
            (gates, 0),
            (gain_head, None),
            (qo, 0),
        ]
        + [(a, None) for a in out_pieces]
        + [(down_part, "any")]
        + held,
        [
            (shape_of(per_token + (width,), bf16), 0),
            (shape_of(per_token + (local_width,), f32), 0),
            (shape_of((seqs, 1, width), f32), 0),
            (shape_of(per_token + (inner,), f32), 0),
            (shape_of(per_token + (inner,), bf16), 0),
            (shape_of((seqs, 1, DK), f32), 0),
            (shape_of(square, bf16), 0),
        ],
        seqs,
        scalar=jnp.stack([turn, column_about]),
        scratch=[pltpu.VMEM((block, width), f32)],
    )
    directs = [shifted(direct, "dp", -c) for c in range(1, dp)]
    if near_four:
        pair_grads = call(
            partial(pair_gradient_kernel, [(k * size, size) for k in range(4)]),
            [(flat(a), None) for a in (hidden_one, dgate, normed, grad_mix)],
            [(shape_of((2, size, inner), bf16), None)] * 4,
            1,
        )
        down_total = sum_last(down_sums, pair_grads[3])
        held = [(a, "any") for a in (pair_grads[3], down_total)]
    else:
        grad_outgate = jnp.einsum(
            "td,tc->dc", flat(hidden_one), flat(dgate), preferred_element_type=f32
        )
        grad_outproj = jnp.einsum(
            "tc,td->cd", flat(normed), flat(grad_mix), preferred_element_type=f32
        )
        held = []
    dproj, last, first, dtaps, dlogits = call(
        partial(back_kernel, len(directs)),
        [
            (proj, 1),
            (before, 1),
            (full_conv, None),
            (logits, 0),
            (inverse, 0),
            (wu, 0),
            (state, 0),
            (drule, 0),
        ]
        + [(a, 0) for a in directs + nexts]
        + held,
        [
            (shape_of((3,) + per_token + (inner,), bf16), 1),
            (shape_of((3, seqs, PAD, inner), f32), 1),
            (shape_of((3, seqs, PAD, inner), f32), 1),
            (shape_of((seqs, 3 * KW, inner), f32), 0),
            (shape_of(per_token + (heads,), bf16), 0),
        ],
        seqs,
    )
    late = []
    if near_four:
        gateup_total = sum_last(gateup_sums, dlogits)
        late = [(gateup_total, "any")]
    later = shifted(first, "dp", -1)
    dproj = lax.dynamic_update_slice(dproj, (last + later).astype(bf16), (0, 0, block - PAD, 0))
    one_low, row_part, gain_part = call(
        partial(first_back_kernel, layout, pair_layout, len(gate_pieces)),
        [
            (flat(dproj), None),
            (flat(dgate), None),
            (flat(dlogits), None),
            (flat(proj), None),
            (flat(gates), None),
            (flat(logits), None),
            (about_beta.T.astype(f32), None),
            (flat(rows_about), None),
            (flat(scale_one), None),
        ]
        + [(a, None) for a in qkv + gate_pieces]
        + late,
        [
            (shape_of((count_rows, width), bf16), None),
            (shape_of((1, count_rows), f32), None),
            (shape_of((1, width), f32), None),
        ],
        1,
        scalar=turn_one,
    )
    one_share = lax.psum_scatter(
        one_low.reshape(seqs, block, width), "mp", scatter_dimension=2, tiled=True
    ).astype(f32)
    made = call(
        partial(qkv_gradient_kernel, ranges),
        [(flat(hidden_one), None), (flat(dproj), None), (flat(dlogits), None), (row_part, "any")],
        [(shape_of((3, n, inner), bf16), None) for _, n in ranges]
        + [(shape_of((heads, width), f32), None)],
        1,
    )

    def pieces(array, axis, about):
        shape = array.shape
        cut = array.reshape(shape[:axis] + (dp, shape[axis] // dp) + shape[axis + 1 :])
        cut = jnp.moveaxis(cut, axis, 0).reshape(dp, -1)
        return blocks_about(cut, 0) if about else cut

    smalls = jnp.concatenate(
        [
            pieces(jnp.sum(dtaps, 0).reshape(3, KW, heads, DK), 3, True),
            pieces(made[-1].T, 0, False),
            pieces(gain_part[0], 0, False),
            pieces(jnp.sum(mlpgain, (0, 1)), 0, False),
            pieces(jnp.sum(dgain, (0, 1)), 0, True),
        ],
        1,
    )
    small_shapes = [a.shape for a in (conv_weight, w_beta, mixer_gain, mlp_gain, head_gain)]
    if near_four:
        own_qkv, *near_qkv = near_sums(made[:3], far_hop(made[3], made[4]))
        smalls = jnp.pad(smalls, ((0, 0), (0, -smalls.shape[1] % 1024))).reshape(dp, -1, 128)
        sent = smalls.astype(bf16)
        got = [swap(sent[bits], bits) for bits in (1, 2, 3)]
        first_mix = (conv_weight.size + w_beta.size) // 128
        last_mix = first_mix + mixer_gain.size // 128
        lines = count_rows // 128 + last_mix - first_mix
        mine, rest = call(
            partial(
                add_small_kernel,
                slice(first_mix, last_mix),
                last_mix + mlp_gain.size // 128,
            ),
            [(a, None) for a in [smalls[0]] + got + [row_part]],
            [
                (shape_of(smalls.shape[1:], f32), None),
                (shape_of((lines + 8 - lines % 8, 128), f32), None),
            ],
            1,
        )
        pair_far = after(jnp.split(pair_grads[3], 2, 1), made[0])
        pair_near = near_sums(pair_grads[:3], far_hop(*pair_far))[1:]
        mine = mine.reshape(-1)
        sum_qkv = sum_last(near_hop((own_qkv, *near_qkv)))
        sum_gateup = jnp.swapaxes(gateup_total, 1, 2)
        sum_down = down_total[0]
        pair_sums = near_hop((pair_grads[0], *pair_near))
    else:
        gathered = lax.all_gather(smalls.astype(bf16), "dp")
        mine = jnp.sum(
            lax.dynamic_index_in_dim(gathered, place, 1, keepdims=False).astype(f32), 0
        )

        def scattered(array, axis):
            return lax.psum_scatter(array, "dp", scatter_dimension=axis, tiled=True).astype(f32)

        sum_qkv = scattered(made[0], 1)
        sum_outgate = scattered(grad_outgate.astype(bf16), 0)
        sum_out = scattered(grad_outproj.astype(bf16), 1)
        sum_gateup = jnp.swapaxes(scattered(grad_gateup, 2), 1, 2)
        sum_down = scattered(grad_down[0], 1)
    sum_conv, sum_beta, sum_mix, sum_mlp, sum_head = unpack(mine, small_shapes)
    if near_four:
        bit = 1
        while bit < lax.axis_size("mp"):
            devices = lax.axis_size("mp")
            rest = rest + lax.ppermute(rest, "mp", [(i, i ^ bit) for i in range(devices)])
            bit *= 2
        rest_sum = rest.reshape(-1)
    else:
        rest_sum = lax.psum(pack([row_part, sum_mix, sum_head]), "mp")
    row_sum, sum_mix, sum_head = unpack(rest_sum, [(count_rows,), sum_mix.shape, sum_head.shape])

    own_tokens = tokens.astype(f32)
    mixed_out = (own_tokens + own(total).astype(f32) + mlp_share.astype(f32)).astype(bf16)
    row_mean = (row_sum / width).reshape(seqs, block, 1)
    gain_own = lax.dynamic_slice_in_dim(gain_one, column, local_width, 1)
    tokens_grad = middle_own + scale_one * (
        one_share * gain_own - own_tokens * scale_one * row_mean
    )
    tokens_grad = tokens_grad.astype(bf16)
    if near_four:
        done = [(a, "any") for a in (sum_qkv, tokens_grad, mixed_out)]
        sum_outgate, sum_out = call(
            add_pair_kernel,
            [(a, None) for a in pair_sums] + done,
            [(shape_of(w_outgate.shape, f32), None), (shape_of(w_out.shape, f32), None)],
            1,
        )
    return (
        mixed_out,
        tokens_grad,
        sum_qkv,
        sum_conv,
        sum_beta,
        sum_outgate,
        sum_head,
        sum_out,
        sum_mix,
        sum_mlp,
        sum_gateup,
        sum_down,
    )


def solution(mesh):
    return jax.shard_map(
        body,
        mesh=mesh,
        in_specs=(
            P(None, "dp", "mp"),
            P(None, "dp", None),
            P(None, "dp"),
            P(),
            P(None, "dp", "mp"),
            P(None, None, "mp", "dp"),
            P("dp", "mp"),
            P("dp", "mp"),
            P("dp"),
            P("mp", "dp"),
            P("dp"),
            P("dp"),
            P(None, "dp", "mp"),
            P("mp", "dp"),
        ),
        out_specs=(
            P(None, "dp", "mp"),
            P(None, "dp", "mp"),
            P(None, "dp", "mp"),
            P(None, None, "mp", "dp"),
            P("dp", "mp"),
            P("dp", "mp"),
            P("dp"),
            P("mp", "dp"),
            P("dp"),
            P("dp"),
            P(None, "dp", "mp"),
            P("mp", "dp"),
        ),
        check_vma=False,
    )
```

```python
from functools import partial

import jax
import jax.numpy as jnp
from jax import lax
from jax.experimental import pallas as pl
from jax.experimental.pallas import tpu as pltpu
from jax.sharding import PartitionSpec as P

DK = 128
KW = 4
PAD = 8
HALO = 16
ROWS = 16
VMEM = 58 * 2**20
SMALL = 12 * 2**20
FREE = pl.CostEstimate(flops=0, transcendentals=0, bytes_accessed=0)

eps_norm = 1e-06
eps_unit = 1e-06

f32 = jnp.float32
bf16 = jnp.bfloat16


def split(v):
    if v.dtype == bf16:
        return v, None
    high = v.astype(bf16)
    return high, (v - high.astype(f32)).astype(bf16)


def mm(a, b, ca=1, cb=0, passes=3):
    def one(x, y):
        return lax.dot_general(x, y, (((ca,), (cb,)), ((), ())), preferred_element_type=f32)

    if passes == 1:
        return one(a.astype(bf16), b.astype(bf16))
    (ah, al), (bh, bl) = split(a), split(b)
    out = one(ah, bh)
    if bl is not None:
        out = out + one(ah, bl)
    if al is not None:
        out = out + one(al, bh)
    return out


def places(rows, cols):
    return (
        lax.broadcasted_iota(jnp.int32, (rows, cols), 0),
        lax.broadcasted_iota(jnp.int32, (rows, cols), 1),
    )


def unit_lower_inverses(blocks):
    size = blocks[0].shape[0]
    if size > 128:
        half = size // 2
        parts = unit_lower_inverses(
            [a[:half, :half] for a in blocks] + [a[half:, half:] for a in blocks]
        )
        firsts, seconds = parts[: len(blocks)], parts[len(blocks) :]
        inner = [mm(a[half:, :half], x) for a, x in zip(blocks, firsts)]
        lower = [-mm(x, y) for x, y in zip(seconds, inner)]
        zero = jnp.zeros((half, half), f32)
        return [
            jnp.concatenate(
                [jnp.concatenate([x, zero], 1), jnp.concatenate([y, z], 1)], 0
            )
            for x, y, z in zip(firsts, lower, seconds)
        ]
    rows, cols = places(size, size)
    eye = (rows == cols).astype(f32)
    level = 0
    inverses = None
    while (1 << level) < size:
        mask = (
            ((rows >> (level + 1)) == (cols >> (level + 1)))
            & (((rows >> level) & 1) == 1)
            & (((cols >> level) & 1) == 0)
        ).astype(f32)
        lows = [a * mask for a in blocks]
        if level == 0:
            inverses = [eye - low for low in lows]
        else:
            inner = [mm(low, x) for low, x in zip(lows, inverses)]
            inverses = [x - mm(x, y) for x, y in zip(inverses, inner)]
        level += 1
    return inverses


def head_slice(h):
    return slice(h * DK, (h + 1) * DK)


def convolve(proj_ref, before_ref, taps, i, h):
    own = proj_ref[i, 0, :, head_slice(h)].astype(f32)
    length = own.shape[0]
    ext = jnp.concatenate([before_ref[i, 0, :, head_slice(h)].astype(f32), own], 0)
    shifts = [ext[HALO - KW + 1 + j : HALO - KW + 1 + j + length] for j in range(KW)]
    out = None
    for j in range(KW):
        tap = taps[i * KW + j : i * KW + j + 1, head_slice(h)]
        out = tap * shifts[j] if out is None else out + tap * shifts[j]
    sig = jax.nn.sigmoid(out)
    return shifts, out, sig, out * sig


def unit(acts):
    inv = lax.rsqrt(jnp.sum(acts * acts, -1, keepdims=True) + eps_unit)
    return acts * inv, inv


def rule_inputs(proj_ref, before_ref, taps, h):
    parts = [convolve(proj_ref, before_ref, taps, i, h) for i in range(3)]
    q, q_inv = unit(parts[0][3])
    k, k_inv = unit(parts[1][3])
    return parts, (q, q_inv), (k, k_inv), parts[2][3]


def norm_factor(values):
    return lax.rsqrt(jnp.mean(values * values, -1, keepdims=True) + eps_norm)


def project_kernel(layout, *refs):
    place_ref, rows_ref, gain_ref, beta_ref = refs[:4]
    pieces = refs[4 : 4 + len(layout)]
    hidden_ref, proj_ref, tail_ref, logit_ref, scale_ref, keep_ref = refs[4 + len(layout) :]
    rows = rows_ref[0].astype(f32)
    scale = norm_factor(rows)
    scale_ref[0] = scale
    keep_ref[...] = (rows * scale * gain_ref[...]).astype(bf16)
    logits = mm(keep_ref[...], beta_ref[...])
    logit_ref[0] = logits[:, : logit_ref.shape[2]]
    sums = [None] * 3
    for (k, start, size, block), piece in zip(layout, pieces):
        at = pl.multiple_of((place_ref[0] ^ k) * block + start, 128)
        part = keep_ref[:, pl.ds(at, size)]
        hidden_ref[0, :, k * block + start : k * block + start + size] = part
        for i in range(3):
            term = mm(part, piece[i])
            sums[i] = term if sums[i] is None else sums[i] + term
    for i in range(3):
        low = sums[i].astype(bf16)
        proj_ref[i, 0] = low
        tail_ref[i, 0] = low[low.shape[0] - HALO :]


def pre_kernel(proj_ref, before_ref, taps_ref, logit_ref, x_ref, wu_ref, qo_ref, to_ref, t_ref, o_ref):
    seqs, heads = to_ref.shape[:2]
    taps = taps_ref[...]
    length = proj_ref.shape[2]
    r, c = places(length, length)
    strict = (r > c).astype(f32)
    full = (r >= c).astype(f32)
    saved, blocks = [], []
    for s in range(seqs):
        betas = jax.nn.sigmoid(logit_ref[s])
        rows, before = proj_ref.at[:, s : s + 1], before_ref.at[:, s : s + 1]
        for h in range(heads):
            _, (q, _), (k, _), v = rule_inputs(rows, before, taps, h)
            q, k, v = q.astype(bf16), k.astype(bf16), v.astype(bf16)
            beta = betas[:, h : h + 1]
            blocks.append(beta * mm(k, k, 1, 1) * strict)
            saved.append((s, h, q, k, v, beta))
    inverses = unit_lower_inverses(blocks)
    r, c = places(DK, DK)
    eye = (r == c).astype(f32)
    for (s, h, q, k, v, beta), x in zip(saved, inverses):
        x_ref[s, h] = x
        kv = jnp.concatenate([k.astype(f32), v.astype(f32)], 1) * beta
        wu = mm(x, kv)
        wu_ref[s, h] = wu
        scores = mm(q, k, 1, 1) * full
        pwu = mm(scores, wu)
        qo_ref[s, h, :, :DK] = q.astype(f32) - pwu[:, :DK]
        qo_ref[s, h, :, DK:] = pwu[:, DK:]
        kwu = mm(k, wu, 0, 0)
        transfer, offset = (eye - kwu[:, :DK]).astype(bf16), kwu[:, DK:].astype(bf16)
        to_ref[s, h, :, :DK] = transfer
        to_ref[s, h, :, DK:] = offset
        t_ref[s, h] = transfer
        o_ref[s, h] = offset


def by_piece(place_ref, refs):
    if len(refs) > 1 or len(refs[0].shape) < 4:
        return refs
    return [refs[0].at[place_ref[0] ^ k] for k in range(4)]


def gate_part(ref):
    return ref.at[0] if len(ref.shape) == 3 else ref


def out_columns(layout, refs):
    for (k, start, size, block), ref in zip(layout, refs):
        at, half = k * block + start, size // 2
        if len(ref.shape) == 2:
            yield at, size, ref
            continue
        inner = ref.shape[1] // 2
        yield at, half, ref.at[1, :inner]
        yield at + half, half, ref.at[1, inner:]


def mix_kernel(layout, count, pieces, place_ref, *refs):
    near, rest = refs[:count], refs[count:]
    qo_ref, hidden_ref, gain_ref = rest[:3]
    gate_pieces = by_piece(place_ref, rest[3 : 3 + pieces])
    outs = by_piece(place_ref, rest[3 + pieces : 3 + 2 * pieces])
    part_ref, normed_ref, rule_ref, state_ref, gate_ref = rest[-5:]
    gates = None
    for (k, start, size, block), ref in zip(layout, gate_pieces):
        at = k * block + start
        term = mm(hidden_ref[0, :, at : at + size], gate_part(ref)[...])
        gates = term if gates is None else gates + term
    gate_ref[0] = gates
    heads = state_ref.shape[1]
    for h in range(heads):
        state = near[-1][0, h].astype(f32)
        for ref in reversed(near[:-1]):
            state = mm(ref[0, h, :, :DK], state) + ref[0, h, :, DK:].astype(f32)
        state_ref[0, h] = state
        qo = qo_ref[0, h]
        out = (mm(qo[:, :DK], state) + qo[:, DK:]) * DK ** (-0.5)
        rule_ref[0, :, head_slice(h)] = out
        gate = gate_ref[0, :, head_slice(h)]
        normed = out * norm_factor(out) * gain_ref[...] * (gate * jax.nn.sigmoid(gate))
        normed_ref[0, :, head_slice(h)] = normed.astype(bf16)
    for at, size, ref in out_columns(layout, outs):
        part_ref[0, :, at : at + size] = mm(normed_ref[0], ref[...]).astype(bf16)


def prepare_kernel(layout, place_ref, rows_ref, grad_ref, factor_ref, about_ref, cot_ref):
    for k, start, size, block in layout:
        at = pl.multiple_of((place_ref[0] ^ k) * block + start, 128)
        to = slice(k * block + start, k * block + start + size)
        about_ref[0, :, to] = rows_ref[0, :, pl.ds(at, size)]
        grad = grad_ref[0, :, pl.ds(at, size)].astype(f32) * factor_ref[0]
        cot_ref[0, :, to] = grad.astype(bf16)


def down_kernel(layout, place_ref, mlp_ref, *refs):
    part_ref = refs[-1]
    for (k, start, size, block), ref in zip(layout, refs):
        at = pl.multiple_of((place_ref[0] ^ k) * block + start, 128)
        part_ref[0, :, pl.ds(at, size)] = mm(mlp_ref[0], ref[...]).astype(bf16)


def feed_gradient_kernel(base, ranges, hidden_ref, cot_ref, pair_ref, mlp_ref, *outs):
    outs = outs[-2 * len(ranges) :]
    for n, (start, size) in enumerate(ranges):
        start = start - base
        hidden = hidden_ref[:, start : start + size]
        outs[2 * n][0] = mm(pair_ref[0], hidden, 0, 0).astype(bf16)
        outs[2 * n][1] = mm(pair_ref[1], hidden, 0, 0).astype(bf16)
        outs[2 * n + 1][0] = mm(mlp_ref[...], cot_ref[:, start : start + size], 0, 0).astype(bf16)


def qkv_gradient_kernel(ranges, hidden_ref, dproj_ref, dlogit_ref, *outs):
    outs = outs[-len(ranges) - 1 :]
    for (start, size), out in zip(ranges, outs[:-1]):
        hidden = hidden_ref[:, start : start + size]
        for i in range(3):
            out[i] = mm(hidden, dproj_ref[i], 0, 0).astype(bf16)
    outs[-1][...] = mm(dlogit_ref[...], hidden_ref[...], 0, 0)


def pair_gradient_kernel(ranges, hidden_ref, dgate_ref, normed_ref, mix_ref, *outs):
    inner = normed_ref.shape[1]
    for (start, size), out in zip(ranges, outs):
        out[0] = mm(hidden_ref[:, start : start + size], dgate_ref[...], 0, 0).astype(bf16)
        for n in range(2):
            at = start + n * size // 2
            mix = mix_ref[:, at : at + size // 2]
            out[1, n * inner : (n + 1) * inner] = mm(normed_ref[...], mix, 0, 0).astype(bf16)


def add_halves_kernel(*refs):
    one_ref, two_ref, low_ref, high_ref, one_out, two_out = refs[:4] + refs[-2:]
    one_out[...] = (one_ref[...].astype(f32) + high_ref[...].astype(f32)).astype(bf16)
    two_out[...] = (two_ref[...].astype(f32) + low_ref[...].astype(f32)).astype(bf16)


def add_small_kernel(mix_rows, head_row, *refs):
    *parts, row_ref, out_ref, rest_ref = refs
    total = sum(ref[...].astype(f32) for ref in parts)
    out_ref[...] = total
    lines = [row_ref[:, n * 128 : (n + 1) * 128] for n in range(row_ref.shape[1] // 128)]
    lines += [total[mix_rows], total[head_row : head_row + 1]]
    used = len(lines) - 2 + mix_rows.stop - mix_rows.start + 1
    lines.append(jnp.zeros((rest_ref.shape[0] - used, 128), f32))
    rest_ref[...] = jnp.concatenate(lines, 0)


def add_last_kernel(*refs):
    own_ref, one_ref, two_ref, out_ref = refs[:3] + refs[-1:]
    out_ref[...] = own_ref[...].astype(f32) + one_ref[...].astype(f32) + two_ref[...].astype(f32)


def feed_kernel(layout, *refs):
    rows_ref, total_ref, cot_ref, gain_ref = refs[:4]
    count = len(layout)
    gateups, downs = (refs[4 + n * count : 4 + (n + 1) * count] for n in range(2))
    two_ref, hidden_ref, mlp_ref, pair_ref = refs[-4:]
    middle = rows_ref[0].astype(f32) + total_ref[0].astype(f32)
    hidden_ref[0] = (middle * norm_factor(middle) * gain_ref[...]).astype(bf16)
    gate, up, grad = None, None, None
    for (k, start, size, block), w_gateup, w_down in zip(layout, gateups, downs):
        lanes = slice(k * block + start, k * block + start + size)
        hidden = hidden_ref[0, :, lanes]
        terms = (
            mm(hidden, w_gateup[0], 1, 1),
            mm(hidden, w_gateup[1], 1, 1),
            mm(cot_ref[0, :, lanes], w_down[...], 1, 1),
        )
        if gate is None:
            gate, up, grad = terms
        else:
            gate, up, grad = gate + terms[0], up + terms[1], grad + terms[2]
    sig = jax.nn.sigmoid(gate)
    silu = gate * sig
    mlp_ref[0] = (silu * up).astype(bf16)
    first = (grad * up * (sig + silu * (1.0 - sig))).astype(bf16)
    second = (grad * silu).astype(bf16)
    pair_ref[0, 0] = first
    pair_ref[1, 0] = second
    for (k, start, size, block), w_gateup in zip(layout, gateups):
        lanes = slice(k * block + start, k * block + start + size)
        two = mm(first, w_gateup[0]) + mm(second, w_gateup[1])
        two_ref[0, :, lanes] = two.astype(bf16)


def middle_back_kernel(layout, pieces, at_ref, *refs):
    two_ref, cot_ref, rows_ref, total_ref, gain_ref, rule_ref, gate_ref, head_gain_ref, qo_ref = refs[:9]
    outs = by_piece(at_ref, refs[9 : 9 + pieces])
    mix_ref, own_ref, mlpgain_ref, drule_ref, dgate_ref, dgain_ref, direct_ref, keep_ref = refs[-8:]
    full = rows_ref.shape[2]
    gain_sum = None
    for start in range(0, rows_ref.shape[1], ROWS):
        at = slice(start, start + ROWS)
        middle = rows_ref[0, at].astype(f32) + total_ref[0, at].astype(f32)
        two = two_ref[0, at].astype(f32)
        factor = norm_factor(middle)
        normal = middle * factor
        term = jnp.sum((two * normal).reshape(ROWS // 8, 8, full), 0)
        gain_sum = term if gain_sum is None else gain_sum + term
        scaled = two * gain_ref[...]
        mean = jnp.mean(scaled * normal, -1, keepdims=True)
        keep = cot_ref[0, at].astype(f32) + factor * (scaled - normal * mean)
        keep_ref[at] = keep
        mix_ref[0, at] = keep.astype(bf16)
    mlpgain_ref[0] = jnp.sum(gain_sum, 0, keepdims=True)
    width = own_ref.shape[2]
    own_ref[0] = keep_ref[:, pl.ds(pl.multiple_of(at_ref[1], 128), width)]
    grads = None
    for at, size, ref in out_columns(layout, outs):
        term = mm(mix_ref[0, :, at : at + size], ref[...], 1, 1)
        grads = term if grads is None else grads + term
    total = jnp.zeros((1, DK), f32)
    for h in range(direct_ref.shape[1]):
        grad = grads[:, head_slice(h)]
        out = rule_ref[0, :, head_slice(h)]
        gate = gate_ref[0, :, head_slice(h)]
        inv = norm_factor(out)
        n = out * inv
        sig = jax.nn.sigmoid(gate)
        silu = gate * sig
        gg = grad * head_gain_ref[...]
        dn = gg * silu
        drule = inv * (dn - n * jnp.mean(dn * n, -1, keepdims=True))
        drule_ref[0, :, head_slice(h)] = drule
        dgate = gg * n * sig * (1.0 + gate * (1.0 - sig))
        dgate_ref[0, :, head_slice(h)] = dgate.astype(bf16)
        total = total + jnp.sum(grad * n * silu, 0, keepdims=True)
        direct = mm(qo_ref[0, h, :, :DK], drule, 0, 0) * DK ** (-0.5)
        direct_ref[0, h] = direct.astype(bf16)
    dgain_ref[0] = total


def first_back_kernel(layout, pair_layout, count, place_ref, *refs):
    dproj_ref, dgate_ref, dlogit_ref, proj_ref, gate_ref, logit_ref, beta_ref, rows_ref, scale_ref = refs[:9]
    pieces = refs[9 : 9 + len(layout)]
    pairs = by_piece(place_ref, refs[9 + len(layout) : 9 + len(layout) + count])
    one_ref, rowsum_ref, gainsum_ref = refs[-3:]
    gates = {}
    for (k, start, size, block), ref in zip(pair_layout, pairs):
        gates[k] = ref
    for (k, start, size, block), piece in zip(layout, pieces):
        lanes = slice(k * block + start, k * block + start + size)
        grad = mm(dgate_ref[...], gate_part(gates[k])[start : start + size], 1, 1)
        for i in range(3):
            grad = grad + mm(dproj_ref[i], piece[i], 1, 1)
        for h in range(beta_ref.shape[0]):
            grad = grad + dlogit_ref[:, h : h + 1].astype(f32) * beta_ref[h : h + 1, lanes]
        at = pl.multiple_of((place_ref[0] ^ k) * block + start, 128)
        one_ref[:, pl.ds(at, size)] = grad.astype(bf16)
        gainsum_ref[:, lanes] = jnp.sum(
            grad * (rows_ref[:, lanes].astype(f32) * scale_ref[...]), 0, keepdims=True
        )
    total = dgate_ref[...].astype(f32) * gate_ref[...]
    for i in range(3):
        total = total + dproj_ref[i].astype(f32) * proj_ref[i].astype(f32)
    lane = lax.broadcasted_iota(jnp.int32, total.shape, 1) == 0
    logits = jnp.sum(dlogit_ref[...].astype(f32) * logit_ref[...], -1, keepdims=True)
    logits_sum = jnp.where(lane, logits, 0.0)
    total = total + logits_sum
    ones = jnp.ones((8, total.shape[1]), f32)
    rowsum_ref[...] = mm(ones, total, 1, 1)[:1]


def back_kernel(count, *refs):
    (
        proj_ref,
        before_ref,
        taps_ref,
        logit_ref,
        x_ref,
        wu_ref,
        state_ref,
        drule_ref,
    ) = refs[:8]
    dproj_ref, last_ref, first_ref, dtaps_ref, dlogit_ref = refs[-5:]
    others = refs[8 : 8 + 2 * count - 1]
    directs, nexts = others[:count], others[count:]
    heads = state_ref.shape[1]
    taps = taps_ref[...]
    length = proj_ref.shape[2]
    betas = jax.nn.sigmoid(logit_ref[0])
    r, c = places(length, length)
    strict = (r > c).astype(f32)
    full = (r >= c).astype(f32)
    zeros = jnp.zeros((PAD, DK), f32)
    for h in range(heads):
        parts, (qu, q_inv), (ku, k_inv), vu = rule_inputs(proj_ref, before_ref, taps, h)
        q, k, v = qu.astype(bf16), ku.astype(bf16), vu.astype(bf16)
        beta = betas[:, h : h + 1]
        leave = jnp.zeros((DK, DK), f32)
        for j in reversed(range(count)):
            here = directs[j][0, h].astype(f32)
            leave = here if j == count - 1 else mm(nexts[j][0, h], leave, 0, 0) + here
        state = state_ref[0, h]
        wu = wu_ref[0, h]
        u = wu[:, DK:] - mm(wu[:, :DK], state)
        resid = v.astype(f32) - mm(k, state)
        dout = drule_ref[0, :, head_slice(h)] * DK ** (-0.5)
        gram = mm(k, k, 1, 1)
        scores = mm(q, k, 1, 1) * full
        du = mm(scores, dout, 0, 0) + mm(k, leave)
        y = mm(x_ref[0, h], du, 0, 0)
        by = beta * y
        da = -(mm(y, u, 1, 1, 1) * strict)
        dbeta = jnp.sum(y * resid, -1, keepdims=True) + jnp.sum(da * gram, -1, keepdims=True)
        dgram = beta * da
        dscores = mm(dout, u, 1, 1, 1) * full
        dq = mm(dout, state, 1, 1, 1) + mm(dscores, k, 1, 0, 1)
        dk = (
            mm(dgram, k, 1, 0, 1)
            + mm(dgram, k, 0, 0, 1)
            + mm(dscores, q, 0, 0, 1)
            + mm(u, leave, 1, 1, 1)
            - mm(by, state, 1, 1, 1)
        )
        dlogit_ref[0, :, h : h + 1] = (dbeta * beta * (1.0 - beta)).astype(bf16)
        dq = (dq - qu * jnp.sum(qu * dq, -1, keepdims=True)) * q_inv
        dk = (dk - ku * jnp.sum(ku * dk, -1, keepdims=True)) * k_inv
        for i, dact in enumerate((dq, dk, by)):
            shifts, out, sig, _ = parts[i]
            dconv = dact * sig * (1.0 + out * (1.0 - sig))
            ext = jnp.concatenate([zeros, dconv, zeros], 0)
            total = None
            for j in range(KW):
                at = i * KW + j
                dtaps_ref[0, at : at + 1, head_slice(h)] = jnp.sum(
                    dconv * shifts[j], 0, keepdims=True
                )
                tap = taps[at : at + 1, head_slice(h)]
                term = tap * ext[KW - 1 - j : KW - 1 - j + PAD + length]
                total = term if total is None else total + term
            first_ref[i, 0, :, head_slice(h)] = total[:PAD]
            last_ref[i, 0, :, head_slice(h)] = total[length:]
            dproj_ref[i, 0, :, head_slice(h)] = total[PAD:].astype(bf16)


def call(kernel, ins, outs, steps, scalar=None, scratch=(), limit=VMEM, alias=None):
    def spec(shape, axis):
        if axis == "any":
            return pl.BlockSpec(memory_space=pl.ANY)
        block = tuple(1 if n == axis else size for n, size in enumerate(shape))
        where = lambda s, *_: tuple(s if n == axis else 0 for n in range(len(shape)))
        if axis is None:
            return pl.BlockSpec(block, where, pipeline_mode=pl.Buffered(1))
        return pl.BlockSpec(block, where)

    given = [] if scalar is None else [scalar]
    return pl.pallas_call(
        kernel,
        cost_estimate=FREE,
        grid_spec=pltpu.PrefetchScalarGridSpec(
            num_scalar_prefetch=len(given),
            grid=(steps,),
            in_specs=[spec(a.shape, axis) for a, axis in ins],
            out_specs=[spec(o.shape, axis) for o, axis in outs],
            scratch_shapes=scratch,
        ),
        out_shape=[o for o, _ in outs],
        input_output_aliases=alias or {},
        compiler_params=pltpu.CompilerParams(vmem_limit_bytes=limit),
    )(*given, *[a for a, _ in ins])


def shape_of(shape, dtype):
    return jax.ShapeDtypeStruct(shape, dtype)


def shifted(array, axis, by):
    devices = lax.axis_size(axis)
    pairs = [(i, i + by) for i in range(devices) if 0 <= i + by < devices]
    return lax.ppermute(array, axis, pairs)


def after(values, *others):
    flat, tree = jax.tree.flatten(values)
    others = jax.tree.leaves(others)
    here = pl.BlockSpec(memory_space=pl.ANY)
    out = pl.pallas_call(
        lambda *refs: None,
        cost_estimate=FREE,
        in_specs=[here] * (len(flat) + len(others)),
        out_specs=[here] * len(flat),
        out_shape=[shape_of(a.shape, a.dtype) for a in flat],
        input_output_aliases={n: n for n in range(len(flat))},
    )(*flat, *others)
    return jax.tree.unflatten(tree, out)


def copies(values):
    count = len(values)

    def kernel(*refs):
        for n in range(count):
            refs[n - count][...] = refs[n][...]

    outs = [(shape_of(a.shape, a.dtype), None) for a in values]
    return call(kernel, [(a, None) for a in values], outs, 1)


def swap(array, bits):
    return lax.ppermute(array, "dp", [(i, i ^ bits) for i in range(4)])


def first_hop(own):
    return swap(own, 1), swap(own, 2)


def halves_of(hop, axis):
    low, high = (jnp.split(part, 2, axis) for part in hop)
    return low[0], high[1]


def gathered_pieces(own, axis, hop=None, halves=None):
    hop = hop or first_hop(own)
    low, high = halves or halves_of(hop, axis)
    return [own, *hop, swap(low, 2), swap(high, 1)]


def far_hop(low, high):
    return swap(low, 1), swap(high, 2)


def near_sums(pieces, far_in, *others):
    own, one, two = pieces
    half = far_in[0].shape
    along = 1 if half[1] < one.shape[1] else 2

    def spec(place):
        where = tuple(place if n == along else 0 for n in range(3))
        return pl.BlockSpec(half, lambda s: where)

    first, second = spec(0), spec(1)
    here = pl.BlockSpec(memory_space=pl.ANY)
    one, two = pl.pallas_call(
        add_halves_kernel,
        cost_estimate=FREE,
        grid=(1,),
        in_specs=[second, first, first, first] + [here] * len(others),
        out_specs=[second, first],
        out_shape=[shape_of(a.shape, a.dtype) for a in (one, two)],
        input_output_aliases={0: 0, 1: 1},
        compiler_params=pltpu.CompilerParams(vmem_limit_bytes=SMALL),
    )(one, two, *far_in, *others)
    return own, one, two


def near_hop(pieces):
    own, one, two = pieces
    return own, swap(one, 1), swap(two, 2)


def add_pair_kernel(own_ref, one_ref, two_ref, *refs):
    gate_ref, out_ref = refs[-2:]
    inner = out_ref.shape[0]

    def added(i, rows):
        parts = (ref[i, rows].astype(f32) for ref in (own_ref, one_ref, two_ref))
        return sum(parts)

    gate_ref[...] = added(0, slice(None))
    for n in range(2):
        out_ref[:, n * inner : (n + 1) * inner] = added(1, slice(n * inner, (n + 1) * inner))


def sum_last(parts, *others):
    own = parts[0]
    ins = [(a, 0) for a in parts] + [(a, "any") for a in others]
    [total] = call(add_last_kernel, ins, [(shape_of(own.shape, f32), 0)], own.shape[0], limit=SMALL)
    return total


def pack(parts):
    return jnp.concatenate([p.reshape(-1) for p in parts])


def unpack(flat, shapes):
    out, at = [], 0
    for shape in shapes:
        size = 1
        for n in shape:
            size *= n
        out.append(flat[..., at : at + size].reshape(flat.shape[:-1] + tuple(shape)))
        at += size
    return out


def padded(flat, multiple=1024):
    return jnp.pad(flat, (0, -flat.shape[0] % multiple))


def body(
    tokens,
    out_grad,
    domain,
    group_weight,
    w_qkv,
    conv_weight,
    w_beta,
    w_outgate,
    head_gain,
    w_out,
    mixer_gain,
    mlp_gain,
    w_gateup,
    w_down,
):
    dp = lax.axis_size("dp")
    place = lax.axis_index("dp")
    seqs, block, local_width = tokens.shape
    count_rows = seqs * block
    heads = conv_weight.shape[2]
    inner = heads * DK
    column = lax.axis_index("mp") * local_width
    near_four = dp == 4

    def blocks_about(array, axis):
        if not near_four:
            return array
        size = array.shape[axis] // 4
        return jnp.concatenate(
            [lax.dynamic_slice_in_dim(array, (place ^ k) * size, size, axis) for k in range(4)],
            axis,
        )

    width = out_grad.shape[2]
    turn = place if near_four else jnp.int32(0)
    column_about = ((column // (width // 4)) ^ turn) * (width // 4) + column % (width // 4)

    def own(array):
        array = array.reshape(seqs, block, width)
        return lax.dynamic_slice_in_dim(array, column_about, local_width, 2)

    onehot = (domain[..., None] == jnp.arange(3, dtype=jnp.int32)).astype(f32)
    own_counts = jnp.sum(onehot, axis=(0, 1))
    high = jnp.floor(own_counts / 128.0)
    digits = jnp.concatenate([high, own_counts - 128.0 * high]).astype(bf16)
    small = [w_beta, conv_weight, head_gain, mixer_gain, mlp_gain, digits]
    packed = padded(pack(small))
    size = width // 4
    if near_four:
        qkv_hop = first_hop(w_qkv)
        qkv_halves = halves_of(qkv_hop, 1)
        qkv = gathered_pieces(w_qkv, 1, qkv_hop, qkv_halves)
        packed = after(packed, qkv_halves)
        gathered = jnp.stack([packed] + [swap(packed, bits) for bits in (1, 2, 3)])
        half = w_out.shape[1] // 2
        pair_own = jnp.stack(
            [w_outgate, jnp.concatenate([w_out[:, :half], w_out[:, half:]], 0)]
        )
        pair_layout = [(k, 0, size, size) for k in range(4)]
        layout = pair_layout[:3] + [(3, 0, size // 2, size), (3, size // 2, size // 2, size)]
    else:
        gathered = lax.all_gather(packed, "dp")
        qkv = [lax.all_gather(w_qkv, "dp", axis=1, tiled=True)]
        gate_pieces = [lax.all_gather(w_outgate, "dp", axis=0, tiled=True)]
        out_pieces = [lax.all_gather(w_out, "dp", axis=1, tiled=True)]
        layout = pair_layout = [(0, 0, width, width)]
    ranges = [(k * step + start, n) for k, start, n, step in layout]
    g_beta, g_conv, g_head, g_mix, g_mlp, g_digits = unpack(gathered, [a.shape for a in small])
    about_beta = g_beta.reshape(-1, heads)
    full_beta = blocks_about(about_beta, 0)
    full_conv = jnp.moveaxis(blocks_about(g_conv, 0), 0, 3).reshape(3 * KW, inner).astype(f32)
    gain_head = blocks_about(g_head, 0).reshape(1, DK).astype(f32)
    gain_one = blocks_about(g_mix.reshape(1, -1).astype(f32), 1)
    gain_two = g_mlp.reshape(1, -1).astype(f32)
    sums = jnp.sum(g_digits.astype(f32), 0)
    counts = 128.0 * sums[:3] + sums[3:]
    table = group_weight * (domain.shape[0] * domain.shape[1] * dp) / counts
    factor = jnp.sum(onehot * table, -1)[..., None]

    def flat(array):
        return array.reshape(array.shape[:-3] + (count_rows, array.shape[-1]))

    rows = lax.all_gather(tokens, "mp", axis=2, tiled=True)
    if near_four:
        gate_pieces = out_pieces = [lax.all_gather(after(pair_own, packed), "dp")]
    turn_one = turn.reshape(1)
    per_token = (seqs, block)
    square = (seqs, heads, DK, DK)
    hidden_one, proj, tail, logits, scale_one = call(
        partial(project_kernel, layout),
        [(rows, 0), (gain_one, None), (jnp.pad(full_beta, ((0, 0), (0, 128 - heads))), None)]
        + [(a, None) for a in qkv],
        [
            (shape_of(per_token + (width,), bf16), 0),
            (shape_of((3,) + per_token + (inner,), bf16), 1),
            (shape_of((3, seqs, HALO, inner), bf16), 1),
            (shape_of(per_token + (heads,), f32), 0),
            (shape_of(per_token + (1,), f32), 0),
        ],
        seqs,
        scalar=turn_one,
        scratch=[pltpu.VMEM((block, width), bf16)],
    )
    before = shifted(tail, "dp", 1)
    inverse, wu, qo, to, transfer, offset = call(
        pre_kernel,
        [(proj, None), (before, None), (full_conv, None), (logits, None)],
        [
            (shape_of((seqs, heads, block, block), f32), None),
            (shape_of((seqs, heads, block, 2 * DK), f32), None),
            (shape_of((seqs, heads, block, 2 * DK), f32), None),
            (shape_of((seqs, heads, DK, 2 * DK), bf16), None),
            (shape_of(square, bf16), None),
            (shape_of(square, bf16), None),
        ],
        1,
    )
    near = [shifted(to, "dp", c) for c in range(1, dp - 1)] + [shifted(offset, "dp", dp - 1)]
    rows_about, cotangent = call(
        partial(prepare_kernel, layout),
        [(rows, 0), (out_grad, 0), (factor, 0)],
        [(shape_of(per_token + (width,), bf16), 0)] * 2,
        seqs,
        scalar=turn_one,
    )
    turned = jnp.swapaxes(w_gateup, 1, 2)
    feed_own = [turned, w_down]
    mixer_part, normed, rule, state, gates = call(
        partial(mix_kernel, pair_layout, len(near), len(out_pieces)),
        [(a, 0) for a in near]
        + [(qo, 0), (hidden_one, 0), (gain_head, None)]
        + [(a, None) for a in gate_pieces + out_pieces],
        [
            (shape_of(per_token + (width,), bf16), 0),
            (shape_of(per_token + (inner,), bf16), 0),
            (shape_of(per_token + (inner,), f32), 0),
            (shape_of(square, f32), 0),
            (shape_of(per_token + (inner,), f32), 0),
        ],
        seqs,
        scalar=turn_one,
    )
    total = lax.psum(mixer_part, "mp")
    nexts = [shifted(transfer, "dp", -c) for c in range(1, dp - 1)]
    if near_four:
        gateup, down = (gathered_pieces(a, a.ndim - 1) for a in after(copies(feed_own), mixer_part, nexts))
    else:
        gateup, down = (
            [lax.all_gather(a, "dp", axis=a.ndim - 1, tiled=True)] for a in feed_own
        )
    units = w_down.shape[0]
    two_part, hidden_two, hidden_mlp, grad_pair = call(
        partial(feed_kernel, layout),
        [(rows_about, 0), (total, 0), (cotangent, 0), (gain_two, None)]
        + [(a, None) for a in gateup + down],
        [
            (shape_of(per_token + (width,), bf16), 0),
            (shape_of(per_token + (width,), bf16), 0),
            (shape_of(per_token + (units,), bf16), 0),
            (shape_of((2,) + per_token + (units,), bf16), 1),
        ],
        seqs,
    )
    grad_two = lax.psum(two_part, "mp")

    def feed_gradients(some, *others):
        outs = [(shape_of((m, units, n), bf16), None) for _, n in some for m in (2, 1)]
        base, span = some[0][0], sum(n for _, n in some)
        aligned = base % span == 0
        at = base // span if aligned else 0
        cols = pl.BlockSpec((count_rows, span if aligned else width), lambda s: (0, at))
        made = pl.pallas_call(
            partial(feed_gradient_kernel, base if aligned else 0, some),
            cost_estimate=FREE,
            grid=(1,),
            in_specs=[
                cols,
                cols,
                pl.BlockSpec((2, count_rows, units), lambda s: (0, 0, 0)),
                pl.BlockSpec((count_rows, units), lambda s: (0, 0)),
            ]
            + [pl.BlockSpec(memory_space=pl.ANY)] * len(others),
            out_specs=[pl.BlockSpec(o.shape, lambda s: (0, 0, 0)) for o, _ in outs],
            out_shape=[o for o, _ in outs],
            compiler_params=pltpu.CompilerParams(vmem_limit_bytes=VMEM),
        )(flat(hidden_two), flat(cotangent), flat(grad_pair), flat(hidden_mlp), *others)
        return made[::2], made[1::2]

    if near_four:
        feed_far = feed_gradients(ranges[3:])
        feed_in = [far_hop(*far) for far in feed_far]
        near_gateup, near_down = feed_gradients(ranges[:3], feed_far[0][0])
        first_made = [(near_gateup[0], "any")]
    else:
        [grad_gateup], [grad_down] = feed_gradients(ranges)
        held = first_made = []
    [down_part] = call(
        partial(down_kernel, layout),
        [(hidden_mlp, 0)] + [(a, None) for a in down] + first_made,
        [(shape_of(per_token + (width,), bf16), 0)],
        seqs,
        scalar=turn_one,
    )
    if near_four:
        gateup_added = near_sums(near_gateup, feed_in[0], *feed_in[1], down_part)
        down_added = near_sums(near_down, feed_in[1])
        gateup_sums, down_sums = near_hop(gateup_added), near_hop(down_added)
        down_part = after(down_part, gateup_added[1])
        held = [(a, "any") for a in gateup_sums[1:]]
    mlp_share = lax.psum_scatter(down_part, "mp", scatter_dimension=2, tiled=True)
    grad_mix, middle_own, mlpgain, drule, dgate, dgain, direct = call(
        partial(middle_back_kernel, pair_layout, len(out_pieces)),
        [
            (grad_two, 0),
            (cotangent, 0),
            (rows_about, 0),
            (total, 0),
            (gain_two, None),
            (rule, 0),
            (gates, 0),
            (gain_head, None),
            (qo, 0),
        ]
        + [(a, None) for a in out_pieces]
        + [(down_part, "any")]
        + held,
        [
            (shape_of(per_token + (width,), bf16), 0),
            (shape_of(per_token + (local_width,), f32), 0),
            (shape_of((seqs, 1, width), f32), 0),
            (shape_of(per_token + (inner,), f32), 0),
            (shape_of(per_token + (inner,), bf16), 0),
            (shape_of((seqs, 1, DK), f32), 0),
            (shape_of(square, bf16), 0),
        ],
        seqs,
        scalar=jnp.stack([turn, column_about]),
        scratch=[pltpu.VMEM((block, width), f32)],
    )
    directs = [shifted(direct, "dp", -c) for c in range(1, dp)]
    if near_four:
        pair_grads = call(
            partial(pair_gradient_kernel, [(k * size, size) for k in range(4)]),
            [(flat(a), None) for a in (hidden_one, dgate, normed, grad_mix)],
            [(shape_of((2, size, inner), bf16), None)] * 4,
            1,
        )
        down_total = sum_last(down_sums, pair_grads[3])
        held = [(a, "any") for a in (pair_grads[3], down_total)]
    else:
        grad_outgate = jnp.einsum(
            "td,tc->dc", flat(hidden_one), flat(dgate), preferred_element_type=f32
        )
        grad_outproj = jnp.einsum(
            "tc,td->cd", flat(normed), flat(grad_mix), preferred_element_type=f32
        )
        held = []
    dproj, last, first, dtaps, dlogits = call(
        partial(back_kernel, len(directs)),
        [
            (proj, 1),
            (before, 1),
            (full_conv, None),
            (logits, 0),
            (inverse, 0),
            (wu, 0),
            (state, 0),
            (drule, 0),
        ]
        + [(a, 0) for a in directs + nexts]
        + held,
        [
            (shape_of((3,) + per_token + (inner,), bf16), 1),
            (shape_of((3, seqs, PAD, inner), f32), 1),
            (shape_of((3, seqs, PAD, inner), f32), 1),
            (shape_of((seqs, 3 * KW, inner), f32), 0),
            (shape_of(per_token + (heads,), bf16), 0),
        ],
        seqs,
    )
    late = []
    if near_four:
        gateup_total = sum_last(gateup_sums, dlogits)
        late = [(gateup_total, "any")]
    later = shifted(first, "dp", -1)
    dproj = lax.dynamic_update_slice(dproj, (last + later).astype(bf16), (0, 0, block - PAD, 0))
    one_low, row_part, gain_part = call(
        partial(first_back_kernel, layout, pair_layout, len(gate_pieces)),
        [
            (flat(dproj), None),
            (flat(dgate), None),
            (flat(dlogits), None),
            (flat(proj), None),
            (flat(gates), None),
            (flat(logits), None),
            (about_beta.T.astype(f32), None),
            (flat(rows_about), None),
            (flat(scale_one), None),
        ]
        + [(a, None) for a in qkv + gate_pieces]
        + late,
        [
            (shape_of((count_rows, width), bf16), None),
            (shape_of((1, count_rows), f32), None),
            (shape_of((1, width), f32), None),
        ],
        1,
        scalar=turn_one,
    )
    one_share = lax.psum_scatter(
        one_low.reshape(seqs, block, width), "mp", scatter_dimension=2, tiled=True
    ).astype(f32)
    made = call(
        partial(qkv_gradient_kernel, ranges),
        [(flat(hidden_one), None), (flat(dproj), None), (flat(dlogits), None), (row_part, "any")],
        [(shape_of((3, n, inner), bf16), None) for _, n in ranges]
        + [(shape_of((heads, width), f32), None)],
        1,
    )

    def pieces(array, axis, about):
        shape = array.shape
        cut = array.reshape(shape[:axis] + (dp, shape[axis] // dp) + shape[axis + 1 :])
        cut = jnp.moveaxis(cut, axis, 0).reshape(dp, -1)
        return blocks_about(cut, 0) if about else cut

    smalls = jnp.concatenate(
        [
            pieces(jnp.sum(dtaps, 0).reshape(3, KW, heads, DK), 3, True),
            pieces(made[-1].T, 0, False),
            pieces(gain_part[0], 0, False),
            pieces(jnp.sum(mlpgain, (0, 1)), 0, False),
            pieces(jnp.sum(dgain, (0, 1)), 0, True),
        ],
        1,
    )
    small_shapes = [a.shape for a in (conv_weight, w_beta, mixer_gain, mlp_gain, head_gain)]
    if near_four:
        own_qkv, *near_qkv = near_sums(made[:3], far_hop(made[3], made[4]))
        smalls = jnp.pad(smalls, ((0, 0), (0, -smalls.shape[1] % 1024))).reshape(dp, -1, 128)
        sent = smalls.astype(bf16)
        got = [swap(sent[bits], bits) for bits in (1, 2, 3)]
        first_mix = (conv_weight.size + w_beta.size) // 128
        last_mix = first_mix + mixer_gain.size // 128
        lines = count_rows // 128 + last_mix - first_mix
        mine, rest = call(
            partial(
                add_small_kernel,
                slice(first_mix, last_mix),
                last_mix + mlp_gain.size // 128,
            ),
            [(a, None) for a in [smalls[0]] + got + [row_part]],
            [
                (shape_of(smalls.shape[1:], f32), None),
                (shape_of((lines + 8 - lines % 8, 128), f32), None),
            ],
            1,
        )
        pair_far = after(jnp.split(pair_grads[3], 2, 1), made[0])
        pair_near = near_sums(pair_grads[:3], far_hop(*pair_far))[1:]
        mine = mine.reshape(-1)
        sum_qkv = sum_last(near_hop((own_qkv, *near_qkv)))
        sum_gateup = jnp.swapaxes(gateup_total, 1, 2)
        sum_down = down_total[0]
        pair_sums = near_hop((pair_grads[0], *pair_near))
    else:
        gathered = lax.all_gather(smalls.astype(bf16), "dp")
        mine = jnp.sum(
            lax.dynamic_index_in_dim(gathered, place, 1, keepdims=False).astype(f32), 0
        )

        def scattered(array, axis):
            return lax.psum_scatter(array, "dp", scatter_dimension=axis, tiled=True).astype(f32)

        sum_qkv = scattered(made[0], 1)
        sum_outgate = scattered(grad_outgate.astype(bf16), 0)
        sum_out = scattered(grad_outproj.astype(bf16), 1)
        sum_gateup = jnp.swapaxes(scattered(grad_gateup, 2), 1, 2)
        sum_down = scattered(grad_down[0], 1)
    sum_conv, sum_beta, sum_mix, sum_mlp, sum_head = unpack(mine, small_shapes)
    if near_four:
        bit = 1
        while bit < lax.axis_size("mp"):
            devices = lax.axis_size("mp")
            rest = rest + lax.ppermute(rest, "mp", [(i, i ^ bit) for i in range(devices)])
            bit *= 2
        rest_sum = rest.reshape(-1)
    else:
        rest_sum = lax.psum(pack([row_part, sum_mix, sum_head]), "mp")
    row_sum, sum_mix, sum_head = unpack(rest_sum, [(count_rows,), sum_mix.shape, sum_head.shape])

    own_tokens = tokens.astype(f32)
    mixed_out = (own_tokens + own(total).astype(f32) + mlp_share.astype(f32)).astype(bf16)
    row_mean = (row_sum / width).reshape(seqs, block, 1)
    gain_own = lax.dynamic_slice_in_dim(gain_one, column, local_width, 1)
    tokens_grad = middle_own + scale_one * (
        one_share * gain_own - own_tokens * scale_one * row_mean
    )
    tokens_grad = tokens_grad.astype(bf16)
    if near_four:
        done = [(a, "any") for a in (sum_qkv, tokens_grad, mixed_out)]
        sum_outgate, sum_out = call(
            add_pair_kernel,
            [(a, None) for a in pair_sums] + done,
            [(shape_of(w_outgate.shape, f32), None), (shape_of(w_out.shape, f32), None)],
            1,
            limit=SMALL,
        )
    return (
        mixed_out,
        tokens_grad,
        sum_qkv,
        sum_conv,
        sum_beta,
        sum_outgate,
        sum_head,
        sum_out,
        sum_mix,
        sum_mlp,
        sum_gateup,
        sum_down,
    )


def solution(mesh):
    return jax.shard_map(
        body,
        mesh=mesh,
        in_specs=(
            P(None, "dp", "mp"),
            P(None, "dp", None),
            P(None, "dp"),
            P(),
            P(None, "dp", "mp"),
            P(None, None, "mp", "dp"),
            P("dp", "mp"),
            P("dp", "mp"),
            P("dp"),
            P("mp", "dp"),
            P("dp"),
            P("dp"),
            P(None, "dp", "mp"),
            P("mp", "dp"),
        ),
        out_specs=(
            P(None, "dp", "mp"),
            P(None, "dp", "mp"),
            P(None, "dp", "mp"),
            P(None, None, "mp", "dp"),
            P("dp", "mp"),
            P("dp", "mp"),
            P("dp"),
            P("mp", "dp"),
            P("dp"),
            P("dp"),
            P(None, "dp", "mp"),
            P("mp", "dp"),
        ),
        check_vma=False,
    )
```
